32 devices in a mesh: space: 16 (over z, y, core), ens: 2 (over x).
Axes of the slice: x: 2, y: 2, z: 4, core: 2. Of those that a mesh axis runs over, the one named last changes fastest.
Arguments:
- members: bfloat16 [2, 2048, 1024], P('ens', 'space'), may hold values from -6 to 6
- w_attn: bfloat16 [1024, 3072], P(('space', 'ens'))
- w_mix: bfloat16 [1024, 1024], P(('space', 'ens')), may hold values from -0.1875 to 0.1875
- readout_matrix: bfloat16 [1024, 100], P(('space', 'ens')), may hold values from -0.1875 to 0.1875
- observed_truth: float32 [100, 2048], P(None, 'space'), may hold values from -6 to 6
- cell_surface_factor: float32 [2048], P('space'), may hold values from 0.3 to 3
- neighbours: int32 [32, 4], P('space'), may hold values from -1 to 31, as said below
Outputs:
- prediction: float32 [2, 100, 2048], P('ens', None, 'space')
- grad_kv: float32 [1024, 2048], P(('space', 'ens'))
The draws below stay inside these ranges and needn't reach their ends.
Inputs may be any that keep to these rules, and one draw needn't show every extreme that they name: `neighbours`: row t holds t itself in slot 0 and 3 distinct other tiles of t - 2 to t + 2; a slot whose tile lies outside the grid holds -1.
All inputs are finite; a program needn't handle non-finite values.
Results may differ from the reference program's by a relative error of at most 0.013.
Values may be sent and summed in bfloat16 or wider, within the bound.
No kernel may reach another device: no remote copies, remote signals or barrier semaphores. Data moves between devices by JAX's collectives and lax.ppermute only.
A program may use at most 64 MiB of HBM per device.

```python
import math
import jax
import jax.numpy as jnp
from jax import lax

LATENT_DIM = 1024
HEADS = 16
HEAD = 64
FIELD_NUM = 100
TILE = 64
RADIUS = 2
K_NB = 4
REALIZATION_NUM = 2
NODES = 2048


def draw_w_attn(key, part):
    key = jax.random.fold_in(key, 11)
    key_base = jax.random.fold_in(key, 0)
    normal_part = jax.random.normal(key_base, (LATENT_DIM, 3 * LATENT_DIM), jnp.float32) * LATENT_DIM ** (-0.5)
    return normal_part.astype(jnp.bfloat16)


def draw_neighbours(key, part):
    key = jax.random.fold_in(key, 5)
    tile_count = NODES // TILE
    row_keys = jax.random.split(key, tile_count)
    offsets = jnp.concatenate([jnp.arange(-RADIUS, 0), jnp.arange(1, RADIUS + 1)]).astype(jnp.int32)
    chosen_steps = jax.vmap(lambda row_key: jax.random.permutation(row_key, offsets))(row_keys)[:, :K_NB - 1]
    tile_index = jnp.arange(tile_count, dtype=jnp.int32)[:, None]
    chosen = tile_index + chosen_steps
    chosen = jnp.where((chosen >= 0) & (chosen < tile_count), chosen, -1)
    return jnp.concatenate([tile_index, chosen], axis=1).astype(jnp.int32)


def levels(rng, dims, cuts, smallest, largest):
    def one(axis_at, shards_of):
        draws = jax.random.uniform(jax.random.fold_in(jax.random.fold_in(rng, 6), axis_at), (shards_of,), jnp.float32, smallest / len(cuts), largest / len(cuts))
        return jnp.repeat(jnp.exp(draws), dims[axis_at] // shards_of).reshape((-1,) + (1,) * (len(dims) - axis_at - 1))

    level = one(*cuts[0])
    for cut in cuts[1:]:
        level = level * one(*cut)
    return level


def normal_values(stream_key, dims, deviation, limit, cuts=(), kind=jnp.bfloat16):
    array = deviation * jax.random.normal(stream_key, dims, jnp.float32)
    if cuts:
        array = array * levels(stream_key, dims, cuts, -0.22, 0.18)
    return jnp.clip(array, -limit, limit).astype(kind)


def setup_inputs(seed: int = 0) -> dict:
    keys = jax.random.split(jax.random.key(seed), 8)
    members = normal_values(keys[0], (REALIZATION_NUM, NODES, LATENT_DIM), 1.0, 6.0, ((0, 2), (1, 16)))
    w_attn = draw_w_attn(jax.random.fold_in(keys[7], 71), 0)
    w_mix = normal_values(keys[2], (LATENT_DIM, LATENT_DIM), LATENT_DIM ** -0.5, 0.1875, ((0, 32),))
    readout_matrix = normal_values(keys[3], (LATENT_DIM, FIELD_NUM), LATENT_DIM ** -0.5, 0.1875, ((0, 32),))
    observed_truth = normal_values(keys[4], (FIELD_NUM, NODES), 1.0, 6.0, ((1, 16),), jnp.float32)
    cell_surface_factor = jnp.clip(jnp.exp(math.log(3.0) - 2.3025851 * jax.random.uniform(keys[5], (NODES,), jnp.float32) ** levels(keys[5], (NODES,), ((0, 16),), -0.2, 0.2)), 0.3, 3.0)
    neighbours = draw_neighbours(jax.random.fold_in(keys[7], 71), 0)
    return {"members": members, "w_attn": w_attn, "w_mix": w_mix, "readout_matrix": readout_matrix, "observed_truth": observed_truth, "cell_surface_factor": cell_surface_factor, "neighbours": neighbours}


NORM_EPS = 1e-06
SOFT_WIDTH = 0.0625
MASKED = -1e+30

def exact_dot(left, right):
    return jnp.dot(left.astype(jnp.float32), right.astype(jnp.float32), precision=lax.Precision.HIGHEST)

def rms_rows(matrix):
    return matrix * lax.rsqrt(lax.optimization_barrier(jnp.mean(matrix * matrix, axis=-1, keepdims=True)) + NORM_EPS)

def rms_back(matrix, upstream):
    inverse = lax.rsqrt(lax.optimization_barrier(jnp.mean(matrix * matrix, axis=-1, keepdims=True)) + NORM_EPS)
    return inverse * upstream - matrix * inverse ** 3 * lax.optimization_barrier(jnp.mean(upstream * matrix, axis=-1, keepdims=True))

def softened_derivative(spread):
    return spread * lax.rsqrt(spread * spread + SOFT_WIDTH)

def attend(queries, key_rows, values, usable):
    factor = HEAD ** (-0.5)
    scores = jnp.einsum('bihc,bjhc->bhij', queries.astype(jnp.float32), key_rows.astype(jnp.float32), precision=lax.Precision.HIGHEST) * factor
    scores = jnp.where(usable[:, None, None, :], scores, MASKED)
    peak_score = lax.optimization_barrier(jnp.max(scores, axis=-1, keepdims=True))
    raised = jnp.exp(scores - peak_score)
    attn_probs = raised / lax.optimization_barrier(jnp.sum(raised, axis=-1, keepdims=True))
    outcome = jnp.einsum('bhij,bjhc->bihc', attn_probs.astype(jnp.bfloat16).astype(jnp.float32), values.astype(jnp.float32), precision=lax.Precision.HIGHEST)
    return (attn_probs, outcome.astype(jnp.bfloat16))

def attend_back(attn_probs, queries, key_rows, values, grad_out):
    factor = HEAD ** (-0.5)
    highest = lax.Precision.HIGHEST
    grad_probs = jnp.einsum('bihc,bjhc->bhij', grad_out.astype(jnp.float32), values.astype(jnp.float32), precision=highest)
    row_delta = lax.optimization_barrier(jnp.sum(attn_probs * grad_probs, axis=-1, keepdims=True))
    grad_scores = (attn_probs * (grad_probs - row_delta) * factor).astype(jnp.bfloat16).astype(jnp.float32)
    key_grad = jnp.einsum('bhij,bihc->bjhc', grad_scores, queries.astype(jnp.float32), precision=highest).astype(jnp.bfloat16)
    value_grad = jnp.einsum('bhij,bihc->bjhc', attn_probs.astype(jnp.bfloat16).astype(jnp.float32), grad_out.astype(jnp.float32), precision=highest).astype(jnp.bfloat16)
    return (key_grad, value_grad)

def member_forward(member_state, w_attn, w_mix, tile_ids, usable_slot):
    tile_count = NODES // TILE
    key_count = K_NB * TILE
    source = member_state.astype(jnp.float32)
    normed = rms_rows(source).astype(jnp.bfloat16)
    projected = exact_dot(normed, w_attn).astype(jnp.bfloat16)
    query_tiles = projected[:, :LATENT_DIM].reshape(tile_count, TILE, HEADS, HEAD)
    kv_tiles = projected[:, LATENT_DIM:].reshape(tile_count, TILE, 2 * LATENT_DIM)

    def forward_tile(packed):
        queries, id_row, usable_row = packed
        kv_block = kv_tiles[id_row].reshape(key_count, 2 * LATENT_DIM)
        key_rows = kv_block[:, :LATENT_DIM].reshape(1, key_count, HEADS, HEAD)
        value_rows = kv_block[:, LATENT_DIM:].reshape(1, key_count, HEADS, HEAD)
        usable = jnp.repeat(usable_row, TILE)[None]
        attn_probs, outcome = attend(queries[None], key_rows, value_rows, usable)
        return outcome[0]
    attn_out = lax.map(forward_tile, (query_tiles, tile_ids, usable_slot)).reshape(NODES, LATENT_DIM)
    hidden = source + exact_dot(attn_out, w_mix)
    predicted_fields = rms_rows(hidden).astype(jnp.bfloat16)
    return (normed, query_tiles, kv_tiles, attn_out, hidden, predicted_fields)

def reference(members, w_attn, w_mix, readout_matrix, observed_truth, cell_surface_factor, neighbours):
    tile_count = NODES // TILE
    key_count = K_NB * TILE
    usable_slot = neighbours >= 0
    tile_ids = jnp.clip(neighbours, 0, tile_count - 1).astype(jnp.int32)

    def predict_member(member_state):
        outs = member_forward(member_state, w_attn, w_mix, tile_ids, usable_slot)
        return exact_dot(outs[5], readout_matrix).T
    prediction = lax.map(predict_member, members)
    spread_pair_values = jnp.zeros_like(prediction)
    for other_realization in range(REALIZATION_NUM):
        spread_pair_values = spread_pair_values + softened_derivative(prediction - prediction[other_realization][None])
    derivative_sum_all = cell_surface_factor[None, None, :] / FIELD_NUM * (softened_derivative(prediction - observed_truth[None]) - spread_pair_values / (REALIZATION_NUM - 1))

    def member_backward(accumulated_values, packed):
        member_state, member_derivative = packed
        normed, query_tiles, kv_tiles, attn_out, hidden, predicted_fields = member_forward(member_state, w_attn, w_mix, tile_ids, usable_slot)
        grad_fore = member_derivative.astype(jnp.bfloat16)
        grad_decoded = exact_dot(grad_fore.T, readout_matrix.T)
        grad_hidden = rms_back(hidden, grad_decoded).astype(jnp.bfloat16)
        grad_attn_out = exact_dot(grad_hidden, w_mix.T).astype(jnp.bfloat16)
        grad_tiles = grad_attn_out.reshape(tile_count, TILE, HEADS, HEAD)

        def backward_tile(inner):
            queries, id_row, usable_row, grad_out = inner
            kv_block = kv_tiles[id_row].reshape(key_count, 2 * LATENT_DIM)
            key_rows = kv_block[:, :LATENT_DIM].reshape(1, key_count, HEADS, HEAD)
            value_rows = kv_block[:, LATENT_DIM:].reshape(1, key_count, HEADS, HEAD)
            usable = jnp.repeat(usable_row, TILE)[None]
            attn_probs, outcome = attend(queries[None], key_rows, value_rows, usable)
            key_grad, value_grad = attend_back(attn_probs, queries[None], key_rows, value_rows, grad_out[None])
            return jnp.concatenate([key_grad.reshape(K_NB, TILE, LATENT_DIM), value_grad.reshape(K_NB, TILE, LATENT_DIM)], axis=2)
        contrib = lax.map(backward_tile, (query_tiles, tile_ids, usable_slot, grad_tiles))
        kv_grads = jnp.zeros((tile_count, TILE, 2 * LATENT_DIM), jnp.float32).at[tile_ids.reshape(-1)].add(contrib.reshape(tile_count * K_NB, TILE, 2 * LATENT_DIM).astype(jnp.float32)).reshape(NODES, 2 * LATENT_DIM)
        kv_high = kv_grads.astype(jnp.bfloat16)
        kv_low = (kv_grads - kv_high.astype(jnp.float32)).astype(jnp.bfloat16)
        term_kv = exact_dot(normed.T, kv_high) + exact_dot(normed.T, kv_low)
        return (accumulated_values + term_kv, None)
    start_values = jnp.zeros((LATENT_DIM, 2 * LATENT_DIM), jnp.float32)
    accumulated_values, unused = lax.scan(member_backward, start_values, (members, derivative_sum_all))
    return (prediction, accumulated_values)
```

```python
import functools

import jax
import jax.numpy as jnp
from jax import lax
from jax.experimental import pallas as pl
from jax.experimental.pallas import tpu as pltpu
from jax.sharding import Mesh
from jax.sharding import PartitionSpec as P

LATENT_DIM = 1024
HEADS = 16
HEAD = 64
FIELD_NUM = 100
TILE = 64
RADIUS = 2
K_NB = 4
GROUP = 8
COLS = LATENT_DIM // GROUP
RIM = RADIUS * TILE
FIELD_PAD = 128

NORM_EPS = 1e-06
SOFT_WIDTH = 0.0625
MASKED = -1e30

F32 = jnp.float32
BF16 = jnp.bfloat16


def rms_rows(matrix):
    return matrix * lax.rsqrt(jnp.mean(matrix * matrix, axis=-1, keepdims=True) + NORM_EPS)


def rms_back(matrix, upstream):
    inverse = lax.rsqrt(jnp.mean(matrix * matrix, axis=-1, keepdims=True) + NORM_EPS)
    return inverse * upstream - matrix * inverse**3 * jnp.mean(
        upstream * matrix, axis=-1, keepdims=True
    )


def softened_derivative(spread):
    return spread * lax.rsqrt(spread * spread + SOFT_WIDTH)


def by_head(rows):
    lane = lax.broadcasted_iota(jnp.int32, rows.shape, 1)
    zero = jnp.zeros_like(rows)
    return jnp.concatenate(
        [jnp.where(lane < HEAD, rows, zero), jnp.where(lane < HEAD, zero, rows)], axis=0
    )


def tile_keys(slots_ref, tile, last_tile, kv):
    lane = lax.broadcasted_iota(jnp.int32, (1, K_NB * TILE), 1)
    usable = jnp.zeros((1, K_NB * TILE), jnp.int32)
    places, keys, values = [], [], []
    for slot in range(K_NB):
        at = slots_ref[tile, slot]
        usable = jnp.where(lane // TILE == slot, (at >= 0).astype(jnp.int32), usable)
        place = pl.multiple_of(jnp.clip(at, 0, last_tile) * TILE, TILE)
        places.append(place)
        keys.append(kv[pl.ds(place, TILE), :COLS])
        values.append(kv[pl.ds(place, TILE), COLS:])
    return places, usable > 0, jnp.concatenate(keys, axis=0), jnp.concatenate(values, axis=0)


def probabilities(queries, keys, usable):
    scores = lax.dot_general(
        queries, keys, (((1,), (1,)), ((), ())), preferred_element_type=F32
    ) * (HEAD**-0.5)
    scores = jnp.where(usable, scores, MASKED)
    raised = jnp.exp(scores - jnp.max(scores, axis=-1, keepdims=True))
    return raised * (1.0 / jnp.sum(raised, axis=-1, keepdims=True))


def fill(kv, low_ref, own_ref, high_ref):
    rows = own_ref.shape[0]
    kv[0:RIM, :] = low_ref[...]
    kv[RIM : RIM + rows, :] = own_ref[...]
    kv[RIM + rows : 2 * RIM + rows, :] = high_ref[...]


def forward_kernel(slots_ref, q_ref, low_ref, own_ref, high_ref, out_ref, kv):
    tiles = q_ref.shape[0] // TILE
    last_tile = tiles + 2 * RADIUS - 1
    fill(kv, low_ref, own_ref, high_ref)

    def step(tile, carry):
        rows = pl.ds(pl.multiple_of(tile * TILE, TILE), TILE)
        _, usable, keys, values = tile_keys(slots_ref, tile, last_tile, kv)
        probs = probabilities(by_head(q_ref[rows, :]), keys, usable)
        both = jnp.dot(probs.astype(BF16), values, preferred_element_type=F32)
        lane = lax.broadcasted_iota(jnp.int32, (TILE, COLS), 1)
        out_ref[rows, :] = jnp.where(lane < HEAD, both[:TILE], both[TILE:]).astype(BF16)
        return carry

    lax.fori_loop(0, tiles, step, 0, unroll=4)


def backward_kernel(slots_ref, q_ref, low_ref, own_ref, high_ref, g_ref, out_ref, kv, total):
    tiles = q_ref.shape[0] // TILE
    last_tile = tiles + 2 * RADIUS - 1
    fill(kv, low_ref, own_ref, high_ref)
    total[...] = jnp.zeros_like(total)
    over_rows = (((0,), (0,)), ((), ()))

    def step(tile, carry):
        rows = pl.ds(pl.multiple_of(tile * TILE, TILE), TILE)
        places, usable, keys, values = tile_keys(slots_ref, tile, last_tile, kv)
        queries = by_head(q_ref[rows, :])
        grads = by_head(g_ref[rows, :])
        probs = probabilities(queries, keys, usable)
        grad_probs = lax.dot_general(
            grads, values, (((1,), (1,)), ((), ())), preferred_element_type=F32
        )
        row_delta = jnp.sum(probs * grad_probs, axis=-1, keepdims=True)
        grad_scores = (probs * (grad_probs - row_delta) * (HEAD**-0.5)).astype(BF16)
        key_grad = lax.dot_general(grad_scores, queries, over_rows, preferred_element_type=F32)
        value_grad = lax.dot_general(
            probs.astype(BF16), grads, over_rows, preferred_element_type=F32
        )
        key_grad = key_grad.astype(BF16).astype(F32)
        value_grad = value_grad.astype(BF16).astype(F32)
        for slot in range(K_NB):
            part = slice(slot * TILE, (slot + 1) * TILE)
            total[pl.ds(places[slot], TILE), :COLS] += key_grad[part]
            total[pl.ds(places[slot], TILE), COLS:] += value_grad[part]
        return carry

    lax.fori_loop(0, tiles, step, 0, unroll=2)
    high = total[...].astype(BF16)
    out_ref[:, : 2 * COLS] = high
    out_ref[:, 2 * COLS :] = (total[...] - high.astype(F32)).astype(BF16)


VMEM = pl.BlockSpec(memory_space=pltpu.VMEM)
SMEM = pl.BlockSpec(memory_space=pltpu.SMEM)


def attention_forward(slots, queries, low, own, high):
    rows = queries.shape[0]
    return pl.pallas_call(
        forward_kernel,
        out_shape=jax.ShapeDtypeStruct((rows, COLS), BF16),
        in_specs=[SMEM] + [VMEM] * 4,
        out_specs=VMEM,
        scratch_shapes=[pltpu.VMEM((rows + 2 * RIM, 2 * COLS), BF16)],
        compiler_params=pltpu.CompilerParams(vmem_limit_bytes=24 * 2**20),
        cost_estimate=pl.CostEstimate(
            flops=rows * COLS * 4 * 512, bytes_accessed=rows * COLS * 8, transcendentals=rows * 512
        ),
        name="attention_forward",
    )(slots, queries, low, own, high)


def attention_backward(slots, queries, low, own, high, grads):
    rows = queries.shape[0]
    ext = rows + 2 * RIM
    return pl.pallas_call(
        backward_kernel,
        out_shape=jax.ShapeDtypeStruct((ext, 4 * COLS), BF16),
        in_specs=[SMEM] + [VMEM] * 5,
        out_specs=VMEM,
        scratch_shapes=[pltpu.VMEM((ext, 2 * COLS), BF16), pltpu.VMEM((ext, 2 * COLS), F32)],
        compiler_params=pltpu.CompilerParams(vmem_limit_bytes=24 * 2**20),
        cost_estimate=pl.CostEstimate(
            flops=rows * COLS * 10 * 512, bytes_accessed=rows * COLS * 16, transcendentals=rows * 512
        ),
        name="attention_backward",
    )(slots, queries, low, own, high, grads)


def body(members, w_attn, w_mix, readout_matrix, observed_truth, cell_surface_factor, neighbours):
    halves, group, members_num = (lax.axis_size(axis) for axis in ("half", "group", "ens"))
    shard = w_attn.shape[0]
    node_rows = members.shape[1]
    up = [(i, i + 1) for i in range(halves - 1)]
    down = [(target, source) for source, target in up]

    source = members[0].astype(F32)
    normed = rms_rows(source).astype(BF16)
    normed_all = lax.all_gather(normed, "group", axis=0, tiled=True)
    slots = lax.all_gather(neighbours, "group", axis=0, tiled=True)
    tiles = slots.shape[0]
    slots = jnp.where(slots >= 0, slots - lax.axis_index("half") * tiles + RADIUS, -1)

    columns = w_attn.reshape(shard, 3, group, COLS).transpose(2, 0, 1, 3).reshape(group, shard, 3 * COLS)
    columns = lax.all_to_all(columns, "group", 0, 0)
    columns = lax.all_gather(columns, ("half", "ens"), axis=0)
    columns = columns.reshape(halves, members_num, group, shard, 3 * COLS)
    columns = columns.transpose(0, 2, 1, 3, 4).reshape(LATENT_DIM, 3 * COLS)

    packed = jnp.concatenate(
        [w_mix, jnp.pad(readout_matrix, ((0, 0), (0, FIELD_PAD - FIELD_NUM)))], axis=1
    )
    width = packed.shape[1]
    packed = lax.all_gather(packed, "ens", axis=0, tiled=True)
    packed = lax.all_gather(packed, "half", axis=0)
    packed = lax.all_gather(packed, "group", axis=0)
    packed = packed.transpose(1, 0, 2, 3).reshape(LATENT_DIM, width)
    mix_full = packed[:, :LATENT_DIM]
    dec_full = packed[:, LATENT_DIM : LATENT_DIM + FIELD_NUM]

    projected = jnp.dot(normed_all, columns, preferred_element_type=F32).astype(BF16)
    queries, own = projected[:, :COLS], projected[:, COLS:]
    low = lax.ppermute(own[-RIM:], "half", up)
    high = lax.ppermute(own[:RIM], "half", down)
    normed_low = lax.ppermute(normed_all[-RIM:], "half", up)
    normed_high = lax.ppermute(normed_all[:RIM], "half", down)

    outcome = attention_forward(slots, queries, low, own, high)
    attn_out = lax.all_to_all(outcome.reshape(group, node_rows, COLS), "group", 0, 0)
    attn_out = attn_out.transpose(1, 0, 2).reshape(node_rows, LATENT_DIM)
    hidden = source + jnp.dot(attn_out, mix_full, preferred_element_type=F32)
    predicted_fields = rms_rows(hidden).astype(BF16)
    prediction = lax.dot_general(
        dec_full, predicted_fields, (((0,), (1,)), ((), ())), preferred_element_type=F32
    )[None]
    spread_pair_values = jnp.sum(
        softened_derivative(prediction - lax.all_gather(prediction, "ens", axis=0, tiled=True)),
        axis=0,
        keepdims=True,
    )
    derivative_sum_all = (
        cell_surface_factor[None, None, :]
        / FIELD_NUM
        * (
            softened_derivative(prediction - observed_truth[None])
            - spread_pair_values / (members_num - 1)
        )
    )
    grad_fore = derivative_sum_all[0].astype(BF16)
    grad_decoded = lax.dot_general(
        grad_fore, dec_full, (((0,), (1,)), ((), ())), preferred_element_type=F32
    )
    grad_hidden = rms_back(hidden, grad_decoded).astype(BF16)
    grad_attn_out = lax.dot_general(
        grad_hidden, mix_full, (((1,), (1,)), ((), ())), preferred_element_type=F32
    ).astype(BF16)
    grads = grad_attn_out.reshape(node_rows, group, COLS).transpose(1, 0, 2)
    grads = lax.all_to_all(grads, "group", 0, 0).reshape(group * node_rows, COLS)

    kv_grads = attention_backward(slots, queries, low, own, high, grads)
    normed_ext = jnp.concatenate([normed_low, normed_all, normed_high], axis=0)
    over_rows = (((0,), (0,)), ((), ()))
    term = lax.dot_general(normed_ext, kv_grads[:, : 2 * COLS], over_rows, preferred_element_type=F32)
    term = term + lax.dot_general(
        normed_ext, kv_grads[:, 2 * COLS :], over_rows, preferred_element_type=F32
    )
    term = term.astype(BF16).reshape(halves, group, members_num, shard, 2 * COLS)
    term = term.transpose(0, 2, 1, 3, 4).reshape(halves * members_num, group, shard, 2 * COLS)
    term = lax.all_to_all(term, ("half", "ens"), 0, 0)
    term = jnp.sum(term.astype(F32), axis=0)
    term = lax.all_to_all(term, "group", 0, 0)
    grad_kv = term.reshape(group, shard, 2, COLS).transpose(1, 2, 0, 3).reshape(shard, 2 * LATENT_DIM)
    return (prediction, grad_kv)


def solution(mesh):
    space, ens = mesh.shape["space"], mesh.shape["ens"]
    split = Mesh(mesh.devices.reshape(space // GROUP, GROUP, ens), ("half", "group", "ens"))
    nodes, rows = ("half", "group"), ("half", "group", "ens")
    in_specs = (
        P("ens", nodes, None),
        P(rows, None),
        P(rows, None),
        P(rows, None),
        P(None, nodes),
        P(nodes),
        P(nodes, None),
    )
    out_specs = (P("ens", None, nodes), P(rows, None))
    return jax.shard_map(body, mesh=split, in_specs=in_specs, out_specs=out_specs, check_vma=False)
```

```python
import functools

import jax
import jax.numpy as jnp
from jax import lax
from jax.experimental import pallas as pl
from jax.experimental.pallas import tpu as pltpu
from jax.sharding import Mesh
from jax.sharding import PartitionSpec as P

LATENT_DIM = 1024
HEADS = 16
HEAD = 64
FIELD_NUM = 100
TILE = 64
RADIUS = 2
K_NB = 4
QUAD = 4
CORES = 2
GROUP = QUAD * CORES
COLS = LATENT_DIM // GROUP
RIM = RADIUS * TILE
FIELD_PAD = 128

NORM_EPS = 1e-06
SOFT_WIDTH = 0.0625
MASKED = -1e30

F32 = jnp.float32
BF16 = jnp.bfloat16

VMEM = pl.BlockSpec(memory_space=pltpu.VMEM)
SMEM = pl.BlockSpec(memory_space=pltpu.SMEM)
OVER_ROWS = (((0,), (0,)), ((), ()))
OVER_COLUMNS = (((1,), (1,)), ((), ()))


def call(kernel, name, outs, ins, scratch=(), flops=0, moved=0, exps=0):
    return pl.pallas_call(
        kernel,
        out_shape=[jax.ShapeDtypeStruct(shape, kind) for shape, kind in outs],
        in_specs=[SMEM if space == "s" else VMEM for space in ins],
        out_specs=[VMEM] * len(outs),
        scratch_shapes=[pltpu.VMEM(shape, kind) for shape, kind in scratch],
        compiler_params=pltpu.CompilerParams(vmem_limit_bytes=32 * 2**20),
        cost_estimate=pl.CostEstimate(flops=flops, bytes_accessed=moved, transcendentals=exps),
        name=name,
    )


def norm_kernel(source_ref, out_ref):
    source = source_ref[...].astype(F32)
    inverse = lax.rsqrt(jnp.mean(source * source, axis=-1, keepdims=True) + NORM_EPS)
    normed = (source * inverse).astype(BF16)
    for copy in range(out_ref.shape[0]):
        out_ref[copy] = normed


def project_kernel(core_ref, mine_ref, other_ref, w_ref, q_ref, kv_ref, rims_ref, normed_rims_ref):
    core = core_ref[0]
    block = mine_ref.shape[1]
    for rows_ref, owner in ((mine_ref, core), (other_ref, 1 - core)):
        for quad in range(QUAD):
            rows = rows_ref[quad]
            projected = jnp.dot(rows, w_ref[...], preferred_element_type=F32).astype(BF16)
            at = pl.ds(pl.multiple_of((quad * CORES + owner) * block, block), block)
            q_ref[at, :] = projected[:, :COLS]
            kv_ref[at, :] = projected[:, COLS:]
            if quad == 0:

                @pl.when(owner == 0)
                def _():
                    rims_ref[0] = projected[:RIM, COLS:]
                    normed_rims_ref[0] = rows[:RIM]

            if quad == QUAD - 1:

                @pl.when(owner == CORES - 1)
                def _():
                    rims_ref[1] = projected[block - RIM :, COLS:]
                    normed_rims_ref[1] = rows[block - RIM :]


def by_head(rows):
    lane = lax.broadcasted_iota(jnp.int32, rows.shape, 1)
    zero = jnp.zeros_like(rows)
    return jnp.concatenate(
        [jnp.where(lane < HEAD, rows, zero), jnp.where(lane < HEAD, zero, rows)], axis=0
    )


def tile_keys(slots_ref, first, tile, last_tile, kv):
    lane = lax.broadcasted_iota(jnp.int32, (1, K_NB * TILE), 1)
    usable = jnp.zeros((1, K_NB * TILE), jnp.int32)
    places, keys, values = [], [], []
    for slot in range(K_NB):
        at = slots_ref[tile, slot]
        usable = jnp.where(lane // TILE == slot, (at >= 0).astype(jnp.int32), usable)
        place = jnp.clip(at - first + RADIUS, 0, last_tile) * TILE
        place = pl.multiple_of(place, TILE)
        places.append(place)
        keys.append(kv[pl.ds(place, TILE), :COLS])
        values.append(kv[pl.ds(place, TILE), COLS:])
    return places, usable > 0, jnp.concatenate(keys, axis=0), jnp.concatenate(values, axis=0)


def probabilities(queries, keys, usable):
    scores = lax.dot_general(queries, keys, OVER_COLUMNS, preferred_element_type=F32) * (HEAD**-0.5)
    scores = jnp.where(usable, scores, MASKED)
    raised = jnp.exp(scores - jnp.max(scores, axis=-1, keepdims=True))
    return raised * (1.0 / jnp.sum(raised, axis=-1, keepdims=True))


def fill(kv, low_ref, own_ref, high_ref):
    rows = own_ref.shape[0]
    kv[0:RIM, :] = low_ref[...]
    kv[RIM : RIM + rows, :] = own_ref[...]
    kv[RIM + rows : 2 * RIM + rows, :] = high_ref[...]


def forward_kernel(where_ref, slots_ref, q_ref, low_ref, own_ref, high_ref, out_ref, kv):
    tiles = q_ref.shape[0] // TILE
    last_tile = tiles + 2 * RADIUS - 1
    fill(kv, low_ref, own_ref, high_ref)

    def step(tile, carry):
        rows = pl.ds(pl.multiple_of(tile * TILE, TILE), TILE)
        _, usable, keys, values = tile_keys(slots_ref, where_ref[1], tile, last_tile, kv)
        probs = probabilities(by_head(q_ref[rows, :]), keys, usable)
        both = jnp.dot(probs.astype(BF16), values, preferred_element_type=F32)
        lane = lax.broadcasted_iota(jnp.int32, (TILE, COLS), 1)
        out_ref[rows, :] = jnp.where(lane < HEAD, both[:TILE], both[TILE:]).astype(BF16)
        return carry

    lax.fori_loop(0, tiles, step, 0, unroll=4)


def backward_kernel(
    where_ref, slots_ref, q_ref, low_ref, own_ref, high_ref, g_ref, out_ref, kv, total
):
    tiles = q_ref.shape[0] // TILE
    last_tile = tiles + 2 * RADIUS - 1
    fill(kv, low_ref, own_ref, high_ref)
    total[...] = jnp.zeros_like(total)

    def step(tile, carry):
        rows = pl.ds(pl.multiple_of(tile * TILE, TILE), TILE)
        places, usable, keys, values = tile_keys(slots_ref, where_ref[1], tile, last_tile, kv)
        queries = by_head(q_ref[rows, :])
        grads = by_head(g_ref[rows, :])
        probs = probabilities(queries, keys, usable)
        grad_probs = lax.dot_general(grads, values, OVER_COLUMNS, preferred_element_type=F32)
        row_delta = jnp.sum(probs * grad_probs, axis=-1, keepdims=True)
        grad_scores = (probs * (grad_probs - row_delta) * (HEAD**-0.5)).astype(BF16)
        key_grad = lax.dot_general(grad_scores, queries, OVER_ROWS, preferred_element_type=F32)
        value_grad = lax.dot_general(
            probs.astype(BF16), grads, OVER_ROWS, preferred_element_type=F32
        )
        key_grad = key_grad.astype(BF16).astype(F32)
        value_grad = value_grad.astype(BF16).astype(F32)
        for slot in range(K_NB):
            part = slice(slot * TILE, (slot + 1) * TILE)
            total[pl.ds(places[slot], TILE), :COLS] += key_grad[part]
            total[pl.ds(places[slot], TILE), COLS:] += value_grad[part]
        return carry

    lax.fori_loop(0, tiles, step, 0, unroll=2)

    core = where_ref[0]
    rows = q_ref.shape[0]
    block = rows // GROUP

    def split(to, place, count):
        both = total[pl.ds(place, count), :]
        high = both.astype(BF16)
        out_ref[to : to + count, : 2 * COLS] = high
        out_ref[to : to + count, 2 * COLS :] = (both - high.astype(F32)).astype(BF16)

    for at, owner in ((0, core), (QUAD, 1 - core)):
        for quad in range(QUAD):
            place = pl.multiple_of((quad * CORES + owner) * block + RIM, RIM)
            split((at + quad) * block, place, block)
    split(rows, 0, RIM)
    split(rows + RIM, rows + RIM, RIM)


def slope(spread):
    return spread * lax.rsqrt(spread * spread + SOFT_WIDTH)


def mix_kernel(att_ref, source_ref, packed_ref, truth_ref, factor_ref, pred_ref, grad_ref, w, a):
    group, halves, block, _ = packed_ref.shape
    members_num, part, _ = source_ref.shape
    for g in range(group):
        for half in range(halves):
            at = (half * group + g) * block
            w[at : at + block, :] = packed_ref[g, half]
        for m in range(members_num):
            a[m * part : (m + 1) * part, g * COLS : (g + 1) * COLS] = att_ref[g * members_num + m]
    mix, readout = w[:, :LATENT_DIM], w[:, LATENT_DIM:]
    rows = members_num * part
    source = source_ref[...].reshape(rows, LATENT_DIM).astype(F32)
    hidden = source + jnp.dot(a[...], mix, preferred_element_type=F32)
    inverse = lax.rsqrt(jnp.mean(hidden * hidden, axis=-1, keepdims=True) + NORM_EPS)
    decoded = (hidden * inverse).astype(BF16)
    prediction = lax.dot_general(
        readout, decoded, (((0,), (1,)), ((), ())), preferred_element_type=F32
    )
    pred_ref[...] = prediction[:FIELD_NUM]
    spread = jnp.zeros_like(prediction)
    for other in range(1, members_num):
        spread = spread + slope(prediction - pltpu.roll(prediction, other * part, 1))
    derivative = factor_ref[...] / FIELD_NUM * (
        slope(prediction - truth_ref[...]) - spread / (members_num - 1)
    )
    grad_decoded = lax.dot_general(
        derivative.astype(BF16), readout, (((0,), (1,)), ((), ())), preferred_element_type=F32
    )
    grad_hidden = inverse * grad_decoded - hidden * inverse**3 * jnp.mean(
        grad_decoded * hidden, axis=-1, keepdims=True
    )
    grads = lax.dot_general(
        grad_hidden.astype(BF16), mix, OVER_COLUMNS, preferred_element_type=F32
    ).astype(BF16)
    for g in range(group):
        for m in range(members_num):
            grad_ref[g * members_num + m] = grads[
                m * part : (m + 1) * part, g * COLS : (g + 1) * COLS
            ]


def product_kernel(mine_ref, other_ref, rims_ref, kv_ref, out_ref):
    def term(rows, at):
        both = lax.dot_general(
            rows, kv_ref[at : at + rows.shape[0], :], OVER_ROWS, preferred_element_type=F32
        )
        return both[:, : 2 * COLS] + both[:, 2 * COLS :]

    count = mine_ref.shape[0] * mine_ref.shape[1]
    total = term(mine_ref[...].reshape(count, LATENT_DIM), 0)
    total += term(other_ref[...].reshape(count, LATENT_DIM), count)
    total += term(rims_ref[...].reshape(2 * RIM, LATENT_DIM), 2 * count)
    out_ref[...] = total.astype(BF16)


def exchange(chunks, axes):
    return lax.all_to_all(chunks, axes, 0, 0)


def body(members, w_attn, w_mix, readout_matrix, observed_truth, cell_surface_factor, neighbours):
    halves, members_num = lax.axis_size("half"), lax.axis_size("ens")
    everyone = ("half", "quad", "core", "ens")
    shard = w_attn.shape[0]
    node_rows = members.shape[1]
    rows = GROUP * node_rows
    part = node_rows // members_num
    tiles = rows // TILE
    up = [(i, i + 1) for i in range(halves - 1)]
    down = [(target, source) for source, target in up]
    core, ens = lax.axis_index("core"), lax.axis_index("ens")
    where = jnp.stack([core, lax.axis_index("half") * tiles]).astype(jnp.int32)

    (normed,) = call(
        norm_kernel, "norm", [((QUAD, node_rows, LATENT_DIM), BF16)], "v", flops=10, moved=2**20
    )(members.reshape(node_rows, LATENT_DIM))
    mine = exchange(normed, "quad")
    other = lax.ppermute(mine, "core", [(i, (i + 1) % CORES) for i in range(CORES)])

    columns = w_attn.reshape(shard, 3, GROUP, COLS).transpose(2, 0, 1, 3)
    columns = columns.reshape(1, GROUP, 1, shard, 3 * COLS)
    columns = jnp.broadcast_to(columns, (halves, GROUP, members_num, shard, 3 * COLS))
    columns = exchange(columns.reshape(-1, shard, 3 * COLS), everyone)
    columns = columns.reshape(LATENT_DIM, 3 * COLS)

    packed = jnp.concatenate(
        [w_mix, jnp.pad(readout_matrix, ((0, 0), (0, FIELD_PAD - FIELD_NUM)))], axis=1
    )
    width = packed.shape[1]
    packed = jnp.broadcast_to(packed, (halves * members_num, shard, width))
    packed = exchange(packed, ("half", "ens"))
    packed = lax.all_gather(packed, ("quad", "core"), axis=0)
    packed = packed.reshape(GROUP, halves, members_num * shard, width)

    slots = exchange(jnp.broadcast_to(neighbours, (GROUP,) + neighbours.shape), ("quad", "core"))
    slots = slots.reshape(tiles, K_NB)
    sources = exchange(members.reshape(members_num, part, LATENT_DIM), "ens")
    truth = lax.dynamic_slice_in_dim(observed_truth, ens * part, part, 1)
    truth = jnp.tile(jnp.pad(truth, ((0, FIELD_PAD - FIELD_NUM), (0, 0))), (1, members_num))
    factor = lax.dynamic_slice_in_dim(cell_surface_factor, ens * part, part, 0)
    factor = jnp.tile(factor[None], (1, members_num))

    queries, own, rims, normed_rims = call(
        project_kernel,
        "project",
        [
            ((rows, COLS), BF16),
            ((rows, 2 * COLS), BF16),
            ((2, RIM, 2 * COLS), BF16),
            ((2, RIM, LATENT_DIM), BF16),
        ],
        "svvv",
        flops=rows * LATENT_DIM * 6 * COLS,
        moved=4 * 2**20,
    )(where, mine, other, columns)
    low = lax.ppermute(rims[1], "half", up)
    high = lax.ppermute(rims[0], "half", down)
    normed_low = lax.ppermute(normed_rims[1], "half", up)
    normed_high = lax.ppermute(normed_rims[0], "half", down)

    (outcome,) = call(
        forward_kernel,
        "attention_forward",
        [((rows, COLS), BF16)],
        "ssvvvv",
        [((rows + 2 * RIM, 2 * COLS), BF16)],
        flops=rows * COLS * 2048,
        moved=2**21,
        exps=rows * 512,
    )(where, slots, queries, low, own, high)
    attended = exchange(outcome.reshape(GROUP * members_num, part, COLS), ("quad", "core", "ens"))

    prediction, grads = call(
        mix_kernel,
        "mix_loss_backward",
        [((FIELD_NUM, node_rows), F32), ((GROUP * members_num, part, COLS), BF16)],
        "vvvvv",
        [((LATENT_DIM, width), BF16), ((node_rows, LATENT_DIM), BF16)],
        flops=node_rows * LATENT_DIM * 4 * width,
        moved=2**22,
    )(attended, sources, packed, truth, factor)
    grads = exchange(grads, ("quad", "core", "ens")).reshape(rows, COLS)

    normed_low, normed_high, grads = lax.optimization_barrier((normed_low, normed_high, grads))
    (kv_grads,) = call(
        backward_kernel,
        "attention_backward",
        [((rows + 2 * RIM, 4 * COLS), BF16)],
        "ssvvvvv",
        [((rows + 2 * RIM, 2 * COLS), BF16), ((rows + 2 * RIM, 2 * COLS), F32)],
        flops=rows * COLS * 5120,
        moved=2**22,
        exps=rows * 512,
    )(where, slots, queries, low, own, high, grads)
    (term,) = call(
        product_kernel,
        "product",
        [((LATENT_DIM, 2 * COLS), BF16)],
        "vvvv",
        flops=(rows + 2 * RIM) * LATENT_DIM * 8 * COLS,
        moved=2**22,
    )(mine, other, jnp.stack([normed_low, normed_high]), kv_grads)
    term = exchange(term.reshape(-1, shard, 2 * COLS), everyone)
    term = term.reshape(halves, GROUP, members_num, shard, 2, COLS).astype(F32)
    grad_kv = jnp.sum(term, axis=(0, 2)).transpose(1, 2, 0, 3).reshape(shard, 2 * LATENT_DIM)

    prediction = prediction.reshape(FIELD_NUM, members_num, part).transpose(1, 0, 2)
    prediction = exchange(prediction, "ens").transpose(1, 0, 2).reshape(1, FIELD_NUM, node_rows)
    return (prediction, grad_kv)


def solution(mesh):
    space, ens = mesh.shape["space"], mesh.shape["ens"]
    split = Mesh(
        mesh.devices.reshape(space // GROUP, QUAD, CORES, ens), ("half", "quad", "core", "ens")
    )
    nodes = ("half", "quad", "core")
    shards = nodes + ("ens",)
    in_specs = (
        P("ens", nodes, None),
        P(shards, None),
        P(shards, None),
        P(shards, None),
        P(None, nodes),
        P(nodes),
        P(nodes, None),
    )
    out_specs = (P("ens", None, nodes), P(shards, None))
    return jax.shard_map(body, mesh=split, in_specs=in_specs, out_specs=out_specs, check_vma=False)
```

```python
import functools

import jax
import jax.numpy as jnp
from jax import lax
from jax.experimental import pallas as pl
from jax.experimental.pallas import tpu as pltpu
from jax.sharding import Mesh
from jax.sharding import PartitionSpec as P

LATENT_DIM = 1024
HEADS = 16
HEAD = 64
FIELD_NUM = 100
TILE = 64
RADIUS = 2
K_NB = 4
QUAD = 4
CORES = 2
GROUP = QUAD * CORES
COLS = LATENT_DIM // GROUP
RIM = RADIUS * TILE
FIELD_PAD = 128
PAIR = 2
WINDOW = (PAIR + 2 * RADIUS) * TILE
NOWHERE = 100

NORM_EPS = 1e-06
SOFT_WIDTH = 0.0625
MASKED = -1e30

F32 = jnp.float32
BF16 = jnp.bfloat16

VMEM = pl.BlockSpec(memory_space=pltpu.VMEM)
SMEM = pl.BlockSpec(memory_space=pltpu.SMEM)
OVER_ROWS = (((0,), (0,)), ((), ()))
OVER_COLUMNS = (((1,), (1,)), ((), ()))


def call(kernel, name, outs, ins, scratch=(), flops=0, moved=0, exps=0):
    return pl.pallas_call(
        kernel,
        out_shape=[jax.ShapeDtypeStruct(shape, kind) for shape, kind in outs],
        in_specs=[SMEM if space == "s" else VMEM for space in ins],
        out_specs=[VMEM] * len(outs),
        scratch_shapes=[pltpu.VMEM(shape, kind) for shape, kind in scratch],
        compiler_params=pltpu.CompilerParams(vmem_limit_bytes=32 * 2**20),
        cost_estimate=pl.CostEstimate(flops=flops, bytes_accessed=moved, transcendentals=exps),
        name=name,
    )


def norm_kernel(source_ref, out_ref):
    source = source_ref[...].astype(F32)
    inverse = lax.rsqrt(jnp.mean(source * source, axis=-1, keepdims=True) + NORM_EPS)
    out_ref[...] = (source * inverse).astype(BF16)


def owners(where_ref):
    core, quad = where_ref[0], where_ref[1]
    return [(quad ^ step) * CORES + (core ^ flip) for flip in range(CORES) for step in range(QUAD)]


def project_kernel(where_ref, *refs):
    blocks, (w_ref, q_ref, kv_ref, rims_ref, normed_rims_ref) = refs[:GROUP], refs[GROUP:]
    block = blocks[0].shape[0]
    for rows_ref, owner in zip(blocks, owners(where_ref)):
        projected = jnp.dot(rows_ref[...], w_ref[...], preferred_element_type=F32).astype(BF16)
        at = pl.ds(pl.multiple_of(owner * block, block), block)
        q_ref[at, :] = projected[:, :COLS]
        kv_ref[at, :] = projected[:, COLS:]

        @pl.when(owner == 0)
        def _():
            rims_ref[0] = projected[:RIM, COLS:]
            normed_rims_ref[0] = rows_ref[:RIM, :]

        @pl.when(owner == GROUP - 1)
        def _():
            rims_ref[1] = projected[block - RIM :, COLS:]
            normed_rims_ref[1] = rows_ref[block - RIM :, :]


def by_head(rows):
    lane = lax.broadcasted_iota(jnp.int32, rows.shape, 1)
    zero = jnp.zeros_like(rows)
    return jnp.concatenate(
        [jnp.where(lane < HEAD, rows, zero), jnp.where(lane < HEAD, zero, rows)], axis=0
    )


def usable_keys(steps_ref, pair):
    lane = lax.broadcasted_iota(jnp.int32, (1, WINDOW), 1) // TILE - RADIUS
    masks = []
    for query_tile in range(PAIR):
        found = jnp.zeros((1, WINDOW), jnp.int32)
        for slot in range(K_NB):
            step = steps_ref[pair, query_tile : query_tile + 1, slot : slot + 1]
            found = jnp.where(lane - query_tile == step, 1, found)
        masks.append(found)
    row = lax.broadcasted_iota(jnp.int32, (2 * PAIR * TILE, 1), 0) // TILE % PAIR
    return jnp.where(row == 0, masks[0], masks[1]) > 0


def probabilities(queries, keys, usable):
    scores = lax.dot_general(queries, keys, OVER_COLUMNS, preferred_element_type=F32) * (HEAD**-0.5)
    scores = jnp.where(usable, scores, MASKED)
    raised = jnp.exp(scores - jnp.max(scores, axis=-1, keepdims=True))
    return raised * (1.0 / jnp.sum(raised, axis=-1, keepdims=True))


def attend(steps_ref, pair, queries, keys, values):
    probs = probabilities(by_head(queries), keys, usable_keys(steps_ref, pair))
    both = jnp.dot(probs.astype(BF16), values, preferred_element_type=F32)
    lane = lax.broadcasted_iota(jnp.int32, queries.shape, 1)
    half = PAIR * TILE
    return jnp.where(lane < HEAD, both[:half], both[half:]).astype(BF16)


def interior_kernel(steps_ref, q_ref, kv_ref, out_ref):
    step = PAIR * TILE
    pairs = q_ref.shape[0] // step
    for pair in range(1, pairs - 1):
        window = slice((pair - 1) * step, (pair + 2) * step)
        rows = slice(pair * step, (pair + 1) * step)
        out_ref[rows, :] = attend(
            steps_ref, pair, q_ref[rows, :], kv_ref[window, :COLS], kv_ref[window, COLS:]
        )


def edge_kernel(steps_ref, q_ref, kv_ref, low_ref, high_ref, done_ref, out_ref):
    step = PAIR * TILE
    count = q_ref.shape[0]
    pairs = count // step
    out_ref[step : count - step, :] = done_ref[step : count - step, :]
    first = jnp.concatenate([low_ref[...], kv_ref[: 2 * step, :]], axis=0)
    last = jnp.concatenate([kv_ref[count - 2 * step :, :], high_ref[...]], axis=0)
    for pair, window in ((0, first), (pairs - 1, last)):
        rows = slice(pair * step, (pair + 1) * step)
        out_ref[rows, :] = attend(
            steps_ref, pair, q_ref[rows, :], window[:, :COLS], window[:, COLS:]
        )


def backward_kernel(steps_ref, q_ref, low_ref, own_ref, high_ref, g_ref, out_ref, kv, total):
    count = q_ref.shape[0]
    step = PAIR * TILE
    kv[0:RIM, :] = low_ref[...]
    kv[RIM : RIM + count, :] = own_ref[...]
    kv[RIM + count : 2 * RIM + count, :] = high_ref[...]
    total[...] = jnp.zeros_like(total)
    for pair in range(count // step):
        rows = slice(pair * step, (pair + 1) * step)
        window = slice(pair * step, pair * step + WINDOW)
        keys, values = kv[window, :COLS], kv[window, COLS:]
        queries, grads = by_head(q_ref[rows, :]), by_head(g_ref[rows, :])
        probs = probabilities(queries, keys, usable_keys(steps_ref, pair))
        grad_probs = lax.dot_general(grads, values, OVER_COLUMNS, preferred_element_type=F32)
        row_delta = jnp.sum(probs * grad_probs, axis=-1, keepdims=True)
        grad_scores = (probs * (grad_probs - row_delta) * (HEAD**-0.5)).astype(BF16)
        total[window, :COLS] += lax.dot_general(
            grad_scores, queries, OVER_ROWS, preferred_element_type=F32
        )
        total[window, COLS:] += lax.dot_general(
            probs.astype(BF16), grads, OVER_ROWS, preferred_element_type=F32
        )
    both = total[...]
    high = both.astype(BF16)
    out_ref[:, : 2 * COLS] = high
    out_ref[:, 2 * COLS :] = (both - high.astype(F32)).astype(BF16)


def slope(spread):
    return spread * lax.rsqrt(spread * spread + SOFT_WIDTH)


def mix_kernel(where_ref, att_ref, source_ref, *refs):
    pieces = refs[:GROUP]
    truth_ref, factor_ref, pred_ref, grad_ref, w, a = refs[GROUP:]
    halves, block, _ = pieces[0].shape
    members_num, part, _ = source_ref.shape
    for piece, owner in zip(pieces, owners(where_ref)):
        for half in range(halves):
            at = pl.multiple_of((half * GROUP + owner) * block, block)
            w[pl.ds(at, block), :] = piece[half]
    for g in range(GROUP):
        for m in range(members_num):
            a[m * part : (m + 1) * part, g * COLS : (g + 1) * COLS] = att_ref[g * members_num + m]
    mix, readout = w[:, :LATENT_DIM], w[:, LATENT_DIM:]
    rows = members_num * part
    source = source_ref[...].reshape(rows, LATENT_DIM).astype(F32)
    hidden = source + jnp.dot(a[...], mix, preferred_element_type=F32)
    inverse = lax.rsqrt(jnp.mean(hidden * hidden, axis=-1, keepdims=True) + NORM_EPS)
    decoded = (hidden * inverse).astype(BF16)
    prediction = lax.dot_general(
        readout, decoded, (((0,), (1,)), ((), ())), preferred_element_type=F32
    )
    pred_ref[...] = prediction[:FIELD_NUM]
    spread = jnp.zeros_like(prediction)
    for other in range(1, members_num):
        spread = spread + slope(prediction - pltpu.roll(prediction, other * part, 1))
    derivative = factor_ref[...] / FIELD_NUM * (
        slope(prediction - truth_ref[...]) - spread / (members_num - 1)
    )
    grad_decoded = lax.dot_general(
        derivative.astype(BF16), readout, (((0,), (1,)), ((), ())), preferred_element_type=F32
    )
    grad_hidden = inverse * grad_decoded - hidden * inverse**3 * jnp.mean(
        grad_decoded * hidden, axis=-1, keepdims=True
    )
    grads = lax.dot_general(
        grad_hidden.astype(BF16), mix, OVER_COLUMNS, preferred_element_type=F32
    ).astype(BF16)
    for g in range(GROUP):
        for m in range(members_num):
            grad_ref[g * members_num + m] = grads[
                m * part : (m + 1) * part, g * COLS : (g + 1) * COLS
            ]


def product_kernel(where_ref, *refs):
    blocks, (low_ref, high_ref, kv_ref, out_ref) = refs[:GROUP], refs[GROUP:]
    places = [(owner + 1) * RIM for owner in owners(where_ref)]
    places += [0, (GROUP + 1) * RIM]
    blocks = list(blocks) + [low_ref, high_ref]
    total = None
    for at in range(0, len(blocks), 2):
        rows = jnp.concatenate([blocks[at][...], blocks[at + 1][...]], axis=0)
        kv = jnp.concatenate(
            [kv_ref[pl.ds(pl.multiple_of(place, RIM), RIM), :] for place in places[at : at + 2]], axis=0
        )
        both = lax.dot_general(rows, kv, OVER_ROWS, preferred_element_type=F32)
        term = both[:, : 2 * COLS] + both[:, 2 * COLS :]
        total = term if total is None else total + term
    out_ref[...] = total.astype(BF16)


def exchange(chunks, axes):
    return lax.all_to_all(chunks, axes, 0, 0)


def swap(value, axis, step):
    return lax.ppermute(value, axis, [(i, i ^ step) for i in range(lax.axis_size(axis))])


def in_order(mine, axis, at):
    if lax.axis_size(axis) != 2:
        return lax.all_gather(mine, axis, axis=at)
    other = swap(mine, axis, 1)
    first = lax.axis_index(axis) == 0
    return jnp.stack([jnp.where(first, mine, other), jnp.where(first, other, mine)], axis=at)


def group_pieces(mine):
    near = [mine] + [swap(mine, "quad", step) for step in range(1, QUAD)]
    return near, [swap(piece, "core", 1) for piece in near]


def body(members, w_attn, w_mix, readout_matrix, observed_truth, cell_surface_factor, neighbours):
    halves, members_num = lax.axis_size("half"), lax.axis_size("ens")
    everyone = ("half", "quad", "core", "ens")
    shard = w_attn.shape[0]
    node_rows = members.shape[1]
    rows = GROUP * node_rows
    part = node_rows // members_num
    up = [(i, i + 1) for i in range(halves - 1)]
    down = [(target, source) for source, target in up]
    core, quad, ens = (lax.axis_index(axis) for axis in ("core", "quad", "ens"))
    where = jnp.stack([core, quad]).astype(jnp.int32)

    (normed,) = call(
        norm_kernel, "norm", [((node_rows, LATENT_DIM), BF16)], "v", flops=10, moved=2**20
    )(members.reshape(node_rows, LATENT_DIM))
    near, far = group_pieces(normed)
    blocks = near + far

    columns = w_attn.reshape(shard, 3, GROUP, COLS).transpose(2, 0, 1, 3)
    columns = columns.reshape(1, GROUP, 1, shard, 3 * COLS)
    columns = jnp.broadcast_to(columns, (halves, GROUP, members_num, shard, 3 * COLS))
    columns = exchange(columns.reshape(-1, shard, 3 * COLS), everyone)
    columns = columns.reshape(LATENT_DIM, 3 * COLS)

    local_tiles = neighbours.shape[0]
    first_tile = lax.axis_index(("half", "quad", "core")) * local_tiles
    steps = neighbours - first_tile - jnp.arange(local_tiles, dtype=jnp.int32)[:, None]
    steps = jnp.where(neighbours >= 0, steps, NOWHERE)
    steps = jnp.pad(steps, ((0, 8 - local_tiles), (0, 128 - K_NB)))
    steps = lax.all_gather(steps, ("quad", "core"), axis=0)

    packed = jnp.concatenate(
        [w_mix, jnp.pad(readout_matrix, ((0, 0), (0, FIELD_PAD - FIELD_NUM)))], axis=1
    )
    width = packed.shape[1]
    packed = in_order(packed, "half", 0)
    packed = in_order(packed, "ens", 1).reshape(halves, members_num * shard, width)
    packed, near[3] = lax.optimization_barrier((packed, near[3]))
    mix_near, mix_far = group_pieces(packed)

    sources = members.reshape(members_num, part, LATENT_DIM)
    if members_num == 2:
        kept = lax.dynamic_index_in_dim(sources, ens, 0, keepdims=False)
        sent = swap(lax.dynamic_index_in_dim(sources, 1 - ens, 0, keepdims=False), "ens", 1)
        sources = jnp.stack([jnp.where(ens == 0, kept, sent), jnp.where(ens == 0, sent, kept)])
    else:
        sources = exchange(sources, "ens")
    truth = lax.dynamic_slice_in_dim(observed_truth, ens * part, part, 1)
    truth = jnp.tile(jnp.pad(truth, ((0, FIELD_PAD - FIELD_NUM), (0, 0))), (1, members_num))
    factor = lax.dynamic_slice_in_dim(cell_surface_factor, ens * part, part, 0)
    factor = jnp.tile(factor[None], (1, members_num))

    queries, own, rims, normed_rims = call(
        project_kernel,
        "project",
        [
            ((rows, COLS), BF16),
            ((rows, 2 * COLS), BF16),
            ((2, RIM, 2 * COLS), BF16),
            ((2, RIM, LATENT_DIM), BF16),
        ],
        "s" + "v" * (GROUP + 1),
        flops=rows * LATENT_DIM * 6 * COLS,
        moved=4 * 2**20,
    )(where, *blocks, columns)
    low = lax.ppermute(rims[1], "half", up)
    high = lax.ppermute(rims[0], "half", down)

    (outcome,) = call(
        interior_kernel,
        "attention_interior",
        [((rows, COLS), BF16)],
        "vvv",
        flops=rows * COLS * 2048,
        moved=2**21,
        exps=rows * 512,
    )(steps, queries, own)
    (outcome,) = call(
        edge_kernel,
        "attention_edges",
        [((rows, COLS), BF16)],
        "vvvvvv",
        flops=rows * COLS * 512,
        moved=2**20,
        exps=rows * 128,
    )(steps, queries, own, low, high, outcome)
    attended = exchange(outcome.reshape(GROUP * members_num, part, COLS), ("quad", "core", "ens"))
    normed_rims, attended = lax.optimization_barrier((normed_rims, attended))
    normed_low = lax.ppermute(normed_rims[1], "half", up)
    normed_high = lax.ppermute(normed_rims[0], "half", down)

    prediction, grads = call(
        mix_kernel,
        "mix_loss_backward",
        [((FIELD_NUM, node_rows), F32), ((GROUP * members_num, part, COLS), BF16)],
        "s" + "v" * (GROUP + 4),
        [((LATENT_DIM, width), BF16), ((node_rows, LATENT_DIM), BF16)],
        flops=node_rows * LATENT_DIM * 4 * width,
        moved=2**22,
    )(where, attended, sources, *mix_near, *mix_far, truth, factor)
    grads = exchange(grads, ("quad", "core", "ens")).reshape(rows, COLS)

    (kv_grads,) = call(
        backward_kernel,
        "attention_backward",
        [((rows + 2 * RIM, 4 * COLS), BF16)],
        "vvvvvv",
        [((rows + 2 * RIM, 2 * COLS), BF16), ((rows + 2 * RIM, 2 * COLS), F32)],
        flops=rows * COLS * 5120,
        moved=2**22,
        exps=rows * 512,
    )(steps, queries, low, own, high, grads)
    (term,) = call(
        product_kernel,
        "product",
        [((LATENT_DIM, 2 * COLS), BF16)],
        "s" + "v" * (GROUP + 3),
        flops=(rows + 2 * RIM) * LATENT_DIM * 8 * COLS,
        moved=2**22,
    )(where, *blocks, normed_low, normed_high, kv_grads)
    term, prediction = lax.optimization_barrier((term, prediction))
    term = exchange(term.reshape(-1, shard, 2 * COLS), everyone)
    term = term.reshape(halves, GROUP, members_num, shard, 2, COLS).astype(F32)
    grad_kv = jnp.sum(term, axis=(0, 2)).transpose(1, 2, 0, 3).reshape(shard, 2 * LATENT_DIM)

    if members_num == 2:
        got = jnp.roll(swap(prediction, "ens", 1), part, axis=1)
        lane = lax.broadcasted_iota(jnp.int32, prediction.shape, 1)
        prediction = jnp.where(lane // part == ens, prediction, got)
    else:
        prediction = prediction.reshape(FIELD_NUM, members_num, part).transpose(1, 0, 2)
        prediction = exchange(prediction, "ens").transpose(1, 0, 2)
    return (prediction.reshape(1, FIELD_NUM, node_rows), grad_kv)


def solution(mesh):
    space, ens = mesh.shape["space"], mesh.shape["ens"]
    split = Mesh(
        mesh.devices.reshape(space // GROUP, QUAD, CORES, ens), ("half", "quad", "core", "ens")
    )
    nodes = ("half", "quad", "core")
    shards = nodes + ("ens",)
    in_specs = (
        P("ens", nodes, None),
        P(shards, None),
        P(shards, None),
        P(shards, None),
        P(None, nodes),
        P(nodes),
        P(nodes, None),
    )
    out_specs = (P("ens", None, nodes), P(shards, None))
    return jax.shard_map(body, mesh=split, in_specs=in_specs, out_specs=out_specs, check_vma=False)
```

```python
import functools

import jax
import jax.numpy as jnp
from jax import lax
from jax.experimental import pallas as pl
from jax.experimental.pallas import tpu as pltpu
from jax.sharding import Mesh
from jax.sharding import PartitionSpec as P

LATENT_DIM = 1024
HEADS = 16
HEAD = 64
FIELD_NUM = 100
TILE = 64
RADIUS = 2
K_NB = 4
QUAD = 4
CORES = 2
GROUP = QUAD * CORES
COLS = LATENT_DIM // GROUP
RIM = RADIUS * TILE
FIELD_PAD = 128
PAIR = 2
WINDOW = (PAIR + 2 * RADIUS) * TILE
NOWHERE = 100
NOTE_ROWS = 16

NORM_EPS = 1e-06
SOFT_WIDTH = 0.0625
MASKED = -1e30

F32 = jnp.float32
BF16 = jnp.bfloat16

VMEM = pl.BlockSpec(memory_space=pltpu.VMEM)
SMEM = pl.BlockSpec(memory_space=pltpu.SMEM)
OVER_ROWS = (((0,), (0,)), ((), ()))
OVER_COLUMNS = (((1,), (1,)), ((), ()))


def call(kernel, name, outs, ins, scratch=(), flops=0, moved=0, exps=0, room=8):
    return pl.pallas_call(
        kernel,
        out_shape=[jax.ShapeDtypeStruct(shape, kind) for shape, kind in outs],
        in_specs=[SMEM if space == "s" else VMEM for space in ins],
        out_specs=[VMEM] * len(outs),
        scratch_shapes=[pltpu.VMEM(shape, kind) for shape, kind in scratch],
        compiler_params=pltpu.CompilerParams(vmem_limit_bytes=room * 2**20),
        cost_estimate=pl.CostEstimate(flops=flops, bytes_accessed=moved, transcendentals=exps),
        name=name,
    )


def prepare_kernel(
    where_ref, source_ref, w_ref, mix_ref, readout_ref, near_ref, normed_ref, columns_ref, packed_ref
):
    halves, _, members_num = columns_ref.shape[:3]
    for g in range(GROUP):
        chunk = jnp.concatenate(
            [w_ref[:, (part * GROUP + g) * COLS : (part * GROUP + g + 1) * COLS] for part in range(3)],
            axis=1,
        )
        for half in range(halves):
            for m in range(members_num):
                columns_ref[half, g, m] = chunk
    rows = source_ref.shape[0]
    source = source_ref[...].astype(F32)
    inverse = lax.rsqrt(jnp.mean(source * source, axis=-1, keepdims=True) + NORM_EPS)
    normed_ref[:rows, :] = (source * inverse).astype(BF16)
    normed_ref[rows:, :] = jnp.zeros((NOTE_ROWS, LATENT_DIM), BF16)
    row = lax.broadcasted_iota(jnp.int32, (NOTE_ROWS, 128), 0)
    lane = lax.broadcasted_iota(jnp.int32, (NOTE_ROWS, 128), 1)
    note = jnp.zeros((NOTE_ROWS, 128), F32)
    for tile in range(near_ref.shape[0]):
        for slot in range(K_NB):
            at = near_ref[tile, slot]
            step = jnp.where(at >= 0, at - where_ref[2] - tile, NOWHERE).astype(F32)
            note = jnp.where((row == tile) & (lane == slot), step, note)
    normed_ref[rows:, :128] = note.astype(BF16)
    packed_ref[:, :LATENT_DIM] = mix_ref[...]
    packed_ref[:, LATENT_DIM:] = jnp.zeros((packed_ref.shape[0], FIELD_PAD), BF16)
    packed_ref[:, LATENT_DIM : LATENT_DIM + FIELD_NUM] = readout_ref[...]


def owners(where_ref):
    core, quad = where_ref[0], where_ref[1]
    return [(quad ^ step) * CORES + (core ^ flip) for flip in range(CORES) for step in range(QUAD)]


def project_kernel(where_ref, *refs):
    blocks = refs[:GROUP]
    w_ref, normed_ref, q_ref, kv_ref, steps_ref, first_ref, last_ref = refs[GROUP:]
    block = blocks[0].shape[0] - NOTE_ROWS
    for rows_ref, owner in zip(blocks, owners(where_ref)):
        at = pl.ds(pl.multiple_of(owner * block, block), block)
        normed_ref[at, :] = rows_ref[:block, :]
        steps_ref[owner] = rows_ref[block:, :128].astype(F32)
    projected = jnp.dot(normed_ref[...], w_ref[...], preferred_element_type=F32).astype(BF16)
    q_ref[...] = projected[:, :COLS]
    kv_ref[...] = projected[:, COLS:]
    first_ref[...] = projected[:RIM, COLS:]
    last_ref[...] = projected[GROUP * block - RIM :, COLS:]


def by_head(rows):
    lane = lax.broadcasted_iota(jnp.int32, rows.shape, 1)
    zero = jnp.zeros_like(rows)
    return jnp.concatenate(
        [jnp.where(lane < HEAD, rows, zero), jnp.where(lane < HEAD, zero, rows)], axis=0
    )


def usable_keys(steps_ref, pair):
    lane = (lax.broadcasted_iota(jnp.int32, (1, WINDOW), 1) // TILE - RADIUS).astype(F32)
    masks = []
    for query_tile in range(PAIR):
        found = jnp.zeros((1, WINDOW), F32)
        for slot in range(K_NB):
            step = steps_ref[pair, query_tile : query_tile + 1, slot : slot + 1]
            found = jnp.where(lane - query_tile == step, 1.0, found)
        masks.append(found)
    row = lax.broadcasted_iota(jnp.int32, (2 * PAIR * TILE, 1), 0) // TILE % PAIR
    return jnp.where(row == 0, masks[0], masks[1]) > 0


def probabilities(queries, keys, usable):
    scores = lax.dot_general(queries, keys, OVER_COLUMNS, preferred_element_type=F32) * (HEAD**-0.5)
    scores = jnp.where(usable, scores, MASKED)
    raised = jnp.exp(scores - jnp.max(scores, axis=-1, keepdims=True))
    return raised * (1.0 / jnp.sum(raised, axis=-1, keepdims=True))


def attend(steps_ref, pair, queries, keys, values):
    probs = probabilities(by_head(queries), keys, usable_keys(steps_ref, pair))
    both = jnp.dot(probs.astype(BF16), values, preferred_element_type=F32)
    lane = lax.broadcasted_iota(jnp.int32, queries.shape, 1)
    half = PAIR * TILE
    return jnp.where(lane < HEAD, both[:half], both[half:]).astype(BF16)


def interior_kernel(steps_ref, q_ref, kv_ref, out_ref):
    step = PAIR * TILE
    pairs = q_ref.shape[0] // step
    for pair in range(1, pairs - 1):
        window = slice((pair - 1) * step, (pair + 2) * step)
        rows = slice(pair * step, (pair + 1) * step)
        out_ref[rows, :] = attend(
            steps_ref, pair, q_ref[rows, :], kv_ref[window, :COLS], kv_ref[window, COLS:]
        )


def edge_kernel(steps_ref, q_ref, kv_ref, low_ref, high_ref, done_ref, out_ref):
    step = PAIR * TILE
    count = q_ref.shape[0]
    pairs = count // step
    out_ref[step : count - step, :] = done_ref[step : count - step, :]
    first = jnp.concatenate([low_ref[...], kv_ref[: 2 * step, :]], axis=0)
    last = jnp.concatenate([kv_ref[count - 2 * step :, :], high_ref[...]], axis=0)
    for pair, window in ((0, first), (pairs - 1, last)):
        rows = slice(pair * step, (pair + 1) * step)
        out_ref[rows, :] = attend(
            steps_ref, pair, q_ref[rows, :], window[:, :COLS], window[:, COLS:]
        )


def backward_kernel(steps_ref, q_ref, low_ref, own_ref, high_ref, g_ref, out_ref, kv, total):
    count = q_ref.shape[0]
    step = PAIR * TILE
    kv[0:RIM, :] = low_ref[...]
    kv[RIM : RIM + count, :] = own_ref[...]
    kv[RIM + count : 2 * RIM + count, :] = high_ref[...]
    total[...] = jnp.zeros_like(total)
    for pair in range(count // step):
        rows = slice(pair * step, (pair + 1) * step)
        window = slice(pair * step, pair * step + WINDOW)
        keys, values = kv[window, :COLS], kv[window, COLS:]
        queries, grads = by_head(q_ref[rows, :]), by_head(g_ref[rows, :])
        probs = probabilities(queries, keys, usable_keys(steps_ref, pair))
        grad_probs = lax.dot_general(grads, values, OVER_COLUMNS, preferred_element_type=F32)
        row_delta = jnp.sum(probs * grad_probs, axis=-1, keepdims=True)
        grad_scores = (probs * (grad_probs - row_delta) * (HEAD**-0.5)).astype(BF16)
        total[window, :COLS] += lax.dot_general(
            grad_scores, queries, OVER_ROWS, preferred_element_type=F32
        )
        total[window, COLS:] += lax.dot_general(
            probs.astype(BF16), grads, OVER_ROWS, preferred_element_type=F32
        )
    both = total[...]
    high = both.astype(BF16)
    out_ref[:, : 2 * COLS] = high
    out_ref[:, 2 * COLS :] = (both - high.astype(F32)).astype(BF16)


def slope(spread):
    return spread * lax.rsqrt(spread * spread + SOFT_WIDTH)


def mix_kernel(where_ref, att_ref, source_ref, *refs):
    pieces = refs[:GROUP]
    truth_ref, factor_ref, pred_ref, grad_ref, w, a = refs[GROUP:]
    halves, block, _ = pieces[0].shape
    members_num, part, _ = source_ref.shape
    for piece, owner in zip(pieces, owners(where_ref)):
        for half in range(halves):
            at = pl.multiple_of((half * GROUP + owner) * block, block)
            w[pl.ds(at, block), :] = piece[half]
    for g in range(GROUP):
        for m in range(members_num):
            a[m * part : (m + 1) * part, g * COLS : (g + 1) * COLS] = att_ref[g * members_num + m]
    mix, readout = w[:, :LATENT_DIM], w[:, LATENT_DIM:]
    rows = members_num * part
    source = source_ref[...].reshape(rows, LATENT_DIM).astype(F32)
    hidden = source + jnp.dot(a[...], mix, preferred_element_type=F32)
    inverse = lax.rsqrt(jnp.mean(hidden * hidden, axis=-1, keepdims=True) + NORM_EPS)
    decoded = (hidden * inverse).astype(BF16)
    prediction = lax.dot_general(
        readout, decoded, (((0,), (1,)), ((), ())), preferred_element_type=F32
    )
    pred_ref[...] = prediction[:FIELD_NUM]
    spread = jnp.zeros_like(prediction)
    for other in range(1, members_num):
        spread = spread + slope(prediction - pltpu.roll(prediction, other * part, 1))
    derivative = factor_ref[...] / FIELD_NUM * (
        slope(prediction - truth_ref[...]) - spread / (members_num - 1)
    )
    grad_decoded = lax.dot_general(
        derivative.astype(BF16), readout, (((0,), (1,)), ((), ())), preferred_element_type=F32
    )
    grad_hidden = inverse * grad_decoded - hidden * inverse**3 * jnp.mean(
        grad_decoded * hidden, axis=-1, keepdims=True
    )
    grads = lax.dot_general(
        grad_hidden.astype(BF16), mix, OVER_COLUMNS, preferred_element_type=F32
    ).astype(BF16)
    for g in range(GROUP):
        for m in range(members_num):
            grad_ref[g * members_num + m] = grads[
                m * part : (m + 1) * part, g * COLS : (g + 1) * COLS
            ]


def product_kernel(normed_ref, low_ref, high_ref, kv_ref, out_ref):
    def term(rows_ref, at):
        kv = kv_ref[at : at + rows_ref.shape[0], :]
        both = lax.dot_general(rows_ref[...], kv, OVER_ROWS, preferred_element_type=F32)
        return both[:, : 2 * COLS] + both[:, 2 * COLS :]

    count = normed_ref.shape[0]
    total = term(normed_ref, RIM) + term(low_ref, 0) + term(high_ref, RIM + count)
    out_ref[...] = total.astype(BF16)


def gather_kernel(parts_ref, out_ref):
    halves, _, members_num = parts_ref.shape[:3]
    for g in range(GROUP):
        total = None
        for half in range(halves):
            for m in range(members_num):
                part = parts_ref[half, g, m].astype(F32)
                total = part if total is None else total + part
        out_ref[:, g * COLS : (g + 1) * COLS] = total[:, :COLS]
        out_ref[:, LATENT_DIM + g * COLS : LATENT_DIM + (g + 1) * COLS] = total[:, COLS:]


def exchange(chunks, axes):
    return lax.all_to_all(chunks, axes, 0, 0)


def swap(value, axis, step):
    return lax.ppermute(value, axis, [(i, i ^ step) for i in range(lax.axis_size(axis))])


def in_order(mine, axis, at):
    if lax.axis_size(axis) != 2:
        return lax.all_gather(mine, axis, axis=at)
    other = swap(mine, axis, 1)
    first = lax.axis_index(axis) == 0
    return jnp.stack([jnp.where(first, mine, other), jnp.where(first, other, mine)], axis=at)


def group_pieces(mine):
    near = [mine] + [swap(mine, "quad", step) for step in range(1, QUAD)]
    return near, [swap(piece, "core", 1) for piece in near]


def body(members, w_attn, w_mix, readout_matrix, observed_truth, cell_surface_factor, neighbours):
    halves, members_num = lax.axis_size("half"), lax.axis_size("ens")
    everyone = ("half", "quad", "core", "ens")
    shard = w_attn.shape[0]
    node_rows = members.shape[1]
    rows = GROUP * node_rows
    part = node_rows // members_num
    up = [(i, i + 1) for i in range(halves - 1)]
    down = [(target, source) for source, target in up]
    core, quad, ens = (lax.axis_index(axis) for axis in ("core", "quad", "ens"))
    first_tile = lax.axis_index(("half", "quad", "core")) * neighbours.shape[0]
    where = jnp.stack([core, quad, first_tile]).astype(jnp.int32)
    width = LATENT_DIM + FIELD_PAD

    normed, columns, packed = call(
        prepare_kernel,
        "prepare",
        [
            ((node_rows + NOTE_ROWS, LATENT_DIM), BF16),
            ((halves, GROUP, members_num, shard, 3 * COLS), BF16),
            ((shard, width), BF16),
        ],
        "svvvvs",
        flops=2**20,
        moved=2**20,
        room=10,
    )(
        where,
        members.reshape(node_rows, LATENT_DIM),
        w_attn,
        w_mix,
        readout_matrix,
        neighbours,
    )
    columns = exchange(columns.reshape(-1, shard, 3 * COLS), everyone)
    columns = columns.reshape(LATENT_DIM, 3 * COLS)
    near, far = group_pieces(normed)
    blocks = near + far

    packed = in_order(packed, "half", 0)
    packed = in_order(packed, "ens", 1).reshape(halves, members_num * shard, width)
    packed, near[3] = lax.optimization_barrier((packed, near[3]))
    mix_near, mix_far = group_pieces(packed)

    sources = members.reshape(members_num, part, LATENT_DIM)
    if members_num == 2:
        kept = lax.dynamic_index_in_dim(sources, ens, 0, keepdims=False)
        sent = swap(lax.dynamic_index_in_dim(sources, 1 - ens, 0, keepdims=False), "ens", 1)
        sources = jnp.stack([jnp.where(ens == 0, kept, sent), jnp.where(ens == 0, sent, kept)])
    else:
        sources = exchange(sources, "ens")
    truth = lax.dynamic_slice_in_dim(observed_truth, ens * part, part, 1)
    truth = jnp.tile(jnp.pad(truth, ((0, FIELD_PAD - FIELD_NUM), (0, 0))), (1, members_num))
    factor = lax.dynamic_slice_in_dim(cell_surface_factor, ens * part, part, 0)
    factor = jnp.tile(factor[None], (1, members_num))

    normed, queries, own, steps, first, last = call(
        project_kernel,
        "project",
        [
            ((rows, LATENT_DIM), BF16),
            ((rows, COLS), BF16),
            ((rows, 2 * COLS), BF16),
            ((GROUP, NOTE_ROWS, 128), F32),
            ((RIM, 2 * COLS), BF16),
            ((RIM, 2 * COLS), BF16),
        ],
        "s" + "v" * (GROUP + 1),
        flops=rows * LATENT_DIM * 6 * COLS,
        moved=4 * 2**20,
        room=14,
    )(where, *blocks, columns)
    low = lax.ppermute(last, "half", up)
    high = lax.ppermute(first, "half", down)

    (outcome,) = call(
        interior_kernel,
        "attention_interior",
        [((rows, COLS), BF16)],
        "vvv",
        flops=rows * COLS * 2048,
        moved=2**21,
        exps=rows * 512,
    )(steps, queries, own)
    (outcome,) = call(
        edge_kernel,
        "attention_edges",
        [((rows, COLS), BF16)],
        "vvvvvv",
        flops=rows * COLS * 512,
        moved=2**20,
        exps=rows * 128,
    )(steps, queries, own, low, high, outcome)
    normed, outcome = lax.optimization_barrier((normed, outcome))
    normed_low = lax.ppermute(normed[rows - RIM :], "half", up)
    normed_high = lax.ppermute(normed[:RIM], "half", down)
    attended = exchange(outcome.reshape(GROUP * members_num, part, COLS), ("quad", "core", "ens"))

    prediction, grads = call(
        mix_kernel,
        "mix_loss_backward",
        [((FIELD_NUM, node_rows), F32), ((GROUP * members_num, part, COLS), BF16)],
        "s" + "v" * (GROUP + 4),
        [((LATENT_DIM, width), BF16), ((node_rows, LATENT_DIM), BF16)],
        flops=node_rows * LATENT_DIM * 4 * width,
        moved=2**22,
        room=14,
    )(where, attended, sources, *mix_near, *mix_far, truth, factor)
    grads = exchange(grads, ("quad", "core", "ens")).reshape(rows, COLS)

    (kv_grads,) = call(
        backward_kernel,
        "attention_backward",
        [((rows + 2 * RIM, 4 * COLS), BF16)],
        "vvvvvv",
        [((rows + 2 * RIM, 2 * COLS), BF16), ((rows + 2 * RIM, 2 * COLS), F32)],
        flops=rows * COLS * 5120,
        moved=2**22,
        exps=rows * 512,
        room=14,
    )(steps, queries, low, own, high, grads)
    (term,) = call(
        product_kernel,
        "product",
        [((LATENT_DIM, 2 * COLS), BF16)],
        "vvvv",
        flops=(rows + 2 * RIM) * LATENT_DIM * 8 * COLS,
        moved=2**22,
        room=16,
    )(normed, normed_low, normed_high, kv_grads)
    term, prediction = lax.optimization_barrier((term, prediction))
    term = exchange(term.reshape(-1, shard, 2 * COLS), everyone)
    (grad_kv,) = call(
        gather_kernel, "gather_sums", [((shard, 2 * LATENT_DIM), F32)], "v", flops=2**17, moved=2**20
    )(term.reshape(halves, GROUP, members_num, shard, 2 * COLS))

    if members_num == 2:
        got = jnp.roll(swap(prediction, "ens", 1), part, axis=1)
        lane = lax.broadcasted_iota(jnp.int32, prediction.shape, 1)
        prediction = jnp.where(lane // part == ens, prediction, got)
    else:
        prediction = prediction.reshape(FIELD_NUM, members_num, part).transpose(1, 0, 2)
        prediction = exchange(prediction, "ens").transpose(1, 0, 2)
    return (prediction.reshape(1, FIELD_NUM, node_rows), grad_kv)


def solution(mesh):
    space, ens = mesh.shape["space"], mesh.shape["ens"]
    split = Mesh(
        mesh.devices.reshape(space // GROUP, QUAD, CORES, ens), ("half", "quad", "core", "ens")
    )
    nodes = ("half", "quad", "core")
    shards = nodes + ("ens",)
    in_specs = (
        P("ens", nodes, None),
        P(shards, None),
        P(shards, None),
        P(shards, None),
        P(None, nodes),
        P(nodes),
        P(nodes, None),
    )
    out_specs = (P("ens", None, nodes), P(shards, None))
    return jax.shard_map(body, mesh=split, in_specs=in_specs, out_specs=out_specs, check_vma=False)
```

```python
import functools

import jax
import jax.numpy as jnp
from jax import lax
from jax.experimental import pallas as pl
from jax.experimental.pallas import tpu as pltpu
from jax.sharding import Mesh
from jax.sharding import PartitionSpec as P

LATENT_DIM = 1024
HEADS = 16
HEAD = 64
FIELD_NUM = 100
TILE = 64
RADIUS = 2
K_NB = 4
QUAD = 4
CORES = 2
GROUP = QUAD * CORES
COLS = LATENT_DIM // GROUP
RIM = RADIUS * TILE
FIELD_PAD = 128
PAIR = 2
WINDOW = (PAIR + 2 * RADIUS) * TILE
NOWHERE = 100
NOTE_ROWS = 16

NORM_EPS = 1e-06
SOFT_WIDTH = 0.0625
MASKED = -1e30

F32 = jnp.float32
BF16 = jnp.bfloat16

VMEM = pl.BlockSpec(memory_space=pltpu.VMEM)
SMEM = pl.BlockSpec(memory_space=pltpu.SMEM)
ANYWHERE = pl.BlockSpec(memory_space=pl.ANY)
OVER_ROWS = (((0,), (0,)), ((), ()))
OVER_COLUMNS = (((1,), (1,)), ((), ()))


def call(kernel, name, outs, ins, scratch=(), flops=0, moved=0, exps=0, room=8, results=None):
    spaces = {"s": SMEM, "v": VMEM, "a": ANYWHERE}
    return pl.pallas_call(
        kernel,
        out_shape=[jax.ShapeDtypeStruct(shape, kind) for shape, kind in outs],
        in_specs=[spaces[space] for space in ins],
        out_specs=[spaces[space] for space in results or "v" * len(outs)],
        scratch_shapes=list(scratch),
        compiler_params=pltpu.CompilerParams(vmem_limit_bytes=room * 2**20),
        cost_estimate=pl.CostEstimate(flops=flops, bytes_accessed=moved, transcendentals=exps),
        name=name,
    )


def fetch(pairs, sems):
    copies = [
        pltpu.make_async_copy(source, target, sems.at[at]) for at, (source, target) in enumerate(pairs)
    ]
    for copy in copies:
        copy.start()
    return copies


def prepare_kernel(
    where_ref,
    near_ref,
    source_any,
    w_any,
    mix_any,
    readout_any,
    normed_ref,
    columns_ref,
    packed_ref,
    source_ref,
    w_ref,
    readout_ref,
    sems,
):
    copies = fetch(
        [
            (w_any, w_ref),
            (source_any, source_ref),
            (readout_any, readout_ref),
            (mix_any, packed_ref.at[:, :LATENT_DIM]),
        ],
        sems,
    )
    copies[1].wait()
    rows = source_ref.shape[0]
    source = source_ref[...].astype(F32)
    inverse = lax.rsqrt(jnp.mean(source * source, axis=-1, keepdims=True) + NORM_EPS)
    normed_ref[:rows, :] = (source * inverse).astype(BF16)
    normed_ref[rows:, :] = jnp.zeros((NOTE_ROWS, LATENT_DIM), BF16)
    row = lax.broadcasted_iota(jnp.int32, (NOTE_ROWS, 128), 0)
    lane = lax.broadcasted_iota(jnp.int32, (NOTE_ROWS, 128), 1)
    note = jnp.zeros((NOTE_ROWS, 128), F32)
    for tile in range(near_ref.shape[0]):
        for slot in range(K_NB):
            at = near_ref[tile, slot]
            step = jnp.where(at >= 0, at - where_ref[3] - tile, NOWHERE).astype(F32)
            note = jnp.where((row == tile) & (lane == slot), step, note)
    normed_ref[rows:, :128] = note.astype(BF16)
    copies[0].wait()
    halves, _, members_num = columns_ref.shape[:3]
    for g in range(GROUP):
        chunk = jnp.concatenate(
            [w_ref[:, (part * GROUP + g) * COLS : (part * GROUP + g + 1) * COLS] for part in range(3)],
            axis=1,
        )
        for half in range(halves):
            for m in range(members_num):
                columns_ref[half, g, m] = chunk
    copies[2].wait()
    packed_ref[:, LATENT_DIM:] = jnp.zeros((packed_ref.shape[0], FIELD_PAD), BF16)
    packed_ref[:, LATENT_DIM : LATENT_DIM + FIELD_NUM] = readout_ref[...]
    copies[3].wait()


def owners(where_ref):
    core, quad = where_ref[0], where_ref[1]
    return [(quad ^ step) * CORES + (core ^ flip) for flip in range(CORES) for step in range(QUAD)]


def project_kernel(where_ref, *refs):
    blocks, refs = refs[:GROUP], refs[GROUP:]
    columns, refs = refs[:-12], refs[-12:]
    q_ref, kv_ref, steps_ref, first_ref, last_ref, first_n_ref, last_n_ref, normed_any = refs[:8]
    notes, normed, w, sems = refs[8:]
    block = blocks[0].shape[0] - NOTE_ROWS
    pairs = []
    for at, (rows_ref, owner) in enumerate(zip(blocks, owners(where_ref))):
        place = pl.ds(pl.multiple_of(owner * block, block), block)
        pairs.append((rows_ref.at[:block], normed.at[place]))
        pairs.append((rows_ref.at[block:, :128], notes.at[owner]))
    if len(columns) == 1:
        pairs.append((columns[0], w))
    else:
        for step, part in enumerate(columns):
            count, shard, _ = part.shape
            for at in range(count):
                place = pl.multiple_of((at * 2 + (where_ref[2] ^ step)) * shard, shard)
                pairs.append((part.at[at], w.at[pl.ds(place, shard)]))
    copies = fetch(pairs, sems)
    for copy in copies:
        copy.wait()
    keep = pltpu.make_async_copy(normed, normed_any, sems.at[0])
    keep.start()
    projected = jnp.dot(normed[...], w[...], preferred_element_type=F32).astype(BF16)
    q_ref[...] = projected[:, :COLS]
    kv_ref[...] = projected[:, COLS:]
    last = GROUP * block - RIM
    first_ref[...] = projected[:RIM, COLS:]
    last_ref[...] = projected[last:, COLS:]
    first_n_ref[...] = normed[:RIM, :]
    last_n_ref[...] = normed[last:, :]
    steps_ref[...] = notes[...].astype(F32)
    keep.wait()


def weights_kernel(where_ref, *refs):
    pieces, (w_ref, sems) = refs[:-2], refs[-2:]
    pairs = []
    for piece, (first, stride, count, shift) in zip(pieces, placements(where_ref, pieces)):
        halves, block = piece.shape[-3], piece.shape[-2]
        for at in range(count):
            for half in range(halves):
                owner = (where_ref[1] ^ (first + at)) * CORES + (where_ref[0] ^ shift[0])
                place = (half * GROUP + owner) * stride + shift[1]
                source = piece.at[at, half] if len(piece.shape) == 4 else piece.at[half]
                pairs.append((source, w_ref.at[pl.ds(pl.multiple_of(place, block), block)]))
    for copy in fetch(pairs, sems):
        copy.wait()


def placements(where_ref, pieces):
    block = pieces[0].shape[-2]
    if len(pieces[0].shape) == 3:
        return [(at % QUAD, block, 1, (at // QUAD, 0)) for at in range(len(pieces))]
    ens = where_ref[2]
    return [(0, 2 * block, QUAD, (at // 2, (ens ^ (at % 2)) * block)) for at in range(len(pieces))]


def by_head(rows):
    lane = lax.broadcasted_iota(jnp.int32, rows.shape, 1)
    zero = jnp.zeros_like(rows)
    return jnp.concatenate(
        [jnp.where(lane < HEAD, rows, zero), jnp.where(lane < HEAD, zero, rows)], axis=0
    )


def usable_keys(steps_ref, pair):
    lane = (lax.broadcasted_iota(jnp.int32, (1, WINDOW), 1) // TILE - RADIUS).astype(F32)
    masks = []
    for query_tile in range(PAIR):
        found = jnp.zeros((1, WINDOW), F32)
        for slot in range(K_NB):
            step = steps_ref[pair, query_tile : query_tile + 1, slot : slot + 1]
            found = jnp.where(lane - query_tile == step, 1.0, found)
        masks.append(found)
    row = lax.broadcasted_iota(jnp.int32, (2 * PAIR * TILE, 1), 0) // TILE % PAIR
    return jnp.where(row == 0, masks[0], masks[1]) > 0


def probabilities(queries, keys, usable):
    scores = lax.dot_general(queries, keys, OVER_COLUMNS, preferred_element_type=F32) * (HEAD**-0.5)
    scores = jnp.where(usable, scores, MASKED)
    raised = jnp.exp(scores - jnp.max(scores, axis=-1, keepdims=True))
    return raised * (1.0 / jnp.sum(raised, axis=-1, keepdims=True))


def attend(steps_ref, pair, queries, keys, values):
    probs = probabilities(by_head(queries), keys, usable_keys(steps_ref, pair))
    both = jnp.dot(probs.astype(BF16), values, preferred_element_type=F32)
    lane = lax.broadcasted_iota(jnp.int32, queries.shape, 1)
    half = PAIR * TILE
    return jnp.where(lane < HEAD, both[:half], both[half:]).astype(BF16)


def interior_kernel(steps_ref, q_ref, kv_ref, out_ref):
    step = PAIR * TILE
    pairs = q_ref.shape[0] // step
    for pair in range(1, pairs - 1):
        window = slice((pair - 1) * step, (pair + 2) * step)
        rows = slice(pair * step, (pair + 1) * step)
        out_ref[rows, :] = attend(
            steps_ref, pair, q_ref[rows, :], kv_ref[window, :COLS], kv_ref[window, COLS:]
        )


def edge_kernel(steps_ref, q_ref, kv_ref, low_ref, high_ref, done_ref, out_ref):
    step = PAIR * TILE
    count = q_ref.shape[0]
    pairs = count // step
    out_ref[step : count - step, :] = done_ref[step : count - step, :]
    first = jnp.concatenate([low_ref[...], kv_ref[: 2 * step, :]], axis=0)
    last = jnp.concatenate([kv_ref[count - 2 * step :, :], high_ref[...]], axis=0)
    for pair, window in ((0, first), (pairs - 1, last)):
        rows = slice(pair * step, (pair + 1) * step)
        out_ref[rows, :] = attend(
            steps_ref, pair, q_ref[rows, :], window[:, :COLS], window[:, COLS:]
        )


def backward_kernel(steps_ref, q_ref, low_ref, own_ref, high_ref, g_ref, out_ref, kv, total):
    count = q_ref.shape[0]
    step = PAIR * TILE
    kv[0:RIM, :] = low_ref[...]
    kv[RIM : RIM + count, :] = own_ref[...]
    kv[RIM + count : 2 * RIM + count, :] = high_ref[...]
    total[...] = jnp.zeros_like(total)
    for pair in range(count // step):
        rows = slice(pair * step, (pair + 1) * step)
        window = slice(pair * step, pair * step + WINDOW)
        keys, values = kv[window, :COLS], kv[window, COLS:]
        queries, grads = by_head(q_ref[rows, :]), by_head(g_ref[rows, :])
        probs = probabilities(queries, keys, usable_keys(steps_ref, pair))
        grad_probs = lax.dot_general(grads, values, OVER_COLUMNS, preferred_element_type=F32)
        row_delta = jnp.sum(probs * grad_probs, axis=-1, keepdims=True)
        grad_scores = (probs * (grad_probs - row_delta) * (HEAD**-0.5)).astype(BF16)
        total[window, :COLS] += lax.dot_general(
            grad_scores, queries, OVER_ROWS, preferred_element_type=F32
        )
        total[window, COLS:] += lax.dot_general(
            probs.astype(BF16), grads, OVER_ROWS, preferred_element_type=F32
        )
    both = total[...]
    high = both.astype(BF16)
    out_ref[:, : 2 * COLS] = high
    out_ref[:, 2 * COLS :] = (both - high.astype(F32)).astype(BF16)


def slope(spread):
    return spread * lax.rsqrt(spread * spread + SOFT_WIDTH)


def mix_kernel(att_ref, source_ref, w, truth_ref, factor_ref, pred_ref, grad_ref, a):
    members_num, part, _ = source_ref.shape
    for g in range(GROUP):
        for m in range(members_num):
            a[m * part : (m + 1) * part, g * COLS : (g + 1) * COLS] = att_ref[g * members_num + m]
    mix, readout = w[:, :LATENT_DIM], w[:, LATENT_DIM:]
    rows = members_num * part
    source = source_ref[...].reshape(rows, LATENT_DIM).astype(F32)
    hidden = source + jnp.dot(a[...], mix, preferred_element_type=F32)
    inverse = lax.rsqrt(jnp.mean(hidden * hidden, axis=-1, keepdims=True) + NORM_EPS)
    decoded = (hidden * inverse).astype(BF16)
    prediction = lax.dot_general(
        readout, decoded, (((0,), (1,)), ((), ())), preferred_element_type=F32
    )
    pred_ref[...] = prediction[:FIELD_NUM]
    spread = jnp.zeros_like(prediction)
    for other in range(1, members_num):
        spread = spread + slope(prediction - pltpu.roll(prediction, other * part, 1))
    derivative = factor_ref[...] / FIELD_NUM * (
        slope(prediction - truth_ref[...]) - spread / (members_num - 1)
    )
    grad_decoded = lax.dot_general(
        derivative.astype(BF16), readout, (((0,), (1,)), ((), ())), preferred_element_type=F32
    )
    grad_hidden = inverse * grad_decoded - hidden * inverse**3 * jnp.mean(
        grad_decoded * hidden, axis=-1, keepdims=True
    )
    grads = lax.dot_general(
        grad_hidden.astype(BF16), mix, OVER_COLUMNS, preferred_element_type=F32
    ).astype(BF16)
    for g in range(GROUP):
        for m in range(members_num):
            grad_ref[g * members_num + m] = grads[
                m * part : (m + 1) * part, g * COLS : (g + 1) * COLS
            ]


def product_kernel(normed_ref, low_ref, high_ref, kv_ref, out_ref):
    def term(rows_ref, at):
        kv = kv_ref[at : at + rows_ref.shape[0], :]
        both = lax.dot_general(rows_ref[...], kv, OVER_ROWS, preferred_element_type=F32)
        return both[:, : 2 * COLS] + both[:, 2 * COLS :]

    count = normed_ref.shape[0]
    total = term(normed_ref, RIM) + term(low_ref, 0) + term(high_ref, RIM + count)
    out_ref[...] = total.astype(BF16)


def gather_kernel(parts_ref, out_ref):
    halves, _, members_num = parts_ref.shape[:3]
    for g in range(GROUP):
        total = None
        for half in range(halves):
            for m in range(members_num):
                part = parts_ref[half, g, m].astype(F32)
                total = part if total is None else total + part
        out_ref[:, g * COLS : (g + 1) * COLS] = total[:, :COLS]
        out_ref[:, LATENT_DIM + g * COLS : LATENT_DIM + (g + 1) * COLS] = total[:, COLS:]


def exchange(chunks, axes):
    return lax.all_to_all(chunks, axes, 0, 0)


def swap(value, axis, step):
    return lax.ppermute(value, axis, [(i, i ^ step) for i in range(lax.axis_size(axis))])


def in_order(mine, axis, at):
    if lax.axis_size(axis) != 2:
        return lax.all_gather(mine, axis, axis=at)
    other = swap(mine, axis, 1)
    first = lax.axis_index(axis) == 0
    return jnp.stack([jnp.where(first, mine, other), jnp.where(first, other, mine)], axis=at)


def body(members, w_attn, w_mix, readout_matrix, observed_truth, cell_surface_factor, neighbours):
    halves, members_num = lax.axis_size("half"), lax.axis_size("ens")
    nodes = ("half", "quad", "core")
    everyone = nodes + ("ens",)
    shard = w_attn.shape[0]
    node_rows = members.shape[1]
    rows = GROUP * node_rows
    part = node_rows // members_num
    up = [(i, i + 1) for i in range(halves - 1)]
    down = [(target, source) for source, target in up]
    core, quad, ens = (lax.axis_index(axis) for axis in ("core", "quad", "ens"))
    first_tile = lax.axis_index(("half", "quad", "core")) * neighbours.shape[0]
    where = jnp.stack([core, quad, ens, first_tile]).astype(jnp.int32)
    width = LATENT_DIM + FIELD_PAD
    paired = members_num == 2
    copies = 1 if paired else members_num

    normed, columns, packed = call(
        prepare_kernel,
        "prepare",
        [
            ((node_rows + NOTE_ROWS, LATENT_DIM), BF16),
            ((halves, GROUP, copies, shard, 3 * COLS), BF16),
            ((shard, width), BF16),
        ],
        "ssaaaa",
        [
            pltpu.VMEM((node_rows, LATENT_DIM), BF16),
            pltpu.VMEM(w_attn.shape, BF16),
            pltpu.VMEM(readout_matrix.shape, BF16),
            pltpu.SemaphoreType.DMA((4,)),
        ],
        flops=2**20,
        moved=2**20,
    )(where, neighbours, members.reshape(node_rows, LATENT_DIM), w_attn, w_mix, readout_matrix)

    packed = in_order(packed, "half", 0)
    near = [normed] + [swap(normed, "quad", step) for step in range(1, QUAD)]
    if paired:
        columns = exchange(columns.reshape(-1, shard, 3 * COLS), nodes)
        columns = [columns, swap(columns, "ens", 1)]
    else:
        columns = [exchange(columns.reshape(-1, shard, 3 * COLS), everyone)]
        columns = [columns[0].reshape(LATENT_DIM, 3 * COLS)]
    far = [swap(piece, "core", 1) for piece in near]

    sources = members.reshape(members_num, part, LATENT_DIM)
    if paired:
        kept = lax.dynamic_index_in_dim(sources, ens, 0, keepdims=False)
        sent = swap(lax.dynamic_index_in_dim(sources, 1 - ens, 0, keepdims=False), "ens", 1)
        sources = jnp.stack([jnp.where(ens == 0, kept, sent), jnp.where(ens == 0, sent, kept)])
    else:
        sources = exchange(sources, "ens")

    packed, near[3] = lax.optimization_barrier((packed, near[3]))
    if paired:
        pieces = jnp.stack([packed] + [swap(packed, "quad", step) for step in range(1, QUAD)])
        pieces, columns[1] = lax.optimization_barrier((pieces, columns[1]))
        pieces = [pieces, swap(pieces, "ens", 1)]
    else:
        packed = in_order(packed, "ens", 1).reshape(halves, members_num * shard, width)
        pieces = [packed] + [swap(packed, "quad", step) for step in range(1, QUAD)]
    pieces = pieces + [swap(piece, "core", 1) for piece in pieces]
    columns[-1], sources = lax.optimization_barrier((columns[-1], sources))

    truth = lax.dynamic_slice_in_dim(observed_truth, ens * part, part, 1)
    truth = jnp.tile(jnp.pad(truth, ((0, FIELD_PAD - FIELD_NUM), (0, 0))), (1, members_num))
    factor = lax.dynamic_slice_in_dim(cell_surface_factor, ens * part, part, 0)
    factor = jnp.tile(factor[None], (1, members_num))

    queries, own, steps, first, last, first_normed, last_normed, normed = call(
        project_kernel,
        "project",
        [
            ((rows, COLS), BF16),
            ((rows, 2 * COLS), BF16),
            ((GROUP, NOTE_ROWS, 128), F32),
            ((RIM, 2 * COLS), BF16),
            ((RIM, 2 * COLS), BF16),
            ((RIM, LATENT_DIM), BF16),
            ((RIM, LATENT_DIM), BF16),
            ((rows, LATENT_DIM), BF16),
        ],
        "s" + "a" * (GROUP + len(columns)),
        [
            pltpu.VMEM((GROUP, NOTE_ROWS, 128), BF16),
            pltpu.VMEM((rows, LATENT_DIM), BF16),
            pltpu.VMEM((LATENT_DIM, 3 * COLS), BF16),
            pltpu.SemaphoreType.DMA((2 * GROUP + (2 * GROUP * halves if paired else 1),)),
        ],
        flops=rows * LATENT_DIM * 6 * COLS,
        moved=4 * 2**20,
        room=14,
        results="vvvvvvva",
    )(where, *near, *far, *columns)
    low = lax.ppermute(last, "half", up)
    high = lax.ppermute(first, "half", down)
    normed_low = lax.ppermute(last_normed, "half", up)
    normed_high = lax.ppermute(first_normed, "half", down)

    (outcome,) = call(
        interior_kernel,
        "attention_interior",
        [((rows, COLS), BF16)],
        "vvv",
        flops=rows * COLS * 2048,
        moved=2**21,
        exps=rows * 512,
    )(steps, queries, own)
    (outcome,) = call(
        edge_kernel,
        "attention_edges",
        [((rows, COLS), BF16)],
        "vvvvvv",
        flops=rows * COLS * 512,
        moved=2**20,
        exps=rows * 128,
    )(steps, queries, own, low, high, outcome)
    attended = exchange(outcome.reshape(GROUP * members_num, part, COLS), ("quad", "core", "ens"))
    (weights,) = call(
        weights_kernel,
        "weights",
        [((LATENT_DIM, width), BF16)],
        "s" + "a" * len(pieces),
        [pltpu.SemaphoreType.DMA((2 * GROUP * halves,))],
        moved=4 * 2**20,
    )(where, *pieces)
    attended, normed_low, normed_high = lax.optimization_barrier((attended, normed_low, normed_high))

    prediction, grads = call(
        mix_kernel,
        "mix_loss_backward",
        [((FIELD_NUM, node_rows), F32), ((GROUP * members_num, part, COLS), BF16)],
        "vvvvv",
        [pltpu.VMEM((node_rows, LATENT_DIM), BF16)],
        flops=node_rows * LATENT_DIM * 4 * width,
        moved=2**22,
        room=14,
    )(attended, sources, weights, truth, factor)
    grads = exchange(grads, ("quad", "core", "ens")).reshape(rows, COLS)

    (kv_grads,) = call(
        backward_kernel,
        "attention_backward",
        [((rows + 2 * RIM, 4 * COLS), BF16)],
        "vvvvvv",
        [
            pltpu.VMEM((rows + 2 * RIM, 2 * COLS), BF16),
            pltpu.VMEM((rows + 2 * RIM, 2 * COLS), F32),
        ],
        flops=rows * COLS * 5120,
        moved=2**22,
        exps=rows * 512,
        room=14,
    )(steps, queries, low, own, high, grads)
    (term,) = call(
        product_kernel,
        "product",
        [((LATENT_DIM, 2 * COLS), BF16)],
        "vvvv",
        flops=(rows + 2 * RIM) * LATENT_DIM * 8 * COLS,
        moved=2**22,
        room=16,
    )(normed, normed_low, normed_high, kv_grads)
    term, prediction = lax.optimization_barrier((term, prediction))
    term = exchange(term.reshape(-1, shard, 2 * COLS), everyone)
    (grad_kv,) = call(
        gather_kernel, "gather_sums", [((shard, 2 * LATENT_DIM), F32)], "v", flops=2**17, moved=2**20
    )(term.reshape(halves, GROUP, members_num, shard, 2 * COLS))

    if members_num == 2:
        got = jnp.roll(swap(prediction, "ens", 1), part, axis=1)
        lane = lax.broadcasted_iota(jnp.int32, prediction.shape, 1)
        prediction = jnp.where(lane // part == ens, prediction, got)
    else:
        prediction = prediction.reshape(FIELD_NUM, members_num, part).transpose(1, 0, 2)
        prediction = exchange(prediction, "ens").transpose(1, 0, 2)
    return (prediction.reshape(1, FIELD_NUM, node_rows), grad_kv)


def solution(mesh):
    space, ens = mesh.shape["space"], mesh.shape["ens"]
    split = Mesh(
        mesh.devices.reshape(space // GROUP, QUAD, CORES, ens), ("half", "quad", "core", "ens")
    )
    nodes = ("half", "quad", "core")
    shards = nodes + ("ens",)
    in_specs = (
        P("ens", nodes, None),
        P(shards, None),
        P(shards, None),
        P(shards, None),
        P(None, nodes),
        P(nodes),
        P(nodes, None),
    )
    out_specs = (P("ens", None, nodes), P(shards, None))
    return jax.shard_map(body, mesh=split, in_specs=in_specs, out_specs=out_specs, check_vma=False)
```

```python
import functools

import jax
import jax.numpy as jnp
from jax import lax
from jax.experimental import pallas as pl
from jax.experimental.pallas import tpu as pltpu
from jax.sharding import Mesh
from jax.sharding import PartitionSpec as P

LATENT_DIM = 1024
HEADS = 16
HEAD = 64
FIELD_NUM = 100
TILE = 64
RADIUS = 2
K_NB = 4
QUAD = 4
CORES = 2
GROUP = QUAD * CORES
COLS = LATENT_DIM // GROUP
RIM = RADIUS * TILE
FIELD_PAD = 128
PAIR = 2
WINDOW = (PAIR + 2 * RADIUS) * TILE
NOWHERE = 100
NOTE_ROWS = 16

NORM_EPS = 1e-06
SOFT_WIDTH = 0.0625
MASKED = -1e30

F32 = jnp.float32
BF16 = jnp.bfloat16

VMEM = pl.BlockSpec(memory_space=pltpu.VMEM)
SMEM = pl.BlockSpec(memory_space=pltpu.SMEM)
ANYWHERE = pl.BlockSpec(memory_space=pltpu.HBM)
OVER_ROWS = (((0,), (0,)), ((), ()))
OVER_COLUMNS = (((1,), (1,)), ((), ()))


def call(kernel, name, outs, ins, scratch=(), flops=0, moved=0, exps=0, room=8, results=None):
    spaces = {"s": SMEM, "v": VMEM, "a": ANYWHERE}
    return pl.pallas_call(
        kernel,
        out_shape=[jax.ShapeDtypeStruct(shape, kind) for shape, kind in outs],
        in_specs=[spaces[space] for space in ins],
        out_specs=[spaces[space] for space in results or "v" * len(outs)],
        scratch_shapes=list(scratch),
        compiler_params=pltpu.CompilerParams(vmem_limit_bytes=room * 2**20),
        cost_estimate=pl.CostEstimate(flops=flops, bytes_accessed=moved, transcendentals=exps),
        name=name,
    )


def fetch(pairs, sems):
    copies = [
        pltpu.make_async_copy(source, target, sems.at[at]) for at, (source, target) in enumerate(pairs)
    ]
    for copy in copies:
        copy.start()
    return copies


def prepare_kernel(
    where_ref,
    near_ref,
    source_any,
    w_any,
    mix_any,
    readout_any,
    normed_ref,
    columns_ref,
    packed_ref,
    *refs,
):
    parts, (source_ref, w_ref, readout_ref, sems) = refs[:-4], refs[-4:]
    copies = fetch(
        [
            (w_any, w_ref),
            (source_any, source_ref),
            (readout_any, readout_ref),
            (mix_any, packed_ref.at[:, :LATENT_DIM]),
        ],
        sems,
    )
    copies[1].wait()
    rows = source_ref.shape[0]
    source = source_ref[...].astype(F32)
    inverse = lax.rsqrt(jnp.mean(source * source, axis=-1, keepdims=True) + NORM_EPS)
    normed_ref[:rows, :] = (source * inverse).astype(BF16)
    if len(parts) == 1:
        parts[0][...] = source_ref[...].reshape(parts[0].shape)
    else:
        for step, part_ref in enumerate(parts):
            part = part_ref.shape[1]
            place = pl.multiple_of((where_ref[2] ^ step) * part, part)
            part_ref[0] = source_ref[pl.ds(place, part), :]
    normed_ref[rows:, :] = jnp.zeros((NOTE_ROWS, LATENT_DIM), BF16)
    row = lax.broadcasted_iota(jnp.int32, (NOTE_ROWS, 128), 0)
    lane = lax.broadcasted_iota(jnp.int32, (NOTE_ROWS, 128), 1)
    note = jnp.zeros((NOTE_ROWS, 128), F32)
    for tile in range(near_ref.shape[0]):
        for slot in range(K_NB):
            at = near_ref[tile, slot]
            step = jnp.where(at >= 0, at - where_ref[3] - tile, NOWHERE).astype(F32)
            note = jnp.where((row == tile) & (lane == slot), step, note)
    normed_ref[rows:, :128] = note.astype(BF16)
    copies[0].wait()
    halves, _, members_num = columns_ref.shape[:3]
    for g in range(GROUP):
        chunk = jnp.concatenate(
            [w_ref[:, (part * GROUP + g) * COLS : (part * GROUP + g + 1) * COLS] for part in range(3)],
            axis=1,
        )
        for half in range(halves):
            for m in range(members_num):
                columns_ref[half, g, m] = chunk
    copies[2].wait()
    packed_ref[:, LATENT_DIM:] = jnp.zeros((packed_ref.shape[0], FIELD_PAD), BF16)
    packed_ref[:, LATENT_DIM : LATENT_DIM + FIELD_NUM] = readout_ref[...]
    copies[3].wait()


def owners(where_ref):
    core, quad = where_ref[0], where_ref[1]
    return [(quad ^ step) * CORES + (core ^ flip) for flip in range(CORES) for step in range(QUAD)]


def project_kernel(where_ref, *refs):
    blocks, refs = refs[:GROUP], refs[GROUP:]
    columns, refs = refs[:-10], refs[-10:]
    q_ref, kv_ref, steps_ref, first_ref, last_ref, normed_any = refs[:6]
    notes, normed, w, sems = refs[6:]
    block = blocks[0].shape[0] - NOTE_ROWS
    pairs = []
    for at, (rows_ref, owner) in enumerate(zip(blocks, owners(where_ref))):
        place = pl.ds(pl.multiple_of(owner * block, block), block)
        pairs.append((rows_ref.at[:block], normed.at[place]))
        pairs.append((rows_ref.at[block:, :128], notes.at[owner]))
    if len(columns) == 1:
        pairs.append((columns[0], w))
    else:
        for step, part in enumerate(columns):
            pairs.append((part, w.at[:, where_ref[2] ^ step]))
    copies = fetch(pairs, sems)
    for copy in copies:
        copy.wait()
    keep = pltpu.make_async_copy(normed, normed_any, sems.at[0])
    keep.start()
    weights = w[...].reshape(LATENT_DIM, 3 * COLS)
    projected = jnp.dot(normed[...], weights, preferred_element_type=F32).astype(BF16)
    q_ref[...] = projected[:, :COLS]
    kv_ref[...] = projected[:, COLS:]
    last = GROUP * block - RIM
    first_ref[...] = projected[:RIM, COLS:]
    last_ref[...] = projected[last:, COLS:]
    steps_ref[...] = notes[...].astype(F32)
    keep.wait()


def weights_kernel(where_ref, *refs):
    pieces, (w_ref, sems) = refs[:-2], refs[-2:]
    core, quad, ens = where_ref[0], where_ref[1], where_ref[2]
    pairs = []
    if len(pieces) == GROUP:
        for at, piece in enumerate(pieces):
            place = (quad ^ (at % QUAD), core ^ (at // QUAD))
            pairs.append((piece, w_ref.at[:, place[0], place[1], 0]))
    else:
        for at, piece in enumerate(pieces):
            for step in range(QUAD):
                place = (quad ^ step, core ^ (at // 2), ens ^ (at % 2))
                pairs.append((piece.at[step], w_ref.at[:, place[0], place[1], place[2]]))
    for copy in fetch(pairs, sems):
        copy.wait()


def by_head(rows):
    lane = lax.broadcasted_iota(jnp.int32, rows.shape, 1)
    zero = jnp.zeros_like(rows)
    return jnp.concatenate(
        [jnp.where(lane < HEAD, rows, zero), jnp.where(lane < HEAD, zero, rows)], axis=0
    )


def usable_keys(steps_ref, pair):
    lane = (lax.broadcasted_iota(jnp.int32, (1, WINDOW), 1) // TILE - RADIUS).astype(F32)
    masks = []
    for query_tile in range(PAIR):
        found = jnp.zeros((1, WINDOW), F32)
        for slot in range(K_NB):
            step = steps_ref[pair, query_tile : query_tile + 1, slot : slot + 1]
            found = jnp.where(lane - query_tile == step, 1.0, found)
        masks.append(found)
    row = lax.broadcasted_iota(jnp.int32, (2 * PAIR * TILE, 1), 0) // TILE % PAIR
    return jnp.where(row == 0, masks[0], masks[1]) > 0


def probabilities(queries, keys, usable):
    scores = lax.dot_general(queries, keys, OVER_COLUMNS, preferred_element_type=F32) * (HEAD**-0.5)
    scores = jnp.where(usable, scores, MASKED)
    raised = jnp.exp(scores - jnp.max(scores, axis=-1, keepdims=True))
    return raised * (1.0 / jnp.sum(raised, axis=-1, keepdims=True))


def attend(steps_ref, pair, queries, keys, values):
    probs = probabilities(by_head(queries), keys, usable_keys(steps_ref, pair))
    both = jnp.dot(probs.astype(BF16), values, preferred_element_type=F32)
    lane = lax.broadcasted_iota(jnp.int32, queries.shape, 1)
    half = PAIR * TILE
    return jnp.where(lane < HEAD, both[:half], both[half:]).astype(BF16)


def interior_kernel(steps_ref, q_ref, kv_ref, out_ref):
    step = PAIR * TILE
    pairs = q_ref.shape[0] // step
    for pair in range(1, pairs - 1):
        window = slice((pair - 1) * step, (pair + 2) * step)
        rows = slice(pair * step, (pair + 1) * step)
        out_ref[rows, :] = attend(
            steps_ref, pair, q_ref[rows, :], kv_ref[window, :COLS], kv_ref[window, COLS:]
        )


def edge_kernel(steps_ref, q_ref, kv_ref, low_ref, high_ref, done_ref, out_ref):
    step = PAIR * TILE
    count = q_ref.shape[0]
    pairs = count // step
    out_ref[step : count - step, :] = done_ref[step : count - step, :]
    first = jnp.concatenate([low_ref[...], kv_ref[: 2 * step, :]], axis=0)
    last = jnp.concatenate([kv_ref[count - 2 * step :, :], high_ref[...]], axis=0)
    for pair, window in ((0, first), (pairs - 1, last)):
        rows = slice(pair * step, (pair + 1) * step)
        out_ref[rows, :] = attend(
            steps_ref, pair, q_ref[rows, :], window[:, :COLS], window[:, COLS:]
        )


def attend_back(steps_ref, pair, queries, grads, keys, values):
    queries, grads = by_head(queries), by_head(grads)
    probs = probabilities(queries, keys, usable_keys(steps_ref, pair))
    grad_probs = lax.dot_general(grads, values, OVER_COLUMNS, preferred_element_type=F32)
    row_delta = jnp.sum(probs * grad_probs, axis=-1, keepdims=True)
    grad_scores = (probs * (grad_probs - row_delta) * (HEAD**-0.5)).astype(BF16)
    key_grad = lax.dot_general(grad_scores, queries, OVER_ROWS, preferred_element_type=F32)
    value_grad = lax.dot_general(probs.astype(BF16), grads, OVER_ROWS, preferred_element_type=F32)
    return key_grad, value_grad


def edge_back_kernel(
    steps_ref, q_ref, kv_ref, low_ref, high_ref, g_ref, rim_low_ref, rim_high_ref, part_ref
):
    step = PAIR * TILE
    count = q_ref.shape[0]
    first = jnp.concatenate([low_ref[...], kv_ref[: 2 * step, :]], axis=0)
    last = jnp.concatenate([kv_ref[count - 2 * step :, :], high_ref[...]], axis=0)
    pairs = count // step
    for edge, pair, window, rim_ref in ((0, 0, first, rim_low_ref), (1, pairs - 1, last, rim_high_ref)):
        rows = slice(pair * step, (pair + 1) * step)
        grads = attend_back(
            steps_ref, pair, q_ref[rows, :], g_ref[rows, :], window[:, :COLS], window[:, COLS:]
        )
        rim = slice(0, RIM) if edge == 0 else slice(WINDOW - RIM, WINDOW)
        own = slice(RIM, WINDOW) if edge == 0 else slice(0, WINDOW - RIM)
        for at, grad in enumerate(grads):
            columns = slice(at * COLS, (at + 1) * COLS)
            rim_ref[:, columns] = grad[rim].astype(BF16)
            part_ref[edge, :, columns] = grad[own]


def interior_back_kernel(steps_ref, q_ref, kv_ref, g_ref, part_ref, out_ref):
    step = PAIR * TILE
    count = q_ref.shape[0]
    pairs = count // step
    reach = 2 * step
    out_ref[:reach, :] = part_ref[0]
    out_ref[reach : count - reach, :] = jnp.zeros((count - 2 * reach, 2 * COLS), F32)
    out_ref[count - reach :, :] = part_ref[1]
    for pair in range(1, pairs - 1):
        window = slice((pair - 1) * step, (pair + 2) * step)
        rows = slice(pair * step, (pair + 1) * step)
        key_grad, value_grad = attend_back(
            steps_ref,
            pair,
            q_ref[rows, :],
            g_ref[rows, :],
            kv_ref[window, :COLS],
            kv_ref[window, COLS:],
        )
        out_ref[window, :COLS] += key_grad
        out_ref[window, COLS:] += value_grad


def slope(spread):
    return spread * lax.rsqrt(spread * spread + SOFT_WIDTH)


def mix_kernel(
    where_ref,
    att_ref,
    kept_ref,
    sent_ref,
    w,
    truth_ref,
    factor_ref,
    pred_ref,
    grad_ref,
    a,
    source,
    truth,
):
    part = kept_ref.shape[1]
    members_num = a.shape[0] // part
    if members_num == 2:
        for step, rows_ref in enumerate((kept_ref, sent_ref)):
            place = pl.multiple_of((where_ref[2] ^ step) * part, part)
            source[pl.ds(place, part), :] = rows_ref[0]
    else:
        source[...] = sent_ref[...].reshape(source.shape)
    for g in range(GROUP):
        for m in range(members_num):
            a[m * part : (m + 1) * part, g * COLS : (g + 1) * COLS] = att_ref[g * members_num + m]
    lane_part = lax.broadcasted_iota(jnp.int32, (1, a.shape[0]), 1) // part
    own_truth, own_factor = truth_ref[...], factor_ref[...]
    for turn in range(1, members_num):
        at = lane_part - turn
        here = jnp.where(at < 0, at + members_num, at) == where_ref[2]
        own_truth = jnp.where(here, pltpu.roll(truth_ref[...], turn * part, 1), own_truth)
        own_factor = jnp.where(here, pltpu.roll(factor_ref[...], turn * part, 1), own_factor)
    truth[...] = jnp.zeros_like(truth)
    truth[:FIELD_NUM, :] = own_truth
    both = w[...].reshape(LATENT_DIM, LATENT_DIM + FIELD_PAD)
    mix, readout = both[:, :LATENT_DIM], both[:, LATENT_DIM:]
    hidden = source[...].astype(F32) + jnp.dot(a[...], mix, preferred_element_type=F32)
    inverse = lax.rsqrt(jnp.mean(hidden * hidden, axis=-1, keepdims=True) + NORM_EPS)
    decoded = (hidden * inverse).astype(BF16)
    prediction = lax.dot_general(
        readout, decoded, (((0,), (1,)), ((), ())), preferred_element_type=F32
    )
    pred_ref[...] = prediction[:FIELD_NUM]
    spread = jnp.zeros_like(prediction)
    for other in range(1, members_num):
        spread = spread + slope(prediction - pltpu.roll(prediction, other * part, 1))
    derivative = own_factor / FIELD_NUM * (
        slope(prediction - truth[...]) - spread / (members_num - 1)
    )
    grad_decoded = lax.dot_general(
        derivative.astype(BF16), readout, (((0,), (1,)), ((), ())), preferred_element_type=F32
    )
    grad_hidden = inverse * grad_decoded - hidden * inverse**3 * jnp.mean(
        grad_decoded * hidden, axis=-1, keepdims=True
    )
    grads = lax.dot_general(
        grad_hidden.astype(BF16), mix, OVER_COLUMNS, preferred_element_type=F32
    ).astype(BF16)
    for g in range(GROUP):
        for m in range(members_num):
            grad_ref[g * members_num + m] = grads[
                m * part : (m + 1) * part, g * COLS : (g + 1) * COLS
            ]


def product_kernel(normed_ref, from_low_ref, from_high_ref, grads_ref, out_ref):
    count = normed_ref.shape[0]
    grads = grads_ref[...]
    grads = jnp.concatenate(
        [
            grads[:RIM] + from_low_ref[...].astype(F32),
            grads[RIM : count - RIM],
            grads[count - RIM :] + from_high_ref[...].astype(F32),
        ],
        axis=0,
    )
    high = grads.astype(BF16)
    low = (grads - high.astype(F32)).astype(BF16)
    both = lax.dot_general(
        normed_ref[...], jnp.concatenate([high, low], axis=1), OVER_ROWS, preferred_element_type=F32
    )
    out_ref[...] = (both[:, : 2 * COLS] + both[:, 2 * COLS :]).astype(BF16)


def gather_kernel(parts_ref, out_ref):
    halves, _, members_num = parts_ref.shape[:3]
    for g in range(GROUP):
        total = None
        for half in range(halves):
            for m in range(members_num):
                part = parts_ref[half, g, m].astype(F32)
                total = part if total is None else total + part
        out_ref[:, g * COLS : (g + 1) * COLS] = total[:, :COLS]
        out_ref[:, LATENT_DIM + g * COLS : LATENT_DIM + (g + 1) * COLS] = total[:, COLS:]


def exchange(chunks, axes):
    return lax.all_to_all(chunks, axes, 0, 0)


def swap(value, axis, step):
    return lax.ppermute(value, axis, [(i, i ^ step) for i in range(lax.axis_size(axis))])


def in_order(mine, axis, at):
    if lax.axis_size(axis) != 2:
        return lax.all_gather(mine, axis, axis=at)
    other = swap(mine, axis, 1)
    first = lax.axis_index(axis) == 0
    return jnp.stack([jnp.where(first, mine, other), jnp.where(first, other, mine)], axis=at)


def body(members, w_attn, w_mix, readout_matrix, observed_truth, cell_surface_factor, neighbours):
    halves, members_num = lax.axis_size("half"), lax.axis_size("ens")
    nodes = ("half", "quad", "core")
    everyone = nodes + ("ens",)
    shard = w_attn.shape[0]
    node_rows = members.shape[1]
    rows = GROUP * node_rows
    part = node_rows // members_num
    up = [(i, i + 1) for i in range(halves - 1)]
    down = [(target, source) for source, target in up]
    core, quad, ens = (lax.axis_index(axis) for axis in ("core", "quad", "ens"))
    first_tile = lax.axis_index(("half", "quad", "core")) * neighbours.shape[0]
    where = jnp.stack([core, quad, ens, first_tile]).astype(jnp.int32)
    width = LATENT_DIM + FIELD_PAD
    paired = members_num == 2
    copies = 1 if paired else members_num

    normed, columns, packed, *sources = call(
        prepare_kernel,
        "prepare",
        [
            ((node_rows + NOTE_ROWS, LATENT_DIM), BF16),
            ((halves, GROUP, copies, shard, 3 * COLS), BF16),
            ((shard, width), BF16),
        ]
        + [((1 if paired else members_num, part, LATENT_DIM), BF16)] * (2 if paired else 1),
        "ssaaaa",
        [
            pltpu.VMEM((node_rows, LATENT_DIM), BF16),
            pltpu.VMEM(w_attn.shape, BF16),
            pltpu.VMEM(readout_matrix.shape, BF16),
            pltpu.SemaphoreType.DMA((4,)),
        ],
        flops=2**20,
        moved=2**20,
        room=56,
    )(where, neighbours, members.reshape(node_rows, LATENT_DIM), w_attn, w_mix, readout_matrix)

    packed = in_order(packed, "half", 0)
    near = [normed] + [swap(normed, "quad", step) for step in range(1, QUAD)]
    if paired:
        columns = exchange(columns.reshape(-1, shard, 3 * COLS), nodes)
        columns = [columns, swap(columns, "ens", 1)]
    else:
        columns = [exchange(columns.reshape(-1, shard, 3 * COLS), everyone)]
        columns = [columns[0].reshape(LATENT_DIM, 3 * COLS)]
    far = [swap(piece, "core", 1) for piece in near]

    if paired:
        kept, sent = sources[0], swap(sources[1], "ens", 1)
        packed, columns[0] = lax.optimization_barrier((packed, columns[0]))
        pieces = [packed] + [swap(packed, "quad", step) for step in range(1, QUAD)]
    else:
        kept = sent = exchange(sources[0], "ens")
        packed = in_order(packed, "ens", 1).reshape(halves, members_num * shard, width)
        pieces = [packed] + [swap(packed, "quad", step) for step in range(1, QUAD)]

    queries, own, steps, first, last, normed = call(
        project_kernel,
        "project",
        [
            ((rows, COLS), BF16),
            ((rows, 2 * COLS), BF16),
            ((GROUP, NOTE_ROWS, 128), F32),
            ((RIM, 2 * COLS), BF16),
            ((RIM, 2 * COLS), BF16),
            ((rows, LATENT_DIM), BF16),
        ],
        "s" + "a" * (GROUP + len(columns)),
        [
            pltpu.VMEM((GROUP, NOTE_ROWS, 128), BF16),
            pltpu.VMEM((rows, LATENT_DIM), BF16),
            pltpu.VMEM(
                (GROUP * halves, 2, shard, 3 * COLS) if paired else (LATENT_DIM, 3 * COLS), BF16
            ),
            pltpu.SemaphoreType.DMA((2 * GROUP + 2,)),
        ],
        flops=rows * LATENT_DIM * 6 * COLS,
        moved=4 * 2**20,
        room=14,
        results="vvvvva",
    )(where, *near, *far, *columns)
    low = lax.ppermute(last, "half", up)
    high = lax.ppermute(first, "half", down)
    if paired:
        pieces = jnp.stack(pieces)
        pieces, own = lax.optimization_barrier((pieces, own))
        pieces = [pieces, swap(pieces, "ens", 1)]

    (outcome,) = call(
        interior_kernel,
        "attention_interior",
        [((rows, COLS), BF16)],
        "vvv",
        flops=rows * COLS * 2048,
        moved=2**21,
        exps=rows * 512,
    )(steps, queries, own)
    (outcome,) = call(
        edge_kernel,
        "attention_edges",
        [((rows, COLS), BF16)],
        "vvvvvv",
        flops=rows * COLS * 512,
        moved=2**20,
        exps=rows * 128,
    )(steps, queries, own, low, high, outcome)
    *pieces, outcome = lax.optimization_barrier((*pieces, outcome))
    attended = exchange(outcome.reshape(GROUP * members_num, part, COLS), ("quad", "core", "ens"))
    pieces = pieces + [swap(piece, "core", 1) for piece in pieces]
    block = (halves, QUAD, CORES) + ((2, shard) if paired else (1, members_num * shard)) + (width,)
    (weights,) = call(
        weights_kernel,
        "weights",
        [(block, BF16)],
        "s" + "a" * len(pieces),
        [pltpu.SemaphoreType.DMA((4 * QUAD,))],
        moved=4 * 2**20,
    )(where, *pieces)

    prediction, grads = call(
        mix_kernel,
        "mix_loss_backward",
        [((FIELD_NUM, node_rows), F32), ((GROUP * members_num, part, COLS), BF16)],
        "svvvvvv",
        [
            pltpu.VMEM((node_rows, LATENT_DIM), BF16),
            pltpu.VMEM((node_rows, LATENT_DIM), BF16),
            pltpu.VMEM((FIELD_PAD, node_rows), F32),
        ],
        flops=node_rows * LATENT_DIM * 4 * width,
        moved=2**22,
        room=14,
    )(where, attended, kept, sent, weights, observed_truth, cell_surface_factor[None])
    grads = exchange(grads, ("quad", "core", "ens")).reshape(rows, COLS)

    rim_low, rim_high, edges = call(
        edge_back_kernel,
        "attention_edges_back",
        [
            ((RIM, 2 * COLS), BF16),
            ((RIM, 2 * COLS), BF16),
            ((2, WINDOW - RIM, 2 * COLS), F32),
        ],
        "vvvvvv",
        flops=rows * COLS * 1280,
        moved=2**20,
        exps=rows * 128,
    )(steps, queries, own, low, high, grads)
    from_low = lax.ppermute(rim_high, "half", up)
    from_high = lax.ppermute(rim_low, "half", down)
    (kv_grads,) = call(
        interior_back_kernel,
        "attention_interior_back",
        [((rows, 2 * COLS), F32)],
        "vvvvv",
        flops=rows * COLS * 4096,
        moved=2**22,
        exps=rows * 512,
        room=10,
    )(steps, queries, own, grads, edges)
    (term,) = call(
        product_kernel,
        "product",
        [((LATENT_DIM, 2 * COLS), BF16)],
        "vvvv",
        flops=rows * LATENT_DIM * 8 * COLS,
        moved=2**22,
        room=16,
    )(normed, from_low, from_high, kv_grads)
    term, prediction = lax.optimization_barrier((term, prediction))
    term = exchange(term.reshape(-1, shard, 2 * COLS), everyone)
    (grad_kv,) = call(
        gather_kernel, "gather_sums", [((shard, 2 * LATENT_DIM), F32)], "v", flops=2**17, moved=2**20
    )(term.reshape(halves, GROUP, members_num, shard, 2 * COLS))

    if members_num == 2:
        got = jnp.roll(swap(prediction, "ens", 1), part, axis=1)
        lane = lax.broadcasted_iota(jnp.int32, prediction.shape, 1)
        prediction = jnp.where(lane // part == ens, prediction, got)
    else:
        prediction = prediction.reshape(FIELD_NUM, members_num, part).transpose(1, 0, 2)
        prediction = exchange(prediction, "ens").transpose(1, 0, 2)
    return (prediction.reshape(1, FIELD_NUM, node_rows), grad_kv)


def solution(mesh):
    space, ens = mesh.shape["space"], mesh.shape["ens"]
    split = Mesh(
        mesh.devices.reshape(space // GROUP, QUAD, CORES, ens), ("half", "quad", "core", "ens")
    )
    nodes = ("half", "quad", "core")
    shards = nodes + ("ens",)
    in_specs = (
        P("ens", nodes, None),
        P(shards, None),
        P(shards, None),
        P(shards, None),
        P(None, nodes),
        P(nodes),
        P(nodes, None),
    )
    out_specs = (P("ens", None, nodes), P(shards, None))
    return jax.shard_map(body, mesh=split, in_specs=in_specs, out_specs=out_specs, check_vma=False)
```

```python
import functools

import jax
import jax.numpy as jnp
from jax import lax
from jax.experimental import pallas as pl
from jax.experimental.pallas import tpu as pltpu
from jax.sharding import Mesh
from jax.sharding import PartitionSpec as P

LATENT_DIM = 1024
HEADS = 16
HEAD = 64
FIELD_NUM = 100
TILE = 64
RADIUS = 2
K_NB = 4
QUAD = 4
CORES = 2
GROUP = QUAD * CORES
COLS = LATENT_DIM // GROUP
RIM = RADIUS * TILE
FIELD_PAD = 128
PAIR = 2
WINDOW = (PAIR + 2 * RADIUS) * TILE
NOWHERE = 100
NOTE_ROWS = 16

NORM_EPS = 1e-06
SOFT_WIDTH = 0.0625
MASKED = -1e30

F32 = jnp.float32
BF16 = jnp.bfloat16

VMEM = pl.BlockSpec(memory_space=pltpu.VMEM)
SMEM = pl.BlockSpec(memory_space=pltpu.SMEM)
ANYWHERE = pl.BlockSpec(memory_space=pltpu.HBM)
OVER_ROWS = (((0,), (0,)), ((), ()))
OVER_COLUMNS = (((1,), (1,)), ((), ()))


def call(kernel, name, outs, ins, scratch=(), flops=0, moved=0, exps=0, room=8, results=None):
    spaces = {"s": SMEM, "v": VMEM, "a": ANYWHERE}
    return pl.pallas_call(
        kernel,
        out_shape=[jax.ShapeDtypeStruct(shape, kind) for shape, kind in outs],
        in_specs=[spaces[space] for space in ins],
        out_specs=[spaces[space] for space in results or "v" * len(outs)],
        scratch_shapes=list(scratch),
        compiler_params=pltpu.CompilerParams(vmem_limit_bytes=room * 2**20),
        cost_estimate=pl.CostEstimate(flops=flops, bytes_accessed=moved, transcendentals=exps),
        name=name,
    )


def fetch(pairs, sems):
    copies = [
        pltpu.make_async_copy(source, target, sems.at[at]) for at, (source, target) in enumerate(pairs)
    ]
    for copy in copies:
        copy.start()
    return copies


def prepare_kernel(
    where_ref,
    near_ref,
    source_any,
    w_any,
    mix_any,
    readout_any,
    normed_ref,
    columns_ref,
    packed_ref,
    *refs,
):
    parts, (source_ref, w_ref, readout_ref, sems) = refs[:-4], refs[-4:]
    copies = fetch(
        [
            (w_any, w_ref),
            (source_any, source_ref),
            (readout_any, readout_ref),
            (mix_any, packed_ref.at[:, :LATENT_DIM]),
        ],
        sems,
    )
    copies[1].wait()
    rows = source_ref.shape[0]
    source = source_ref[...].astype(F32)
    inverse = lax.rsqrt(jnp.mean(source * source, axis=-1, keepdims=True) + NORM_EPS)
    normed_ref[:rows, :] = (source * inverse).astype(BF16)
    if len(parts) == 1:
        parts[0][...] = source_ref[...].reshape(parts[0].shape)
    else:
        for step, part_ref in enumerate(parts):
            part = part_ref.shape[1]
            place = pl.multiple_of((where_ref[2] ^ step) * part, part)
            part_ref[0] = source_ref[pl.ds(place, part), :]
    normed_ref[rows:, :] = jnp.zeros((NOTE_ROWS, LATENT_DIM), BF16)
    row = lax.broadcasted_iota(jnp.int32, (NOTE_ROWS, 128), 0)
    lane = lax.broadcasted_iota(jnp.int32, (NOTE_ROWS, 128), 1)
    note = jnp.zeros((NOTE_ROWS, 128), F32)
    for tile in range(near_ref.shape[0]):
        for slot in range(K_NB):
            at = near_ref[tile, slot]
            step = jnp.where(at >= 0, at - where_ref[3] - tile, NOWHERE).astype(F32)
            note = jnp.where((row == tile) & (lane == slot), step, note)
    normed_ref[rows:, :128] = note.astype(BF16)
    copies[0].wait()
    halves, _, members_num = columns_ref.shape[:3]
    for g in range(GROUP):
        chunk = jnp.concatenate(
            [w_ref[:, (part * GROUP + g) * COLS : (part * GROUP + g + 1) * COLS] for part in range(3)],
            axis=1,
        )
        for half in range(halves):
            for m in range(members_num):
                columns_ref[half, g, m] = chunk
    copies[2].wait()
    packed_ref[:, LATENT_DIM:] = jnp.zeros((packed_ref.shape[0], FIELD_PAD), BF16)
    packed_ref[:, LATENT_DIM : LATENT_DIM + FIELD_NUM] = readout_ref[...]
    copies[3].wait()


def owners(where_ref):
    core, quad = where_ref[0], where_ref[1]
    return [(quad ^ step) * CORES + (core ^ flip) for flip in range(CORES) for step in range(QUAD)]


def put_rims(where_ref, rims, first, last):
    if len(rims) == 1:
        rims[0][...] = jnp.where(where_ref[4] == 0, last, first)
    else:
        rims[0][...], rims[1][...] = first, last


def project_kernel(parts, where_ref, *refs):
    blocks, refs = refs[:GROUP], refs[GROUP:]
    columns, refs = refs[:parts], refs[parts:]
    q_ref, kv_ref, steps_ref, normed_any, *rims = refs[:-4]
    notes, normed, w, sems = refs[-4:]
    block = blocks[0].shape[0] - NOTE_ROWS
    pairs = []
    for at, (rows_ref, owner) in enumerate(zip(blocks, owners(where_ref))):
        place = pl.ds(pl.multiple_of(owner * block, block), block)
        pairs.append((rows_ref.at[:block], normed.at[place]))
        pairs.append((rows_ref.at[block:, :128], notes.at[owner]))
    if len(columns) == 1:
        pairs.append((columns[0], w))
    else:
        for step, part in enumerate(columns):
            pairs.append((part, w.at[:, where_ref[2] ^ step]))
    copies = fetch(pairs, sems)
    for copy in copies:
        copy.wait()
    keep = pltpu.make_async_copy(normed, normed_any, sems.at[0])
    keep.start()
    weights = w[...].reshape(LATENT_DIM, 3 * COLS)
    projected = jnp.dot(normed[...], weights, preferred_element_type=F32).astype(BF16)
    q_ref[...] = projected[:, :COLS]
    kv_ref[...] = projected[:, COLS:]
    last = GROUP * block - RIM
    put_rims(where_ref, rims, projected[:RIM, COLS:], projected[last:, COLS:])
    steps_ref[...] = notes[...].astype(F32)
    keep.wait()


def assemble_kernel(where_ref, *refs):
    pieces, refs = refs[:GROUP], refs[GROUP:]
    sources, (truth_any, w_ref, source_ref, truth_ref, sems) = refs[:-5], refs[-5:]
    core, quad, ens = where_ref[0], where_ref[1], where_ref[2]
    pairs = [(truth_any, truth_ref)]
    if len(sources) == 1:
        pairs.append((sources[0], source_ref))
    else:
        for step, part in enumerate(sources):
            pairs.append((part.at[0], source_ref.at[ens ^ step]))
    for at, piece in enumerate(pieces):
        pairs.append((piece, w_ref.at[:, quad ^ (at % QUAD), core ^ (at // QUAD)]))
    for copy in fetch(pairs, sems):
        copy.wait()


def by_head(rows):
    lane = lax.broadcasted_iota(jnp.int32, rows.shape, 1)
    zero = jnp.zeros_like(rows)
    return jnp.concatenate(
        [jnp.where(lane < HEAD, rows, zero), jnp.where(lane < HEAD, zero, rows)], axis=0
    )


def usable_keys(steps_ref, pair):
    lane = (lax.broadcasted_iota(jnp.int32, (1, WINDOW), 1) // TILE - RADIUS).astype(F32)
    masks = []
    for query_tile in range(PAIR):
        found = jnp.zeros((1, WINDOW), F32)
        for slot in range(K_NB):
            step = steps_ref[pair, query_tile : query_tile + 1, slot : slot + 1]
            found = jnp.where(lane - query_tile == step, 1.0, found)
        masks.append(found)
    row = lax.broadcasted_iota(jnp.int32, (2 * PAIR * TILE, 1), 0) // TILE % PAIR
    return jnp.where(row == 0, masks[0], masks[1]) > 0


def probabilities(queries, keys, usable):
    scores = lax.dot_general(queries, keys, OVER_COLUMNS, preferred_element_type=F32) * (HEAD**-0.5)
    scores = jnp.where(usable, scores, MASKED)
    raised = jnp.exp(scores - jnp.max(scores, axis=-1, keepdims=True))
    return raised * (1.0 / jnp.sum(raised, axis=-1, keepdims=True))


def attend(steps_ref, pair, queries, keys, values):
    probs = probabilities(by_head(queries), keys, usable_keys(steps_ref, pair))
    both = jnp.dot(probs.astype(BF16), values, preferred_element_type=F32)
    lane = lax.broadcasted_iota(jnp.int32, queries.shape, 1)
    half = PAIR * TILE
    return jnp.where(lane < HEAD, both[:half], both[half:]).astype(BF16)


def interior_kernel(steps_ref, q_ref, kv_ref, out_ref):
    step = PAIR * TILE
    pairs = q_ref.shape[0] // step
    for pair in range(1, pairs - 1):
        window = slice((pair - 1) * step, (pair + 2) * step)
        rows = slice(pair * step, (pair + 1) * step)
        out_ref[rows, :] = attend(
            steps_ref, pair, q_ref[rows, :], kv_ref[window, :COLS], kv_ref[window, COLS:]
        )


def edge_kernel(steps_ref, q_ref, kv_ref, low_ref, high_ref, done_ref, out_ref):
    step = PAIR * TILE
    count = q_ref.shape[0]
    pairs = count // step
    out_ref[step : count - step, :] = done_ref[step : count - step, :]
    first = jnp.concatenate([low_ref[...], kv_ref[: 2 * step, :]], axis=0)
    last = jnp.concatenate([kv_ref[count - 2 * step :, :], high_ref[...]], axis=0)
    for pair, window in ((0, first), (pairs - 1, last)):
        rows = slice(pair * step, (pair + 1) * step)
        out_ref[rows, :] = attend(
            steps_ref, pair, q_ref[rows, :], window[:, :COLS], window[:, COLS:]
        )


def attend_back(steps_ref, pair, queries, grads, keys, values):
    queries, grads = by_head(queries), by_head(grads)
    probs = probabilities(queries, keys, usable_keys(steps_ref, pair))
    grad_probs = lax.dot_general(grads, values, OVER_COLUMNS, preferred_element_type=F32)
    row_delta = jnp.sum(probs * grad_probs, axis=-1, keepdims=True)
    grad_scores = (probs * (grad_probs - row_delta) * (HEAD**-0.5)).astype(BF16)
    key_grad = lax.dot_general(grad_scores, queries, OVER_ROWS, preferred_element_type=F32)
    value_grad = lax.dot_general(probs.astype(BF16), grads, OVER_ROWS, preferred_element_type=F32)
    return key_grad, value_grad


def edge_back_kernel(
    where_ref, steps_ref, q_ref, kv_ref, low_ref, high_ref, g_ref, part_ref, *rims
):
    outer = []
    step = PAIR * TILE
    count = q_ref.shape[0]
    first = jnp.concatenate([low_ref[...], kv_ref[: 2 * step, :]], axis=0)
    last = jnp.concatenate([kv_ref[count - 2 * step :, :], high_ref[...]], axis=0)
    pairs = count // step
    for edge, pair, window in ((0, 0, first), (1, pairs - 1, last)):
        rows = slice(pair * step, (pair + 1) * step)
        grads = attend_back(
            steps_ref, pair, q_ref[rows, :], g_ref[rows, :], window[:, :COLS], window[:, COLS:]
        )
        rim = slice(0, RIM) if edge == 0 else slice(WINDOW - RIM, WINDOW)
        own = slice(RIM, WINDOW) if edge == 0 else slice(0, WINDOW - RIM)
        for at, grad in enumerate(grads):
            columns = slice(at * COLS, (at + 1) * COLS)
            part_ref[edge, :, columns] = grad[own]
        outer.append(jnp.concatenate([grad[rim].astype(BF16) for grad in grads], axis=1))
    put_rims(where_ref, rims, *outer)


def interior_back_kernel(steps_ref, q_ref, kv_ref, g_ref, part_ref, out_ref):
    step = PAIR * TILE
    count = q_ref.shape[0]
    pairs = count // step
    reach = 2 * step
    out_ref[:reach, :] = part_ref[0]
    out_ref[reach : count - reach, :] = jnp.zeros((count - 2 * reach, 2 * COLS), F32)
    out_ref[count - reach :, :] = part_ref[1]
    for pair in range(1, pairs - 1):
        window = slice((pair - 1) * step, (pair + 2) * step)
        rows = slice(pair * step, (pair + 1) * step)
        key_grad, value_grad = attend_back(
            steps_ref,
            pair,
            q_ref[rows, :],
            g_ref[rows, :],
            kv_ref[window, :COLS],
            kv_ref[window, COLS:],
        )
        out_ref[window, :COLS] += key_grad
        out_ref[window, COLS:] += value_grad


def slope(spread):
    return spread * lax.rsqrt(spread * spread + SOFT_WIDTH)


def mix_kernel(
    where_ref, att_ref, source_ref, w, truth_ref, factor_ref, pred_ref, grad_ref, a, truth
):
    members_num, part, _ = source_ref.shape
    for g in range(GROUP):
        for m in range(members_num):
            a[m * part : (m + 1) * part, g * COLS : (g + 1) * COLS] = att_ref[g * members_num + m]
    lane_part = lax.broadcasted_iota(jnp.int32, (1, a.shape[0]), 1) // part
    own_truth, own_factor = truth_ref[...], factor_ref[...]
    for turn in range(1, members_num):
        at = lane_part - turn
        here = jnp.where(at < 0, at + members_num, at) == where_ref[2]
        own_truth = jnp.where(here, pltpu.roll(truth_ref[...], turn * part, 1), own_truth)
        own_factor = jnp.where(here, pltpu.roll(factor_ref[...], turn * part, 1), own_factor)
    truth[...] = jnp.zeros_like(truth)
    truth[:FIELD_NUM, :] = own_truth
    both = w[...].reshape(LATENT_DIM, LATENT_DIM + FIELD_PAD)
    mix, readout = both[:, :LATENT_DIM], both[:, LATENT_DIM:]
    source = source_ref[...].reshape(a.shape).astype(F32)
    hidden = source + jnp.dot(a[...], mix, preferred_element_type=F32)
    inverse = lax.rsqrt(jnp.mean(hidden * hidden, axis=-1, keepdims=True) + NORM_EPS)
    decoded = (hidden * inverse).astype(BF16)
    prediction = lax.dot_general(
        readout, decoded, (((0,), (1,)), ((), ())), preferred_element_type=F32
    )
    pred_ref[...] = prediction[:FIELD_NUM]
    spread = jnp.zeros_like(prediction)
    for other in range(1, members_num):
        spread = spread + slope(prediction - pltpu.roll(prediction, other * part, 1))
    derivative = own_factor / FIELD_NUM * (
        slope(prediction - truth[...]) - spread / (members_num - 1)
    )
    grad_decoded = lax.dot_general(
        derivative.astype(BF16), readout, (((0,), (1,)), ((), ())), preferred_element_type=F32
    )
    grad_hidden = inverse * grad_decoded - hidden * inverse**3 * jnp.mean(
        grad_decoded * hidden, axis=-1, keepdims=True
    )
    grads = lax.dot_general(
        grad_hidden.astype(BF16), mix, OVER_COLUMNS, preferred_element_type=F32
    ).astype(BF16)
    for g in range(GROUP):
        for m in range(members_num):
            grad_ref[g * members_num + m] = grads[
                m * part : (m + 1) * part, g * COLS : (g + 1) * COLS
            ]


def product_kernel(where_ref, normed_ref, from_low_ref, from_high_ref, grads_ref, out_ref):
    count = normed_ref.shape[0]
    from_low = jnp.where(where_ref[4] > 0, from_low_ref[...].astype(F32), 0.0)
    from_high = jnp.where(where_ref[4] < where_ref[5], from_high_ref[...].astype(F32), 0.0)
    grads = grads_ref[...]
    grads = jnp.concatenate(
        [
            grads[:RIM] + from_low,
            grads[RIM : count - RIM],
            grads[count - RIM :] + from_high,
        ],
        axis=0,
    )
    high = grads.astype(BF16)
    low = (grads - high.astype(F32)).astype(BF16)
    both = lax.dot_general(
        normed_ref[...], jnp.concatenate([high, low], axis=1), OVER_ROWS, preferred_element_type=F32
    )
    out_ref[...] = (both[:, : 2 * COLS] + both[:, 2 * COLS :]).astype(BF16)


def gather_kernel(parts_ref, out_ref):
    halves, _, members_num = parts_ref.shape[:3]
    for g in range(GROUP):
        total = None
        for half in range(halves):
            for m in range(members_num):
                part = parts_ref[half, g, m].astype(F32)
                total = part if total is None else total + part
        out_ref[:, g * COLS : (g + 1) * COLS] = total[:, :COLS]
        out_ref[:, LATENT_DIM + g * COLS : LATENT_DIM + (g + 1) * COLS] = total[:, COLS:]


def exchange(chunks, axes):
    return lax.all_to_all(chunks, axes, 0, 0)


def swap(value, axis, step):
    return lax.ppermute(value, axis, [(i, i ^ step) for i in range(lax.axis_size(axis))])


def in_order(mine, axis, at):
    if lax.axis_size(axis) != 2:
        return lax.all_gather(mine, axis, axis=at)
    other = swap(mine, axis, 1)
    first = lax.axis_index(axis) == 0
    return jnp.stack([jnp.where(first, mine, other), jnp.where(first, other, mine)], axis=at)


def body(members, w_attn, w_mix, readout_matrix, observed_truth, cell_surface_factor, neighbours):
    halves, members_num = lax.axis_size("half"), lax.axis_size("ens")
    nodes = ("half", "quad", "core")
    everyone = nodes + ("ens",)
    shard = w_attn.shape[0]
    node_rows = members.shape[1]
    rows = GROUP * node_rows
    part = node_rows // members_num
    up = [(i, i + 1) for i in range(halves - 1)]
    down = [(target, source) for source, target in up]
    core, quad, ens = (lax.axis_index(axis) for axis in ("core", "quad", "ens"))
    first_tile = lax.axis_index(("half", "quad", "core")) * neighbours.shape[0]
    half = lax.axis_index("half")
    where = jnp.stack([core, quad, ens, first_tile, half, halves - 1]).astype(jnp.int32)
    width = LATENT_DIM + FIELD_PAD
    paired = members_num == 2
    copies = 1 if paired else members_num

    normed, columns, packed, *sources = call(
        prepare_kernel,
        "prepare",
        [
            ((node_rows + NOTE_ROWS, LATENT_DIM), BF16),
            ((halves, GROUP, copies, shard, 3 * COLS), BF16),
            ((shard, width), BF16),
        ]
        + [((1 if paired else members_num, part, LATENT_DIM), BF16)] * (2 if paired else 1),
        "ssaaaa",
        [
            pltpu.VMEM((node_rows, LATENT_DIM), BF16),
            pltpu.VMEM(w_attn.shape, BF16),
            pltpu.VMEM(readout_matrix.shape, BF16),
            pltpu.SemaphoreType.DMA((4,)),
        ],
        flops=2**20,
        moved=2**20,
        room=56,
    )(where, neighbours, members.reshape(node_rows, LATENT_DIM), w_attn, w_mix, readout_matrix)

    packed = in_order(packed, "half", 0)
    near = [normed] + [swap(normed, "quad", step) for step in range(1, QUAD)]
    if paired:
        columns = exchange(columns.reshape(-1, shard, 3 * COLS), nodes)
        columns = [columns, swap(columns, "ens", 1)]
    else:
        columns = [exchange(columns.reshape(-1, shard, 3 * COLS), everyone)]
        columns = [columns[0].reshape(LATENT_DIM, 3 * COLS)]
    far = [swap(piece, "core", 1) for piece in near]

    packed = in_order(packed, "ens", 1).reshape(halves, members_num * shard, width)
    if paired:
        sources = [sources[0], swap(sources[1], "ens", 1)]
        columns[1], sources[1] = lax.optimization_barrier((columns[1], sources[1]))
    else:
        sources = [exchange(sources[0], "ens")]

    rim = ((RIM, 2 * COLS), BF16)
    rims = [rim] if halves == 2 else [rim, rim]
    queries, own, steps, normed, *inner = call(
        functools.partial(project_kernel, len(columns)),
        "project",
        [
            ((rows, COLS), BF16),
            ((rows, 2 * COLS), BF16),
            ((GROUP, NOTE_ROWS, 128), F32),
            ((rows, LATENT_DIM), BF16),
        ]
        + rims,
        "s" + "a" * (GROUP + len(columns)),
        [
            pltpu.VMEM((GROUP, NOTE_ROWS, 128), BF16),
            pltpu.VMEM((rows, LATENT_DIM), BF16),
            pltpu.VMEM(
                (GROUP * halves, 2, shard, 3 * COLS) if paired else (LATENT_DIM, 3 * COLS), BF16
            ),
            pltpu.SemaphoreType.DMA((2 * GROUP + 2,)),
        ],
        flops=rows * LATENT_DIM * 6 * COLS,
        moved=4 * 2**20,
        room=14,
        results="vvvavv"[: 4 + len(rims)],
    )(where, *near, *far, *columns)

    def across(inner):
        if halves == 2:
            got = swap(inner[0], "half", 1)
            return got, got
        return lax.ppermute(inner[1], "half", up), lax.ppermute(inner[0], "half", down)

    low, high = across(inner)

    (outcome,) = call(
        interior_kernel,
        "attention_interior",
        [((rows, COLS), BF16)],
        "vvv",
        flops=rows * COLS * 2048,
        moved=2**21,
        exps=rows * 512,
    )(steps, queries, own)
    (outcome,) = call(
        edge_kernel,
        "attention_edges",
        [((rows, COLS), BF16)],
        "vvvvvv",
        flops=rows * COLS * 512,
        moved=2**20,
        exps=rows * 128,
    )(steps, queries, own, low, high, outcome)
    packed, own = lax.optimization_barrier((packed, own))
    pieces = [packed] + [swap(packed, "quad", step) for step in range(1, QUAD)]
    pieces = pieces + [swap(piece, "core", 1) for piece in pieces]
    attended = exchange(outcome.reshape(GROUP * members_num, part, COLS), ("quad", "core", "ens"))
    weights, sources, truth = call(
        assemble_kernel,
        "assemble",
        [
            ((halves, QUAD, CORES, members_num * shard, width), BF16),
            ((members_num, part, LATENT_DIM), BF16),
            (observed_truth.shape, F32),
        ],
        "s" + "a" * (len(pieces) + len(sources) + 1),
        [pltpu.SemaphoreType.DMA((GROUP + len(sources) + 1,))],
        moved=4 * 2**20,
        room=48,
    )(where, *pieces, *sources, observed_truth)

    prediction, grads = call(
        mix_kernel,
        "mix_loss_backward",
        [((FIELD_NUM, node_rows), F32), ((GROUP * members_num, part, COLS), BF16)],
        "svvvvv",
        [
            pltpu.VMEM((node_rows, LATENT_DIM), BF16),
            pltpu.VMEM((FIELD_PAD, node_rows), F32),
        ],
        flops=node_rows * LATENT_DIM * 4 * width,
        moved=2**22,
        room=14,
    )(where, attended, sources, weights, truth, cell_surface_factor[None])
    grads = exchange(grads, ("quad", "core", "ens")).reshape(rows, COLS)

    edges, *inner = call(
        edge_back_kernel,
        "attention_edges_back",
        [((2, WINDOW - RIM, 2 * COLS), F32)] + rims,
        "svvvvvv",
        flops=rows * COLS * 1280,
        moved=2**20,
        exps=rows * 128,
    )(where, steps, queries, own, low, high, grads)
    from_low, from_high = across(inner)
    (kv_grads,) = call(
        interior_back_kernel,
        "attention_interior_back",
        [((rows, 2 * COLS), F32)],
        "vvvvv",
        flops=rows * COLS * 4096,
        moved=2**22,
        exps=rows * 512,
        room=10,
    )(steps, queries, own, grads, edges)
    (term,) = call(
        product_kernel,
        "product",
        [((LATENT_DIM, 2 * COLS), BF16)],
        "svvvv",
        flops=rows * LATENT_DIM * 8 * COLS,
        moved=2**22,
        room=16,
    )(where, normed, from_low, from_high, kv_grads)
    term, prediction = lax.optimization_barrier((term, prediction))
    term = exchange(term.reshape(-1, shard, 2 * COLS), everyone)
    (grad_kv,) = call(
        gather_kernel, "gather_sums", [((shard, 2 * LATENT_DIM), F32)], "v", flops=2**17, moved=2**20
    )(term.reshape(halves, GROUP, members_num, shard, 2 * COLS))

    if members_num == 2:
        got = jnp.roll(swap(prediction, "ens", 1), part, axis=1)
        lane = lax.broadcasted_iota(jnp.int32, prediction.shape, 1)
        prediction = jnp.where(lane // part == ens, prediction, got)
    else:
        prediction = prediction.reshape(FIELD_NUM, members_num, part).transpose(1, 0, 2)
        prediction = exchange(prediction, "ens").transpose(1, 0, 2)
    return (prediction.reshape(1, FIELD_NUM, node_rows), grad_kv)


def solution(mesh):
    space, ens = mesh.shape["space"], mesh.shape["ens"]
    split = Mesh(
        mesh.devices.reshape(space // GROUP, QUAD, CORES, ens), ("half", "quad", "core", "ens")
    )
    nodes = ("half", "quad", "core")
    shards = nodes + ("ens",)
    in_specs = (
        P("ens", nodes, None),
        P(shards, None),
        P(shards, None),
        P(shards, None),
        P(None, nodes),
        P(nodes),
        P(nodes, None),
    )
    out_specs = (P("ens", None, nodes), P(shards, None))
    return jax.shard_map(body, mesh=split, in_specs=in_specs, out_specs=out_specs, check_vma=False)
```

```python
import functools

import jax
import jax.numpy as jnp
from jax import lax
from jax.experimental import pallas as pl
from jax.experimental.pallas import tpu as pltpu
from jax.sharding import Mesh
from jax.sharding import PartitionSpec as P

LATENT_DIM = 1024
HEADS = 16
HEAD = 64
FIELD_NUM = 100
TILE = 64
RADIUS = 2
K_NB = 4
QUAD = 4
CORES = 2
GROUP = QUAD * CORES
COLS = LATENT_DIM // GROUP
RIM = RADIUS * TILE
FIELD_PAD = 128
PAIR = 2
WINDOW = (PAIR + 2 * RADIUS) * TILE
NOWHERE = 100
NOTE_ROWS = 16
CHUNKS = 4

NORM_EPS = 1e-06
SOFT_WIDTH = 0.0625
MASKED = -1e30

F32 = jnp.float32
BF16 = jnp.bfloat16

VMEM = pl.BlockSpec(memory_space=pltpu.VMEM)
SMEM = pl.BlockSpec(memory_space=pltpu.SMEM)
HBM = pl.BlockSpec(memory_space=pltpu.HBM)
ANYWHERE = pl.BlockSpec(memory_space=pl.ANY)
OVER_ROWS = (((0,), (0,)), ((), ()))
OVER_COLUMNS = (((1,), (1,)), ((), ()))


def call(kernel, name, outs, ins, scratch=(), flops=0, moved=0, exps=0, room=8, results=None):
    results = results or "v" * len(outs)
    spaces = {"s": SMEM, "v": VMEM, "h": HBM, "a": ANYWHERE}
    made = pl.pallas_call(
        kernel,
        out_shape=[
            pltpu.HBM(shape, kind) if space == "h" else jax.ShapeDtypeStruct(shape, kind)
            for (shape, kind), space in zip(outs, results)
        ],
        in_specs=[spaces[space] for space in ins],
        out_specs=[spaces[space] for space in results],
        scratch_shapes=list(scratch),
        compiler_params=pltpu.CompilerParams(vmem_limit_bytes=room * 2**20),
        cost_estimate=pl.CostEstimate(flops=flops, bytes_accessed=moved, transcendentals=exps),
        name=name,
    )

    def run(*args):
        return made(
            *[
                pltpu.with_memory_space_constraint(arg, pltpu.HBM) if space == "h" else arg
                for arg, space in zip(args, ins)
            ]
        )

    return run


def fetch(pairs, sems, first=0):
    copies = [
        pltpu.make_async_copy(source, target, sems.at[first + at])
        for at, (source, target) in enumerate(pairs)
    ]
    for copy in copies:
        copy.start()
    return copies


def wait(copies):
    for copy in copies:
        copy.wait()


def prepare_kernel(
    near_ref,
    source_any,
    w_any,
    mix_any,
    readout_any,
    normed_any,
    columns_any,
    packed_any,
    *refs,
):
    parts, (source, normed, w, columns, readout, readout_pad, sems) = refs[:-7], refs[-7:]
    ens = lax.axis_index("ens")
    copies = fetch([(source_any, source), (w_any, w), (readout_any, readout)], sems)
    moves = [(mix_any, packed_any.at[:, :LATENT_DIM])]
    for step, part_any in enumerate(parts):
        if len(parts) == 1:
            moves += [
                (source_any.at[pl.ds(m * part_any.shape[1], part_any.shape[1])], part_any.at[m])
                for m in range(part_any.shape[0])
            ]
        else:
            part = part_any.shape[1]
            place = pl.multiple_of((ens ^ step) * part, part)
            moves.append((source_any.at[pl.ds(place, part)], part_any.at[0]))
    moves = fetch(moves, sems, 3)
    rows = source.shape[0]
    row = lax.broadcasted_iota(jnp.int32, (NOTE_ROWS, 128), 0)
    lane = lax.broadcasted_iota(jnp.int32, (NOTE_ROWS, 128), 1)
    note = jnp.zeros((NOTE_ROWS, 128), F32)
    tiles = near_ref.shape[0]
    first_tile = lax.axis_index(("half", "quad", "core")) * tiles
    for tile in range(tiles):
        for slot in range(K_NB):
            at = near_ref[tile, slot]
            step = jnp.where(at >= 0, at - first_tile - tile, NOWHERE).astype(F32)
            note = jnp.where((row == tile) & (lane == slot), step, note)
    normed[rows:, :] = jnp.zeros((NOTE_ROWS, LATENT_DIM), BF16)
    normed[rows:, :128] = note.astype(BF16)
    copies[0].wait()
    states = source[...].astype(F32)
    inverse = lax.rsqrt(jnp.mean(states * states, axis=-1, keepdims=True) + NORM_EPS)
    normed[:rows, :] = (states * inverse).astype(BF16)
    first = 3 + len(moves)
    out = fetch([(normed, normed_any)], sems, first)
    copies[1].wait()
    for g in range(GROUP):
        for part in range(3):
            at = (part * GROUP + g) * COLS
            columns[g, :, part * COLS : (part + 1) * COLS] = w[:, at : at + COLS]
    halves, _, members_num = columns_any.shape[:3]
    out += fetch(
        [
            (columns, columns_any.at[half, :, m])
            for half in range(halves)
            for m in range(members_num)
        ],
        sems,
        first + 1,
    )
    copies[2].wait()
    readout_pad[...] = jnp.zeros_like(readout_pad)
    readout_pad[:, :FIELD_NUM] = readout[...]
    out += fetch([(readout_pad, packed_any.at[:, LATENT_DIM:])], sems, first + len(out))
    wait(moves + out)


def owners():
    core, quad = lax.axis_index("core"), lax.axis_index("quad")
    return [(quad ^ step) * CORES + (core ^ flip) for flip in range(CORES) for step in range(QUAD)]


def collect_kernel(*refs):
    blocks, (normed_any, steps_ref, notes, sems) = refs[:GROUP], refs[GROUP:]
    block = blocks[0].shape[0] - NOTE_ROWS
    pairs = []
    for rows_ref, owner in zip(blocks, owners()):
        place = pl.ds(pl.multiple_of(owner * block, block), block)
        pairs.append((rows_ref.at[:block], normed_any.at[place]))
        pairs.append((rows_ref.at[block:, :128], notes.at[owner]))
    wait(fetch(pairs, sems))
    steps_ref[...] = notes[...].astype(F32)


def put_rims(rims, first, last):
    if len(rims) == 1:
        rims[0][...] = jnp.where(lax.axis_index("half") == 0, last, first)
    else:
        rims[0][...], rims[1][...] = first, last


def project_kernel(normed_any, *refs):
    columns, (normed, w, sems) = refs[:-3], refs[-3:]
    columns, (q_ref, kv_ref, *rims) = columns[: w.shape[1] if len(w.shape) == 4 else 1], columns[
        w.shape[1] if len(w.shape) == 4 else 1 :
    ]
    count = normed.shape[0]
    chunk = count // CHUNKS
    rows = [slice(at * chunk, (at + 1) * chunk) for at in range(CHUNKS)]
    if len(columns) == 1:
        pairs = [(columns[0], w)]
    else:
        ens = lax.axis_index("ens")
        pairs = [(part, w.at[:, ens ^ step]) for step, part in enumerate(columns)]
    copies = fetch(pairs + [(normed_any.at[part], normed.at[part]) for part in rows], sems)
    wait(copies[: len(pairs)])
    weights = w[...].reshape(LATENT_DIM, 3 * COLS)
    for part, copy in zip(rows, copies[len(pairs) :]):
        copy.wait()
        projected = jnp.dot(normed[part, :], weights, preferred_element_type=F32).astype(BF16)
        q_ref[part, :] = projected[:, :COLS]
        kv_ref[part, :] = projected[:, COLS:]
    put_rims(rims, kv_ref[:RIM, :], kv_ref[count - RIM :, :])


def assemble_kernel(*refs):
    pieces, (w_any, sems) = refs[:GROUP], refs[GROUP:]
    core, quad = lax.axis_index("core"), lax.axis_index("quad")
    pairs = [
        (piece, w_any.at[:, quad ^ (at % QUAD), core ^ (at // QUAD)])
        for at, piece in enumerate(pieces)
    ]
    wait(fetch(pairs, sems))


def by_head(rows):
    lane = lax.broadcasted_iota(jnp.int32, rows.shape, 1)
    zero = jnp.zeros_like(rows)
    return jnp.concatenate(
        [jnp.where(lane < HEAD, rows, zero), jnp.where(lane < HEAD, zero, rows)], axis=0
    )


def usable_keys(steps_ref, pair):
    lane = (lax.broadcasted_iota(jnp.int32, (1, WINDOW), 1) // TILE - RADIUS).astype(F32)
    masks = []
    for query_tile in range(PAIR):
        found = jnp.zeros((1, WINDOW), F32)
        for slot in range(K_NB):
            step = steps_ref[pair, query_tile : query_tile + 1, slot : slot + 1]
            found = jnp.where(lane - query_tile == step, 1.0, found)
        masks.append(found)
    row = lax.broadcasted_iota(jnp.int32, (2 * PAIR * TILE, 1), 0) // TILE % PAIR
    return jnp.where(row == 0, masks[0], masks[1]) > 0


def probabilities(queries, keys, usable):
    scores = lax.dot_general(queries, keys, OVER_COLUMNS, preferred_element_type=F32) * (HEAD**-0.5)
    scores = jnp.where(usable, scores, MASKED)
    raised = jnp.exp(scores - jnp.max(scores, axis=-1, keepdims=True))
    return raised * (1.0 / jnp.sum(raised, axis=-1, keepdims=True))


def attend(steps_ref, pair, queries, keys, values):
    probs = probabilities(by_head(queries), keys, usable_keys(steps_ref, pair))
    both = jnp.dot(probs.astype(BF16), values, preferred_element_type=F32)
    lane = lax.broadcasted_iota(jnp.int32, queries.shape, 1)
    half = PAIR * TILE
    return jnp.where(lane < HEAD, both[:half], both[half:]).astype(BF16)


def interior_kernel(steps_ref, q_ref, kv_ref, out_ref):
    step = PAIR * TILE
    pairs = q_ref.shape[0] // step
    for pair in range(1, pairs - 1):
        window = slice((pair - 1) * step, (pair + 2) * step)
        rows = slice(pair * step, (pair + 1) * step)
        out_ref[rows, :] = attend(
            steps_ref, pair, q_ref[rows, :], kv_ref[window, :COLS], kv_ref[window, COLS:]
        )


def edge_kernel(steps_ref, q_ref, kv_ref, low_ref, high_ref, done_ref, out_ref):
    step = PAIR * TILE
    count = q_ref.shape[0]
    pairs = count // step
    out_ref[step : count - step, :] = done_ref[step : count - step, :]
    first = jnp.concatenate([low_ref[...], kv_ref[: 2 * step, :]], axis=0)
    last = jnp.concatenate([kv_ref[count - 2 * step :, :], high_ref[...]], axis=0)
    for pair, window in ((0, first), (pairs - 1, last)):
        rows = slice(pair * step, (pair + 1) * step)
        out_ref[rows, :] = attend(
            steps_ref, pair, q_ref[rows, :], window[:, :COLS], window[:, COLS:]
        )


def attend_back(steps_ref, pair, queries, grads, keys, values):
    queries, grads = by_head(queries), by_head(grads)
    probs = probabilities(queries, keys, usable_keys(steps_ref, pair))
    grad_probs = lax.dot_general(grads, values, OVER_COLUMNS, preferred_element_type=F32)
    row_delta = jnp.sum(probs * grad_probs, axis=-1, keepdims=True)
    grad_scores = (probs * (grad_probs - row_delta) * (HEAD**-0.5)).astype(BF16)
    key_grad = lax.dot_general(grad_scores, queries, OVER_ROWS, preferred_element_type=F32)
    value_grad = lax.dot_general(probs.astype(BF16), grads, OVER_ROWS, preferred_element_type=F32)
    return key_grad, value_grad


def edge_back_kernel(
    steps_ref, q_ref, kv_ref, low_ref, high_ref, g_ref, part_ref, *rims
):
    outer = []
    step = PAIR * TILE
    count = q_ref.shape[0]
    first = jnp.concatenate([low_ref[...], kv_ref[: 2 * step, :]], axis=0)
    last = jnp.concatenate([kv_ref[count - 2 * step :, :], high_ref[...]], axis=0)
    pairs = count // step
    for edge, pair, window in ((0, 0, first), (1, pairs - 1, last)):
        rows = slice(pair * step, (pair + 1) * step)
        grads = attend_back(
            steps_ref, pair, q_ref[rows, :], g_ref[rows, :], window[:, :COLS], window[:, COLS:]
        )
        rim = slice(0, RIM) if edge == 0 else slice(WINDOW - RIM, WINDOW)
        own = slice(RIM, WINDOW) if edge == 0 else slice(0, WINDOW - RIM)
        for at, grad in enumerate(grads):
            columns = slice(at * COLS, (at + 1) * COLS)
            part_ref[edge, :, columns] = grad[own]
        outer.append(jnp.concatenate([grad[rim].astype(BF16) for grad in grads], axis=1))
    put_rims(rims, *outer)


def interior_back_kernel(steps_ref, q_ref, kv_ref, g_ref, part_ref, out_ref):
    step = PAIR * TILE
    count = q_ref.shape[0]
    pairs = count // step
    reach = 2 * step
    out_ref[:reach, :] = part_ref[0]
    out_ref[reach : count - reach, :] = jnp.zeros((count - 2 * reach, 2 * COLS), F32)
    out_ref[count - reach :, :] = part_ref[1]
    for pair in range(1, pairs - 1):
        window = slice((pair - 1) * step, (pair + 2) * step)
        rows = slice(pair * step, (pair + 1) * step)
        key_grad, value_grad = attend_back(
            steps_ref,
            pair,
            q_ref[rows, :],
            g_ref[rows, :],
            kv_ref[window, :COLS],
            kv_ref[window, COLS:],
        )
        out_ref[window, :COLS] += key_grad
        out_ref[window, COLS:] += value_grad


def slope(spread):
    return spread * lax.rsqrt(spread * spread + SOFT_WIDTH)


def mix_kernel(att_ref, factor_ref, truth_any, w_any, *refs):
    sources, refs = refs[:-8], refs[-8:]
    pred_ref, grad_ref, a, truth_ref, truth, source, w, sems = refs
    members_num, part, _ = source.shape
    halves = w.shape[0]
    ens = lax.axis_index("ens")
    copies = fetch([(w_any.at[half], w.at[half]) for half in range(halves)], sems)
    pairs = [(truth_any, truth_ref)]
    if len(sources) == 1:
        pairs.append((sources[0], source))
    else:
        pairs += [(rows.at[0], source.at[ens ^ step]) for step, rows in enumerate(sources)]
    others = fetch(pairs, sems, halves)
    for g in range(GROUP):
        for m in range(members_num):
            a[m * part : (m + 1) * part, g * COLS : (g + 1) * COLS] = att_ref[g * members_num + m]
    wait(others)
    lane_part = lax.broadcasted_iota(jnp.int32, (1, a.shape[0]), 1) // part
    own_truth, own_factor = truth_ref[...], factor_ref[...]
    for turn in range(1, members_num):
        at = lane_part - turn
        here = jnp.where(at < 0, at + members_num, at) == ens
        own_truth = jnp.where(here, pltpu.roll(truth_ref[...], turn * part, 1), own_truth)
        own_factor = jnp.where(here, pltpu.roll(factor_ref[...], turn * part, 1), own_factor)
    truth[...] = jnp.zeros_like(truth)
    truth[:FIELD_NUM, :] = own_truth
    hidden = source[...].reshape(a.shape).astype(F32)
    count = LATENT_DIM // halves
    for half in range(halves):
        copies[half].wait()
        mix = w[half].reshape(count, LATENT_DIM + FIELD_PAD)[:, :LATENT_DIM]
        hidden += jnp.dot(
            a[:, half * count : (half + 1) * count], mix, preferred_element_type=F32
        )
    both = w[...].reshape(LATENT_DIM, LATENT_DIM + FIELD_PAD)
    mix, readout = both[:, :LATENT_DIM], both[:, LATENT_DIM:]
    inverse = lax.rsqrt(jnp.mean(hidden * hidden, axis=-1, keepdims=True) + NORM_EPS)
    decoded = (hidden * inverse).astype(BF16)
    prediction = lax.dot_general(
        readout, decoded, (((0,), (1,)), ((), ())), preferred_element_type=F32
    )
    pred_ref[...] = prediction[:FIELD_NUM]
    spread = jnp.zeros_like(prediction)
    for other in range(1, members_num):
        spread = spread + slope(prediction - pltpu.roll(prediction, other * part, 1))
    derivative = own_factor / FIELD_NUM * (
        slope(prediction - truth[...]) - spread / (members_num - 1)
    )
    grad_decoded = lax.dot_general(
        derivative.astype(BF16), readout, (((0,), (1,)), ((), ())), preferred_element_type=F32
    )
    grad_hidden = inverse * grad_decoded - hidden * inverse**3 * jnp.mean(
        grad_decoded * hidden, axis=-1, keepdims=True
    )
    grads = lax.dot_general(
        grad_hidden.astype(BF16), mix, OVER_COLUMNS, preferred_element_type=F32
    ).astype(BF16)
    for g in range(GROUP):
        for m in range(members_num):
            grad_ref[g * members_num + m] = grads[
                m * part : (m + 1) * part, g * COLS : (g + 1) * COLS
            ]


def product_kernel(normed_ref, from_low_ref, from_high_ref, grads_ref, out_ref):
    count = normed_ref.shape[0]
    half, last = lax.axis_index("half"), lax.axis_size("half") - 1
    from_low = jnp.where(half > 0, from_low_ref[...].astype(F32), 0.0)
    from_high = jnp.where(half < last, from_high_ref[...].astype(F32), 0.0)
    grads = grads_ref[...]
    grads = jnp.concatenate(
        [
            grads[:RIM] + from_low,
            grads[RIM : count - RIM],
            grads[count - RIM :] + from_high,
        ],
        axis=0,
    )
    high = grads.astype(BF16)
    low = (grads - high.astype(F32)).astype(BF16)
    both = lax.dot_general(
        normed_ref[...], jnp.concatenate([high, low], axis=1), OVER_ROWS, preferred_element_type=F32
    )
    out_ref[...] = (both[:, : 2 * COLS] + both[:, 2 * COLS :]).astype(BF16)


def gather_kernel(parts_ref, out_ref):
    halves, _, members_num = parts_ref.shape[:3]
    for g in range(GROUP):
        total = None
        for half in range(halves):
            for m in range(members_num):
                part = parts_ref[half, g, m].astype(F32)
                total = part if total is None else total + part
        out_ref[:, g * COLS : (g + 1) * COLS] = total[:, :COLS]
        out_ref[:, LATENT_DIM + g * COLS : LATENT_DIM + (g + 1) * COLS] = total[:, COLS:]


def exchange(chunks, axes):
    return lax.all_to_all(chunks, axes, 0, 0)


def swap(value, axis, step):
    return lax.ppermute(value, axis, [(i, i ^ step) for i in range(lax.axis_size(axis))])


def in_order(mine, axis, at):
    if lax.axis_size(axis) != 2:
        return lax.all_gather(mine, axis, axis=at)
    other = swap(mine, axis, 1)
    first = lax.axis_index(axis) == 0
    return jnp.stack([jnp.where(first, mine, other), jnp.where(first, other, mine)], axis=at)


def body(members, w_attn, w_mix, readout_matrix, observed_truth, cell_surface_factor, neighbours):
    halves, members_num = lax.axis_size("half"), lax.axis_size("ens")
    nodes = ("half", "quad", "core")
    everyone = nodes + ("ens",)
    shard = w_attn.shape[0]
    node_rows = members.shape[1]
    rows = GROUP * node_rows
    part = node_rows // members_num
    up = [(i, i + 1) for i in range(halves - 1)]
    down = [(target, source) for source, target in up]
    ens = lax.axis_index("ens")
    width = LATENT_DIM + FIELD_PAD
    paired = members_num == 2
    copies = 1 if paired else members_num
    source_parts = 2 if paired else 1

    normed, columns, packed, *sources = call(
        prepare_kernel,
        "prepare",
        [
            ((node_rows + NOTE_ROWS, LATENT_DIM), BF16),
            ((halves, GROUP, copies, shard, 3 * COLS), BF16),
            ((shard, width), BF16),
        ]
        + [((1 if paired else members_num, part, LATENT_DIM), BF16)] * source_parts,
        "shhhh",
        [
            pltpu.VMEM((node_rows, LATENT_DIM), BF16),
            pltpu.VMEM((node_rows + NOTE_ROWS, LATENT_DIM), BF16),
            pltpu.VMEM(w_attn.shape, BF16),
            pltpu.VMEM((GROUP, shard, 3 * COLS), BF16),
            pltpu.VMEM(readout_matrix.shape, BF16),
            pltpu.VMEM((shard, FIELD_PAD), BF16),
            pltpu.SemaphoreType.DMA((6 + max(2, members_num) + halves * copies,)),
        ],
        flops=2**20,
        moved=2**20,
        results="hhh" + "h" * source_parts,
    )(neighbours, members.reshape(node_rows, LATENT_DIM), w_attn, w_mix, readout_matrix)

    packed = in_order(packed, "half", 0)
    near = [normed] + [swap(normed, "quad", step) for step in range(1, QUAD)]
    if paired:
        columns = exchange(columns.reshape(-1, shard, 3 * COLS), nodes)
        columns = [columns, swap(columns, "ens", 1)]
    else:
        columns = [exchange(columns.reshape(-1, shard, 3 * COLS), everyone)]
        columns = [columns[0].reshape(LATENT_DIM, 3 * COLS)]
    far = [swap(piece, "core", 1) for piece in near]
    normed, steps = call(
        collect_kernel,
        "collect",
        [((rows, LATENT_DIM), BF16), ((GROUP, NOTE_ROWS, 128), F32)],
        "a" * (2 * QUAD),
        [pltpu.VMEM((GROUP, NOTE_ROWS, 128), BF16), pltpu.SemaphoreType.DMA((2 * GROUP,))],
        moved=4 * 2**20,
        results="hv",
    )(*near, *far)

    packed = in_order(packed, "ens", 1).reshape(halves, members_num * shard, width)
    if paired:
        sources = [sources[0], swap(sources[1], "ens", 1)]
        columns[1], sources[1] = lax.optimization_barrier((columns[1], sources[1]))
    else:
        sources = [exchange(sources[0], "ens")]
    packed, far[3], columns[0] = lax.optimization_barrier((packed, far[3], columns[0]))
    pieces = [packed] + [swap(packed, "quad", step) for step in range(1, QUAD)]

    rim = ((RIM, 2 * COLS), BF16)
    rims = [rim] if halves == 2 else [rim, rim]
    queries, own, *inner = call(
        project_kernel,
        "project",
        [((rows, COLS), BF16), ((rows, 2 * COLS), BF16)] + rims,
        "h" + "a" * len(columns),
        [
            pltpu.VMEM((rows, LATENT_DIM), BF16),
            pltpu.VMEM(
                (GROUP * halves, 2, shard, 3 * COLS) if paired else (LATENT_DIM, 3 * COLS), BF16
            ),
            pltpu.SemaphoreType.DMA((CHUNKS + 2,)),
        ],
        flops=rows * LATENT_DIM * 6 * COLS,
        moved=4 * 2**20,
        room=10,
    )(normed, *columns)

    def across(inner):
        if halves == 2:
            got = swap(inner[0], "half", 1)
            return got, got
        return lax.ppermute(inner[1], "half", up), lax.ppermute(inner[0], "half", down)

    low, high = across(inner)

    (outcome,) = call(
        interior_kernel,
        "attention_interior",
        [((rows, COLS), BF16)],
        "vvv",
        flops=rows * COLS * 2048,
        moved=2**21,
        exps=rows * 512,
    )(steps, queries, own)
    (outcome,) = call(
        edge_kernel,
        "attention_edges",
        [((rows, COLS), BF16)],
        "vvvvvv",
        flops=rows * COLS * 512,
        moved=2**20,
        exps=rows * 128,
    )(steps, queries, own, low, high, outcome)
    *pieces, own = lax.optimization_barrier((*pieces, own))
    pieces = pieces + [swap(piece, "core", 1) for piece in pieces]
    attended = exchange(outcome.reshape(GROUP * members_num, part, COLS), ("quad", "core", "ens"))
    block = (halves, QUAD, CORES, members_num * shard, width)
    (weights,) = call(
        assemble_kernel,
        "assemble",
        [(block, BF16)],
        "a" * len(pieces),
        [pltpu.SemaphoreType.DMA((GROUP,))],
        moved=4 * 2**20,
        results="h",
    )(*pieces)

    prediction, grads = call(
        mix_kernel,
        "mix_loss_backward",
        [((FIELD_NUM, node_rows), F32), ((GROUP * members_num, part, COLS), BF16)],
        "vvhh" + "a" * len(sources),
        [
            pltpu.VMEM((node_rows, LATENT_DIM), BF16),
            pltpu.VMEM(observed_truth.shape, F32),
            pltpu.VMEM((FIELD_PAD, node_rows), F32),
            pltpu.VMEM((members_num, part, LATENT_DIM), BF16),
            pltpu.VMEM(block, BF16),
            pltpu.SemaphoreType.DMA((halves + 1 + len(sources),)),
        ],
        flops=node_rows * LATENT_DIM * 4 * width,
        moved=2**22,
        room=14,
    )(attended, cell_surface_factor[None], observed_truth, weights, *sources)
    grads = exchange(grads, ("quad", "core", "ens")).reshape(rows, COLS)

    edges, *inner = call(
        edge_back_kernel,
        "attention_edges_back",
        [((2, WINDOW - RIM, 2 * COLS), F32)] + rims,
        "vvvvvv",
        flops=rows * COLS * 1280,
        moved=2**20,
        exps=rows * 128,
    )(steps, queries, own, low, high, grads)
    from_low, from_high = across(inner)
    (kv_grads,) = call(
        interior_back_kernel,
        "attention_interior_back",
        [((rows, 2 * COLS), F32)],
        "vvvvv",
        flops=rows * COLS * 4096,
        moved=2**22,
        exps=rows * 512,
        room=10,
    )(steps, queries, own, grads, edges)
    (term,) = call(
        product_kernel,
        "product",
        [((LATENT_DIM, 2 * COLS), BF16)],
        "vvvv",
        flops=rows * LATENT_DIM * 8 * COLS,
        moved=2**22,
        room=16,
    )(normed, from_low, from_high, kv_grads)
    term, prediction = lax.optimization_barrier((term, prediction))
    term = exchange(term.reshape(-1, shard, 2 * COLS), everyone)
    (grad_kv,) = call(
        gather_kernel, "gather_sums", [((shard, 2 * LATENT_DIM), F32)], "v", flops=2**17, moved=2**20
    )(term.reshape(halves, GROUP, members_num, shard, 2 * COLS))

    if members_num == 2:
        got = jnp.roll(swap(prediction, "ens", 1), part, axis=1)
        lane = lax.broadcasted_iota(jnp.int32, prediction.shape, 1)
        prediction = jnp.where(lane // part == ens, prediction, got)
    else:
        prediction = prediction.reshape(FIELD_NUM, members_num, part).transpose(1, 0, 2)
        prediction = exchange(prediction, "ens").transpose(1, 0, 2)
    return (prediction.reshape(1, FIELD_NUM, node_rows), grad_kv)


def solution(mesh):
    space, ens = mesh.shape["space"], mesh.shape["ens"]
    split = Mesh(
        mesh.devices.reshape(space // GROUP, QUAD, CORES, ens), ("half", "quad", "core", "ens")
    )
    nodes = ("half", "quad", "core")
    shards = nodes + ("ens",)
    in_specs = (
        P("ens", nodes, None),
        P(shards, None),
        P(shards, None),
        P(shards, None),
        P(None, nodes),
        P(nodes),
        P(nodes, None),
    )
    out_specs = (P("ens", None, nodes), P(shards, None))
    return jax.shard_map(body, mesh=split, in_specs=in_specs, out_specs=out_specs, check_vma=False)
```

```python
import functools

import jax
import jax.numpy as jnp
from jax import lax
from jax.experimental import pallas as pl
from jax.experimental.pallas import tpu as pltpu
from jax.sharding import Mesh
from jax.sharding import PartitionSpec as P

LATENT_DIM = 1024
HEADS = 16
HEAD = 64
FIELD_NUM = 100
TILE = 64
RADIUS = 2
K_NB = 4
QUAD = 4
CORES = 2
GROUP = QUAD * CORES
COLS = LATENT_DIM // GROUP
RIM = RADIUS * TILE
FIELD_PAD = 128
PAIR = 2
WINDOW = (PAIR + 2 * RADIUS) * TILE
NOWHERE = 100
NOTE_ROWS = 16
CHUNKS = 4

NORM_EPS = 1e-06
SOFT_WIDTH = 0.0625
MASKED = -1e30

F32 = jnp.float32
BF16 = jnp.bfloat16

VMEM = pl.BlockSpec(memory_space=pltpu.VMEM)
SMEM = pl.BlockSpec(memory_space=pltpu.SMEM)
HBM = pl.BlockSpec(memory_space=pltpu.HBM)
ANYWHERE = pl.BlockSpec(memory_space=pl.ANY)
OVER_ROWS = (((0,), (0,)), ((), ()))
OVER_COLUMNS = (((1,), (1,)), ((), ()))


def call(kernel, name, outs, ins, scratch=(), flops=0, moved=0, exps=0, room=8, results=None):
    results = results or "v" * len(outs)
    spaces = {"s": SMEM, "v": VMEM, "h": HBM, "a": ANYWHERE}
    made = pl.pallas_call(
        kernel,
        out_shape=[
            pltpu.HBM(shape, kind) if space == "h" else jax.ShapeDtypeStruct(shape, kind)
            for (shape, kind), space in zip(outs, results)
        ],
        in_specs=[spaces[space] for space in ins],
        out_specs=[spaces[space] for space in results],
        scratch_shapes=list(scratch),
        compiler_params=pltpu.CompilerParams(vmem_limit_bytes=room * 2**20),
        cost_estimate=pl.CostEstimate(flops=flops, bytes_accessed=moved, transcendentals=exps),
        name=name,
    )

    def run(*args):
        return made(
            *[
                pltpu.with_memory_space_constraint(arg, pltpu.HBM) if space == "h" else arg
                for arg, space in zip(args, ins)
            ]
        )

    return run


def fetch(pairs, sems, first=0):
    copies = [
        pltpu.make_async_copy(source, target, sems.at[first + at])
        for at, (source, target) in enumerate(pairs)
    ]
    for copy in copies:
        copy.start()
    return copies


def wait(copies):
    for copy in copies:
        copy.wait()


def prepare_kernel(
    near_ref,
    source_any,
    w_any,
    mix_any,
    readout_any,
    normed_any,
    columns_any,
    packed_any,
    *refs,
):
    parts, (source, normed, w, columns, readout, packed, sems) = refs[:-7], refs[-7:]
    ens = lax.axis_index("ens")
    copies = fetch(
        [
            (source_any, source),
            (w_any, w),
            (readout_any, readout),
            (mix_any, packed.at[:, :LATENT_DIM]),
        ],
        sems,
    )
    rows = source.shape[0]
    row = lax.broadcasted_iota(jnp.int32, (NOTE_ROWS, 128), 0)
    lane = lax.broadcasted_iota(jnp.int32, (NOTE_ROWS, 128), 1)
    note = jnp.zeros((NOTE_ROWS, 128), F32)
    tiles = near_ref.shape[0]
    first_tile = lax.axis_index(("half", "quad", "core")) * tiles
    for tile in range(tiles):
        for slot in range(K_NB):
            at = near_ref[tile, slot]
            step = jnp.where(at >= 0, at - first_tile - tile, NOWHERE).astype(F32)
            note = jnp.where((row == tile) & (lane == slot), step, note)
    normed[rows:, :] = jnp.zeros((NOTE_ROWS, LATENT_DIM), BF16)
    normed[rows:, :128] = note.astype(BF16)
    copies[0].wait()
    states = source[...].astype(F32)
    inverse = lax.rsqrt(jnp.mean(states * states, axis=-1, keepdims=True) + NORM_EPS)
    normed[:rows, :] = (states * inverse).astype(BF16)
    moves = [(normed, normed_any)]
    for step, part_any in enumerate(parts):
        count, part, _ = part_any.shape
        for m in range(count):
            place = (ens ^ step) if len(parts) == 2 else m
            place = pl.multiple_of(place * part, part)
            moves.append((source.at[pl.ds(place, part)], part_any.at[m]))
    out = fetch(moves, sems, 4)
    copies[1].wait()
    for g in range(GROUP):
        for part in range(3):
            at = (part * GROUP + g) * COLS
            columns[g, :, part * COLS : (part + 1) * COLS] = w[:, at : at + COLS]
    halves, _, members_num = columns_any.shape[:3]
    out += fetch(
        [
            (columns, columns_any.at[half, :, m])
            for half in range(halves)
            for m in range(members_num)
        ],
        sems,
        4 + len(out),
    )
    copies[2].wait()
    copies[3].wait()
    packed[:, LATENT_DIM:] = jnp.zeros((packed.shape[0], FIELD_PAD), BF16)
    packed[:, LATENT_DIM : LATENT_DIM + FIELD_NUM] = readout[...]
    out += fetch([(packed, packed_any)], sems, 4 + len(out))
    wait(out)


def owners():
    core, quad = lax.axis_index("core"), lax.axis_index("quad")
    return [(quad ^ step) * CORES + (core ^ flip) for flip in range(CORES) for step in range(QUAD)]


def collect_kernel(*refs):
    blocks, (normed_any, steps_ref, notes, sems) = refs[:GROUP], refs[GROUP:]
    block = blocks[0].shape[0] - NOTE_ROWS
    pairs = []
    for rows_ref, owner in zip(blocks, owners()):
        place = pl.ds(pl.multiple_of(owner * block, block), block)
        pairs.append((rows_ref.at[:block], normed_any.at[place]))
        pairs.append((rows_ref.at[block:, :128], notes.at[owner]))
    wait(fetch(pairs, sems))
    steps_ref[...] = notes[...].astype(F32)


def put_rims(rims, first, last):
    if len(rims) == 1:
        rims[0][...] = jnp.where(lax.axis_index("half") == 0, last, first)
    else:
        rims[0][...], rims[1][...] = first, last


def rims_kernel(normed_any, *refs):
    rows, sems = refs[-2:]
    if len(refs[0].shape) == 2:
        columns, w, rims = refs[:1], refs[1], refs[2:-2]
        pairs = [(columns[0], w)]
    else:
        columns, w, rims = refs[:2], refs[2], refs[3:-2]
        ens = lax.axis_index("ens")
        pairs = [(part, w.at[:, ens ^ step]) for step, part in enumerate(columns)]
    last = normed_any.shape[0] - RIM
    if len(rims) == 1:
        place = pl.multiple_of(jnp.where(lax.axis_index("half") == 0, last, 0), RIM)
        pairs.append((normed_any.at[pl.ds(place, RIM)], rows.at[0]))
    else:
        pairs += [(normed_any.at[:RIM], rows.at[0]), (normed_any.at[last:], rows.at[1])]
    wait(fetch(pairs, sems))
    weights = w[...].reshape(LATENT_DIM, 3 * COLS)[:, COLS:]
    for at, rim_ref in enumerate(rims):
        rim_ref[...] = jnp.dot(rows[at], weights, preferred_element_type=F32).astype(BF16)


def project_kernel(normed_any, w_ref, q_ref, kv_ref, normed, sems):
    chunk = normed.shape[0] // CHUNKS
    rows = [slice(at * chunk, (at + 1) * chunk) for at in range(CHUNKS)]
    copies = fetch([(normed_any.at[part], normed.at[part]) for part in rows], sems)
    weights = w_ref[...].reshape(LATENT_DIM, 3 * COLS)
    for part, copy in zip(rows, copies):
        copy.wait()
        projected = jnp.dot(normed[part, :], weights, preferred_element_type=F32).astype(BF16)
        q_ref[part, :] = projected[:, :COLS] * jnp.asarray(HEAD**-0.5, BF16)
        kv_ref[part, :] = projected[:, COLS:]


def assemble_kernel(*refs):
    pieces, (w_any, sems) = refs[:GROUP], refs[GROUP:]
    core, quad = lax.axis_index("core"), lax.axis_index("quad")
    pairs = [
        (piece, w_any.at[:, quad ^ (at % QUAD), core ^ (at // QUAD)])
        for at, piece in enumerate(pieces)
    ]
    wait(fetch(pairs, sems))


def by_head(rows):
    lane = lax.broadcasted_iota(jnp.int32, rows.shape, 1)
    zero = jnp.zeros_like(rows)
    return jnp.concatenate(
        [jnp.where(lane < HEAD, rows, zero), jnp.where(lane < HEAD, zero, rows)], axis=0
    )


def usable_keys(steps_ref, pair):
    lane = (lax.broadcasted_iota(jnp.int32, (1, WINDOW), 1) // TILE - RADIUS).astype(F32)
    masks = []
    for query_tile in range(PAIR):
        found = jnp.zeros((1, WINDOW), F32)
        for slot in range(K_NB):
            step = steps_ref[pair, query_tile : query_tile + 1, slot : slot + 1]
            found = jnp.where(lane - query_tile == step, 1.0, found)
        masks.append(found)
    row = lax.broadcasted_iota(jnp.int32, (2 * PAIR * TILE, 1), 0) // TILE % PAIR
    return jnp.where(row == 0, masks[0], masks[1]) > 0


def raised_scores(queries, keys, usable):
    scores = lax.dot_general(queries, keys, OVER_COLUMNS, preferred_element_type=F32)
    scores = jnp.where(usable, scores, MASKED)
    raised = jnp.exp(scores - jnp.max(scores, axis=-1, keepdims=True))
    return raised, 1.0 / jnp.sum(raised, axis=-1, keepdims=True)


def attend(steps_ref, pair, queries, keys, values):
    raised, share = raised_scores(by_head(queries), keys, usable_keys(steps_ref, pair))
    both = jnp.dot(raised.astype(BF16), values, preferred_element_type=F32) * share
    lane = lax.broadcasted_iota(jnp.int32, queries.shape, 1)
    half = PAIR * TILE
    return jnp.where(lane < HEAD, both[:half], both[half:]).astype(BF16)


def interior_kernel(steps_ref, q_ref, kv_ref, out_ref):
    step = PAIR * TILE
    pairs = q_ref.shape[0] // step
    for pair in range(1, pairs - 1):
        window = slice((pair - 1) * step, (pair + 2) * step)
        rows = slice(pair * step, (pair + 1) * step)
        out_ref[rows, :] = attend(
            steps_ref, pair, q_ref[rows, :], kv_ref[window, :COLS], kv_ref[window, COLS:]
        )


def edge_kernel(steps_ref, q_ref, kv_ref, low_ref, high_ref, done_ref, out_ref):
    step = PAIR * TILE
    count = q_ref.shape[0]
    pairs = count // step
    out_ref[step : count - step, :] = done_ref[step : count - step, :]
    first = jnp.concatenate([low_ref[...], kv_ref[: 2 * step, :]], axis=0)
    last = jnp.concatenate([kv_ref[count - 2 * step :, :], high_ref[...]], axis=0)
    for pair, window in ((0, first), (pairs - 1, last)):
        rows = slice(pair * step, (pair + 1) * step)
        out_ref[rows, :] = attend(
            steps_ref, pair, q_ref[rows, :], window[:, :COLS], window[:, COLS:]
        )


def attend_back(steps_ref, pair, queries, grads, keys, values):
    queries, grads = by_head(queries), by_head(grads)
    raised, share = raised_scores(queries, keys, usable_keys(steps_ref, pair))
    probs = raised * share
    grad_probs = lax.dot_general(grads, values, OVER_COLUMNS, preferred_element_type=F32)
    row_delta = jnp.sum(probs * grad_probs, axis=-1, keepdims=True)
    grad_scores = (probs * (grad_probs - row_delta)).astype(BF16)
    key_grad = lax.dot_general(grad_scores, queries, OVER_ROWS, preferred_element_type=F32)
    value_grad = lax.dot_general(probs.astype(BF16), grads, OVER_ROWS, preferred_element_type=F32)
    return key_grad, value_grad


def edge_back_kernel(
    steps_ref, q_ref, kv_ref, low_ref, high_ref, g_ref, part_ref, *rims
):
    outer = []
    step = PAIR * TILE
    count = q_ref.shape[0]
    first = jnp.concatenate([low_ref[...], kv_ref[: 2 * step, :]], axis=0)
    last = jnp.concatenate([kv_ref[count - 2 * step :, :], high_ref[...]], axis=0)
    pairs = count // step
    for edge, pair, window in ((0, 0, first), (1, pairs - 1, last)):
        rows = slice(pair * step, (pair + 1) * step)
        grads = attend_back(
            steps_ref, pair, q_ref[rows, :], g_ref[rows, :], window[:, :COLS], window[:, COLS:]
        )
        rim = slice(0, RIM) if edge == 0 else slice(WINDOW - RIM, WINDOW)
        own = slice(RIM, WINDOW) if edge == 0 else slice(0, WINDOW - RIM)
        for at, grad in enumerate(grads):
            columns = slice(at * COLS, (at + 1) * COLS)
            part_ref[edge, :, columns] = grad[own]
        outer.append(jnp.concatenate([grad[rim].astype(BF16) for grad in grads], axis=1))
    put_rims(rims, *outer)


def interior_back_kernel(steps_ref, q_ref, kv_ref, g_ref, part_ref, out_ref):
    step = PAIR * TILE
    count = q_ref.shape[0]
    pairs = count // step
    reach = 2 * step
    out_ref[:reach, :] = part_ref[0]
    out_ref[reach : count - reach, :] = jnp.zeros((count - 2 * reach, 2 * COLS), F32)
    out_ref[count - reach :, :] = part_ref[1]
    for pair in range(1, pairs - 1):
        window = slice((pair - 1) * step, (pair + 2) * step)
        rows = slice(pair * step, (pair + 1) * step)
        key_grad, value_grad = attend_back(
            steps_ref,
            pair,
            q_ref[rows, :],
            g_ref[rows, :],
            kv_ref[window, :COLS],
            kv_ref[window, COLS:],
        )
        out_ref[window, :COLS] += key_grad
        out_ref[window, COLS:] += value_grad


def slope(spread):
    return spread * lax.rsqrt(spread * spread + SOFT_WIDTH)


def mix_kernel(att_ref, factor_ref, truth_any, w_any, *refs):
    sources, refs = refs[:-8], refs[-8:]
    pred_ref, grad_ref, a, truth_ref, truth, source, w, sems = refs
    members_num, part, _ = source.shape
    halves = w.shape[0]
    ens = lax.axis_index("ens")
    copies = fetch([(w_any.at[half], w.at[half]) for half in range(halves)], sems)
    pairs = [(truth_any, truth_ref)]
    if len(sources) == 1:
        pairs.append((sources[0], source))
    else:
        pairs += [(rows.at[0], source.at[ens ^ step]) for step, rows in enumerate(sources)]
    others = fetch(pairs, sems, halves)
    for g in range(GROUP):
        for m in range(members_num):
            a[m * part : (m + 1) * part, g * COLS : (g + 1) * COLS] = att_ref[g * members_num + m]
    wait(others)
    lane_part = lax.broadcasted_iota(jnp.int32, (1, a.shape[0]), 1) // part
    own_truth, own_factor = truth_ref[...], factor_ref[...]
    for turn in range(1, members_num):
        at = lane_part - turn
        here = jnp.where(at < 0, at + members_num, at) == ens
        own_truth = jnp.where(here, pltpu.roll(truth_ref[...], turn * part, 1), own_truth)
        own_factor = jnp.where(here, pltpu.roll(factor_ref[...], turn * part, 1), own_factor)
    truth[...] = jnp.zeros_like(truth)
    truth[:FIELD_NUM, :] = own_truth
    hidden = source[...].reshape(a.shape).astype(F32)
    count = LATENT_DIM // halves
    for half in range(halves):
        copies[half].wait()
        mix = w[half].reshape(count, LATENT_DIM + FIELD_PAD)[:, :LATENT_DIM]
        hidden += jnp.dot(
            a[:, half * count : (half + 1) * count], mix, preferred_element_type=F32
        )
    both = w[...].reshape(LATENT_DIM, LATENT_DIM + FIELD_PAD)
    mix, readout = both[:, :LATENT_DIM], both[:, LATENT_DIM:]
    inverse = lax.rsqrt(jnp.mean(hidden * hidden, axis=-1, keepdims=True) + NORM_EPS)
    decoded = (hidden * inverse).astype(BF16)
    prediction = lax.dot_general(
        readout, decoded, (((0,), (1,)), ((), ())), preferred_element_type=F32
    )
    pred_ref[...] = prediction[:FIELD_NUM]
    spread = jnp.zeros_like(prediction)
    for other in range(1, members_num):
        spread = spread + slope(prediction - pltpu.roll(prediction, other * part, 1))
    derivative = own_factor / FIELD_NUM * (
        slope(prediction - truth[...]) - spread / (members_num - 1)
    )
    grad_decoded = lax.dot_general(
        derivative.astype(BF16), readout, (((0,), (1,)), ((), ())), preferred_element_type=F32
    )
    grad_hidden = inverse * grad_decoded - hidden * inverse**3 * jnp.mean(
        grad_decoded * hidden, axis=-1, keepdims=True
    )
    grads = lax.dot_general(
        grad_hidden.astype(BF16), mix, OVER_COLUMNS, preferred_element_type=F32
    ).astype(BF16)
    for g in range(GROUP):
        for m in range(members_num):
            grad_ref[g * members_num + m] = grads[
                m * part : (m + 1) * part, g * COLS : (g + 1) * COLS
            ]


def product_kernel(normed_ref, from_low_ref, from_high_ref, grads_ref, out_ref):
    count = normed_ref.shape[0]
    half, last = lax.axis_index("half"), lax.axis_size("half") - 1
    from_low = jnp.where(half > 0, from_low_ref[...].astype(F32), 0.0)
    from_high = jnp.where(half < last, from_high_ref[...].astype(F32), 0.0)
    grads = grads_ref[...]
    grads = jnp.concatenate(
        [
            grads[:RIM] + from_low,
            grads[RIM : count - RIM],
            grads[count - RIM :] + from_high,
        ],
        axis=0,
    )
    high = grads.astype(BF16)
    low = (grads - high.astype(F32)).astype(BF16)
    both = lax.dot_general(
        normed_ref[...], jnp.concatenate([high, low], axis=1), OVER_ROWS, preferred_element_type=F32
    )
    out_ref[...] = (both[:, : 2 * COLS] + both[:, 2 * COLS :]).astype(BF16)


def gather_kernel(parts_ref, out_ref):
    halves, _, members_num = parts_ref.shape[:3]
    for g in range(GROUP):
        total = None
        for half in range(halves):
            for m in range(members_num):
                part = parts_ref[half, g, m].astype(F32)
                total = part if total is None else total + part
        out_ref[:, g * COLS : (g + 1) * COLS] = total[:, :COLS]
        out_ref[:, LATENT_DIM + g * COLS : LATENT_DIM + (g + 1) * COLS] = total[:, COLS:]


def exchange(chunks, axes):
    return lax.all_to_all(chunks, axes, 0, 0)


def swap(value, axis, step):
    return lax.ppermute(value, axis, [(i, i ^ step) for i in range(lax.axis_size(axis))])


def in_order(mine, axis, at):
    if lax.axis_size(axis) != 2:
        return lax.all_gather(mine, axis, axis=at)
    other = swap(mine, axis, 1)
    first = lax.axis_index(axis) == 0
    return jnp.stack([jnp.where(first, mine, other), jnp.where(first, other, mine)], axis=at)


def body(members, w_attn, w_mix, readout_matrix, observed_truth, cell_surface_factor, neighbours):
    halves, members_num = lax.axis_size("half"), lax.axis_size("ens")
    nodes = ("half", "quad", "core")
    everyone = nodes + ("ens",)
    shard = w_attn.shape[0]
    node_rows = members.shape[1]
    rows = GROUP * node_rows
    part = node_rows // members_num
    up = [(i, i + 1) for i in range(halves - 1)]
    down = [(target, source) for source, target in up]
    ens = lax.axis_index("ens")
    width = LATENT_DIM + FIELD_PAD
    paired = members_num == 2
    copies = 1 if paired else members_num
    source_parts = 2 if paired else 1

    normed, columns, packed, *sources = call(
        prepare_kernel,
        "prepare",
        [
            ((node_rows + NOTE_ROWS, LATENT_DIM), BF16),
            ((halves, GROUP, copies, shard, 3 * COLS), BF16),
            ((shard, width), BF16),
        ]
        + [((1 if paired else members_num, part, LATENT_DIM), BF16)] * source_parts,
        "shhhh",
        [
            pltpu.VMEM((node_rows, LATENT_DIM), BF16),
            pltpu.VMEM((node_rows + NOTE_ROWS, LATENT_DIM), BF16),
            pltpu.VMEM(w_attn.shape, BF16),
            pltpu.VMEM((GROUP, shard, 3 * COLS), BF16),
            pltpu.VMEM(readout_matrix.shape, BF16),
            pltpu.VMEM((shard, width), BF16),
            pltpu.SemaphoreType.DMA((6 + max(2, members_num) + halves * copies,)),
        ],
        flops=2**20,
        moved=2**20,
        results="hhh" + "h" * source_parts,
    )(neighbours, members.reshape(node_rows, LATENT_DIM), w_attn, w_mix, readout_matrix)

    packed, normed = lax.optimization_barrier((in_order(packed, "half", 0), normed))
    near = [normed] + [swap(normed, "quad", step) for step in range(1, QUAD)]
    if paired:
        columns = exchange(columns.reshape(-1, shard, 3 * COLS), nodes)
        columns = [columns, swap(columns, "ens", 1)]
    else:
        columns = [exchange(columns.reshape(-1, shard, 3 * COLS), everyone)]
        columns = [columns[0].reshape(LATENT_DIM, 3 * COLS)]
    far = [swap(piece, "core", 1) for piece in near]
    normed, steps = call(
        collect_kernel,
        "collect",
        [((rows, LATENT_DIM), BF16), ((GROUP, NOTE_ROWS, 128), F32)],
        "a" * (2 * QUAD),
        [pltpu.VMEM((GROUP, NOTE_ROWS, 128), BF16), pltpu.SemaphoreType.DMA((2 * GROUP,))],
        moved=4 * 2**20,
        results="hv",
    )(*near, *far)

    packed = in_order(packed, "ens", 1).reshape(halves, members_num * shard, width)
    if paired:
        sources = [sources[0], swap(sources[1], "ens", 1)]
        columns[1], sources[1] = lax.optimization_barrier((columns[1], sources[1]))
    else:
        sources = [exchange(sources[0], "ens")]
    packed, far[3], columns[0] = lax.optimization_barrier((packed, far[3], columns[0]))
    pieces = [packed] + [swap(packed, "quad", step) for step in range(1, QUAD)]

    rim = ((RIM, 2 * COLS), BF16)
    rims = [rim] if halves == 2 else [rim, rim]
    w_shape = (GROUP * halves, 2, shard, 3 * COLS) if paired else (LATENT_DIM, 3 * COLS)
    weights, *inner = call(
        rims_kernel,
        "project_rims",
        [(w_shape, BF16)] + rims,
        "h" + "a" * len(columns),
        [pltpu.VMEM((len(rims), RIM, LATENT_DIM), BF16), pltpu.SemaphoreType.DMA((4,))],
        flops=RIM * LATENT_DIM * 4 * COLS,
        moved=2**20,
    )(normed, *columns)
    def across(inner):
        if halves == 2:
            got = swap(inner[0], "half", 1)
            return got, got
        return lax.ppermute(inner[1], "half", up), lax.ppermute(inner[0], "half", down)

    low, high = across(inner)
    queries, own = call(
        project_kernel,
        "project",
        [((rows, COLS), BF16), ((rows, 2 * COLS), BF16)],
        "hv",
        [pltpu.VMEM((rows, LATENT_DIM), BF16), pltpu.SemaphoreType.DMA((CHUNKS,))],
        flops=rows * LATENT_DIM * 6 * COLS,
        moved=4 * 2**20,
    )(normed, weights)

    (outcome,) = call(
        interior_kernel,
        "attention_interior",
        [((rows, COLS), BF16)],
        "vvv",
        flops=rows * COLS * 2048,
        moved=2**21,
        exps=rows * 512,
    )(steps, queries, own)
    (outcome,) = call(
        edge_kernel,
        "attention_edges",
        [((rows, COLS), BF16)],
        "vvvvvv",
        flops=rows * COLS * 512,
        moved=2**20,
        exps=rows * 128,
    )(steps, queries, own, low, high, outcome)
    *pieces, own = lax.optimization_barrier((*pieces, own))
    pieces = pieces + [swap(piece, "core", 1) for piece in pieces]
    attended = exchange(outcome.reshape(GROUP * members_num, part, COLS), ("quad", "core", "ens"))
    block = (halves, QUAD, CORES, members_num * shard, width)
    (weights,) = call(
        assemble_kernel,
        "assemble",
        [(block, BF16)],
        "a" * len(pieces),
        [pltpu.SemaphoreType.DMA((GROUP,))],
        moved=4 * 2**20,
        results="h",
    )(*pieces)

    prediction, grads = call(
        mix_kernel,
        "mix_loss_backward",
        [((FIELD_NUM, node_rows), F32), ((GROUP * members_num, part, COLS), BF16)],
        "vvhh" + "a" * len(sources),
        [
            pltpu.VMEM((node_rows, LATENT_DIM), BF16),
            pltpu.VMEM(observed_truth.shape, F32),
            pltpu.VMEM((FIELD_PAD, node_rows), F32),
            pltpu.VMEM((members_num, part, LATENT_DIM), BF16),
            pltpu.VMEM(block, BF16),
            pltpu.SemaphoreType.DMA((halves + 1 + len(sources),)),
        ],
        flops=node_rows * LATENT_DIM * 4 * width,
        moved=2**22,
        room=14,
    )(attended, cell_surface_factor[None], observed_truth, weights, *sources)
    grads = exchange(grads, ("quad", "core", "ens")).reshape(rows, COLS)

    edges, *inner = call(
        edge_back_kernel,
        "attention_edges_back",
        [((2, WINDOW - RIM, 2 * COLS), F32)] + rims,
        "vvvvvv",
        flops=rows * COLS * 1280,
        moved=2**20,
        exps=rows * 128,
    )(steps, queries, own, low, high, grads)
    from_low, from_high = across(inner)
    (kv_grads,) = call(
        interior_back_kernel,
        "attention_interior_back",
        [((rows, 2 * COLS), F32)],
        "vvvvv",
        flops=rows * COLS * 4096,
        moved=2**22,
        exps=rows * 512,
        room=10,
    )(steps, queries, own, grads, edges)
    (term,) = call(
        product_kernel,
        "product",
        [((LATENT_DIM, 2 * COLS), BF16)],
        "vvvv",
        flops=rows * LATENT_DIM * 8 * COLS,
        moved=2**22,
        room=16,
    )(normed, from_low, from_high, kv_grads)
    term, prediction = lax.optimization_barrier((term, prediction))
    term = exchange(term.reshape(-1, shard, 2 * COLS), everyone)
    (grad_kv,) = call(
        gather_kernel, "gather_sums", [((shard, 2 * LATENT_DIM), F32)], "v", flops=2**17, moved=2**20
    )(term.reshape(halves, GROUP, members_num, shard, 2 * COLS))

    if members_num == 2:
        got = jnp.roll(swap(prediction, "ens", 1), part, axis=1)
        lane = lax.broadcasted_iota(jnp.int32, prediction.shape, 1)
        prediction = jnp.where(lane // part == ens, prediction, got)
    else:
        prediction = prediction.reshape(FIELD_NUM, members_num, part).transpose(1, 0, 2)
        prediction = exchange(prediction, "ens").transpose(1, 0, 2)
    return (prediction.reshape(1, FIELD_NUM, node_rows), grad_kv)


def solution(mesh):
    space, ens = mesh.shape["space"], mesh.shape["ens"]
    split = Mesh(
        mesh.devices.reshape(space // GROUP, QUAD, CORES, ens), ("half", "quad", "core", "ens")
    )
    nodes = ("half", "quad", "core")
    shards = nodes + ("ens",)
    in_specs = (
        P("ens", nodes, None),
        P(shards, None),
        P(shards, None),
        P(shards, None),
        P(None, nodes),
        P(nodes),
        P(nodes, None),
    )
    out_specs = (P("ens", None, nodes), P(shards, None))
    return jax.shard_map(body, mesh=split, in_specs=in_specs, out_specs=out_specs, check_vma=False)
```

```python
import functools

import jax
import jax.numpy as jnp
from jax import lax
from jax.experimental import pallas as pl
from jax.experimental.pallas import tpu as pltpu
from jax.sharding import Mesh
from jax.sharding import PartitionSpec as P

LATENT_DIM = 1024
HEADS = 16
HEAD = 64
FIELD_NUM = 100
TILE = 64
RADIUS = 2
K_NB = 4
QUAD = 4
CORES = 2
GROUP = QUAD * CORES
COLS = LATENT_DIM // GROUP
RIM = RADIUS * TILE
FIELD_PAD = 128
PAIR = 2
WINDOW = (PAIR + 2 * RADIUS) * TILE
NOWHERE = 100
NOTE_ROWS = 16
CHUNKS = 4

NORM_EPS = 1e-06
SOFT_WIDTH = 0.0625
MASKED = -1e30

F32 = jnp.float32
BF16 = jnp.bfloat16

VMEM = pl.BlockSpec(memory_space=pltpu.VMEM)
SMEM = pl.BlockSpec(memory_space=pltpu.SMEM)
HBM = pl.BlockSpec(memory_space=pltpu.HBM)
ANYWHERE = pl.BlockSpec(memory_space=pl.ANY)
OVER_ROWS = (((0,), (0,)), ((), ()))
OVER_COLUMNS = (((1,), (1,)), ((), ()))


def call(kernel, name, outs, ins, scratch=(), flops=0, moved=0, exps=0, room=8, results=None):
    results = results or "v" * len(outs)
    spaces = {"s": SMEM, "v": VMEM, "h": HBM, "a": ANYWHERE}
    made = pl.pallas_call(
        kernel,
        out_shape=[
            pltpu.HBM(shape, kind) if space == "h" else jax.ShapeDtypeStruct(shape, kind)
            for (shape, kind), space in zip(outs, results)
        ],
        in_specs=[spaces[space] for space in ins],
        out_specs=[spaces[space] for space in results],
        scratch_shapes=list(scratch),
        compiler_params=pltpu.CompilerParams(vmem_limit_bytes=room * 2**20),
        cost_estimate=pl.CostEstimate(flops=flops, bytes_accessed=moved, transcendentals=exps),
        name=name,
    )

    def run(*args):
        return made(
            *[
                pltpu.with_memory_space_constraint(arg, pltpu.HBM) if space == "h" else arg
                for arg, space in zip(args, ins)
            ]
        )

    return run


def fetch(pairs, sems, first=0):
    copies = [
        pltpu.make_async_copy(source, target, sems.at[first + at])
        for at, (source, target) in enumerate(pairs)
    ]
    for copy in copies:
        copy.start()
    return copies


def wait(copies):
    for copy in copies:
        copy.wait()


def weights_kernel(w_any, mix_any, readout_any, columns_any, packed_any, *refs):
    w, columns, readout, packed, sems = refs
    copies = fetch(
        [(w_any, w), (readout_any, readout), (mix_any, packed.at[:, :LATENT_DIM])], sems
    )
    copies[0].wait()
    for g in range(GROUP):
        for part in range(3):
            at = (part * GROUP + g) * COLS
            columns[g, :, part * COLS : (part + 1) * COLS] = w[:, at : at + COLS]
    halves, _, members_num = columns_any.shape[:3]
    out = fetch(
        [
            (columns, columns_any.at[half, :, m])
            for half in range(halves)
            for m in range(members_num)
        ],
        sems,
        3,
    )
    wait(copies[1:])
    packed[:, LATENT_DIM:] = jnp.zeros((packed.shape[0], FIELD_PAD), BF16)
    packed[:, LATENT_DIM : LATENT_DIM + FIELD_NUM] = readout[...]
    wait(out + fetch([(packed, packed_any)], sems, 3 + len(out)))


def norm_kernel(near_any, source_any, normed_any, *refs):
    parts, (near, source, normed, sems) = refs[:-4], refs[-4:]
    ens = lax.axis_index("ens")
    copies = fetch([(source_any, source), (near_any, near)], sems)
    rows = source.shape[0]
    copies[0].wait()
    moves = []
    for step, part_any in enumerate(parts):
        count, part, _ = part_any.shape
        for m in range(count):
            place = (ens ^ step) if len(parts) == 2 else m
            place = pl.multiple_of(place * part, part)
            moves.append((source.at[pl.ds(place, part)], part_any.at[m]))
    out = fetch(moves, sems, 2)
    states = source[...].astype(F32)
    inverse = lax.rsqrt(jnp.mean(states * states, axis=-1, keepdims=True) + NORM_EPS)
    normed[:rows, :] = (states * inverse).astype(BF16)
    copies[1].wait()
    row = lax.broadcasted_iota(jnp.int32, (NOTE_ROWS, 128), 0)
    lane = lax.broadcasted_iota(jnp.int32, (NOTE_ROWS, 128), 1)
    note = jnp.zeros((NOTE_ROWS, 128), F32)
    tiles = near.shape[0]
    first_tile = lax.axis_index(("half", "quad", "core")) * tiles
    for tile in range(tiles):
        for slot in range(K_NB):
            at = near[tile, slot]
            step = jnp.where(at >= 0, at - first_tile - tile, NOWHERE).astype(F32)
            note = jnp.where((row == tile) & (lane == slot), step, note)
    normed[rows:, :] = jnp.zeros((NOTE_ROWS, LATENT_DIM), BF16)
    normed[rows:, :128] = note.astype(BF16)
    wait(out + fetch([(normed, normed_any)], sems, 2 + len(out)))


def owners():
    core, quad = lax.axis_index("core"), lax.axis_index("quad")
    return [(quad ^ step) * CORES + (core ^ flip) for flip in range(CORES) for step in range(QUAD)]


def collect_kernel(*refs):
    blocks, (normed_any, steps_ref, notes, sems) = refs[:GROUP], refs[GROUP:]
    block = blocks[0].shape[0] - NOTE_ROWS
    pairs = []
    for rows_ref, owner in zip(blocks, owners()):
        place = pl.ds(pl.multiple_of(owner * block, block), block)
        pairs.append((rows_ref.at[:block], normed_any.at[place]))
        pairs.append((rows_ref.at[block:, :128], notes.at[owner]))
    wait(fetch(pairs, sems))
    steps_ref[...] = notes[...].astype(F32)


def put_rims(rims, first, last):
    if len(rims) == 1:
        rims[0][...] = jnp.where(lax.axis_index("half") == 0, last, first)
    else:
        rims[0][...], rims[1][...] = first, last


def rims_kernel(normed_any, *refs):
    rows, sems = refs[-2:]
    if len(refs[0].shape) == 2:
        columns, w, rims = refs[:1], refs[1], refs[2:-2]
        pairs = [(columns[0], w)]
    else:
        columns, w, rims = refs[:2], refs[2], refs[3:-2]
        ens = lax.axis_index("ens")
        pairs = [(part, w.at[:, ens ^ step]) for step, part in enumerate(columns)]
    last = normed_any.shape[0] - RIM
    if len(rims) == 1:
        place = pl.multiple_of(jnp.where(lax.axis_index("half") == 0, last, 0), RIM)
        pairs.append((normed_any.at[pl.ds(place, RIM)], rows.at[0]))
    else:
        pairs += [(normed_any.at[:RIM], rows.at[0]), (normed_any.at[last:], rows.at[1])]
    wait(fetch(pairs, sems))
    weights = w[...].reshape(LATENT_DIM, 3 * COLS)[:, COLS:]
    for at, rim_ref in enumerate(rims):
        rim_ref[...] = jnp.dot(rows[at], weights, preferred_element_type=F32).astype(BF16)


def project_kernel(normed_any, w_ref, q_ref, kv_ref, normed, sems):
    chunk = normed.shape[0] // CHUNKS
    rows = [slice(at * chunk, (at + 1) * chunk) for at in range(CHUNKS)]
    copies = fetch([(normed_any.at[part], normed.at[part]) for part in rows], sems)
    weights = w_ref[...].reshape(LATENT_DIM, 3 * COLS)
    for part, copy in zip(rows, copies):
        copy.wait()
        projected = jnp.dot(normed[part, :], weights, preferred_element_type=F32).astype(BF16)
        q_ref[part, :] = projected[:, :COLS] * jnp.asarray(HEAD**-0.5, BF16)
        kv_ref[part, :] = projected[:, COLS:]


def assemble_kernel(*refs):
    pieces, (w_any, sems) = refs[:GROUP], refs[GROUP:]
    core, quad = lax.axis_index("core"), lax.axis_index("quad")
    pairs = [
        (piece, w_any.at[:, quad ^ (at % QUAD), core ^ (at // QUAD)])
        for at, piece in enumerate(pieces)
    ]
    wait(fetch(pairs, sems))


def by_head(rows):
    lane = lax.broadcasted_iota(jnp.int32, rows.shape, 1)
    zero = jnp.zeros_like(rows)
    return jnp.concatenate(
        [jnp.where(lane < HEAD, rows, zero), jnp.where(lane < HEAD, zero, rows)], axis=0
    )


def usable_keys(steps_ref, pair):
    lane = (lax.broadcasted_iota(jnp.int32, (1, WINDOW), 1) // TILE - RADIUS).astype(F32)
    masks = []
    for query_tile in range(PAIR):
        found = jnp.zeros((1, WINDOW), F32)
        for slot in range(K_NB):
            step = steps_ref[pair, query_tile : query_tile + 1, slot : slot + 1]
            found = jnp.where(lane - query_tile == step, 1.0, found)
        masks.append(found)
    row = lax.broadcasted_iota(jnp.int32, (2 * PAIR * TILE, 1), 0) // TILE % PAIR
    return jnp.where(row == 0, masks[0], masks[1]) > 0


def raised_scores(queries, keys, usable):
    scores = lax.dot_general(queries, keys, OVER_COLUMNS, preferred_element_type=F32)
    scores = jnp.where(usable, scores, MASKED)
    raised = jnp.exp(scores - jnp.max(scores, axis=-1, keepdims=True))
    return raised, 1.0 / jnp.sum(raised, axis=-1, keepdims=True)


def attend(steps_ref, pair, queries, keys, values):
    raised, share = raised_scores(by_head(queries), keys, usable_keys(steps_ref, pair))
    both = jnp.dot(raised.astype(BF16), values, preferred_element_type=F32) * share
    lane = lax.broadcasted_iota(jnp.int32, queries.shape, 1)
    half = PAIR * TILE
    return jnp.where(lane < HEAD, both[:half], both[half:]).astype(BF16)


def interior_kernel(steps_ref, q_ref, kv_ref, out_ref):
    step = PAIR * TILE
    pairs = q_ref.shape[0] // step
    for pair in range(1, pairs - 1):
        window = slice((pair - 1) * step, (pair + 2) * step)
        rows = slice(pair * step, (pair + 1) * step)
        out_ref[rows, :] = attend(
            steps_ref, pair, q_ref[rows, :], kv_ref[window, :COLS], kv_ref[window, COLS:]
        )


def edge_kernel(steps_ref, q_ref, kv_ref, low_ref, high_ref, done_ref, out_ref):
    step = PAIR * TILE
    count = q_ref.shape[0]
    pairs = count // step
    out_ref[step : count - step, :] = done_ref[step : count - step, :]
    first = jnp.concatenate([low_ref[...], kv_ref[: 2 * step, :]], axis=0)
    last = jnp.concatenate([kv_ref[count - 2 * step :, :], high_ref[...]], axis=0)
    for pair, window in ((0, first), (pairs - 1, last)):
        rows = slice(pair * step, (pair + 1) * step)
        out_ref[rows, :] = attend(
            steps_ref, pair, q_ref[rows, :], window[:, :COLS], window[:, COLS:]
        )


def attend_back(steps_ref, pair, queries, grads, keys, values):
    queries, grads = by_head(queries), by_head(grads)
    raised, share = raised_scores(queries, keys, usable_keys(steps_ref, pair))
    probs = raised * share
    grad_probs = lax.dot_general(grads, values, OVER_COLUMNS, preferred_element_type=F32)
    row_delta = jnp.sum(probs * grad_probs, axis=-1, keepdims=True)
    grad_scores = (probs * (grad_probs - row_delta)).astype(BF16)
    key_grad = lax.dot_general(grad_scores, queries, OVER_ROWS, preferred_element_type=F32)
    value_grad = lax.dot_general(probs.astype(BF16), grads, OVER_ROWS, preferred_element_type=F32)
    return key_grad, value_grad


def edge_back_kernel(
    steps_ref, q_ref, kv_ref, low_ref, high_ref, g_ref, part_ref, *rims
):
    outer = []
    step = PAIR * TILE
    count = q_ref.shape[0]
    first = jnp.concatenate([low_ref[...], kv_ref[: 2 * step, :]], axis=0)
    last = jnp.concatenate([kv_ref[count - 2 * step :, :], high_ref[...]], axis=0)
    pairs = count // step
    for edge, pair, window in ((0, 0, first), (1, pairs - 1, last)):
        rows = slice(pair * step, (pair + 1) * step)
        grads = attend_back(
            steps_ref, pair, q_ref[rows, :], g_ref[rows, :], window[:, :COLS], window[:, COLS:]
        )
        rim = slice(0, RIM) if edge == 0 else slice(WINDOW - RIM, WINDOW)
        own = slice(RIM, WINDOW) if edge == 0 else slice(0, WINDOW - RIM)
        for at, grad in enumerate(grads):
            columns = slice(at * COLS, (at + 1) * COLS)
            part_ref[edge, :, columns] = grad[own]
        outer.append(jnp.concatenate([grad[rim].astype(BF16) for grad in grads], axis=1))
    put_rims(rims, *outer)


def interior_back_kernel(steps_ref, q_ref, kv_ref, g_ref, part_ref, out_ref):
    step = PAIR * TILE
    count = q_ref.shape[0]
    pairs = count // step
    reach = 2 * step
    out_ref[:reach, :] = part_ref[0]
    out_ref[reach : count - reach, :] = jnp.zeros((count - 2 * reach, 2 * COLS), F32)
    out_ref[count - reach :, :] = part_ref[1]
    for pair in range(1, pairs - 1):
        window = slice((pair - 1) * step, (pair + 2) * step)
        rows = slice(pair * step, (pair + 1) * step)
        key_grad, value_grad = attend_back(
            steps_ref,
            pair,
            q_ref[rows, :],
            g_ref[rows, :],
            kv_ref[window, :COLS],
            kv_ref[window, COLS:],
        )
        out_ref[window, :COLS] += key_grad
        out_ref[window, COLS:] += value_grad


def slope(spread):
    return spread * lax.rsqrt(spread * spread + SOFT_WIDTH)


def mix_kernel(att_ref, factor_ref, truth_any, w_any, *refs):
    sources, refs = refs[:-8], refs[-8:]
    pred_ref, grad_ref, a, truth_ref, truth, source, w, sems = refs
    members_num, part, _ = source.shape
    halves = w.shape[0]
    ens = lax.axis_index("ens")
    copies = fetch([(w_any.at[half], w.at[half]) for half in range(halves)], sems)
    pairs = [(truth_any, truth_ref)]
    if len(sources) == 1:
        pairs.append((sources[0], source))
    else:
        pairs += [(rows.at[0], source.at[ens ^ step]) for step, rows in enumerate(sources)]
    others = fetch(pairs, sems, halves)
    for g in range(GROUP):
        for m in range(members_num):
            a[m * part : (m + 1) * part, g * COLS : (g + 1) * COLS] = att_ref[g * members_num + m]
    wait(others)
    lane_part = lax.broadcasted_iota(jnp.int32, (1, a.shape[0]), 1) // part
    own_truth, own_factor = truth_ref[...], factor_ref[...]
    for turn in range(1, members_num):
        at = lane_part - turn
        here = jnp.where(at < 0, at + members_num, at) == ens
        own_truth = jnp.where(here, pltpu.roll(truth_ref[...], turn * part, 1), own_truth)
        own_factor = jnp.where(here, pltpu.roll(factor_ref[...], turn * part, 1), own_factor)
    truth[...] = jnp.zeros_like(truth)
    truth[:FIELD_NUM, :] = own_truth
    hidden = source[...].reshape(a.shape).astype(F32)
    count = LATENT_DIM // halves
    for half in range(halves):
        copies[half].wait()
        mix = w[half].reshape(count, LATENT_DIM + FIELD_PAD)[:, :LATENT_DIM]
        hidden += jnp.dot(
            a[:, half * count : (half + 1) * count], mix, preferred_element_type=F32
        )
    both = w[...].reshape(LATENT_DIM, LATENT_DIM + FIELD_PAD)
    mix, readout = both[:, :LATENT_DIM], both[:, LATENT_DIM:]
    inverse = lax.rsqrt(jnp.mean(hidden * hidden, axis=-1, keepdims=True) + NORM_EPS)
    decoded = (hidden * inverse).astype(BF16)
    prediction = lax.dot_general(
        readout, decoded, (((0,), (1,)), ((), ())), preferred_element_type=F32
    )
    pred_ref[...] = prediction[:FIELD_NUM]
    spread = jnp.zeros_like(prediction)
    for other in range(1, members_num):
        spread = spread + slope(prediction - pltpu.roll(prediction, other * part, 1))
    derivative = own_factor / FIELD_NUM * (
        slope(prediction - truth[...]) - spread / (members_num - 1)
    )
    grad_decoded = lax.dot_general(
        derivative.astype(BF16), readout, (((0,), (1,)), ((), ())), preferred_element_type=F32
    )
    grad_hidden = inverse * grad_decoded - hidden * inverse**3 * jnp.mean(
        grad_decoded * hidden, axis=-1, keepdims=True
    )
    grads = lax.dot_general(
        grad_hidden.astype(BF16), mix, OVER_COLUMNS, preferred_element_type=F32
    ).astype(BF16)
    for g in range(GROUP):
        for m in range(members_num):
            grad_ref[g * members_num + m] = grads[
                m * part : (m + 1) * part, g * COLS : (g + 1) * COLS
            ]


def product_kernel(normed_ref, from_low_ref, from_high_ref, grads_ref, out_ref):
    count = normed_ref.shape[0]
    half, last = lax.axis_index("half"), lax.axis_size("half") - 1
    from_low = jnp.where(half > 0, from_low_ref[...].astype(F32), 0.0)
    from_high = jnp.where(half < last, from_high_ref[...].astype(F32), 0.0)
    grads = grads_ref[...]
    grads = jnp.concatenate(
        [
            grads[:RIM] + from_low,
            grads[RIM : count - RIM],
            grads[count - RIM :] + from_high,
        ],
        axis=0,
    )
    high = grads.astype(BF16)
    low = (grads - high.astype(F32)).astype(BF16)
    both = lax.dot_general(
        normed_ref[...], jnp.concatenate([high, low], axis=1), OVER_ROWS, preferred_element_type=F32
    )
    out_ref[...] = (both[:, : 2 * COLS] + both[:, 2 * COLS :]).astype(BF16)


def gather_kernel(parts_ref, out_ref):
    halves, _, members_num = parts_ref.shape[:3]
    for g in range(GROUP):
        total = None
        for half in range(halves):
            for m in range(members_num):
                part = parts_ref[half, g, m].astype(F32)
                total = part if total is None else total + part
        out_ref[:, g * COLS : (g + 1) * COLS] = total[:, :COLS]
        out_ref[:, LATENT_DIM + g * COLS : LATENT_DIM + (g + 1) * COLS] = total[:, COLS:]


def exchange(chunks, axes):
    return lax.all_to_all(chunks, axes, 0, 0)


def swap(value, axis, step):
    return lax.ppermute(value, axis, [(i, i ^ step) for i in range(lax.axis_size(axis))])


def in_order(mine, axis, at):
    if lax.axis_size(axis) != 2:
        return lax.all_gather(mine, axis, axis=at)
    other = swap(mine, axis, 1)
    first = lax.axis_index(axis) == 0
    return jnp.stack([jnp.where(first, mine, other), jnp.where(first, other, mine)], axis=at)


def body(members, w_attn, w_mix, readout_matrix, observed_truth, cell_surface_factor, neighbours):
    halves, members_num = lax.axis_size("half"), lax.axis_size("ens")
    nodes = ("half", "quad", "core")
    everyone = nodes + ("ens",)
    shard = w_attn.shape[0]
    node_rows = members.shape[1]
    rows = GROUP * node_rows
    part = node_rows // members_num
    up = [(i, i + 1) for i in range(halves - 1)]
    down = [(target, source) for source, target in up]
    ens = lax.axis_index("ens")
    width = LATENT_DIM + FIELD_PAD
    paired = members_num == 2
    copies = 1 if paired else members_num
    source_parts = 2 if paired else 1

    columns, packed = call(
        weights_kernel,
        "prepare_weights",
        [((halves, GROUP, copies, shard, 3 * COLS), BF16), ((shard, width), BF16)],
        "hhh",
        [
            pltpu.VMEM(w_attn.shape, BF16),
            pltpu.VMEM((GROUP, shard, 3 * COLS), BF16),
            pltpu.VMEM(readout_matrix.shape, BF16),
            pltpu.VMEM((shard, width), BF16),
            pltpu.SemaphoreType.DMA((4 + halves * copies,)),
        ],
        moved=2**20,
        results="hh",
    )(w_attn, w_mix, readout_matrix)
    normed, *sources = call(
        norm_kernel,
        "norm",
        [((node_rows + NOTE_ROWS, LATENT_DIM), BF16)]
        + [((1 if paired else members_num, part, LATENT_DIM), BF16)] * source_parts,
        "hh",
        [
            pltpu.SMEM(neighbours.shape, jnp.int32),
            pltpu.VMEM((node_rows, LATENT_DIM), BF16),
            pltpu.VMEM((node_rows + NOTE_ROWS, LATENT_DIM), BF16),
            pltpu.SemaphoreType.DMA((3 + max(2, members_num),)),
        ],
        flops=2**20,
        moved=2**20,
        results="h" + "h" * source_parts,
    )(neighbours, members.reshape(node_rows, LATENT_DIM))

    packed, normed = lax.optimization_barrier((in_order(packed, "half", 0), normed))
    near = [normed, swap(normed, "quad", 1), None, swap(normed, "quad", 3)]
    if paired:
        columns = exchange(columns.reshape(-1, shard, 3 * COLS), nodes)
        columns, late = lax.optimization_barrier((columns, normed))
        columns = [columns, swap(columns, "ens", 1)]
    else:
        columns = [exchange(columns.reshape(-1, shard, 3 * COLS), everyone)]
        columns = [columns[0].reshape(LATENT_DIM, 3 * COLS)]
        late = normed
    near[2] = swap(late, "quad", 2)
    far = [swap(piece, "core", 1) for piece in near]
    normed, steps = call(
        collect_kernel,
        "collect",
        [((rows, LATENT_DIM), BF16), ((GROUP, NOTE_ROWS, 128), F32)],
        "a" * (2 * QUAD),
        [pltpu.VMEM((GROUP, NOTE_ROWS, 128), BF16), pltpu.SemaphoreType.DMA((2 * GROUP,))],
        moved=4 * 2**20,
        results="hv",
    )(*near, *far)

    packed = in_order(packed, "ens", 1).reshape(halves, members_num * shard, width)
    if paired:
        sources = [sources[0], swap(sources[1], "ens", 1)]
        columns[1], sources[1] = lax.optimization_barrier((columns[1], sources[1]))
    else:
        sources = [exchange(sources[0], "ens")]
    packed, near[2] = lax.optimization_barrier((packed, near[2]))
    pieces = [packed] + [swap(packed, "quad", step) for step in range(1, QUAD)]

    rim = ((RIM, 2 * COLS), BF16)
    rims = [rim] if halves == 2 else [rim, rim]
    w_shape = (GROUP * halves, 2, shard, 3 * COLS) if paired else (LATENT_DIM, 3 * COLS)
    weights, *inner = call(
        rims_kernel,
        "project_rims",
        [(w_shape, BF16)] + rims,
        "h" + "a" * len(columns),
        [pltpu.VMEM((len(rims), RIM, LATENT_DIM), BF16), pltpu.SemaphoreType.DMA((4,))],
        flops=RIM * LATENT_DIM * 4 * COLS,
        moved=2**20,
    )(normed, *columns)
    def across(inner):
        if halves == 2:
            got = swap(inner[0], "half", 1)
            return got, got
        return lax.ppermute(inner[1], "half", up), lax.ppermute(inner[0], "half", down)

    low, high = across(inner)
    queries, own = call(
        project_kernel,
        "project",
        [((rows, COLS), BF16), ((rows, 2 * COLS), BF16)],
        "hv",
        [pltpu.VMEM((rows, LATENT_DIM), BF16), pltpu.SemaphoreType.DMA((CHUNKS,))],
        flops=rows * LATENT_DIM * 6 * COLS,
        moved=4 * 2**20,
    )(normed, weights)

    (outcome,) = call(
        interior_kernel,
        "attention_interior",
        [((rows, COLS), BF16)],
        "vvv",
        flops=rows * COLS * 2048,
        moved=2**21,
        exps=rows * 512,
    )(steps, queries, own)
    (outcome,) = call(
        edge_kernel,
        "attention_edges",
        [((rows, COLS), BF16)],
        "vvvvvv",
        flops=rows * COLS * 512,
        moved=2**20,
        exps=rows * 128,
    )(steps, queries, own, low, high, outcome)
    *pieces, own = lax.optimization_barrier((*pieces, own))
    pieces = pieces + [swap(piece, "core", 1) for piece in pieces]
    attended = exchange(outcome.reshape(GROUP * members_num, part, COLS), ("quad", "core", "ens"))
    block = (halves, QUAD, CORES, members_num * shard, width)
    (weights,) = call(
        assemble_kernel,
        "assemble",
        [(block, BF16)],
        "a" * len(pieces),
        [pltpu.SemaphoreType.DMA((GROUP,))],
        moved=4 * 2**20,
        results="h",
    )(*pieces)

    prediction, grads = call(
        mix_kernel,
        "mix_loss_backward",
        [((FIELD_NUM, node_rows), F32), ((GROUP * members_num, part, COLS), BF16)],
        "vvhh" + "a" * len(sources),
        [
            pltpu.VMEM((node_rows, LATENT_DIM), BF16),
            pltpu.VMEM(observed_truth.shape, F32),
            pltpu.VMEM((FIELD_PAD, node_rows), F32),
            pltpu.VMEM((members_num, part, LATENT_DIM), BF16),
            pltpu.VMEM(block, BF16),
            pltpu.SemaphoreType.DMA((halves + 1 + len(sources),)),
        ],
        flops=node_rows * LATENT_DIM * 4 * width,
        moved=2**22,
        room=14,
    )(attended, cell_surface_factor[None], observed_truth, weights, *sources)
    grads = exchange(grads, ("quad", "core", "ens")).reshape(rows, COLS)

    edges, *inner = call(
        edge_back_kernel,
        "attention_edges_back",
        [((2, WINDOW - RIM, 2 * COLS), F32)] + rims,
        "vvvvvv",
        flops=rows * COLS * 1280,
        moved=2**20,
        exps=rows * 128,
    )(steps, queries, own, low, high, grads)
    from_low, from_high = across(inner)
    (kv_grads,) = call(
        interior_back_kernel,
        "attention_interior_back",
        [((rows, 2 * COLS), F32)],
        "vvvvv",
        flops=rows * COLS * 4096,
        moved=2**22,
        exps=rows * 512,
        room=10,
    )(steps, queries, own, grads, edges)
    (term,) = call(
        product_kernel,
        "product",
        [((LATENT_DIM, 2 * COLS), BF16)],
        "vvvv",
        flops=rows * LATENT_DIM * 8 * COLS,
        moved=2**22,
        room=16,
    )(normed, from_low, from_high, kv_grads)
    term, prediction = lax.optimization_barrier((term, prediction))
    term = exchange(term.reshape(-1, shard, 2 * COLS), everyone)
    (grad_kv,) = call(
        gather_kernel, "gather_sums", [((shard, 2 * LATENT_DIM), F32)], "v", flops=2**17, moved=2**20
    )(term.reshape(halves, GROUP, members_num, shard, 2 * COLS))

    if members_num == 2:
        got = jnp.roll(swap(prediction, "ens", 1), part, axis=1)
        lane = lax.broadcasted_iota(jnp.int32, prediction.shape, 1)
        prediction = jnp.where(lane // part == ens, prediction, got)
    else:
        prediction = prediction.reshape(FIELD_NUM, members_num, part).transpose(1, 0, 2)
        prediction = exchange(prediction, "ens").transpose(1, 0, 2)
    return (prediction.reshape(1, FIELD_NUM, node_rows), grad_kv)


def solution(mesh):
    space, ens = mesh.shape["space"], mesh.shape["ens"]
    split = Mesh(
        mesh.devices.reshape(space // GROUP, QUAD, CORES, ens), ("half", "quad", "core", "ens")
    )
    nodes = ("half", "quad", "core")
    shards = nodes + ("ens",)
    in_specs = (
        P("ens", nodes, None),
        P(shards, None),
        P(shards, None),
        P(shards, None),
        P(None, nodes),
        P(nodes),
        P(nodes, None),
    )
    out_specs = (P("ens", None, nodes), P(shards, None))
    return jax.shard_map(body, mesh=split, in_specs=in_specs, out_specs=out_specs, check_vma=False)
```

```python
import functools

import jax
import jax.numpy as jnp
from jax import lax
from jax.experimental import pallas as pl
from jax.experimental.pallas import tpu as pltpu
from jax.sharding import Mesh
from jax.sharding import PartitionSpec as P

LATENT_DIM = 1024
HEADS = 16
HEAD = 64
FIELD_NUM = 100
TILE = 64
RADIUS = 2
K_NB = 4
QUAD = 4
CORES = 2
GROUP = QUAD * CORES
COLS = LATENT_DIM // GROUP
RIM = RADIUS * TILE
FIELD_PAD = 128
PAIR = 2
WINDOW = (PAIR + 2 * RADIUS) * TILE
NOWHERE = 100
NOTE_ROWS = 16
CHUNKS = 4

NORM_EPS = 1e-06
SOFT_WIDTH = 0.0625
MASKED = -1e30

F32 = jnp.float32
BF16 = jnp.bfloat16

VMEM = pl.BlockSpec(memory_space=pltpu.VMEM)
SMEM = pl.BlockSpec(memory_space=pltpu.SMEM)
HBM = pl.BlockSpec(memory_space=pltpu.HBM)
ANYWHERE = pl.BlockSpec(memory_space=pl.ANY)
OVER_ROWS = (((0,), (0,)), ((), ()))
OVER_COLUMNS = (((1,), (1,)), ((), ()))


def call(kernel, name, outs, ins, scratch=(), flops=0, moved=0, exps=0, room=8, results=None):
    results = results or "v" * len(outs)
    spaces = {"s": SMEM, "v": VMEM, "h": HBM, "a": ANYWHERE}
    made = pl.pallas_call(
        kernel,
        out_shape=[
            pltpu.HBM(shape, kind) if space == "h" else jax.ShapeDtypeStruct(shape, kind)
            for (shape, kind), space in zip(outs, results)
        ],
        in_specs=[spaces[space] for space in ins],
        out_specs=[spaces[space] for space in results],
        scratch_shapes=list(scratch),
        compiler_params=pltpu.CompilerParams(vmem_limit_bytes=room * 2**20),
        cost_estimate=pl.CostEstimate(flops=flops, bytes_accessed=moved, transcendentals=exps),
        name=name,
    )

    def run(*args):
        return made(
            *[
                pltpu.with_memory_space_constraint(arg, pltpu.HBM) if space == "h" else arg
                for arg, space in zip(args, ins)
            ]
        )

    return run


def fetch(pairs, sems, first=0):
    copies = [
        pltpu.make_async_copy(source, target, sems.at[first + at])
        for at, (source, target) in enumerate(pairs)
    ]
    for copy in copies:
        copy.start()
    return copies


def wait(copies):
    for copy in copies:
        copy.wait()


def weights_kernel(w_any, mix_any, readout_any, columns_any, packed_any, *refs):
    w, columns, readout, packed, sems = refs
    copies = fetch(
        [(w_any, w), (readout_any, readout), (mix_any, packed.at[:, :LATENT_DIM])], sems
    )
    copies[0].wait()
    for g in range(GROUP):
        for part in range(3):
            at = (part * GROUP + g) * COLS
            columns[g, :, part * COLS : (part + 1) * COLS] = w[:, at : at + COLS]
    halves, _, members_num = columns_any.shape[:3]
    out = fetch(
        [
            (columns, columns_any.at[half, :, m])
            for half in range(halves)
            for m in range(members_num)
        ],
        sems,
        3,
    )
    wait(copies[1:])
    packed[:, LATENT_DIM:] = jnp.zeros((packed.shape[0], FIELD_PAD), BF16)
    packed[:, LATENT_DIM : LATENT_DIM + FIELD_NUM] = readout[...]
    wait(out + fetch([(packed, packed_any)], sems, 3 + len(out)))


def norm_kernel(near_any, source_any, normed_any, *refs):
    parts, (near, source, normed, sems) = refs[:-4], refs[-4:]
    ens = lax.axis_index("ens")
    copies = fetch([(source_any, source), (near_any, near)], sems)
    rows = source.shape[0]
    copies[0].wait()
    moves = []
    for step, part_any in enumerate(parts):
        count, part, _ = part_any.shape
        for m in range(count):
            place = (ens ^ step) if len(parts) == 2 else m
            place = pl.multiple_of(place * part, part)
            moves.append((source.at[pl.ds(place, part)], part_any.at[m]))
    out = fetch(moves, sems, 2)
    states = source[...].astype(F32)
    inverse = lax.rsqrt(jnp.mean(states * states, axis=-1, keepdims=True) + NORM_EPS)
    normed[:rows, :] = (states * inverse).astype(BF16)
    copies[1].wait()
    row = lax.broadcasted_iota(jnp.int32, (NOTE_ROWS, 128), 0)
    lane = lax.broadcasted_iota(jnp.int32, (NOTE_ROWS, 128), 1)
    note = jnp.zeros((NOTE_ROWS, 128), F32)
    tiles = near.shape[0]
    first_tile = lax.axis_index(("half", "quad", "core")) * tiles
    for tile in range(tiles):
        for slot in range(K_NB):
            at = near[tile, slot]
            step = jnp.where(at >= 0, at - first_tile - tile, NOWHERE).astype(F32)
            note = jnp.where((row == tile) & (lane == slot), step, note)
    normed[rows:, :] = jnp.zeros((NOTE_ROWS, LATENT_DIM), BF16)
    normed[rows:, :128] = note.astype(BF16)
    wait(out + fetch([(normed, normed_any)], sems, 2 + len(out)))


def owners():
    core, quad = lax.axis_index("core"), lax.axis_index("quad")
    return [(quad ^ step) * CORES + (core ^ flip) for flip in range(CORES) for step in range(QUAD)]


def collect_kernel(*refs):
    blocks, (normed_any, steps_ref, notes, sems) = refs[:GROUP], refs[GROUP:]
    block = blocks[0].shape[0] - NOTE_ROWS
    pairs = []
    for rows_ref, owner in zip(blocks, owners()):
        place = pl.ds(pl.multiple_of(owner * block, block), block)
        pairs.append((rows_ref.at[:block], normed_any.at[place]))
        pairs.append((rows_ref.at[block:, :128], notes.at[owner]))
    wait(fetch(pairs, sems))
    steps_ref[...] = notes[...].astype(F32)


def put_rims(rims, first, last):
    if len(rims) == 1:
        rims[0][...] = jnp.where(lax.axis_index("half") == 0, last, first)
    else:
        rims[0][...], rims[1][...] = first, last


def rims_kernel(normed_any, *refs):
    rows, sems = refs[-2:]
    if len(refs[0].shape) == 2:
        columns, w, rims = refs[:1], refs[1], refs[2:-2]
        pairs = [(columns[0], w)]
    else:
        columns, w, rims = refs[:2], refs[2], refs[3:-2]
        ens = lax.axis_index("ens")
        pairs = [(part, w.at[:, ens ^ step]) for step, part in enumerate(columns)]
    last = normed_any.shape[0] - RIM
    if len(rims) == 1:
        place = pl.multiple_of(jnp.where(lax.axis_index("half") == 0, last, 0), RIM)
        pairs.append((normed_any.at[pl.ds(place, RIM)], rows.at[0]))
    else:
        pairs += [(normed_any.at[:RIM], rows.at[0]), (normed_any.at[last:], rows.at[1])]
    wait(fetch(pairs, sems))
    weights = w[...].reshape(LATENT_DIM, 3 * COLS)[:, COLS:]
    for at, rim_ref in enumerate(rims):
        rim_ref[...] = jnp.dot(rows[at], weights, preferred_element_type=F32).astype(BF16)


def project_kernel(normed_any, w_ref, q_ref, kv_ref, normed, sems):
    chunk = normed.shape[0] // CHUNKS
    rows = [slice(at * chunk, (at + 1) * chunk) for at in range(CHUNKS)]
    copies = fetch([(normed_any.at[part], normed.at[part]) for part in rows], sems)
    weights = w_ref[...].reshape(LATENT_DIM, 3 * COLS)
    for part, copy in zip(rows, copies):
        copy.wait()
        projected = jnp.dot(normed[part, :], weights, preferred_element_type=F32).astype(BF16)
        q_ref[part, :] = projected[:, :COLS] * jnp.asarray(HEAD**-0.5, BF16)
        kv_ref[part, :] = projected[:, COLS:]


def assemble_kernel(*refs):
    pieces, (w_any, sems) = refs[:GROUP], refs[GROUP:]
    core, quad = lax.axis_index("core"), lax.axis_index("quad")
    pairs = [
        (piece, w_any.at[:, quad ^ (at % QUAD), core ^ (at // QUAD)])
        for at, piece in enumerate(pieces)
    ]
    wait(fetch(pairs, sems))


def by_head(rows):
    lane = lax.broadcasted_iota(jnp.int32, rows.shape, 1)
    zero = jnp.zeros_like(rows)
    return jnp.concatenate(
        [jnp.where(lane < HEAD, rows, zero), jnp.where(lane < HEAD, zero, rows)], axis=0
    )


def usable_keys(steps_ref, pair):
    lane = (lax.broadcasted_iota(jnp.int32, (1, WINDOW), 1) // TILE - RADIUS).astype(F32)
    masks = []
    for query_tile in range(PAIR):
        found = jnp.zeros((1, WINDOW), F32)
        for slot in range(K_NB):
            step = steps_ref[pair, query_tile : query_tile + 1, slot : slot + 1]
            found = jnp.where(lane - query_tile == step, 1.0, found)
        masks.append(found)
    row = lax.broadcasted_iota(jnp.int32, (2 * PAIR * TILE, 1), 0) // TILE % PAIR
    return jnp.where(row == 0, masks[0], masks[1]) > 0


def raised_scores(queries, keys, usable):
    scores = lax.dot_general(queries, keys, OVER_COLUMNS, preferred_element_type=F32)
    scores = jnp.where(usable, scores, MASKED)
    raised = jnp.exp(scores - jnp.max(scores, axis=-1, keepdims=True))
    return raised, 1.0 / jnp.sum(raised, axis=-1, keepdims=True)


def attend(steps_ref, pair, queries, keys, values):
    raised, share = raised_scores(by_head(queries), keys, usable_keys(steps_ref, pair))
    both = jnp.dot(raised.astype(BF16), values, preferred_element_type=F32) * share
    lane = lax.broadcasted_iota(jnp.int32, queries.shape, 1)
    half = PAIR * TILE
    return jnp.where(lane < HEAD, both[:half], both[half:]).astype(BF16)


def interior_kernel(steps_ref, q_ref, kv_ref, out_ref):
    step = PAIR * TILE
    pairs = q_ref.shape[0] // step
    for pair in range(1, pairs - 1):
        window = slice((pair - 1) * step, (pair + 2) * step)
        rows = slice(pair * step, (pair + 1) * step)
        out_ref[rows, :] = attend(
            steps_ref, pair, q_ref[rows, :], kv_ref[window, :COLS], kv_ref[window, COLS:]
        )


def edge_kernel(steps_ref, q_ref, kv_ref, low_ref, high_ref, done_ref, out_ref):
    step = PAIR * TILE
    count = q_ref.shape[0]
    pairs = count // step
    out_ref[step : count - step, :] = done_ref[step : count - step, :]
    first = jnp.concatenate([low_ref[...], kv_ref[: 2 * step, :]], axis=0)
    last = jnp.concatenate([kv_ref[count - 2 * step :, :], high_ref[...]], axis=0)
    for pair, window in ((0, first), (pairs - 1, last)):
        rows = slice(pair * step, (pair + 1) * step)
        out_ref[rows, :] = attend(
            steps_ref, pair, q_ref[rows, :], window[:, :COLS], window[:, COLS:]
        )


def attend_back(steps_ref, pair, queries, grads, keys, values):
    queries, grads = by_head(queries), by_head(grads)
    raised, share = raised_scores(queries, keys, usable_keys(steps_ref, pair))
    probs = raised * share
    grad_probs = lax.dot_general(grads, values, OVER_COLUMNS, preferred_element_type=F32)
    row_delta = jnp.sum(probs * grad_probs, axis=-1, keepdims=True)
    grad_scores = (probs * (grad_probs - row_delta)).astype(BF16)
    key_grad = lax.dot_general(grad_scores, queries, OVER_ROWS, preferred_element_type=F32)
    value_grad = lax.dot_general(probs.astype(BF16), grads, OVER_ROWS, preferred_element_type=F32)
    return key_grad, value_grad


def edge_back_kernel(
    steps_ref, q_ref, kv_ref, low_ref, high_ref, g_ref, part_ref, *rims
):
    outer = []
    step = PAIR * TILE
    count = q_ref.shape[0]
    first = jnp.concatenate([low_ref[...], kv_ref[: 2 * step, :]], axis=0)
    last = jnp.concatenate([kv_ref[count - 2 * step :, :], high_ref[...]], axis=0)
    pairs = count // step
    for edge, pair, window in ((0, 0, first), (1, pairs - 1, last)):
        rows = slice(pair * step, (pair + 1) * step)
        grads = attend_back(
            steps_ref, pair, q_ref[rows, :], g_ref[rows, :], window[:, :COLS], window[:, COLS:]
        )
        rim = slice(0, RIM) if edge == 0 else slice(WINDOW - RIM, WINDOW)
        own = slice(RIM, WINDOW) if edge == 0 else slice(0, WINDOW - RIM)
        for at, grad in enumerate(grads):
            columns = slice(at * COLS, (at + 1) * COLS)
            part_ref[edge, :, columns] = grad[own]
        outer.append(jnp.concatenate([grad[rim].astype(BF16) for grad in grads], axis=1))
    put_rims(rims, *outer)


def interior_back_kernel(steps_ref, q_ref, kv_ref, g_ref, part_ref, out_ref):
    step = PAIR * TILE
    count = q_ref.shape[0]
    pairs = count // step
    reach = 2 * step
    out_ref[:reach, :] = part_ref[0]
    out_ref[reach : count - reach, :] = jnp.zeros((count - 2 * reach, 2 * COLS), F32)
    out_ref[count - reach :, :] = part_ref[1]
    for pair in range(1, pairs - 1):
        window = slice((pair - 1) * step, (pair + 2) * step)
        rows = slice(pair * step, (pair + 1) * step)
        key_grad, value_grad = attend_back(
            steps_ref,
            pair,
            q_ref[rows, :],
            g_ref[rows, :],
            kv_ref[window, :COLS],
            kv_ref[window, COLS:],
        )
        out_ref[window, :COLS] += key_grad
        out_ref[window, COLS:] += value_grad


def slope(spread):
    return spread * lax.rsqrt(spread * spread + SOFT_WIDTH)


def mix_kernel(att_ref, factor_ref, truth_any, w_any, *refs):
    sources, refs = refs[:-8], refs[-8:]
    pred_ref, grad_ref, a, truth_ref, truth, source, w, sems = refs
    members_num, part, _ = source.shape
    halves = w.shape[0]
    ens = lax.axis_index("ens")
    copies = fetch([(w_any.at[half], w.at[half]) for half in range(halves)], sems)
    pairs = [(truth_any, truth_ref)]
    if len(sources) == 1:
        pairs.append((sources[0], source))
    else:
        pairs += [(rows.at[0], source.at[ens ^ step]) for step, rows in enumerate(sources)]
    others = fetch(pairs, sems, halves)
    for g in range(GROUP):
        for m in range(members_num):
            a[m * part : (m + 1) * part, g * COLS : (g + 1) * COLS] = att_ref[g * members_num + m]
    wait(others)
    lane_part = lax.broadcasted_iota(jnp.int32, (1, a.shape[0]), 1) // part
    own_truth, own_factor = truth_ref[...], factor_ref[...]
    for turn in range(1, members_num):
        at = lane_part - turn
        here = jnp.where(at < 0, at + members_num, at) == ens
        own_truth = jnp.where(here, pltpu.roll(truth_ref[...], turn * part, 1), own_truth)
        own_factor = jnp.where(here, pltpu.roll(factor_ref[...], turn * part, 1), own_factor)
    truth[...] = jnp.zeros_like(truth)
    truth[:FIELD_NUM, :] = own_truth
    hidden = source[...].reshape(a.shape).astype(F32)
    count = LATENT_DIM // halves
    for half in range(halves):
        copies[half].wait()
        mix = w[half].reshape(count, LATENT_DIM + FIELD_PAD)[:, :LATENT_DIM]
        hidden += jnp.dot(
            a[:, half * count : (half + 1) * count], mix, preferred_element_type=F32
        )
    both = w[...].reshape(LATENT_DIM, LATENT_DIM + FIELD_PAD)
    mix, readout = both[:, :LATENT_DIM], both[:, LATENT_DIM:]
    inverse = lax.rsqrt(jnp.mean(hidden * hidden, axis=-1, keepdims=True) + NORM_EPS)
    decoded = (hidden * inverse).astype(BF16)
    prediction = lax.dot_general(
        readout, decoded, (((0,), (1,)), ((), ())), preferred_element_type=F32
    )
    pred_ref[...] = prediction[:FIELD_NUM]
    spread = jnp.zeros_like(prediction)
    for other in range(1, members_num):
        spread = spread + slope(prediction - pltpu.roll(prediction, other * part, 1))
    derivative = own_factor / FIELD_NUM * (
        slope(prediction - truth[...]) - spread / (members_num - 1)
    )
    grad_decoded = lax.dot_general(
        derivative.astype(BF16), readout, (((0,), (1,)), ((), ())), preferred_element_type=F32
    )
    grad_hidden = inverse * grad_decoded - hidden * inverse**3 * jnp.mean(
        grad_decoded * hidden, axis=-1, keepdims=True
    )
    grads = lax.dot_general(
        grad_hidden.astype(BF16), mix, OVER_COLUMNS, preferred_element_type=F32
    ).astype(BF16)
    for g in range(GROUP):
        for m in range(members_num):
            grad_ref[g * members_num + m] = grads[
                m * part : (m + 1) * part, g * COLS : (g + 1) * COLS
            ]


def product_kernel(normed_ref, from_low_ref, from_high_ref, grads_ref, out_ref):
    count = normed_ref.shape[0]
    half, last = lax.axis_index("half"), lax.axis_size("half") - 1
    from_low = jnp.where(half > 0, from_low_ref[...].astype(F32), 0.0)
    from_high = jnp.where(half < last, from_high_ref[...].astype(F32), 0.0)
    grads = grads_ref[...]
    grads = jnp.concatenate(
        [
            grads[:RIM] + from_low,
            grads[RIM : count - RIM],
            grads[count - RIM :] + from_high,
        ],
        axis=0,
    )
    high = grads.astype(BF16)
    low = (grads - high.astype(F32)).astype(BF16)
    both = lax.dot_general(
        normed_ref[...], jnp.concatenate([high, low], axis=1), OVER_ROWS, preferred_element_type=F32
    )
    out_ref[...] = (both[:, : 2 * COLS] + both[:, 2 * COLS :]).astype(BF16)


def gather_kernel(parts_ref, out_ref):
    halves, _, members_num = parts_ref.shape[:3]
    for g in range(GROUP):
        total = None
        for half in range(halves):
            for m in range(members_num):
                part = parts_ref[half, g, m].astype(F32)
                total = part if total is None else total + part
        out_ref[:, g * COLS : (g + 1) * COLS] = total[:, :COLS]
        out_ref[:, LATENT_DIM + g * COLS : LATENT_DIM + (g + 1) * COLS] = total[:, COLS:]


def exchange(chunks, axes):
    return lax.all_to_all(chunks, axes, 0, 0)


def swap(value, axis, step):
    return lax.ppermute(value, axis, [(i, i ^ step) for i in range(lax.axis_size(axis))])


def in_order(mine, axis, at):
    if lax.axis_size(axis) != 2:
        return lax.all_gather(mine, axis, axis=at)
    other = swap(mine, axis, 1)
    first = lax.axis_index(axis) == 0
    return jnp.stack([jnp.where(first, mine, other), jnp.where(first, other, mine)], axis=at)


def body(members, w_attn, w_mix, readout_matrix, observed_truth, cell_surface_factor, neighbours):
    halves, members_num = lax.axis_size("half"), lax.axis_size("ens")
    nodes = ("half", "quad", "core")
    everyone = nodes + ("ens",)
    shard = w_attn.shape[0]
    node_rows = members.shape[1]
    rows = GROUP * node_rows
    part = node_rows // members_num
    up = [(i, i + 1) for i in range(halves - 1)]
    down = [(target, source) for source, target in up]
    ens = lax.axis_index("ens")
    width = LATENT_DIM + FIELD_PAD
    paired = members_num == 2
    copies = 1 if paired else members_num
    source_parts = 2 if paired else 1

    columns, packed = call(
        weights_kernel,
        "prepare_weights",
        [((halves, GROUP, copies, shard, 3 * COLS), BF16), ((shard, width), BF16)],
        "hhh",
        [
            pltpu.VMEM(w_attn.shape, BF16),
            pltpu.VMEM((GROUP, shard, 3 * COLS), BF16),
            pltpu.VMEM(readout_matrix.shape, BF16),
            pltpu.VMEM((shard, width), BF16),
            pltpu.SemaphoreType.DMA((4 + halves * copies,)),
        ],
        moved=2**20,
        results="hh",
    )(w_attn, w_mix, readout_matrix)
    normed, *sources = call(
        norm_kernel,
        "norm",
        [((node_rows + NOTE_ROWS, LATENT_DIM), BF16)]
        + [((1 if paired else members_num, part, LATENT_DIM), BF16)] * source_parts,
        "hh",
        [
            pltpu.SMEM(neighbours.shape, jnp.int32),
            pltpu.VMEM((node_rows, LATENT_DIM), BF16),
            pltpu.VMEM((node_rows + NOTE_ROWS, LATENT_DIM), BF16),
            pltpu.SemaphoreType.DMA((3 + max(2, members_num),)),
        ],
        flops=2**20,
        moved=2**20,
        results="h" + "h" * source_parts,
    )(neighbours, members.reshape(node_rows, LATENT_DIM))

    packed, normed = lax.optimization_barrier((in_order(packed, "half", 0), normed))
    near = [normed, swap(normed, "quad", 1), None, swap(normed, "quad", 3)]
    if paired:
        columns = exchange(columns.reshape(-1, shard, 3 * COLS), nodes)
        packed = in_order(packed, "ens", 1)
        columns, late, packed = lax.optimization_barrier((columns, normed, packed))
        columns = [columns, swap(columns, "ens", 1)]
    else:
        columns = [exchange(columns.reshape(-1, shard, 3 * COLS), everyone)]
        columns = [columns[0].reshape(LATENT_DIM, 3 * COLS)]
        late = normed
        packed = in_order(packed, "ens", 1)
    near[2] = swap(late, "quad", 2)
    far = [swap(piece, "core", 1) for piece in near]
    normed, steps = call(
        collect_kernel,
        "collect",
        [((rows, LATENT_DIM), BF16), ((GROUP, NOTE_ROWS, 128), F32)],
        "a" * (2 * QUAD),
        [pltpu.VMEM((GROUP, NOTE_ROWS, 128), BF16), pltpu.SemaphoreType.DMA((2 * GROUP,))],
        moved=4 * 2**20,
        results="hv",
    )(*near, *far)

    packed = packed.reshape(halves, members_num * shard, width)
    packed, near[2] = lax.optimization_barrier((packed, near[2]))
    pieces = [packed] + [swap(packed, "quad", step) for step in range(1, QUAD)]

    rim = ((RIM, 2 * COLS), BF16)
    rims = [rim] if halves == 2 else [rim, rim]
    w_shape = (GROUP * halves, 2, shard, 3 * COLS) if paired else (LATENT_DIM, 3 * COLS)
    weights, *inner = call(
        rims_kernel,
        "project_rims",
        [(w_shape, BF16)] + rims,
        "h" + "a" * len(columns),
        [pltpu.VMEM((len(rims), RIM, LATENT_DIM), BF16), pltpu.SemaphoreType.DMA((4,))],
        flops=RIM * LATENT_DIM * 4 * COLS,
        moved=2**20,
    )(normed, *columns)
    def across(inner):
        if halves == 2:
            got = swap(inner[0], "half", 1)
            return got, got
        return lax.ppermute(inner[1], "half", up), lax.ppermute(inner[0], "half", down)

    low, high = across(inner)
    queries, own = call(
        project_kernel,
        "project",
        [((rows, COLS), BF16), ((rows, 2 * COLS), BF16)],
        "hv",
        [pltpu.VMEM((rows, LATENT_DIM), BF16), pltpu.SemaphoreType.DMA((CHUNKS,))],
        flops=rows * LATENT_DIM * 6 * COLS,
        moved=4 * 2**20,
    )(normed, weights)

    (outcome,) = call(
        interior_kernel,
        "attention_interior",
        [((rows, COLS), BF16)],
        "vvv",
        flops=rows * COLS * 2048,
        moved=2**21,
        exps=rows * 512,
    )(steps, queries, own)
    (outcome,) = call(
        edge_kernel,
        "attention_edges",
        [((rows, COLS), BF16)],
        "vvvvvv",
        flops=rows * COLS * 512,
        moved=2**20,
        exps=rows * 128,
    )(steps, queries, own, low, high, outcome)
    *pieces, sources[-1], own = lax.optimization_barrier((*pieces, sources[-1], own))
    if paired:
        sources[1] = swap(sources[1], "ens", 1)
    else:
        sources = [exchange(sources[0], "ens")]
    pieces = pieces + [swap(piece, "core", 1) for piece in pieces]
    attended = exchange(outcome.reshape(GROUP * members_num, part, COLS), ("quad", "core", "ens"))
    block = (halves, QUAD, CORES, members_num * shard, width)
    (weights,) = call(
        assemble_kernel,
        "assemble",
        [(block, BF16)],
        "a" * len(pieces),
        [pltpu.SemaphoreType.DMA((GROUP,))],
        moved=4 * 2**20,
        results="h",
    )(*pieces)

    prediction, grads = call(
        mix_kernel,
        "mix_loss_backward",
        [((FIELD_NUM, node_rows), F32), ((GROUP * members_num, part, COLS), BF16)],
        "vvhh" + "a" * len(sources),
        [
            pltpu.VMEM((node_rows, LATENT_DIM), BF16),
            pltpu.VMEM(observed_truth.shape, F32),
            pltpu.VMEM((FIELD_PAD, node_rows), F32),
            pltpu.VMEM((members_num, part, LATENT_DIM), BF16),
            pltpu.VMEM(block, BF16),
            pltpu.SemaphoreType.DMA((halves + 1 + len(sources),)),
        ],
        flops=node_rows * LATENT_DIM * 4 * width,
        moved=2**22,
        room=14,
    )(attended, cell_surface_factor[None], observed_truth, weights, *sources)
    grads = exchange(grads, ("quad", "core", "ens")).reshape(rows, COLS)

    edges, *inner = call(
        edge_back_kernel,
        "attention_edges_back",
        [((2, WINDOW - RIM, 2 * COLS), F32)] + rims,
        "vvvvvv",
        flops=rows * COLS * 1280,
        moved=2**20,
        exps=rows * 128,
    )(steps, queries, own, low, high, grads)
    from_low, from_high = across(inner)
    (kv_grads,) = call(
        interior_back_kernel,
        "attention_interior_back",
        [((rows, 2 * COLS), F32)],
        "vvvvv",
        flops=rows * COLS * 4096,
        moved=2**22,
        exps=rows * 512,
        room=10,
    )(steps, queries, own, grads, edges)
    (term,) = call(
        product_kernel,
        "product",
        [((LATENT_DIM, 2 * COLS), BF16)],
        "vvvv",
        flops=rows * LATENT_DIM * 8 * COLS,
        moved=2**22,
        room=16,
    )(normed, from_low, from_high, kv_grads)
    term, prediction = lax.optimization_barrier((term, prediction))
    term = exchange(term.reshape(-1, shard, 2 * COLS), everyone)
    (grad_kv,) = call(
        gather_kernel, "gather_sums", [((shard, 2 * LATENT_DIM), F32)], "v", flops=2**17, moved=2**20
    )(term.reshape(halves, GROUP, members_num, shard, 2 * COLS))

    if members_num == 2:
        got = jnp.roll(swap(prediction, "ens", 1), part, axis=1)
        lane = lax.broadcasted_iota(jnp.int32, prediction.shape, 1)
        prediction = jnp.where(lane // part == ens, prediction, got)
    else:
        prediction = prediction.reshape(FIELD_NUM, members_num, part).transpose(1, 0, 2)
        prediction = exchange(prediction, "ens").transpose(1, 0, 2)
    return (prediction.reshape(1, FIELD_NUM, node_rows), grad_kv)


def solution(mesh):
    space, ens = mesh.shape["space"], mesh.shape["ens"]
    split = Mesh(
        mesh.devices.reshape(space // GROUP, QUAD, CORES, ens), ("half", "quad", "core", "ens")
    )
    nodes = ("half", "quad", "core")
    shards = nodes + ("ens",)
    in_specs = (
        P("ens", nodes, None),
        P(shards, None),
        P(shards, None),
        P(shards, None),
        P(None, nodes),
        P(nodes),
        P(nodes, None),
    )
    out_specs = (P("ens", None, nodes), P(shards, None))
    return jax.shard_map(body, mesh=split, in_specs=in_specs, out_specs=out_specs, check_vma=False)
```

```python
import functools

import jax
import jax.numpy as jnp
from jax import lax
from jax.experimental import pallas as pl
from jax.experimental.pallas import tpu as pltpu
from jax.sharding import Mesh
from jax.sharding import PartitionSpec as P

LATENT_DIM = 1024
HEADS = 16
HEAD = 64
FIELD_NUM = 100
TILE = 64
RADIUS = 2
K_NB = 4
QUAD = 4
CORES = 2
GROUP = QUAD * CORES
COLS = LATENT_DIM // GROUP
RIM = RADIUS * TILE
FIELD_PAD = 128
PAIR = 2
WINDOW = (PAIR + 2 * RADIUS) * TILE
NOWHERE = 100
NOTE_ROWS = 16
CHUNKS = 4

NORM_EPS = 1e-06
SOFT_WIDTH = 0.0625
MASKED = -1e30

F32 = jnp.float32
BF16 = jnp.bfloat16

VMEM = pl.BlockSpec(memory_space=pltpu.VMEM)
SMEM = pl.BlockSpec(memory_space=pltpu.SMEM)
HBM = pl.BlockSpec(memory_space=pltpu.HBM)
ANYWHERE = pl.BlockSpec(memory_space=pl.ANY)
OVER_ROWS = (((0,), (0,)), ((), ()))
OVER_COLUMNS = (((1,), (1,)), ((), ()))


def call(kernel, name, outs, ins, scratch=(), flops=0, moved=0, exps=0, room=8, results=None):
    results = results or "v" * len(outs)
    spaces = {"s": SMEM, "v": VMEM, "h": HBM, "a": ANYWHERE}
    made = pl.pallas_call(
        kernel,
        out_shape=[
            pltpu.HBM(shape, kind) if space == "h" else jax.ShapeDtypeStruct(shape, kind)
            for (shape, kind), space in zip(outs, results)
        ],
        in_specs=[spaces[space] for space in ins],
        out_specs=[spaces[space] for space in results],
        scratch_shapes=list(scratch),
        compiler_params=pltpu.CompilerParams(vmem_limit_bytes=room * 2**20),
        cost_estimate=pl.CostEstimate(flops=flops, bytes_accessed=moved, transcendentals=exps),
        name=name,
    )

    def run(*args):
        return made(
            *[
                pltpu.with_memory_space_constraint(arg, pltpu.HBM) if space == "h" else arg
                for arg, space in zip(args, ins)
            ]
        )

    return run


def fetch(pairs, sems, first=0):
    copies = [
        pltpu.make_async_copy(source, target, sems.at[first + at])
        for at, (source, target) in enumerate(pairs)
    ]
    for copy in copies:
        copy.start()
    return copies


def wait(copies):
    for copy in copies:
        copy.wait()


def weights_kernel(w_any, mix_any, readout_any, columns_any, packed_any, *refs):
    w, columns, readout, packed, sems = refs
    copies = fetch(
        [(w_any, w), (readout_any, readout), (mix_any, packed.at[:, :LATENT_DIM])], sems
    )
    copies[0].wait()
    for g in range(GROUP):
        for part in range(3):
            at = (part * GROUP + g) * COLS
            columns[g, :, part * COLS : (part + 1) * COLS] = w[:, at : at + COLS]
    halves, _, members_num = columns_any.shape[:3]
    out = fetch(
        [
            (columns, columns_any.at[half, :, m])
            for half in range(halves)
            for m in range(members_num)
        ],
        sems,
        3,
    )
    wait(copies[1:])
    packed[:, LATENT_DIM:] = jnp.zeros((packed.shape[0], FIELD_PAD), BF16)
    packed[:, LATENT_DIM : LATENT_DIM + FIELD_NUM] = readout[...]
    wait(out + fetch([(packed, packed_any)], sems, 3 + len(out)))


def norm_kernel(near_any, source_any, normed_any, *refs):
    parts, (near, source, normed, sems) = refs[:-4], refs[-4:]
    ens = lax.axis_index("ens")
    copies = fetch([(source_any, source), (near_any, near)], sems)
    rows = source.shape[0]
    copies[0].wait()
    moves = []
    for step, part_any in enumerate(parts):
        count, part, _ = part_any.shape
        for m in range(count):
            place = (ens ^ step) if len(parts) == 2 else m
            place = pl.multiple_of(place * part, part)
            moves.append((source.at[pl.ds(place, part)], part_any.at[m]))
    out = fetch(moves, sems, 2)
    states = source[...].astype(F32)
    inverse = lax.rsqrt(jnp.mean(states * states, axis=-1, keepdims=True) + NORM_EPS)
    normed[:rows, :] = (states * inverse).astype(BF16)
    copies[1].wait()
    row = lax.broadcasted_iota(jnp.int32, (NOTE_ROWS, 128), 0)
    lane = lax.broadcasted_iota(jnp.int32, (NOTE_ROWS, 128), 1)
    note = jnp.zeros((NOTE_ROWS, 128), F32)
    tiles = near.shape[0]
    first_tile = lax.axis_index(("half", "quad", "core")) * tiles
    for tile in range(tiles):
        for slot in range(K_NB):
            at = near[tile, slot]
            step = jnp.where(at >= 0, at - first_tile - tile, NOWHERE).astype(F32)
            note = jnp.where((row == tile) & (lane == slot), step, note)
    normed[rows:, :] = jnp.zeros((NOTE_ROWS, LATENT_DIM), BF16)
    normed[rows:, :128] = note.astype(BF16)
    wait(out + fetch([(normed, normed_any)], sems, 2 + len(out)))


def owners():
    core, quad = lax.axis_index("core"), lax.axis_index("quad")
    return [(quad ^ step) * CORES + (core ^ flip) for flip in range(CORES) for step in range(QUAD)]


def collect_kernel(*refs):
    blocks, (normed_any, steps_ref, notes, sems) = refs[:GROUP], refs[GROUP:]
    block = blocks[0].shape[0] - NOTE_ROWS
    pairs = []
    for rows_ref, owner in zip(blocks, owners()):
        place = pl.ds(pl.multiple_of(owner * block, block), block)
        pairs.append((rows_ref.at[:block], normed_any.at[place]))
        pairs.append((rows_ref.at[block:, :128], notes.at[owner]))
    wait(fetch(pairs, sems))
    steps_ref[...] = notes[...].astype(F32)


def put_rims(rims, first, last):
    if len(rims) == 1:
        rims[0][...] = jnp.where(lax.axis_index("half") == 0, last, first)
    else:
        rims[0][...], rims[1][...] = first, last


def rims_kernel(normed_any, *refs):
    rows, sems = refs[-2:]
    if len(refs[0].shape) == 2:
        columns, w, rims = refs[:1], refs[1], refs[2:-2]
        pairs = [(columns[0], w)]
    else:
        columns, w, rims = refs[:2], refs[2], refs[3:-2]
        ens = lax.axis_index("ens")
        pairs = [(part, w.at[:, ens ^ step]) for step, part in enumerate(columns)]
    last = normed_any.shape[0] - RIM
    if len(rims) == 1:
        place = pl.multiple_of(jnp.where(lax.axis_index("half") == 0, last, 0), RIM)
        pairs.append((normed_any.at[pl.ds(place, RIM)], rows.at[0]))
    else:
        pairs += [(normed_any.at[:RIM], rows.at[0]), (normed_any.at[last:], rows.at[1])]
    wait(fetch(pairs, sems))
    weights = w[...].reshape(LATENT_DIM, 3 * COLS)[:, COLS:]
    for at, rim_ref in enumerate(rims):
        rim_ref[...] = jnp.dot(rows[at], weights, preferred_element_type=F32).astype(BF16)


def project_kernel(normed_any, w_ref, q_ref, kv_ref, normed, sems):
    chunk = normed.shape[0] // CHUNKS
    rows = [slice(at * chunk, (at + 1) * chunk) for at in range(CHUNKS)]
    copies = fetch([(normed_any.at[part], normed.at[part]) for part in rows], sems)
    weights = w_ref[...].reshape(LATENT_DIM, 3 * COLS)
    for part, copy in zip(rows, copies):
        copy.wait()
        projected = jnp.dot(normed[part, :], weights, preferred_element_type=F32).astype(BF16)
        q_ref[part, :] = projected[:, :COLS] * jnp.asarray(HEAD**-0.5, BF16)
        kv_ref[part, :] = projected[:, COLS:]


def assemble_kernel(*refs):
    pieces, (w_any, sems) = refs[:GROUP], refs[GROUP:]
    core, quad = lax.axis_index("core"), lax.axis_index("quad")
    pairs = [
        (piece, w_any.at[:, quad ^ (at % QUAD), core ^ (at // QUAD)])
        for at, piece in enumerate(pieces)
    ]
    wait(fetch(pairs, sems))


def by_head(rows):
    lane = lax.broadcasted_iota(jnp.int32, rows.shape, 1)
    zero = jnp.zeros_like(rows)
    return jnp.concatenate(
        [jnp.where(lane < HEAD, rows, zero), jnp.where(lane < HEAD, zero, rows)], axis=0
    )


def usable_keys(steps_ref, pair):
    lane = (lax.broadcasted_iota(jnp.int32, (1, WINDOW), 1) // TILE - RADIUS).astype(F32)
    masks = []
    for query_tile in range(PAIR):
        found = jnp.zeros((1, WINDOW), F32)
        for slot in range(K_NB):
            step = steps_ref[pair, query_tile : query_tile + 1, slot : slot + 1]
            found = jnp.where(lane - query_tile == step, 1.0, found)
        masks.append(found)
    row = lax.broadcasted_iota(jnp.int32, (2 * PAIR * TILE, 1), 0) // TILE % PAIR
    return jnp.where(row == 0, masks[0], masks[1]) > 0


def raised_scores(queries, keys, usable):
    scores = lax.dot_general(queries, keys, OVER_COLUMNS, preferred_element_type=F32)
    scores = jnp.where(usable, scores, MASKED)
    raised = jnp.exp(scores - jnp.max(scores, axis=-1, keepdims=True))
    return raised, 1.0 / jnp.sum(raised, axis=-1, keepdims=True)


def attend(steps_ref, pair, queries, keys, values):
    raised, share = raised_scores(by_head(queries), keys, usable_keys(steps_ref, pair))
    both = jnp.dot(raised.astype(BF16), values, preferred_element_type=F32) * share
    lane = lax.broadcasted_iota(jnp.int32, queries.shape, 1)
    half = PAIR * TILE
    return jnp.where(lane < HEAD, both[:half], both[half:]).astype(BF16)


def interior_kernel(steps_ref, q_ref, kv_ref, out_ref):
    step = PAIR * TILE
    pairs = q_ref.shape[0] // step
    for pair in range(1, pairs - 1):
        window = slice((pair - 1) * step, (pair + 2) * step)
        rows = slice(pair * step, (pair + 1) * step)
        out_ref[rows, :] = attend(
            steps_ref, pair, q_ref[rows, :], kv_ref[window, :COLS], kv_ref[window, COLS:]
        )


def edge_kernel(steps_ref, q_ref, kv_ref, low_ref, high_ref, done_ref, out_ref):
    step = PAIR * TILE
    count = q_ref.shape[0]
    pairs = count // step
    out_ref[step : count - step, :] = done_ref[step : count - step, :]
    first = jnp.concatenate([low_ref[...], kv_ref[: 2 * step, :]], axis=0)
    last = jnp.concatenate([kv_ref[count - 2 * step :, :], high_ref[...]], axis=0)
    for pair, window in ((0, first), (pairs - 1, last)):
        rows = slice(pair * step, (pair + 1) * step)
        out_ref[rows, :] = attend(
            steps_ref, pair, q_ref[rows, :], window[:, :COLS], window[:, COLS:]
        )


def attend_back(steps_ref, pair, queries, grads, keys, values):
    queries, grads = by_head(queries), by_head(grads)
    raised, share = raised_scores(queries, keys, usable_keys(steps_ref, pair))
    probs = raised * share
    grad_probs = lax.dot_general(grads, values, OVER_COLUMNS, preferred_element_type=F32)
    row_delta = jnp.sum(probs * grad_probs, axis=-1, keepdims=True)
    grad_scores = (probs * (grad_probs - row_delta)).astype(BF16)
    key_grad = lax.dot_general(grad_scores, queries, OVER_ROWS, preferred_element_type=F32)
    value_grad = lax.dot_general(probs.astype(BF16), grads, OVER_ROWS, preferred_element_type=F32)
    return key_grad, value_grad


def edge_back_kernel(
    steps_ref, q_ref, kv_ref, low_ref, high_ref, g_ref, part_ref, *rims
):
    outer = []
    step = PAIR * TILE
    count = q_ref.shape[0]
    first = jnp.concatenate([low_ref[...], kv_ref[: 2 * step, :]], axis=0)
    last = jnp.concatenate([kv_ref[count - 2 * step :, :], high_ref[...]], axis=0)
    pairs = count // step
    for edge, pair, window in ((0, 0, first), (1, pairs - 1, last)):
        rows = slice(pair * step, (pair + 1) * step)
        grads = attend_back(
            steps_ref, pair, q_ref[rows, :], g_ref[rows, :], window[:, :COLS], window[:, COLS:]
        )
        rim = slice(0, RIM) if edge == 0 else slice(WINDOW - RIM, WINDOW)
        own = slice(RIM, WINDOW) if edge == 0 else slice(0, WINDOW - RIM)
        for at, grad in enumerate(grads):
            columns = slice(at * COLS, (at + 1) * COLS)
            part_ref[edge, :, columns] = grad[own]
        outer.append(jnp.concatenate([grad[rim].astype(BF16) for grad in grads], axis=1))
    put_rims(rims, *outer)


def interior_back_kernel(steps_ref, q_ref, kv_ref, g_ref, part_ref, out_ref):
    step = PAIR * TILE
    count = q_ref.shape[0]
    pairs = count // step
    reach = 2 * step
    out_ref[:reach, :] = part_ref[0]
    out_ref[reach : count - reach, :] = jnp.zeros((count - 2 * reach, 2 * COLS), F32)
    out_ref[count - reach :, :] = part_ref[1]
    for pair in range(1, pairs - 1):
        window = slice((pair - 1) * step, (pair + 2) * step)
        rows = slice(pair * step, (pair + 1) * step)
        key_grad, value_grad = attend_back(
            steps_ref,
            pair,
            q_ref[rows, :],
            g_ref[rows, :],
            kv_ref[window, :COLS],
            kv_ref[window, COLS:],
        )
        out_ref[window, :COLS] += key_grad
        out_ref[window, COLS:] += value_grad


def slope(spread):
    return spread * lax.rsqrt(spread * spread + SOFT_WIDTH)


def mix_kernel(att_ref, factor_ref, truth_any, w_any, *refs):
    sources, refs = refs[:-8], refs[-8:]
    pred_ref, grad_ref, a, truth_ref, truth, source, w, sems = refs
    members_num, part, _ = source.shape
    halves = w.shape[0]
    ens = lax.axis_index("ens")
    copies = fetch([(w_any.at[half], w.at[half]) for half in range(halves)], sems)
    pairs = [(truth_any, truth_ref)]
    if len(sources) == 1:
        pairs.append((sources[0], source))
    else:
        pairs += [(rows.at[0], source.at[ens ^ step]) for step, rows in enumerate(sources)]
    others = fetch(pairs, sems, halves)
    for g in range(GROUP):
        for m in range(members_num):
            a[m * part : (m + 1) * part, g * COLS : (g + 1) * COLS] = att_ref[g * members_num + m]
    wait(others)
    lane_part = lax.broadcasted_iota(jnp.int32, (1, a.shape[0]), 1) // part
    own_truth, own_factor = truth_ref[...], factor_ref[...]
    for turn in range(1, members_num):
        at = lane_part - turn
        here = jnp.where(at < 0, at + members_num, at) == ens
        own_truth = jnp.where(here, pltpu.roll(truth_ref[...], turn * part, 1), own_truth)
        own_factor = jnp.where(here, pltpu.roll(factor_ref[...], turn * part, 1), own_factor)
    truth[...] = jnp.zeros_like(truth)
    truth[:FIELD_NUM, :] = own_truth
    hidden = source[...].reshape(a.shape).astype(F32)
    count = LATENT_DIM // halves
    for half in range(halves):
        copies[half].wait()
        mix = w[half].reshape(count, LATENT_DIM + FIELD_PAD)[:, :LATENT_DIM]
        hidden += jnp.dot(
            a[:, half * count : (half + 1) * count], mix, preferred_element_type=F32
        )
    both = w[...].reshape(LATENT_DIM, LATENT_DIM + FIELD_PAD)
    mix, readout = both[:, :LATENT_DIM], both[:, LATENT_DIM:]
    inverse = lax.rsqrt(jnp.mean(hidden * hidden, axis=-1, keepdims=True) + NORM_EPS)
    decoded = (hidden * inverse).astype(BF16)
    prediction = lax.dot_general(
        readout, decoded, (((0,), (1,)), ((), ())), preferred_element_type=F32
    )
    pred_ref[...] = prediction[:FIELD_NUM]
    spread = jnp.zeros_like(prediction)
    for other in range(1, members_num):
        spread = spread + slope(prediction - pltpu.roll(prediction, other * part, 1))
    derivative = own_factor / FIELD_NUM * (
        slope(prediction - truth[...]) - spread / (members_num - 1)
    )
    grad_decoded = lax.dot_general(
        derivative.astype(BF16), readout, (((0,), (1,)), ((), ())), preferred_element_type=F32
    )
    grad_hidden = inverse * grad_decoded - hidden * inverse**3 * jnp.mean(
        grad_decoded * hidden, axis=-1, keepdims=True
    )
    grads = lax.dot_general(
        grad_hidden.astype(BF16), mix, OVER_COLUMNS, preferred_element_type=F32
    ).astype(BF16)
    for g in range(GROUP):
        for m in range(members_num):
            grad_ref[g * members_num + m] = grads[
                m * part : (m + 1) * part, g * COLS : (g + 1) * COLS
            ]


def product_kernel(normed_ref, from_low_ref, from_high_ref, grads_ref, out_ref):
    count = normed_ref.shape[0]
    half, last = lax.axis_index("half"), lax.axis_size("half") - 1
    from_low = jnp.where(half > 0, from_low_ref[...].astype(F32), 0.0)
    from_high = jnp.where(half < last, from_high_ref[...].astype(F32), 0.0)
    grads = grads_ref[...]
    grads = jnp.concatenate(
        [
            grads[:RIM] + from_low,
            grads[RIM : count - RIM],
            grads[count - RIM :] + from_high,
        ],
        axis=0,
    )
    high = grads.astype(BF16)
    low = (grads - high.astype(F32)).astype(BF16)
    both = lax.dot_general(
        normed_ref[...], jnp.concatenate([high, low], axis=1), OVER_ROWS, preferred_element_type=F32
    )
    out_ref[...] = (both[:, : 2 * COLS] + both[:, 2 * COLS :]).astype(BF16)


def gather_kernel(parts_ref, out_ref):
    halves, _, members_num = parts_ref.shape[:3]
    for g in range(GROUP):
        total = None
        for half in range(halves):
            for m in range(members_num):
                part = parts_ref[half, g, m].astype(F32)
                total = part if total is None else total + part
        out_ref[:, g * COLS : (g + 1) * COLS] = total[:, :COLS]
        out_ref[:, LATENT_DIM + g * COLS : LATENT_DIM + (g + 1) * COLS] = total[:, COLS:]


def exchange(chunks, axes):
    return lax.all_to_all(chunks, axes, 0, 0)


def swap(value, axis, step):
    return lax.ppermute(value, axis, [(i, i ^ step) for i in range(lax.axis_size(axis))])


def in_order(mine, axis, at):
    if lax.axis_size(axis) != 2:
        return lax.all_gather(mine, axis, axis=at)
    other = swap(mine, axis, 1)
    first = lax.axis_index(axis) == 0
    return jnp.stack([jnp.where(first, mine, other), jnp.where(first, other, mine)], axis=at)


def body(members, w_attn, w_mix, readout_matrix, observed_truth, cell_surface_factor, neighbours):
    halves, members_num = lax.axis_size("half"), lax.axis_size("ens")
    nodes = ("half", "quad", "core")
    everyone = nodes + ("ens",)
    shard = w_attn.shape[0]
    node_rows = members.shape[1]
    rows = GROUP * node_rows
    part = node_rows // members_num
    up = [(i, i + 1) for i in range(halves - 1)]
    down = [(target, source) for source, target in up]
    ens = lax.axis_index("ens")
    width = LATENT_DIM + FIELD_PAD
    paired = members_num == 2
    copies = 1 if paired else members_num
    source_parts = 2 if paired else 1

    columns, packed = call(
        weights_kernel,
        "prepare_weights",
        [((halves, GROUP, copies, shard, 3 * COLS), BF16), ((shard, width), BF16)],
        "hhh",
        [
            pltpu.VMEM(w_attn.shape, BF16),
            pltpu.VMEM((GROUP, shard, 3 * COLS), BF16),
            pltpu.VMEM(readout_matrix.shape, BF16),
            pltpu.VMEM((shard, width), BF16),
            pltpu.SemaphoreType.DMA((4 + halves * copies,)),
        ],
        moved=2**20,
        results="hh",
    )(w_attn, w_mix, readout_matrix)
    normed, *sources = call(
        norm_kernel,
        "norm",
        [((node_rows + NOTE_ROWS, LATENT_DIM), BF16)]
        + [((1 if paired else members_num, part, LATENT_DIM), BF16)] * source_parts,
        "hh",
        [
            pltpu.SMEM(neighbours.shape, jnp.int32),
            pltpu.VMEM((node_rows, LATENT_DIM), BF16),
            pltpu.VMEM((node_rows + NOTE_ROWS, LATENT_DIM), BF16),
            pltpu.SemaphoreType.DMA((3 + max(2, members_num),)),
        ],
        flops=2**20,
        moved=2**20,
        results="h" + "h" * source_parts,
    )(neighbours, members.reshape(node_rows, LATENT_DIM))

    packed, normed = lax.optimization_barrier((in_order(packed, "half", 0), normed))
    near = [normed, swap(normed, "quad", 1), swap(normed, "quad", 2)]
    packed, last = lax.optimization_barrier((in_order(packed, "ens", 1), normed))
    near.append(swap(last, "quad", 3))
    if paired:
        columns = exchange(columns.reshape(-1, shard, 3 * COLS), nodes)
        columns = [columns, swap(columns, "ens", 1)]
    else:
        columns = [exchange(columns.reshape(-1, shard, 3 * COLS), everyone)]
        columns = [columns[0].reshape(LATENT_DIM, 3 * COLS)]
    far = [swap(piece, "core", 1) for piece in near]
    normed, steps = call(
        collect_kernel,
        "collect",
        [((rows, LATENT_DIM), BF16), ((GROUP, NOTE_ROWS, 128), F32)],
        "a" * (2 * QUAD),
        [pltpu.VMEM((GROUP, NOTE_ROWS, 128), BF16), pltpu.SemaphoreType.DMA((2 * GROUP,))],
        moved=4 * 2**20,
        results="hv",
    )(*near, *far)

    packed = packed.reshape(halves, members_num * shard, width)
    packed, near[2] = lax.optimization_barrier((packed, near[2]))
    pieces = [packed] + [swap(packed, "quad", step) for step in range(1, QUAD)]

    rim = ((RIM, 2 * COLS), BF16)
    rims = [rim] if halves == 2 else [rim, rim]
    w_shape = (GROUP * halves, 2, shard, 3 * COLS) if paired else (LATENT_DIM, 3 * COLS)
    weights, *inner = call(
        rims_kernel,
        "project_rims",
        [(w_shape, BF16)] + rims,
        "h" + "a" * len(columns),
        [pltpu.VMEM((len(rims), RIM, LATENT_DIM), BF16), pltpu.SemaphoreType.DMA((4,))],
        flops=RIM * LATENT_DIM * 4 * COLS,
        moved=2**20,
    )(normed, *columns)
    def across(inner):
        if halves == 2:
            got = swap(inner[0], "half", 1)
            return got, got
        return lax.ppermute(inner[1], "half", up), lax.ppermute(inner[0], "half", down)

    low, high = across(inner)
    queries, own = call(
        project_kernel,
        "project",
        [((rows, COLS), BF16), ((rows, 2 * COLS), BF16)],
        "hv",
        [pltpu.VMEM((rows, LATENT_DIM), BF16), pltpu.SemaphoreType.DMA((CHUNKS,))],
        flops=rows * LATENT_DIM * 6 * COLS,
        moved=4 * 2**20,
    )(normed, weights)

    (outcome,) = call(
        interior_kernel,
        "attention_interior",
        [((rows, COLS), BF16)],
        "vvv",
        flops=rows * COLS * 2048,
        moved=2**21,
        exps=rows * 512,
    )(steps, queries, own)
    (outcome,) = call(
        edge_kernel,
        "attention_edges",
        [((rows, COLS), BF16)],
        "vvvvvv",
        flops=rows * COLS * 512,
        moved=2**20,
        exps=rows * 128,
    )(steps, queries, own, low, high, outcome)
    *pieces, sources[-1], own = lax.optimization_barrier((*pieces, sources[-1], own))
    if paired:
        sources[1] = swap(sources[1], "ens", 1)
    else:
        sources = [exchange(sources[0], "ens")]
    pieces = pieces + [swap(piece, "core", 1) for piece in pieces]
    attended = exchange(outcome.reshape(GROUP * members_num, part, COLS), ("quad", "core", "ens"))
    block = (halves, QUAD, CORES, members_num * shard, width)
    (weights,) = call(
        assemble_kernel,
        "assemble",
        [(block, BF16)],
        "a" * len(pieces),
        [pltpu.SemaphoreType.DMA((GROUP,))],
        moved=4 * 2**20,
        results="h",
    )(*pieces)

    prediction, grads = call(
        mix_kernel,
        "mix_loss_backward",
        [((FIELD_NUM, node_rows), F32), ((GROUP * members_num, part, COLS), BF16)],
        "vvhh" + "a" * len(sources),
        [
            pltpu.VMEM((node_rows, LATENT_DIM), BF16),
            pltpu.VMEM(observed_truth.shape, F32),
            pltpu.VMEM((FIELD_PAD, node_rows), F32),
            pltpu.VMEM((members_num, part, LATENT_DIM), BF16),
            pltpu.VMEM(block, BF16),
            pltpu.SemaphoreType.DMA((halves + 1 + len(sources),)),
        ],
        flops=node_rows * LATENT_DIM * 4 * width,
        moved=2**22,
        room=14,
    )(attended, cell_surface_factor[None], observed_truth, weights, *sources)
    grads = exchange(grads, ("quad", "core", "ens")).reshape(rows, COLS)

    edges, *inner = call(
        edge_back_kernel,
        "attention_edges_back",
        [((2, WINDOW - RIM, 2 * COLS), F32)] + rims,
        "vvvvvv",
        flops=rows * COLS * 1280,
        moved=2**20,
        exps=rows * 128,
    )(steps, queries, own, low, high, grads)
    from_low, from_high = across(inner)
    (kv_grads,) = call(
        interior_back_kernel,
        "attention_interior_back",
        [((rows, 2 * COLS), F32)],
        "vvvvv",
        flops=rows * COLS * 4096,
        moved=2**22,
        exps=rows * 512,
        room=10,
    )(steps, queries, own, grads, edges)
    (term,) = call(
        product_kernel,
        "product",
        [((LATENT_DIM, 2 * COLS), BF16)],
        "vvvv",
        flops=rows * LATENT_DIM * 8 * COLS,
        moved=2**22,
        room=16,
    )(normed, from_low, from_high, kv_grads)
    term, prediction = lax.optimization_barrier((term, prediction))
    term = exchange(term.reshape(-1, shard, 2 * COLS), everyone)
    (grad_kv,) = call(
        gather_kernel, "gather_sums", [((shard, 2 * LATENT_DIM), F32)], "v", flops=2**17, moved=2**20
    )(term.reshape(halves, GROUP, members_num, shard, 2 * COLS))

    if members_num == 2:
        got = jnp.roll(swap(prediction, "ens", 1), part, axis=1)
        lane = lax.broadcasted_iota(jnp.int32, prediction.shape, 1)
        prediction = jnp.where(lane // part == ens, prediction, got)
    else:
        prediction = prediction.reshape(FIELD_NUM, members_num, part).transpose(1, 0, 2)
        prediction = exchange(prediction, "ens").transpose(1, 0, 2)
    return (prediction.reshape(1, FIELD_NUM, node_rows), grad_kv)


def solution(mesh):
    space, ens = mesh.shape["space"], mesh.shape["ens"]
    split = Mesh(
        mesh.devices.reshape(space // GROUP, QUAD, CORES, ens), ("half", "quad", "core", "ens")
    )
    nodes = ("half", "quad", "core")
    shards = nodes + ("ens",)
    in_specs = (
        P("ens", nodes, None),
        P(shards, None),
        P(shards, None),
        P(shards, None),
        P(None, nodes),
        P(nodes),
        P(nodes, None),
    )
    out_specs = (P("ens", None, nodes), P(shards, None))
    return jax.shard_map(body, mesh=split, in_specs=in_specs, out_specs=out_specs, check_vma=False)
```

```python
import functools

import jax
import jax.numpy as jnp
from jax import lax
from jax.experimental import pallas as pl
from jax.experimental.pallas import tpu as pltpu
from jax.sharding import Mesh
from jax.sharding import PartitionSpec as P

LATENT_DIM = 1024
HEADS = 16
HEAD = 64
FIELD_NUM = 100
TILE = 64
RADIUS = 2
K_NB = 4
QUAD = 4
CORES = 2
GROUP = QUAD * CORES
COLS = LATENT_DIM // GROUP
RIM = RADIUS * TILE
FIELD_PAD = 128
PAIR = 2
WINDOW = (PAIR + 2 * RADIUS) * TILE
NOWHERE = 100
NOTE_ROWS = 16
CHUNKS = 4

NORM_EPS = 1e-06
SOFT_WIDTH = 0.0625
MASKED = -1e30

F32 = jnp.float32
BF16 = jnp.bfloat16

VMEM = pl.BlockSpec(memory_space=pltpu.VMEM)
SMEM = pl.BlockSpec(memory_space=pltpu.SMEM)
HBM = pl.BlockSpec(memory_space=pltpu.HBM)
ANYWHERE = pl.BlockSpec(memory_space=pl.ANY)
OVER_ROWS = (((0,), (0,)), ((), ()))
OVER_COLUMNS = (((1,), (1,)), ((), ()))


def call(kernel, name, outs, ins, scratch=(), flops=0, moved=0, exps=0, room=8, results=None):
    results = results or "v" * len(outs)
    spaces = {"s": SMEM, "v": VMEM, "h": HBM, "a": ANYWHERE}
    made = pl.pallas_call(
        kernel,
        out_shape=[
            pltpu.HBM(shape, kind) if space == "h" else jax.ShapeDtypeStruct(shape, kind)
            for (shape, kind), space in zip(outs, results)
        ],
        in_specs=[spaces[space] for space in ins],
        out_specs=[spaces[space] for space in results],
        scratch_shapes=list(scratch),
        compiler_params=pltpu.CompilerParams(vmem_limit_bytes=room * 2**20),
        cost_estimate=pl.CostEstimate(flops=flops, bytes_accessed=moved, transcendentals=exps),
        name=name,
    )

    def run(*args):
        return made(
            *[
                pltpu.with_memory_space_constraint(arg, pltpu.HBM) if space == "h" else arg
                for arg, space in zip(args, ins)
            ]
        )

    return run


def fetch(pairs, sems, first=0):
    copies = [
        pltpu.make_async_copy(source, target, sems.at[first + at])
        for at, (source, target) in enumerate(pairs)
    ]
    for copy in copies:
        copy.start()
    return copies


def wait(copies):
    for copy in copies:
        copy.wait()


def weights_kernel(w_any, mix_any, readout_any, columns_any, packed_any, *refs):
    w, columns, readout, packed, sems = refs
    copies = fetch(
        [(w_any, w), (readout_any, readout), (mix_any, packed.at[:, :LATENT_DIM])], sems
    )
    copies[0].wait()
    for g in range(GROUP):
        for part in range(3):
            at = (part * GROUP + g) * COLS
            columns[g, :, part * COLS : (part + 1) * COLS] = w[:, at : at + COLS]
    halves, _, members_num = columns_any.shape[:3]
    out = fetch(
        [
            (columns, columns_any.at[half, :, m])
            for half in range(halves)
            for m in range(members_num)
        ],
        sems,
        3,
    )
    wait(copies[1:])
    packed[:, LATENT_DIM:] = jnp.zeros((packed.shape[0], FIELD_PAD), BF16)
    packed[:, LATENT_DIM : LATENT_DIM + FIELD_NUM] = readout[...]
    wait(out + fetch([(packed, packed_any)], sems, 3 + len(out)))


def norm_kernel(near_any, source_any, normed_any, *refs):
    parts, (near, source, normed, sems) = refs[:-4], refs[-4:]
    ens = lax.axis_index("ens")
    copies = fetch([(source_any, source), (near_any, near)], sems)
    rows = source.shape[0]
    copies[0].wait()
    moves = []
    for step, part_any in enumerate(parts):
        count, part, _ = part_any.shape
        for m in range(count):
            place = (ens ^ step) if len(parts) == 2 else m
            place = pl.multiple_of(place * part, part)
            moves.append((source.at[pl.ds(place, part)], part_any.at[m]))
    out = fetch(moves, sems, 2)
    states = source[...].astype(F32)
    inverse = lax.rsqrt(jnp.mean(states * states, axis=-1, keepdims=True) + NORM_EPS)
    normed[:rows, :] = (states * inverse).astype(BF16)
    copies[1].wait()
    row = lax.broadcasted_iota(jnp.int32, (NOTE_ROWS, 128), 0)
    lane = lax.broadcasted_iota(jnp.int32, (NOTE_ROWS, 128), 1)
    note = jnp.zeros((NOTE_ROWS, 128), F32)
    tiles = near.shape[0]
    first_tile = lax.axis_index(("half", "quad", "core")) * tiles
    for tile in range(tiles):
        for slot in range(K_NB):
            at = near[tile, slot]
            step = jnp.where(at >= 0, at - first_tile - tile, NOWHERE).astype(F32)
            note = jnp.where((row == tile) & (lane == slot), step, note)
    normed[rows:, :] = jnp.zeros((NOTE_ROWS, LATENT_DIM), BF16)
    normed[rows:, :128] = note.astype(BF16)
    wait(out + fetch([(normed, normed_any)], sems, 2 + len(out)))


def owners():
    core, quad = lax.axis_index("core"), lax.axis_index("quad")
    return [(quad ^ step) * CORES + (core ^ flip) for flip in range(CORES) for step in range(QUAD)]


def collect_kernel(*refs):
    blocks, (normed_any, steps_ref, notes, sems) = refs[:GROUP], refs[GROUP:]
    block = blocks[0].shape[0] - NOTE_ROWS
    pairs = []
    for rows_ref, owner in zip(blocks, owners()):
        place = pl.ds(pl.multiple_of(owner * block, block), block)
        pairs.append((rows_ref.at[:block], normed_any.at[place]))
        pairs.append((rows_ref.at[block:, :128], notes.at[owner]))
    wait(fetch(pairs, sems))
    steps_ref[...] = notes[...].astype(F32)


def put_rims(rims, first, last):
    if len(rims) == 1:
        rims[0][...] = jnp.where(lax.axis_index("half") == 0, last, first)
    else:
        rims[0][...], rims[1][...] = first, last


def rims_kernel(normed_any, *refs):
    rows, sems = refs[-2:]
    if len(refs[0].shape) == 2:
        columns, w, rims = refs[:1], refs[1], refs[2:-2]
        pairs = [(columns[0], w)]
    else:
        columns, w, rims = refs[:2], refs[2], refs[3:-2]
        ens = lax.axis_index("ens")
        pairs = [(part, w.at[:, ens ^ step]) for step, part in enumerate(columns)]
    last = normed_any.shape[0] - RIM
    if len(rims) == 1:
        place = pl.multiple_of(jnp.where(lax.axis_index("half") == 0, last, 0), RIM)
        pairs.append((normed_any.at[pl.ds(place, RIM)], rows.at[0]))
    else:
        pairs += [(normed_any.at[:RIM], rows.at[0]), (normed_any.at[last:], rows.at[1])]
    wait(fetch(pairs, sems))
    weights = w[...].reshape(LATENT_DIM, 3 * COLS)[:, COLS:]
    for at, rim_ref in enumerate(rims):
        rim_ref[...] = jnp.dot(rows[at], weights, preferred_element_type=F32).astype(BF16)


def project_kernel(normed_any, w_ref, q_ref, kv_ref, normed, sems):
    chunk = normed.shape[0] // CHUNKS
    rows = [slice(at * chunk, (at + 1) * chunk) for at in range(CHUNKS)]
    copies = fetch([(normed_any.at[part], normed.at[part]) for part in rows], sems)
    weights = w_ref[...].reshape(LATENT_DIM, 3 * COLS)
    for part, copy in zip(rows, copies):
        copy.wait()
        projected = jnp.dot(normed[part, :], weights, preferred_element_type=F32).astype(BF16)
        q_ref[part, :] = projected[:, :COLS] * jnp.asarray(HEAD**-0.5, BF16)
        kv_ref[part, :] = projected[:, COLS:]


def assemble_kernel(*refs):
    pieces, (w_any, sems) = refs[:GROUP], refs[GROUP:]
    core, quad = lax.axis_index("core"), lax.axis_index("quad")
    pairs = [
        (piece, w_any.at[:, quad ^ (at % QUAD), core ^ (at // QUAD)])
        for at, piece in enumerate(pieces)
    ]
    wait(fetch(pairs, sems))


def by_head(rows):
    lane = lax.broadcasted_iota(jnp.int32, rows.shape, 1)
    zero = jnp.zeros_like(rows)
    return jnp.concatenate(
        [jnp.where(lane < HEAD, rows, zero), jnp.where(lane < HEAD, zero, rows)], axis=0
    )


def usable_keys(steps_ref, pair):
    lane = (lax.broadcasted_iota(jnp.int32, (1, WINDOW), 1) // TILE - RADIUS).astype(F32)
    masks = []
    for query_tile in range(PAIR):
        found = jnp.zeros((1, WINDOW), F32)
        for slot in range(K_NB):
            step = steps_ref[pair, query_tile : query_tile + 1, slot : slot + 1]
            found = jnp.where(lane - query_tile == step, 1.0, found)
        masks.append(found)
    row = lax.broadcasted_iota(jnp.int32, (2 * PAIR * TILE, 1), 0) // TILE % PAIR
    return jnp.where(row == 0, masks[0], masks[1]) > 0


def raised_scores(queries, keys, usable):
    scores = lax.dot_general(queries, keys, OVER_COLUMNS, preferred_element_type=F32)
    scores = jnp.where(usable, scores, MASKED)
    raised = jnp.exp(scores - jnp.max(scores, axis=-1, keepdims=True))
    return raised, 1.0 / jnp.sum(raised, axis=-1, keepdims=True)


def attend(steps_ref, pair, queries, keys, values):
    raised, share = raised_scores(by_head(queries), keys, usable_keys(steps_ref, pair))
    both = jnp.dot(raised.astype(BF16), values, preferred_element_type=F32) * share
    lane = lax.broadcasted_iota(jnp.int32, queries.shape, 1)
    half = PAIR * TILE
    return jnp.where(lane < HEAD, both[:half], both[half:]).astype(BF16)


def interior_kernel(steps_ref, q_ref, kv_ref, out_ref):
    step = PAIR * TILE
    pairs = q_ref.shape[0] // step
    for pair in range(1, pairs - 1):
        window = slice((pair - 1) * step, (pair + 2) * step)
        rows = slice(pair * step, (pair + 1) * step)
        out_ref[rows, :] = attend(
            steps_ref, pair, q_ref[rows, :], kv_ref[window, :COLS], kv_ref[window, COLS:]
        )


def edge_kernel(steps_ref, q_ref, kv_ref, low_ref, high_ref, done_ref, out_ref):
    step = PAIR * TILE
    count = q_ref.shape[0]
    pairs = count // step
    out_ref[step : count - step, :] = done_ref[step : count - step, :]
    first = jnp.concatenate([low_ref[...], kv_ref[: 2 * step, :]], axis=0)
    last = jnp.concatenate([kv_ref[count - 2 * step :, :], high_ref[...]], axis=0)
    for pair, window in ((0, first), (pairs - 1, last)):
        rows = slice(pair * step, (pair + 1) * step)
        out_ref[rows, :] = attend(
            steps_ref, pair, q_ref[rows, :], window[:, :COLS], window[:, COLS:]
        )


def attend_back(steps_ref, pair, queries, grads, keys, values):
    queries, grads = by_head(queries), by_head(grads)
    raised, share = raised_scores(queries, keys, usable_keys(steps_ref, pair))
    probs = raised * share
    grad_probs = lax.dot_general(grads, values, OVER_COLUMNS, preferred_element_type=F32)
    row_delta = jnp.sum(probs * grad_probs, axis=-1, keepdims=True)
    grad_scores = (probs * (grad_probs - row_delta)).astype(BF16)
    key_grad = lax.dot_general(grad_scores, queries, OVER_ROWS, preferred_element_type=F32)
    value_grad = lax.dot_general(probs.astype(BF16), grads, OVER_ROWS, preferred_element_type=F32)
    return key_grad, value_grad


def edge_back_kernel(
    steps_ref, q_ref, kv_ref, low_ref, high_ref, g_ref, part_ref, *rims
):
    outer = []
    step = PAIR * TILE
    count = q_ref.shape[0]
    first = jnp.concatenate([low_ref[...], kv_ref[: 2 * step, :]], axis=0)
    last = jnp.concatenate([kv_ref[count - 2 * step :, :], high_ref[...]], axis=0)
    pairs = count // step
    for edge, pair, window in ((0, 0, first), (1, pairs - 1, last)):
        rows = slice(pair * step, (pair + 1) * step)
        grads = attend_back(
            steps_ref, pair, q_ref[rows, :], g_ref[rows, :], window[:, :COLS], window[:, COLS:]
        )
        rim = slice(0, RIM) if edge == 0 else slice(WINDOW - RIM, WINDOW)
        own = slice(RIM, WINDOW) if edge == 0 else slice(0, WINDOW - RIM)
        for at, grad in enumerate(grads):
            columns = slice(at * COLS, (at + 1) * COLS)
            part_ref[edge, :, columns] = grad[own]
        outer.append(jnp.concatenate([grad[rim].astype(BF16) for grad in grads], axis=1))
    put_rims(rims, *outer)


def interior_back_kernel(steps_ref, q_ref, kv_ref, g_ref, part_ref, out_ref):
    step = PAIR * TILE
    count = q_ref.shape[0]
    pairs = count // step
    reach = 2 * step
    out_ref[:reach, :] = part_ref[0]
    out_ref[reach : count - reach, :] = jnp.zeros((count - 2 * reach, 2 * COLS), F32)
    out_ref[count - reach :, :] = part_ref[1]
    for pair in range(1, pairs - 1):
        window = slice((pair - 1) * step, (pair + 2) * step)
        rows = slice(pair * step, (pair + 1) * step)
        key_grad, value_grad = attend_back(
            steps_ref,
            pair,
            q_ref[rows, :],
            g_ref[rows, :],
            kv_ref[window, :COLS],
            kv_ref[window, COLS:],
        )
        out_ref[window, :COLS] += key_grad
        out_ref[window, COLS:] += value_grad


def slope(spread):
    return spread * lax.rsqrt(spread * spread + SOFT_WIDTH)


def mix_kernel(att_ref, factor_ref, truth_any, w_any, *refs):
    sources, refs = refs[:-8], refs[-8:]
    pred_ref, grad_ref, a, truth_ref, truth, source, w, sems = refs
    members_num, part, _ = source.shape
    halves = w.shape[0]
    ens = lax.axis_index("ens")
    copies = fetch([(w_any.at[half], w.at[half]) for half in range(halves)], sems)
    pairs = [(truth_any, truth_ref)]
    if len(sources) == 1:
        pairs.append((sources[0], source))
    else:
        pairs += [(rows.at[0], source.at[ens ^ step]) for step, rows in enumerate(sources)]
    others = fetch(pairs, sems, halves)
    for g in range(GROUP):
        for m in range(members_num):
            a[m * part : (m + 1) * part, g * COLS : (g + 1) * COLS] = att_ref[g * members_num + m]
    wait(others)
    lane_part = lax.broadcasted_iota(jnp.int32, (1, a.shape[0]), 1) // part
    own_truth, own_factor = truth_ref[...], factor_ref[...]
    for turn in range(1, members_num):
        at = lane_part - turn
        here = jnp.where(at < 0, at + members_num, at) == ens
        own_truth = jnp.where(here, pltpu.roll(truth_ref[...], turn * part, 1), own_truth)
        own_factor = jnp.where(here, pltpu.roll(factor_ref[...], turn * part, 1), own_factor)
    truth[...] = jnp.zeros_like(truth)
    truth[:FIELD_NUM, :] = own_truth
    hidden = source[...].reshape(a.shape).astype(F32)
    count = LATENT_DIM // halves
    for half in range(halves):
        copies[half].wait()
        mix = w[half].reshape(count, LATENT_DIM + FIELD_PAD)[:, :LATENT_DIM]
        hidden += jnp.dot(
            a[:, half * count : (half + 1) * count], mix, preferred_element_type=F32
        )
    both = w[...].reshape(LATENT_DIM, LATENT_DIM + FIELD_PAD)
    mix, readout = both[:, :LATENT_DIM], both[:, LATENT_DIM:]
    inverse = lax.rsqrt(jnp.mean(hidden * hidden, axis=-1, keepdims=True) + NORM_EPS)
    decoded = (hidden * inverse).astype(BF16)
    prediction = lax.dot_general(
        readout, decoded, (((0,), (1,)), ((), ())), preferred_element_type=F32
    )
    pred_ref[...] = prediction[:FIELD_NUM]
    spread = jnp.zeros_like(prediction)
    for other in range(1, members_num):
        spread = spread + slope(prediction - pltpu.roll(prediction, other * part, 1))
    derivative = own_factor / FIELD_NUM * (
        slope(prediction - truth[...]) - spread / (members_num - 1)
    )
    grad_decoded = lax.dot_general(
        derivative.astype(BF16), readout, (((0,), (1,)), ((), ())), preferred_element_type=F32
    )
    grad_hidden = inverse * grad_decoded - hidden * inverse**3 * jnp.mean(
        grad_decoded * hidden, axis=-1, keepdims=True
    )
    grads = lax.dot_general(
        grad_hidden.astype(BF16), mix, OVER_COLUMNS, preferred_element_type=F32
    ).astype(BF16)
    for g in range(GROUP):
        for m in range(members_num):
            grad_ref[g * members_num + m] = grads[
                m * part : (m + 1) * part, g * COLS : (g + 1) * COLS
            ]


def product_kernel(normed_ref, from_low_ref, from_high_ref, grads_ref, out_ref):
    count = normed_ref.shape[0]
    half, last = lax.axis_index("half"), lax.axis_size("half") - 1
    from_low = jnp.where(half > 0, from_low_ref[...].astype(F32), 0.0)
    from_high = jnp.where(half < last, from_high_ref[...].astype(F32), 0.0)
    grads = grads_ref[...]
    grads = jnp.concatenate(
        [
            grads[:RIM] + from_low,
            grads[RIM : count - RIM],
            grads[count - RIM :] + from_high,
        ],
        axis=0,
    )
    high = grads.astype(BF16)
    low = (grads - high.astype(F32)).astype(BF16)
    both = lax.dot_general(
        normed_ref[...], jnp.concatenate([high, low], axis=1), OVER_ROWS, preferred_element_type=F32
    )
    out_ref[...] = (both[:, : 2 * COLS] + both[:, 2 * COLS :]).astype(BF16)


def gather_kernel(parts_ref, out_ref):
    halves, _, members_num = parts_ref.shape[:3]
    for g in range(GROUP):
        total = None
        for half in range(halves):
            for m in range(members_num):
                part = parts_ref[half, g, m].astype(F32)
                total = part if total is None else total + part
        out_ref[:, g * COLS : (g + 1) * COLS] = total[:, :COLS]
        out_ref[:, LATENT_DIM + g * COLS : LATENT_DIM + (g + 1) * COLS] = total[:, COLS:]


def exchange(chunks, axes):
    return lax.all_to_all(chunks, axes, 0, 0)


def swap(value, axis, step):
    return lax.ppermute(value, axis, [(i, i ^ step) for i in range(lax.axis_size(axis))])


def in_order(mine, axis, at):
    if lax.axis_size(axis) != 2:
        return lax.all_gather(mine, axis, axis=at)
    other = swap(mine, axis, 1)
    first = lax.axis_index(axis) == 0
    return jnp.stack([jnp.where(first, mine, other), jnp.where(first, other, mine)], axis=at)


def body(members, w_attn, w_mix, readout_matrix, observed_truth, cell_surface_factor, neighbours):
    halves, members_num = lax.axis_size("half"), lax.axis_size("ens")
    nodes = ("half", "quad", "core")
    everyone = nodes + ("ens",)
    shard = w_attn.shape[0]
    node_rows = members.shape[1]
    rows = GROUP * node_rows
    part = node_rows // members_num
    up = [(i, i + 1) for i in range(halves - 1)]
    down = [(target, source) for source, target in up]
    ens = lax.axis_index("ens")
    width = LATENT_DIM + FIELD_PAD
    paired = members_num == 2
    copies = 1 if paired else members_num
    source_parts = 2 if paired else 1

    columns, packed = call(
        weights_kernel,
        "prepare_weights",
        [((halves, GROUP, copies, shard, 3 * COLS), BF16), ((shard, width), BF16)],
        "hhh",
        [
            pltpu.VMEM(w_attn.shape, BF16),
            pltpu.VMEM((GROUP, shard, 3 * COLS), BF16),
            pltpu.VMEM(readout_matrix.shape, BF16),
            pltpu.VMEM((shard, width), BF16),
            pltpu.SemaphoreType.DMA((4 + halves * copies,)),
        ],
        moved=2**20,
        results="hh",
    )(w_attn, w_mix, readout_matrix)
    normed, *sources = call(
        norm_kernel,
        "norm",
        [((node_rows + NOTE_ROWS, LATENT_DIM), BF16)]
        + [((1 if paired else members_num, part, LATENT_DIM), BF16)] * source_parts,
        "hh",
        [
            pltpu.SMEM(neighbours.shape, jnp.int32),
            pltpu.VMEM((node_rows, LATENT_DIM), BF16),
            pltpu.VMEM((node_rows + NOTE_ROWS, LATENT_DIM), BF16),
            pltpu.SemaphoreType.DMA((3 + max(2, members_num),)),
        ],
        flops=2**20,
        moved=2**20,
        results="h" + "h" * source_parts,
    )(neighbours, members.reshape(node_rows, LATENT_DIM))

    packed, normed = lax.optimization_barrier((in_order(packed, "half", 0), normed))
    near = [normed, swap(normed, "quad", 1), None, swap(normed, "quad", 3)]
    if paired:
        columns = exchange(columns.reshape(-1, shard, 3 * COLS), nodes)
        columns, late = lax.optimization_barrier((columns, normed))
        columns = [columns, swap(columns, "ens", 1)]
    else:
        columns = [exchange(columns.reshape(-1, shard, 3 * COLS), everyone)]
        columns = [columns[0].reshape(LATENT_DIM, 3 * COLS)]
        late = normed
    near[2] = swap(late, "quad", 2)
    far = [swap(piece, "core", 1) for piece in near]
    normed, steps = call(
        collect_kernel,
        "collect",
        [((rows, LATENT_DIM), BF16), ((GROUP, NOTE_ROWS, 128), F32)],
        "a" * (2 * QUAD),
        [pltpu.VMEM((GROUP, NOTE_ROWS, 128), BF16), pltpu.SemaphoreType.DMA((2 * GROUP,))],
        moved=4 * 2**20,
        results="hv",
    )(*near, *far)

    packed = in_order(packed, "ens", 1).reshape(halves, members_num * shard, width)
    packed, near[2] = lax.optimization_barrier((packed, near[2]))
    pieces = [packed] + [swap(packed, "quad", step) for step in range(1, QUAD)]

    rim = ((RIM, 2 * COLS), BF16)
    rims = [rim] if halves == 2 else [rim, rim]
    w_shape = (GROUP * halves, 2, shard, 3 * COLS) if paired else (LATENT_DIM, 3 * COLS)
    weights, *inner = call(
        rims_kernel,
        "project_rims",
        [(w_shape, BF16)] + rims,
        "h" + "a" * len(columns),
        [pltpu.VMEM((len(rims), RIM, LATENT_DIM), BF16), pltpu.SemaphoreType.DMA((4,))],
        flops=RIM * LATENT_DIM * 4 * COLS,
        moved=2**20,
    )(normed, *columns)
    def across(inner):
        if halves == 2:
            got = swap(inner[0], "half", 1)
            return got, got
        return lax.ppermute(inner[1], "half", up), lax.ppermute(inner[0], "half", down)

    weights, sources[-1] = lax.optimization_barrier((weights, sources[-1]))
    sources = [sources[0], swap(sources[1], "ens", 1)] if paired else [exchange(sources[0], "ens")]
    low, high = across(inner)
    queries, own = call(
        project_kernel,
        "project",
        [((rows, COLS), BF16), ((rows, 2 * COLS), BF16)],
        "hv",
        [pltpu.VMEM((rows, LATENT_DIM), BF16), pltpu.SemaphoreType.DMA((CHUNKS,))],
        flops=rows * LATENT_DIM * 6 * COLS,
        moved=4 * 2**20,
    )(normed, weights)

    (outcome,) = call(
        interior_kernel,
        "attention_interior",
        [((rows, COLS), BF16)],
        "vvv",
        flops=rows * COLS * 2048,
        moved=2**21,
        exps=rows * 512,
    )(steps, queries, own)
    (outcome,) = call(
        edge_kernel,
        "attention_edges",
        [((rows, COLS), BF16)],
        "vvvvvv",
        flops=rows * COLS * 512,
        moved=2**20,
        exps=rows * 128,
    )(steps, queries, own, low, high, outcome)
    *pieces, own = lax.optimization_barrier((*pieces, own))
    pieces = pieces + [swap(piece, "core", 1) for piece in pieces]
    attended = exchange(outcome.reshape(GROUP * members_num, part, COLS), ("quad", "core", "ens"))
    block = (halves, QUAD, CORES, members_num * shard, width)
    (weights,) = call(
        assemble_kernel,
        "assemble",
        [(block, BF16)],
        "a" * len(pieces),
        [pltpu.SemaphoreType.DMA((GROUP,))],
        moved=4 * 2**20,
        results="h",
    )(*pieces)

    prediction, grads = call(
        mix_kernel,
        "mix_loss_backward",
        [((FIELD_NUM, node_rows), F32), ((GROUP * members_num, part, COLS), BF16)],
        "vvhh" + "a" * len(sources),
        [
            pltpu.VMEM((node_rows, LATENT_DIM), BF16),
            pltpu.VMEM(observed_truth.shape, F32),
            pltpu.VMEM((FIELD_PAD, node_rows), F32),
            pltpu.VMEM((members_num, part, LATENT_DIM), BF16),
            pltpu.VMEM(block, BF16),
            pltpu.SemaphoreType.DMA((halves + 1 + len(sources),)),
        ],
        flops=node_rows * LATENT_DIM * 4 * width,
        moved=2**22,
        room=14,
    )(attended, cell_surface_factor[None], observed_truth, weights, *sources)
    grads = exchange(grads, ("quad", "core", "ens")).reshape(rows, COLS)

    edges, *inner = call(
        edge_back_kernel,
        "attention_edges_back",
        [((2, WINDOW - RIM, 2 * COLS), F32)] + rims,
        "vvvvvv",
        flops=rows * COLS * 1280,
        moved=2**20,
        exps=rows * 128,
    )(steps, queries, own, low, high, grads)
    from_low, from_high = across(inner)
    (kv_grads,) = call(
        interior_back_kernel,
        "attention_interior_back",
        [((rows, 2 * COLS), F32)],
        "vvvvv",
        flops=rows * COLS * 4096,
        moved=2**22,
        exps=rows * 512,
        room=10,
    )(steps, queries, own, grads, edges)
    (term,) = call(
        product_kernel,
        "product",
        [((LATENT_DIM, 2 * COLS), BF16)],
        "vvvv",
        flops=rows * LATENT_DIM * 8 * COLS,
        moved=2**22,
        room=16,
    )(normed, from_low, from_high, kv_grads)
    term, prediction = lax.optimization_barrier((term, prediction))
    term = exchange(term.reshape(-1, shard, 2 * COLS), everyone)
    (grad_kv,) = call(
        gather_kernel, "gather_sums", [((shard, 2 * LATENT_DIM), F32)], "v", flops=2**17, moved=2**20
    )(term.reshape(halves, GROUP, members_num, shard, 2 * COLS))

    if members_num == 2:
        got = jnp.roll(swap(prediction, "ens", 1), part, axis=1)
        lane = lax.broadcasted_iota(jnp.int32, prediction.shape, 1)
        prediction = jnp.where(lane // part == ens, prediction, got)
    else:
        prediction = prediction.reshape(FIELD_NUM, members_num, part).transpose(1, 0, 2)
        prediction = exchange(prediction, "ens").transpose(1, 0, 2)
    return (prediction.reshape(1, FIELD_NUM, node_rows), grad_kv)


def solution(mesh):
    space, ens = mesh.shape["space"], mesh.shape["ens"]
    split = Mesh(
        mesh.devices.reshape(space // GROUP, QUAD, CORES, ens), ("half", "quad", "core", "ens")
    )
    nodes = ("half", "quad", "core")
    shards = nodes + ("ens",)
    in_specs = (
        P("ens", nodes, None),
        P(shards, None),
        P(shards, None),
        P(shards, None),
        P(None, nodes),
        P(nodes),
        P(nodes, None),
    )
    out_specs = (P("ens", None, nodes), P(shards, None))
    return jax.shard_map(body, mesh=split, in_specs=in_specs, out_specs=out_specs, check_vma=False)
```

```python
import functools

import jax
import jax.numpy as jnp
from jax import lax
from jax.experimental import pallas as pl
from jax.experimental.pallas import tpu as pltpu
from jax.sharding import Mesh
from jax.sharding import PartitionSpec as P

LATENT_DIM = 1024
HEADS = 16
HEAD = 64
FIELD_NUM = 100
TILE = 64
RADIUS = 2
K_NB = 4
QUAD = 4
CORES = 2
GROUP = QUAD * CORES
COLS = LATENT_DIM // GROUP
RIM = RADIUS * TILE
FIELD_PAD = 128
PAIR = 2
WINDOW = (PAIR + 2 * RADIUS) * TILE
NOWHERE = 100
NOTE_ROWS = 16
CHUNKS = 4

NORM_EPS = 1e-06
SOFT_WIDTH = 0.0625
MASKED = -1e30

F32 = jnp.float32
BF16 = jnp.bfloat16

VMEM = pl.BlockSpec(memory_space=pltpu.VMEM)
SMEM = pl.BlockSpec(memory_space=pltpu.SMEM)
HBM = pl.BlockSpec(memory_space=pltpu.HBM)
ANYWHERE = pl.BlockSpec(memory_space=pl.ANY)
OVER_ROWS = (((0,), (0,)), ((), ()))
OVER_COLUMNS = (((1,), (1,)), ((), ()))


def call(kernel, name, outs, ins, scratch=(), flops=0, moved=0, exps=0, room=8, results=None):
    results = results or "v" * len(outs)
    spaces = {"s": SMEM, "v": VMEM, "h": HBM, "a": ANYWHERE}
    made = pl.pallas_call(
        kernel,
        out_shape=[
            pltpu.HBM(shape, kind) if space == "h" else jax.ShapeDtypeStruct(shape, kind)
            for (shape, kind), space in zip(outs, results)
        ],
        in_specs=[spaces[space] for space in ins],
        out_specs=[spaces[space] for space in results],
        scratch_shapes=list(scratch),
        compiler_params=pltpu.CompilerParams(vmem_limit_bytes=room * 2**20),
        cost_estimate=pl.CostEstimate(flops=flops, bytes_accessed=moved, transcendentals=exps),
        name=name,
    )

    def run(*args):
        return made(
            *[
                pltpu.with_memory_space_constraint(arg, pltpu.HBM) if space == "h" else arg
                for arg, space in zip(args, ins)
            ]
        )

    return run


def fetch(pairs, sems, first=0):
    copies = [
        pltpu.make_async_copy(source, target, sems.at[first + at])
        for at, (source, target) in enumerate(pairs)
    ]
    for copy in copies:
        copy.start()
    return copies


def wait(copies):
    for copy in copies:
        copy.wait()


def weights_kernel(w_any, mix_any, readout_any, columns_any, packed_any, *refs):
    w, columns, readout, packed, sems = refs
    copies = fetch(
        [(w_any, w), (readout_any, readout), (mix_any, packed.at[:, :LATENT_DIM])], sems
    )
    copies[0].wait()
    for g in range(GROUP):
        for part in range(3):
            at = (part * GROUP + g) * COLS
            columns[g, :, part * COLS : (part + 1) * COLS] = w[:, at : at + COLS]
    halves, _, members_num = columns_any.shape[:3]
    out = fetch(
        [
            (columns, columns_any.at[half, :, m])
            for half in range(halves)
            for m in range(members_num)
        ],
        sems,
        3,
    )
    wait(copies[1:])
    packed[:, LATENT_DIM:] = jnp.zeros((packed.shape[0], FIELD_PAD), BF16)
    packed[:, LATENT_DIM : LATENT_DIM + FIELD_NUM] = readout[...]
    wait(out + fetch([(packed, packed_any)], sems, 3 + len(out)))


def norm_kernel(near_any, source_any, normed_any, *refs):
    parts, (near, source, normed, sems) = refs[:-4], refs[-4:]
    ens = lax.axis_index("ens")
    copies = fetch([(source_any, source), (near_any, near)], sems)
    rows = source.shape[0]
    copies[0].wait()
    moves = []
    for step, part_any in enumerate(parts):
        count, part, _ = part_any.shape
        for m in range(count):
            place = (ens ^ step) if len(parts) == 2 else m
            place = pl.multiple_of(place * part, part)
            moves.append((source.at[pl.ds(place, part)], part_any.at[m]))
    out = fetch(moves, sems, 2)
    states = source[...].astype(F32)
    inverse = lax.rsqrt(jnp.mean(states * states, axis=-1, keepdims=True) + NORM_EPS)
    normed[:rows, :] = (states * inverse).astype(BF16)
    copies[1].wait()
    row = lax.broadcasted_iota(jnp.int32, (NOTE_ROWS, 128), 0)
    lane = lax.broadcasted_iota(jnp.int32, (NOTE_ROWS, 128), 1)
    note = jnp.zeros((NOTE_ROWS, 128), F32)
    tiles = near.shape[0]
    first_tile = lax.axis_index(("half", "quad", "core")) * tiles
    for tile in range(tiles):
        for slot in range(K_NB):
            at = near[tile, slot]
            step = jnp.where(at >= 0, at - first_tile - tile, NOWHERE).astype(F32)
            note = jnp.where((row == tile) & (lane == slot), step, note)
    normed[rows:, :] = jnp.zeros((NOTE_ROWS, LATENT_DIM), BF16)
    normed[rows:, :128] = note.astype(BF16)
    wait(out + fetch([(normed, normed_any)], sems, 2 + len(out)))


def owners():
    core, quad = lax.axis_index("core"), lax.axis_index("quad")
    return [(quad ^ step) * CORES + (core ^ flip) for flip in range(CORES) for step in range(QUAD)]


def collect_kernel(*refs):
    blocks, (normed_any, steps_ref, notes, sems) = refs[:GROUP], refs[GROUP:]
    block = blocks[0].shape[0] - NOTE_ROWS
    pairs = []
    for rows_ref, owner in zip(blocks, owners()):
        place = pl.ds(pl.multiple_of(owner * block, block), block)
        pairs.append((rows_ref.at[:block], normed_any.at[place]))
        pairs.append((rows_ref.at[block:, :128], notes.at[owner]))
    wait(fetch(pairs, sems))
    steps_ref[...] = notes[...].astype(F32)


def put_rims(rims, first, last):
    if len(rims) == 1:
        rims[0][...] = jnp.where(lax.axis_index("half") == 0, last, first)
    else:
        rims[0][...], rims[1][...] = first, last


def rims_kernel(normed_any, *refs):
    rows, sems = refs[-2:]
    if len(refs[0].shape) == 2:
        columns, w, rims = refs[:1], refs[1], refs[2:-2]
        pairs = [(columns[0], w)]
    else:
        columns, w, rims = refs[:2], refs[2], refs[3:-2]
        ens = lax.axis_index("ens")
        pairs = [(part, w.at[:, ens ^ step]) for step, part in enumerate(columns)]
    last = normed_any.shape[0] - RIM
    if len(rims) == 1:
        place = pl.multiple_of(jnp.where(lax.axis_index("half") == 0, last, 0), RIM)
        pairs.append((normed_any.at[pl.ds(place, RIM)], rows.at[0]))
    else:
        pairs += [(normed_any.at[:RIM], rows.at[0]), (normed_any.at[last:], rows.at[1])]
    wait(fetch(pairs, sems))
    weights = w[...].reshape(LATENT_DIM, 3 * COLS)[:, COLS:]
    for at, rim_ref in enumerate(rims):
        rim_ref[...] = jnp.dot(rows[at], weights, preferred_element_type=F32).astype(BF16)


def project_kernel(normed_any, w_ref, q_ref, kv_ref, normed, sems):
    chunk = normed.shape[0] // CHUNKS
    rows = [slice(at * chunk, (at + 1) * chunk) for at in range(CHUNKS)]
    copies = fetch([(normed_any.at[part], normed.at[part]) for part in rows], sems)
    weights = w_ref[...].reshape(LATENT_DIM, 3 * COLS)
    for part, copy in zip(rows, copies):
        copy.wait()
        projected = jnp.dot(normed[part, :], weights, preferred_element_type=F32).astype(BF16)
        q_ref[part, :] = projected[:, :COLS] * jnp.asarray(HEAD**-0.5, BF16)
        kv_ref[part, :] = projected[:, COLS:]


def assemble_kernel(*refs):
    pieces, (w_any, sems) = refs[:GROUP], refs[GROUP:]
    core, quad = lax.axis_index("core"), lax.axis_index("quad")
    pairs = [
        (piece, w_any.at[:, quad ^ (at % QUAD), core ^ (at // QUAD)])
        for at, piece in enumerate(pieces)
    ]
    wait(fetch(pairs, sems))


def by_head(rows):
    lane = lax.broadcasted_iota(jnp.int32, rows.shape, 1)
    zero = jnp.zeros_like(rows)
    return jnp.concatenate(
        [jnp.where(lane < HEAD, rows, zero), jnp.where(lane < HEAD, zero, rows)], axis=0
    )


def usable_keys(steps_ref, pair):
    lane = (lax.broadcasted_iota(jnp.int32, (1, WINDOW), 1) // TILE - RADIUS).astype(F32)
    masks = []
    for query_tile in range(PAIR):
        found = jnp.zeros((1, WINDOW), F32)
        for slot in range(K_NB):
            step = steps_ref[pair, query_tile : query_tile + 1, slot : slot + 1]
            found = jnp.where(lane - query_tile == step, 1.0, found)
        masks.append(found)
    row = lax.broadcasted_iota(jnp.int32, (2 * PAIR * TILE, 1), 0) // TILE % PAIR
    return jnp.where(row == 0, masks[0], masks[1]) > 0


def raised_scores(queries, keys, usable):
    scores = lax.dot_general(queries, keys, OVER_COLUMNS, preferred_element_type=F32)
    scores = jnp.where(usable, scores, MASKED)
    raised = jnp.exp(scores - jnp.max(scores, axis=-1, keepdims=True))
    return raised, 1.0 / jnp.sum(raised, axis=-1, keepdims=True)


def attend(steps_ref, pair, queries, keys, values):
    raised, share = raised_scores(by_head(queries), keys, usable_keys(steps_ref, pair))
    both = jnp.dot(raised.astype(BF16), values, preferred_element_type=F32) * share
    lane = lax.broadcasted_iota(jnp.int32, queries.shape, 1)
    half = PAIR * TILE
    return jnp.where(lane < HEAD, both[:half], both[half:]).astype(BF16)


def interior_kernel(steps_ref, q_ref, kv_ref, out_ref):
    step = PAIR * TILE
    pairs = q_ref.shape[0] // step
    for pair in range(1, pairs - 1):
        window = slice((pair - 1) * step, (pair + 2) * step)
        rows = slice(pair * step, (pair + 1) * step)
        out_ref[rows, :] = attend(
            steps_ref, pair, q_ref[rows, :], kv_ref[window, :COLS], kv_ref[window, COLS:]
        )


def edge_kernel(steps_ref, q_ref, kv_ref, low_ref, high_ref, done_ref, out_ref):
    step = PAIR * TILE
    count = q_ref.shape[0]
    pairs = count // step
    out_ref[step : count - step, :] = done_ref[step : count - step, :]
    first = jnp.concatenate([low_ref[...], kv_ref[: 2 * step, :]], axis=0)
    last = jnp.concatenate([kv_ref[count - 2 * step :, :], high_ref[...]], axis=0)
    for pair, window in ((0, first), (pairs - 1, last)):
        rows = slice(pair * step, (pair + 1) * step)
        out_ref[rows, :] = attend(
            steps_ref, pair, q_ref[rows, :], window[:, :COLS], window[:, COLS:]
        )


def attend_back(steps_ref, pair, queries, grads, keys, values):
    queries, grads = by_head(queries), by_head(grads)
    raised, share = raised_scores(queries, keys, usable_keys(steps_ref, pair))
    probs = raised * share
    grad_probs = lax.dot_general(grads, values, OVER_COLUMNS, preferred_element_type=F32)
    row_delta = jnp.sum(probs * grad_probs, axis=-1, keepdims=True)
    grad_scores = (probs * (grad_probs - row_delta)).astype(BF16)
    key_grad = lax.dot_general(grad_scores, queries, OVER_ROWS, preferred_element_type=F32)
    value_grad = lax.dot_general(probs.astype(BF16), grads, OVER_ROWS, preferred_element_type=F32)
    return key_grad, value_grad


def edge_back_kernel(
    steps_ref, q_ref, kv_ref, low_ref, high_ref, g_ref, part_ref, *rims
):
    outer = []
    step = PAIR * TILE
    count = q_ref.shape[0]
    first = jnp.concatenate([low_ref[...], kv_ref[: 2 * step, :]], axis=0)
    last = jnp.concatenate([kv_ref[count - 2 * step :, :], high_ref[...]], axis=0)
    pairs = count // step
    for edge, pair, window in ((0, 0, first), (1, pairs - 1, last)):
        rows = slice(pair * step, (pair + 1) * step)
        grads = attend_back(
            steps_ref, pair, q_ref[rows, :], g_ref[rows, :], window[:, :COLS], window[:, COLS:]
        )
        rim = slice(0, RIM) if edge == 0 else slice(WINDOW - RIM, WINDOW)
        own = slice(RIM, WINDOW) if edge == 0 else slice(0, WINDOW - RIM)
        for at, grad in enumerate(grads):
            columns = slice(at * COLS, (at + 1) * COLS)
            part_ref[edge, :, columns] = grad[own]
        outer.append(jnp.concatenate([grad[rim].astype(BF16) for grad in grads], axis=1))
    put_rims(rims, *outer)


def interior_back_kernel(steps_ref, q_ref, kv_ref, g_ref, part_ref, out_ref):
    step = PAIR * TILE
    count = q_ref.shape[0]
    pairs = count // step
    reach = 2 * step
    out_ref[:reach, :] = part_ref[0]
    out_ref[reach : count - reach, :] = jnp.zeros((count - 2 * reach, 2 * COLS), F32)
    out_ref[count - reach :, :] = part_ref[1]
    for pair in range(1, pairs - 1):
        window = slice((pair - 1) * step, (pair + 2) * step)
        rows = slice(pair * step, (pair + 1) * step)
        key_grad, value_grad = attend_back(
            steps_ref,
            pair,
            q_ref[rows, :],
            g_ref[rows, :],
            kv_ref[window, :COLS],
            kv_ref[window, COLS:],
        )
        out_ref[window, :COLS] += key_grad
        out_ref[window, COLS:] += value_grad


def slope(spread):
    return spread * lax.rsqrt(spread * spread + SOFT_WIDTH)


def mix_kernel(att_ref, factor_ref, truth_any, w_any, *refs):
    sources, refs = refs[:-8], refs[-8:]
    pred_ref, grad_ref, a, truth_ref, truth, source, w, sems = refs
    members_num, part, _ = source.shape
    halves = w.shape[0]
    ens = lax.axis_index("ens")
    copies = fetch([(w_any.at[half], w.at[half]) for half in range(halves)], sems)
    pairs = [(truth_any, truth_ref)]
    if len(sources) == 1:
        pairs.append((sources[0], source))
    else:
        pairs += [(rows.at[0], source.at[ens ^ step]) for step, rows in enumerate(sources)]
    others = fetch(pairs, sems, halves)
    for g in range(GROUP):
        for m in range(members_num):
            a[m * part : (m + 1) * part, g * COLS : (g + 1) * COLS] = att_ref[g * members_num + m]
    wait(others)
    lane_part = lax.broadcasted_iota(jnp.int32, (1, a.shape[0]), 1) // part
    own_truth, own_factor = truth_ref[...], factor_ref[...]
    for turn in range(1, members_num):
        at = lane_part - turn
        here = jnp.where(at < 0, at + members_num, at) == ens
        own_truth = jnp.where(here, pltpu.roll(truth_ref[...], turn * part, 1), own_truth)
        own_factor = jnp.where(here, pltpu.roll(factor_ref[...], turn * part, 1), own_factor)
    truth[...] = jnp.zeros_like(truth)
    truth[:FIELD_NUM, :] = own_truth
    hidden = source[...].reshape(a.shape).astype(F32)
    count = LATENT_DIM // halves
    for half in range(halves):
        copies[half].wait()
        mix = w[half].reshape(count, LATENT_DIM + FIELD_PAD)[:, :LATENT_DIM]
        hidden += jnp.dot(
            a[:, half * count : (half + 1) * count], mix, preferred_element_type=F32
        )
    both = w[...].reshape(LATENT_DIM, LATENT_DIM + FIELD_PAD)
    mix, readout = both[:, :LATENT_DIM], both[:, LATENT_DIM:]
    inverse = lax.rsqrt(jnp.mean(hidden * hidden, axis=-1, keepdims=True) + NORM_EPS)
    decoded = (hidden * inverse).astype(BF16)
    prediction = lax.dot_general(
        readout, decoded, (((0,), (1,)), ((), ())), preferred_element_type=F32
    )
    pred_ref[...] = prediction[:FIELD_NUM]
    spread = jnp.zeros_like(prediction)
    for other in range(1, members_num):
        spread = spread + slope(prediction - pltpu.roll(prediction, other * part, 1))
    derivative = own_factor / FIELD_NUM * (
        slope(prediction - truth[...]) - spread / (members_num - 1)
    )
    grad_decoded = lax.dot_general(
        derivative.astype(BF16), readout, (((0,), (1,)), ((), ())), preferred_element_type=F32
    )
    grad_hidden = inverse * grad_decoded - hidden * inverse**3 * jnp.mean(
        grad_decoded * hidden, axis=-1, keepdims=True
    )
    grads = lax.dot_general(
        grad_hidden.astype(BF16), mix, OVER_COLUMNS, preferred_element_type=F32
    ).astype(BF16)
    for g in range(GROUP):
        for m in range(members_num):
            grad_ref[g * members_num + m] = grads[
                m * part : (m + 1) * part, g * COLS : (g + 1) * COLS
            ]


def product_kernel(normed_ref, from_low_ref, from_high_ref, grads_ref, out_ref):
    count = normed_ref.shape[0]
    half, last = lax.axis_index("half"), lax.axis_size("half") - 1
    from_low = jnp.where(half > 0, from_low_ref[...].astype(F32), 0.0)
    from_high = jnp.where(half < last, from_high_ref[...].astype(F32), 0.0)
    grads = grads_ref[...]
    grads = jnp.concatenate(
        [
            grads[:RIM] + from_low,
            grads[RIM : count - RIM],
            grads[count - RIM :] + from_high,
        ],
        axis=0,
    )
    high = grads.astype(BF16)
    low = (grads - high.astype(F32)).astype(BF16)
    both = lax.dot_general(
        normed_ref[...], jnp.concatenate([high, low], axis=1), OVER_ROWS, preferred_element_type=F32
    )
    out_ref[...] = (both[:, : 2 * COLS] + both[:, 2 * COLS :]).astype(BF16)


def gather_kernel(parts_ref, out_ref):
    halves, _, members_num = parts_ref.shape[:3]
    for g in range(GROUP):
        total = None
        for half in range(halves):
            for m in range(members_num):
                part = parts_ref[half, g, m].astype(F32)
                total = part if total is None else total + part
        out_ref[:, g * COLS : (g + 1) * COLS] = total[:, :COLS]
        out_ref[:, LATENT_DIM + g * COLS : LATENT_DIM + (g + 1) * COLS] = total[:, COLS:]


def exchange(chunks, axes):
    return lax.all_to_all(chunks, axes, 0, 0)


def swap(value, axis, step):
    return lax.ppermute(value, axis, [(i, i ^ step) for i in range(lax.axis_size(axis))])


def in_order(mine, axis, at):
    if lax.axis_size(axis) != 2:
        return lax.all_gather(mine, axis, axis=at)
    other = swap(mine, axis, 1)
    first = lax.axis_index(axis) == 0
    return jnp.stack([jnp.where(first, mine, other), jnp.where(first, other, mine)], axis=at)


def body(members, w_attn, w_mix, readout_matrix, observed_truth, cell_surface_factor, neighbours):
    halves, members_num = lax.axis_size("half"), lax.axis_size("ens")
    nodes = ("half", "quad", "core")
    everyone = nodes + ("ens",)
    shard = w_attn.shape[0]
    node_rows = members.shape[1]
    rows = GROUP * node_rows
    part = node_rows // members_num
    up = [(i, i + 1) for i in range(halves - 1)]
    down = [(target, source) for source, target in up]
    ens = lax.axis_index("ens")
    width = LATENT_DIM + FIELD_PAD
    paired = members_num == 2
    copies = 1 if paired else members_num
    source_parts = 2 if paired else 1

    columns, packed = call(
        weights_kernel,
        "prepare_weights",
        [((halves, GROUP, copies, shard, 3 * COLS), BF16), ((shard, width), BF16)],
        "hhh",
        [
            pltpu.VMEM(w_attn.shape, BF16),
            pltpu.VMEM((GROUP, shard, 3 * COLS), BF16),
            pltpu.VMEM(readout_matrix.shape, BF16),
            pltpu.VMEM((shard, width), BF16),
            pltpu.SemaphoreType.DMA((4 + halves * copies,)),
        ],
        moved=2**20,
        results="hh",
    )(w_attn, w_mix, readout_matrix)
    normed, *sources = call(
        norm_kernel,
        "norm",
        [((node_rows + NOTE_ROWS, LATENT_DIM), BF16)]
        + [((1 if paired else members_num, part, LATENT_DIM), BF16)] * source_parts,
        "hh",
        [
            pltpu.SMEM(neighbours.shape, jnp.int32),
            pltpu.VMEM((node_rows, LATENT_DIM), BF16),
            pltpu.VMEM((node_rows + NOTE_ROWS, LATENT_DIM), BF16),
            pltpu.SemaphoreType.DMA((3 + max(2, members_num),)),
        ],
        flops=2**20,
        moved=2**20,
        results="h" + "h" * source_parts,
    )(neighbours, members.reshape(node_rows, LATENT_DIM))

    packed, normed = lax.optimization_barrier((in_order(packed, "half", 0), normed))
    near = [normed, swap(normed, "quad", 1), None, swap(normed, "quad", 3)]
    if paired:
        columns = exchange(columns.reshape(-1, shard, 3 * COLS), nodes)
        columns, late = lax.optimization_barrier((columns, normed))
        columns = [columns, swap(columns, "ens", 1)]
    else:
        columns = [exchange(columns.reshape(-1, shard, 3 * COLS), everyone)]
        columns = [columns[0].reshape(LATENT_DIM, 3 * COLS)]
        late = normed
    near[2] = swap(late, "quad", 2)
    far = [swap(piece, "core", 1) for piece in near]
    normed, steps = call(
        collect_kernel,
        "collect",
        [((rows, LATENT_DIM), BF16), ((GROUP, NOTE_ROWS, 128), F32)],
        "a" * (2 * QUAD),
        [pltpu.VMEM((GROUP, NOTE_ROWS, 128), BF16), pltpu.SemaphoreType.DMA((2 * GROUP,))],
        moved=4 * 2**20,
        results="hv",
    )(*near, *far)

    packed, near[1] = lax.optimization_barrier((packed, near[1]))
    packed = in_order(packed, "ens", 1).reshape(halves, members_num * shard, width)
    packed, near[2] = lax.optimization_barrier((packed, near[2]))
    pieces = [packed] + [swap(packed, "quad", step) for step in range(1, QUAD)]

    rim = ((RIM, 2 * COLS), BF16)
    rims = [rim] if halves == 2 else [rim, rim]
    w_shape = (GROUP * halves, 2, shard, 3 * COLS) if paired else (LATENT_DIM, 3 * COLS)
    weights, *inner = call(
        rims_kernel,
        "project_rims",
        [(w_shape, BF16)] + rims,
        "h" + "a" * len(columns),
        [pltpu.VMEM((len(rims), RIM, LATENT_DIM), BF16), pltpu.SemaphoreType.DMA((4,))],
        flops=RIM * LATENT_DIM * 4 * COLS,
        moved=2**20,
    )(normed, *columns)
    def across(inner):
        if halves == 2:
            got = swap(inner[0], "half", 1)
            return got, got
        return lax.ppermute(inner[1], "half", up), lax.ppermute(inner[0], "half", down)

    weights, sources[-1] = lax.optimization_barrier((weights, sources[-1]))
    sources = [sources[0], swap(sources[1], "ens", 1)] if paired else [exchange(sources[0], "ens")]
    low, high = across(inner)
    queries, own = call(
        project_kernel,
        "project",
        [((rows, COLS), BF16), ((rows, 2 * COLS), BF16)],
        "hv",
        [pltpu.VMEM((rows, LATENT_DIM), BF16), pltpu.SemaphoreType.DMA((CHUNKS,))],
        flops=rows * LATENT_DIM * 6 * COLS,
        moved=4 * 2**20,
    )(normed, weights)

    (outcome,) = call(
        interior_kernel,
        "attention_interior",
        [((rows, COLS), BF16)],
        "vvv",
        flops=rows * COLS * 2048,
        moved=2**21,
        exps=rows * 512,
    )(steps, queries, own)
    (outcome,) = call(
        edge_kernel,
        "attention_edges",
        [((rows, COLS), BF16)],
        "vvvvvv",
        flops=rows * COLS * 512,
        moved=2**20,
        exps=rows * 128,
    )(steps, queries, own, low, high, outcome)
    *pieces, own = lax.optimization_barrier((*pieces, own))
    pieces = pieces + [swap(piece, "core", 1) for piece in pieces]
    outcome, sources[-1] = lax.optimization_barrier((outcome, sources[-1]))
    attended = exchange(outcome.reshape(GROUP * members_num, part, COLS), ("quad", "core", "ens"))
    block = (halves, QUAD, CORES, members_num * shard, width)
    (weights,) = call(
        assemble_kernel,
        "assemble",
        [(block, BF16)],
        "a" * len(pieces),
        [pltpu.SemaphoreType.DMA((GROUP,))],
        moved=4 * 2**20,
        results="h",
    )(*pieces)

    prediction, grads = call(
        mix_kernel,
        "mix_loss_backward",
        [((FIELD_NUM, node_rows), F32), ((GROUP * members_num, part, COLS), BF16)],
        "vvhh" + "a" * len(sources),
        [
            pltpu.VMEM((node_rows, LATENT_DIM), BF16),
            pltpu.VMEM(observed_truth.shape, F32),
            pltpu.VMEM((FIELD_PAD, node_rows), F32),
            pltpu.VMEM((members_num, part, LATENT_DIM), BF16),
            pltpu.VMEM(block, BF16),
            pltpu.SemaphoreType.DMA((halves + 1 + len(sources),)),
        ],
        flops=node_rows * LATENT_DIM * 4 * width,
        moved=2**22,
        room=14,
    )(attended, cell_surface_factor[None], observed_truth, weights, *sources)
    grads = exchange(grads, ("quad", "core", "ens")).reshape(rows, COLS)

    edges, *inner = call(
        edge_back_kernel,
        "attention_edges_back",
        [((2, WINDOW - RIM, 2 * COLS), F32)] + rims,
        "vvvvvv",
        flops=rows * COLS * 1280,
        moved=2**20,
        exps=rows * 128,
    )(steps, queries, own, low, high, grads)
    from_low, from_high = across(inner)
    (kv_grads,) = call(
        interior_back_kernel,
        "attention_interior_back",
        [((rows, 2 * COLS), F32)],
        "vvvvv",
        flops=rows * COLS * 4096,
        moved=2**22,
        exps=rows * 512,
        room=10,
    )(steps, queries, own, grads, edges)
    (term,) = call(
        product_kernel,
        "product",
        [((LATENT_DIM, 2 * COLS), BF16)],
        "vvvv",
        flops=rows * LATENT_DIM * 8 * COLS,
        moved=2**22,
        room=16,
    )(normed, from_low, from_high, kv_grads)
    term, prediction = lax.optimization_barrier((term, prediction))
    term = exchange(term.reshape(-1, shard, 2 * COLS), everyone)
    (grad_kv,) = call(
        gather_kernel, "gather_sums", [((shard, 2 * LATENT_DIM), F32)], "v", flops=2**17, moved=2**20
    )(term.reshape(halves, GROUP, members_num, shard, 2 * COLS))

    if members_num == 2:
        got = jnp.roll(swap(prediction, "ens", 1), part, axis=1)
        lane = lax.broadcasted_iota(jnp.int32, prediction.shape, 1)
        prediction = jnp.where(lane // part == ens, prediction, got)
    else:
        prediction = prediction.reshape(FIELD_NUM, members_num, part).transpose(1, 0, 2)
        prediction = exchange(prediction, "ens").transpose(1, 0, 2)
    return (prediction.reshape(1, FIELD_NUM, node_rows), grad_kv)


def solution(mesh):
    space, ens = mesh.shape["space"], mesh.shape["ens"]
    split = Mesh(
        mesh.devices.reshape(space // GROUP, QUAD, CORES, ens), ("half", "quad", "core", "ens")
    )
    nodes = ("half", "quad", "core")
    shards = nodes + ("ens",)
    in_specs = (
        P("ens", nodes, None),
        P(shards, None),
        P(shards, None),
        P(shards, None),
        P(None, nodes),
        P(nodes),
        P(nodes, None),
    )
    out_specs = (P("ens", None, nodes), P(shards, None))
    return jax.shard_map(body, mesh=split, in_specs=in_specs, out_specs=out_specs, check_vma=False)
```

```python
import functools

import jax
import jax.numpy as jnp
from jax import lax
from jax.experimental import pallas as pl
from jax.experimental.pallas import tpu as pltpu
from jax.sharding import Mesh
from jax.sharding import PartitionSpec as P

LATENT_DIM = 1024
HEADS = 16
HEAD = 64
FIELD_NUM = 100
TILE = 64
RADIUS = 2
K_NB = 4
QUAD = 4
CORES = 2
GROUP = QUAD * CORES
COLS = LATENT_DIM // GROUP
RIM = RADIUS * TILE
FIELD_PAD = 128
PAIR = 2
WINDOW = (PAIR + 2 * RADIUS) * TILE
NOWHERE = 100
NOTE_ROWS = 16
CHUNKS = 4

NORM_EPS = 1e-06
SOFT_WIDTH = 0.0625
MASKED = -1e30

F32 = jnp.float32
BF16 = jnp.bfloat16

VMEM = pl.BlockSpec(memory_space=pltpu.VMEM)
SMEM = pl.BlockSpec(memory_space=pltpu.SMEM)
HBM = pl.BlockSpec(memory_space=pltpu.HBM)
ANYWHERE = pl.BlockSpec(memory_space=pl.ANY)
OVER_ROWS = (((0,), (0,)), ((), ()))
OVER_COLUMNS = (((1,), (1,)), ((), ()))


def call(kernel, name, outs, ins, scratch=(), flops=0, moved=0, exps=0, room=8, results=None):
    results = results or "v" * len(outs)
    spaces = {"s": SMEM, "v": VMEM, "h": HBM, "a": ANYWHERE}
    made = pl.pallas_call(
        kernel,
        out_shape=[
            pltpu.HBM(shape, kind) if space == "h" else jax.ShapeDtypeStruct(shape, kind)
            for (shape, kind), space in zip(outs, results)
        ],
        in_specs=[spaces[space] for space in ins],
        out_specs=[spaces[space] for space in results],
        scratch_shapes=list(scratch),
        compiler_params=pltpu.CompilerParams(vmem_limit_bytes=room * 2**20),
        cost_estimate=pl.CostEstimate(flops=flops, bytes_accessed=moved, transcendentals=exps),
        name=name,
    )

    def run(*args):
        return made(
            *[
                pltpu.with_memory_space_constraint(arg, pltpu.HBM) if space == "h" else arg
                for arg, space in zip(args, ins)
            ]
        )

    return run


def fetch(pairs, sems, first=0):
    copies = [
        pltpu.make_async_copy(source, target, sems.at[first + at])
        for at, (source, target) in enumerate(pairs)
    ]
    for copy in copies:
        copy.start()
    return copies


def wait(copies):
    for copy in copies:
        copy.wait()


def weights_kernel(w_any, mix_any, readout_any, columns_any, packed_any, *refs):
    w, columns, readout, packed, sems = refs
    copies = fetch(
        [(w_any, w), (readout_any, readout), (mix_any, packed.at[:, :LATENT_DIM])], sems
    )
    copies[0].wait()
    for g in range(GROUP):
        for part in range(3):
            at = (part * GROUP + g) * COLS
            columns[g, :, part * COLS : (part + 1) * COLS] = w[:, at : at + COLS]
    halves, _, members_num = columns_any.shape[:3]
    out = fetch(
        [
            (columns, columns_any.at[half, :, m])
            for half in range(halves)
            for m in range(members_num)
        ],
        sems,
        3,
    )
    wait(copies[1:])
    packed[:, LATENT_DIM:] = jnp.zeros((packed.shape[0], FIELD_PAD), BF16)
    packed[:, LATENT_DIM : LATENT_DIM + FIELD_NUM] = readout[...]
    wait(out + fetch([(packed, packed_any)], sems, 3 + len(out)))


def norm_kernel(near_any, source_any, normed_any, *refs):
    parts, (near, source, normed, sems) = refs[:-4], refs[-4:]
    ens = lax.axis_index("ens")
    copies = fetch([(source_any, source), (near_any, near)], sems)
    rows = source.shape[0]
    copies[0].wait()
    moves = []
    for step, part_any in enumerate(parts):
        count, part, _ = part_any.shape
        for m in range(count):
            place = (ens ^ step) if len(parts) == 2 else m
            place = pl.multiple_of(place * part, part)
            moves.append((source.at[pl.ds(place, part)], part_any.at[m]))
    out = fetch(moves, sems, 2)
    states = source[...].astype(F32)
    inverse = lax.rsqrt(jnp.mean(states * states, axis=-1, keepdims=True) + NORM_EPS)
    normed[:rows, :] = (states * inverse).astype(BF16)
    copies[1].wait()
    row = lax.broadcasted_iota(jnp.int32, (NOTE_ROWS, 128), 0)
    lane = lax.broadcasted_iota(jnp.int32, (NOTE_ROWS, 128), 1)
    note = jnp.zeros((NOTE_ROWS, 128), F32)
    tiles = near.shape[0]
    first_tile = lax.axis_index(("half", "quad", "core")) * tiles
    for tile in range(tiles):
        for slot in range(K_NB):
            at = near[tile, slot]
            step = jnp.where(at >= 0, at - first_tile - tile, NOWHERE).astype(F32)
            note = jnp.where((row == tile) & (lane == slot), step, note)
    normed[rows:, :] = jnp.zeros((NOTE_ROWS, LATENT_DIM), BF16)
    normed[rows:, :128] = note.astype(BF16)
    wait(out + fetch([(normed, normed_any)], sems, 2 + len(out)))


def owners():
    core, quad = lax.axis_index("core"), lax.axis_index("quad")
    return [(quad ^ step) * CORES + (core ^ flip) for flip in range(CORES) for step in range(QUAD)]


def collect_kernel(*refs):
    blocks, (normed_any, steps_ref, notes, sems) = refs[:GROUP], refs[GROUP:]
    block = blocks[0].shape[0] - NOTE_ROWS
    pairs = []
    for rows_ref, owner in zip(blocks, owners()):
        place = pl.ds(pl.multiple_of(owner * block, block), block)
        pairs.append((rows_ref.at[:block], normed_any.at[place]))
        pairs.append((rows_ref.at[block:, :128], notes.at[owner]))
    wait(fetch(pairs, sems))
    steps_ref[...] = notes[...].astype(F32)


def put_rims(rims, first, last):
    if len(rims) == 1:
        rims[0][...] = jnp.where(lax.axis_index("half") == 0, last, first)
    else:
        rims[0][...], rims[1][...] = first, last


def rims_kernel(normed_any, *refs):
    rows, sems = refs[-2:]
    if len(refs[0].shape) == 2:
        columns, w, rims = refs[:1], refs[1], refs[2:-2]
        pairs = [(columns[0], w)]
    else:
        columns, w, rims = refs[:2], refs[2], refs[3:-2]
        ens = lax.axis_index("ens")
        pairs = [(part, w.at[:, ens ^ step]) for step, part in enumerate(columns)]
    last = normed_any.shape[0] - RIM
    if len(rims) == 1:
        place = pl.multiple_of(jnp.where(lax.axis_index("half") == 0, last, 0), RIM)
        pairs.append((normed_any.at[pl.ds(place, RIM)], rows.at[0]))
    else:
        pairs += [(normed_any.at[:RIM], rows.at[0]), (normed_any.at[last:], rows.at[1])]
    wait(fetch(pairs, sems))
    weights = w[...].reshape(LATENT_DIM, 3 * COLS)[:, COLS:]
    for at, rim_ref in enumerate(rims):
        rim_ref[...] = jnp.dot(rows[at], weights, preferred_element_type=F32).astype(BF16)


def project_kernel(normed_any, w_ref, q_ref, kv_ref, normed, sems):
    chunk = normed.shape[0] // CHUNKS
    rows = [slice(at * chunk, (at + 1) * chunk) for at in range(CHUNKS)]
    copies = fetch([(normed_any.at[part], normed.at[part]) for part in rows], sems)
    weights = w_ref[...].reshape(LATENT_DIM, 3 * COLS)
    for part, copy in zip(rows, copies):
        copy.wait()
        projected = jnp.dot(normed[part, :], weights, preferred_element_type=F32).astype(BF16)
        q_ref[part, :] = projected[:, :COLS] * jnp.asarray(HEAD**-0.5, BF16)
        kv_ref[part, :] = projected[:, COLS:]


def assemble_kernel(*refs):
    pieces, (w_any, sems) = refs[:GROUP], refs[GROUP:]
    core, quad = lax.axis_index("core"), lax.axis_index("quad")
    pairs = [
        (piece, w_any.at[:, quad ^ (at % QUAD), core ^ (at // QUAD)])
        for at, piece in enumerate(pieces)
    ]
    wait(fetch(pairs, sems))


def by_head(rows):
    lane = lax.broadcasted_iota(jnp.int32, rows.shape, 1)
    zero = jnp.zeros_like(rows)
    return jnp.concatenate(
        [jnp.where(lane < HEAD, rows, zero), jnp.where(lane < HEAD, zero, rows)], axis=0
    )


def usable_keys(steps_ref, pair):
    lane = (lax.broadcasted_iota(jnp.int32, (1, WINDOW), 1) // TILE - RADIUS).astype(F32)
    masks = []
    for query_tile in range(PAIR):
        found = jnp.zeros((1, WINDOW), F32)
        for slot in range(K_NB):
            step = steps_ref[pair, query_tile : query_tile + 1, slot : slot + 1]
            found = jnp.where(lane - query_tile == step, 1.0, found)
        masks.append(found)
    row = lax.broadcasted_iota(jnp.int32, (2 * PAIR * TILE, 1), 0) // TILE % PAIR
    return jnp.where(row == 0, masks[0], masks[1]) > 0


def raised_scores(queries, keys, usable):
    scores = lax.dot_general(queries, keys, OVER_COLUMNS, preferred_element_type=F32)
    scores = jnp.where(usable, scores, MASKED)
    raised = jnp.exp(scores - jnp.max(scores, axis=-1, keepdims=True))
    return raised, 1.0 / jnp.sum(raised, axis=-1, keepdims=True)


def attend(steps_ref, pair, queries, keys, values):
    raised, share = raised_scores(by_head(queries), keys, usable_keys(steps_ref, pair))
    both = jnp.dot(raised.astype(BF16), values, preferred_element_type=F32) * share
    lane = lax.broadcasted_iota(jnp.int32, queries.shape, 1)
    half = PAIR * TILE
    return jnp.where(lane < HEAD, both[:half], both[half:]).astype(BF16)


def interior_kernel(steps_ref, q_ref, kv_ref, out_ref):
    step = PAIR * TILE
    pairs = q_ref.shape[0] // step
    for pair in range(1, pairs - 1):
        window = slice((pair - 1) * step, (pair + 2) * step)
        rows = slice(pair * step, (pair + 1) * step)
        out_ref[rows, :] = attend(
            steps_ref, pair, q_ref[rows, :], kv_ref[window, :COLS], kv_ref[window, COLS:]
        )


def edge_kernel(steps_ref, q_ref, kv_ref, low_ref, high_ref, done_ref, out_ref):
    step = PAIR * TILE
    count = q_ref.shape[0]
    pairs = count // step
    out_ref[step : count - step, :] = done_ref[step : count - step, :]
    first = jnp.concatenate([low_ref[...], kv_ref[: 2 * step, :]], axis=0)
    last = jnp.concatenate([kv_ref[count - 2 * step :, :], high_ref[...]], axis=0)
    for pair, window in ((0, first), (pairs - 1, last)):
        rows = slice(pair * step, (pair + 1) * step)
        out_ref[rows, :] = attend(
            steps_ref, pair, q_ref[rows, :], window[:, :COLS], window[:, COLS:]
        )


def attend_back(steps_ref, pair, queries, grads, keys, values):
    queries, grads = by_head(queries), by_head(grads)
    raised, share = raised_scores(queries, keys, usable_keys(steps_ref, pair))
    probs = raised * share
    grad_probs = lax.dot_general(grads, values, OVER_COLUMNS, preferred_element_type=F32)
    row_delta = jnp.sum(probs * grad_probs, axis=-1, keepdims=True)
    grad_scores = (probs * (grad_probs - row_delta)).astype(BF16)
    key_grad = lax.dot_general(grad_scores, queries, OVER_ROWS, preferred_element_type=F32)
    value_grad = lax.dot_general(probs.astype(BF16), grads, OVER_ROWS, preferred_element_type=F32)
    return key_grad, value_grad


def edge_back_kernel(
    steps_ref, q_ref, kv_ref, low_ref, high_ref, g_ref, part_ref, *rims
):
    outer = []
    step = PAIR * TILE
    count = q_ref.shape[0]
    first = jnp.concatenate([low_ref[...], kv_ref[: 2 * step, :]], axis=0)
    last = jnp.concatenate([kv_ref[count - 2 * step :, :], high_ref[...]], axis=0)
    pairs = count // step
    for edge, pair, window in ((0, 0, first), (1, pairs - 1, last)):
        rows = slice(pair * step, (pair + 1) * step)
        grads = attend_back(
            steps_ref, pair, q_ref[rows, :], g_ref[rows, :], window[:, :COLS], window[:, COLS:]
        )
        rim = slice(0, RIM) if edge == 0 else slice(WINDOW - RIM, WINDOW)
        own = slice(RIM, WINDOW) if edge == 0 else slice(0, WINDOW - RIM)
        for at, grad in enumerate(grads):
            columns = slice(at * COLS, (at + 1) * COLS)
            part_ref[edge, :, columns] = grad[own]
        outer.append(jnp.concatenate([grad[rim].astype(BF16) for grad in grads], axis=1))
    put_rims(rims, *outer)


def interior_back_kernel(steps_ref, q_ref, kv_ref, g_ref, part_ref, out_ref):
    step = PAIR * TILE
    count = q_ref.shape[0]
    pairs = count // step
    reach = 2 * step
    out_ref[:reach, :] = part_ref[0]
    out_ref[reach : count - reach, :] = jnp.zeros((count - 2 * reach, 2 * COLS), F32)
    out_ref[count - reach :, :] = part_ref[1]
    for pair in range(1, pairs - 1):
        window = slice((pair - 1) * step, (pair + 2) * step)
        rows = slice(pair * step, (pair + 1) * step)
        key_grad, value_grad = attend_back(
            steps_ref,
            pair,
            q_ref[rows, :],
            g_ref[rows, :],
            kv_ref[window, :COLS],
            kv_ref[window, COLS:],
        )
        out_ref[window, :COLS] += key_grad
        out_ref[window, COLS:] += value_grad


def slope(spread):
    return spread * lax.rsqrt(spread * spread + SOFT_WIDTH)


def mix_kernel(att_ref, factor_ref, truth_any, w_any, *refs):
    sources, refs = refs[:-8], refs[-8:]
    pred_ref, grad_ref, a, truth_ref, truth, source, w, sems = refs
    members_num, part, _ = source.shape
    halves = w.shape[0]
    ens = lax.axis_index("ens")
    copies = fetch([(w_any.at[half], w.at[half]) for half in range(halves)], sems)
    pairs = [(truth_any, truth_ref)]
    if len(sources) == 1:
        pairs.append((sources[0], source))
    else:
        pairs += [(rows.at[0], source.at[ens ^ step]) for step, rows in enumerate(sources)]
    others = fetch(pairs, sems, halves)
    for g in range(GROUP):
        for m in range(members_num):
            a[m * part : (m + 1) * part, g * COLS : (g + 1) * COLS] = att_ref[g * members_num + m]
    wait(others)
    lane_part = lax.broadcasted_iota(jnp.int32, (1, a.shape[0]), 1) // part
    own_truth, own_factor = truth_ref[...], factor_ref[...]
    for turn in range(1, members_num):
        at = lane_part - turn
        here = jnp.where(at < 0, at + members_num, at) == ens
        own_truth = jnp.where(here, pltpu.roll(truth_ref[...], turn * part, 1), own_truth)
        own_factor = jnp.where(here, pltpu.roll(factor_ref[...], turn * part, 1), own_factor)
    truth[...] = jnp.zeros_like(truth)
    truth[:FIELD_NUM, :] = own_truth
    hidden = source[...].reshape(a.shape).astype(F32)
    count = LATENT_DIM // halves
    for half in range(halves):
        copies[half].wait()
        mix = w[half].reshape(count, LATENT_DIM + FIELD_PAD)[:, :LATENT_DIM]
        hidden += jnp.dot(
            a[:, half * count : (half + 1) * count], mix, preferred_element_type=F32
        )
    both = w[...].reshape(LATENT_DIM, LATENT_DIM + FIELD_PAD)
    mix, readout = both[:, :LATENT_DIM], both[:, LATENT_DIM:]
    inverse = lax.rsqrt(jnp.mean(hidden * hidden, axis=-1, keepdims=True) + NORM_EPS)
    decoded = (hidden * inverse).astype(BF16)
    prediction = lax.dot_general(
        readout, decoded, (((0,), (1,)), ((), ())), preferred_element_type=F32
    )
    pred_ref[...] = prediction[:FIELD_NUM]
    spread = jnp.zeros_like(prediction)
    for other in range(1, members_num):
        spread = spread + slope(prediction - pltpu.roll(prediction, other * part, 1))
    derivative = own_factor / FIELD_NUM * (
        slope(prediction - truth[...]) - spread / (members_num - 1)
    )
    grad_decoded = lax.dot_general(
        derivative.astype(BF16), readout, (((0,), (1,)), ((), ())), preferred_element_type=F32
    )
    grad_hidden = inverse * grad_decoded - hidden * inverse**3 * jnp.mean(
        grad_decoded * hidden, axis=-1, keepdims=True
    )
    grads = lax.dot_general(
        grad_hidden.astype(BF16), mix, OVER_COLUMNS, preferred_element_type=F32
    ).astype(BF16)
    for g in range(GROUP):
        for m in range(members_num):
            grad_ref[g * members_num + m] = grads[
                m * part : (m + 1) * part, g * COLS : (g + 1) * COLS
            ]


def product_kernel(normed_ref, from_low_ref, from_high_ref, grads_ref, out_ref):
    count = normed_ref.shape[0]
    half, last = lax.axis_index("half"), lax.axis_size("half") - 1
    from_low = jnp.where(half > 0, from_low_ref[...].astype(F32), 0.0)
    from_high = jnp.where(half < last, from_high_ref[...].astype(F32), 0.0)
    grads = grads_ref[...]
    grads = jnp.concatenate(
        [
            grads[:RIM] + from_low,
            grads[RIM : count - RIM],
            grads[count - RIM :] + from_high,
        ],
        axis=0,
    )
    high = grads.astype(BF16)
    low = (grads - high.astype(F32)).astype(BF16)
    both = lax.dot_general(
        normed_ref[...], jnp.concatenate([high, low], axis=1), OVER_ROWS, preferred_element_type=F32
    )
    out_ref[...] = (both[:, : 2 * COLS] + both[:, 2 * COLS :]).astype(BF16)


def gather_kernel(parts_ref, out_ref):
    halves, _, members_num = parts_ref.shape[:3]
    for g in range(GROUP):
        total = None
        for half in range(halves):
            for m in range(members_num):
                part = parts_ref[half, g, m].astype(F32)
                total = part if total is None else total + part
        out_ref[:, g * COLS : (g + 1) * COLS] = total[:, :COLS]
        out_ref[:, LATENT_DIM + g * COLS : LATENT_DIM + (g + 1) * COLS] = total[:, COLS:]


def exchange(chunks, axes):
    return lax.all_to_all(chunks, axes, 0, 0)


def swap(value, axis, step):
    return lax.ppermute(value, axis, [(i, i ^ step) for i in range(lax.axis_size(axis))])


def in_order(mine, axis, at):
    if lax.axis_size(axis) != 2:
        return lax.all_gather(mine, axis, axis=at)
    other = swap(mine, axis, 1)
    first = lax.axis_index(axis) == 0
    return jnp.stack([jnp.where(first, mine, other), jnp.where(first, other, mine)], axis=at)


def body(members, w_attn, w_mix, readout_matrix, observed_truth, cell_surface_factor, neighbours):
    halves, members_num = lax.axis_size("half"), lax.axis_size("ens")
    nodes = ("half", "quad", "core")
    everyone = nodes + ("ens",)
    shard = w_attn.shape[0]
    node_rows = members.shape[1]
    rows = GROUP * node_rows
    part = node_rows // members_num
    up = [(i, i + 1) for i in range(halves - 1)]
    down = [(target, source) for source, target in up]
    ens = lax.axis_index("ens")
    width = LATENT_DIM + FIELD_PAD
    paired = members_num == 2
    copies = 1 if paired else members_num
    source_parts = 2 if paired else 1

    columns, packed = call(
        weights_kernel,
        "prepare_weights",
        [((halves, GROUP, copies, shard, 3 * COLS), BF16), ((shard, width), BF16)],
        "hhh",
        [
            pltpu.VMEM(w_attn.shape, BF16),
            pltpu.VMEM((GROUP, shard, 3 * COLS), BF16),
            pltpu.VMEM(readout_matrix.shape, BF16),
            pltpu.VMEM((shard, width), BF16),
            pltpu.SemaphoreType.DMA((4 + halves * copies,)),
        ],
        moved=2**20,
        results="hh",
    )(w_attn, w_mix, readout_matrix)
    normed, *sources = call(
        norm_kernel,
        "norm",
        [((node_rows + NOTE_ROWS, LATENT_DIM), BF16)]
        + [((1 if paired else members_num, part, LATENT_DIM), BF16)] * source_parts,
        "hh",
        [
            pltpu.SMEM(neighbours.shape, jnp.int32),
            pltpu.VMEM((node_rows, LATENT_DIM), BF16),
            pltpu.VMEM((node_rows + NOTE_ROWS, LATENT_DIM), BF16),
            pltpu.SemaphoreType.DMA((3 + max(2, members_num),)),
        ],
        flops=2**20,
        moved=2**20,
        results="h" + "h" * source_parts,
    )(neighbours, members.reshape(node_rows, LATENT_DIM))

    packed, normed = lax.optimization_barrier((in_order(packed, "half", 0), normed))
    near = [normed, swap(normed, "quad", 1)]
    if paired:
        columns = exchange(columns.reshape(-1, shard, 3 * COLS), nodes)
        columns, late = lax.optimization_barrier((columns, normed))
        columns = [columns, swap(columns, "ens", 1)]
    else:
        columns = [exchange(columns.reshape(-1, shard, 3 * COLS), everyone)]
        columns = [columns[0].reshape(LATENT_DIM, 3 * COLS)]
        late = normed
    near += [swap(late, "quad", step) for step in range(2, QUAD)]
    far = [swap(piece, "core", 1) for piece in near]
    normed, steps = call(
        collect_kernel,
        "collect",
        [((rows, LATENT_DIM), BF16), ((GROUP, NOTE_ROWS, 128), F32)],
        "a" * (2 * QUAD),
        [pltpu.VMEM((GROUP, NOTE_ROWS, 128), BF16), pltpu.SemaphoreType.DMA((2 * GROUP,))],
        results="hv",
    )(*near, *far)

    packed = in_order(packed, "ens", 1).reshape(halves, members_num * shard, width)
    packed, near[2] = lax.optimization_barrier((packed, near[2]))
    pieces = [packed] + [swap(packed, "quad", step) for step in range(1, QUAD)]

    rim = ((RIM, 2 * COLS), BF16)
    rims = [rim] if halves == 2 else [rim, rim]
    w_shape = (GROUP * halves, 2, shard, 3 * COLS) if paired else (LATENT_DIM, 3 * COLS)
    weights, *inner = call(
        rims_kernel,
        "project_rims",
        [(w_shape, BF16)] + rims,
        "h" + "a" * len(columns),
        [pltpu.VMEM((len(rims), RIM, LATENT_DIM), BF16), pltpu.SemaphoreType.DMA((4,))],
        flops=RIM * LATENT_DIM * 4 * COLS,
        moved=2**20,
    )(normed, *columns)
    def across(inner):
        if halves == 2:
            got = swap(inner[0], "half", 1)
            return got, got
        return lax.ppermute(inner[1], "half", up), lax.ppermute(inner[0], "half", down)

    weights, sources[-1] = lax.optimization_barrier((weights, sources[-1]))
    sources = [sources[0], swap(sources[1], "ens", 1)] if paired else [exchange(sources[0], "ens")]
    low, high = across(inner)
    queries, own = call(
        project_kernel,
        "project",
        [((rows, COLS), BF16), ((rows, 2 * COLS), BF16)],
        "hv",
        [pltpu.VMEM((rows, LATENT_DIM), BF16), pltpu.SemaphoreType.DMA((CHUNKS,))],
        flops=rows * LATENT_DIM * 6 * COLS,
        moved=4 * 2**20,
    )(normed, weights)

    (outcome,) = call(
        interior_kernel,
        "attention_interior",
        [((rows, COLS), BF16)],
        "vvv",
        flops=rows * COLS * 2048,
        moved=2**21,
        exps=rows * 512,
    )(steps, queries, own)
    (outcome,) = call(
        edge_kernel,
        "attention_edges",
        [((rows, COLS), BF16)],
        "vvvvvv",
        flops=rows * COLS * 512,
        moved=2**20,
        exps=rows * 128,
    )(steps, queries, own, low, high, outcome)
    *pieces, own = lax.optimization_barrier((*pieces, own))
    pieces = pieces + [swap(piece, "core", 1) for piece in pieces]
    attended = exchange(outcome.reshape(GROUP * members_num, part, COLS), ("quad", "core", "ens"))
    block = (halves, QUAD, CORES, members_num * shard, width)
    (weights,) = call(
        assemble_kernel,
        "assemble",
        [(block, BF16)],
        "a" * len(pieces),
        [pltpu.SemaphoreType.DMA((GROUP,))],
        moved=4 * 2**20,
        results="h",
    )(*pieces)

    prediction, grads = call(
        mix_kernel,
        "mix_loss_backward",
        [((FIELD_NUM, node_rows), F32), ((GROUP * members_num, part, COLS), BF16)],
        "vvhh" + "a" * len(sources),
        [
            pltpu.VMEM((node_rows, LATENT_DIM), BF16),
            pltpu.VMEM(observed_truth.shape, F32),
            pltpu.VMEM((FIELD_PAD, node_rows), F32),
            pltpu.VMEM((members_num, part, LATENT_DIM), BF16),
            pltpu.VMEM(block, BF16),
            pltpu.SemaphoreType.DMA((halves + 1 + len(sources),)),
        ],
        flops=node_rows * LATENT_DIM * 4 * width,
        moved=2**22,
        room=14,
    )(attended, cell_surface_factor[None], observed_truth, weights, *sources)
    grads = exchange(grads, ("quad", "core", "ens")).reshape(rows, COLS)

    edges, *inner = call(
        edge_back_kernel,
        "attention_edges_back",
        [((2, WINDOW - RIM, 2 * COLS), F32)] + rims,
        "vvvvvv",
        flops=rows * COLS * 1280,
        moved=2**20,
        exps=rows * 128,
    )(steps, queries, own, low, high, grads)
    from_low, from_high = across(inner)
    (kv_grads,) = call(
        interior_back_kernel,
        "attention_interior_back",
        [((rows, 2 * COLS), F32)],
        "vvvvv",
        flops=rows * COLS * 4096,
        moved=2**22,
        exps=rows * 512,
        room=10,
    )(steps, queries, own, grads, edges)
    (term,) = call(
        product_kernel,
        "product",
        [((LATENT_DIM, 2 * COLS), BF16)],
        "vvvv",
        flops=rows * LATENT_DIM * 8 * COLS,
        moved=2**22,
        room=16,
    )(normed, from_low, from_high, kv_grads)
    term, prediction = lax.optimization_barrier((term, prediction))
    term = exchange(term.reshape(-1, shard, 2 * COLS), everyone)
    (grad_kv,) = call(
        gather_kernel, "gather_sums", [((shard, 2 * LATENT_DIM), F32)], "v", flops=2**17, moved=2**20
    )(term.reshape(halves, GROUP, members_num, shard, 2 * COLS))

    if members_num == 2:
        got = jnp.roll(swap(prediction, "ens", 1), part, axis=1)
        lane = lax.broadcasted_iota(jnp.int32, prediction.shape, 1)
        prediction = jnp.where(lane // part == ens, prediction, got)
    else:
        prediction = prediction.reshape(FIELD_NUM, members_num, part).transpose(1, 0, 2)
        prediction = exchange(prediction, "ens").transpose(1, 0, 2)
    return (prediction.reshape(1, FIELD_NUM, node_rows), grad_kv)


def solution(mesh):
    space, ens = mesh.shape["space"], mesh.shape["ens"]
    split = Mesh(
        mesh.devices.reshape(space // GROUP, QUAD, CORES, ens), ("half", "quad", "core", "ens")
    )
    nodes = ("half", "quad", "core")
    shards = nodes + ("ens",)
    in_specs = (
        P("ens", nodes, None),
        P(shards, None),
        P(shards, None),
        P(shards, None),
        P(None, nodes),
        P(nodes),
        P(nodes, None),
    )
    out_specs = (P("ens", None, nodes), P(shards, None))
    return jax.shard_map(body, mesh=split, in_specs=in_specs, out_specs=out_specs, check_vma=False)
```

```python
import functools

import jax
import jax.numpy as jnp
from jax import lax
from jax.experimental import pallas as pl
from jax.experimental.pallas import tpu as pltpu
from jax.sharding import Mesh
from jax.sharding import PartitionSpec as P

LATENT_DIM = 1024
HEADS = 16
HEAD = 64
FIELD_NUM = 100
TILE = 64
RADIUS = 2
K_NB = 4
QUAD = 4
CORES = 2
GROUP = QUAD * CORES
COLS = LATENT_DIM // GROUP
RIM = RADIUS * TILE
FIELD_PAD = 128
PAIR = 2
WINDOW = (PAIR + 2 * RADIUS) * TILE
NOWHERE = 100
NOTE_ROWS = 16
CHUNKS = 4

NORM_EPS = 1e-06
SOFT_WIDTH = 0.0625
MASKED = -1e30

F32 = jnp.float32
BF16 = jnp.bfloat16

VMEM = pl.BlockSpec(memory_space=pltpu.VMEM)
SMEM = pl.BlockSpec(memory_space=pltpu.SMEM)
HBM = pl.BlockSpec(memory_space=pltpu.HBM)
ANYWHERE = pl.BlockSpec(memory_space=pl.ANY)
OVER_ROWS = (((0,), (0,)), ((), ()))
OVER_COLUMNS = (((1,), (1,)), ((), ()))


def call(kernel, name, outs, ins, scratch=(), flops=0, moved=0, exps=0, room=8, results=None):
    results = results or "v" * len(outs)
    spaces = {"s": SMEM, "v": VMEM, "h": HBM, "a": ANYWHERE}
    made = pl.pallas_call(
        kernel,
        out_shape=[
            pltpu.HBM(shape, kind) if space == "h" else jax.ShapeDtypeStruct(shape, kind)
            for (shape, kind), space in zip(outs, results)
        ],
        in_specs=[spaces[space] for space in ins],
        out_specs=[spaces[space] for space in results],
        scratch_shapes=list(scratch),
        compiler_params=pltpu.CompilerParams(vmem_limit_bytes=room * 2**20),
        cost_estimate=pl.CostEstimate(flops=flops, bytes_accessed=moved, transcendentals=exps),
        name=name,
    )

    def run(*args):
        return made(
            *[
                pltpu.with_memory_space_constraint(arg, pltpu.HBM) if space == "h" else arg
                for arg, space in zip(args, ins)
            ]
        )

    return run


def fetch(pairs, sems, first=0):
    copies = [
        pltpu.make_async_copy(source, target, sems.at[first + at])
        for at, (source, target) in enumerate(pairs)
    ]
    for copy in copies:
        copy.start()
    return copies


def wait(copies):
    for copy in copies:
        copy.wait()


def weights_kernel(w_any, mix_any, readout_any, columns_any, packed_any, *refs):
    w, columns, readout, packed, sems = refs
    copies = fetch(
        [(w_any, w), (readout_any, readout), (mix_any, packed.at[:, :LATENT_DIM])], sems
    )
    copies[0].wait()
    for g in range(GROUP):
        for part in range(3):
            at = (part * GROUP + g) * COLS
            columns[g, :, part * COLS : (part + 1) * COLS] = w[:, at : at + COLS]
    halves, _, members_num = columns_any.shape[:3]
    out = fetch(
        [
            (columns, columns_any.at[half, :, m])
            for half in range(halves)
            for m in range(members_num)
        ],
        sems,
        3,
    )
    wait(copies[1:])
    packed[:, LATENT_DIM:] = jnp.zeros((packed.shape[0], FIELD_PAD), BF16)
    packed[:, LATENT_DIM : LATENT_DIM + FIELD_NUM] = readout[...]
    wait(out + fetch([(packed, packed_any)], sems, 3 + len(out)))


def norm_kernel(near_any, source_any, normed_any, *refs):
    parts, (near, source, normed, sems) = refs[:-4], refs[-4:]
    ens = lax.axis_index("ens")
    copies = fetch([(source_any, source), (near_any, near)], sems)
    rows = source.shape[0]
    copies[0].wait()
    moves = []
    for step, part_any in enumerate(parts):
        count, part, _ = part_any.shape
        for m in range(count):
            place = (ens ^ step) if len(parts) == 2 else m
            place = pl.multiple_of(place * part, part)
            moves.append((source.at[pl.ds(place, part)], part_any.at[m]))
    out = fetch(moves, sems, 2)
    states = source[...].astype(F32)
    inverse = lax.rsqrt(jnp.mean(states * states, axis=-1, keepdims=True) + NORM_EPS)
    normed[:rows, :] = (states * inverse).astype(BF16)
    copies[1].wait()
    row = lax.broadcasted_iota(jnp.int32, (NOTE_ROWS, 128), 0)
    lane = lax.broadcasted_iota(jnp.int32, (NOTE_ROWS, 128), 1)
    note = jnp.zeros((NOTE_ROWS, 128), F32)
    tiles = near.shape[0]
    first_tile = lax.axis_index(("half", "quad", "core")) * tiles
    for tile in range(tiles):
        for slot in range(K_NB):
            at = near[tile, slot]
            step = jnp.where(at >= 0, at - first_tile - tile, NOWHERE).astype(F32)
            note = jnp.where((row == tile) & (lane == slot), step, note)
    normed[rows:, :] = jnp.zeros((NOTE_ROWS, LATENT_DIM), BF16)
    normed[rows:, :128] = note.astype(BF16)
    wait(out + fetch([(normed, normed_any)], sems, 2 + len(out)))


def owners():
    core, quad = lax.axis_index("core"), lax.axis_index("quad")
    return [(quad ^ step) * CORES + (core ^ flip) for flip in range(CORES) for step in range(QUAD)]


def collect_kernel(*refs):
    blocks, (normed_any, steps_ref, notes, sems) = refs[:GROUP], refs[GROUP:]
    block = blocks[0].shape[0] - NOTE_ROWS
    pairs = []
    for rows_ref, owner in zip(blocks, owners()):
        place = pl.ds(pl.multiple_of(owner * block, block), block)
        pairs.append((rows_ref.at[:block], normed_any.at[place]))
        pairs.append((rows_ref.at[block:, :128], notes.at[owner]))
    wait(fetch(pairs, sems))
    steps_ref[...] = notes[...].astype(F32)


def put_rims(rims, first, last):
    if len(rims) == 1:
        rims[0][...] = jnp.where(lax.axis_index("half") == 0, last, first)
    else:
        rims[0][...], rims[1][...] = first, last


def rims_kernel(normed_any, *refs):
    rows, sems = refs[-2:]
    if len(refs[0].shape) == 2:
        columns, w, rims = refs[:1], refs[1], refs[2:-2]
        pairs = [(columns[0], w)]
    else:
        columns, w, rims = refs[:2], refs[2], refs[3:-2]
        ens = lax.axis_index("ens")
        pairs = [(part, w.at[:, ens ^ step]) for step, part in enumerate(columns)]
    last = normed_any.shape[0] - RIM
    if len(rims) == 1:
        place = pl.multiple_of(jnp.where(lax.axis_index("half") == 0, last, 0), RIM)
        pairs.append((normed_any.at[pl.ds(place, RIM)], rows.at[0]))
    else:
        pairs += [(normed_any.at[:RIM], rows.at[0]), (normed_any.at[last:], rows.at[1])]
    wait(fetch(pairs, sems))
    weights = w[...].reshape(LATENT_DIM, 3 * COLS)[:, COLS:]
    for at, rim_ref in enumerate(rims):
        rim_ref[...] = jnp.dot(rows[at], weights, preferred_element_type=F32).astype(BF16)


def project_kernel(normed_any, w_ref, q_ref, kv_ref, normed, sems):
    chunk = normed.shape[0] // CHUNKS
    rows = [slice(at * chunk, (at + 1) * chunk) for at in range(CHUNKS)]
    copies = fetch([(normed_any.at[part], normed.at[part]) for part in rows], sems)
    weights = w_ref[...].reshape(LATENT_DIM, 3 * COLS)
    for part, copy in zip(rows, copies):
        copy.wait()
        projected = jnp.dot(normed[part, :], weights, preferred_element_type=F32).astype(BF16)
        q_ref[part, :] = projected[:, :COLS] * jnp.asarray(HEAD**-0.5, BF16)
        kv_ref[part, :] = projected[:, COLS:]


def assemble_kernel(*refs):
    pieces, (w_any, sems) = refs[:-2], refs[-2:]
    core, quad, ens = (lax.axis_index(axis) for axis in ("core", "quad", "ens"))
    pairs = []
    for at, piece in enumerate(pieces):
        if len(pieces) == GROUP:
            pairs.append((piece, w_any.at[:, quad ^ (at % QUAD), core ^ (at // QUAD), 0]))
        else:
            pairs += [
                (piece.at[step], w_any.at[:, quad ^ step, core ^ (at // 2), ens ^ (at % 2)])
                for step in range(QUAD)
            ]
    wait(fetch(pairs, sems))


def by_head(rows):
    lane = lax.broadcasted_iota(jnp.int32, rows.shape, 1)
    zero = jnp.zeros_like(rows)
    return jnp.concatenate(
        [jnp.where(lane < HEAD, rows, zero), jnp.where(lane < HEAD, zero, rows)], axis=0
    )


def usable_keys(steps_ref, pair):
    lane = (lax.broadcasted_iota(jnp.int32, (1, WINDOW), 1) // TILE - RADIUS).astype(F32)
    masks = []
    for query_tile in range(PAIR):
        found = jnp.zeros((1, WINDOW), F32)
        for slot in range(K_NB):
            step = steps_ref[pair, query_tile : query_tile + 1, slot : slot + 1]
            found = jnp.where(lane - query_tile == step, 1.0, found)
        masks.append(found)
    row = lax.broadcasted_iota(jnp.int32, (2 * PAIR * TILE, 1), 0) // TILE % PAIR
    return jnp.where(row == 0, masks[0], masks[1]) > 0


def raised_scores(queries, keys, usable):
    scores = lax.dot_general(queries, keys, OVER_COLUMNS, preferred_element_type=F32)
    scores = jnp.where(usable, scores, MASKED)
    raised = jnp.exp(scores - jnp.max(scores, axis=-1, keepdims=True))
    return raised, 1.0 / jnp.sum(raised, axis=-1, keepdims=True)


def attend(steps_ref, pair, queries, keys, values):
    raised, share = raised_scores(by_head(queries), keys, usable_keys(steps_ref, pair))
    both = jnp.dot(raised.astype(BF16), values, preferred_element_type=F32) * share
    lane = lax.broadcasted_iota(jnp.int32, queries.shape, 1)
    half = PAIR * TILE
    return jnp.where(lane < HEAD, both[:half], both[half:]).astype(BF16)


def interior_kernel(steps_ref, q_ref, kv_ref, out_ref):
    step = PAIR * TILE
    pairs = q_ref.shape[0] // step
    for pair in range(1, pairs - 1):
        window = slice((pair - 1) * step, (pair + 2) * step)
        rows = slice(pair * step, (pair + 1) * step)
        out_ref[rows, :] = attend(
            steps_ref, pair, q_ref[rows, :], kv_ref[window, :COLS], kv_ref[window, COLS:]
        )


def edge_kernel(steps_ref, q_ref, kv_ref, low_ref, high_ref, done_ref, out_ref):
    step = PAIR * TILE
    count = q_ref.shape[0]
    pairs = count // step
    out_ref[step : count - step, :] = done_ref[step : count - step, :]
    first = jnp.concatenate([low_ref[...], kv_ref[: 2 * step, :]], axis=0)
    last = jnp.concatenate([kv_ref[count - 2 * step :, :], high_ref[...]], axis=0)
    for pair, window in ((0, first), (pairs - 1, last)):
        rows = slice(pair * step, (pair + 1) * step)
        out_ref[rows, :] = attend(
            steps_ref, pair, q_ref[rows, :], window[:, :COLS], window[:, COLS:]
        )


def attend_back(steps_ref, pair, queries, grads, keys, values):
    queries, grads = by_head(queries), by_head(grads)
    raised, share = raised_scores(queries, keys, usable_keys(steps_ref, pair))
    probs = raised * share
    grad_probs = lax.dot_general(grads, values, OVER_COLUMNS, preferred_element_type=F32)
    row_delta = jnp.sum(probs * grad_probs, axis=-1, keepdims=True)
    grad_scores = (probs * (grad_probs - row_delta)).astype(BF16)
    key_grad = lax.dot_general(grad_scores, queries, OVER_ROWS, preferred_element_type=F32)
    value_grad = lax.dot_general(probs.astype(BF16), grads, OVER_ROWS, preferred_element_type=F32)
    return key_grad, value_grad


def edge_back_kernel(
    steps_ref, q_ref, kv_ref, low_ref, high_ref, g_ref, part_ref, *rims
):
    outer = []
    step = PAIR * TILE
    count = q_ref.shape[0]
    first = jnp.concatenate([low_ref[...], kv_ref[: 2 * step, :]], axis=0)
    last = jnp.concatenate([kv_ref[count - 2 * step :, :], high_ref[...]], axis=0)
    pairs = count // step
    for edge, pair, window in ((0, 0, first), (1, pairs - 1, last)):
        rows = slice(pair * step, (pair + 1) * step)
        grads = attend_back(
            steps_ref, pair, q_ref[rows, :], g_ref[rows, :], window[:, :COLS], window[:, COLS:]
        )
        rim = slice(0, RIM) if edge == 0 else slice(WINDOW - RIM, WINDOW)
        own = slice(RIM, WINDOW) if edge == 0 else slice(0, WINDOW - RIM)
        for at, grad in enumerate(grads):
            columns = slice(at * COLS, (at + 1) * COLS)
            part_ref[edge, :, columns] = grad[own]
        outer.append(jnp.concatenate([grad[rim].astype(BF16) for grad in grads], axis=1))
    put_rims(rims, *outer)


def interior_back_kernel(steps_ref, q_ref, kv_ref, g_ref, part_ref, out_ref):
    step = PAIR * TILE
    count = q_ref.shape[0]
    pairs = count // step
    reach = 2 * step
    out_ref[:reach, :] = part_ref[0]
    out_ref[reach : count - reach, :] = jnp.zeros((count - 2 * reach, 2 * COLS), F32)
    out_ref[count - reach :, :] = part_ref[1]
    for pair in range(1, pairs - 1):
        window = slice((pair - 1) * step, (pair + 2) * step)
        rows = slice(pair * step, (pair + 1) * step)
        key_grad, value_grad = attend_back(
            steps_ref,
            pair,
            q_ref[rows, :],
            g_ref[rows, :],
            kv_ref[window, :COLS],
            kv_ref[window, COLS:],
        )
        out_ref[window, :COLS] += key_grad
        out_ref[window, COLS:] += value_grad


def slope(spread):
    return spread * lax.rsqrt(spread * spread + SOFT_WIDTH)


def mix_kernel(att_ref, factor_ref, truth_any, w_any, *refs):
    sources, refs = refs[:-8], refs[-8:]
    pred_ref, grad_ref, a, truth_ref, truth, source, w, sems = refs
    members_num, part, _ = source.shape
    halves = w.shape[0]
    ens = lax.axis_index("ens")
    copies = fetch([(w_any.at[half], w.at[half]) for half in range(halves)], sems)
    pairs = [(truth_any, truth_ref)]
    if len(sources) == 1:
        pairs.append((sources[0], source))
    else:
        pairs += [(rows.at[0], source.at[ens ^ step]) for step, rows in enumerate(sources)]
    others = fetch(pairs, sems, halves)
    for g in range(GROUP):
        for m in range(members_num):
            a[m * part : (m + 1) * part, g * COLS : (g + 1) * COLS] = att_ref[g * members_num + m]
    wait(others)
    lane_part = lax.broadcasted_iota(jnp.int32, (1, a.shape[0]), 1) // part
    own_truth, own_factor = truth_ref[...], factor_ref[...]
    for turn in range(1, members_num):
        at = lane_part - turn
        here = jnp.where(at < 0, at + members_num, at) == ens
        own_truth = jnp.where(here, pltpu.roll(truth_ref[...], turn * part, 1), own_truth)
        own_factor = jnp.where(here, pltpu.roll(factor_ref[...], turn * part, 1), own_factor)
    truth[...] = jnp.zeros_like(truth)
    truth[:FIELD_NUM, :] = own_truth
    hidden = source[...].reshape(a.shape).astype(F32)
    count = LATENT_DIM // halves
    for half in range(halves):
        copies[half].wait()
        mix = w[half].reshape(count, LATENT_DIM + FIELD_PAD)[:, :LATENT_DIM]
        hidden += jnp.dot(
            a[:, half * count : (half + 1) * count], mix, preferred_element_type=F32
        )
    both = w[...].reshape(LATENT_DIM, LATENT_DIM + FIELD_PAD)
    mix, readout = both[:, :LATENT_DIM], both[:, LATENT_DIM:]
    inverse = lax.rsqrt(jnp.mean(hidden * hidden, axis=-1, keepdims=True) + NORM_EPS)
    decoded = (hidden * inverse).astype(BF16)
    prediction = lax.dot_general(
        readout, decoded, (((0,), (1,)), ((), ())), preferred_element_type=F32
    )
    pred_ref[...] = prediction[:FIELD_NUM]
    spread = jnp.zeros_like(prediction)
    for other in range(1, members_num):
        spread = spread + slope(prediction - pltpu.roll(prediction, other * part, 1))
    derivative = own_factor / FIELD_NUM * (
        slope(prediction - truth[...]) - spread / (members_num - 1)
    )
    grad_decoded = lax.dot_general(
        derivative.astype(BF16), readout, (((0,), (1,)), ((), ())), preferred_element_type=F32
    )
    grad_hidden = inverse * grad_decoded - hidden * inverse**3 * jnp.mean(
        grad_decoded * hidden, axis=-1, keepdims=True
    )
    grads = lax.dot_general(
        grad_hidden.astype(BF16), mix, OVER_COLUMNS, preferred_element_type=F32
    ).astype(BF16)
    for g in range(GROUP):
        for m in range(members_num):
            grad_ref[g * members_num + m] = grads[
                m * part : (m + 1) * part, g * COLS : (g + 1) * COLS
            ]


def product_kernel(normed_ref, from_low_ref, from_high_ref, grads_ref, out_ref):
    count = normed_ref.shape[0]
    half, last = lax.axis_index("half"), lax.axis_size("half") - 1
    from_low = jnp.where(half > 0, from_low_ref[...].astype(F32), 0.0)
    from_high = jnp.where(half < last, from_high_ref[...].astype(F32), 0.0)
    grads = grads_ref[...]
    grads = jnp.concatenate(
        [
            grads[:RIM] + from_low,
            grads[RIM : count - RIM],
            grads[count - RIM :] + from_high,
        ],
        axis=0,
    )
    high = grads.astype(BF16)
    low = (grads - high.astype(F32)).astype(BF16)
    both = lax.dot_general(
        normed_ref[...], jnp.concatenate([high, low], axis=1), OVER_ROWS, preferred_element_type=F32
    )
    out_ref[...] = (both[:, : 2 * COLS] + both[:, 2 * COLS :]).astype(BF16)


def gather_kernel(parts_ref, out_ref):
    halves, _, members_num = parts_ref.shape[:3]
    for g in range(GROUP):
        total = None
        for half in range(halves):
            for m in range(members_num):
                part = parts_ref[half, g, m].astype(F32)
                total = part if total is None else total + part
        out_ref[:, g * COLS : (g + 1) * COLS] = total[:, :COLS]
        out_ref[:, LATENT_DIM + g * COLS : LATENT_DIM + (g + 1) * COLS] = total[:, COLS:]


def exchange(chunks, axes):
    return lax.all_to_all(chunks, axes, 0, 0)


def swap(value, axis, step):
    return lax.ppermute(value, axis, [(i, i ^ step) for i in range(lax.axis_size(axis))])


def in_order(mine, axis, at):
    if lax.axis_size(axis) != 2:
        return lax.all_gather(mine, axis, axis=at)
    other = swap(mine, axis, 1)
    first = lax.axis_index(axis) == 0
    return jnp.stack([jnp.where(first, mine, other), jnp.where(first, other, mine)], axis=at)


def body(members, w_attn, w_mix, readout_matrix, observed_truth, cell_surface_factor, neighbours):
    halves, members_num = lax.axis_size("half"), lax.axis_size("ens")
    nodes = ("half", "quad", "core")
    everyone = nodes + ("ens",)
    shard = w_attn.shape[0]
    node_rows = members.shape[1]
    rows = GROUP * node_rows
    part = node_rows // members_num
    up = [(i, i + 1) for i in range(halves - 1)]
    down = [(target, source) for source, target in up]
    ens = lax.axis_index("ens")
    width = LATENT_DIM + FIELD_PAD
    paired = members_num == 2
    copies = 1 if paired else members_num
    source_parts = 2 if paired else 1

    columns, packed = call(
        weights_kernel,
        "prepare_weights",
        [((halves, GROUP, copies, shard, 3 * COLS), BF16), ((shard, width), BF16)],
        "hhh",
        [
            pltpu.VMEM(w_attn.shape, BF16),
            pltpu.VMEM((GROUP, shard, 3 * COLS), BF16),
            pltpu.VMEM(readout_matrix.shape, BF16),
            pltpu.VMEM((shard, width), BF16),
            pltpu.SemaphoreType.DMA((4 + halves * copies,)),
        ],
        moved=2**20,
        results="hh",
    )(w_attn, w_mix, readout_matrix)
    normed, *sources = call(
        norm_kernel,
        "norm",
        [((node_rows + NOTE_ROWS, LATENT_DIM), BF16)]
        + [((1 if paired else members_num, part, LATENT_DIM), BF16)] * source_parts,
        "hh",
        [
            pltpu.SMEM(neighbours.shape, jnp.int32),
            pltpu.VMEM((node_rows, LATENT_DIM), BF16),
            pltpu.VMEM((node_rows + NOTE_ROWS, LATENT_DIM), BF16),
            pltpu.SemaphoreType.DMA((3 + max(2, members_num),)),
        ],
        flops=2**20,
        moved=2**20,
        results="h" + "h" * source_parts,
    )(neighbours, members.reshape(node_rows, LATENT_DIM))

    packed, normed = lax.optimization_barrier((in_order(packed, "half", 0), normed))
    near = [normed, swap(normed, "quad", 1), None, swap(normed, "quad", 3)]
    if paired:
        columns = exchange(columns.reshape(-1, shard, 3 * COLS), nodes)
        columns, late = lax.optimization_barrier((columns, normed))
        columns = [columns, swap(columns, "ens", 1)]
    else:
        columns = [exchange(columns.reshape(-1, shard, 3 * COLS), everyone)]
        columns = [columns[0].reshape(LATENT_DIM, 3 * COLS)]
        late = normed
    near[2] = swap(late, "quad", 2)
    far = [swap(piece, "core", 1) for piece in near]
    normed, steps = call(
        collect_kernel,
        "collect",
        [((rows, LATENT_DIM), BF16), ((GROUP, NOTE_ROWS, 128), F32)],
        "a" * (2 * QUAD),
        [pltpu.VMEM((GROUP, NOTE_ROWS, 128), BF16), pltpu.SemaphoreType.DMA((2 * GROUP,))],
        moved=4 * 2**20,
        results="hv",
    )(*near, *far)

    if not paired:
        packed = in_order(packed, "ens", 1).reshape(halves, members_num * shard, width)
    packed, near[3] = lax.optimization_barrier((packed, near[3]))
    pieces = [packed] + [swap(packed, "quad", step) for step in range(1, QUAD)]

    rim = ((RIM, 2 * COLS), BF16)
    rims = [rim] if halves == 2 else [rim, rim]
    w_shape = (GROUP * halves, 2, shard, 3 * COLS) if paired else (LATENT_DIM, 3 * COLS)
    weights, *inner = call(
        rims_kernel,
        "project_rims",
        [(w_shape, BF16)] + rims,
        "h" + "a" * len(columns),
        [pltpu.VMEM((len(rims), RIM, LATENT_DIM), BF16), pltpu.SemaphoreType.DMA((4,))],
        flops=RIM * LATENT_DIM * 4 * COLS,
        moved=2**20,
    )(normed, *columns)
    def across(inner):
        if halves == 2:
            got = swap(inner[0], "half", 1)
            return got, got
        return lax.ppermute(inner[1], "half", up), lax.ppermute(inner[0], "half", down)

    if paired:
        pieces = jnp.stack(pieces)
        weights, pieces = lax.optimization_barrier((weights, pieces))
        pieces = [pieces, swap(pieces, "ens", 1)]
    weights, sources[-1] = lax.optimization_barrier((weights, sources[-1]))
    sources = [sources[0], swap(sources[1], "ens", 1)] if paired else [exchange(sources[0], "ens")]
    low, high = across(inner)
    queries, own = call(
        project_kernel,
        "project",
        [((rows, COLS), BF16), ((rows, 2 * COLS), BF16)],
        "hv",
        [pltpu.VMEM((rows, LATENT_DIM), BF16), pltpu.SemaphoreType.DMA((CHUNKS,))],
        flops=rows * LATENT_DIM * 6 * COLS,
        moved=4 * 2**20,
    )(normed, weights)

    (outcome,) = call(
        interior_kernel,
        "attention_interior",
        [((rows, COLS), BF16)],
        "vvv",
        flops=rows * COLS * 2048,
        moved=2**21,
        exps=rows * 512,
    )(steps, queries, own)
    (outcome,) = call(
        edge_kernel,
        "attention_edges",
        [((rows, COLS), BF16)],
        "vvvvvv",
        flops=rows * COLS * 512,
        moved=2**20,
        exps=rows * 128,
    )(steps, queries, own, low, high, outcome)
    *pieces, own = lax.optimization_barrier((*pieces, own))
    pieces = pieces + [swap(piece, "core", 1) for piece in pieces]
    attended = exchange(outcome.reshape(GROUP * members_num, part, COLS), ("quad", "core", "ens"))
    block = (halves, QUAD, CORES) + ((2, shard) if paired else (1, members_num * shard)) + (width,)
    (weights,) = call(
        assemble_kernel,
        "assemble",
        [(block, BF16)],
        "a" * len(pieces),
        [pltpu.SemaphoreType.DMA((2 * GROUP,))],
        moved=4 * 2**20,
        results="h",
    )(*pieces)

    prediction, grads = call(
        mix_kernel,
        "mix_loss_backward",
        [((FIELD_NUM, node_rows), F32), ((GROUP * members_num, part, COLS), BF16)],
        "vvhh" + "a" * len(sources),
        [
            pltpu.VMEM((node_rows, LATENT_DIM), BF16),
            pltpu.VMEM(observed_truth.shape, F32),
            pltpu.VMEM((FIELD_PAD, node_rows), F32),
            pltpu.VMEM((members_num, part, LATENT_DIM), BF16),
            pltpu.VMEM(block, BF16),
            pltpu.SemaphoreType.DMA((halves + 1 + len(sources),)),
        ],
        flops=node_rows * LATENT_DIM * 4 * width,
        moved=2**22,
        room=14,
    )(attended, cell_surface_factor[None], observed_truth, weights, *sources)
    grads = exchange(grads, ("quad", "core", "ens")).reshape(rows, COLS)

    edges, *inner = call(
        edge_back_kernel,
        "attention_edges_back",
        [((2, WINDOW - RIM, 2 * COLS), F32)] + rims,
        "vvvvvv",
        flops=rows * COLS * 1280,
        moved=2**20,
        exps=rows * 128,
    )(steps, queries, own, low, high, grads)
    from_low, from_high = across(inner)
    (kv_grads,) = call(
        interior_back_kernel,
        "attention_interior_back",
        [((rows, 2 * COLS), F32)],
        "vvvvv",
        flops=rows * COLS * 4096,
        moved=2**22,
        exps=rows * 512,
        room=10,
    )(steps, queries, own, grads, edges)
    (term,) = call(
        product_kernel,
        "product",
        [((LATENT_DIM, 2 * COLS), BF16)],
        "vvvv",
        flops=rows * LATENT_DIM * 8 * COLS,
        moved=2**22,
        room=16,
    )(normed, from_low, from_high, kv_grads)
    term, prediction = lax.optimization_barrier((term, prediction))
    term = exchange(term.reshape(-1, shard, 2 * COLS), everyone)
    (grad_kv,) = call(
        gather_kernel, "gather_sums", [((shard, 2 * LATENT_DIM), F32)], "v", flops=2**17, moved=2**20
    )(term.reshape(halves, GROUP, members_num, shard, 2 * COLS))

    if members_num == 2:
        got = jnp.roll(swap(prediction, "ens", 1), part, axis=1)
        lane = lax.broadcasted_iota(jnp.int32, prediction.shape, 1)
        prediction = jnp.where(lane // part == ens, prediction, got)
    else:
        prediction = prediction.reshape(FIELD_NUM, members_num, part).transpose(1, 0, 2)
        prediction = exchange(prediction, "ens").transpose(1, 0, 2)
    return (prediction.reshape(1, FIELD_NUM, node_rows), grad_kv)


def solution(mesh):
    space, ens = mesh.shape["space"], mesh.shape["ens"]
    split = Mesh(
        mesh.devices.reshape(space // GROUP, QUAD, CORES, ens), ("half", "quad", "core", "ens")
    )
    nodes = ("half", "quad", "core")
    shards = nodes + ("ens",)
    in_specs = (
        P("ens", nodes, None),
        P(shards, None),
        P(shards, None),
        P(shards, None),
        P(None, nodes),
        P(nodes),
        P(nodes, None),
    )
    out_specs = (P("ens", None, nodes), P(shards, None))
    return jax.shard_map(body, mesh=split, in_specs=in_specs, out_specs=out_specs, check_vma=False)
```

```python
import functools

import jax
import jax.numpy as jnp
from jax import lax
from jax.experimental import pallas as pl
from jax.experimental.pallas import tpu as pltpu
from jax.sharding import Mesh
from jax.sharding import PartitionSpec as P

LATENT_DIM = 1024
HEADS = 16
HEAD = 64
FIELD_NUM = 100
TILE = 64
RADIUS = 2
K_NB = 4
QUAD = 4
CORES = 2
GROUP = QUAD * CORES
COLS = LATENT_DIM // GROUP
RIM = RADIUS * TILE
FIELD_PAD = 128
PAIR = 2
WINDOW = (PAIR + 2 * RADIUS) * TILE
NOWHERE = 100
NOTE_ROWS = 16
CHUNKS = 4

NORM_EPS = 1e-06
SOFT_WIDTH = 0.0625
MASKED = -1e30

F32 = jnp.float32
BF16 = jnp.bfloat16

VMEM = pl.BlockSpec(memory_space=pltpu.VMEM)
SMEM = pl.BlockSpec(memory_space=pltpu.SMEM)
HBM = pl.BlockSpec(memory_space=pltpu.HBM)
ANYWHERE = pl.BlockSpec(memory_space=pl.ANY)
OVER_ROWS = (((0,), (0,)), ((), ()))
OVER_COLUMNS = (((1,), (1,)), ((), ()))


def call(kernel, name, outs, ins, scratch=(), flops=0, moved=0, exps=0, room=8, results=None):
    results = results or "v" * len(outs)
    spaces = {"s": SMEM, "v": VMEM, "h": HBM, "a": ANYWHERE}
    made = pl.pallas_call(
        kernel,
        out_shape=[
            pltpu.HBM(shape, kind) if space == "h" else jax.ShapeDtypeStruct(shape, kind)
            for (shape, kind), space in zip(outs, results)
        ],
        in_specs=[spaces[space] for space in ins],
        out_specs=[spaces[space] for space in results],
        scratch_shapes=list(scratch),
        compiler_params=pltpu.CompilerParams(vmem_limit_bytes=room * 2**20),
        cost_estimate=pl.CostEstimate(flops=flops, bytes_accessed=moved, transcendentals=exps),
        name=name,
    )

    def run(*args):
        return made(
            *[
                pltpu.with_memory_space_constraint(arg, pltpu.HBM) if space == "h" else arg
                for arg, space in zip(args, ins)
            ]
        )

    return run


def fetch(pairs, sems, first=0):
    copies = [
        pltpu.make_async_copy(source, target, sems.at[first + at])
        for at, (source, target) in enumerate(pairs)
    ]
    for copy in copies:
        copy.start()
    return copies


def wait(copies):
    for copy in copies:
        copy.wait()


def weights_kernel(w_any, mix_any, readout_any, columns_any, packed_any, *refs):
    w, columns, readout, packed, sems = refs
    copies = fetch(
        [(w_any, w), (readout_any, readout), (mix_any, packed.at[:, :LATENT_DIM])], sems
    )
    copies[0].wait()
    for g in range(GROUP):
        for part in range(3):
            at = (part * GROUP + g) * COLS
            columns[g, :, part * COLS : (part + 1) * COLS] = w[:, at : at + COLS]
    halves, _, members_num = columns_any.shape[:3]
    out = fetch(
        [
            (columns, columns_any.at[half, :, m])
            for half in range(halves)
            for m in range(members_num)
        ],
        sems,
        3,
    )
    wait(copies[1:])
    packed[:, LATENT_DIM:] = jnp.zeros((packed.shape[0], FIELD_PAD), BF16)
    packed[:, LATENT_DIM : LATENT_DIM + FIELD_NUM] = readout[...]
    wait(out + fetch([(packed, packed_any)], sems, 3 + len(out)))


def norm_kernel(near_any, source_any, normed_any, *refs):
    parts, (near, source, normed, sems) = refs[:-4], refs[-4:]
    ens = lax.axis_index("ens")
    copies = fetch([(source_any, source), (near_any, near)], sems)
    rows = source.shape[0]
    copies[0].wait()
    moves = []
    for step, part_any in enumerate(parts):
        count, part, _ = part_any.shape
        for m in range(count):
            place = (ens ^ step) if len(parts) == 2 else m
            place = pl.multiple_of(place * part, part)
            moves.append((source.at[pl.ds(place, part)], part_any.at[m]))
    out = fetch(moves, sems, 2)
    states = source[...].astype(F32)
    inverse = lax.rsqrt(jnp.mean(states * states, axis=-1, keepdims=True) + NORM_EPS)
    normed[:rows, :] = (states * inverse).astype(BF16)
    copies[1].wait()
    row = lax.broadcasted_iota(jnp.int32, (NOTE_ROWS, 128), 0)
    lane = lax.broadcasted_iota(jnp.int32, (NOTE_ROWS, 128), 1)
    note = jnp.zeros((NOTE_ROWS, 128), F32)
    tiles = near.shape[0]
    first_tile = lax.axis_index(("half", "quad", "core")) * tiles
    for tile in range(tiles):
        for slot in range(K_NB):
            at = near[tile, slot]
            step = jnp.where(at >= 0, at - first_tile - tile, NOWHERE).astype(F32)
            note = jnp.where((row == tile) & (lane == slot), step, note)
    normed[rows:, :] = jnp.zeros((NOTE_ROWS, LATENT_DIM), BF16)
    normed[rows:, :128] = note.astype(BF16)
    wait(out + fetch([(normed, normed_any)], sems, 2 + len(out)))


def owners():
    core, quad = lax.axis_index("core"), lax.axis_index("quad")
    return [(quad ^ step) * CORES + (core ^ flip) for flip in range(CORES) for step in range(QUAD)]


def collect_kernel(*refs):
    blocks, (normed_any, steps_ref, notes, sems) = refs[:GROUP], refs[GROUP:]
    block = blocks[0].shape[0] - NOTE_ROWS
    pairs = []
    for rows_ref, owner in zip(blocks, owners()):
        place = pl.ds(pl.multiple_of(owner * block, block), block)
        pairs.append((rows_ref.at[:block], normed_any.at[place]))
        pairs.append((rows_ref.at[block:, :128], notes.at[owner]))
    wait(fetch(pairs, sems))
    steps_ref[...] = notes[...].astype(F32)


def put_rims(rims, first, last):
    if len(rims) == 1:
        rims[0][...] = jnp.where(lax.axis_index("half") == 0, last, first)
    else:
        rims[0][...], rims[1][...] = first, last


def rims_kernel(normed_any, *refs):
    rows, sems = refs[-2:]
    if len(refs[0].shape) == 2:
        columns, w, rims = refs[:1], refs[1], refs[2:-2]
        pairs = [(columns[0], w)]
    else:
        columns, w, rims = refs[:2], refs[2], refs[3:-2]
        ens = lax.axis_index("ens")
        pairs = [(part, w.at[:, ens ^ step]) for step, part in enumerate(columns)]
    last = normed_any.shape[0] - RIM
    if len(rims) == 1:
        place = pl.multiple_of(jnp.where(lax.axis_index("half") == 0, last, 0), RIM)
        pairs.append((normed_any.at[pl.ds(place, RIM)], rows.at[0]))
    else:
        pairs += [(normed_any.at[:RIM], rows.at[0]), (normed_any.at[last:], rows.at[1])]
    wait(fetch(pairs, sems))
    weights = w[...].reshape(LATENT_DIM, 3 * COLS)[:, COLS:]
    for at, rim_ref in enumerate(rims):
        rim_ref[...] = jnp.dot(rows[at], weights, preferred_element_type=F32).astype(BF16)


def project_kernel(normed_any, w_ref, q_ref, kv_ref, normed, sems):
    chunk = normed.shape[0] // CHUNKS
    rows = [slice(at * chunk, (at + 1) * chunk) for at in range(CHUNKS)]
    copies = fetch([(normed_any.at[part], normed.at[part]) for part in rows], sems)
    weights = w_ref[...].reshape(LATENT_DIM, 3 * COLS)
    for part, copy in zip(rows, copies):
        copy.wait()
        projected = jnp.dot(normed[part, :], weights, preferred_element_type=F32).astype(BF16)
        q_ref[part, :] = projected[:, :COLS] * jnp.asarray(HEAD**-0.5, BF16)
        kv_ref[part, :] = projected[:, COLS:]


def assemble_kernel(*refs):
    pieces, (w_any, sems) = refs[:GROUP], refs[GROUP:]
    core, quad = lax.axis_index("core"), lax.axis_index("quad")
    pairs = []
    for at, piece in enumerate(pieces):
        place = (quad ^ (at % QUAD), core ^ (at // QUAD))
        if piece.shape[0] == w_any.shape[0]:
            pairs.append((piece, w_any.at[:, place[0], place[1], 0]))
        else:
            half, ens = lax.axis_index("half"), lax.axis_index("ens")
            pairs += [
                (piece.at[step], w_any.at[half ^ (step % 2), place[0], place[1], ens ^ (step // 2)])
                for step in range(4)
            ]
    wait(fetch(pairs, sems))


def by_head(rows):
    lane = lax.broadcasted_iota(jnp.int32, rows.shape, 1)
    zero = jnp.zeros_like(rows)
    return jnp.concatenate(
        [jnp.where(lane < HEAD, rows, zero), jnp.where(lane < HEAD, zero, rows)], axis=0
    )


def usable_keys(steps_ref, pair):
    lane = (lax.broadcasted_iota(jnp.int32, (1, WINDOW), 1) // TILE - RADIUS).astype(F32)
    masks = []
    for query_tile in range(PAIR):
        found = jnp.zeros((1, WINDOW), F32)
        for slot in range(K_NB):
            step = steps_ref[pair, query_tile : query_tile + 1, slot : slot + 1]
            found = jnp.where(lane - query_tile == step, 1.0, found)
        masks.append(found)
    row = lax.broadcasted_iota(jnp.int32, (2 * PAIR * TILE, 1), 0) // TILE % PAIR
    return jnp.where(row == 0, masks[0], masks[1]) > 0


def raised_scores(queries, keys, usable):
    scores = lax.dot_general(queries, keys, OVER_COLUMNS, preferred_element_type=F32)
    scores = jnp.where(usable, scores, MASKED)
    raised = jnp.exp(scores - jnp.max(scores, axis=-1, keepdims=True))
    return raised, 1.0 / jnp.sum(raised, axis=-1, keepdims=True)


def attend(steps_ref, pair, queries, keys, values):
    raised, share = raised_scores(by_head(queries), keys, usable_keys(steps_ref, pair))
    both = jnp.dot(raised.astype(BF16), values, preferred_element_type=F32) * share
    lane = lax.broadcasted_iota(jnp.int32, queries.shape, 1)
    half = PAIR * TILE
    return jnp.where(lane < HEAD, both[:half], both[half:]).astype(BF16)


def interior_kernel(steps_ref, q_ref, kv_ref, out_ref):
    step = PAIR * TILE
    pairs = q_ref.shape[0] // step
    for pair in range(1, pairs - 1):
        window = slice((pair - 1) * step, (pair + 2) * step)
        rows = slice(pair * step, (pair + 1) * step)
        out_ref[rows, :] = attend(
            steps_ref, pair, q_ref[rows, :], kv_ref[window, :COLS], kv_ref[window, COLS:]
        )


def edge_kernel(steps_ref, q_ref, kv_ref, low_ref, high_ref, done_ref, out_ref):
    step = PAIR * TILE
    count = q_ref.shape[0]
    pairs = count // step
    out_ref[step : count - step, :] = done_ref[step : count - step, :]
    first = jnp.concatenate([low_ref[...], kv_ref[: 2 * step, :]], axis=0)
    last = jnp.concatenate([kv_ref[count - 2 * step :, :], high_ref[...]], axis=0)
    for pair, window in ((0, first), (pairs - 1, last)):
        rows = slice(pair * step, (pair + 1) * step)
        out_ref[rows, :] = attend(
            steps_ref, pair, q_ref[rows, :], window[:, :COLS], window[:, COLS:]
        )


def attend_back(steps_ref, pair, queries, grads, keys, values):
    queries, grads = by_head(queries), by_head(grads)
    raised, share = raised_scores(queries, keys, usable_keys(steps_ref, pair))
    probs = raised * share
    grad_probs = lax.dot_general(grads, values, OVER_COLUMNS, preferred_element_type=F32)
    row_delta = jnp.sum(probs * grad_probs, axis=-1, keepdims=True)
    grad_scores = (probs * (grad_probs - row_delta)).astype(BF16)
    key_grad = lax.dot_general(grad_scores, queries, OVER_ROWS, preferred_element_type=F32)
    value_grad = lax.dot_general(probs.astype(BF16), grads, OVER_ROWS, preferred_element_type=F32)
    return key_grad, value_grad


def edge_back_kernel(
    steps_ref, q_ref, kv_ref, low_ref, high_ref, g_ref, part_ref, *rims
):
    outer = []
    step = PAIR * TILE
    count = q_ref.shape[0]
    first = jnp.concatenate([low_ref[...], kv_ref[: 2 * step, :]], axis=0)
    last = jnp.concatenate([kv_ref[count - 2 * step :, :], high_ref[...]], axis=0)
    pairs = count // step
    for edge, pair, window in ((0, 0, first), (1, pairs - 1, last)):
        rows = slice(pair * step, (pair + 1) * step)
        grads = attend_back(
            steps_ref, pair, q_ref[rows, :], g_ref[rows, :], window[:, :COLS], window[:, COLS:]
        )
        rim = slice(0, RIM) if edge == 0 else slice(WINDOW - RIM, WINDOW)
        own = slice(RIM, WINDOW) if edge == 0 else slice(0, WINDOW - RIM)
        for at, grad in enumerate(grads):
            columns = slice(at * COLS, (at + 1) * COLS)
            part_ref[edge, :, columns] = grad[own]
        outer.append(jnp.concatenate([grad[rim].astype(BF16) for grad in grads], axis=1))
    put_rims(rims, *outer)


def interior_back_kernel(steps_ref, q_ref, kv_ref, g_ref, part_ref, out_ref):
    step = PAIR * TILE
    count = q_ref.shape[0]
    pairs = count // step
    reach = 2 * step
    out_ref[:reach, :] = part_ref[0]
    out_ref[reach : count - reach, :] = jnp.zeros((count - 2 * reach, 2 * COLS), F32)
    out_ref[count - reach :, :] = part_ref[1]
    for pair in range(1, pairs - 1):
        window = slice((pair - 1) * step, (pair + 2) * step)
        rows = slice(pair * step, (pair + 1) * step)
        key_grad, value_grad = attend_back(
            steps_ref,
            pair,
            q_ref[rows, :],
            g_ref[rows, :],
            kv_ref[window, :COLS],
            kv_ref[window, COLS:],
        )
        out_ref[window, :COLS] += key_grad
        out_ref[window, COLS:] += value_grad


def slope(spread):
    return spread * lax.rsqrt(spread * spread + SOFT_WIDTH)


def mix_kernel(att_ref, factor_ref, truth_any, w_any, *refs):
    sources, refs = refs[:-8], refs[-8:]
    pred_ref, grad_ref, a, truth_ref, truth, source, w, sems = refs
    members_num, part, _ = source.shape
    halves = w.shape[0]
    ens = lax.axis_index("ens")
    copies = fetch([(w_any.at[half], w.at[half]) for half in range(halves)], sems)
    pairs = [(truth_any, truth_ref)]
    if len(sources) == 1:
        pairs.append((sources[0], source))
    else:
        pairs += [(rows.at[0], source.at[ens ^ step]) for step, rows in enumerate(sources)]
    others = fetch(pairs, sems, halves)
    for g in range(GROUP):
        for m in range(members_num):
            a[m * part : (m + 1) * part, g * COLS : (g + 1) * COLS] = att_ref[g * members_num + m]
    wait(others)
    lane_part = lax.broadcasted_iota(jnp.int32, (1, a.shape[0]), 1) // part
    own_truth, own_factor = truth_ref[...], factor_ref[...]
    for turn in range(1, members_num):
        at = lane_part - turn
        here = jnp.where(at < 0, at + members_num, at) == ens
        own_truth = jnp.where(here, pltpu.roll(truth_ref[...], turn * part, 1), own_truth)
        own_factor = jnp.where(here, pltpu.roll(factor_ref[...], turn * part, 1), own_factor)
    truth[...] = jnp.zeros_like(truth)
    truth[:FIELD_NUM, :] = own_truth
    hidden = source[...].reshape(a.shape).astype(F32)
    count = LATENT_DIM // halves
    for half in range(halves):
        copies[half].wait()
        mix = w[half].reshape(count, LATENT_DIM + FIELD_PAD)[:, :LATENT_DIM]
        hidden += jnp.dot(
            a[:, half * count : (half + 1) * count], mix, preferred_element_type=F32
        )
    both = w[...].reshape(LATENT_DIM, LATENT_DIM + FIELD_PAD)
    mix, readout = both[:, :LATENT_DIM], both[:, LATENT_DIM:]
    inverse = lax.rsqrt(jnp.mean(hidden * hidden, axis=-1, keepdims=True) + NORM_EPS)
    decoded = (hidden * inverse).astype(BF16)
    prediction = lax.dot_general(
        readout, decoded, (((0,), (1,)), ((), ())), preferred_element_type=F32
    )
    pred_ref[...] = prediction[:FIELD_NUM]
    spread = jnp.zeros_like(prediction)
    for other in range(1, members_num):
        spread = spread + slope(prediction - pltpu.roll(prediction, other * part, 1))
    derivative = own_factor / FIELD_NUM * (
        slope(prediction - truth[...]) - spread / (members_num - 1)
    )
    grad_decoded = lax.dot_general(
        derivative.astype(BF16), readout, (((0,), (1,)), ((), ())), preferred_element_type=F32
    )
    grad_hidden = inverse * grad_decoded - hidden * inverse**3 * jnp.mean(
        grad_decoded * hidden, axis=-1, keepdims=True
    )
    grads = lax.dot_general(
        grad_hidden.astype(BF16), mix, OVER_COLUMNS, preferred_element_type=F32
    ).astype(BF16)
    for g in range(GROUP):
        for m in range(members_num):
            grad_ref[g * members_num + m] = grads[
                m * part : (m + 1) * part, g * COLS : (g + 1) * COLS
            ]


def product_kernel(normed_ref, from_low_ref, from_high_ref, grads_ref, out_ref):
    count = normed_ref.shape[0]
    half, last = lax.axis_index("half"), lax.axis_size("half") - 1
    from_low = jnp.where(half > 0, from_low_ref[...].astype(F32), 0.0)
    from_high = jnp.where(half < last, from_high_ref[...].astype(F32), 0.0)
    grads = grads_ref[...]
    grads = jnp.concatenate(
        [
            grads[:RIM] + from_low,
            grads[RIM : count - RIM],
            grads[count - RIM :] + from_high,
        ],
        axis=0,
    )
    high = grads.astype(BF16)
    low = (grads - high.astype(F32)).astype(BF16)
    both = lax.dot_general(
        normed_ref[...], jnp.concatenate([high, low], axis=1), OVER_ROWS, preferred_element_type=F32
    )
    out_ref[...] = (both[:, : 2 * COLS] + both[:, 2 * COLS :]).astype(BF16)


def gather_kernel(parts_ref, out_ref):
    halves, _, members_num = parts_ref.shape[:3]
    for g in range(GROUP):
        total = None
        for half in range(halves):
            for m in range(members_num):
                part = parts_ref[half, g, m].astype(F32)
                total = part if total is None else total + part
        out_ref[:, g * COLS : (g + 1) * COLS] = total[:, :COLS]
        out_ref[:, LATENT_DIM + g * COLS : LATENT_DIM + (g + 1) * COLS] = total[:, COLS:]


def exchange(chunks, axes):
    return lax.all_to_all(chunks, axes, 0, 0)


def swap(value, axis, step):
    return lax.ppermute(value, axis, [(i, i ^ step) for i in range(lax.axis_size(axis))])


def in_order(mine, axis, at):
    if lax.axis_size(axis) != 2:
        return lax.all_gather(mine, axis, axis=at)
    other = swap(mine, axis, 1)
    first = lax.axis_index(axis) == 0
    return jnp.stack([jnp.where(first, mine, other), jnp.where(first, other, mine)], axis=at)


def body(members, w_attn, w_mix, readout_matrix, observed_truth, cell_surface_factor, neighbours):
    halves, members_num = lax.axis_size("half"), lax.axis_size("ens")
    nodes = ("half", "quad", "core")
    everyone = nodes + ("ens",)
    shard = w_attn.shape[0]
    node_rows = members.shape[1]
    rows = GROUP * node_rows
    part = node_rows // members_num
    up = [(i, i + 1) for i in range(halves - 1)]
    down = [(target, source) for source, target in up]
    ens = lax.axis_index("ens")
    width = LATENT_DIM + FIELD_PAD
    paired = members_num == 2
    copies = 1 if paired else members_num
    source_parts = 2 if paired else 1

    columns, packed = call(
        weights_kernel,
        "prepare_weights",
        [((halves, GROUP, copies, shard, 3 * COLS), BF16), ((shard, width), BF16)],
        "hhh",
        [
            pltpu.VMEM(w_attn.shape, BF16),
            pltpu.VMEM((GROUP, shard, 3 * COLS), BF16),
            pltpu.VMEM(readout_matrix.shape, BF16),
            pltpu.VMEM((shard, width), BF16),
            pltpu.SemaphoreType.DMA((4 + halves * copies,)),
        ],
        moved=2**20,
        results="hh",
    )(w_attn, w_mix, readout_matrix)
    normed, *sources = call(
        norm_kernel,
        "norm",
        [((node_rows + NOTE_ROWS, LATENT_DIM), BF16)]
        + [((1 if paired else members_num, part, LATENT_DIM), BF16)] * source_parts,
        "hh",
        [
            pltpu.SMEM(neighbours.shape, jnp.int32),
            pltpu.VMEM((node_rows, LATENT_DIM), BF16),
            pltpu.VMEM((node_rows + NOTE_ROWS, LATENT_DIM), BF16),
            pltpu.SemaphoreType.DMA((3 + max(2, members_num),)),
        ],
        flops=2**20,
        moved=2**20,
        results="h" + "h" * source_parts,
    )(neighbours, members.reshape(node_rows, LATENT_DIM))

    square = paired and halves == 2
    if square:
        both = [(at, at ^ 3) for at in range(4)]
        spread = [swap(packed, "half", 1), swap(packed, "ens", 1)]
        spread = [packed] + spread + [lax.ppermute(packed, ("half", "ens"), both)]
        spread[1], normed = lax.optimization_barrier((spread[1], normed))
    else:
        packed, normed = lax.optimization_barrier((in_order(packed, "half", 0), normed))
    near = [normed, swap(normed, "quad", 1), None, swap(normed, "quad", 3)]
    if paired:
        columns = exchange(columns.reshape(-1, shard, 3 * COLS), nodes)
        columns, late = lax.optimization_barrier((columns, normed))
        columns = [columns, swap(columns, "ens", 1)]
    else:
        columns = [exchange(columns.reshape(-1, shard, 3 * COLS), everyone)]
        columns = [columns[0].reshape(LATENT_DIM, 3 * COLS)]
        late = normed
    near[2] = swap(late, "quad", 2)
    far = [swap(piece, "core", 1) for piece in near]
    normed, steps = call(
        collect_kernel,
        "collect",
        [((rows, LATENT_DIM), BF16), ((GROUP, NOTE_ROWS, 128), F32)],
        "a" * (2 * QUAD),
        [pltpu.VMEM((GROUP, NOTE_ROWS, 128), BF16), pltpu.SemaphoreType.DMA((2 * GROUP,))],
        results="hv",
    )(*near, *far)

    if square:
        packed = jnp.stack(spread)
    else:
        packed = in_order(packed, "ens", 1).reshape(halves, members_num * shard, width)

    rim = ((RIM, 2 * COLS), BF16)
    rims = [rim] if halves == 2 else [rim, rim]
    w_shape = (GROUP * halves, 2, shard, 3 * COLS) if paired else (LATENT_DIM, 3 * COLS)
    weights, *inner = call(
        rims_kernel,
        "project_rims",
        [(w_shape, BF16)] + rims,
        "h" + "a" * len(columns),
        [pltpu.VMEM((len(rims), RIM, LATENT_DIM), BF16), pltpu.SemaphoreType.DMA((4,))],
        flops=RIM * LATENT_DIM * 4 * COLS,
        moved=2**20,
    )(normed, *columns)
    def across(inner):
        if halves == 2:
            got = swap(inner[0], "half", 1)
            return got, got
        return lax.ppermute(inner[1], "half", up), lax.ppermute(inner[0], "half", down)

    weights, sources[-1], packed = lax.optimization_barrier((weights, sources[-1], packed))
    sources = [sources[0], swap(sources[1], "ens", 1)] if paired else [exchange(sources[0], "ens")]
    low, high = across(inner)
    pieces = [packed] + [swap(packed, "quad", step) for step in range(1, QUAD)]
    queries, own = call(
        project_kernel,
        "project",
        [((rows, COLS), BF16), ((rows, 2 * COLS), BF16)],
        "hv",
        [pltpu.VMEM((rows, LATENT_DIM), BF16), pltpu.SemaphoreType.DMA((CHUNKS,))],
        flops=rows * LATENT_DIM * 6 * COLS,
        moved=4 * 2**20,
    )(normed, weights)

    (outcome,) = call(
        interior_kernel,
        "attention_interior",
        [((rows, COLS), BF16)],
        "vvv",
        flops=rows * COLS * 2048,
        moved=2**21,
        exps=rows * 512,
    )(steps, queries, own)
    (outcome,) = call(
        edge_kernel,
        "attention_edges",
        [((rows, COLS), BF16)],
        "vvvvvv",
        flops=rows * COLS * 512,
        moved=2**20,
        exps=rows * 128,
    )(steps, queries, own, low, high, outcome)
    *pieces, own = lax.optimization_barrier((*pieces, own))
    pieces = pieces + [swap(piece, "core", 1) for piece in pieces]
    attended = exchange(outcome.reshape(GROUP * members_num, part, COLS), ("quad", "core", "ens"))
    block = (halves, QUAD, CORES) + ((2, shard) if square else (1, members_num * shard)) + (width,)
    (weights,) = call(
        assemble_kernel,
        "assemble",
        [(block, BF16)],
        "a" * len(pieces),
        [pltpu.SemaphoreType.DMA((4 * GROUP,))],
        moved=4 * 2**20,
        results="h",
    )(*pieces)

    prediction, grads = call(
        mix_kernel,
        "mix_loss_backward",
        [((FIELD_NUM, node_rows), F32), ((GROUP * members_num, part, COLS), BF16)],
        "vvhh" + "a" * len(sources),
        [
            pltpu.VMEM((node_rows, LATENT_DIM), BF16),
            pltpu.VMEM(observed_truth.shape, F32),
            pltpu.VMEM((FIELD_PAD, node_rows), F32),
            pltpu.VMEM((members_num, part, LATENT_DIM), BF16),
            pltpu.VMEM(block, BF16),
            pltpu.SemaphoreType.DMA((halves + 1 + len(sources),)),
        ],
        flops=node_rows * LATENT_DIM * 4 * width,
        moved=2**22,
        room=14,
    )(attended, cell_surface_factor[None], observed_truth, weights, *sources)
    grads = exchange(grads, ("quad", "core", "ens")).reshape(rows, COLS)

    edges, *inner = call(
        edge_back_kernel,
        "attention_edges_back",
        [((2, WINDOW - RIM, 2 * COLS), F32)] + rims,
        "vvvvvv",
        flops=rows * COLS * 1280,
        moved=2**20,
        exps=rows * 128,
    )(steps, queries, own, low, high, grads)
    from_low, from_high = across(inner)
    (kv_grads,) = call(
        interior_back_kernel,
        "attention_interior_back",
        [((rows, 2 * COLS), F32)],
        "vvvvv",
        flops=rows * COLS * 4096,
        moved=2**22,
        exps=rows * 512,
        room=10,
    )(steps, queries, own, grads, edges)
    (term,) = call(
        product_kernel,
        "product",
        [((LATENT_DIM, 2 * COLS), BF16)],
        "vvvv",
        flops=rows * LATENT_DIM * 8 * COLS,
        moved=2**22,
        room=16,
    )(normed, from_low, from_high, kv_grads)
    term, prediction = lax.optimization_barrier((term, prediction))
    term = exchange(term.reshape(-1, shard, 2 * COLS), everyone)
    (grad_kv,) = call(
        gather_kernel, "gather_sums", [((shard, 2 * LATENT_DIM), F32)], "v", flops=2**17, moved=2**20
    )(term.reshape(halves, GROUP, members_num, shard, 2 * COLS))

    if members_num == 2:
        got = jnp.roll(swap(prediction, "ens", 1), part, axis=1)
        lane = lax.broadcasted_iota(jnp.int32, prediction.shape, 1)
        prediction = jnp.where(lane // part == ens, prediction, got)
    else:
        prediction = prediction.reshape(FIELD_NUM, members_num, part).transpose(1, 0, 2)
        prediction = exchange(prediction, "ens").transpose(1, 0, 2)
    return (prediction.reshape(1, FIELD_NUM, node_rows), grad_kv)


def solution(mesh):
    space, ens = mesh.shape["space"], mesh.shape["ens"]
    split = Mesh(
        mesh.devices.reshape(space // GROUP, QUAD, CORES, ens), ("half", "quad", "core", "ens")
    )
    nodes = ("half", "quad", "core")
    shards = nodes + ("ens",)
    in_specs = (
        P("ens", nodes, None),
        P(shards, None),
        P(shards, None),
        P(shards, None),
        P(None, nodes),
        P(nodes),
        P(nodes, None),
    )
    out_specs = (P("ens", None, nodes), P(shards, None))
    return jax.shard_map(body, mesh=split, in_specs=in_specs, out_specs=out_specs, check_vma=False)
```

```python
import functools

import jax
import jax.numpy as jnp
from jax import lax
from jax.experimental import pallas as pl
from jax.experimental.pallas import tpu as pltpu
from jax.sharding import Mesh
from jax.sharding import PartitionSpec as P

LATENT_DIM = 1024
HEADS = 16
HEAD = 64
FIELD_NUM = 100
TILE = 64
RADIUS = 2
K_NB = 4
QUAD = 4
CORES = 2
GROUP = QUAD * CORES
COLS = LATENT_DIM // GROUP
RIM = RADIUS * TILE
FIELD_PAD = 128
PAIR = 2
WINDOW = (PAIR + 2 * RADIUS) * TILE
NOWHERE = 100
NOTE_ROWS = 16
CHUNKS = 4

NORM_EPS = 1e-06
SOFT_WIDTH = 0.0625
MASKED = -1e30

F32 = jnp.float32
BF16 = jnp.bfloat16

VMEM = pl.BlockSpec(memory_space=pltpu.VMEM)
SMEM = pl.BlockSpec(memory_space=pltpu.SMEM)
HBM = pl.BlockSpec(memory_space=pltpu.HBM)
ANYWHERE = pl.BlockSpec(memory_space=pl.ANY)
OVER_ROWS = (((0,), (0,)), ((), ()))
OVER_COLUMNS = (((1,), (1,)), ((), ()))


def call(kernel, name, outs, ins, scratch=(), flops=0, moved=0, exps=0, room=8, results=None):
    results = results or "v" * len(outs)
    spaces = {"s": SMEM, "v": VMEM, "h": HBM, "a": ANYWHERE}
    made = pl.pallas_call(
        kernel,
        out_shape=[
            pltpu.HBM(shape, kind) if space == "h" else jax.ShapeDtypeStruct(shape, kind)
            for (shape, kind), space in zip(outs, results)
        ],
        in_specs=[spaces[space] for space in ins],
        out_specs=[spaces[space] for space in results],
        scratch_shapes=list(scratch),
        compiler_params=pltpu.CompilerParams(vmem_limit_bytes=room * 2**20),
        cost_estimate=pl.CostEstimate(flops=flops, bytes_accessed=moved, transcendentals=exps),
        name=name,
    )

    def run(*args):
        return made(
            *[
                pltpu.with_memory_space_constraint(arg, pltpu.HBM) if space == "h" else arg
                for arg, space in zip(args, ins)
            ]
        )

    return run


def fetch(pairs, sems, first=0):
    copies = [
        pltpu.make_async_copy(source, target, sems.at[first + at])
        for at, (source, target) in enumerate(pairs)
    ]
    for copy in copies:
        copy.start()
    return copies


def wait(copies):
    for copy in copies:
        copy.wait()


def weights_kernel(w_any, mix_any, readout_any, columns_any, packed_any, *refs):
    w, columns, readout, packed, sems = refs
    copies = fetch(
        [(w_any, w), (readout_any, readout), (mix_any, packed.at[:, :LATENT_DIM])], sems
    )
    copies[0].wait()
    for g in range(GROUP):
        for part in range(3):
            at = (part * GROUP + g) * COLS
            columns[g, :, part * COLS : (part + 1) * COLS] = w[:, at : at + COLS]
    halves, _, members_num = columns_any.shape[:3]
    out = fetch(
        [
            (columns, columns_any.at[half, :, m])
            for half in range(halves)
            for m in range(members_num)
        ],
        sems,
        3,
    )
    wait(copies[1:])
    packed[:, LATENT_DIM:] = jnp.zeros((packed.shape[0], FIELD_PAD), BF16)
    packed[:, LATENT_DIM : LATENT_DIM + FIELD_NUM] = readout[...]
    wait(out + fetch([(packed, packed_any)], sems, 3 + len(out)))


def norm_kernel(near_any, source_any, normed_any, *refs):
    parts, (near, source, normed, sems) = refs[:-4], refs[-4:]
    ens = lax.axis_index("ens")
    copies = fetch([(source_any, source), (near_any, near)], sems)
    rows = source.shape[0]
    copies[0].wait()
    moves = []
    for step, part_any in enumerate(parts):
        count, part, _ = part_any.shape
        for m in range(count):
            place = (ens ^ step) if len(parts) == 2 else m
            place = pl.multiple_of(place * part, part)
            moves.append((source.at[pl.ds(place, part)], part_any.at[m]))
    out = fetch(moves, sems, 2)
    states = source[...].astype(F32)
    inverse = lax.rsqrt(jnp.mean(states * states, axis=-1, keepdims=True) + NORM_EPS)
    normed[:rows, :] = (states * inverse).astype(BF16)
    copies[1].wait()
    row = lax.broadcasted_iota(jnp.int32, (NOTE_ROWS, 128), 0)
    lane = lax.broadcasted_iota(jnp.int32, (NOTE_ROWS, 128), 1)
    note = jnp.zeros((NOTE_ROWS, 128), F32)
    tiles = near.shape[0]
    first_tile = lax.axis_index(("half", "quad", "core")) * tiles
    for tile in range(tiles):
        for slot in range(K_NB):
            at = near[tile, slot]
            step = jnp.where(at >= 0, at - first_tile - tile, NOWHERE).astype(F32)
            note = jnp.where((row == tile) & (lane == slot), step, note)
    normed[rows:, :] = jnp.zeros((NOTE_ROWS, LATENT_DIM), BF16)
    normed[rows:, :128] = note.astype(BF16)
    wait(out + fetch([(normed, normed_any)], sems, 2 + len(out)))


def merge_halves_kernel(mine_ref, other_ref, sent_ref, out_ref):
    half = lax.axis_index("half")
    width = mine_ref.shape[1]
    out_ref[half, :, :width] = mine_ref[...]
    out_ref[half ^ 1, :, :width] = other_ref[...]
    out_ref[:, :, width:] = sent_ref[...].reshape(2, -1, LATENT_DIM)


def merge_members_kernel(mine_ref, other_ref, packed_ref, source_ref):
    ens = lax.axis_index("ens")
    width = packed_ref.shape[3]
    for half in range(2):
        packed_ref[half, ens] = mine_ref[half, :, :width]
        packed_ref[half, ens ^ 1] = other_ref[half, :, :width]
    source_ref[...] = other_ref[:, :, width:].reshape(source_ref.shape)


def owners():
    core, quad = lax.axis_index("core"), lax.axis_index("quad")
    return [(quad ^ step) * CORES + (core ^ flip) for flip in range(CORES) for step in range(QUAD)]


def collect_kernel(*refs):
    blocks, (normed_any, steps_ref, notes, sems) = refs[:GROUP], refs[GROUP:]
    block = blocks[0].shape[0] - NOTE_ROWS
    pairs = []
    for rows_ref, owner in zip(blocks, owners()):
        place = pl.ds(pl.multiple_of(owner * block, block), block)
        pairs.append((rows_ref.at[:block], normed_any.at[place]))
        pairs.append((rows_ref.at[block:, :128], notes.at[owner]))
    wait(fetch(pairs, sems))
    steps_ref[...] = notes[...].astype(F32)


def put_rims(rims, first, last):
    if len(rims) == 1:
        rims[0][...] = jnp.where(lax.axis_index("half") == 0, last, first)
    else:
        rims[0][...], rims[1][...] = first, last


def rims_kernel(normed_any, *refs):
    rows, sems = refs[-2:]
    if len(refs[0].shape) == 2:
        columns, w, rims = refs[:1], refs[1], refs[2:-2]
        pairs = [(columns[0], w)]
    else:
        columns, w, rims = refs[:2], refs[2], refs[3:-2]
        ens = lax.axis_index("ens")
        pairs = [(part, w.at[:, ens ^ step]) for step, part in enumerate(columns)]
    last = normed_any.shape[0] - RIM
    if len(rims) == 1:
        place = pl.multiple_of(jnp.where(lax.axis_index("half") == 0, last, 0), RIM)
        pairs.append((normed_any.at[pl.ds(place, RIM)], rows.at[0]))
    else:
        pairs += [(normed_any.at[:RIM], rows.at[0]), (normed_any.at[last:], rows.at[1])]
    wait(fetch(pairs, sems))
    weights = w[...].reshape(LATENT_DIM, 3 * COLS)[:, COLS:]
    for at, rim_ref in enumerate(rims):
        rim_ref[...] = jnp.dot(rows[at], weights, preferred_element_type=F32).astype(BF16)


def project_kernel(normed_any, w_ref, q_ref, kv_ref, normed, sems):
    chunk = normed.shape[0] // CHUNKS
    rows = [slice(at * chunk, (at + 1) * chunk) for at in range(CHUNKS)]
    copies = fetch([(normed_any.at[part], normed.at[part]) for part in rows], sems)
    weights = w_ref[...].reshape(LATENT_DIM, 3 * COLS)
    for part, copy in zip(rows, copies):
        copy.wait()
        projected = jnp.dot(normed[part, :], weights, preferred_element_type=F32).astype(BF16)
        q_ref[part, :] = projected[:, :COLS] * jnp.asarray(HEAD**-0.5, BF16)
        kv_ref[part, :] = projected[:, COLS:]


def assemble_kernel(*refs):
    pieces, (w_any, sems) = refs[:GROUP], refs[GROUP:]
    core, quad = lax.axis_index("core"), lax.axis_index("quad")
    pairs = [
        (piece, w_any.at[:, quad ^ (at % QUAD), core ^ (at // QUAD)])
        for at, piece in enumerate(pieces)
    ]
    wait(fetch(pairs, sems))


def by_head(rows):
    lane = lax.broadcasted_iota(jnp.int32, rows.shape, 1)
    zero = jnp.zeros_like(rows)
    return jnp.concatenate(
        [jnp.where(lane < HEAD, rows, zero), jnp.where(lane < HEAD, zero, rows)], axis=0
    )


def usable_keys(steps_ref, pair):
    lane = (lax.broadcasted_iota(jnp.int32, (1, WINDOW), 1) // TILE - RADIUS).astype(F32)
    masks = []
    for query_tile in range(PAIR):
        found = jnp.zeros((1, WINDOW), F32)
        for slot in range(K_NB):
            step = steps_ref[pair, query_tile : query_tile + 1, slot : slot + 1]
            found = jnp.where(lane - query_tile == step, 1.0, found)
        masks.append(found)
    row = lax.broadcasted_iota(jnp.int32, (2 * PAIR * TILE, 1), 0) // TILE % PAIR
    return jnp.where(row == 0, masks[0], masks[1]) > 0


def raised_scores(queries, keys, usable):
    scores = lax.dot_general(queries, keys, OVER_COLUMNS, preferred_element_type=F32)
    scores = jnp.where(usable, scores, MASKED)
    raised = jnp.exp(scores - jnp.max(scores, axis=-1, keepdims=True))
    return raised, 1.0 / jnp.sum(raised, axis=-1, keepdims=True)


def attend(steps_ref, pair, queries, keys, values):
    raised, share = raised_scores(by_head(queries), keys, usable_keys(steps_ref, pair))
    both = jnp.dot(raised.astype(BF16), values, preferred_element_type=F32) * share
    lane = lax.broadcasted_iota(jnp.int32, queries.shape, 1)
    half = PAIR * TILE
    return jnp.where(lane < HEAD, both[:half], both[half:]).astype(BF16)


def interior_kernel(steps_ref, q_ref, kv_ref, out_ref):
    step = PAIR * TILE
    pairs = q_ref.shape[0] // step
    for pair in range(1, pairs - 1):
        window = slice((pair - 1) * step, (pair + 2) * step)
        rows = slice(pair * step, (pair + 1) * step)
        out_ref[rows, :] = attend(
            steps_ref, pair, q_ref[rows, :], kv_ref[window, :COLS], kv_ref[window, COLS:]
        )


def edge_kernel(steps_ref, q_ref, kv_ref, low_ref, high_ref, done_ref, out_ref):
    step = PAIR * TILE
    count = q_ref.shape[0]
    pairs = count // step
    out_ref[step : count - step, :] = done_ref[step : count - step, :]
    first = jnp.concatenate([low_ref[...], kv_ref[: 2 * step, :]], axis=0)
    last = jnp.concatenate([kv_ref[count - 2 * step :, :], high_ref[...]], axis=0)
    for pair, window in ((0, first), (pairs - 1, last)):
        rows = slice(pair * step, (pair + 1) * step)
        out_ref[rows, :] = attend(
            steps_ref, pair, q_ref[rows, :], window[:, :COLS], window[:, COLS:]
        )


def attend_back(steps_ref, pair, queries, grads, keys, values):
    queries, grads = by_head(queries), by_head(grads)
    raised, share = raised_scores(queries, keys, usable_keys(steps_ref, pair))
    probs = raised * share
    grad_probs = lax.dot_general(grads, values, OVER_COLUMNS, preferred_element_type=F32)
    row_delta = jnp.sum(probs * grad_probs, axis=-1, keepdims=True)
    grad_scores = (probs * (grad_probs - row_delta)).astype(BF16)
    key_grad = lax.dot_general(grad_scores, queries, OVER_ROWS, preferred_element_type=F32)
    value_grad = lax.dot_general(probs.astype(BF16), grads, OVER_ROWS, preferred_element_type=F32)
    return key_grad, value_grad


def edge_back_kernel(
    steps_ref, q_ref, kv_ref, low_ref, high_ref, g_ref, part_ref, *rims
):
    outer = []
    step = PAIR * TILE
    count = q_ref.shape[0]
    first = jnp.concatenate([low_ref[...], kv_ref[: 2 * step, :]], axis=0)
    last = jnp.concatenate([kv_ref[count - 2 * step :, :], high_ref[...]], axis=0)
    pairs = count // step
    for edge, pair, window in ((0, 0, first), (1, pairs - 1, last)):
        rows = slice(pair * step, (pair + 1) * step)
        grads = attend_back(
            steps_ref, pair, q_ref[rows, :], g_ref[rows, :], window[:, :COLS], window[:, COLS:]
        )
        rim = slice(0, RIM) if edge == 0 else slice(WINDOW - RIM, WINDOW)
        own = slice(RIM, WINDOW) if edge == 0 else slice(0, WINDOW - RIM)
        for at, grad in enumerate(grads):
            columns = slice(at * COLS, (at + 1) * COLS)
            part_ref[edge, :, columns] = grad[own]
        outer.append(jnp.concatenate([grad[rim].astype(BF16) for grad in grads], axis=1))
    put_rims(rims, *outer)


def interior_back_kernel(steps_ref, q_ref, kv_ref, g_ref, part_ref, out_ref):
    step = PAIR * TILE
    count = q_ref.shape[0]
    pairs = count // step
    reach = 2 * step
    out_ref[:reach, :] = part_ref[0]
    out_ref[reach : count - reach, :] = jnp.zeros((count - 2 * reach, 2 * COLS), F32)
    out_ref[count - reach :, :] = part_ref[1]
    for pair in range(1, pairs - 1):
        window = slice((pair - 1) * step, (pair + 2) * step)
        rows = slice(pair * step, (pair + 1) * step)
        key_grad, value_grad = attend_back(
            steps_ref,
            pair,
            q_ref[rows, :],
            g_ref[rows, :],
            kv_ref[window, :COLS],
            kv_ref[window, COLS:],
        )
        out_ref[window, :COLS] += key_grad
        out_ref[window, COLS:] += value_grad


def slope(spread):
    return spread * lax.rsqrt(spread * spread + SOFT_WIDTH)


def mix_kernel(att_ref, factor_ref, truth_any, w_any, *refs):
    sources, refs = refs[:-8], refs[-8:]
    pred_ref, grad_ref, a, truth_ref, truth, source, w, sems = refs
    members_num, part, _ = source.shape
    halves = w.shape[0]
    ens = lax.axis_index("ens")
    copies = fetch([(w_any.at[half], w.at[half]) for half in range(halves)], sems)
    pairs = [(truth_any, truth_ref)]
    if len(sources) == 1:
        pairs.append((sources[0], source))
    else:
        pairs += [(rows.at[0], source.at[ens ^ step]) for step, rows in enumerate(sources)]
    others = fetch(pairs, sems, halves)
    for g in range(GROUP):
        for m in range(members_num):
            a[m * part : (m + 1) * part, g * COLS : (g + 1) * COLS] = att_ref[g * members_num + m]
    wait(others)
    lane_part = lax.broadcasted_iota(jnp.int32, (1, a.shape[0]), 1) // part
    own_truth, own_factor = truth_ref[...], factor_ref[...]
    for turn in range(1, members_num):
        at = lane_part - turn
        here = jnp.where(at < 0, at + members_num, at) == ens
        own_truth = jnp.where(here, pltpu.roll(truth_ref[...], turn * part, 1), own_truth)
        own_factor = jnp.where(here, pltpu.roll(factor_ref[...], turn * part, 1), own_factor)
    truth[...] = jnp.zeros_like(truth)
    truth[:FIELD_NUM, :] = own_truth
    hidden = source[...].reshape(a.shape).astype(F32)
    count = LATENT_DIM // halves
    for half in range(halves):
        copies[half].wait()
        mix = w[half].reshape(count, LATENT_DIM + FIELD_PAD)[:, :LATENT_DIM]
        hidden += jnp.dot(
            a[:, half * count : (half + 1) * count], mix, preferred_element_type=F32
        )
    both = w[...].reshape(LATENT_DIM, LATENT_DIM + FIELD_PAD)
    mix, readout = both[:, :LATENT_DIM], both[:, LATENT_DIM:]
    inverse = lax.rsqrt(jnp.mean(hidden * hidden, axis=-1, keepdims=True) + NORM_EPS)
    decoded = (hidden * inverse).astype(BF16)
    prediction = lax.dot_general(
        readout, decoded, (((0,), (1,)), ((), ())), preferred_element_type=F32
    )
    pred_ref[...] = prediction[:FIELD_NUM]
    spread = jnp.zeros_like(prediction)
    for other in range(1, members_num):
        spread = spread + slope(prediction - pltpu.roll(prediction, other * part, 1))
    derivative = own_factor / FIELD_NUM * (
        slope(prediction - truth[...]) - spread / (members_num - 1)
    )
    grad_decoded = lax.dot_general(
        derivative.astype(BF16), readout, (((0,), (1,)), ((), ())), preferred_element_type=F32
    )
    grad_hidden = inverse * grad_decoded - hidden * inverse**3 * jnp.mean(
        grad_decoded * hidden, axis=-1, keepdims=True
    )
    grads = lax.dot_general(
        grad_hidden.astype(BF16), mix, OVER_COLUMNS, preferred_element_type=F32
    ).astype(BF16)
    for g in range(GROUP):
        for m in range(members_num):
            grad_ref[g * members_num + m] = grads[
                m * part : (m + 1) * part, g * COLS : (g + 1) * COLS
            ]


def product_kernel(normed_ref, from_low_ref, from_high_ref, grads_ref, out_ref):
    count = normed_ref.shape[0]
    half, last = lax.axis_index("half"), lax.axis_size("half") - 1
    from_low = jnp.where(half > 0, from_low_ref[...].astype(F32), 0.0)
    from_high = jnp.where(half < last, from_high_ref[...].astype(F32), 0.0)
    grads = grads_ref[...]
    grads = jnp.concatenate(
        [
            grads[:RIM] + from_low,
            grads[RIM : count - RIM],
            grads[count - RIM :] + from_high,
        ],
        axis=0,
    )
    high = grads.astype(BF16)
    low = (grads - high.astype(F32)).astype(BF16)
    both = lax.dot_general(
        normed_ref[...], jnp.concatenate([high, low], axis=1), OVER_ROWS, preferred_element_type=F32
    )
    out_ref[...] = (both[:, : 2 * COLS] + both[:, 2 * COLS :]).astype(BF16)


def gather_kernel(parts_ref, out_ref):
    halves, _, members_num = parts_ref.shape[:3]
    for g in range(GROUP):
        total = None
        for half in range(halves):
            for m in range(members_num):
                part = parts_ref[half, g, m].astype(F32)
                total = part if total is None else total + part
        out_ref[:, g * COLS : (g + 1) * COLS] = total[:, :COLS]
        out_ref[:, LATENT_DIM + g * COLS : LATENT_DIM + (g + 1) * COLS] = total[:, COLS:]


def exchange(chunks, axes):
    return lax.all_to_all(chunks, axes, 0, 0)


def swap(value, axis, step):
    return lax.ppermute(value, axis, [(i, i ^ step) for i in range(lax.axis_size(axis))])


def in_order(mine, axis, at):
    if lax.axis_size(axis) != 2:
        return lax.all_gather(mine, axis, axis=at)
    other = swap(mine, axis, 1)
    first = lax.axis_index(axis) == 0
    return jnp.stack([jnp.where(first, mine, other), jnp.where(first, other, mine)], axis=at)


def body(members, w_attn, w_mix, readout_matrix, observed_truth, cell_surface_factor, neighbours):
    halves, members_num = lax.axis_size("half"), lax.axis_size("ens")
    nodes = ("half", "quad", "core")
    everyone = nodes + ("ens",)
    shard = w_attn.shape[0]
    node_rows = members.shape[1]
    rows = GROUP * node_rows
    part = node_rows // members_num
    up = [(i, i + 1) for i in range(halves - 1)]
    down = [(target, source) for source, target in up]
    ens = lax.axis_index("ens")
    width = LATENT_DIM + FIELD_PAD
    paired = members_num == 2
    copies = 1 if paired else members_num
    source_parts = 2 if paired else 1

    columns, packed = call(
        weights_kernel,
        "prepare_weights",
        [((halves, GROUP, copies, shard, 3 * COLS), BF16), ((shard, width), BF16)],
        "hhh",
        [
            pltpu.VMEM(w_attn.shape, BF16),
            pltpu.VMEM((GROUP, shard, 3 * COLS), BF16),
            pltpu.VMEM(readout_matrix.shape, BF16),
            pltpu.VMEM((shard, width), BF16),
            pltpu.SemaphoreType.DMA((4 + halves * copies,)),
        ],
        moved=2**20,
        results="hh",
    )(w_attn, w_mix, readout_matrix)
    normed, *sources = call(
        norm_kernel,
        "norm",
        [((node_rows + NOTE_ROWS, LATENT_DIM), BF16)]
        + [((1 if paired else members_num, part, LATENT_DIM), BF16)] * source_parts,
        "hh",
        [
            pltpu.SMEM(neighbours.shape, jnp.int32),
            pltpu.VMEM((node_rows, LATENT_DIM), BF16),
            pltpu.VMEM((node_rows + NOTE_ROWS, LATENT_DIM), BF16),
            pltpu.SemaphoreType.DMA((3 + max(2, members_num),)),
        ],
        flops=2**20,
        moved=2**20,
        results="h" + "h" * source_parts,
    )(neighbours, members.reshape(node_rows, LATENT_DIM))

    square = paired and halves == 2 and shard % 16 == 0
    if square:
        (packed,) = call(
            merge_halves_kernel,
            "merge_halves",
            [((2, shard, width + LATENT_DIM), BF16)],
            "vvv",
            moved=2**18,
        )(packed, swap(packed, "half", 1), sources[1])
    else:
        packed = in_order(packed, "half", 0)
    packed, normed = lax.optimization_barrier((packed, normed))
    near = [normed, swap(normed, "quad", 1), None, swap(normed, "quad", 3)]
    if paired:
        columns = exchange(columns.reshape(-1, shard, 3 * COLS), nodes)
        columns, late = lax.optimization_barrier((columns, normed))
        columns = [columns, swap(columns, "ens", 1)]
    else:
        columns = [exchange(columns.reshape(-1, shard, 3 * COLS), everyone)]
        columns = [columns[0].reshape(LATENT_DIM, 3 * COLS)]
        late = normed
    near[2] = swap(late, "quad", 2)
    far = [swap(piece, "core", 1) for piece in near]
    normed, steps = call(
        collect_kernel,
        "collect",
        [((rows, LATENT_DIM), BF16), ((GROUP, NOTE_ROWS, 128), F32)],
        "a" * (2 * QUAD),
        [pltpu.VMEM((GROUP, NOTE_ROWS, 128), BF16), pltpu.SemaphoreType.DMA((2 * GROUP,))],
        moved=4 * 2**20,
        results="hv",
    )(*near, *far)

    if square:
        packed, arrived = call(
            merge_members_kernel,
            "merge_members",
            [((2, 2, shard, width), BF16), ((1, part, LATENT_DIM), BF16)],
            "vv",
            moved=2**19,
        )(packed, swap(packed, "ens", 1))
        packed = packed.reshape(2, 2 * shard, width)
        sources = [sources[0], arrived]
    else:
        packed = in_order(packed, "ens", 1).reshape(halves, members_num * shard, width)
    packed, near[2] = lax.optimization_barrier((packed, near[2]))
    pieces = [packed] + [swap(packed, "quad", step) for step in range(1, QUAD)]

    rim = ((RIM, 2 * COLS), BF16)
    rims = [rim] if halves == 2 else [rim, rim]
    w_shape = (GROUP * halves, 2, shard, 3 * COLS) if paired else (LATENT_DIM, 3 * COLS)
    weights, *inner = call(
        rims_kernel,
        "project_rims",
        [(w_shape, BF16)] + rims,
        "h" + "a" * len(columns),
        [pltpu.VMEM((len(rims), RIM, LATENT_DIM), BF16), pltpu.SemaphoreType.DMA((4,))],
        flops=RIM * LATENT_DIM * 4 * COLS,
        moved=2**20,
    )(normed, *columns)
    def across(inner):
        if halves == 2:
            got = swap(inner[0], "half", 1)
            return got, got
        return lax.ppermute(inner[1], "half", up), lax.ppermute(inner[0], "half", down)

    if not paired:
        sources = [exchange(sources[0], "ens")]
    elif not square:
        sources = [sources[0], swap(sources[1], "ens", 1)]
    low, high = across(inner)
    queries, own = call(
        project_kernel,
        "project",
        [((rows, COLS), BF16), ((rows, 2 * COLS), BF16)],
        "hv",
        [pltpu.VMEM((rows, LATENT_DIM), BF16), pltpu.SemaphoreType.DMA((CHUNKS,))],
        flops=rows * LATENT_DIM * 6 * COLS,
        moved=4 * 2**20,
    )(normed, weights)

    (outcome,) = call(
        interior_kernel,
        "attention_interior",
        [((rows, COLS), BF16)],
        "vvv",
        flops=rows * COLS * 2048,
        moved=2**21,
        exps=rows * 512,
    )(steps, queries, own)
    (outcome,) = call(
        edge_kernel,
        "attention_edges",
        [((rows, COLS), BF16)],
        "vvvvvv",
        flops=rows * COLS * 512,
        moved=2**20,
        exps=rows * 128,
    )(steps, queries, own, low, high, outcome)
    *pieces, own = lax.optimization_barrier((*pieces, own))
    pieces = pieces + [swap(piece, "core", 1) for piece in pieces]
    attended = exchange(outcome.reshape(GROUP * members_num, part, COLS), ("quad", "core", "ens"))
    block = (halves, QUAD, CORES, members_num * shard, width)
    (weights,) = call(
        assemble_kernel,
        "assemble",
        [(block, BF16)],
        "a" * len(pieces),
        [pltpu.SemaphoreType.DMA((GROUP,))],
        moved=4 * 2**20,
        results="h",
    )(*pieces)

    prediction, grads = call(
        mix_kernel,
        "mix_loss_backward",
        [((FIELD_NUM, node_rows), F32), ((GROUP * members_num, part, COLS), BF16)],
        "vvhh" + "a" * len(sources),
        [
            pltpu.VMEM((node_rows, LATENT_DIM), BF16),
            pltpu.VMEM(observed_truth.shape, F32),
            pltpu.VMEM((FIELD_PAD, node_rows), F32),
            pltpu.VMEM((members_num, part, LATENT_DIM), BF16),
            pltpu.VMEM(block, BF16),
            pltpu.SemaphoreType.DMA((halves + 1 + len(sources),)),
        ],
        flops=node_rows * LATENT_DIM * 4 * width,
        moved=2**22,
        room=14,
    )(attended, cell_surface_factor[None], observed_truth, weights, *sources)
    grads = exchange(grads, ("quad", "core", "ens")).reshape(rows, COLS)

    edges, *inner = call(
        edge_back_kernel,
        "attention_edges_back",
        [((2, WINDOW - RIM, 2 * COLS), F32)] + rims,
        "vvvvvv",
        flops=rows * COLS * 1280,
        moved=2**20,
        exps=rows * 128,
    )(steps, queries, own, low, high, grads)
    from_low, from_high = across(inner)
    (kv_grads,) = call(
        interior_back_kernel,
        "attention_interior_back",
        [((rows, 2 * COLS), F32)],
        "vvvvv",
        flops=rows * COLS * 4096,
        moved=2**22,
        exps=rows * 512,
        room=10,
    )(steps, queries, own, grads, edges)
    (term,) = call(
        product_kernel,
        "product",
        [((LATENT_DIM, 2 * COLS), BF16)],
        "vvvv",
        flops=rows * LATENT_DIM * 8 * COLS,
        moved=2**22,
        room=16,
    )(normed, from_low, from_high, kv_grads)
    term, prediction = lax.optimization_barrier((term, prediction))
    term = exchange(term.reshape(-1, shard, 2 * COLS), everyone)
    (grad_kv,) = call(
        gather_kernel, "gather_sums", [((shard, 2 * LATENT_DIM), F32)], "v", flops=2**17, moved=2**20
    )(term.reshape(halves, GROUP, members_num, shard, 2 * COLS))

    if members_num == 2:
        got = jnp.roll(swap(prediction, "ens", 1), part, axis=1)
        lane = lax.broadcasted_iota(jnp.int32, prediction.shape, 1)
        prediction = jnp.where(lane // part == ens, prediction, got)
    else:
        prediction = prediction.reshape(FIELD_NUM, members_num, part).transpose(1, 0, 2)
        prediction = exchange(prediction, "ens").transpose(1, 0, 2)
    return (prediction.reshape(1, FIELD_NUM, node_rows), grad_kv)


def solution(mesh):
    space, ens = mesh.shape["space"], mesh.shape["ens"]
    split = Mesh(
        mesh.devices.reshape(space // GROUP, QUAD, CORES, ens), ("half", "quad", "core", "ens")
    )
    nodes = ("half", "quad", "core")
    shards = nodes + ("ens",)
    in_specs = (
        P("ens", nodes, None),
        P(shards, None),
        P(shards, None),
        P(shards, None),
        P(None, nodes),
        P(nodes),
        P(nodes, None),
    )
    out_specs = (P("ens", None, nodes), P(shards, None))
    return jax.shard_map(body, mesh=split, in_specs=in_specs, out_specs=out_specs, check_vma=False)
```

```python
import functools

import jax
import jax.numpy as jnp
from jax import lax
from jax.experimental import pallas as pl
from jax.experimental.pallas import tpu as pltpu
from jax.sharding import Mesh
from jax.sharding import PartitionSpec as P

LATENT_DIM = 1024
HEADS = 16
HEAD = 64
FIELD_NUM = 100
TILE = 64
RADIUS = 2
K_NB = 4
QUAD = 4
CORES = 2
GROUP = QUAD * CORES
COLS = LATENT_DIM // GROUP
RIM = RADIUS * TILE
FIELD_PAD = 128
PAIR = 2
WINDOW = (PAIR + 2 * RADIUS) * TILE
NOWHERE = 100
NOTE_ROWS = 16
CHUNKS = 4

NORM_EPS = 1e-06
SOFT_WIDTH = 0.0625
MASKED = -1e30

F32 = jnp.float32
BF16 = jnp.bfloat16

VMEM = pl.BlockSpec(memory_space=pltpu.VMEM)
SMEM = pl.BlockSpec(memory_space=pltpu.SMEM)
HBM = pl.BlockSpec(memory_space=pltpu.HBM)
ANYWHERE = pl.BlockSpec(memory_space=pl.ANY)
OVER_ROWS = (((0,), (0,)), ((), ()))
OVER_COLUMNS = (((1,), (1,)), ((), ()))


def call(kernel, name, outs, ins, scratch=(), flops=0, moved=0, exps=0, room=8, results=None):
    results = results or "v" * len(outs)
    spaces = {"s": SMEM, "v": VMEM, "h": HBM, "a": ANYWHERE}
    made = pl.pallas_call(
        kernel,
        out_shape=[
            pltpu.HBM(shape, kind) if space == "h" else jax.ShapeDtypeStruct(shape, kind)
            for (shape, kind), space in zip(outs, results)
        ],
        in_specs=[spaces[space] for space in ins],
        out_specs=[spaces[space] for space in results],
        scratch_shapes=list(scratch),
        compiler_params=pltpu.CompilerParams(vmem_limit_bytes=room * 2**20),
        cost_estimate=pl.CostEstimate(flops=flops, bytes_accessed=moved, transcendentals=exps),
        name=name,
    )

    def run(*args):
        return made(
            *[
                pltpu.with_memory_space_constraint(arg, pltpu.HBM) if space == "h" else arg
                for arg, space in zip(args, ins)
            ]
        )

    return run


def fetch(pairs, sems, first=0):
    copies = [
        pltpu.make_async_copy(source, target, sems.at[first + at])
        for at, (source, target) in enumerate(pairs)
    ]
    for copy in copies:
        copy.start()
    return copies


def wait(copies):
    for copy in copies:
        copy.wait()


def weights_kernel(w_any, mix_any, readout_any, columns_any, packed_any, *refs):
    w, columns, readout, packed, sems = refs
    copies = fetch(
        [(w_any, w), (readout_any, readout), (mix_any, packed.at[:, :LATENT_DIM])], sems
    )
    copies[0].wait()
    for g in range(GROUP):
        for part in range(3):
            at = (part * GROUP + g) * COLS
            columns[g, :, part * COLS : (part + 1) * COLS] = w[:, at : at + COLS]
    halves, _, members_num = columns_any.shape[:3]
    out = fetch(
        [
            (columns, columns_any.at[half, :, m])
            for half in range(halves)
            for m in range(members_num)
        ],
        sems,
        3,
    )
    wait(copies[1:])
    packed[:, LATENT_DIM:] = jnp.zeros((packed.shape[0], FIELD_PAD), BF16)
    packed[:, LATENT_DIM : LATENT_DIM + FIELD_NUM] = readout[...]
    wait(out + fetch([(packed, packed_any)], sems, 3 + len(out)))


def norm_kernel(near_any, source_any, normed_any, *refs):
    parts, (near, source, normed, sems) = refs[:-4], refs[-4:]
    ens = lax.axis_index("ens")
    copies = fetch([(source_any, source), (near_any, near)], sems)
    rows = source.shape[0]
    copies[0].wait()
    moves = []
    for step, part_any in enumerate(parts):
        count, part, _ = part_any.shape
        for m in range(count):
            place = (ens ^ step) if len(parts) == 2 else m
            place = pl.multiple_of(place * part, part)
            moves.append((source.at[pl.ds(place, part)], part_any.at[m]))
    out = fetch(moves, sems, 2)
    states = source[...].astype(F32)
    inverse = lax.rsqrt(jnp.mean(states * states, axis=-1, keepdims=True) + NORM_EPS)
    normed[:rows, :] = (states * inverse).astype(BF16)
    copies[1].wait()
    row = lax.broadcasted_iota(jnp.int32, (NOTE_ROWS, 128), 0)
    lane = lax.broadcasted_iota(jnp.int32, (NOTE_ROWS, 128), 1)
    note = jnp.zeros((NOTE_ROWS, 128), F32)
    tiles = near.shape[0]
    first_tile = lax.axis_index(("half", "quad", "core")) * tiles
    for tile in range(tiles):
        for slot in range(K_NB):
            at = near[tile, slot]
            step = jnp.where(at >= 0, at - first_tile - tile, NOWHERE).astype(F32)
            note = jnp.where((row == tile) & (lane == slot), step, note)
    normed[rows:, :] = jnp.zeros((NOTE_ROWS, LATENT_DIM), BF16)
    normed[rows:, :128] = note.astype(BF16)
    wait(out + fetch([(normed, normed_any)], sems, 2 + len(out)))


def merge_halves_kernel(mine_ref, other_ref, sent_ref, out_ref):
    half = lax.axis_index("half")
    width = mine_ref.shape[1]
    out_ref[half, :, :width] = mine_ref[...]
    out_ref[half ^ 1, :, :width] = other_ref[...]
    out_ref[:, :, width:] = sent_ref[...].reshape(2, -1, LATENT_DIM)


def merge_members_kernel(mine_ref, other_ref, packed_ref, source_ref):
    ens = lax.axis_index("ens")
    width = packed_ref.shape[3]
    for half in range(2):
        packed_ref[half, ens] = mine_ref[half, :, :width]
        packed_ref[half, ens ^ 1] = other_ref[half, :, :width]
    source_ref[...] = other_ref[:, :, width:].reshape(source_ref.shape)


def owners():
    core, quad = lax.axis_index("core"), lax.axis_index("quad")
    return [(quad ^ step) * CORES + (core ^ flip) for flip in range(CORES) for step in range(QUAD)]


def collect_kernel(*refs):
    blocks, (normed_any, steps_ref, notes, sems) = refs[:GROUP], refs[GROUP:]
    block = blocks[0].shape[0] - NOTE_ROWS
    pairs = []
    for rows_ref, owner in zip(blocks, owners()):
        place = pl.ds(pl.multiple_of(owner * block, block), block)
        pairs.append((rows_ref.at[:block], normed_any.at[place]))
        pairs.append((rows_ref.at[block:, :128], notes.at[owner]))
    wait(fetch(pairs, sems))
    steps_ref[...] = notes[...].astype(F32)


def put_rims(rims, first, last):
    if len(rims) == 1:
        rims[0][...] = jnp.where(lax.axis_index("half") == 0, last, first)
    else:
        rims[0][...], rims[1][...] = first, last


def rims_kernel(normed_any, *refs):
    rows, sems = refs[-2:]
    if len(refs[0].shape) == 2:
        columns, w, rims = refs[:1], refs[1], refs[2:-2]
        pairs = [(columns[0], w)]
    else:
        columns, w, rims = refs[:2], refs[2], refs[3:-2]
        ens = lax.axis_index("ens")
        pairs = [(part, w.at[:, ens ^ step]) for step, part in enumerate(columns)]
    last = normed_any.shape[0] - RIM
    if len(rims) == 1:
        place = pl.multiple_of(jnp.where(lax.axis_index("half") == 0, last, 0), RIM)
        pairs.append((normed_any.at[pl.ds(place, RIM)], rows.at[0]))
    else:
        pairs += [(normed_any.at[:RIM], rows.at[0]), (normed_any.at[last:], rows.at[1])]
    wait(fetch(pairs, sems))
    weights = w[...].reshape(LATENT_DIM, 3 * COLS)[:, COLS:]
    for at, rim_ref in enumerate(rims):
        rim_ref[...] = jnp.dot(rows[at], weights, preferred_element_type=F32).astype(BF16)


def project_kernel(normed_any, w_ref, q_ref, kv_ref, normed, sems):
    chunk = normed.shape[0] // CHUNKS
    rows = [slice(at * chunk, (at + 1) * chunk) for at in range(CHUNKS)]
    copies = fetch([(normed_any.at[part], normed.at[part]) for part in rows], sems)
    weights = w_ref[...].reshape(LATENT_DIM, 3 * COLS)
    for part, copy in zip(rows, copies):
        copy.wait()
        projected = jnp.dot(normed[part, :], weights, preferred_element_type=F32).astype(BF16)
        q_ref[part, :] = projected[:, :COLS] * jnp.asarray(HEAD**-0.5, BF16)
        kv_ref[part, :] = projected[:, COLS:]


def assemble_kernel(*refs):
    pieces, (w_any, sems) = refs[:GROUP], refs[GROUP:]
    core, quad = lax.axis_index("core"), lax.axis_index("quad")
    pairs = [
        (piece, w_any.at[:, quad ^ (at % QUAD), core ^ (at // QUAD)])
        for at, piece in enumerate(pieces)
    ]
    wait(fetch(pairs, sems))


def by_head(rows):
    lane = lax.broadcasted_iota(jnp.int32, rows.shape, 1)
    zero = jnp.zeros_like(rows)
    return jnp.concatenate(
        [jnp.where(lane < HEAD, rows, zero), jnp.where(lane < HEAD, zero, rows)], axis=0
    )


def usable_keys(steps_ref, pair):
    lane = (lax.broadcasted_iota(jnp.int32, (1, WINDOW), 1) // TILE - RADIUS).astype(F32)
    masks = []
    for query_tile in range(PAIR):
        found = jnp.zeros((1, WINDOW), F32)
        for slot in range(K_NB):
            step = steps_ref[pair, query_tile : query_tile + 1, slot : slot + 1]
            found = jnp.where(lane - query_tile == step, 1.0, found)
        masks.append(found)
    row = lax.broadcasted_iota(jnp.int32, (2 * PAIR * TILE, 1), 0) // TILE % PAIR
    return jnp.where(row == 0, masks[0], masks[1]) > 0


def raised_scores(queries, keys, usable):
    scores = lax.dot_general(queries, keys, OVER_COLUMNS, preferred_element_type=F32)
    scores = jnp.where(usable, scores, MASKED)
    raised = jnp.exp(scores - jnp.max(scores, axis=-1, keepdims=True))
    return raised, 1.0 / jnp.sum(raised, axis=-1, keepdims=True)


def attend(steps_ref, pair, queries, keys, values):
    raised, share = raised_scores(by_head(queries), keys, usable_keys(steps_ref, pair))
    both = jnp.dot(raised.astype(BF16), values, preferred_element_type=F32) * share
    lane = lax.broadcasted_iota(jnp.int32, queries.shape, 1)
    half = PAIR * TILE
    return jnp.where(lane < HEAD, both[:half], both[half:]).astype(BF16)


def interior_kernel(steps_ref, q_ref, kv_ref, out_ref):
    step = PAIR * TILE
    pairs = q_ref.shape[0] // step
    for pair in range(1, pairs - 1):
        window = slice((pair - 1) * step, (pair + 2) * step)
        rows = slice(pair * step, (pair + 1) * step)
        out_ref[rows, :] = attend(
            steps_ref, pair, q_ref[rows, :], kv_ref[window, :COLS], kv_ref[window, COLS:]
        )


def edge_kernel(steps_ref, q_ref, kv_ref, low_ref, high_ref, done_ref, out_ref):
    step = PAIR * TILE
    count = q_ref.shape[0]
    pairs = count // step
    out_ref[step : count - step, :] = done_ref[step : count - step, :]
    first = jnp.concatenate([low_ref[...], kv_ref[: 2 * step, :]], axis=0)
    last = jnp.concatenate([kv_ref[count - 2 * step :, :], high_ref[...]], axis=0)
    for pair, window in ((0, first), (pairs - 1, last)):
        rows = slice(pair * step, (pair + 1) * step)
        out_ref[rows, :] = attend(
            steps_ref, pair, q_ref[rows, :], window[:, :COLS], window[:, COLS:]
        )


def attend_back(steps_ref, pair, queries, grads, keys, values):
    queries, grads = by_head(queries), by_head(grads)
    raised, share = raised_scores(queries, keys, usable_keys(steps_ref, pair))
    probs = raised * share
    grad_probs = lax.dot_general(grads, values, OVER_COLUMNS, preferred_element_type=F32)
    row_delta = jnp.sum(probs * grad_probs, axis=-1, keepdims=True)
    grad_scores = (probs * (grad_probs - row_delta)).astype(BF16)
    key_grad = lax.dot_general(grad_scores, queries, OVER_ROWS, preferred_element_type=F32)
    value_grad = lax.dot_general(probs.astype(BF16), grads, OVER_ROWS, preferred_element_type=F32)
    return key_grad, value_grad


def edge_back_kernel(
    steps_ref, q_ref, kv_ref, low_ref, high_ref, g_ref, part_ref, *rims
):
    outer = []
    step = PAIR * TILE
    count = q_ref.shape[0]
    first = jnp.concatenate([low_ref[...], kv_ref[: 2 * step, :]], axis=0)
    last = jnp.concatenate([kv_ref[count - 2 * step :, :], high_ref[...]], axis=0)
    pairs = count // step
    for edge, pair, window in ((0, 0, first), (1, pairs - 1, last)):
        rows = slice(pair * step, (pair + 1) * step)
        grads = attend_back(
            steps_ref, pair, q_ref[rows, :], g_ref[rows, :], window[:, :COLS], window[:, COLS:]
        )
        rim = slice(0, RIM) if edge == 0 else slice(WINDOW - RIM, WINDOW)
        own = slice(RIM, WINDOW) if edge == 0 else slice(0, WINDOW - RIM)
        for at, grad in enumerate(grads):
            columns = slice(at * COLS, (at + 1) * COLS)
            part_ref[edge, :, columns] = grad[own]
        outer.append(jnp.concatenate([grad[rim].astype(BF16) for grad in grads], axis=1))
    put_rims(rims, *outer)


def interior_back_kernel(steps_ref, q_ref, kv_ref, g_ref, part_ref, out_ref):
    step = PAIR * TILE
    count = q_ref.shape[0]
    pairs = count // step
    reach = 2 * step
    out_ref[:reach, :] = part_ref[0]
    out_ref[reach : count - reach, :] = jnp.zeros((count - 2 * reach, 2 * COLS), F32)
    out_ref[count - reach :, :] = part_ref[1]
    for pair in range(1, pairs - 1):
        window = slice((pair - 1) * step, (pair + 2) * step)
        rows = slice(pair * step, (pair + 1) * step)
        key_grad, value_grad = attend_back(
            steps_ref,
            pair,
            q_ref[rows, :],
            g_ref[rows, :],
            kv_ref[window, :COLS],
            kv_ref[window, COLS:],
        )
        out_ref[window, :COLS] += key_grad
        out_ref[window, COLS:] += value_grad


def slope(spread):
    return spread * lax.rsqrt(spread * spread + SOFT_WIDTH)


def mix_kernel(att_ref, factor_ref, truth_any, w_any, *refs):
    sources, refs = refs[:-8], refs[-8:]
    pred_ref, grad_ref, a, truth_ref, truth, source, w, sems = refs
    members_num, part, _ = source.shape
    halves = w.shape[0]
    ens = lax.axis_index("ens")
    copies = fetch([(w_any.at[half], w.at[half]) for half in range(halves)], sems)
    pairs = [(truth_any, truth_ref)]
    if len(sources) == 1:
        pairs.append((sources[0], source))
    else:
        pairs += [(rows.at[0], source.at[ens ^ step]) for step, rows in enumerate(sources)]
    others = fetch(pairs, sems, halves)
    for g in range(GROUP):
        for m in range(members_num):
            a[m * part : (m + 1) * part, g * COLS : (g + 1) * COLS] = att_ref[g * members_num + m]
    wait(others)
    lane_part = lax.broadcasted_iota(jnp.int32, (1, a.shape[0]), 1) // part
    own_truth, own_factor = truth_ref[...], factor_ref[...]
    for turn in range(1, members_num):
        at = lane_part - turn
        here = jnp.where(at < 0, at + members_num, at) == ens
        own_truth = jnp.where(here, pltpu.roll(truth_ref[...], turn * part, 1), own_truth)
        own_factor = jnp.where(here, pltpu.roll(factor_ref[...], turn * part, 1), own_factor)
    truth[...] = jnp.zeros_like(truth)
    truth[:FIELD_NUM, :] = own_truth
    hidden = source[...].reshape(a.shape).astype(F32)
    count = LATENT_DIM // halves
    for half in range(halves):
        copies[half].wait()
        mix = w[half].reshape(count, LATENT_DIM + FIELD_PAD)[:, :LATENT_DIM]
        hidden += jnp.dot(
            a[:, half * count : (half + 1) * count], mix, preferred_element_type=F32
        )
    both = w[...].reshape(LATENT_DIM, LATENT_DIM + FIELD_PAD)
    mix, readout = both[:, :LATENT_DIM], both[:, LATENT_DIM:]
    inverse = lax.rsqrt(jnp.mean(hidden * hidden, axis=-1, keepdims=True) + NORM_EPS)
    decoded = (hidden * inverse).astype(BF16)
    prediction = lax.dot_general(
        readout, decoded, (((0,), (1,)), ((), ())), preferred_element_type=F32
    )
    pred_ref[...] = prediction[:FIELD_NUM]
    spread = jnp.zeros_like(prediction)
    for other in range(1, members_num):
        spread = spread + slope(prediction - pltpu.roll(prediction, other * part, 1))
    derivative = own_factor / FIELD_NUM * (
        slope(prediction - truth[...]) - spread / (members_num - 1)
    )
    grad_decoded = lax.dot_general(
        derivative.astype(BF16), readout, (((0,), (1,)), ((), ())), preferred_element_type=F32
    )
    grad_hidden = inverse * grad_decoded - hidden * inverse**3 * jnp.mean(
        grad_decoded * hidden, axis=-1, keepdims=True
    )
    grads = lax.dot_general(
        grad_hidden.astype(BF16), mix, OVER_COLUMNS, preferred_element_type=F32
    ).astype(BF16)
    for g in range(GROUP):
        for m in range(members_num):
            grad_ref[g * members_num + m] = grads[
                m * part : (m + 1) * part, g * COLS : (g + 1) * COLS
            ]


def product_kernel(normed_ref, from_low_ref, from_high_ref, grads_ref, out_ref):
    count = normed_ref.shape[0]
    half, last = lax.axis_index("half"), lax.axis_size("half") - 1
    from_low = jnp.where(half > 0, from_low_ref[...].astype(F32), 0.0)
    from_high = jnp.where(half < last, from_high_ref[...].astype(F32), 0.0)
    grads = grads_ref[...]
    grads = jnp.concatenate(
        [
            grads[:RIM] + from_low,
            grads[RIM : count - RIM],
            grads[count - RIM :] + from_high,
        ],
        axis=0,
    )
    high = grads.astype(BF16)
    low = (grads - high.astype(F32)).astype(BF16)
    both = lax.dot_general(
        normed_ref[...], jnp.concatenate([high, low], axis=1), OVER_ROWS, preferred_element_type=F32
    )
    out_ref[...] = (both[:, : 2 * COLS] + both[:, 2 * COLS :]).astype(BF16)


def gather_kernel(parts_ref, out_ref):
    halves, _, members_num = parts_ref.shape[:3]
    for g in range(GROUP):
        total = None
        for half in range(halves):
            for m in range(members_num):
                part = parts_ref[half, g, m].astype(F32)
                total = part if total is None else total + part
        out_ref[:, g * COLS : (g + 1) * COLS] = total[:, :COLS]
        out_ref[:, LATENT_DIM + g * COLS : LATENT_DIM + (g + 1) * COLS] = total[:, COLS:]


def exchange(chunks, axes):
    return lax.all_to_all(chunks, axes, 0, 0)


def swap(value, axis, step):
    return lax.ppermute(value, axis, [(i, i ^ step) for i in range(lax.axis_size(axis))])


def in_order(mine, axis, at):
    if lax.axis_size(axis) != 2:
        return lax.all_gather(mine, axis, axis=at)
    other = swap(mine, axis, 1)
    first = lax.axis_index(axis) == 0
    return jnp.stack([jnp.where(first, mine, other), jnp.where(first, other, mine)], axis=at)


def body(members, w_attn, w_mix, readout_matrix, observed_truth, cell_surface_factor, neighbours):
    halves, members_num = lax.axis_size("half"), lax.axis_size("ens")
    nodes = ("half", "quad", "core")
    everyone = nodes + ("ens",)
    shard = w_attn.shape[0]
    node_rows = members.shape[1]
    rows = GROUP * node_rows
    part = node_rows // members_num
    up = [(i, i + 1) for i in range(halves - 1)]
    down = [(target, source) for source, target in up]
    ens = lax.axis_index("ens")
    width = LATENT_DIM + FIELD_PAD
    paired = members_num == 2
    copies = 1 if paired else members_num
    source_parts = 2 if paired else 1

    columns, packed = call(
        weights_kernel,
        "prepare_weights",
        [((halves, GROUP, copies, shard, 3 * COLS), BF16), ((shard, width), BF16)],
        "hhh",
        [
            pltpu.VMEM(w_attn.shape, BF16),
            pltpu.VMEM((GROUP, shard, 3 * COLS), BF16),
            pltpu.VMEM(readout_matrix.shape, BF16),
            pltpu.VMEM((shard, width), BF16),
            pltpu.SemaphoreType.DMA((4 + halves * copies,)),
        ],
        moved=2**20,
        results="hh",
    )(w_attn, w_mix, readout_matrix)
    normed, *sources = call(
        norm_kernel,
        "norm",
        [((node_rows + NOTE_ROWS, LATENT_DIM), BF16)]
        + [((1 if paired else members_num, part, LATENT_DIM), BF16)] * source_parts,
        "hh",
        [
            pltpu.SMEM(neighbours.shape, jnp.int32),
            pltpu.VMEM((node_rows, LATENT_DIM), BF16),
            pltpu.VMEM((node_rows + NOTE_ROWS, LATENT_DIM), BF16),
            pltpu.SemaphoreType.DMA((3 + max(2, members_num),)),
        ],
        flops=2**20,
        moved=2**20,
        results="h" + "h" * source_parts,
    )(neighbours, members.reshape(node_rows, LATENT_DIM))

    square = paired and halves == 2 and shard % 16 == 0
    if square:
        other = swap(packed, "half", 1)
        columns, other, normed = lax.optimization_barrier((columns, other, normed))
        (packed,) = call(
            merge_halves_kernel,
            "merge_halves",
            [((2, shard, width + LATENT_DIM), BF16)],
            "vvv",
            moved=2**18,
        )(packed, other, sources[1])
    else:
        packed = in_order(packed, "half", 0)
    near = [normed, swap(normed, "quad", 1), None, swap(normed, "quad", 3)]
    if paired:
        columns = exchange(columns.reshape(-1, shard, 3 * COLS), nodes)
        columns, late = lax.optimization_barrier((columns, normed))
        columns = [columns, swap(columns, "ens", 1)]
    else:
        columns = [exchange(columns.reshape(-1, shard, 3 * COLS), everyone)]
        columns = [columns[0].reshape(LATENT_DIM, 3 * COLS)]
        late = normed
    near[2] = swap(late, "quad", 2)
    far = [swap(piece, "core", 1) for piece in near]
    normed, steps = call(
        collect_kernel,
        "collect",
        [((rows, LATENT_DIM), BF16), ((GROUP, NOTE_ROWS, 128), F32)],
        "a" * (2 * QUAD),
        [pltpu.VMEM((GROUP, NOTE_ROWS, 128), BF16), pltpu.SemaphoreType.DMA((2 * GROUP,))],
        moved=4 * 2**20,
        results="hv",
    )(*near, *far)

    if square:
        packed, arrived = call(
            merge_members_kernel,
            "merge_members",
            [((2, 2, shard, width), BF16), ((1, part, LATENT_DIM), BF16)],
            "vv",
            moved=2**19,
        )(packed, swap(packed, "ens", 1))
        packed = packed.reshape(2, 2 * shard, width)
        sources = [sources[0], arrived]
    else:
        packed = in_order(packed, "ens", 1).reshape(halves, members_num * shard, width)
    packed, near[2] = lax.optimization_barrier((packed, near[2]))
    pieces = [packed] + [swap(packed, "quad", step) for step in range(1, QUAD)]

    rim = ((RIM, 2 * COLS), BF16)
    rims = [rim] if halves == 2 else [rim, rim]
    w_shape = (GROUP * halves, 2, shard, 3 * COLS) if paired else (LATENT_DIM, 3 * COLS)
    weights, *inner = call(
        rims_kernel,
        "project_rims",
        [(w_shape, BF16)] + rims,
        "h" + "a" * len(columns),
        [pltpu.VMEM((len(rims), RIM, LATENT_DIM), BF16), pltpu.SemaphoreType.DMA((4,))],
        flops=RIM * LATENT_DIM * 4 * COLS,
        moved=2**20,
    )(normed, *columns)
    def across(inner):
        if halves == 2:
            got = swap(inner[0], "half", 1)
            return got, got
        return lax.ppermute(inner[1], "half", up), lax.ppermute(inner[0], "half", down)

    if not paired:
        sources = [exchange(sources[0], "ens")]
    elif not square:
        sources = [sources[0], swap(sources[1], "ens", 1)]
    low, high = across(inner)
    queries, own = call(
        project_kernel,
        "project",
        [((rows, COLS), BF16), ((rows, 2 * COLS), BF16)],
        "hv",
        [pltpu.VMEM((rows, LATENT_DIM), BF16), pltpu.SemaphoreType.DMA((CHUNKS,))],
        flops=rows * LATENT_DIM * 6 * COLS,
        moved=4 * 2**20,
    )(normed, weights)

    (outcome,) = call(
        interior_kernel,
        "attention_interior",
        [((rows, COLS), BF16)],
        "vvv",
        flops=rows * COLS * 2048,
        moved=2**21,
        exps=rows * 512,
    )(steps, queries, own)
    (outcome,) = call(
        edge_kernel,
        "attention_edges",
        [((rows, COLS), BF16)],
        "vvvvvv",
        flops=rows * COLS * 512,
        moved=2**20,
        exps=rows * 128,
    )(steps, queries, own, low, high, outcome)
    *pieces, own = lax.optimization_barrier((*pieces, own))
    pieces = pieces + [swap(piece, "core", 1) for piece in pieces]
    attended = exchange(outcome.reshape(GROUP * members_num, part, COLS), ("quad", "core", "ens"))
    block = (halves, QUAD, CORES, members_num * shard, width)
    (weights,) = call(
        assemble_kernel,
        "assemble",
        [(block, BF16)],
        "a" * len(pieces),
        [pltpu.SemaphoreType.DMA((GROUP,))],
        moved=4 * 2**20,
        results="h",
    )(*pieces)

    prediction, grads = call(
        mix_kernel,
        "mix_loss_backward",
        [((FIELD_NUM, node_rows), F32), ((GROUP * members_num, part, COLS), BF16)],
        "vvhh" + "a" * len(sources),
        [
            pltpu.VMEM((node_rows, LATENT_DIM), BF16),
            pltpu.VMEM(observed_truth.shape, F32),
            pltpu.VMEM((FIELD_PAD, node_rows), F32),
            pltpu.VMEM((members_num, part, LATENT_DIM), BF16),
            pltpu.VMEM(block, BF16),
            pltpu.SemaphoreType.DMA((halves + 1 + len(sources),)),
        ],
        flops=node_rows * LATENT_DIM * 4 * width,
        moved=2**22,
        room=14,
    )(attended, cell_surface_factor[None], observed_truth, weights, *sources)
    grads = exchange(grads, ("quad", "core", "ens")).reshape(rows, COLS)

    edges, *inner = call(
        edge_back_kernel,
        "attention_edges_back",
        [((2, WINDOW - RIM, 2 * COLS), F32)] + rims,
        "vvvvvv",
        flops=rows * COLS * 1280,
        moved=2**20,
        exps=rows * 128,
    )(steps, queries, own, low, high, grads)
    from_low, from_high = across(inner)
    (kv_grads,) = call(
        interior_back_kernel,
        "attention_interior_back",
        [((rows, 2 * COLS), F32)],
        "vvvvv",
        flops=rows * COLS * 4096,
        moved=2**22,
        exps=rows * 512,
        room=10,
    )(steps, queries, own, grads, edges)
    (term,) = call(
        product_kernel,
        "product",
        [((LATENT_DIM, 2 * COLS), BF16)],
        "vvvv",
        flops=rows * LATENT_DIM * 8 * COLS,
        moved=2**22,
        room=16,
    )(normed, from_low, from_high, kv_grads)
    term, prediction = lax.optimization_barrier((term, prediction))
    term = exchange(term.reshape(-1, shard, 2 * COLS), everyone)
    (grad_kv,) = call(
        gather_kernel, "gather_sums", [((shard, 2 * LATENT_DIM), F32)], "v", flops=2**17, moved=2**20
    )(term.reshape(halves, GROUP, members_num, shard, 2 * COLS))

    if members_num == 2:
        got = jnp.roll(swap(prediction, "ens", 1), part, axis=1)
        lane = lax.broadcasted_iota(jnp.int32, prediction.shape, 1)
        prediction = jnp.where(lane // part == ens, prediction, got)
    else:
        prediction = prediction.reshape(FIELD_NUM, members_num, part).transpose(1, 0, 2)
        prediction = exchange(prediction, "ens").transpose(1, 0, 2)
    return (prediction.reshape(1, FIELD_NUM, node_rows), grad_kv)


def solution(mesh):
    space, ens = mesh.shape["space"], mesh.shape["ens"]
    split = Mesh(
        mesh.devices.reshape(space // GROUP, QUAD, CORES, ens), ("half", "quad", "core", "ens")
    )
    nodes = ("half", "quad", "core")
    shards = nodes + ("ens",)
    in_specs = (
        P("ens", nodes, None),
        P(shards, None),
        P(shards, None),
        P(shards, None),
        P(None, nodes),
        P(nodes),
        P(nodes, None),
    )
    out_specs = (P("ens", None, nodes), P(shards, None))
    return jax.shard_map(body, mesh=split, in_specs=in_specs, out_specs=out_specs, check_vma=False)
```

```python
import functools

import jax
import jax.numpy as jnp
from jax import lax
from jax.experimental import pallas as pl
from jax.experimental.pallas import tpu as pltpu
from jax.sharding import Mesh
from jax.sharding import PartitionSpec as P

LATENT_DIM = 1024
HEADS = 16
HEAD = 64
FIELD_NUM = 100
TILE = 64
RADIUS = 2
K_NB = 4
QUAD = 4
CORES = 2
GROUP = QUAD * CORES
COLS = LATENT_DIM // GROUP
RIM = RADIUS * TILE
FIELD_PAD = 128
PAIR = 2
WINDOW = (PAIR + 2 * RADIUS) * TILE
NOWHERE = 100
NOTE_ROWS = 16
CHUNKS = 4

NORM_EPS = 1e-06
SOFT_WIDTH = 0.0625
MASKED = -1e30

F32 = jnp.float32
BF16 = jnp.bfloat16

VMEM = pl.BlockSpec(memory_space=pltpu.VMEM)
SMEM = pl.BlockSpec(memory_space=pltpu.SMEM)
HBM = pl.BlockSpec(memory_space=pltpu.HBM)
ANYWHERE = pl.BlockSpec(memory_space=pl.ANY)
OVER_ROWS = (((0,), (0,)), ((), ()))
OVER_COLUMNS = (((1,), (1,)), ((), ()))


def call(kernel, name, outs, ins, scratch=(), flops=0, moved=0, exps=0, room=8, results=None):
    results = results or "v" * len(outs)
    spaces = {"s": SMEM, "v": VMEM, "h": HBM, "a": ANYWHERE}
    made = pl.pallas_call(
        kernel,
        out_shape=[
            pltpu.HBM(shape, kind) if space == "h" else jax.ShapeDtypeStruct(shape, kind)
            for (shape, kind), space in zip(outs, results)
        ],
        in_specs=[spaces[space] for space in ins],
        out_specs=[spaces[space] for space in results],
        scratch_shapes=list(scratch),
        compiler_params=pltpu.CompilerParams(vmem_limit_bytes=room * 2**20),
        cost_estimate=pl.CostEstimate(flops=flops, bytes_accessed=moved, transcendentals=exps),
        name=name,
    )

    def run(*args):
        return made(
            *[
                pltpu.with_memory_space_constraint(arg, pltpu.HBM) if space == "h" else arg
                for arg, space in zip(args, ins)
            ]
        )

    return run


def fetch(pairs, sems, first=0):
    copies = [
        pltpu.make_async_copy(source, target, sems.at[first + at])
        for at, (source, target) in enumerate(pairs)
    ]
    for copy in copies:
        copy.start()
    return copies


def wait(copies):
    for copy in copies:
        copy.wait()


def weights_kernel(w_any, mix_any, readout_any, columns_any, packed_any, *refs):
    w, columns, readout, packed, sems = refs
    copies = fetch(
        [(w_any, w), (readout_any, readout), (mix_any, packed.at[:, :LATENT_DIM])], sems
    )
    copies[0].wait()
    for g in range(GROUP):
        for part in range(3):
            at = (part * GROUP + g) * COLS
            columns[g, :, part * COLS : (part + 1) * COLS] = w[:, at : at + COLS]
    halves, _, members_num = columns_any.shape[:3]
    out = fetch(
        [
            (columns, columns_any.at[half, :, m])
            for half in range(halves)
            for m in range(members_num)
        ],
        sems,
        3,
    )
    wait(copies[1:])
    packed[:, LATENT_DIM:] = jnp.zeros((packed.shape[0], FIELD_PAD), BF16)
    packed[:, LATENT_DIM : LATENT_DIM + FIELD_NUM] = readout[...]
    wait(out + fetch([(packed, packed_any)], sems, 3 + len(out)))


def norm_kernel(near_any, source_any, normed_any, *refs):
    parts, (near, source, normed, sems) = refs[:-4], refs[-4:]
    ens = lax.axis_index("ens")
    copies = fetch([(source_any, source), (near_any, near)], sems)
    rows = source.shape[0]
    copies[0].wait()
    moves = []
    for step, part_any in enumerate(parts):
        count, part, _ = part_any.shape
        for m in range(count):
            place = (ens ^ step) if len(parts) == 2 else m
            place = pl.multiple_of(place * part, part)
            moves.append((source.at[pl.ds(place, part)], part_any.at[m]))
    out = fetch(moves, sems, 2)
    states = source[...].astype(F32)
    inverse = lax.rsqrt(jnp.mean(states * states, axis=-1, keepdims=True) + NORM_EPS)
    normed[:rows, :] = (states * inverse).astype(BF16)
    copies[1].wait()
    row = lax.broadcasted_iota(jnp.int32, (NOTE_ROWS, 128), 0)
    lane = lax.broadcasted_iota(jnp.int32, (NOTE_ROWS, 128), 1)
    note = jnp.zeros((NOTE_ROWS, 128), F32)
    tiles = near.shape[0]
    first_tile = lax.axis_index(("half", "quad", "core")) * tiles
    for tile in range(tiles):
        for slot in range(K_NB):
            at = near[tile, slot]
            step = jnp.where(at >= 0, at - first_tile - tile, NOWHERE).astype(F32)
            note = jnp.where((row == tile) & (lane == slot), step, note)
    normed[rows:, :] = jnp.zeros((NOTE_ROWS, LATENT_DIM), BF16)
    normed[rows:, :128] = note.astype(BF16)
    wait(out + fetch([(normed, normed_any)], sems, 2 + len(out)))


def owners():
    core, quad = lax.axis_index("core"), lax.axis_index("quad")
    return [(quad ^ step) * CORES + (core ^ flip) for flip in range(CORES) for step in range(QUAD)]


def collect_kernel(*refs):
    blocks, (normed_any, steps_ref, notes, sems) = refs[:GROUP], refs[GROUP:]
    block = blocks[0].shape[0] - NOTE_ROWS
    pairs = []
    for rows_ref, owner in zip(blocks, owners()):
        place = pl.ds(pl.multiple_of(owner * block, block), block)
        pairs.append((rows_ref.at[:block], normed_any.at[place]))
        pairs.append((rows_ref.at[block:, :128], notes.at[owner]))
    wait(fetch(pairs, sems))
    steps_ref[...] = notes[...].astype(F32)


def put_rims(rims, first, last):
    if len(rims) == 1:
        rims[0][...] = jnp.where(lax.axis_index("half") == 0, last, first)
    else:
        rims[0][...], rims[1][...] = first, last


def rims_kernel(normed_any, *refs):
    rows, sems = refs[-2:]
    if len(refs[0].shape) == 2:
        columns, w, rims = refs[:1], refs[1], refs[2:-2]
        pairs = [(columns[0], w)]
    else:
        columns, w, rims = refs[:2], refs[2], refs[3:-2]
        ens = lax.axis_index("ens")
        pairs = [(part, w.at[:, ens ^ step]) for step, part in enumerate(columns)]
    last = normed_any.shape[0] - RIM
    if len(rims) == 1:
        place = pl.multiple_of(jnp.where(lax.axis_index("half") == 0, last, 0), RIM)
        pairs.append((normed_any.at[pl.ds(place, RIM)], rows.at[0]))
    else:
        pairs += [(normed_any.at[:RIM], rows.at[0]), (normed_any.at[last:], rows.at[1])]
    wait(fetch(pairs, sems))
    weights = w[...].reshape(LATENT_DIM, 3 * COLS)[:, COLS:]
    for at, rim_ref in enumerate(rims):
        rim_ref[...] = jnp.dot(rows[at], weights, preferred_element_type=F32).astype(BF16)


def project_kernel(normed_any, w_ref, q_ref, kv_ref, normed, sems):
    chunk = normed.shape[0] // CHUNKS
    rows = [slice(at * chunk, (at + 1) * chunk) for at in range(CHUNKS)]
    copies = fetch([(normed_any.at[part], normed.at[part]) for part in rows], sems)
    weights = w_ref[...].reshape(LATENT_DIM, 3 * COLS)
    for part, copy in zip(rows, copies):
        copy.wait()
        projected = jnp.dot(normed[part, :], weights, preferred_element_type=F32).astype(BF16)
        q_ref[part, :] = projected[:, :COLS] * jnp.asarray(HEAD**-0.5, BF16)
        kv_ref[part, :] = projected[:, COLS:]


def assemble_kernel(*refs):
    pieces, (w_any, sems) = refs[:GROUP], refs[GROUP:]
    core, quad = lax.axis_index("core"), lax.axis_index("quad")
    pairs = [
        (piece, w_any.at[:, quad ^ (at % QUAD), core ^ (at // QUAD)])
        for at, piece in enumerate(pieces)
    ]
    wait(fetch(pairs, sems))


def by_head(rows):
    lane = lax.broadcasted_iota(jnp.int32, rows.shape, 1)
    zero = jnp.zeros_like(rows)
    return jnp.concatenate(
        [jnp.where(lane < HEAD, rows, zero), jnp.where(lane < HEAD, zero, rows)], axis=0
    )


def usable_keys(steps_ref, pair):
    lane = (lax.broadcasted_iota(jnp.int32, (1, WINDOW), 1) // TILE - RADIUS).astype(F32)
    masks = []
    for query_tile in range(PAIR):
        found = jnp.zeros((1, WINDOW), F32)
        for slot in range(K_NB):
            step = steps_ref[pair, query_tile : query_tile + 1, slot : slot + 1]
            found = jnp.where(lane - query_tile == step, 1.0, found)
        masks.append(found)
    row = lax.broadcasted_iota(jnp.int32, (2 * PAIR * TILE, 1), 0) // TILE % PAIR
    return jnp.where(row == 0, masks[0], masks[1]) > 0


def raised_scores(queries, keys, usable):
    scores = lax.dot_general(queries, keys, OVER_COLUMNS, preferred_element_type=F32)
    scores = jnp.where(usable, scores, MASKED)
    raised = jnp.exp(scores - jnp.max(scores, axis=-1, keepdims=True))
    return raised, 1.0 / jnp.sum(raised, axis=-1, keepdims=True)


def attend(steps_ref, pair, queries, keys, values):
    raised, share = raised_scores(by_head(queries), keys, usable_keys(steps_ref, pair))
    both = jnp.dot(raised.astype(BF16), values, preferred_element_type=F32) * share
    lane = lax.broadcasted_iota(jnp.int32, queries.shape, 1)
    half = PAIR * TILE
    return jnp.where(lane < HEAD, both[:half], both[half:]).astype(BF16)


def interior_kernel(steps_ref, q_ref, kv_ref, out_ref):
    step = PAIR * TILE
    pairs = q_ref.shape[0] // step
    for pair in range(1, pairs - 1):
        window = slice((pair - 1) * step, (pair + 2) * step)
        rows = slice(pair * step, (pair + 1) * step)
        out_ref[rows, :] = attend(
            steps_ref, pair, q_ref[rows, :], kv_ref[window, :COLS], kv_ref[window, COLS:]
        )


def edge_kernel(steps_ref, q_ref, kv_ref, low_ref, high_ref, done_ref, out_ref):
    step = PAIR * TILE
    count = q_ref.shape[0]
    pairs = count // step
    out_ref[step : count - step, :] = done_ref[step : count - step, :]
    first = jnp.concatenate([low_ref[...], kv_ref[: 2 * step, :]], axis=0)
    last = jnp.concatenate([kv_ref[count - 2 * step :, :], high_ref[...]], axis=0)
    for pair, window in ((0, first), (pairs - 1, last)):
        rows = slice(pair * step, (pair + 1) * step)
        out_ref[rows, :] = attend(
            steps_ref, pair, q_ref[rows, :], window[:, :COLS], window[:, COLS:]
        )


def attend_back(steps_ref, pair, queries, grads, keys, values):
    queries, grads = by_head(queries), by_head(grads)
    raised, share = raised_scores(queries, keys, usable_keys(steps_ref, pair))
    probs = raised * share
    grad_probs = lax.dot_general(grads, values, OVER_COLUMNS, preferred_element_type=F32)
    row_delta = jnp.sum(probs * grad_probs, axis=-1, keepdims=True)
    grad_scores = (probs * (grad_probs - row_delta)).astype(BF16)
    key_grad = lax.dot_general(grad_scores, queries, OVER_ROWS, preferred_element_type=F32)
    value_grad = lax.dot_general(probs.astype(BF16), grads, OVER_ROWS, preferred_element_type=F32)
    return key_grad, value_grad


def edge_back_kernel(
    steps_ref, q_ref, kv_ref, low_ref, high_ref, g_ref, part_ref, *rims
):
    outer = []
    step = PAIR * TILE
    count = q_ref.shape[0]
    first = jnp.concatenate([low_ref[...], kv_ref[: 2 * step, :]], axis=0)
    last = jnp.concatenate([kv_ref[count - 2 * step :, :], high_ref[...]], axis=0)
    pairs = count // step
    for edge, pair, window in ((0, 0, first), (1, pairs - 1, last)):
        rows = slice(pair * step, (pair + 1) * step)
        grads = attend_back(
            steps_ref, pair, q_ref[rows, :], g_ref[rows, :], window[:, :COLS], window[:, COLS:]
        )
        rim = slice(0, RIM) if edge == 0 else slice(WINDOW - RIM, WINDOW)
        own = slice(RIM, WINDOW) if edge == 0 else slice(0, WINDOW - RIM)
        for at, grad in enumerate(grads):
            columns = slice(at * COLS, (at + 1) * COLS)
            part_ref[edge, :, columns] = grad[own]
        outer.append(jnp.concatenate([grad[rim].astype(BF16) for grad in grads], axis=1))
    put_rims(rims, *outer)


def interior_back_kernel(steps_ref, q_ref, kv_ref, g_ref, part_ref, out_ref):
    step = PAIR * TILE
    count = q_ref.shape[0]
    pairs = count // step
    reach = 2 * step
    out_ref[:reach, :] = part_ref[0]
    out_ref[reach : count - reach, :] = jnp.zeros((count - 2 * reach, 2 * COLS), F32)
    out_ref[count - reach :, :] = part_ref[1]
    for pair in range(1, pairs - 1):
        window = slice((pair - 1) * step, (pair + 2) * step)
        rows = slice(pair * step, (pair + 1) * step)
        key_grad, value_grad = attend_back(
            steps_ref,
            pair,
            q_ref[rows, :],
            g_ref[rows, :],
            kv_ref[window, :COLS],
            kv_ref[window, COLS:],
        )
        out_ref[window, :COLS] += key_grad
        out_ref[window, COLS:] += value_grad


def slope(spread):
    return spread * lax.rsqrt(spread * spread + SOFT_WIDTH)


def mix_kernel(att_ref, factor_ref, truth_any, w_any, *refs):
    sources, refs = refs[:-8], refs[-8:]
    pred_ref, grad_ref, a, truth_ref, truth, source, w, sems = refs
    members_num, part, _ = source.shape
    halves = w.shape[0]
    ens = lax.axis_index("ens")
    copies = fetch([(w_any.at[half], w.at[half]) for half in range(halves)], sems)
    pairs = [(truth_any, truth_ref)]
    if len(sources) == 1:
        pairs.append((sources[0], source))
    else:
        pairs += [(rows.at[0], source.at[ens ^ step]) for step, rows in enumerate(sources)]
    others = fetch(pairs, sems, halves)
    for g in range(GROUP):
        for m in range(members_num):
            a[m * part : (m + 1) * part, g * COLS : (g + 1) * COLS] = att_ref[g * members_num + m]
    wait(others)
    lane_part = lax.broadcasted_iota(jnp.int32, (1, a.shape[0]), 1) // part
    own_truth, own_factor = truth_ref[...], factor_ref[...]
    for turn in range(1, members_num):
        at = lane_part - turn
        here = jnp.where(at < 0, at + members_num, at) == ens
        own_truth = jnp.where(here, pltpu.roll(truth_ref[...], turn * part, 1), own_truth)
        own_factor = jnp.where(here, pltpu.roll(factor_ref[...], turn * part, 1), own_factor)
    truth[...] = jnp.zeros_like(truth)
    truth[:FIELD_NUM, :] = own_truth
    hidden = source[...].reshape(a.shape).astype(F32)
    count = LATENT_DIM // halves
    for half in range(halves):
        copies[half].wait()
        mix = w[half].reshape(count, LATENT_DIM + FIELD_PAD)[:, :LATENT_DIM]
        hidden += jnp.dot(
            a[:, half * count : (half + 1) * count], mix, preferred_element_type=F32
        )
    both = w[...].reshape(LATENT_DIM, LATENT_DIM + FIELD_PAD)
    mix, readout = both[:, :LATENT_DIM], both[:, LATENT_DIM:]
    inverse = lax.rsqrt(jnp.mean(hidden * hidden, axis=-1, keepdims=True) + NORM_EPS)
    decoded = (hidden * inverse).astype(BF16)
    prediction = lax.dot_general(
        readout, decoded, (((0,), (1,)), ((), ())), preferred_element_type=F32
    )
    pred_ref[...] = prediction[:FIELD_NUM]
    spread = jnp.zeros_like(prediction)
    for other in range(1, members_num):
        spread = spread + slope(prediction - pltpu.roll(prediction, other * part, 1))
    derivative = own_factor / FIELD_NUM * (
        slope(prediction - truth[...]) - spread / (members_num - 1)
    )
    grad_decoded = lax.dot_general(
        derivative.astype(BF16), readout, (((0,), (1,)), ((), ())), preferred_element_type=F32
    )
    grad_hidden = inverse * grad_decoded - hidden * inverse**3 * jnp.mean(
        grad_decoded * hidden, axis=-1, keepdims=True
    )
    grads = lax.dot_general(
        grad_hidden.astype(BF16), mix, OVER_COLUMNS, preferred_element_type=F32
    ).astype(BF16)
    for g in range(GROUP):
        for m in range(members_num):
            grad_ref[g * members_num + m] = grads[
                m * part : (m + 1) * part, g * COLS : (g + 1) * COLS
            ]


def product_kernel(normed_ref, from_low_ref, from_high_ref, grads_ref, out_ref):
    count = normed_ref.shape[0]
    half, last = lax.axis_index("half"), lax.axis_size("half") - 1
    from_low = jnp.where(half > 0, from_low_ref[...].astype(F32), 0.0)
    from_high = jnp.where(half < last, from_high_ref[...].astype(F32), 0.0)
    grads = grads_ref[...]
    grads = jnp.concatenate(
        [
            grads[:RIM] + from_low,
            grads[RIM : count - RIM],
            grads[count - RIM :] + from_high,
        ],
        axis=0,
    )
    high = grads.astype(BF16)
    low = (grads - high.astype(F32)).astype(BF16)
    both = lax.dot_general(
        normed_ref[...], jnp.concatenate([high, low], axis=1), OVER_ROWS, preferred_element_type=F32
    )
    out_ref[...] = (both[:, : 2 * COLS] + both[:, 2 * COLS :]).astype(BF16)


def gather_kernel(parts_ref, out_ref):
    halves, _, members_num = parts_ref.shape[:3]
    for g in range(GROUP):
        total = None
        for half in range(halves):
            for m in range(members_num):
                part = parts_ref[half, g, m].astype(F32)
                total = part if total is None else total + part
        out_ref[:, g * COLS : (g + 1) * COLS] = total[:, :COLS]
        out_ref[:, LATENT_DIM + g * COLS : LATENT_DIM + (g + 1) * COLS] = total[:, COLS:]


def exchange(chunks, axes):
    return lax.all_to_all(chunks, axes, 0, 0)


def swap(value, axis, step):
    return lax.ppermute(value, axis, [(i, i ^ step) for i in range(lax.axis_size(axis))])


def in_order(mine, axis, at):
    if lax.axis_size(axis) != 2:
        return lax.all_gather(mine, axis, axis=at)
    other = swap(mine, axis, 1)
    first = lax.axis_index(axis) == 0
    return jnp.stack([jnp.where(first, mine, other), jnp.where(first, other, mine)], axis=at)


def body(members, w_attn, w_mix, readout_matrix, observed_truth, cell_surface_factor, neighbours):
    halves, members_num = lax.axis_size("half"), lax.axis_size("ens")
    nodes = ("half", "quad", "core")
    everyone = nodes + ("ens",)
    shard = w_attn.shape[0]
    node_rows = members.shape[1]
    rows = GROUP * node_rows
    part = node_rows // members_num
    up = [(i, i + 1) for i in range(halves - 1)]
    down = [(target, source) for source, target in up]
    ens = lax.axis_index("ens")
    width = LATENT_DIM + FIELD_PAD
    paired = members_num == 2
    copies = 1 if paired else members_num
    source_parts = 2 if paired else 1

    columns, packed = call(
        weights_kernel,
        "prepare_weights",
        [((halves, GROUP, copies, shard, 3 * COLS), BF16), ((shard, width), BF16)],
        "hhh",
        [
            pltpu.VMEM(w_attn.shape, BF16),
            pltpu.VMEM((GROUP, shard, 3 * COLS), BF16),
            pltpu.VMEM(readout_matrix.shape, BF16),
            pltpu.VMEM((shard, width), BF16),
            pltpu.SemaphoreType.DMA((4 + halves * copies,)),
        ],
        moved=2**20,
        results="hh",
    )(w_attn, w_mix, readout_matrix)
    normed, *sources = call(
        norm_kernel,
        "norm",
        [((node_rows + NOTE_ROWS, LATENT_DIM), BF16)]
        + [((1 if paired else members_num, part, LATENT_DIM), BF16)] * source_parts,
        "hh",
        [
            pltpu.SMEM(neighbours.shape, jnp.int32),
            pltpu.VMEM((node_rows, LATENT_DIM), BF16),
            pltpu.VMEM((node_rows + NOTE_ROWS, LATENT_DIM), BF16),
            pltpu.SemaphoreType.DMA((3 + max(2, members_num),)),
        ],
        flops=2**20,
        moved=2**20,
        results="h" + "h" * source_parts,
    )(neighbours, members.reshape(node_rows, LATENT_DIM))

    packed, normed = lax.optimization_barrier((in_order(packed, "half", 0), normed))
    near = [normed, swap(normed, "quad", 1), None, swap(normed, "quad", 3)]
    if paired:
        columns = exchange(columns.reshape(-1, shard, 3 * COLS), nodes)
        columns, late = lax.optimization_barrier((columns, normed))
        columns = [columns, swap(columns, "ens", 1)]
    else:
        columns = [exchange(columns.reshape(-1, shard, 3 * COLS), everyone)]
        columns = [columns[0].reshape(LATENT_DIM, 3 * COLS)]
        late = normed
    near[2] = swap(late, "quad", 2)
    near = list(lax.optimization_barrier(tuple(near)))
    far = [swap(piece, "core", 1) for piece in near]
    normed, steps = call(
        collect_kernel,
        "collect",
        [((rows, LATENT_DIM), BF16), ((GROUP, NOTE_ROWS, 128), F32)],
        "a" * (2 * QUAD),
        [pltpu.VMEM((GROUP, NOTE_ROWS, 128), BF16), pltpu.SemaphoreType.DMA((2 * GROUP,))],
        moved=4 * 2**20,
        results="hv",
    )(*near, *far)

    packed = in_order(packed, "ens", 1).reshape(halves, members_num * shard, width)
    packed, near[2] = lax.optimization_barrier((packed, near[2]))
    pieces = [packed] + [swap(packed, "quad", step) for step in range(1, QUAD)]

    rim = ((RIM, 2 * COLS), BF16)
    rims = [rim] if halves == 2 else [rim, rim]
    w_shape = (GROUP * halves, 2, shard, 3 * COLS) if paired else (LATENT_DIM, 3 * COLS)
    weights, *inner = call(
        rims_kernel,
        "project_rims",
        [(w_shape, BF16)] + rims,
        "h" + "a" * len(columns),
        [pltpu.VMEM((len(rims), RIM, LATENT_DIM), BF16), pltpu.SemaphoreType.DMA((4,))],
        flops=RIM * LATENT_DIM * 4 * COLS,
        moved=2**20,
    )(normed, *columns)
    def across(inner):
        if halves == 2:
            got = swap(inner[0], "half", 1)
            return got, got
        return lax.ppermute(inner[1], "half", up), lax.ppermute(inner[0], "half", down)

    weights, sources[-1] = lax.optimization_barrier((weights, sources[-1]))
    sources = [sources[0], swap(sources[1], "ens", 1)] if paired else [exchange(sources[0], "ens")]
    low, high = across(inner)
    queries, own = call(
        project_kernel,
        "project",
        [((rows, COLS), BF16), ((rows, 2 * COLS), BF16)],
        "hv",
        [pltpu.VMEM((rows, LATENT_DIM), BF16), pltpu.SemaphoreType.DMA((CHUNKS,))],
        flops=rows * LATENT_DIM * 6 * COLS,
        moved=4 * 2**20,
    )(normed, weights)

    (outcome,) = call(
        interior_kernel,
        "attention_interior",
        [((rows, COLS), BF16)],
        "vvv",
        flops=rows * COLS * 2048,
        moved=2**21,
        exps=rows * 512,
    )(steps, queries, own)
    (outcome,) = call(
        edge_kernel,
        "attention_edges",
        [((rows, COLS), BF16)],
        "vvvvvv",
        flops=rows * COLS * 512,
        moved=2**20,
        exps=rows * 128,
    )(steps, queries, own, low, high, outcome)
    *pieces, own = lax.optimization_barrier((*pieces, own))
    pieces = pieces + [swap(piece, "core", 1) for piece in pieces]
    attended = exchange(outcome.reshape(GROUP * members_num, part, COLS), ("quad", "core", "ens"))
    block = (halves, QUAD, CORES, members_num * shard, width)
    (weights,) = call(
        assemble_kernel,
        "assemble",
        [(block, BF16)],
        "a" * len(pieces),
        [pltpu.SemaphoreType.DMA((GROUP,))],
        moved=4 * 2**20,
        results="h",
    )(*pieces)

    prediction, grads = call(
        mix_kernel,
        "mix_loss_backward",
        [((FIELD_NUM, node_rows), F32), ((GROUP * members_num, part, COLS), BF16)],
        "vvhh" + "a" * len(sources),
        [
            pltpu.VMEM((node_rows, LATENT_DIM), BF16),
            pltpu.VMEM(observed_truth.shape, F32),
            pltpu.VMEM((FIELD_PAD, node_rows), F32),
            pltpu.VMEM((members_num, part, LATENT_DIM), BF16),
            pltpu.VMEM(block, BF16),
            pltpu.SemaphoreType.DMA((halves + 1 + len(sources),)),
        ],
        flops=node_rows * LATENT_DIM * 4 * width,
        moved=2**22,
        room=14,
    )(attended, cell_surface_factor[None], observed_truth, weights, *sources)
    grads = exchange(grads, ("quad", "core", "ens")).reshape(rows, COLS)

    edges, *inner = call(
        edge_back_kernel,
        "attention_edges_back",
        [((2, WINDOW - RIM, 2 * COLS), F32)] + rims,
        "vvvvvv",
        flops=rows * COLS * 1280,
        moved=2**20,
        exps=rows * 128,
    )(steps, queries, own, low, high, grads)
    from_low, from_high = across(inner)
    (kv_grads,) = call(
        interior_back_kernel,
        "attention_interior_back",
        [((rows, 2 * COLS), F32)],
        "vvvvv",
        flops=rows * COLS * 4096,
        moved=2**22,
        exps=rows * 512,
        room=10,
    )(steps, queries, own, grads, edges)
    (term,) = call(
        product_kernel,
        "product",
        [((LATENT_DIM, 2 * COLS), BF16)],
        "vvvv",
        flops=rows * LATENT_DIM * 8 * COLS,
        moved=2**22,
        room=16,
    )(normed, from_low, from_high, kv_grads)
    term, prediction = lax.optimization_barrier((term, prediction))
    term = exchange(term.reshape(-1, shard, 2 * COLS), everyone)
    (grad_kv,) = call(
        gather_kernel, "gather_sums", [((shard, 2 * LATENT_DIM), F32)], "v", flops=2**17, moved=2**20
    )(term.reshape(halves, GROUP, members_num, shard, 2 * COLS))

    if members_num == 2:
        got = jnp.roll(swap(prediction, "ens", 1), part, axis=1)
        lane = lax.broadcasted_iota(jnp.int32, prediction.shape, 1)
        prediction = jnp.where(lane // part == ens, prediction, got)
    else:
        prediction = prediction.reshape(FIELD_NUM, members_num, part).transpose(1, 0, 2)
        prediction = exchange(prediction, "ens").transpose(1, 0, 2)
    return (prediction.reshape(1, FIELD_NUM, node_rows), grad_kv)


def solution(mesh):
    space, ens = mesh.shape["space"], mesh.shape["ens"]
    split = Mesh(
        mesh.devices.reshape(space // GROUP, QUAD, CORES, ens), ("half", "quad", "core", "ens")
    )
    nodes = ("half", "quad", "core")
    shards = nodes + ("ens",)
    in_specs = (
        P("ens", nodes, None),
        P(shards, None),
        P(shards, None),
        P(shards, None),
        P(None, nodes),
        P(nodes),
        P(nodes, None),
    )
    out_specs = (P("ens", None, nodes), P(shards, None))
    return jax.shard_map(body, mesh=split, in_specs=in_specs, out_specs=out_specs, check_vma=False)
```

```python
import functools

import jax
import jax.numpy as jnp
from jax import lax
from jax.experimental import pallas as pl
from jax.experimental.pallas import tpu as pltpu
from jax.sharding import Mesh
from jax.sharding import PartitionSpec as P

LATENT_DIM = 1024
HEADS = 16
HEAD = 64
FIELD_NUM = 100
TILE = 64
RADIUS = 2
K_NB = 4
QUAD = 4
CORES = 2
GROUP = QUAD * CORES
COLS = LATENT_DIM // GROUP
RIM = RADIUS * TILE
FIELD_PAD = 128
PAIR = 2
WINDOW = (PAIR + 2 * RADIUS) * TILE
NOWHERE = 100
NOTE_ROWS = 16
CHUNKS = 4

NORM_EPS = 1e-06
SOFT_WIDTH = 0.0625
MASKED = -1e30

F32 = jnp.float32
BF16 = jnp.bfloat16

VMEM = pl.BlockSpec(memory_space=pltpu.VMEM)
SMEM = pl.BlockSpec(memory_space=pltpu.SMEM)
HBM = pl.BlockSpec(memory_space=pltpu.HBM)
ANYWHERE = pl.BlockSpec(memory_space=pl.ANY)
OVER_ROWS = (((0,), (0,)), ((), ()))
OVER_COLUMNS = (((1,), (1,)), ((), ()))


def call(kernel, name, outs, ins, scratch=(), flops=0, moved=0, exps=0, room=8, results=None):
    results = results or "v" * len(outs)
    spaces = {"s": SMEM, "v": VMEM, "h": HBM, "a": ANYWHERE}
    made = pl.pallas_call(
        kernel,
        out_shape=[
            pltpu.HBM(shape, kind) if space == "h" else jax.ShapeDtypeStruct(shape, kind)
            for (shape, kind), space in zip(outs, results)
        ],
        in_specs=[spaces[space] for space in ins],
        out_specs=[spaces[space] for space in results],
        scratch_shapes=list(scratch),
        compiler_params=pltpu.CompilerParams(vmem_limit_bytes=room * 2**20),
        cost_estimate=pl.CostEstimate(flops=flops, bytes_accessed=moved, transcendentals=exps),
        name=name,
    )

    def run(*args):
        return made(
            *[
                pltpu.with_memory_space_constraint(arg, pltpu.HBM) if space == "h" else arg
                for arg, space in zip(args, ins)
            ]
        )

    return run


def fetch(pairs, sems, first=0):
    copies = [
        pltpu.make_async_copy(source, target, sems.at[first + at])
        for at, (source, target) in enumerate(pairs)
    ]
    for copy in copies:
        copy.start()
    return copies


def wait(copies):
    for copy in copies:
        copy.wait()


def weights_kernel(
    w_any, mix_any, readout_any, source_any, columns_any, packed_any, sent_any, *refs
):
    w, columns, readout, packed, sent, sems = refs
    part = sent.shape[0]
    place = lax.axis_index("ens") ^ 1 if sent_any.shape[0] == 1 else 0
    place = pl.multiple_of(place * part, part)
    copies = fetch(
        [
            (w_any, w),
            (readout_any, readout),
            (mix_any, packed.at[:, :LATENT_DIM]),
            (source_any.at[pl.ds(place, part)], sent),
        ],
        sems,
    )
    copies[0].wait()
    for g in range(GROUP):
        for part in range(3):
            at = (part * GROUP + g) * COLS
            columns[g, :, part * COLS : (part + 1) * COLS] = w[:, at : at + COLS]
    halves, _, members_num = columns_any.shape[:3]
    out = fetch(
        [
            (columns, columns_any.at[half, :, m])
            for half in range(halves)
            for m in range(members_num)
        ],
        sems,
        4,
    )
    wait(copies[1:])
    out += fetch([(sent, sent_any.at[0])], sems, 4 + len(out))
    packed[:, LATENT_DIM:] = jnp.zeros((packed.shape[0], FIELD_PAD), BF16)
    packed[:, LATENT_DIM : LATENT_DIM + FIELD_NUM] = readout[...]
    wait(out + fetch([(packed, packed_any)], sems, 4 + len(out)))


def norm_kernel(near_any, source_any, normed_any, *refs):
    parts, (near, source, normed, sems) = refs[:-4], refs[-4:]
    ens = lax.axis_index("ens")
    copies = fetch([(source_any, source), (near_any, near)], sems)
    rows = source.shape[0]
    copies[0].wait()
    moves = []
    for step, part_any in enumerate(parts):
        count, part, _ = part_any.shape
        for m in range(count):
            place = (ens ^ step) if len(parts) == 2 else m
            place = pl.multiple_of(place * part, part)
            moves.append((source.at[pl.ds(place, part)], part_any.at[m]))
    out = fetch(moves, sems, 2)
    states = source[...].astype(F32)
    inverse = lax.rsqrt(jnp.mean(states * states, axis=-1, keepdims=True) + NORM_EPS)
    normed[:rows, :] = (states * inverse).astype(BF16)
    copies[1].wait()
    row = lax.broadcasted_iota(jnp.int32, (NOTE_ROWS, 128), 0)
    lane = lax.broadcasted_iota(jnp.int32, (NOTE_ROWS, 128), 1)
    note = jnp.zeros((NOTE_ROWS, 128), F32)
    tiles = near.shape[0]
    first_tile = lax.axis_index(("half", "quad", "core")) * tiles
    for tile in range(tiles):
        for slot in range(K_NB):
            at = near[tile, slot]
            step = jnp.where(at >= 0, at - first_tile - tile, NOWHERE).astype(F32)
            note = jnp.where((row == tile) & (lane == slot), step, note)
    normed[rows:, :] = jnp.zeros((NOTE_ROWS, LATENT_DIM), BF16)
    normed[rows:, :128] = note.astype(BF16)
    wait(out + fetch([(normed, normed_any)], sems, 2 + len(out)))


def merge_halves_kernel(mine_ref, other_ref, sent_ref, out_ref):
    half = lax.axis_index("half")
    width = mine_ref.shape[1]
    out_ref[half, :, :width] = mine_ref[...]
    out_ref[half ^ 1, :, :width] = other_ref[...]
    out_ref[:, :, width:] = sent_ref[...].reshape(2, -1, LATENT_DIM)


def merge_members_kernel(mine_ref, other_ref, packed_ref, source_ref):
    ens = lax.axis_index("ens")
    width = packed_ref.shape[3]
    for half in range(2):
        packed_ref[half, ens] = mine_ref[half, :, :width]
        packed_ref[half, ens ^ 1] = other_ref[half, :, :width]
    source_ref[...] = other_ref[:, :, width:].reshape(source_ref.shape)


def owners():
    core, quad = lax.axis_index("core"), lax.axis_index("quad")
    return [(quad ^ step) * CORES + (core ^ flip) for flip in range(CORES) for step in range(QUAD)]


def collect_kernel(*refs):
    blocks, (normed_any, steps_ref, notes, sems) = refs[:GROUP], refs[GROUP:]
    block = blocks[0].shape[0] - NOTE_ROWS
    pairs = []
    for rows_ref, owner in zip(blocks, owners()):
        place = pl.ds(pl.multiple_of(owner * block, block), block)
        pairs.append((rows_ref.at[:block], normed_any.at[place]))
        pairs.append((rows_ref.at[block:, :128], notes.at[owner]))
    wait(fetch(pairs, sems))
    steps_ref[...] = notes[...].astype(F32)


def put_rims(rims, first, last):
    if len(rims) == 1:
        rims[0][...] = jnp.where(lax.axis_index("half") == 0, last, first)
    else:
        rims[0][...], rims[1][...] = first, last


def rims_kernel(normed_any, *refs):
    rows, sems = refs[-2:]
    if len(refs[0].shape) == 2:
        columns, w, rims = refs[:1], refs[1], refs[2:-2]
        pairs = [(columns[0], w)]
    else:
        columns, w, rims = refs[:2], refs[2], refs[3:-2]
        ens = lax.axis_index("ens")
        pairs = [(part, w.at[:, ens ^ step]) for step, part in enumerate(columns)]
    last = normed_any.shape[0] - RIM
    if len(rims) == 1:
        place = pl.multiple_of(jnp.where(lax.axis_index("half") == 0, last, 0), RIM)
        pairs.append((normed_any.at[pl.ds(place, RIM)], rows.at[0]))
    else:
        pairs += [(normed_any.at[:RIM], rows.at[0]), (normed_any.at[last:], rows.at[1])]
    wait(fetch(pairs, sems))
    weights = w[...].reshape(LATENT_DIM, 3 * COLS)[:, COLS:]
    for at, rim_ref in enumerate(rims):
        rim_ref[...] = jnp.dot(rows[at], weights, preferred_element_type=F32).astype(BF16)


def project_kernel(normed_any, w_ref, q_ref, kv_ref, normed, sems):
    chunk = normed.shape[0] // CHUNKS
    rows = [slice(at * chunk, (at + 1) * chunk) for at in range(CHUNKS)]
    copies = fetch([(normed_any.at[part], normed.at[part]) for part in rows], sems)
    weights = w_ref[...].reshape(LATENT_DIM, 3 * COLS)
    for part, copy in zip(rows, copies):
        copy.wait()
        projected = jnp.dot(normed[part, :], weights, preferred_element_type=F32).astype(BF16)
        q_ref[part, :] = projected[:, :COLS] * jnp.asarray(HEAD**-0.5, BF16)
        kv_ref[part, :] = projected[:, COLS:]


def assemble_kernel(*refs):
    pieces, (w_any, sems) = refs[:GROUP], refs[GROUP:]
    core, quad = lax.axis_index("core"), lax.axis_index("quad")
    pairs = [
        (piece, w_any.at[:, quad ^ (at % QUAD), core ^ (at // QUAD)])
        for at, piece in enumerate(pieces)
    ]
    wait(fetch(pairs, sems))


def by_head(rows):
    lane = lax.broadcasted_iota(jnp.int32, rows.shape, 1)
    zero = jnp.zeros_like(rows)
    return jnp.concatenate(
        [jnp.where(lane < HEAD, rows, zero), jnp.where(lane < HEAD, zero, rows)], axis=0
    )


def usable_keys(steps_ref, pair):
    lane = (lax.broadcasted_iota(jnp.int32, (1, WINDOW), 1) // TILE - RADIUS).astype(F32)
    masks = []
    for query_tile in range(PAIR):
        found = jnp.zeros((1, WINDOW), F32)
        for slot in range(K_NB):
            step = steps_ref[pair, query_tile : query_tile + 1, slot : slot + 1]
            found = jnp.where(lane - query_tile == step, 1.0, found)
        masks.append(found)
    row = lax.broadcasted_iota(jnp.int32, (2 * PAIR * TILE, 1), 0) // TILE % PAIR
    return jnp.where(row == 0, masks[0], masks[1]) > 0


def raised_scores(queries, keys, usable):
    scores = lax.dot_general(queries, keys, OVER_COLUMNS, preferred_element_type=F32)
    scores = jnp.where(usable, scores, MASKED)
    raised = jnp.exp(scores - jnp.max(scores, axis=-1, keepdims=True))
    return raised, 1.0 / jnp.sum(raised, axis=-1, keepdims=True)


def attend(steps_ref, pair, queries, keys, values):
    raised, share = raised_scores(by_head(queries), keys, usable_keys(steps_ref, pair))
    both = jnp.dot(raised.astype(BF16), values, preferred_element_type=F32) * share
    lane = lax.broadcasted_iota(jnp.int32, queries.shape, 1)
    half = PAIR * TILE
    return jnp.where(lane < HEAD, both[:half], both[half:]).astype(BF16)


def interior_kernel(steps_ref, q_ref, kv_ref, out_ref):
    step = PAIR * TILE
    pairs = q_ref.shape[0] // step
    for pair in range(1, pairs - 1):
        window = slice((pair - 1) * step, (pair + 2) * step)
        rows = slice(pair * step, (pair + 1) * step)
        out_ref[rows, :] = attend(
            steps_ref, pair, q_ref[rows, :], kv_ref[window, :COLS], kv_ref[window, COLS:]
        )


def edge_kernel(steps_ref, q_ref, kv_ref, low_ref, high_ref, done_ref, out_ref):
    step = PAIR * TILE
    count = q_ref.shape[0]
    pairs = count // step
    out_ref[step : count - step, :] = done_ref[step : count - step, :]
    first = jnp.concatenate([low_ref[...], kv_ref[: 2 * step, :]], axis=0)
    last = jnp.concatenate([kv_ref[count - 2 * step :, :], high_ref[...]], axis=0)
    for pair, window in ((0, first), (pairs - 1, last)):
        rows = slice(pair * step, (pair + 1) * step)
        out_ref[rows, :] = attend(
            steps_ref, pair, q_ref[rows, :], window[:, :COLS], window[:, COLS:]
        )


def attend_back(steps_ref, pair, queries, grads, keys, values):
    queries, grads = by_head(queries), by_head(grads)
    raised, share = raised_scores(queries, keys, usable_keys(steps_ref, pair))
    probs = raised * share
    grad_probs = lax.dot_general(grads, values, OVER_COLUMNS, preferred_element_type=F32)
    row_delta = jnp.sum(probs * grad_probs, axis=-1, keepdims=True)
    grad_scores = (probs * (grad_probs - row_delta)).astype(BF16)
    key_grad = lax.dot_general(grad_scores, queries, OVER_ROWS, preferred_element_type=F32)
    value_grad = lax.dot_general(probs.astype(BF16), grads, OVER_ROWS, preferred_element_type=F32)
    return key_grad, value_grad


def edge_back_kernel(
    steps_ref, q_ref, kv_ref, low_ref, high_ref, g_ref, part_ref, *rims
):
    outer = []
    step = PAIR * TILE
    count = q_ref.shape[0]
    first = jnp.concatenate([low_ref[...], kv_ref[: 2 * step, :]], axis=0)
    last = jnp.concatenate([kv_ref[count - 2 * step :, :], high_ref[...]], axis=0)
    pairs = count // step
    for edge, pair, window in ((0, 0, first), (1, pairs - 1, last)):
        rows = slice(pair * step, (pair + 1) * step)
        grads = attend_back(
            steps_ref, pair, q_ref[rows, :], g_ref[rows, :], window[:, :COLS], window[:, COLS:]
        )
        rim = slice(0, RIM) if edge == 0 else slice(WINDOW - RIM, WINDOW)
        own = slice(RIM, WINDOW) if edge == 0 else slice(0, WINDOW - RIM)
        for at, grad in enumerate(grads):
            columns = slice(at * COLS, (at + 1) * COLS)
            part_ref[edge, :, columns] = grad[own]
        outer.append(jnp.concatenate([grad[rim].astype(BF16) for grad in grads], axis=1))
    put_rims(rims, *outer)


def interior_back_kernel(steps_ref, q_ref, kv_ref, g_ref, part_ref, out_ref):
    step = PAIR * TILE
    count = q_ref.shape[0]
    pairs = count // step
    reach = 2 * step
    out_ref[:reach, :] = part_ref[0]
    out_ref[reach : count - reach, :] = jnp.zeros((count - 2 * reach, 2 * COLS), F32)
    out_ref[count - reach :, :] = part_ref[1]
    for pair in range(1, pairs - 1):
        window = slice((pair - 1) * step, (pair + 2) * step)
        rows = slice(pair * step, (pair + 1) * step)
        key_grad, value_grad = attend_back(
            steps_ref,
            pair,
            q_ref[rows, :],
            g_ref[rows, :],
            kv_ref[window, :COLS],
            kv_ref[window, COLS:],
        )
        out_ref[window, :COLS] += key_grad
        out_ref[window, COLS:] += value_grad


def slope(spread):
    return spread * lax.rsqrt(spread * spread + SOFT_WIDTH)


def mix_kernel(att_ref, factor_ref, truth_any, w_any, *refs):
    sources, refs = refs[:-8], refs[-8:]
    pred_ref, grad_ref, a, truth_ref, truth, source, w, sems = refs
    members_num, part, _ = source.shape
    halves = w.shape[0]
    ens = lax.axis_index("ens")
    copies = fetch([(w_any.at[half], w.at[half]) for half in range(halves)], sems)
    pairs = [(truth_any, truth_ref)]
    if len(sources) == 1:
        pairs.append((sources[0], source))
    else:
        pairs += [(rows.at[0], source.at[ens ^ step]) for step, rows in enumerate(sources)]
    others = fetch(pairs, sems, halves)
    for g in range(GROUP):
        for m in range(members_num):
            a[m * part : (m + 1) * part, g * COLS : (g + 1) * COLS] = att_ref[g * members_num + m]
    wait(others)
    lane_part = lax.broadcasted_iota(jnp.int32, (1, a.shape[0]), 1) // part
    own_truth, own_factor = truth_ref[...], factor_ref[...]
    for turn in range(1, members_num):
        at = lane_part - turn
        here = jnp.where(at < 0, at + members_num, at) == ens
        own_truth = jnp.where(here, pltpu.roll(truth_ref[...], turn * part, 1), own_truth)
        own_factor = jnp.where(here, pltpu.roll(factor_ref[...], turn * part, 1), own_factor)
    truth[...] = jnp.zeros_like(truth)
    truth[:FIELD_NUM, :] = own_truth
    hidden = source[...].reshape(a.shape).astype(F32)
    count = LATENT_DIM // halves
    for half in range(halves):
        copies[half].wait()
        mix = w[half].reshape(count, LATENT_DIM + FIELD_PAD)[:, :LATENT_DIM]
        hidden += jnp.dot(
            a[:, half * count : (half + 1) * count], mix, preferred_element_type=F32
        )
    both = w[...].reshape(LATENT_DIM, LATENT_DIM + FIELD_PAD)
    mix, readout = both[:, :LATENT_DIM], both[:, LATENT_DIM:]
    inverse = lax.rsqrt(jnp.mean(hidden * hidden, axis=-1, keepdims=True) + NORM_EPS)
    decoded = (hidden * inverse).astype(BF16)
    prediction = lax.dot_general(
        readout, decoded, (((0,), (1,)), ((), ())), preferred_element_type=F32
    )
    pred_ref[...] = prediction[:FIELD_NUM]
    spread = jnp.zeros_like(prediction)
    for other in range(1, members_num):
        spread = spread + slope(prediction - pltpu.roll(prediction, other * part, 1))
    derivative = own_factor / FIELD_NUM * (
        slope(prediction - truth[...]) - spread / (members_num - 1)
    )
    grad_decoded = lax.dot_general(
        derivative.astype(BF16), readout, (((0,), (1,)), ((), ())), preferred_element_type=F32
    )
    grad_hidden = inverse * grad_decoded - hidden * inverse**3 * jnp.mean(
        grad_decoded * hidden, axis=-1, keepdims=True
    )
    grads = lax.dot_general(
        grad_hidden.astype(BF16), mix, OVER_COLUMNS, preferred_element_type=F32
    ).astype(BF16)
    for g in range(GROUP):
        for m in range(members_num):
            grad_ref[g * members_num + m] = grads[
                m * part : (m + 1) * part, g * COLS : (g + 1) * COLS
            ]


def product_kernel(normed_ref, from_low_ref, from_high_ref, grads_ref, out_ref):
    count = normed_ref.shape[0]
    half, last = lax.axis_index("half"), lax.axis_size("half") - 1
    from_low = jnp.where(half > 0, from_low_ref[...].astype(F32), 0.0)
    from_high = jnp.where(half < last, from_high_ref[...].astype(F32), 0.0)
    grads = grads_ref[...]
    grads = jnp.concatenate(
        [
            grads[:RIM] + from_low,
            grads[RIM : count - RIM],
            grads[count - RIM :] + from_high,
        ],
        axis=0,
    )
    high = grads.astype(BF16)
    low = (grads - high.astype(F32)).astype(BF16)
    both = lax.dot_general(
        normed_ref[...], jnp.concatenate([high, low], axis=1), OVER_ROWS, preferred_element_type=F32
    )
    out_ref[...] = (both[:, : 2 * COLS] + both[:, 2 * COLS :]).astype(BF16)


def gather_kernel(parts_ref, out_ref):
    halves, _, members_num = parts_ref.shape[:3]
    for g in range(GROUP):
        total = None
        for half in range(halves):
            for m in range(members_num):
                part = parts_ref[half, g, m].astype(F32)
                total = part if total is None else total + part
        out_ref[:, g * COLS : (g + 1) * COLS] = total[:, :COLS]
        out_ref[:, LATENT_DIM + g * COLS : LATENT_DIM + (g + 1) * COLS] = total[:, COLS:]


def exchange(chunks, axes):
    return lax.all_to_all(chunks, axes, 0, 0)


def swap(value, axis, step):
    return lax.ppermute(value, axis, [(i, i ^ step) for i in range(lax.axis_size(axis))])


def in_order(mine, axis, at):
    if lax.axis_size(axis) != 2:
        return lax.all_gather(mine, axis, axis=at)
    other = swap(mine, axis, 1)
    first = lax.axis_index(axis) == 0
    return jnp.stack([jnp.where(first, mine, other), jnp.where(first, other, mine)], axis=at)


def body(members, w_attn, w_mix, readout_matrix, observed_truth, cell_surface_factor, neighbours):
    halves, members_num = lax.axis_size("half"), lax.axis_size("ens")
    nodes = ("half", "quad", "core")
    everyone = nodes + ("ens",)
    shard = w_attn.shape[0]
    node_rows = members.shape[1]
    rows = GROUP * node_rows
    part = node_rows // members_num
    up = [(i, i + 1) for i in range(halves - 1)]
    down = [(target, source) for source, target in up]
    ens = lax.axis_index("ens")
    width = LATENT_DIM + FIELD_PAD
    paired = members_num == 2
    copies = 1 if paired else members_num
    source_parts = 2 if paired else 1

    columns, packed, leaving = call(
        weights_kernel,
        "prepare_weights",
        [
            ((halves, GROUP, copies, shard, 3 * COLS), BF16),
            ((shard, width), BF16),
            ((1 if paired else members_num, part, LATENT_DIM), BF16),
        ],
        "hhhh",
        [
            pltpu.VMEM(w_attn.shape, BF16),
            pltpu.VMEM((GROUP, shard, 3 * COLS), BF16),
            pltpu.VMEM(readout_matrix.shape, BF16),
            pltpu.VMEM((shard, width), BF16),
            pltpu.VMEM((part, LATENT_DIM), BF16),
            pltpu.SemaphoreType.DMA((6 + halves * copies,)),
        ],
        moved=2**20,
        results="hhh",
    )(w_attn, w_mix, readout_matrix, members.reshape(node_rows, LATENT_DIM))
    normed, *sources = call(
        norm_kernel,
        "norm",
        [((node_rows + NOTE_ROWS, LATENT_DIM), BF16)]
        + [((1 if paired else members_num, part, LATENT_DIM), BF16)] * source_parts,
        "hh",
        [
            pltpu.SMEM(neighbours.shape, jnp.int32),
            pltpu.VMEM((node_rows, LATENT_DIM), BF16),
            pltpu.VMEM((node_rows + NOTE_ROWS, LATENT_DIM), BF16),
            pltpu.SemaphoreType.DMA((3 + max(2, members_num),)),
        ],
        flops=2**20,
        moved=2**20,
        results="h" + "h" * source_parts,
    )(neighbours, members.reshape(node_rows, LATENT_DIM))

    square = paired and halves == 2 and shard % 16 == 0
    if square:
        (packed,) = call(
            merge_halves_kernel,
            "merge_halves",
            [((2, shard, width + LATENT_DIM), BF16)],
            "vvv",
            moved=2**18,
        )(packed, swap(packed, "half", 1), leaving)
    else:
        packed = in_order(packed, "half", 0)
    packed, normed = lax.optimization_barrier((packed, normed))
    near = [normed, swap(normed, "quad", 1), None, swap(normed, "quad", 3)]
    if paired:
        columns = exchange(columns.reshape(-1, shard, 3 * COLS), nodes)
        columns, late = lax.optimization_barrier((columns, normed))
        columns = [columns, swap(columns, "ens", 1)]
    else:
        columns = [exchange(columns.reshape(-1, shard, 3 * COLS), everyone)]
        columns = [columns[0].reshape(LATENT_DIM, 3 * COLS)]
        late = normed
    near[2] = swap(late, "quad", 2)
    near = list(lax.optimization_barrier(tuple(near)))
    far = [swap(piece, "core", 1) for piece in near]
    normed, steps = call(
        collect_kernel,
        "collect",
        [((rows, LATENT_DIM), BF16), ((GROUP, NOTE_ROWS, 128), F32)],
        "a" * (2 * QUAD),
        [pltpu.VMEM((GROUP, NOTE_ROWS, 128), BF16), pltpu.SemaphoreType.DMA((2 * GROUP,))],
        moved=4 * 2**20,
        results="hv",
    )(*near, *far)

    if square:
        packed, arrived = call(
            merge_members_kernel,
            "merge_members",
            [((2, 2, shard, width), BF16), ((1, part, LATENT_DIM), BF16)],
            "vv",
            moved=2**19,
        )(packed, swap(packed, "ens", 1))
        packed = packed.reshape(2, 2 * shard, width)
        sources = [sources[0], arrived]
    else:
        packed = in_order(packed, "ens", 1).reshape(halves, members_num * shard, width)
    packed, near[2] = lax.optimization_barrier((packed, near[2]))
    pieces = [packed] + [swap(packed, "quad", step) for step in range(1, QUAD)]

    rim = ((RIM, 2 * COLS), BF16)
    rims = [rim] if halves == 2 else [rim, rim]
    w_shape = (GROUP * halves, 2, shard, 3 * COLS) if paired else (LATENT_DIM, 3 * COLS)
    weights, *inner = call(
        rims_kernel,
        "project_rims",
        [(w_shape, BF16)] + rims,
        "h" + "a" * len(columns),
        [pltpu.VMEM((len(rims), RIM, LATENT_DIM), BF16), pltpu.SemaphoreType.DMA((4,))],
        flops=RIM * LATENT_DIM * 4 * COLS,
        moved=2**20,
    )(normed, *columns)
    def across(inner):
        if halves == 2:
            got = swap(inner[0], "half", 1)
            return got, got
        return lax.ppermute(inner[1], "half", up), lax.ppermute(inner[0], "half", down)

    if not paired:
        sources = [exchange(sources[0], "ens")]
    elif not square:
        sources = [sources[0], swap(sources[1], "ens", 1)]
    low, high = across(inner)
    queries, own = call(
        project_kernel,
        "project",
        [((rows, COLS), BF16), ((rows, 2 * COLS), BF16)],
        "hv",
        [pltpu.VMEM((rows, LATENT_DIM), BF16), pltpu.SemaphoreType.DMA((CHUNKS,))],
        flops=rows * LATENT_DIM * 6 * COLS,
        moved=4 * 2**20,
    )(normed, weights)

    (outcome,) = call(
        interior_kernel,
        "attention_interior",
        [((rows, COLS), BF16)],
        "vvv",
        flops=rows * COLS * 2048,
        moved=2**21,
        exps=rows * 512,
    )(steps, queries, own)
    (outcome,) = call(
        edge_kernel,
        "attention_edges",
        [((rows, COLS), BF16)],
        "vvvvvv",
        flops=rows * COLS * 512,
        moved=2**20,
        exps=rows * 128,
    )(steps, queries, own, low, high, outcome)
    *pieces, own = lax.optimization_barrier((*pieces, own))
    pieces = pieces + [swap(piece, "core", 1) for piece in pieces]
    attended = exchange(outcome.reshape(GROUP * members_num, part, COLS), ("quad", "core", "ens"))
    block = (halves, QUAD, CORES, members_num * shard, width)
    (weights,) = call(
        assemble_kernel,
        "assemble",
        [(block, BF16)],
        "a" * len(pieces),
        [pltpu.SemaphoreType.DMA((GROUP,))],
        moved=4 * 2**20,
        results="h",
    )(*pieces)

    prediction, grads = call(
        mix_kernel,
        "mix_loss_backward",
        [((FIELD_NUM, node_rows), F32), ((GROUP * members_num, part, COLS), BF16)],
        "vvhh" + "a" * len(sources),
        [
            pltpu.VMEM((node_rows, LATENT_DIM), BF16),
            pltpu.VMEM(observed_truth.shape, F32),
            pltpu.VMEM((FIELD_PAD, node_rows), F32),
            pltpu.VMEM((members_num, part, LATENT_DIM), BF16),
            pltpu.VMEM(block, BF16),
            pltpu.SemaphoreType.DMA((halves + 1 + len(sources),)),
        ],
        flops=node_rows * LATENT_DIM * 4 * width,
        moved=2**22,
        room=14,
    )(attended, cell_surface_factor[None], observed_truth, weights, *sources)
    grads = exchange(grads, ("quad", "core", "ens")).reshape(rows, COLS)

    edges, *inner = call(
        edge_back_kernel,
        "attention_edges_back",
        [((2, WINDOW - RIM, 2 * COLS), F32)] + rims,
        "vvvvvv",
        flops=rows * COLS * 1280,
        moved=2**20,
        exps=rows * 128,
    )(steps, queries, own, low, high, grads)
    from_low, from_high = across(inner)
    (kv_grads,) = call(
        interior_back_kernel,
        "attention_interior_back",
        [((rows, 2 * COLS), F32)],
        "vvvvv",
        flops=rows * COLS * 4096,
        moved=2**22,
        exps=rows * 512,
        room=10,
    )(steps, queries, own, grads, edges)
    (term,) = call(
        product_kernel,
        "product",
        [((LATENT_DIM, 2 * COLS), BF16)],
        "vvvv",
        flops=rows * LATENT_DIM * 8 * COLS,
        moved=2**22,
        room=16,
    )(normed, from_low, from_high, kv_grads)
    term, prediction = lax.optimization_barrier((term, prediction))
    term = exchange(term.reshape(-1, shard, 2 * COLS), everyone)
    (grad_kv,) = call(
        gather_kernel, "gather_sums", [((shard, 2 * LATENT_DIM), F32)], "v", flops=2**17, moved=2**20
    )(term.reshape(halves, GROUP, members_num, shard, 2 * COLS))

    if members_num == 2:
        got = jnp.roll(swap(prediction, "ens", 1), part, axis=1)
        lane = lax.broadcasted_iota(jnp.int32, prediction.shape, 1)
        prediction = jnp.where(lane // part == ens, prediction, got)
    else:
        prediction = prediction.reshape(FIELD_NUM, members_num, part).transpose(1, 0, 2)
        prediction = exchange(prediction, "ens").transpose(1, 0, 2)
    return (prediction.reshape(1, FIELD_NUM, node_rows), grad_kv)


def solution(mesh):
    space, ens = mesh.shape["space"], mesh.shape["ens"]
    split = Mesh(
        mesh.devices.reshape(space // GROUP, QUAD, CORES, ens), ("half", "quad", "core", "ens")
    )
    nodes = ("half", "quad", "core")
    shards = nodes + ("ens",)
    in_specs = (
        P("ens", nodes, None),
        P(shards, None),
        P(shards, None),
        P(shards, None),
        P(None, nodes),
        P(nodes),
        P(nodes, None),
    )
    out_specs = (P("ens", None, nodes), P(shards, None))
    return jax.shard_map(body, mesh=split, in_specs=in_specs, out_specs=out_specs, check_vma=False)
```

```python
import functools

import jax
import jax.numpy as jnp
from jax import lax
from jax.experimental import pallas as pl
from jax.experimental.pallas import tpu as pltpu
from jax.sharding import Mesh
from jax.sharding import PartitionSpec as P

LATENT_DIM = 1024
HEADS = 16
HEAD = 64
FIELD_NUM = 100
TILE = 64
RADIUS = 2
K_NB = 4
QUAD = 4
CORES = 2
GROUP = QUAD * CORES
COLS = LATENT_DIM // GROUP
RIM = RADIUS * TILE
FIELD_PAD = 128
PAIR = 2
WINDOW = (PAIR + 2 * RADIUS) * TILE
NOWHERE = 100
NOTE_ROWS = 16
CHUNKS = 4

NORM_EPS = 1e-06
SOFT_WIDTH = 0.0625
MASKED = -1e30

F32 = jnp.float32
BF16 = jnp.bfloat16

VMEM = pl.BlockSpec(memory_space=pltpu.VMEM)
SMEM = pl.BlockSpec(memory_space=pltpu.SMEM)
HBM = pl.BlockSpec(memory_space=pltpu.HBM)
ANYWHERE = pl.BlockSpec(memory_space=pl.ANY)
OVER_ROWS = (((0,), (0,)), ((), ()))
OVER_COLUMNS = (((1,), (1,)), ((), ()))


def call(kernel, name, outs, ins, scratch=(), flops=0, moved=0, exps=0, room=8, results=None):
    results = results or "v" * len(outs)
    spaces = {"s": SMEM, "v": VMEM, "h": HBM, "a": ANYWHERE}
    made = pl.pallas_call(
        kernel,
        out_shape=[
            pltpu.HBM(shape, kind) if space == "h" else jax.ShapeDtypeStruct(shape, kind)
            for (shape, kind), space in zip(outs, results)
        ],
        in_specs=[spaces[space] for space in ins],
        out_specs=[spaces[space] for space in results],
        scratch_shapes=list(scratch),
        compiler_params=pltpu.CompilerParams(vmem_limit_bytes=room * 2**20),
        cost_estimate=pl.CostEstimate(flops=flops, bytes_accessed=moved, transcendentals=exps),
        name=name,
    )

    def run(*args):
        return made(
            *[
                pltpu.with_memory_space_constraint(arg, pltpu.HBM) if space == "h" else arg
                for arg, space in zip(args, ins)
            ]
        )

    return run


def fetch(pairs, sems, first=0):
    copies = [
        pltpu.make_async_copy(source, target, sems.at[first + at])
        for at, (source, target) in enumerate(pairs)
    ]
    for copy in copies:
        copy.start()
    return copies


def wait(copies):
    for copy in copies:
        copy.wait()


def weights_kernel(
    w_any, mix_any, readout_any, source_any, columns_any, packed_any, sent_any, *refs
):
    w, columns, readout, packed, sent, sems = refs
    part = sent.shape[0]
    place = lax.axis_index("ens") ^ 1 if sent_any.shape[0] == 1 else 0
    place = pl.multiple_of(place * part, part)
    copies = fetch(
        [
            (w_any, w),
            (readout_any, readout),
            (mix_any, packed.at[:, :LATENT_DIM]),
            (source_any.at[pl.ds(place, part)], sent),
        ],
        sems,
    )
    copies[0].wait()
    for g in range(GROUP):
        for part in range(3):
            at = (part * GROUP + g) * COLS
            columns[g, :, part * COLS : (part + 1) * COLS] = w[:, at : at + COLS]
    halves, _, members_num = columns_any.shape[:3]
    out = fetch(
        [
            (columns, columns_any.at[half, :, m])
            for half in range(halves)
            for m in range(members_num)
        ],
        sems,
        4,
    )
    wait(copies[1:])
    out += fetch([(sent, sent_any.at[0])], sems, 4 + len(out))
    packed[:, LATENT_DIM:] = jnp.zeros((packed.shape[0], FIELD_PAD), BF16)
    packed[:, LATENT_DIM : LATENT_DIM + FIELD_NUM] = readout[...]
    wait(out + fetch([(packed, packed_any)], sems, 4 + len(out)))


def norm_kernel(near_any, source_any, normed_any, *refs):
    parts, (near, source, normed, sems) = refs[:-4], refs[-4:]
    ens = lax.axis_index("ens")
    copies = fetch([(source_any, source), (near_any, near)], sems)
    rows = source.shape[0]
    copies[0].wait()
    moves = []
    for step, part_any in enumerate(parts):
        count, part, _ = part_any.shape
        for m in range(count):
            place = (ens ^ step) if len(parts) == 2 else m
            place = pl.multiple_of(place * part, part)
            moves.append((source.at[pl.ds(place, part)], part_any.at[m]))
    out = fetch(moves, sems, 2)
    states = source[...].astype(F32)
    inverse = lax.rsqrt(jnp.mean(states * states, axis=-1, keepdims=True) + NORM_EPS)
    normed[:rows, :] = (states * inverse).astype(BF16)
    copies[1].wait()
    row = lax.broadcasted_iota(jnp.int32, (NOTE_ROWS, 128), 0)
    lane = lax.broadcasted_iota(jnp.int32, (NOTE_ROWS, 128), 1)
    note = jnp.zeros((NOTE_ROWS, 128), F32)
    tiles = near.shape[0]
    first_tile = lax.axis_index(("half", "quad", "core")) * tiles
    for tile in range(tiles):
        for slot in range(K_NB):
            at = near[tile, slot]
            step = jnp.where(at >= 0, at - first_tile - tile, NOWHERE).astype(F32)
            note = jnp.where((row == tile) & (lane == slot), step, note)
    normed[rows:, :] = jnp.zeros((NOTE_ROWS, LATENT_DIM), BF16)
    normed[rows:, :128] = note.astype(BF16)
    wait(out + fetch([(normed, normed_any)], sems, 2 + len(out)))


def merge_halves_kernel(mine_ref, other_ref, sent_ref, out_ref):
    half = lax.axis_index("half")
    width = mine_ref.shape[1]
    out_ref[half, :, :width] = mine_ref[...]
    out_ref[half ^ 1, :, :width] = other_ref[...]
    out_ref[:, :, width:] = sent_ref[...].reshape(2, -1, LATENT_DIM)


def merge_members_kernel(mine_ref, other_ref, packed_ref, source_ref):
    ens = lax.axis_index("ens")
    width = packed_ref.shape[3]
    for half in range(2):
        packed_ref[half, ens] = mine_ref[half, :, :width]
        packed_ref[half, ens ^ 1] = other_ref[half, :, :width]
    source_ref[...] = other_ref[:, :, width:].reshape(source_ref.shape)


def owners():
    core, quad = lax.axis_index("core"), lax.axis_index("quad")
    return [(quad ^ step) * CORES + (core ^ flip) for flip in range(CORES) for step in range(QUAD)]


def collect_kernel(*refs):
    blocks, (normed_any, steps_ref, notes, sems) = refs[:GROUP], refs[GROUP:]
    block = blocks[0].shape[0] - NOTE_ROWS
    pairs = []
    for rows_ref, owner in zip(blocks, owners()):
        place = pl.ds(pl.multiple_of(owner * block, block), block)
        pairs.append((rows_ref.at[:block], normed_any.at[place]))
        pairs.append((rows_ref.at[block:, :128], notes.at[owner]))
    wait(fetch(pairs, sems))
    steps_ref[...] = notes[...].astype(F32)


def put_rims(rims, first, last):
    if len(rims) == 1:
        rims[0][...] = jnp.where(lax.axis_index("half") == 0, last, first)
    else:
        rims[0][...], rims[1][...] = first, last


def rims_kernel(normed_any, *refs):
    rows, sems = refs[-2:]
    if len(refs[0].shape) == 2:
        columns, w, rims = refs[:1], refs[1], refs[2:-2]
        pairs = [(columns[0], w)]
    else:
        columns, w, rims = refs[:2], refs[2], refs[3:-2]
        ens = lax.axis_index("ens")
        pairs = [(part, w.at[:, ens ^ step]) for step, part in enumerate(columns)]
    last = normed_any.shape[0] - RIM
    if len(rims) == 1:
        place = pl.multiple_of(jnp.where(lax.axis_index("half") == 0, last, 0), RIM)
        pairs.append((normed_any.at[pl.ds(place, RIM)], rows.at[0]))
    else:
        pairs += [(normed_any.at[:RIM], rows.at[0]), (normed_any.at[last:], rows.at[1])]
    wait(fetch(pairs, sems))
    weights = w[...].reshape(LATENT_DIM, 3 * COLS)[:, COLS:]
    for at, rim_ref in enumerate(rims):
        rim_ref[...] = jnp.dot(rows[at], weights, preferred_element_type=F32).astype(BF16)


def project_kernel(normed_any, w_ref, q_ref, kv_ref, normed, sems):
    chunk = normed.shape[0] // CHUNKS
    rows = [slice(at * chunk, (at + 1) * chunk) for at in range(CHUNKS)]
    copies = fetch([(normed_any.at[part], normed.at[part]) for part in rows], sems)
    weights = w_ref[...].reshape(LATENT_DIM, 3 * COLS)
    for part, copy in zip(rows, copies):
        copy.wait()
        projected = jnp.dot(normed[part, :], weights, preferred_element_type=F32).astype(BF16)
        q_ref[part, :] = projected[:, :COLS] * jnp.asarray(HEAD**-0.5, BF16)
        kv_ref[part, :] = projected[:, COLS:]


def assemble_kernel(*refs):
    pieces, (w_any, sems) = refs[:GROUP], refs[GROUP:]
    core, quad = lax.axis_index("core"), lax.axis_index("quad")
    pairs = [
        (piece, w_any.at[:, quad ^ (at % QUAD), core ^ (at // QUAD)])
        for at, piece in enumerate(pieces)
    ]
    wait(fetch(pairs, sems))


def by_head(rows):
    lane = lax.broadcasted_iota(jnp.int32, rows.shape, 1)
    zero = jnp.zeros_like(rows)
    return jnp.concatenate(
        [jnp.where(lane < HEAD, rows, zero), jnp.where(lane < HEAD, zero, rows)], axis=0
    )


def usable_keys(steps_ref, pair):
    lane = (lax.broadcasted_iota(jnp.int32, (1, WINDOW), 1) // TILE - RADIUS).astype(F32)
    masks = []
    for query_tile in range(PAIR):
        found = jnp.zeros((1, WINDOW), F32)
        for slot in range(K_NB):
            step = steps_ref[pair, query_tile : query_tile + 1, slot : slot + 1]
            found = jnp.where(lane - query_tile == step, 1.0, found)
        masks.append(found)
    row = lax.broadcasted_iota(jnp.int32, (2 * PAIR * TILE, 1), 0) // TILE % PAIR
    return jnp.where(row == 0, masks[0], masks[1]) > 0


def raised_scores(queries, keys, usable):
    scores = lax.dot_general(queries, keys, OVER_COLUMNS, preferred_element_type=F32)
    scores = jnp.where(usable, scores, MASKED)
    raised = jnp.exp(scores - jnp.max(scores, axis=-1, keepdims=True))
    return raised, 1.0 / jnp.sum(raised, axis=-1, keepdims=True)


def attend(steps_ref, pair, queries, keys, values):
    raised, share = raised_scores(by_head(queries), keys, usable_keys(steps_ref, pair))
    both = jnp.dot(raised.astype(BF16), values, preferred_element_type=F32) * share
    lane = lax.broadcasted_iota(jnp.int32, queries.shape, 1)
    half = PAIR * TILE
    return jnp.where(lane < HEAD, both[:half], both[half:]).astype(BF16)


def interior_kernel(steps_ref, q_ref, kv_ref, out_ref):
    step = PAIR * TILE
    pairs = q_ref.shape[0] // step
    for pair in range(1, pairs - 1):
        window = slice((pair - 1) * step, (pair + 2) * step)
        rows = slice(pair * step, (pair + 1) * step)
        out_ref[rows, :] = attend(
            steps_ref, pair, q_ref[rows, :], kv_ref[window, :COLS], kv_ref[window, COLS:]
        )


def edge_kernel(steps_ref, q_ref, kv_ref, low_ref, high_ref, done_ref, out_ref):
    step = PAIR * TILE
    count = q_ref.shape[0]
    pairs = count // step
    out_ref[step : count - step, :] = done_ref[step : count - step, :]
    first = jnp.concatenate([low_ref[...], kv_ref[: 2 * step, :]], axis=0)
    last = jnp.concatenate([kv_ref[count - 2 * step :, :], high_ref[...]], axis=0)
    for pair, window in ((0, first), (pairs - 1, last)):
        rows = slice(pair * step, (pair + 1) * step)
        out_ref[rows, :] = attend(
            steps_ref, pair, q_ref[rows, :], window[:, :COLS], window[:, COLS:]
        )


def attend_back(steps_ref, pair, queries, grads, keys, values):
    queries, grads = by_head(queries), by_head(grads)
    raised, share = raised_scores(queries, keys, usable_keys(steps_ref, pair))
    probs = raised * share
    grad_probs = lax.dot_general(grads, values, OVER_COLUMNS, preferred_element_type=F32)
    row_delta = jnp.sum(probs * grad_probs, axis=-1, keepdims=True)
    grad_scores = (probs * (grad_probs - row_delta)).astype(BF16)
    key_grad = lax.dot_general(grad_scores, queries, OVER_ROWS, preferred_element_type=F32)
    value_grad = lax.dot_general(probs.astype(BF16), grads, OVER_ROWS, preferred_element_type=F32)
    return key_grad, value_grad


def edge_back_kernel(
    steps_ref, q_ref, kv_ref, low_ref, high_ref, g_ref, part_ref, *rims
):
    outer = []
    step = PAIR * TILE
    count = q_ref.shape[0]
    first = jnp.concatenate([low_ref[...], kv_ref[: 2 * step, :]], axis=0)
    last = jnp.concatenate([kv_ref[count - 2 * step :, :], high_ref[...]], axis=0)
    pairs = count // step
    for edge, pair, window in ((0, 0, first), (1, pairs - 1, last)):
        rows = slice(pair * step, (pair + 1) * step)
        grads = attend_back(
            steps_ref, pair, q_ref[rows, :], g_ref[rows, :], window[:, :COLS], window[:, COLS:]
        )
        rim = slice(0, RIM) if edge == 0 else slice(WINDOW - RIM, WINDOW)
        own = slice(RIM, WINDOW) if edge == 0 else slice(0, WINDOW - RIM)
        for at, grad in enumerate(grads):
            columns = slice(at * COLS, (at + 1) * COLS)
            part_ref[edge, :, columns] = grad[own]
        outer.append(jnp.concatenate([grad[rim].astype(BF16) for grad in grads], axis=1))
    put_rims(rims, *outer)


def interior_back_kernel(steps_ref, q_ref, kv_ref, g_ref, part_ref, out_ref):
    step = PAIR * TILE
    count = q_ref.shape[0]
    pairs = count // step
    reach = 2 * step
    out_ref[:reach, :] = part_ref[0]
    out_ref[reach : count - reach, :] = jnp.zeros((count - 2 * reach, 2 * COLS), F32)
    out_ref[count - reach :, :] = part_ref[1]
    for pair in range(1, pairs - 1):
        window = slice((pair - 1) * step, (pair + 2) * step)
        rows = slice(pair * step, (pair + 1) * step)
        key_grad, value_grad = attend_back(
            steps_ref,
            pair,
            q_ref[rows, :],
            g_ref[rows, :],
            kv_ref[window, :COLS],
            kv_ref[window, COLS:],
        )
        out_ref[window, :COLS] += key_grad
        out_ref[window, COLS:] += value_grad


def slope(spread):
    return spread * lax.rsqrt(spread * spread + SOFT_WIDTH)


def mix_kernel(att_ref, factor_ref, truth_any, w_any, *refs):
    sources, refs = refs[:-8], refs[-8:]
    pred_ref, grad_ref, a, truth_ref, truth, source, w, sems = refs
    members_num, part, _ = source.shape
    halves = w.shape[0]
    ens = lax.axis_index("ens")
    copies = fetch([(w_any.at[half], w.at[half]) for half in range(halves)], sems)
    pairs = [(truth_any, truth_ref)]
    if len(sources) == 1:
        pairs.append((sources[0], source))
    else:
        pairs += [(rows.at[0], source.at[ens ^ step]) for step, rows in enumerate(sources)]
    others = fetch(pairs, sems, halves)
    for g in range(GROUP):
        for m in range(members_num):
            a[m * part : (m + 1) * part, g * COLS : (g + 1) * COLS] = att_ref[g * members_num + m]
    wait(others)
    lane_part = lax.broadcasted_iota(jnp.int32, (1, a.shape[0]), 1) // part
    own_truth, own_factor = truth_ref[...], factor_ref[...]
    for turn in range(1, members_num):
        at = lane_part - turn
        here = jnp.where(at < 0, at + members_num, at) == ens
        own_truth = jnp.where(here, pltpu.roll(truth_ref[...], turn * part, 1), own_truth)
        own_factor = jnp.where(here, pltpu.roll(factor_ref[...], turn * part, 1), own_factor)
    truth[...] = jnp.zeros_like(truth)
    truth[:FIELD_NUM, :] = own_truth
    hidden = source[...].reshape(a.shape).astype(F32)
    count = LATENT_DIM // halves
    for half in range(halves):
        copies[half].wait()
        mix = w[half].reshape(count, LATENT_DIM + FIELD_PAD)[:, :LATENT_DIM]
        hidden += jnp.dot(
            a[:, half * count : (half + 1) * count], mix, preferred_element_type=F32
        )
    both = w[...].reshape(LATENT_DIM, LATENT_DIM + FIELD_PAD)
    mix, readout = both[:, :LATENT_DIM], both[:, LATENT_DIM:]
    inverse = lax.rsqrt(jnp.mean(hidden * hidden, axis=-1, keepdims=True) + NORM_EPS)
    decoded = (hidden * inverse).astype(BF16)
    prediction = lax.dot_general(
        readout, decoded, (((0,), (1,)), ((), ())), preferred_element_type=F32
    )
    pred_ref[...] = prediction[:FIELD_NUM]
    spread = jnp.zeros_like(prediction)
    for other in range(1, members_num):
        spread = spread + slope(prediction - pltpu.roll(prediction, other * part, 1))
    derivative = own_factor / FIELD_NUM * (
        slope(prediction - truth[...]) - spread / (members_num - 1)
    )
    grad_decoded = lax.dot_general(
        derivative.astype(BF16), readout, (((0,), (1,)), ((), ())), preferred_element_type=F32
    )
    grad_hidden = inverse * grad_decoded - hidden * inverse**3 * jnp.mean(
        grad_decoded * hidden, axis=-1, keepdims=True
    )
    grads = lax.dot_general(
        grad_hidden.astype(BF16), mix, OVER_COLUMNS, preferred_element_type=F32
    ).astype(BF16)
    for g in range(GROUP):
        for m in range(members_num):
            grad_ref[g * members_num + m] = grads[
                m * part : (m + 1) * part, g * COLS : (g + 1) * COLS
            ]


def product_kernel(normed_ref, from_low_ref, from_high_ref, grads_ref, out_ref):
    count = normed_ref.shape[0]
    half, last = lax.axis_index("half"), lax.axis_size("half") - 1
    from_low = jnp.where(half > 0, from_low_ref[...].astype(F32), 0.0)
    from_high = jnp.where(half < last, from_high_ref[...].astype(F32), 0.0)
    grads = grads_ref[...]
    grads = jnp.concatenate(
        [
            grads[:RIM] + from_low,
            grads[RIM : count - RIM],
            grads[count - RIM :] + from_high,
        ],
        axis=0,
    )
    high = grads.astype(BF16)
    low = (grads - high.astype(F32)).astype(BF16)
    both = lax.dot_general(
        normed_ref[...], jnp.concatenate([high, low], axis=1), OVER_ROWS, preferred_element_type=F32
    )
    out_ref[...] = (both[:, : 2 * COLS] + both[:, 2 * COLS :]).astype(BF16)


def gather_kernel(parts_ref, out_ref):
    halves, _, members_num = parts_ref.shape[:3]
    for g in range(GROUP):
        total = None
        for half in range(halves):
            for m in range(members_num):
                part = parts_ref[half, g, m].astype(F32)
                total = part if total is None else total + part
        out_ref[:, g * COLS : (g + 1) * COLS] = total[:, :COLS]
        out_ref[:, LATENT_DIM + g * COLS : LATENT_DIM + (g + 1) * COLS] = total[:, COLS:]


def exchange(chunks, axes):
    return lax.all_to_all(chunks, axes, 0, 0)


def swap(value, axis, step):
    return lax.ppermute(value, axis, [(i, i ^ step) for i in range(lax.axis_size(axis))])


def in_order(mine, axis, at):
    if lax.axis_size(axis) != 2:
        return lax.all_gather(mine, axis, axis=at)
    other = swap(mine, axis, 1)
    first = lax.axis_index(axis) == 0
    return jnp.stack([jnp.where(first, mine, other), jnp.where(first, other, mine)], axis=at)


def body(members, w_attn, w_mix, readout_matrix, observed_truth, cell_surface_factor, neighbours):
    halves, members_num = lax.axis_size("half"), lax.axis_size("ens")
    nodes = ("half", "quad", "core")
    everyone = nodes + ("ens",)
    shard = w_attn.shape[0]
    node_rows = members.shape[1]
    rows = GROUP * node_rows
    part = node_rows // members_num
    up = [(i, i + 1) for i in range(halves - 1)]
    down = [(target, source) for source, target in up]
    ens = lax.axis_index("ens")
    width = LATENT_DIM + FIELD_PAD
    paired = members_num == 2
    copies = 1 if paired else members_num
    source_parts = 2 if paired else 1

    columns, packed, leaving = call(
        weights_kernel,
        "prepare_weights",
        [
            ((halves, GROUP, copies, shard, 3 * COLS), BF16),
            ((shard, width), BF16),
            ((1 if paired else members_num, part, LATENT_DIM), BF16),
        ],
        "hhhh",
        [
            pltpu.VMEM(w_attn.shape, BF16),
            pltpu.VMEM((GROUP, shard, 3 * COLS), BF16),
            pltpu.VMEM(readout_matrix.shape, BF16),
            pltpu.VMEM((shard, width), BF16),
            pltpu.VMEM((part, LATENT_DIM), BF16),
            pltpu.SemaphoreType.DMA((6 + halves * copies,)),
        ],
        moved=2**20,
        results="hhh",
    )(w_attn, w_mix, readout_matrix, members.reshape(node_rows, LATENT_DIM))
    normed, *sources = call(
        norm_kernel,
        "norm",
        [((node_rows + NOTE_ROWS, LATENT_DIM), BF16)]
        + [((1 if paired else members_num, part, LATENT_DIM), BF16)] * source_parts,
        "hh",
        [
            pltpu.SMEM(neighbours.shape, jnp.int32),
            pltpu.VMEM((node_rows, LATENT_DIM), BF16),
            pltpu.VMEM((node_rows + NOTE_ROWS, LATENT_DIM), BF16),
            pltpu.SemaphoreType.DMA((3 + max(2, members_num),)),
        ],
        flops=2**20,
        moved=2**20,
        results="h" + "h" * source_parts,
    )(neighbours, members.reshape(node_rows, LATENT_DIM))

    square = paired and halves == 2 and shard % 16 == 0
    if square:
        (packed,) = call(
            merge_halves_kernel,
            "merge_halves",
            [((2, shard, width + LATENT_DIM), BF16)],
            "vvv",
            moved=2**22,
        )(packed, swap(packed, "half", 1), leaving)
    else:
        packed = in_order(packed, "half", 0)
    packed, normed = lax.optimization_barrier((packed, normed))
    near = [normed, swap(normed, "quad", 1), None, swap(normed, "quad", 3)]
    if paired:
        columns = exchange(columns.reshape(-1, shard, 3 * COLS), nodes)
        columns, late = lax.optimization_barrier((columns, normed))
        columns = [columns, swap(columns, "ens", 1)]
    else:
        columns = [exchange(columns.reshape(-1, shard, 3 * COLS), everyone)]
        columns = [columns[0].reshape(LATENT_DIM, 3 * COLS)]
        late = normed
    near[2] = swap(late, "quad", 2)
    near = list(lax.optimization_barrier(tuple(near)))
    far = [swap(piece, "core", 1) for piece in near]
    normed, steps = call(
        collect_kernel,
        "collect",
        [((rows, LATENT_DIM), BF16), ((GROUP, NOTE_ROWS, 128), F32)],
        "a" * (2 * QUAD),
        [pltpu.VMEM((GROUP, NOTE_ROWS, 128), BF16), pltpu.SemaphoreType.DMA((2 * GROUP,))],
        moved=4 * 2**20,
        results="hv",
    )(*near, *far)

    if square:
        packed, arrived = call(
            merge_members_kernel,
            "merge_members",
            [((2, 2, shard, width), BF16), ((1, part, LATENT_DIM), BF16)],
            "vv",
            moved=2**19,
        )(packed, swap(packed, "ens", 1))
        packed = packed.reshape(2, 2 * shard, width)
        sources = [sources[0], arrived]
    else:
        packed = in_order(packed, "ens", 1).reshape(halves, members_num * shard, width)
    packed, near[2] = lax.optimization_barrier((packed, near[2]))
    pieces = [packed] + [swap(packed, "quad", step) for step in range(1, QUAD)]

    rim = ((RIM, 2 * COLS), BF16)
    rims = [rim] if halves == 2 else [rim, rim]
    w_shape = (GROUP * halves, 2, shard, 3 * COLS) if paired else (LATENT_DIM, 3 * COLS)
    weights, *inner = call(
        rims_kernel,
        "project_rims",
        [(w_shape, BF16)] + rims,
        "h" + "a" * len(columns),
        [pltpu.VMEM((len(rims), RIM, LATENT_DIM), BF16), pltpu.SemaphoreType.DMA((4,))],
        flops=RIM * LATENT_DIM * 4 * COLS,
        moved=2**20,
    )(normed, *columns)
    def across(inner):
        if halves == 2:
            got = swap(inner[0], "half", 1)
            return got, got
        return lax.ppermute(inner[1], "half", up), lax.ppermute(inner[0], "half", down)

    if not paired:
        sources = [exchange(sources[0], "ens")]
    elif not square:
        sources = [sources[0], swap(sources[1], "ens", 1)]
    low, high = across(inner)
    queries, own = call(
        project_kernel,
        "project",
        [((rows, COLS), BF16), ((rows, 2 * COLS), BF16)],
        "hv",
        [pltpu.VMEM((rows, LATENT_DIM), BF16), pltpu.SemaphoreType.DMA((CHUNKS,))],
        flops=rows * LATENT_DIM * 6 * COLS,
        moved=4 * 2**20,
    )(normed, weights)

    (outcome,) = call(
        interior_kernel,
        "attention_interior",
        [((rows, COLS), BF16)],
        "vvv",
        flops=rows * COLS * 2048,
        moved=2**21,
        exps=rows * 512,
    )(steps, queries, own)
    (outcome,) = call(
        edge_kernel,
        "attention_edges",
        [((rows, COLS), BF16)],
        "vvvvvv",
        flops=rows * COLS * 512,
        moved=2**20,
        exps=rows * 128,
    )(steps, queries, own, low, high, outcome)
    *pieces, own = lax.optimization_barrier((*pieces, own))
    pieces = pieces + [swap(piece, "core", 1) for piece in pieces]
    attended = exchange(outcome.reshape(GROUP * members_num, part, COLS), ("quad", "core", "ens"))
    block = (halves, QUAD, CORES, members_num * shard, width)
    (weights,) = call(
        assemble_kernel,
        "assemble",
        [(block, BF16)],
        "a" * len(pieces),
        [pltpu.SemaphoreType.DMA((GROUP,))],
        moved=4 * 2**20,
        results="h",
    )(*pieces)

    prediction, grads = call(
        mix_kernel,
        "mix_loss_backward",
        [((FIELD_NUM, node_rows), F32), ((GROUP * members_num, part, COLS), BF16)],
        "vvhh" + "a" * len(sources),
        [
            pltpu.VMEM((node_rows, LATENT_DIM), BF16),
            pltpu.VMEM(observed_truth.shape, F32),
            pltpu.VMEM((FIELD_PAD, node_rows), F32),
            pltpu.VMEM((members_num, part, LATENT_DIM), BF16),
            pltpu.VMEM(block, BF16),
            pltpu.SemaphoreType.DMA((halves + 1 + len(sources),)),
        ],
        flops=node_rows * LATENT_DIM * 4 * width,
        moved=2**22,
        room=14,
    )(attended, cell_surface_factor[None], observed_truth, weights, *sources)
    grads = exchange(grads, ("quad", "core", "ens")).reshape(rows, COLS)

    edges, *inner = call(
        edge_back_kernel,
        "attention_edges_back",
        [((2, WINDOW - RIM, 2 * COLS), F32)] + rims,
        "vvvvvv",
        flops=rows * COLS * 1280,
        moved=2**20,
        exps=rows * 128,
    )(steps, queries, own, low, high, grads)
    from_low, from_high = across(inner)
    (kv_grads,) = call(
        interior_back_kernel,
        "attention_interior_back",
        [((rows, 2 * COLS), F32)],
        "vvvvv",
        flops=rows * COLS * 4096,
        moved=2**22,
        exps=rows * 512,
        room=10,
    )(steps, queries, own, grads, edges)
    (term,) = call(
        product_kernel,
        "product",
        [((LATENT_DIM, 2 * COLS), BF16)],
        "vvvv",
        flops=rows * LATENT_DIM * 8 * COLS,
        moved=2**22,
        room=16,
    )(normed, from_low, from_high, kv_grads)
    term, prediction = lax.optimization_barrier((term, prediction))
    term = exchange(term.reshape(-1, shard, 2 * COLS), everyone)
    (grad_kv,) = call(
        gather_kernel, "gather_sums", [((shard, 2 * LATENT_DIM), F32)], "v", flops=2**17, moved=2**20
    )(term.reshape(halves, GROUP, members_num, shard, 2 * COLS))

    if members_num == 2:
        got = jnp.roll(swap(prediction, "ens", 1), part, axis=1)
        lane = lax.broadcasted_iota(jnp.int32, prediction.shape, 1)
        prediction = jnp.where(lane // part == ens, prediction, got)
    else:
        prediction = prediction.reshape(FIELD_NUM, members_num, part).transpose(1, 0, 2)
        prediction = exchange(prediction, "ens").transpose(1, 0, 2)
    return (prediction.reshape(1, FIELD_NUM, node_rows), grad_kv)


def solution(mesh):
    space, ens = mesh.shape["space"], mesh.shape["ens"]
    split = Mesh(
        mesh.devices.reshape(space // GROUP, QUAD, CORES, ens), ("half", "quad", "core", "ens")
    )
    nodes = ("half", "quad", "core")
    shards = nodes + ("ens",)
    in_specs = (
        P("ens", nodes, None),
        P(shards, None),
        P(shards, None),
        P(shards, None),
        P(None, nodes),
        P(nodes),
        P(nodes, None),
    )
    out_specs = (P("ens", None, nodes), P(shards, None))
    return jax.shard_map(body, mesh=split, in_specs=in_specs, out_specs=out_specs, check_vma=False)
```

```python
import functools

import jax
import jax.numpy as jnp
from jax import lax
from jax.experimental import pallas as pl
from jax.experimental.pallas import tpu as pltpu
from jax.sharding import Mesh
from jax.sharding import PartitionSpec as P

LATENT_DIM = 1024
HEADS = 16
HEAD = 64
FIELD_NUM = 100
TILE = 64
RADIUS = 2
K_NB = 4
QUAD = 4
CORES = 2
GROUP = QUAD * CORES
COLS = LATENT_DIM // GROUP
RIM = RADIUS * TILE
FIELD_PAD = 128
PAIR = 2
WINDOW = (PAIR + 2 * RADIUS) * TILE
NOWHERE = 100
NOTE_ROWS = 16
CHUNKS = 4

NORM_EPS = 1e-06
SOFT_WIDTH = 0.0625
MASKED = -1e30

F32 = jnp.float32
BF16 = jnp.bfloat16

VMEM = pl.BlockSpec(memory_space=pltpu.VMEM)
SMEM = pl.BlockSpec(memory_space=pltpu.SMEM)
HBM = pl.BlockSpec(memory_space=pltpu.HBM)
ANYWHERE = pl.BlockSpec(memory_space=pl.ANY)
OVER_ROWS = (((0,), (0,)), ((), ()))
OVER_COLUMNS = (((1,), (1,)), ((), ()))


def call(kernel, name, outs, ins, scratch=(), flops=0, moved=0, exps=0, room=8, results=None):
    results = results or "v" * len(outs)
    spaces = {"s": SMEM, "v": VMEM, "h": HBM, "a": ANYWHERE}
    made = pl.pallas_call(
        kernel,
        out_shape=[
            pltpu.HBM(shape, kind) if space == "h" else jax.ShapeDtypeStruct(shape, kind)
            for (shape, kind), space in zip(outs, results)
        ],
        in_specs=[spaces[space] for space in ins],
        out_specs=[spaces[space] for space in results],
        scratch_shapes=list(scratch),
        compiler_params=pltpu.CompilerParams(vmem_limit_bytes=room * 2**20),
        cost_estimate=pl.CostEstimate(flops=flops, bytes_accessed=moved, transcendentals=exps),
        name=name,
    )

    def run(*args):
        return made(
            *[
                pltpu.with_memory_space_constraint(arg, pltpu.HBM) if space == "h" else arg
                for arg, space in zip(args, ins)
            ]
        )

    return run


def fetch(pairs, sems, first=0):
    copies = [
        pltpu.make_async_copy(source, target, sems.at[first + at])
        for at, (source, target) in enumerate(pairs)
    ]
    for copy in copies:
        copy.start()
    return copies


def wait(copies):
    for copy in copies:
        copy.wait()


def weights_kernel(w_any, mix_any, readout_any, columns_any, packed_any, *refs):
    w, columns, readout, packed, sems = refs
    copies = fetch(
        [(w_any, w), (readout_any, readout), (mix_any, packed.at[:, :LATENT_DIM])], sems
    )
    copies[0].wait()
    for g in range(GROUP):
        for part in range(3):
            at = (part * GROUP + g) * COLS
            columns[g, :, part * COLS : (part + 1) * COLS] = w[:, at : at + COLS]
    halves, _, members_num = columns_any.shape[:3]
    out = fetch(
        [
            (columns, columns_any.at[half, :, m])
            for half in range(halves)
            for m in range(members_num)
        ],
        sems,
        3,
    )
    wait(copies[1:])
    packed[:, LATENT_DIM:] = jnp.zeros((packed.shape[0], FIELD_PAD), BF16)
    packed[:, LATENT_DIM : LATENT_DIM + FIELD_NUM] = readout[...]
    wait(out + fetch([(packed, packed_any)], sems, 3 + len(out)))


def norm_kernel(near_any, source_any, normed_any, *refs):
    parts, (near, source, normed, sems) = refs[:-4], refs[-4:]
    ens = lax.axis_index("ens")
    copies = fetch([(source_any, source), (near_any, near)], sems)
    rows = source.shape[0]
    copies[0].wait()
    moves = []
    for step, part_any in enumerate(parts):
        count, part, _ = part_any.shape
        for m in range(count):
            place = (ens ^ step) if len(parts) == 2 else m
            place = pl.multiple_of(place * part, part)
            moves.append((source.at[pl.ds(place, part)], part_any.at[m]))
    out = fetch(moves, sems, 2)
    states = source[...].astype(F32)
    inverse = lax.rsqrt(jnp.mean(states * states, axis=-1, keepdims=True) + NORM_EPS)
    normed[:rows, :] = (states * inverse).astype(BF16)
    copies[1].wait()
    row = lax.broadcasted_iota(jnp.int32, (NOTE_ROWS, 128), 0)
    lane = lax.broadcasted_iota(jnp.int32, (NOTE_ROWS, 128), 1)
    note = jnp.zeros((NOTE_ROWS, 128), F32)
    tiles = near.shape[0]
    first_tile = lax.axis_index(("half", "quad", "core")) * tiles
    for tile in range(tiles):
        for slot in range(K_NB):
            at = near[tile, slot]
            step = jnp.where(at >= 0, at - first_tile - tile, NOWHERE).astype(F32)
            note = jnp.where((row == tile) & (lane == slot), step, note)
    normed[rows:, :] = jnp.zeros((NOTE_ROWS, LATENT_DIM), BF16)
    normed[rows:, :128] = note.astype(BF16)
    wait(out + fetch([(normed, normed_any)], sems, 2 + len(out)))


def attach_kernel(packed_ref, sent_ref, out_ref):
    width = packed_ref.shape[2]
    out_ref[:, :, :width] = packed_ref[...]
    out_ref[:, :, width:] = sent_ref[...].reshape(2, -1, LATENT_DIM)


def merge_members_kernel(mine_ref, other_ref, packed_ref, source_ref):
    ens = lax.axis_index("ens")
    width = packed_ref.shape[3]
    for half in range(2):
        packed_ref[half, ens] = mine_ref[half, :, :width]
        packed_ref[half, ens ^ 1] = other_ref[half, :, :width]
    source_ref[...] = other_ref[:, :, width:].reshape(source_ref.shape)


def owners():
    core, quad = lax.axis_index("core"), lax.axis_index("quad")
    return [(quad ^ step) * CORES + (core ^ flip) for flip in range(CORES) for step in range(QUAD)]


def collect_kernel(*refs):
    blocks, (normed_any, steps_ref, notes, sems) = refs[:GROUP], refs[GROUP:]
    block = blocks[0].shape[0] - NOTE_ROWS
    pairs = []
    for rows_ref, owner in zip(blocks, owners()):
        place = pl.ds(pl.multiple_of(owner * block, block), block)
        pairs.append((rows_ref.at[:block], normed_any.at[place]))
        pairs.append((rows_ref.at[block:, :128], notes.at[owner]))
    wait(fetch(pairs, sems))
    steps_ref[...] = notes[...].astype(F32)


def put_rims(rims, first, last):
    if len(rims) == 1:
        rims[0][...] = jnp.where(lax.axis_index("half") == 0, last, first)
    else:
        rims[0][...], rims[1][...] = first, last


def rims_kernel(normed_any, *refs):
    rows, sems = refs[-2:]
    if len(refs[0].shape) == 2:
        columns, w, rims = refs[:1], refs[1], refs[2:-2]
        pairs = [(columns[0], w)]
    else:
        columns, w, rims = refs[:2], refs[2], refs[3:-2]
        ens = lax.axis_index("ens")
        pairs = [(part, w.at[:, ens ^ step]) for step, part in enumerate(columns)]
    last = normed_any.shape[0] - RIM
    if len(rims) == 1:
        place = pl.multiple_of(jnp.where(lax.axis_index("half") == 0, last, 0), RIM)
        pairs.append((normed_any.at[pl.ds(place, RIM)], rows.at[0]))
    else:
        pairs += [(normed_any.at[:RIM], rows.at[0]), (normed_any.at[last:], rows.at[1])]
    wait(fetch(pairs, sems))
    weights = w[...].reshape(LATENT_DIM, 3 * COLS)[:, COLS:]
    for at, rim_ref in enumerate(rims):
        rim_ref[...] = jnp.dot(rows[at], weights, preferred_element_type=F32).astype(BF16)


def project_kernel(normed_any, w_ref, q_ref, kv_ref, normed, sems):
    chunk = normed.shape[0] // CHUNKS
    rows = [slice(at * chunk, (at + 1) * chunk) for at in range(CHUNKS)]
    copies = fetch([(normed_any.at[part], normed.at[part]) for part in rows], sems)
    weights = w_ref[...].reshape(LATENT_DIM, 3 * COLS)
    for part, copy in zip(rows, copies):
        copy.wait()
        projected = jnp.dot(normed[part, :], weights, preferred_element_type=F32).astype(BF16)
        q_ref[part, :] = projected[:, :COLS] * jnp.asarray(HEAD**-0.5, BF16)
        kv_ref[part, :] = projected[:, COLS:]


def assemble_kernel(*refs):
    pieces, (w_any, sems) = refs[:GROUP], refs[GROUP:]
    core, quad = lax.axis_index("core"), lax.axis_index("quad")
    pairs = [
        (piece, w_any.at[:, quad ^ (at % QUAD), core ^ (at // QUAD)])
        for at, piece in enumerate(pieces)
    ]
    wait(fetch(pairs, sems))


def by_head(rows):
    lane = lax.broadcasted_iota(jnp.int32, rows.shape, 1)
    zero = jnp.zeros_like(rows)
    return jnp.concatenate(
        [jnp.where(lane < HEAD, rows, zero), jnp.where(lane < HEAD, zero, rows)], axis=0
    )


def usable_keys(steps_ref, pair):
    lane = (lax.broadcasted_iota(jnp.int32, (1, WINDOW), 1) // TILE - RADIUS).astype(F32)
    masks = []
    for query_tile in range(PAIR):
        found = jnp.zeros((1, WINDOW), F32)
        for slot in range(K_NB):
            step = steps_ref[pair, query_tile : query_tile + 1, slot : slot + 1]
            found = jnp.where(lane - query_tile == step, 1.0, found)
        masks.append(found)
    row = lax.broadcasted_iota(jnp.int32, (2 * PAIR * TILE, 1), 0) // TILE % PAIR
    return jnp.where(row == 0, masks[0], masks[1]) > 0


def raised_scores(queries, keys, usable):
    scores = lax.dot_general(queries, keys, OVER_COLUMNS, preferred_element_type=F32)
    scores = jnp.where(usable, scores, MASKED)
    raised = jnp.exp(scores - jnp.max(scores, axis=-1, keepdims=True))
    return raised, 1.0 / jnp.sum(raised, axis=-1, keepdims=True)


def attend(steps_ref, pair, queries, keys, values):
    raised, share = raised_scores(by_head(queries), keys, usable_keys(steps_ref, pair))
    both = jnp.dot(raised.astype(BF16), values, preferred_element_type=F32) * share
    lane = lax.broadcasted_iota(jnp.int32, queries.shape, 1)
    half = PAIR * TILE
    return jnp.where(lane < HEAD, both[:half], both[half:]).astype(BF16)


def interior_kernel(steps_ref, q_ref, kv_ref, out_ref):
    step = PAIR * TILE
    pairs = q_ref.shape[0] // step
    for pair in range(1, pairs - 1):
        window = slice((pair - 1) * step, (pair + 2) * step)
        rows = slice(pair * step, (pair + 1) * step)
        out_ref[rows, :] = attend(
            steps_ref, pair, q_ref[rows, :], kv_ref[window, :COLS], kv_ref[window, COLS:]
        )


def edge_kernel(steps_ref, q_ref, kv_ref, low_ref, high_ref, done_ref, out_ref):
    step = PAIR * TILE
    count = q_ref.shape[0]
    pairs = count // step
    out_ref[step : count - step, :] = done_ref[step : count - step, :]
    first = jnp.concatenate([low_ref[...], kv_ref[: 2 * step, :]], axis=0)
    last = jnp.concatenate([kv_ref[count - 2 * step :, :], high_ref[...]], axis=0)
    for pair, window in ((0, first), (pairs - 1, last)):
        rows = slice(pair * step, (pair + 1) * step)
        out_ref[rows, :] = attend(
            steps_ref, pair, q_ref[rows, :], window[:, :COLS], window[:, COLS:]
        )


def attend_back(steps_ref, pair, queries, grads, keys, values):
    queries, grads = by_head(queries), by_head(grads)
    raised, share = raised_scores(queries, keys, usable_keys(steps_ref, pair))
    probs = raised * share
    grad_probs = lax.dot_general(grads, values, OVER_COLUMNS, preferred_element_type=F32)
    row_delta = jnp.sum(probs * grad_probs, axis=-1, keepdims=True)
    grad_scores = (probs * (grad_probs - row_delta)).astype(BF16)
    key_grad = lax.dot_general(grad_scores, queries, OVER_ROWS, preferred_element_type=F32)
    value_grad = lax.dot_general(probs.astype(BF16), grads, OVER_ROWS, preferred_element_type=F32)
    return key_grad, value_grad


def edge_back_kernel(
    steps_ref, q_ref, kv_ref, low_ref, high_ref, g_ref, part_ref, *rims
):
    outer = []
    step = PAIR * TILE
    count = q_ref.shape[0]
    first = jnp.concatenate([low_ref[...], kv_ref[: 2 * step, :]], axis=0)
    last = jnp.concatenate([kv_ref[count - 2 * step :, :], high_ref[...]], axis=0)
    pairs = count // step
    for edge, pair, window in ((0, 0, first), (1, pairs - 1, last)):
        rows = slice(pair * step, (pair + 1) * step)
        grads = attend_back(
            steps_ref, pair, q_ref[rows, :], g_ref[rows, :], window[:, :COLS], window[:, COLS:]
        )
        rim = slice(0, RIM) if edge == 0 else slice(WINDOW - RIM, WINDOW)
        own = slice(RIM, WINDOW) if edge == 0 else slice(0, WINDOW - RIM)
        for at, grad in enumerate(grads):
            columns = slice(at * COLS, (at + 1) * COLS)
            part_ref[edge, :, columns] = grad[own]
        outer.append(jnp.concatenate([grad[rim].astype(BF16) for grad in grads], axis=1))
    put_rims(rims, *outer)


def interior_back_kernel(steps_ref, q_ref, kv_ref, g_ref, part_ref, out_ref):
    step = PAIR * TILE
    count = q_ref.shape[0]
    pairs = count // step
    reach = 2 * step
    out_ref[:reach, :] = part_ref[0]
    out_ref[reach : count - reach, :] = jnp.zeros((count - 2 * reach, 2 * COLS), F32)
    out_ref[count - reach :, :] = part_ref[1]
    for pair in range(1, pairs - 1):
        window = slice((pair - 1) * step, (pair + 2) * step)
        rows = slice(pair * step, (pair + 1) * step)
        key_grad, value_grad = attend_back(
            steps_ref,
            pair,
            q_ref[rows, :],
            g_ref[rows, :],
            kv_ref[window, :COLS],
            kv_ref[window, COLS:],
        )
        out_ref[window, :COLS] += key_grad
        out_ref[window, COLS:] += value_grad


def slope(spread):
    return spread * lax.rsqrt(spread * spread + SOFT_WIDTH)


def mix_kernel(att_ref, factor_ref, truth_any, w_any, *refs):
    sources, refs = refs[:-8], refs[-8:]
    pred_ref, grad_ref, a, truth_ref, truth, source, w, sems = refs
    members_num, part, _ = source.shape
    halves = w.shape[0]
    ens = lax.axis_index("ens")
    copies = fetch([(w_any.at[half], w.at[half]) for half in range(halves)], sems)
    pairs = [(truth_any, truth_ref)]
    if len(sources) == 1:
        pairs.append((sources[0], source))
    else:
        pairs += [(rows.at[0], source.at[ens ^ step]) for step, rows in enumerate(sources)]
    others = fetch(pairs, sems, halves)
    for g in range(GROUP):
        for m in range(members_num):
            a[m * part : (m + 1) * part, g * COLS : (g + 1) * COLS] = att_ref[g * members_num + m]
    wait(others)
    lane_part = lax.broadcasted_iota(jnp.int32, (1, a.shape[0]), 1) // part
    own_truth, own_factor = truth_ref[...], factor_ref[...]
    for turn in range(1, members_num):
        at = lane_part - turn
        here = jnp.where(at < 0, at + members_num, at) == ens
        own_truth = jnp.where(here, pltpu.roll(truth_ref[...], turn * part, 1), own_truth)
        own_factor = jnp.where(here, pltpu.roll(factor_ref[...], turn * part, 1), own_factor)
    truth[...] = jnp.zeros_like(truth)
    truth[:FIELD_NUM, :] = own_truth
    hidden = source[...].reshape(a.shape).astype(F32)
    count = LATENT_DIM // halves
    for half in range(halves):
        copies[half].wait()
        mix = w[half].reshape(count, LATENT_DIM + FIELD_PAD)[:, :LATENT_DIM]
        hidden += jnp.dot(
            a[:, half * count : (half + 1) * count], mix, preferred_element_type=F32
        )
    both = w[...].reshape(LATENT_DIM, LATENT_DIM + FIELD_PAD)
    mix, readout = both[:, :LATENT_DIM], both[:, LATENT_DIM:]
    inverse = lax.rsqrt(jnp.mean(hidden * hidden, axis=-1, keepdims=True) + NORM_EPS)
    decoded = (hidden * inverse).astype(BF16)
    prediction = lax.dot_general(
        readout, decoded, (((0,), (1,)), ((), ())), preferred_element_type=F32
    )
    pred_ref[...] = prediction[:FIELD_NUM]
    spread = jnp.zeros_like(prediction)
    for other in range(1, members_num):
        spread = spread + slope(prediction - pltpu.roll(prediction, other * part, 1))
    derivative = own_factor / FIELD_NUM * (
        slope(prediction - truth[...]) - spread / (members_num - 1)
    )
    grad_decoded = lax.dot_general(
        derivative.astype(BF16), readout, (((0,), (1,)), ((), ())), preferred_element_type=F32
    )
    grad_hidden = inverse * grad_decoded - hidden * inverse**3 * jnp.mean(
        grad_decoded * hidden, axis=-1, keepdims=True
    )
    grads = lax.dot_general(
        grad_hidden.astype(BF16), mix, OVER_COLUMNS, preferred_element_type=F32
    ).astype(BF16)
    for g in range(GROUP):
        for m in range(members_num):
            grad_ref[g * members_num + m] = grads[
                m * part : (m + 1) * part, g * COLS : (g + 1) * COLS
            ]


def product_kernel(normed_ref, from_low_ref, from_high_ref, grads_ref, out_ref):
    count = normed_ref.shape[0]
    half, last = lax.axis_index("half"), lax.axis_size("half") - 1
    from_low = jnp.where(half > 0, from_low_ref[...].astype(F32), 0.0)
    from_high = jnp.where(half < last, from_high_ref[...].astype(F32), 0.0)
    grads = grads_ref[...]
    grads = jnp.concatenate(
        [
            grads[:RIM] + from_low,
            grads[RIM : count - RIM],
            grads[count - RIM :] + from_high,
        ],
        axis=0,
    )
    high = grads.astype(BF16)
    low = (grads - high.astype(F32)).astype(BF16)
    both = lax.dot_general(
        normed_ref[...], jnp.concatenate([high, low], axis=1), OVER_ROWS, preferred_element_type=F32
    )
    out_ref[...] = (both[:, : 2 * COLS] + both[:, 2 * COLS :]).astype(BF16)


def gather_kernel(parts_ref, out_ref):
    halves, _, members_num = parts_ref.shape[:3]
    for g in range(GROUP):
        total = None
        for half in range(halves):
            for m in range(members_num):
                part = parts_ref[half, g, m].astype(F32)
                total = part if total is None else total + part
        out_ref[:, g * COLS : (g + 1) * COLS] = total[:, :COLS]
        out_ref[:, LATENT_DIM + g * COLS : LATENT_DIM + (g + 1) * COLS] = total[:, COLS:]


def exchange(chunks, axes):
    return lax.all_to_all(chunks, axes, 0, 0)


def swap(value, axis, step):
    return lax.ppermute(value, axis, [(i, i ^ step) for i in range(lax.axis_size(axis))])


def in_order(mine, axis, at):
    if lax.axis_size(axis) != 2:
        return lax.all_gather(mine, axis, axis=at)
    other = swap(mine, axis, 1)
    first = lax.axis_index(axis) == 0
    return jnp.stack([jnp.where(first, mine, other), jnp.where(first, other, mine)], axis=at)


def body(members, w_attn, w_mix, readout_matrix, observed_truth, cell_surface_factor, neighbours):
    halves, members_num = lax.axis_size("half"), lax.axis_size("ens")
    nodes = ("half", "quad", "core")
    everyone = nodes + ("ens",)
    shard = w_attn.shape[0]
    node_rows = members.shape[1]
    rows = GROUP * node_rows
    part = node_rows // members_num
    up = [(i, i + 1) for i in range(halves - 1)]
    down = [(target, source) for source, target in up]
    ens = lax.axis_index("ens")
    width = LATENT_DIM + FIELD_PAD
    paired = members_num == 2
    copies = 1 if paired else members_num
    source_parts = 2 if paired else 1

    columns, packed = call(
        weights_kernel,
        "prepare_weights",
        [((halves, GROUP, copies, shard, 3 * COLS), BF16), ((shard, width), BF16)],
        "hhh",
        [
            pltpu.VMEM(w_attn.shape, BF16),
            pltpu.VMEM((GROUP, shard, 3 * COLS), BF16),
            pltpu.VMEM(readout_matrix.shape, BF16),
            pltpu.VMEM((shard, width), BF16),
            pltpu.SemaphoreType.DMA((4 + halves * copies,)),
        ],
        moved=2**20,
        results="hh",
    )(w_attn, w_mix, readout_matrix)
    normed, *sources = call(
        norm_kernel,
        "norm",
        [((node_rows + NOTE_ROWS, LATENT_DIM), BF16)]
        + [((1 if paired else members_num, part, LATENT_DIM), BF16)] * source_parts,
        "hh",
        [
            pltpu.SMEM(neighbours.shape, jnp.int32),
            pltpu.VMEM((node_rows, LATENT_DIM), BF16),
            pltpu.VMEM((node_rows + NOTE_ROWS, LATENT_DIM), BF16),
            pltpu.SemaphoreType.DMA((3 + max(2, members_num),)),
        ],
        flops=2**20,
        moved=2**20,
        results="h" + "h" * source_parts,
    )(neighbours, members.reshape(node_rows, LATENT_DIM))

    packed, normed = lax.optimization_barrier((in_order(packed, "half", 0), normed))
    near = [normed, swap(normed, "quad", 1), None, swap(normed, "quad", 3)]
    if paired:
        columns = exchange(columns.reshape(-1, shard, 3 * COLS), nodes)
        columns, late = lax.optimization_barrier((columns, normed))
        columns = [columns, swap(columns, "ens", 1)]
    else:
        columns = [exchange(columns.reshape(-1, shard, 3 * COLS), everyone)]
        columns = [columns[0].reshape(LATENT_DIM, 3 * COLS)]
        late = normed
    near[2] = swap(late, "quad", 2)
    near = list(lax.optimization_barrier(tuple(near)))
    far = [swap(piece, "core", 1) for piece in near]
    normed, steps = call(
        collect_kernel,
        "collect",
        [((rows, LATENT_DIM), BF16), ((GROUP, NOTE_ROWS, 128), F32)],
        "a" * (2 * QUAD),
        [pltpu.VMEM((GROUP, NOTE_ROWS, 128), BF16), pltpu.SemaphoreType.DMA((2 * GROUP,))],
        moved=4 * 2**20,
        results="hv",
    )(*near, *far)

    square = paired and halves == 2 and shard % 16 == 0
    if square:
        (wide,) = call(
            attach_kernel,
            "attach_sources",
            [((2, shard, width + LATENT_DIM), BF16)],
            "vv",
            moved=2**19,
        )(packed, sources[1])
        packed, arrived = call(
            merge_members_kernel,
            "merge_members",
            [((2, 2, shard, width), BF16), ((1, part, LATENT_DIM), BF16)],
            "vv",
            moved=2**19,
        )(wide, swap(wide, "ens", 1))
        packed = packed.reshape(2, 2 * shard, width)
        sources = [sources[0], arrived]
    else:
        packed = in_order(packed, "ens", 1).reshape(halves, members_num * shard, width)
    packed, near[2] = lax.optimization_barrier((packed, near[2]))
    pieces = [packed] + [swap(packed, "quad", step) for step in range(1, QUAD)]

    rim = ((RIM, 2 * COLS), BF16)
    rims = [rim] if halves == 2 else [rim, rim]
    w_shape = (GROUP * halves, 2, shard, 3 * COLS) if paired else (LATENT_DIM, 3 * COLS)
    weights, *inner = call(
        rims_kernel,
        "project_rims",
        [(w_shape, BF16)] + rims,
        "h" + "a" * len(columns),
        [pltpu.VMEM((len(rims), RIM, LATENT_DIM), BF16), pltpu.SemaphoreType.DMA((4,))],
        flops=RIM * LATENT_DIM * 4 * COLS,
        moved=2**20,
    )(normed, *columns)
    def across(inner):
        if halves == 2:
            got = swap(inner[0], "half", 1)
            return got, got
        return lax.ppermute(inner[1], "half", up), lax.ppermute(inner[0], "half", down)

    if not paired:
        sources = [exchange(sources[0], "ens")]
    elif not square:
        sources = [sources[0], swap(sources[1], "ens", 1)]
    low, high = across(inner)
    queries, own = call(
        project_kernel,
        "project",
        [((rows, COLS), BF16), ((rows, 2 * COLS), BF16)],
        "hv",
        [pltpu.VMEM((rows, LATENT_DIM), BF16), pltpu.SemaphoreType.DMA((CHUNKS,))],
        flops=rows * LATENT_DIM * 6 * COLS,
        moved=4 * 2**20,
    )(normed, weights)

    (outcome,) = call(
        interior_kernel,
        "attention_interior",
        [((rows, COLS), BF16)],
        "vvv",
        flops=rows * COLS * 2048,
        moved=2**21,
        exps=rows * 512,
    )(steps, queries, own)
    (outcome,) = call(
        edge_kernel,
        "attention_edges",
        [((rows, COLS), BF16)],
        "vvvvvv",
        flops=rows * COLS * 512,
        moved=2**20,
        exps=rows * 128,
    )(steps, queries, own, low, high, outcome)
    *pieces, own = lax.optimization_barrier((*pieces, own))
    pieces = pieces + [swap(piece, "core", 1) for piece in pieces]
    attended = exchange(outcome.reshape(GROUP * members_num, part, COLS), ("quad", "core", "ens"))
    block = (halves, QUAD, CORES, members_num * shard, width)
    (weights,) = call(
        assemble_kernel,
        "assemble",
        [(block, BF16)],
        "a" * len(pieces),
        [pltpu.SemaphoreType.DMA((GROUP,))],
        moved=4 * 2**20,
        results="h",
    )(*pieces)

    prediction, grads = call(
        mix_kernel,
        "mix_loss_backward",
        [((FIELD_NUM, node_rows), F32), ((GROUP * members_num, part, COLS), BF16)],
        "vvhh" + "a" * len(sources),
        [
            pltpu.VMEM((node_rows, LATENT_DIM), BF16),
            pltpu.VMEM(observed_truth.shape, F32),
            pltpu.VMEM((FIELD_PAD, node_rows), F32),
            pltpu.VMEM((members_num, part, LATENT_DIM), BF16),
            pltpu.VMEM(block, BF16),
            pltpu.SemaphoreType.DMA((halves + 1 + len(sources),)),
        ],
        flops=node_rows * LATENT_DIM * 4 * width,
        moved=2**22,
        room=14,
    )(attended, cell_surface_factor[None], observed_truth, weights, *sources)
    grads = exchange(grads, ("quad", "core", "ens")).reshape(rows, COLS)

    edges, *inner = call(
        edge_back_kernel,
        "attention_edges_back",
        [((2, WINDOW - RIM, 2 * COLS), F32)] + rims,
        "vvvvvv",
        flops=rows * COLS * 1280,
        moved=2**20,
        exps=rows * 128,
    )(steps, queries, own, low, high, grads)
    from_low, from_high = across(inner)
    (kv_grads,) = call(
        interior_back_kernel,
        "attention_interior_back",
        [((rows, 2 * COLS), F32)],
        "vvvvv",
        flops=rows * COLS * 4096,
        moved=2**22,
        exps=rows * 512,
        room=10,
    )(steps, queries, own, grads, edges)
    (term,) = call(
        product_kernel,
        "product",
        [((LATENT_DIM, 2 * COLS), BF16)],
        "vvvv",
        flops=rows * LATENT_DIM * 8 * COLS,
        moved=2**22,
        room=16,
    )(normed, from_low, from_high, kv_grads)
    term, prediction = lax.optimization_barrier((term, prediction))
    term = exchange(term.reshape(-1, shard, 2 * COLS), everyone)
    (grad_kv,) = call(
        gather_kernel, "gather_sums", [((shard, 2 * LATENT_DIM), F32)], "v", flops=2**17, moved=2**20
    )(term.reshape(halves, GROUP, members_num, shard, 2 * COLS))

    if members_num == 2:
        got = jnp.roll(swap(prediction, "ens", 1), part, axis=1)
        lane = lax.broadcasted_iota(jnp.int32, prediction.shape, 1)
        prediction = jnp.where(lane // part == ens, prediction, got)
    else:
        prediction = prediction.reshape(FIELD_NUM, members_num, part).transpose(1, 0, 2)
        prediction = exchange(prediction, "ens").transpose(1, 0, 2)
    return (prediction.reshape(1, FIELD_NUM, node_rows), grad_kv)


def solution(mesh):
    space, ens = mesh.shape["space"], mesh.shape["ens"]
    split = Mesh(
        mesh.devices.reshape(space // GROUP, QUAD, CORES, ens), ("half", "quad", "core", "ens")
    )
    nodes = ("half", "quad", "core")
    shards = nodes + ("ens",)
    in_specs = (
        P("ens", nodes, None),
        P(shards, None),
        P(shards, None),
        P(shards, None),
        P(None, nodes),
        P(nodes),
        P(nodes, None),
    )
    out_specs = (P("ens", None, nodes), P(shards, None))
    return jax.shard_map(body, mesh=split, in_specs=in_specs, out_specs=out_specs, check_vma=False)
```

```python
import functools

import jax
import jax.numpy as jnp
from jax import lax
from jax.experimental import pallas as pl
from jax.experimental.pallas import tpu as pltpu
from jax.sharding import Mesh
from jax.sharding import PartitionSpec as P

LATENT_DIM = 1024
HEADS = 16
HEAD = 64
FIELD_NUM = 100
TILE = 64
RADIUS = 2
K_NB = 4
QUAD = 4
CORES = 2
GROUP = QUAD * CORES
COLS = LATENT_DIM // GROUP
RIM = RADIUS * TILE
FIELD_PAD = 128
PAIR = 2
WINDOW = (PAIR + 2 * RADIUS) * TILE
NOWHERE = 100
NOTE_ROWS = 16
CHUNKS = 4

NORM_EPS = 1e-06
SOFT_WIDTH = 0.0625
MASKED = -1e30

F32 = jnp.float32
BF16 = jnp.bfloat16

VMEM = pl.BlockSpec(memory_space=pltpu.VMEM)
SMEM = pl.BlockSpec(memory_space=pltpu.SMEM)
HBM = pl.BlockSpec(memory_space=pltpu.HBM)
ANYWHERE = pl.BlockSpec(memory_space=pl.ANY)
OVER_ROWS = (((0,), (0,)), ((), ()))
OVER_COLUMNS = (((1,), (1,)), ((), ()))


def call(kernel, name, outs, ins, scratch=(), flops=0, moved=0, exps=0, room=8, results=None):
    results = results or "v" * len(outs)
    spaces = {"s": SMEM, "v": VMEM, "h": HBM, "a": ANYWHERE}
    made = pl.pallas_call(
        kernel,
        out_shape=[
            pltpu.HBM(shape, kind) if space == "h" else jax.ShapeDtypeStruct(shape, kind)
            for (shape, kind), space in zip(outs, results)
        ],
        in_specs=[spaces[space] for space in ins],
        out_specs=[spaces[space] for space in results],
        scratch_shapes=list(scratch),
        compiler_params=pltpu.CompilerParams(vmem_limit_bytes=room * 2**20),
        cost_estimate=pl.CostEstimate(flops=flops, bytes_accessed=moved, transcendentals=exps),
        name=name,
    )

    def run(*args):
        return made(
            *[
                pltpu.with_memory_space_constraint(arg, pltpu.HBM) if space == "h" else arg
                for arg, space in zip(args, ins)
            ]
        )

    return run


def fetch(pairs, sems, first=0):
    copies = [
        pltpu.make_async_copy(source, target, sems.at[first + at])
        for at, (source, target) in enumerate(pairs)
    ]
    for copy in copies:
        copy.start()
    return copies


def wait(copies):
    for copy in copies:
        copy.wait()


def weights_kernel(w_any, mix_any, readout_any, columns_any, packed_any, *refs):
    w, columns, readout, packed, sems = refs
    copies = fetch(
        [(w_any, w), (readout_any, readout), (mix_any, packed.at[:, :LATENT_DIM])], sems
    )
    copies[0].wait()
    for g in range(GROUP):
        for part in range(3):
            at = (part * GROUP + g) * COLS
            columns[g, :, part * COLS : (part + 1) * COLS] = w[:, at : at + COLS]
    halves, _, members_num = columns_any.shape[:3]
    out = fetch(
        [
            (columns, columns_any.at[half, :, m])
            for half in range(halves)
            for m in range(members_num)
        ],
        sems,
        3,
    )
    wait(copies[1:])
    packed[:, LATENT_DIM:] = jnp.zeros((packed.shape[0], FIELD_PAD), BF16)
    packed[:, LATENT_DIM : LATENT_DIM + FIELD_NUM] = readout[...]
    wait(out + fetch([(packed, packed_any)], sems, 3 + len(out)))


def norm_kernel(near_any, source_any, normed_any, *refs):
    parts, (near, source, normed, sems) = refs[:-4], refs[-4:]
    ens = lax.axis_index("ens")
    copies = fetch([(source_any, source), (near_any, near)], sems)
    rows = source.shape[0]
    copies[0].wait()
    moves = []
    for step, part_any in enumerate(parts):
        count, part, _ = part_any.shape
        for m in range(count):
            place = (ens ^ step) if len(parts) == 2 else m
            place = pl.multiple_of(place * part, part)
            moves.append((source.at[pl.ds(place, part)], part_any.at[m]))
    out = fetch(moves, sems, 2)
    states = source[...].astype(F32)
    inverse = lax.rsqrt(jnp.mean(states * states, axis=-1, keepdims=True) + NORM_EPS)
    normed[:rows, :] = (states * inverse).astype(BF16)
    copies[1].wait()
    row = lax.broadcasted_iota(jnp.int32, (NOTE_ROWS, 128), 0)
    lane = lax.broadcasted_iota(jnp.int32, (NOTE_ROWS, 128), 1)
    note = jnp.zeros((NOTE_ROWS, 128), F32)
    tiles = near.shape[0]
    first_tile = lax.axis_index(("half", "quad", "core")) * tiles
    for tile in range(tiles):
        for slot in range(K_NB):
            at = near[tile, slot]
            step = jnp.where(at >= 0, at - first_tile - tile, NOWHERE).astype(F32)
            note = jnp.where((row == tile) & (lane == slot), step, note)
    normed[rows:, :] = jnp.zeros((NOTE_ROWS, LATENT_DIM), BF16)
    normed[rows:, :128] = note.astype(BF16)
    wait(out + fetch([(normed, normed_any)], sems, 2 + len(out)))


def attach_kernel(packed_ref, sent_any, out_ref, sems):
    width, shard = packed_ref.shape[2], packed_ref.shape[1]
    pairs = [
        (sent_any.at[0, pl.ds(at * shard, shard)], out_ref.at[at, :, width:]) for at in range(2)
    ]
    copies = fetch(pairs, sems)
    out_ref[:, :, :width] = packed_ref[...]
    wait(copies)


def merge_members_kernel(mine_ref, other_ref, packed_ref, source_ref):
    ens = lax.axis_index("ens")
    width = packed_ref.shape[3]
    for half in range(2):
        packed_ref[half, ens] = mine_ref[half, :, :width]
        packed_ref[half, ens ^ 1] = other_ref[half, :, :width]
    source_ref[...] = other_ref[:, :, width:].reshape(source_ref.shape)


def owners():
    core, quad = lax.axis_index("core"), lax.axis_index("quad")
    return [(quad ^ step) * CORES + (core ^ flip) for flip in range(CORES) for step in range(QUAD)]


def collect_kernel(*refs):
    blocks, (normed_any, steps_ref, notes, sems) = refs[:GROUP], refs[GROUP:]
    block = blocks[0].shape[0] - NOTE_ROWS
    pairs = []
    for rows_ref, owner in zip(blocks, owners()):
        place = pl.ds(pl.multiple_of(owner * block, block), block)
        pairs.append((rows_ref.at[:block], normed_any.at[place]))
        pairs.append((rows_ref.at[block:, :128], notes.at[owner]))
    wait(fetch(pairs, sems))
    steps_ref[...] = notes[...].astype(F32)


def put_rims(rims, first, last):
    if len(rims) == 1:
        rims[0][...] = jnp.where(lax.axis_index("half") == 0, last, first)
    else:
        rims[0][...], rims[1][...] = first, last


def rims_kernel(normed_any, *refs):
    rows, sems = refs[-2:]
    if len(refs[0].shape) == 2:
        columns, w, rims = refs[:1], refs[1], refs[2:-2]
        pairs = [(columns[0], w)]
    else:
        columns, w, rims = refs[:2], refs[2], refs[3:-2]
        ens = lax.axis_index("ens")
        pairs = [(part, w.at[:, ens ^ step]) for step, part in enumerate(columns)]
    last = normed_any.shape[0] - RIM
    if len(rims) == 1:
        place = pl.multiple_of(jnp.where(lax.axis_index("half") == 0, last, 0), RIM)
        pairs.append((normed_any.at[pl.ds(place, RIM)], rows.at[0]))
    else:
        pairs += [(normed_any.at[:RIM], rows.at[0]), (normed_any.at[last:], rows.at[1])]
    wait(fetch(pairs, sems))
    weights = w[...].reshape(LATENT_DIM, 3 * COLS)[:, COLS:]
    for at, rim_ref in enumerate(rims):
        rim_ref[...] = jnp.dot(rows[at], weights, preferred_element_type=F32).astype(BF16)


def project_kernel(normed_any, w_ref, q_ref, kv_ref, normed, sems):
    chunk = normed.shape[0] // CHUNKS
    rows = [slice(at * chunk, (at + 1) * chunk) for at in range(CHUNKS)]
    copies = fetch([(normed_any.at[part], normed.at[part]) for part in rows], sems)
    weights = w_ref[...].reshape(LATENT_DIM, 3 * COLS)
    for part, copy in zip(rows, copies):
        copy.wait()
        projected = jnp.dot(normed[part, :], weights, preferred_element_type=F32).astype(BF16)
        q_ref[part, :] = projected[:, :COLS] * jnp.asarray(HEAD**-0.5, BF16)
        kv_ref[part, :] = projected[:, COLS:]


def assemble_kernel(*refs):
    pieces, (w_any, sems) = refs[:GROUP], refs[GROUP:]
    core, quad = lax.axis_index("core"), lax.axis_index("quad")
    pairs = [
        (piece, w_any.at[:, quad ^ (at % QUAD), core ^ (at // QUAD)])
        for at, piece in enumerate(pieces)
    ]
    wait(fetch(pairs, sems))


def by_head(rows):
    lane = lax.broadcasted_iota(jnp.int32, rows.shape, 1)
    zero = jnp.zeros_like(rows)
    return jnp.concatenate(
        [jnp.where(lane < HEAD, rows, zero), jnp.where(lane < HEAD, zero, rows)], axis=0
    )


def usable_keys(steps_ref, pair):
    lane = (lax.broadcasted_iota(jnp.int32, (1, WINDOW), 1) // TILE - RADIUS).astype(F32)
    masks = []
    for query_tile in range(PAIR):
        found = jnp.zeros((1, WINDOW), F32)
        for slot in range(K_NB):
            step = steps_ref[pair, query_tile : query_tile + 1, slot : slot + 1]
            found = jnp.where(lane - query_tile == step, 1.0, found)
        masks.append(found)
    row = lax.broadcasted_iota(jnp.int32, (2 * PAIR * TILE, 1), 0) // TILE % PAIR
    return jnp.where(row == 0, masks[0], masks[1]) > 0


def raised_scores(queries, keys, usable):
    scores = lax.dot_general(queries, keys, OVER_COLUMNS, preferred_element_type=F32)
    scores = jnp.where(usable, scores, MASKED)
    raised = jnp.exp(scores - jnp.max(scores, axis=-1, keepdims=True))
    return raised, 1.0 / jnp.sum(raised, axis=-1, keepdims=True)


def attend(steps_ref, pair, queries, keys, values):
    raised, share = raised_scores(by_head(queries), keys, usable_keys(steps_ref, pair))
    both = jnp.dot(raised.astype(BF16), values, preferred_element_type=F32) * share
    lane = lax.broadcasted_iota(jnp.int32, queries.shape, 1)
    half = PAIR * TILE
    return jnp.where(lane < HEAD, both[:half], both[half:]).astype(BF16)


def interior_kernel(steps_ref, q_ref, kv_ref, out_ref):
    step = PAIR * TILE
    pairs = q_ref.shape[0] // step
    for pair in range(1, pairs - 1):
        window = slice((pair - 1) * step, (pair + 2) * step)
        rows = slice(pair * step, (pair + 1) * step)
        out_ref[rows, :] = attend(
            steps_ref, pair, q_ref[rows, :], kv_ref[window, :COLS], kv_ref[window, COLS:]
        )


def edge_kernel(steps_ref, q_ref, kv_ref, low_ref, high_ref, done_ref, out_ref):
    step = PAIR * TILE
    count = q_ref.shape[0]
    pairs = count // step
    out_ref[step : count - step, :] = done_ref[step : count - step, :]
    first = jnp.concatenate([low_ref[...], kv_ref[: 2 * step, :]], axis=0)
    last = jnp.concatenate([kv_ref[count - 2 * step :, :], high_ref[...]], axis=0)
    for pair, window in ((0, first), (pairs - 1, last)):
        rows = slice(pair * step, (pair + 1) * step)
        out_ref[rows, :] = attend(
            steps_ref, pair, q_ref[rows, :], window[:, :COLS], window[:, COLS:]
        )


def attend_back(steps_ref, pair, queries, grads, keys, values):
    queries, grads = by_head(queries), by_head(grads)
    raised, share = raised_scores(queries, keys, usable_keys(steps_ref, pair))
    probs = raised * share
    grad_probs = lax.dot_general(grads, values, OVER_COLUMNS, preferred_element_type=F32)
    row_delta = jnp.sum(probs * grad_probs, axis=-1, keepdims=True)
    grad_scores = (probs * (grad_probs - row_delta)).astype(BF16)
    key_grad = lax.dot_general(grad_scores, queries, OVER_ROWS, preferred_element_type=F32)
    value_grad = lax.dot_general(probs.astype(BF16), grads, OVER_ROWS, preferred_element_type=F32)
    return key_grad, value_grad


def edge_back_kernel(
    steps_ref, q_ref, kv_ref, low_ref, high_ref, g_ref, part_ref, *rims
):
    outer = []
    step = PAIR * TILE
    count = q_ref.shape[0]
    first = jnp.concatenate([low_ref[...], kv_ref[: 2 * step, :]], axis=0)
    last = jnp.concatenate([kv_ref[count - 2 * step :, :], high_ref[...]], axis=0)
    pairs = count // step
    for edge, pair, window in ((0, 0, first), (1, pairs - 1, last)):
        rows = slice(pair * step, (pair + 1) * step)
        grads = attend_back(
            steps_ref, pair, q_ref[rows, :], g_ref[rows, :], window[:, :COLS], window[:, COLS:]
        )
        rim = slice(0, RIM) if edge == 0 else slice(WINDOW - RIM, WINDOW)
        own = slice(RIM, WINDOW) if edge == 0 else slice(0, WINDOW - RIM)
        for at, grad in enumerate(grads):
            columns = slice(at * COLS, (at + 1) * COLS)
            part_ref[edge, :, columns] = grad[own]
        outer.append(jnp.concatenate([grad[rim].astype(BF16) for grad in grads], axis=1))
    put_rims(rims, *outer)


def interior_back_kernel(steps_ref, q_ref, kv_ref, g_ref, part_ref, out_ref):
    step = PAIR * TILE
    count = q_ref.shape[0]
    pairs = count // step
    reach = 2 * step
    out_ref[:reach, :] = part_ref[0]
    out_ref[reach : count - reach, :] = jnp.zeros((count - 2 * reach, 2 * COLS), F32)
    out_ref[count - reach :, :] = part_ref[1]
    for pair in range(1, pairs - 1):
        window = slice((pair - 1) * step, (pair + 2) * step)
        rows = slice(pair * step, (pair + 1) * step)
        key_grad, value_grad = attend_back(
            steps_ref,
            pair,
            q_ref[rows, :],
            g_ref[rows, :],
            kv_ref[window, :COLS],
            kv_ref[window, COLS:],
        )
        out_ref[window, :COLS] += key_grad
        out_ref[window, COLS:] += value_grad


def slope(spread):
    return spread * lax.rsqrt(spread * spread + SOFT_WIDTH)


def mix_kernel(att_ref, factor_ref, truth_any, w_any, *refs):
    sources, refs = refs[:-8], refs[-8:]
    pred_ref, grad_ref, a, truth_ref, truth, source, w, sems = refs
    members_num, part, _ = source.shape
    halves = w.shape[0]
    ens = lax.axis_index("ens")
    copies = fetch([(w_any.at[half], w.at[half]) for half in range(halves)], sems)
    pairs = [(truth_any, truth_ref)]
    if len(sources) == 1:
        pairs.append((sources[0], source))
    else:
        pairs += [(rows.at[0], source.at[ens ^ step]) for step, rows in enumerate(sources)]
    others = fetch(pairs, sems, halves)
    for g in range(GROUP):
        for m in range(members_num):
            a[m * part : (m + 1) * part, g * COLS : (g + 1) * COLS] = att_ref[g * members_num + m]
    wait(others)
    lane_part = lax.broadcasted_iota(jnp.int32, (1, a.shape[0]), 1) // part
    own_truth, own_factor = truth_ref[...], factor_ref[...]
    for turn in range(1, members_num):
        at = lane_part - turn
        here = jnp.where(at < 0, at + members_num, at) == ens
        own_truth = jnp.where(here, pltpu.roll(truth_ref[...], turn * part, 1), own_truth)
        own_factor = jnp.where(here, pltpu.roll(factor_ref[...], turn * part, 1), own_factor)
    truth[...] = jnp.zeros_like(truth)
    truth[:FIELD_NUM, :] = own_truth
    hidden = source[...].reshape(a.shape).astype(F32)
    count = LATENT_DIM // halves
    for half in range(halves):
        copies[half].wait()
        mix = w[half].reshape(count, LATENT_DIM + FIELD_PAD)[:, :LATENT_DIM]
        hidden += jnp.dot(
            a[:, half * count : (half + 1) * count], mix, preferred_element_type=F32
        )
    both = w[...].reshape(LATENT_DIM, LATENT_DIM + FIELD_PAD)
    mix, readout = both[:, :LATENT_DIM], both[:, LATENT_DIM:]
    inverse = lax.rsqrt(jnp.mean(hidden * hidden, axis=-1, keepdims=True) + NORM_EPS)
    decoded = (hidden * inverse).astype(BF16)
    prediction = lax.dot_general(
        readout, decoded, (((0,), (1,)), ((), ())), preferred_element_type=F32
    )
    pred_ref[...] = prediction[:FIELD_NUM]
    spread = jnp.zeros_like(prediction)
    for other in range(1, members_num):
        spread = spread + slope(prediction - pltpu.roll(prediction, other * part, 1))
    derivative = own_factor / FIELD_NUM * (
        slope(prediction - truth[...]) - spread / (members_num - 1)
    )
    grad_decoded = lax.dot_general(
        derivative.astype(BF16), readout, (((0,), (1,)), ((), ())), preferred_element_type=F32
    )
    grad_hidden = inverse * grad_decoded - hidden * inverse**3 * jnp.mean(
        grad_decoded * hidden, axis=-1, keepdims=True
    )
    grads = lax.dot_general(
        grad_hidden.astype(BF16), mix, OVER_COLUMNS, preferred_element_type=F32
    ).astype(BF16)
    for g in range(GROUP):
        for m in range(members_num):
            grad_ref[g * members_num + m] = grads[
                m * part : (m + 1) * part, g * COLS : (g + 1) * COLS
            ]


def product_kernel(normed_ref, grads_ref, out_ref):
    grads = grads_ref[...]
    high = grads.astype(BF16)
    low = (grads - high.astype(F32)).astype(BF16)
    both = lax.dot_general(
        normed_ref[...], jnp.concatenate([high, low], axis=1), OVER_ROWS, preferred_element_type=F32
    )
    out_ref[...] = both[:, : 2 * COLS] + both[:, 2 * COLS :]


def rim_product_kernel(normed_any, total_ref, *refs):
    arrived, (out_ref, rows, sems) = refs[:-3], refs[-3:]
    last_row = normed_any.shape[0] - RIM
    half, last = lax.axis_index("half"), lax.axis_size("half") - 1
    if len(arrived) == 1:
        places = [pl.multiple_of(jnp.where(half == 0, last_row, 0), RIM)]
    else:
        places = [0, last_row]
    wait(
        fetch(
            [(normed_any.at[pl.ds(place, RIM)], rows.at[at]) for at, place in enumerate(places)], sems
        )
    )
    total = total_ref[...]
    for at, arrived_ref in enumerate(arrived):
        grads = arrived_ref[...]
        if len(arrived) == 2:
            grads = jnp.where((half > 0) if at == 0 else (half < last), grads.astype(F32), 0.0)
            grads = grads.astype(BF16)
        total += lax.dot_general(rows[at], grads, OVER_ROWS, preferred_element_type=F32)
    out_ref[...] = total.astype(BF16)


def gather_kernel(parts_ref, out_ref):
    halves, _, members_num = parts_ref.shape[:3]
    for g in range(GROUP):
        total = None
        for half in range(halves):
            for m in range(members_num):
                part = parts_ref[half, g, m].astype(F32)
                total = part if total is None else total + part
        out_ref[:, g * COLS : (g + 1) * COLS] = total[:, :COLS]
        out_ref[:, LATENT_DIM + g * COLS : LATENT_DIM + (g + 1) * COLS] = total[:, COLS:]


def exchange(chunks, axes):
    return lax.all_to_all(chunks, axes, 0, 0)


def swap(value, axis, step):
    return lax.ppermute(value, axis, [(i, i ^ step) for i in range(lax.axis_size(axis))])


def in_order(mine, axis, at):
    if lax.axis_size(axis) != 2:
        return lax.all_gather(mine, axis, axis=at)
    other = swap(mine, axis, 1)
    first = lax.axis_index(axis) == 0
    return jnp.stack([jnp.where(first, mine, other), jnp.where(first, other, mine)], axis=at)


def body(members, w_attn, w_mix, readout_matrix, observed_truth, cell_surface_factor, neighbours):
    halves, members_num = lax.axis_size("half"), lax.axis_size("ens")
    nodes = ("half", "quad", "core")
    everyone = nodes + ("ens",)
    shard = w_attn.shape[0]
    node_rows = members.shape[1]
    rows = GROUP * node_rows
    part = node_rows // members_num
    up = [(i, i + 1) for i in range(halves - 1)]
    down = [(target, source) for source, target in up]
    ens = lax.axis_index("ens")
    width = LATENT_DIM + FIELD_PAD
    paired = members_num == 2
    copies = 1 if paired else members_num
    source_parts = 2 if paired else 1

    columns, packed = call(
        weights_kernel,
        "prepare_weights",
        [((halves, GROUP, copies, shard, 3 * COLS), BF16), ((shard, width), BF16)],
        "hhh",
        [
            pltpu.VMEM(w_attn.shape, BF16),
            pltpu.VMEM((GROUP, shard, 3 * COLS), BF16),
            pltpu.VMEM(readout_matrix.shape, BF16),
            pltpu.VMEM((shard, width), BF16),
            pltpu.SemaphoreType.DMA((4 + halves * copies,)),
        ],
        moved=2**20,
        results="hh",
    )(w_attn, w_mix, readout_matrix)
    normed, *sources = call(
        norm_kernel,
        "norm",
        [((node_rows + NOTE_ROWS, LATENT_DIM), BF16)]
        + [((1 if paired else members_num, part, LATENT_DIM), BF16)] * source_parts,
        "hh",
        [
            pltpu.SMEM(neighbours.shape, jnp.int32),
            pltpu.VMEM((node_rows, LATENT_DIM), BF16),
            pltpu.VMEM((node_rows + NOTE_ROWS, LATENT_DIM), BF16),
            pltpu.SemaphoreType.DMA((3 + max(2, members_num),)),
        ],
        flops=2**20,
        moved=2**20,
        results="h" + "h" * source_parts,
    )(neighbours, members.reshape(node_rows, LATENT_DIM))

    packed, normed = lax.optimization_barrier((in_order(packed, "half", 0), normed))
    near = [normed, swap(normed, "quad", 1), None, swap(normed, "quad", 3)]
    if paired:
        columns = exchange(columns.reshape(-1, shard, 3 * COLS), nodes)
        columns, late = lax.optimization_barrier((columns, normed))
        columns = [columns, swap(columns, "ens", 1)]
    else:
        columns = [exchange(columns.reshape(-1, shard, 3 * COLS), everyone)]
        columns = [columns[0].reshape(LATENT_DIM, 3 * COLS)]
        late = normed
    near[2] = swap(late, "quad", 2)
    near = list(lax.optimization_barrier(tuple(near)))
    far = [swap(piece, "core", 1) for piece in near]
    normed, steps = call(
        collect_kernel,
        "collect",
        [((rows, LATENT_DIM), BF16), ((GROUP, NOTE_ROWS, 128), F32)],
        "a" * (2 * QUAD),
        [pltpu.VMEM((GROUP, NOTE_ROWS, 128), BF16), pltpu.SemaphoreType.DMA((2 * GROUP,))],
        moved=4 * 2**20,
        results="hv",
    )(*near, *far)

    square = paired and halves == 2 and shard % 16 == 0
    if square:
        (wide,) = call(
            attach_kernel,
            "attach_sources",
            [((2, shard, width + LATENT_DIM), BF16)],
            "vh",
            [pltpu.SemaphoreType.DMA((2,))],
            moved=2**19,
        )(packed, sources[1])
        packed, arrived = call(
            merge_members_kernel,
            "merge_members",
            [((2, 2, shard, width), BF16), ((1, part, LATENT_DIM), BF16)],
            "vv",
            moved=2**19,
        )(wide, swap(wide, "ens", 1))
        packed = packed.reshape(2, 2 * shard, width)
        sources = [sources[0], arrived]
    else:
        packed = in_order(packed, "ens", 1).reshape(halves, members_num * shard, width)
    packed, near[2] = lax.optimization_barrier((packed, near[2]))
    pieces = [packed] + [swap(packed, "quad", step) for step in range(1, QUAD)]

    rim = ((RIM, 2 * COLS), BF16)
    rims = [rim] if halves == 2 else [rim, rim]
    w_shape = (GROUP * halves, 2, shard, 3 * COLS) if paired else (LATENT_DIM, 3 * COLS)
    weights, *inner = call(
        rims_kernel,
        "project_rims",
        [(w_shape, BF16)] + rims,
        "h" + "a" * len(columns),
        [pltpu.VMEM((len(rims), RIM, LATENT_DIM), BF16), pltpu.SemaphoreType.DMA((4,))],
        flops=RIM * LATENT_DIM * 4 * COLS,
        moved=2**20,
    )(normed, *columns)
    def across(inner):
        if halves == 2:
            got = swap(inner[0], "half", 1)
            return got, got
        return lax.ppermute(inner[1], "half", up), lax.ppermute(inner[0], "half", down)

    if not paired:
        sources = [exchange(sources[0], "ens")]
    elif not square:
        sources = [sources[0], swap(sources[1], "ens", 1)]
    low, high = across(inner)
    queries, own = call(
        project_kernel,
        "project",
        [((rows, COLS), BF16), ((rows, 2 * COLS), BF16)],
        "hv",
        [pltpu.VMEM((rows, LATENT_DIM), BF16), pltpu.SemaphoreType.DMA((CHUNKS,))],
        flops=rows * LATENT_DIM * 6 * COLS,
        moved=4 * 2**20,
    )(normed, weights)

    (outcome,) = call(
        interior_kernel,
        "attention_interior",
        [((rows, COLS), BF16)],
        "vvv",
        flops=rows * COLS * 2048,
        moved=2**21,
        exps=rows * 512,
    )(steps, queries, own)
    (outcome,) = call(
        edge_kernel,
        "attention_edges",
        [((rows, COLS), BF16)],
        "vvvvvv",
        flops=rows * COLS * 512,
        moved=2**20,
        exps=rows * 128,
    )(steps, queries, own, low, high, outcome)
    *pieces, own = lax.optimization_barrier((*pieces, own))
    pieces = pieces + [swap(piece, "core", 1) for piece in pieces]
    attended = exchange(outcome.reshape(GROUP * members_num, part, COLS), ("quad", "core", "ens"))
    block = (halves, QUAD, CORES, members_num * shard, width)
    (weights,) = call(
        assemble_kernel,
        "assemble",
        [(block, BF16)],
        "a" * len(pieces),
        [pltpu.SemaphoreType.DMA((GROUP,))],
        moved=4 * 2**20,
        results="h",
    )(*pieces)

    prediction, grads = call(
        mix_kernel,
        "mix_loss_backward",
        [((FIELD_NUM, node_rows), F32), ((GROUP * members_num, part, COLS), BF16)],
        "vvhh" + "a" * len(sources),
        [
            pltpu.VMEM((node_rows, LATENT_DIM), BF16),
            pltpu.VMEM(observed_truth.shape, F32),
            pltpu.VMEM((FIELD_PAD, node_rows), F32),
            pltpu.VMEM((members_num, part, LATENT_DIM), BF16),
            pltpu.VMEM(block, BF16),
            pltpu.SemaphoreType.DMA((halves + 1 + len(sources),)),
        ],
        flops=node_rows * LATENT_DIM * 4 * width,
        moved=2**22,
        room=14,
    )(attended, cell_surface_factor[None], observed_truth, weights, *sources)
    grads = exchange(grads, ("quad", "core", "ens")).reshape(rows, COLS)

    edges, *inner = call(
        edge_back_kernel,
        "attention_edges_back",
        [((2, WINDOW - RIM, 2 * COLS), F32)] + rims,
        "vvvvvv",
        flops=rows * COLS * 1280,
        moved=2**20,
        exps=rows * 128,
    )(steps, queries, own, low, high, grads)
    from_low, from_high = across(inner)
    (kv_grads,) = call(
        interior_back_kernel,
        "attention_interior_back",
        [((rows, 2 * COLS), F32)],
        "vvvvv",
        flops=rows * COLS * 4096,
        moved=2**22,
        exps=rows * 512,
        room=10,
    )(steps, queries, own, grads, edges)
    (total,) = call(
        product_kernel,
        "product",
        [((LATENT_DIM, 2 * COLS), F32)],
        "vv",
        flops=rows * LATENT_DIM * 8 * COLS,
        moved=2**22,
        room=16,
    )(normed, kv_grads)
    arrived = [from_low] if halves == 2 else [from_low, from_high]
    (term,) = call(
        rim_product_kernel,
        "product_rims",
        [((LATENT_DIM, 2 * COLS), BF16)],
        "hv" + "v" * len(arrived),
        [pltpu.VMEM((len(arrived), RIM, LATENT_DIM), BF16), pltpu.SemaphoreType.DMA((2,))],
        flops=RIM * LATENT_DIM * 4 * COLS,
        moved=2**21,
    )(normed, total, *arrived)
    term, prediction = lax.optimization_barrier((term, prediction))
    term = exchange(term.reshape(-1, shard, 2 * COLS), everyone)
    (grad_kv,) = call(
        gather_kernel, "gather_sums", [((shard, 2 * LATENT_DIM), F32)], "v", flops=2**17, moved=2**20
    )(term.reshape(halves, GROUP, members_num, shard, 2 * COLS))

    if members_num == 2:
        got = jnp.roll(swap(prediction, "ens", 1), part, axis=1)
        lane = lax.broadcasted_iota(jnp.int32, prediction.shape, 1)
        prediction = jnp.where(lane // part == ens, prediction, got)
    else:
        prediction = prediction.reshape(FIELD_NUM, members_num, part).transpose(1, 0, 2)
        prediction = exchange(prediction, "ens").transpose(1, 0, 2)
    return (prediction.reshape(1, FIELD_NUM, node_rows), grad_kv)


def solution(mesh):
    space, ens = mesh.shape["space"], mesh.shape["ens"]
    split = Mesh(
        mesh.devices.reshape(space // GROUP, QUAD, CORES, ens), ("half", "quad", "core", "ens")
    )
    nodes = ("half", "quad", "core")
    shards = nodes + ("ens",)
    in_specs = (
        P("ens", nodes, None),
        P(shards, None),
        P(shards, None),
        P(shards, None),
        P(None, nodes),
        P(nodes),
        P(nodes, None),
    )
    out_specs = (P("ens", None, nodes), P(shards, None))
    return jax.shard_map(body, mesh=split, in_specs=in_specs, out_specs=out_specs, check_vma=False)
```

```python
import functools

import jax
import jax.numpy as jnp
from jax import lax
from jax.experimental import pallas as pl
from jax.experimental.pallas import tpu as pltpu
from jax.sharding import Mesh
from jax.sharding import PartitionSpec as P

LATENT_DIM = 1024
HEADS = 16
HEAD = 64
FIELD_NUM = 100
TILE = 64
RADIUS = 2
K_NB = 4
QUAD = 4
CORES = 2
GROUP = QUAD * CORES
COLS = LATENT_DIM // GROUP
RIM = RADIUS * TILE
FIELD_PAD = 128
PAIR = 2
WINDOW = (PAIR + 2 * RADIUS) * TILE
NOWHERE = 100
NOTE_ROWS = 16
CHUNKS = 4

NORM_EPS = 1e-06
SOFT_WIDTH = 0.0625
MASKED = -1e30

F32 = jnp.float32
BF16 = jnp.bfloat16

VMEM = pl.BlockSpec(memory_space=pltpu.VMEM)
SMEM = pl.BlockSpec(memory_space=pltpu.SMEM)
HBM = pl.BlockSpec(memory_space=pltpu.HBM)
ANYWHERE = pl.BlockSpec(memory_space=pl.ANY)
OVER_ROWS = (((0,), (0,)), ((), ()))
OVER_COLUMNS = (((1,), (1,)), ((), ()))


def call(kernel, name, outs, ins, scratch=(), flops=0, moved=0, exps=0, room=8, results=None):
    results = results or "v" * len(outs)
    spaces = {"s": SMEM, "v": VMEM, "h": HBM, "a": ANYWHERE}
    made = pl.pallas_call(
        kernel,
        out_shape=[
            pltpu.HBM(shape, kind) if space == "h" else jax.ShapeDtypeStruct(shape, kind)
            for (shape, kind), space in zip(outs, results)
        ],
        in_specs=[spaces[space] for space in ins],
        out_specs=[spaces[space] for space in results],
        scratch_shapes=list(scratch),
        compiler_params=pltpu.CompilerParams(vmem_limit_bytes=room * 2**20),
        cost_estimate=pl.CostEstimate(flops=flops, bytes_accessed=moved, transcendentals=exps),
        name=name,
    )

    def run(*args):
        return made(
            *[
                pltpu.with_memory_space_constraint(arg, pltpu.HBM) if space == "h" else arg
                for arg, space in zip(args, ins)
            ]
        )

    return run


def fetch(pairs, sems, first=0):
    copies = [
        pltpu.make_async_copy(source, target, sems.at[first + at])
        for at, (source, target) in enumerate(pairs)
    ]
    for copy in copies:
        copy.start()
    return copies


def wait(copies):
    for copy in copies:
        copy.wait()


def weights_kernel(w_any, mix_any, readout_any, columns_any, packed_any, *refs):
    w, columns, readout, packed, sems = refs
    copies = fetch(
        [(w_any, w), (readout_any, readout), (mix_any, packed.at[:, :LATENT_DIM])], sems
    )
    copies[0].wait()
    for g in range(GROUP):
        for part in range(3):
            at = (part * GROUP + g) * COLS
            columns[g, :, part * COLS : (part + 1) * COLS] = w[:, at : at + COLS]
    halves, _, members_num = columns_any.shape[:3]
    out = fetch(
        [
            (columns, columns_any.at[half, :, m])
            for half in range(halves)
            for m in range(members_num)
        ],
        sems,
        3,
    )
    wait(copies[1:])
    packed[:, LATENT_DIM:] = jnp.zeros((packed.shape[0], FIELD_PAD), BF16)
    packed[:, LATENT_DIM : LATENT_DIM + FIELD_NUM] = readout[...]
    wait(out + fetch([(packed, packed_any)], sems, 3 + len(out)))


def norm_kernel(near_any, source_any, normed_any, *refs):
    parts, (near, source, normed, sems) = refs[:-4], refs[-4:]
    ens = lax.axis_index("ens")
    copies = fetch([(source_any, source), (near_any, near)], sems)
    rows = source.shape[0]
    copies[0].wait()
    moves = []
    for step, part_any in enumerate(parts):
        count, part, _ = part_any.shape
        for m in range(count):
            place = (ens ^ step) if len(parts) == 2 else m
            place = pl.multiple_of(place * part, part)
            moves.append((source.at[pl.ds(place, part)], part_any.at[m]))
    out = fetch(moves, sems, 2)
    states = source[...].astype(F32)
    inverse = lax.rsqrt(jnp.mean(states * states, axis=-1, keepdims=True) + NORM_EPS)
    normed[:rows, :] = (states * inverse).astype(BF16)
    copies[1].wait()
    row = lax.broadcasted_iota(jnp.int32, (NOTE_ROWS, 128), 0)
    lane = lax.broadcasted_iota(jnp.int32, (NOTE_ROWS, 128), 1)
    note = jnp.zeros((NOTE_ROWS, 128), F32)
    tiles = near.shape[0]
    first_tile = lax.axis_index(("half", "quad", "core")) * tiles
    for tile in range(tiles):
        for slot in range(K_NB):
            at = near[tile, slot]
            step = jnp.where(at >= 0, at - first_tile - tile, NOWHERE).astype(F32)
            note = jnp.where((row == tile) & (lane == slot), step, note)
    normed[rows:, :] = jnp.zeros((NOTE_ROWS, LATENT_DIM), BF16)
    normed[rows:, :128] = note.astype(BF16)
    wait(out + fetch([(normed, normed_any)], sems, 2 + len(out)))


def attach_kernel(packed_ref, sent_any, out_ref, sems):
    width, shard = packed_ref.shape[2], packed_ref.shape[1]
    pairs = [
        (sent_any.at[0, pl.ds(at * shard, shard)], out_ref.at[at, :, width:]) for at in range(2)
    ]
    copies = fetch(pairs, sems)
    out_ref[:, :, :width] = packed_ref[...]
    wait(copies)


def merge_members_kernel(mine_ref, other_ref, packed_ref, source_ref):
    ens = lax.axis_index("ens")
    width = packed_ref.shape[3]
    for half in range(2):
        packed_ref[half, ens] = mine_ref[half, :, :width]
        packed_ref[half, ens ^ 1] = other_ref[half, :, :width]
    source_ref[...] = other_ref[:, :, width:].reshape(source_ref.shape)


def owners():
    core, quad = lax.axis_index("core"), lax.axis_index("quad")
    return [(quad ^ step) * CORES + (core ^ flip) for flip in range(CORES) for step in range(QUAD)]


def collect_kernel(*refs):
    blocks, (normed_any, steps_ref, notes, sems) = refs[:GROUP], refs[GROUP:]
    block = blocks[0].shape[0] - NOTE_ROWS
    pairs = []
    for rows_ref, owner in zip(blocks, owners()):
        place = pl.ds(pl.multiple_of(owner * block, block), block)
        pairs.append((rows_ref.at[:block], normed_any.at[place]))
        pairs.append((rows_ref.at[block:, :128], notes.at[owner]))
    wait(fetch(pairs, sems))
    steps_ref[...] = notes[...].astype(F32)


def put_rims(rims, first, last):
    if len(rims) == 1:
        rims[0][...] = jnp.where(lax.axis_index("half") == 0, last, first)
    else:
        rims[0][...], rims[1][...] = first, last


def rims_kernel(normed_any, *refs):
    rows, sems = refs[-2:]
    if len(refs[0].shape) == 2:
        columns, w, rims = refs[:1], refs[1], refs[2:-2]
        pairs = [(columns[0], w)]
    else:
        columns, w, rims = refs[:2], refs[2], refs[3:-2]
        ens = lax.axis_index("ens")
        pairs = [(part, w.at[:, ens ^ step]) for step, part in enumerate(columns)]
    last = normed_any.shape[0] - RIM
    if len(rims) == 1:
        place = pl.multiple_of(jnp.where(lax.axis_index("half") == 0, last, 0), RIM)
        pairs.append((normed_any.at[pl.ds(place, RIM)], rows.at[0]))
    else:
        pairs += [(normed_any.at[:RIM], rows.at[0]), (normed_any.at[last:], rows.at[1])]
    wait(fetch(pairs, sems))
    weights = w[...].reshape(LATENT_DIM, 3 * COLS)[:, COLS:]
    for at, rim_ref in enumerate(rims):
        rim_ref[...] = jnp.dot(rows[at], weights, preferred_element_type=F32).astype(BF16)


def project_kernel(normed_any, w_ref, q_ref, kv_ref, normed, sems):
    chunk = normed.shape[0] // CHUNKS
    rows = [slice(at * chunk, (at + 1) * chunk) for at in range(CHUNKS)]
    copies = fetch([(normed_any.at[part], normed.at[part]) for part in rows], sems)
    weights = w_ref[...].reshape(LATENT_DIM, 3 * COLS)
    for part, copy in zip(rows, copies):
        copy.wait()
        projected = jnp.dot(normed[part, :], weights, preferred_element_type=F32).astype(BF16)
        q_ref[part, :] = projected[:, :COLS] * jnp.asarray(HEAD**-0.5, BF16)
        kv_ref[part, :] = projected[:, COLS:]


def assemble_kernel(*refs):
    pieces, (w_any, sems) = refs[:GROUP], refs[GROUP:]
    core, quad = lax.axis_index("core"), lax.axis_index("quad")
    pairs = [
        (piece, w_any.at[:, quad ^ (at % QUAD), core ^ (at // QUAD)])
        for at, piece in enumerate(pieces)
    ]
    wait(fetch(pairs, sems))


def by_head(rows):
    lane = lax.broadcasted_iota(jnp.int32, rows.shape, 1)
    zero = jnp.zeros_like(rows)
    return jnp.concatenate(
        [jnp.where(lane < HEAD, rows, zero), jnp.where(lane < HEAD, zero, rows)], axis=0
    )


def usable_keys(steps_ref, pair):
    lane = (lax.broadcasted_iota(jnp.int32, (1, WINDOW), 1) // TILE - RADIUS).astype(F32)
    masks = []
    for query_tile in range(PAIR):
        found = jnp.zeros((1, WINDOW), F32)
        for slot in range(K_NB):
            step = steps_ref[pair, query_tile : query_tile + 1, slot : slot + 1]
            found = jnp.where(lane - query_tile == step, 1.0, found)
        masks.append(found)
    row = lax.broadcasted_iota(jnp.int32, (2 * PAIR * TILE, 1), 0) // TILE % PAIR
    return jnp.where(row == 0, masks[0], masks[1]) > 0


def raised_scores(queries, keys, usable):
    scores = lax.dot_general(queries, keys, OVER_COLUMNS, preferred_element_type=F32)
    scores = jnp.where(usable, scores, MASKED)
    raised = jnp.exp(scores - jnp.max(scores, axis=-1, keepdims=True))
    return raised, 1.0 / jnp.sum(raised, axis=-1, keepdims=True)


def attend(steps_ref, pair, queries, keys, values):
    raised, share = raised_scores(by_head(queries), keys, usable_keys(steps_ref, pair))
    both = jnp.dot(raised.astype(BF16), values, preferred_element_type=F32) * share
    lane = lax.broadcasted_iota(jnp.int32, queries.shape, 1)
    half = PAIR * TILE
    return jnp.where(lane < HEAD, both[:half], both[half:]).astype(BF16)


def interior_kernel(steps_ref, q_ref, kv_ref, out_ref):
    step = PAIR * TILE
    pairs = q_ref.shape[0] // step
    for pair in range(1, pairs - 1):
        window = slice((pair - 1) * step, (pair + 2) * step)
        rows = slice(pair * step, (pair + 1) * step)
        out_ref[rows, :] = attend(
            steps_ref, pair, q_ref[rows, :], kv_ref[window, :COLS], kv_ref[window, COLS:]
        )


def edge_kernel(steps_ref, q_ref, kv_ref, low_ref, high_ref, done_ref, out_ref):
    step = PAIR * TILE
    count = q_ref.shape[0]
    pairs = count // step
    out_ref[step : count - step, :] = done_ref[step : count - step, :]
    first = jnp.concatenate([low_ref[...], kv_ref[: 2 * step, :]], axis=0)
    last = jnp.concatenate([kv_ref[count - 2 * step :, :], high_ref[...]], axis=0)
    for pair, window in ((0, first), (pairs - 1, last)):
        rows = slice(pair * step, (pair + 1) * step)
        out_ref[rows, :] = attend(
            steps_ref, pair, q_ref[rows, :], window[:, :COLS], window[:, COLS:]
        )


def attend_back(steps_ref, pair, queries, grads, keys, values):
    queries, grads = by_head(queries), by_head(grads)
    raised, share = raised_scores(queries, keys, usable_keys(steps_ref, pair))
    probs = raised * share
    grad_probs = lax.dot_general(grads, values, OVER_COLUMNS, preferred_element_type=F32)
    row_delta = jnp.sum(probs * grad_probs, axis=-1, keepdims=True)
    grad_scores = (probs * (grad_probs - row_delta)).astype(BF16)
    key_grad = lax.dot_general(grad_scores, queries, OVER_ROWS, preferred_element_type=F32)
    value_grad = lax.dot_general(probs.astype(BF16), grads, OVER_ROWS, preferred_element_type=F32)
    return key_grad, value_grad


def edge_back_kernel(
    steps_ref, q_ref, kv_ref, low_ref, high_ref, g_ref, part_ref, *rims
):
    outer = []
    step = PAIR * TILE
    count = q_ref.shape[0]
    first = jnp.concatenate([low_ref[...], kv_ref[: 2 * step, :]], axis=0)
    last = jnp.concatenate([kv_ref[count - 2 * step :, :], high_ref[...]], axis=0)
    pairs = count // step
    for edge, pair, window in ((0, 0, first), (1, pairs - 1, last)):
        rows = slice(pair * step, (pair + 1) * step)
        grads = attend_back(
            steps_ref, pair, q_ref[rows, :], g_ref[rows, :], window[:, :COLS], window[:, COLS:]
        )
        rim = slice(0, RIM) if edge == 0 else slice(WINDOW - RIM, WINDOW)
        own = slice(RIM, WINDOW) if edge == 0 else slice(0, WINDOW - RIM)
        for at, grad in enumerate(grads):
            columns = slice(at * COLS, (at + 1) * COLS)
            part_ref[edge, :, columns] = grad[own]
        outer.append(jnp.concatenate([grad[rim].astype(BF16) for grad in grads], axis=1))
    put_rims(rims, *outer)


def interior_back_kernel(steps_ref, q_ref, kv_ref, g_ref, part_ref, out_ref):
    step = PAIR * TILE
    count = q_ref.shape[0]
    pairs = count // step
    reach = 2 * step
    out_ref[:reach, :] = part_ref[0]
    out_ref[reach : count - reach, :] = jnp.zeros((count - 2 * reach, 2 * COLS), F32)
    out_ref[count - reach :, :] = part_ref[1]
    for pair in range(1, pairs - 1):
        window = slice((pair - 1) * step, (pair + 2) * step)
        rows = slice(pair * step, (pair + 1) * step)
        key_grad, value_grad = attend_back(
            steps_ref,
            pair,
            q_ref[rows, :],
            g_ref[rows, :],
            kv_ref[window, :COLS],
            kv_ref[window, COLS:],
        )
        out_ref[window, :COLS] += key_grad
        out_ref[window, COLS:] += value_grad


def slope(spread):
    return spread * lax.rsqrt(spread * spread + SOFT_WIDTH)


def mix_kernel(att_ref, factor_ref, truth_any, w_any, *refs):
    sources, refs = refs[:-8], refs[-8:]
    pred_ref, grad_ref, a, truth_ref, truth, source, w, sems = refs
    members_num, part, _ = source.shape
    halves = w.shape[0]
    ens = lax.axis_index("ens")
    copies = fetch([(w_any.at[half], w.at[half]) for half in range(halves)], sems)
    pairs = [(truth_any, truth_ref)]
    if len(sources) == 1:
        pairs.append((sources[0], source))
    else:
        pairs += [(rows.at[0], source.at[ens ^ step]) for step, rows in enumerate(sources)]
    others = fetch(pairs, sems, halves)
    for g in range(GROUP):
        for m in range(members_num):
            a[m * part : (m + 1) * part, g * COLS : (g + 1) * COLS] = att_ref[g * members_num + m]
    wait(others)
    lane_part = lax.broadcasted_iota(jnp.int32, (1, a.shape[0]), 1) // part
    own_truth, own_factor = truth_ref[...], factor_ref[...]
    for turn in range(1, members_num):
        at = lane_part - turn
        here = jnp.where(at < 0, at + members_num, at) == ens
        own_truth = jnp.where(here, pltpu.roll(truth_ref[...], turn * part, 1), own_truth)
        own_factor = jnp.where(here, pltpu.roll(factor_ref[...], turn * part, 1), own_factor)
    truth[...] = jnp.zeros_like(truth)
    truth[:FIELD_NUM, :] = own_truth
    hidden = source[...].reshape(a.shape).astype(F32)
    count = LATENT_DIM // halves
    for half in range(halves):
        copies[half].wait()
        mix = w[half].reshape(count, LATENT_DIM + FIELD_PAD)[:, :LATENT_DIM]
        hidden += jnp.dot(
            a[:, half * count : (half + 1) * count], mix, preferred_element_type=F32
        )
    both = w[...].reshape(LATENT_DIM, LATENT_DIM + FIELD_PAD)
    mix, readout = both[:, :LATENT_DIM], both[:, LATENT_DIM:]
    inverse = lax.rsqrt(jnp.mean(hidden * hidden, axis=-1, keepdims=True) + NORM_EPS)
    decoded = (hidden * inverse).astype(BF16)
    prediction = lax.dot_general(
        readout, decoded, (((0,), (1,)), ((), ())), preferred_element_type=F32
    )
    pred_ref[...] = prediction[:FIELD_NUM]
    spread = jnp.zeros_like(prediction)
    for other in range(1, members_num):
        spread = spread + slope(prediction - pltpu.roll(prediction, other * part, 1))
    derivative = own_factor / FIELD_NUM * (
        slope(prediction - truth[...]) - spread / (members_num - 1)
    )
    grad_decoded = lax.dot_general(
        derivative.astype(BF16), readout, (((0,), (1,)), ((), ())), preferred_element_type=F32
    )
    grad_hidden = inverse * grad_decoded - hidden * inverse**3 * jnp.mean(
        grad_decoded * hidden, axis=-1, keepdims=True
    )
    grads = lax.dot_general(
        grad_hidden.astype(BF16), mix, OVER_COLUMNS, preferred_element_type=F32
    ).astype(BF16)
    for g in range(GROUP):
        for m in range(members_num):
            grad_ref[g * members_num + m] = grads[
                m * part : (m + 1) * part, g * COLS : (g + 1) * COLS
            ]


def product_kernel(normed_ref, grads_ref, out_ref):
    grads = grads_ref[...]
    high = grads.astype(BF16)
    low = (grads - high.astype(F32)).astype(BF16)
    both = lax.dot_general(
        normed_ref[...], jnp.concatenate([high, low], axis=1), OVER_ROWS, preferred_element_type=F32
    )
    out_ref[...] = both[:, : 2 * COLS] + both[:, 2 * COLS :]


def rim_product_kernel(normed_ref, total_ref, *refs):
    arrived, out_ref = refs[:-1], refs[-1]
    last_row = normed_ref.shape[0] - RIM
    half, last = lax.axis_index("half"), lax.axis_size("half") - 1
    if len(arrived) == 1:
        places = [pl.multiple_of(jnp.where(half == 0, last_row, 0), RIM)]
    else:
        places = [0, last_row]
    total = total_ref[...]
    for at, arrived_ref in enumerate(arrived):
        grads = arrived_ref[...]
        if len(arrived) == 2:
            grads = jnp.where((half > 0) if at == 0 else (half < last), grads.astype(F32), 0.0)
            grads = grads.astype(BF16)
        rows = normed_ref[pl.ds(places[at], RIM), :]
        total += lax.dot_general(rows, grads, OVER_ROWS, preferred_element_type=F32)
    out_ref[...] = total.astype(BF16)


def gather_kernel(parts_ref, out_ref):
    halves, _, members_num = parts_ref.shape[:3]
    for g in range(GROUP):
        total = None
        for half in range(halves):
            for m in range(members_num):
                part = parts_ref[half, g, m].astype(F32)
                total = part if total is None else total + part
        out_ref[:, g * COLS : (g + 1) * COLS] = total[:, :COLS]
        out_ref[:, LATENT_DIM + g * COLS : LATENT_DIM + (g + 1) * COLS] = total[:, COLS:]


def exchange(chunks, axes):
    return lax.all_to_all(chunks, axes, 0, 0)


def swap(value, axis, step):
    return lax.ppermute(value, axis, [(i, i ^ step) for i in range(lax.axis_size(axis))])


def in_order(mine, axis, at):
    if lax.axis_size(axis) != 2:
        return lax.all_gather(mine, axis, axis=at)
    other = swap(mine, axis, 1)
    first = lax.axis_index(axis) == 0
    return jnp.stack([jnp.where(first, mine, other), jnp.where(first, other, mine)], axis=at)


def body(members, w_attn, w_mix, readout_matrix, observed_truth, cell_surface_factor, neighbours):
    halves, members_num = lax.axis_size("half"), lax.axis_size("ens")
    nodes = ("half", "quad", "core")
    everyone = nodes + ("ens",)
    shard = w_attn.shape[0]
    node_rows = members.shape[1]
    rows = GROUP * node_rows
    part = node_rows // members_num
    up = [(i, i + 1) for i in range(halves - 1)]
    down = [(target, source) for source, target in up]
    ens = lax.axis_index("ens")
    width = LATENT_DIM + FIELD_PAD
    paired = members_num == 2
    copies = 1 if paired else members_num
    source_parts = 2 if paired else 1

    columns, packed = call(
        weights_kernel,
        "prepare_weights",
        [((halves, GROUP, copies, shard, 3 * COLS), BF16), ((shard, width), BF16)],
        "hhh",
        [
            pltpu.VMEM(w_attn.shape, BF16),
            pltpu.VMEM((GROUP, shard, 3 * COLS), BF16),
            pltpu.VMEM(readout_matrix.shape, BF16),
            pltpu.VMEM((shard, width), BF16),
            pltpu.SemaphoreType.DMA((4 + halves * copies,)),
        ],
        moved=2**20,
        results="hh",
    )(w_attn, w_mix, readout_matrix)
    normed, *sources = call(
        norm_kernel,
        "norm",
        [((node_rows + NOTE_ROWS, LATENT_DIM), BF16)]
        + [((1 if paired else members_num, part, LATENT_DIM), BF16)] * source_parts,
        "hh",
        [
            pltpu.SMEM(neighbours.shape, jnp.int32),
            pltpu.VMEM((node_rows, LATENT_DIM), BF16),
            pltpu.VMEM((node_rows + NOTE_ROWS, LATENT_DIM), BF16),
            pltpu.SemaphoreType.DMA((3 + max(2, members_num),)),
        ],
        flops=2**20,
        moved=2**20,
        results="h" + "h" * source_parts,
    )(neighbours, members.reshape(node_rows, LATENT_DIM))

    packed, normed = lax.optimization_barrier((in_order(packed, "half", 0), normed))
    near = [normed, swap(normed, "quad", 1), None, swap(normed, "quad", 3)]
    if paired:
        columns = exchange(columns.reshape(-1, shard, 3 * COLS), nodes)
        columns, late = lax.optimization_barrier((columns, normed))
        columns = [columns, swap(columns, "ens", 1)]
    else:
        columns = [exchange(columns.reshape(-1, shard, 3 * COLS), everyone)]
        columns = [columns[0].reshape(LATENT_DIM, 3 * COLS)]
        late = normed
    near[2] = swap(late, "quad", 2)
    near = list(lax.optimization_barrier(tuple(near)))
    far = [swap(piece, "core", 1) for piece in near]
    normed, steps = call(
        collect_kernel,
        "collect",
        [((rows, LATENT_DIM), BF16), ((GROUP, NOTE_ROWS, 128), F32)],
        "a" * (2 * QUAD),
        [pltpu.VMEM((GROUP, NOTE_ROWS, 128), BF16), pltpu.SemaphoreType.DMA((2 * GROUP,))],
        moved=4 * 2**20,
        results="hv",
    )(*near, *far)

    square = paired and halves == 2 and shard % 16 == 0
    if square:
        (wide,) = call(
            attach_kernel,
            "attach_sources",
            [((2, shard, width + LATENT_DIM), BF16)],
            "vh",
            [pltpu.SemaphoreType.DMA((2,))],
            moved=2**19,
        )(packed, sources[1])
        packed, arrived = call(
            merge_members_kernel,
            "merge_members",
            [((2, 2, shard, width), BF16), ((1, part, LATENT_DIM), BF16)],
            "vv",
            moved=2**19,
        )(wide, swap(wide, "ens", 1))
        packed = packed.reshape(2, 2 * shard, width)
        sources = [sources[0], arrived]
    else:
        packed = in_order(packed, "ens", 1).reshape(halves, members_num * shard, width)
    packed, near[2] = lax.optimization_barrier((packed, near[2]))
    pieces = [packed] + [swap(packed, "quad", step) for step in range(1, QUAD)]

    rim = ((RIM, 2 * COLS), BF16)
    rims = [rim] if halves == 2 else [rim, rim]
    w_shape = (GROUP * halves, 2, shard, 3 * COLS) if paired else (LATENT_DIM, 3 * COLS)
    weights, *inner = call(
        rims_kernel,
        "project_rims",
        [(w_shape, BF16)] + rims,
        "h" + "a" * len(columns),
        [pltpu.VMEM((len(rims), RIM, LATENT_DIM), BF16), pltpu.SemaphoreType.DMA((4,))],
        flops=RIM * LATENT_DIM * 4 * COLS,
        moved=2**20,
    )(normed, *columns)
    def across(inner):
        if halves == 2:
            got = swap(inner[0], "half", 1)
            return got, got
        return lax.ppermute(inner[1], "half", up), lax.ppermute(inner[0], "half", down)

    if not paired:
        sources = [exchange(sources[0], "ens")]
    elif not square:
        sources = [sources[0], swap(sources[1], "ens", 1)]
    low, high = across(inner)
    queries, own = call(
        project_kernel,
        "project",
        [((rows, COLS), BF16), ((rows, 2 * COLS), BF16)],
        "hv",
        [pltpu.VMEM((rows, LATENT_DIM), BF16), pltpu.SemaphoreType.DMA((CHUNKS,))],
        flops=rows * LATENT_DIM * 6 * COLS,
        moved=4 * 2**20,
    )(normed, weights)

    (outcome,) = call(
        interior_kernel,
        "attention_interior",
        [((rows, COLS), BF16)],
        "vvv",
        flops=rows * COLS * 2048,
        moved=2**21,
        exps=rows * 512,
    )(steps, queries, own)
    (outcome,) = call(
        edge_kernel,
        "attention_edges",
        [((rows, COLS), BF16)],
        "vvvvvv",
        flops=rows * COLS * 512,
        moved=2**20,
        exps=rows * 128,
    )(steps, queries, own, low, high, outcome)
    *pieces, own = lax.optimization_barrier((*pieces, own))
    pieces = pieces + [swap(piece, "core", 1) for piece in pieces]
    attended = exchange(outcome.reshape(GROUP * members_num, part, COLS), ("quad", "core", "ens"))
    block = (halves, QUAD, CORES, members_num * shard, width)
    (weights,) = call(
        assemble_kernel,
        "assemble",
        [(block, BF16)],
        "a" * len(pieces),
        [pltpu.SemaphoreType.DMA((GROUP,))],
        moved=4 * 2**20,
        results="h",
    )(*pieces)

    prediction, grads = call(
        mix_kernel,
        "mix_loss_backward",
        [((FIELD_NUM, node_rows), F32), ((GROUP * members_num, part, COLS), BF16)],
        "vvhh" + "a" * len(sources),
        [
            pltpu.VMEM((node_rows, LATENT_DIM), BF16),
            pltpu.VMEM(observed_truth.shape, F32),
            pltpu.VMEM((FIELD_PAD, node_rows), F32),
            pltpu.VMEM((members_num, part, LATENT_DIM), BF16),
            pltpu.VMEM(block, BF16),
            pltpu.SemaphoreType.DMA((halves + 1 + len(sources),)),
        ],
        flops=node_rows * LATENT_DIM * 4 * width,
        moved=2**22,
        room=14,
    )(attended, cell_surface_factor[None], observed_truth, weights, *sources)
    grads = exchange(grads, ("quad", "core", "ens")).reshape(rows, COLS)

    edges, *inner = call(
        edge_back_kernel,
        "attention_edges_back",
        [((2, WINDOW - RIM, 2 * COLS), F32)] + rims,
        "vvvvvv",
        flops=rows * COLS * 1280,
        moved=2**20,
        exps=rows * 128,
    )(steps, queries, own, low, high, grads)
    from_low, from_high = across(inner)
    (kv_grads,) = call(
        interior_back_kernel,
        "attention_interior_back",
        [((rows, 2 * COLS), F32)],
        "vvvvv",
        flops=rows * COLS * 4096,
        moved=2**22,
        exps=rows * 512,
        room=10,
    )(steps, queries, own, grads, edges)
    (total,) = call(
        product_kernel,
        "product",
        [((LATENT_DIM, 2 * COLS), F32)],
        "vv",
        room=16,
    )(normed, kv_grads)
    arrived = [from_low] if halves == 2 else [from_low, from_high]
    (term,) = call(
        rim_product_kernel,
        "product_rims",
        [((LATENT_DIM, 2 * COLS), BF16)],
        "vv" + "v" * len(arrived),
        flops=RIM * LATENT_DIM * 4 * COLS,
        moved=2**21,
        room=16,
    )(normed, total, *arrived)
    term, prediction = lax.optimization_barrier((term, prediction))
    term = exchange(term.reshape(-1, shard, 2 * COLS), everyone)
    (grad_kv,) = call(
        gather_kernel, "gather_sums", [((shard, 2 * LATENT_DIM), F32)], "v", flops=2**17, moved=2**20
    )(term.reshape(halves, GROUP, members_num, shard, 2 * COLS))

    if members_num == 2:
        got = jnp.roll(swap(prediction, "ens", 1), part, axis=1)
        lane = lax.broadcasted_iota(jnp.int32, prediction.shape, 1)
        prediction = jnp.where(lane // part == ens, prediction, got)
    else:
        prediction = prediction.reshape(FIELD_NUM, members_num, part).transpose(1, 0, 2)
        prediction = exchange(prediction, "ens").transpose(1, 0, 2)
    return (prediction.reshape(1, FIELD_NUM, node_rows), grad_kv)


def solution(mesh):
    space, ens = mesh.shape["space"], mesh.shape["ens"]
    split = Mesh(
        mesh.devices.reshape(space // GROUP, QUAD, CORES, ens), ("half", "quad", "core", "ens")
    )
    nodes = ("half", "quad", "core")
    shards = nodes + ("ens",)
    in_specs = (
        P("ens", nodes, None),
        P(shards, None),
        P(shards, None),
        P(shards, None),
        P(None, nodes),
        P(nodes),
        P(nodes, None),
    )
    out_specs = (P("ens", None, nodes), P(shards, None))
    return jax.shard_map(body, mesh=split, in_specs=in_specs, out_specs=out_specs, check_vma=False)
```

```python
import functools

import jax
import jax.numpy as jnp
from jax import lax
from jax.experimental import pallas as pl
from jax.experimental.pallas import tpu as pltpu
from jax.sharding import Mesh
from jax.sharding import PartitionSpec as P

LATENT_DIM = 1024
HEADS = 16
HEAD = 64
FIELD_NUM = 100
TILE = 64
RADIUS = 2
K_NB = 4
QUAD = 4
CORES = 2
GROUP = QUAD * CORES
COLS = LATENT_DIM // GROUP
RIM = RADIUS * TILE
FIELD_PAD = 128
PAIR = 2
WINDOW = (PAIR + 2 * RADIUS) * TILE
NOWHERE = 100
NOTE_ROWS = 16
CHUNKS = 4

NORM_EPS = 1e-06
SOFT_WIDTH = 0.0625
MASKED = -1e30

F32 = jnp.float32
BF16 = jnp.bfloat16

VMEM = pl.BlockSpec(memory_space=pltpu.VMEM)
SMEM = pl.BlockSpec(memory_space=pltpu.SMEM)
HBM = pl.BlockSpec(memory_space=pltpu.HBM)
ANYWHERE = pl.BlockSpec(memory_space=pl.ANY)
OVER_ROWS = (((0,), (0,)), ((), ()))
OVER_COLUMNS = (((1,), (1,)), ((), ()))


def call(kernel, name, outs, ins, scratch=(), flops=0, moved=0, exps=0, room=8, results=None):
    results = results or "v" * len(outs)
    spaces = {"s": SMEM, "v": VMEM, "h": HBM, "a": ANYWHERE}
    made = pl.pallas_call(
        kernel,
        out_shape=[
            pltpu.HBM(shape, kind) if space == "h" else jax.ShapeDtypeStruct(shape, kind)
            for (shape, kind), space in zip(outs, results)
        ],
        in_specs=[spaces[space] for space in ins],
        out_specs=[spaces[space] for space in results],
        scratch_shapes=list(scratch),
        compiler_params=pltpu.CompilerParams(vmem_limit_bytes=room * 2**20),
        cost_estimate=pl.CostEstimate(flops=flops, bytes_accessed=moved, transcendentals=exps),
        name=name,
    )

    def run(*args):
        return made(
            *[
                pltpu.with_memory_space_constraint(arg, pltpu.HBM) if space == "h" else arg
                for arg, space in zip(args, ins)
            ]
        )

    return run


def fetch(pairs, sems, first=0):
    copies = [
        pltpu.make_async_copy(source, target, sems.at[first + at])
        for at, (source, target) in enumerate(pairs)
    ]
    for copy in copies:
        copy.start()
    return copies


def wait(copies):
    for copy in copies:
        copy.wait()


def weights_kernel(w_any, mix_any, readout_any, columns_any, packed_any, *refs):
    w, columns, readout, packed, sems = refs
    copies = fetch(
        [(w_any, w), (readout_any, readout), (mix_any, packed.at[:, :LATENT_DIM])], sems
    )
    copies[0].wait()
    for g in range(GROUP):
        for part in range(3):
            at = (part * GROUP + g) * COLS
            columns[g, :, part * COLS : (part + 1) * COLS] = w[:, at : at + COLS]
    halves, _, members_num = columns_any.shape[:3]
    out = fetch(
        [
            (columns, columns_any.at[half, :, m])
            for half in range(halves)
            for m in range(members_num)
        ],
        sems,
        3,
    )
    wait(copies[1:])
    packed[:, LATENT_DIM:] = jnp.zeros((packed.shape[0], FIELD_PAD), BF16)
    packed[:, LATENT_DIM : LATENT_DIM + FIELD_NUM] = readout[...]
    wait(out + fetch([(packed, packed_any)], sems, 3 + len(out)))


def norm_kernel(near_any, source_any, normed_any, *refs):
    parts, (near, source, normed, sems) = refs[:-4], refs[-4:]
    ens = lax.axis_index("ens")
    copies = fetch([(source_any, source), (near_any, near)], sems)
    rows = source.shape[0]
    copies[0].wait()
    moves = []
    for step, part_any in enumerate(parts):
        count, part, _ = part_any.shape
        for m in range(count):
            place = (ens ^ step) if len(parts) == 2 else m
            place = pl.multiple_of(place * part, part)
            moves.append((source.at[pl.ds(place, part)], part_any.at[m]))
    out = fetch(moves, sems, 2)
    states = source[...].astype(F32)
    inverse = lax.rsqrt(jnp.mean(states * states, axis=-1, keepdims=True) + NORM_EPS)
    normed[:rows, :] = (states * inverse).astype(BF16)
    copies[1].wait()
    row = lax.broadcasted_iota(jnp.int32, (NOTE_ROWS, 128), 0)
    lane = lax.broadcasted_iota(jnp.int32, (NOTE_ROWS, 128), 1)
    note = jnp.zeros((NOTE_ROWS, 128), F32)
    tiles = near.shape[0]
    first_tile = lax.axis_index(("half", "quad", "core")) * tiles
    for tile in range(tiles):
        for slot in range(K_NB):
            at = near[tile, slot]
            step = jnp.where(at >= 0, at - first_tile - tile, NOWHERE).astype(F32)
            note = jnp.where((row == tile) & (lane == slot), step, note)
    normed[rows:, :] = jnp.zeros((NOTE_ROWS, LATENT_DIM), BF16)
    normed[rows:, :128] = note.astype(BF16)
    wait(out + fetch([(normed, normed_any)], sems, 2 + len(out)))


def attach_kernel(packed_ref, sent_any, out_ref, sems):
    width, shard = packed_ref.shape[2], packed_ref.shape[1]
    pairs = [
        (sent_any.at[0, pl.ds(at * shard, shard)], out_ref.at[at, :, width:]) for at in range(2)
    ]
    copies = fetch(pairs, sems)
    out_ref[:, :, :width] = packed_ref[...]
    wait(copies)


def merge_members_kernel(mine_ref, other_ref, packed_ref, source_ref):
    ens = lax.axis_index("ens")
    width = packed_ref.shape[3]
    for half in range(2):
        packed_ref[half, ens] = mine_ref[half, :, :width]
        packed_ref[half, ens ^ 1] = other_ref[half, :, :width]
    source_ref[...] = other_ref[:, :, width:].reshape(source_ref.shape)


def owners():
    core, quad = lax.axis_index("core"), lax.axis_index("quad")
    return [(quad ^ step) * CORES + (core ^ flip) for flip in range(CORES) for step in range(QUAD)]


def collect_kernel(*refs):
    blocks, (normed_any, steps_ref, notes, sems) = refs[:GROUP], refs[GROUP:]
    block = blocks[0].shape[0] - NOTE_ROWS
    pairs = []
    for rows_ref, owner in zip(blocks, owners()):
        place = pl.ds(pl.multiple_of(owner * block, block), block)
        pairs.append((rows_ref.at[:block], normed_any.at[place]))
        pairs.append((rows_ref.at[block:, :128], notes.at[owner]))
    wait(fetch(pairs, sems))
    steps_ref[...] = notes[...].astype(F32)


def put_rims(rims, first, last):
    if len(rims) == 1:
        rims[0][...] = jnp.where(lax.axis_index("half") == 0, last, first)
    else:
        rims[0][...], rims[1][...] = first, last


def rims_kernel(normed_any, *refs):
    rows, sems = refs[-2:]
    if len(refs[0].shape) == 2:
        columns, w, rims = refs[:1], refs[1], refs[2:-2]
        pairs = [(columns[0], w)]
    else:
        columns, w, rims = refs[:2], refs[2], refs[3:-2]
        ens = lax.axis_index("ens")
        pairs = [(part, w.at[:, ens ^ step]) for step, part in enumerate(columns)]
    last = normed_any.shape[0] - RIM
    if len(rims) == 1:
        place = pl.multiple_of(jnp.where(lax.axis_index("half") == 0, last, 0), RIM)
        pairs.append((normed_any.at[pl.ds(place, RIM)], rows.at[0]))
    else:
        pairs += [(normed_any.at[:RIM], rows.at[0]), (normed_any.at[last:], rows.at[1])]
    wait(fetch(pairs, sems))
    weights = w[...].reshape(LATENT_DIM, 3 * COLS)[:, COLS:]
    for at, rim_ref in enumerate(rims):
        rim_ref[...] = jnp.dot(rows[at], weights, preferred_element_type=F32).astype(BF16)


def project_kernel(normed_any, w_ref, q_ref, kv_ref, normed, sems):
    chunk = normed.shape[0] // CHUNKS
    rows = [slice(at * chunk, (at + 1) * chunk) for at in range(CHUNKS)]
    copies = fetch([(normed_any.at[part], normed.at[part]) for part in rows], sems)
    weights = w_ref[...].reshape(LATENT_DIM, 3 * COLS)
    for part, copy in zip(rows, copies):
        copy.wait()
        projected = jnp.dot(normed[part, :], weights, preferred_element_type=F32).astype(BF16)
        q_ref[part, :] = projected[:, :COLS] * jnp.asarray(HEAD**-0.5, BF16)
        kv_ref[part, :] = projected[:, COLS:]


def assemble_kernel(*refs):
    pieces, (w_any, sems) = refs[:GROUP], refs[GROUP:]
    core, quad = lax.axis_index("core"), lax.axis_index("quad")
    pairs = [
        (piece, w_any.at[:, quad ^ (at % QUAD), core ^ (at // QUAD)])
        for at, piece in enumerate(pieces)
    ]
    wait(fetch(pairs, sems))


def by_head(rows):
    lane = lax.broadcasted_iota(jnp.int32, rows.shape, 1)
    zero = jnp.zeros_like(rows)
    return jnp.concatenate(
        [jnp.where(lane < HEAD, rows, zero), jnp.where(lane < HEAD, zero, rows)], axis=0
    )


def usable_keys(steps_ref, pair):
    lane = (lax.broadcasted_iota(jnp.int32, (1, WINDOW), 1) // TILE - RADIUS).astype(F32)
    masks = []
    for query_tile in range(PAIR):
        found = jnp.zeros((1, WINDOW), F32)
        for slot in range(K_NB):
            step = steps_ref[pair, query_tile : query_tile + 1, slot : slot + 1]
            found = jnp.where(lane - query_tile == step, 1.0, found)
        masks.append(found)
    row = lax.broadcasted_iota(jnp.int32, (2 * PAIR * TILE, 1), 0) // TILE % PAIR
    return jnp.where(row == 0, masks[0], masks[1]) > 0


def raised_scores(queries, keys, usable):
    scores = lax.dot_general(queries, keys, OVER_COLUMNS, preferred_element_type=F32)
    scores = jnp.where(usable, scores, MASKED)
    raised = jnp.exp(scores - jnp.max(scores, axis=-1, keepdims=True))
    return raised, 1.0 / jnp.sum(raised, axis=-1, keepdims=True)


def attend(steps_ref, pair, queries, keys, values):
    raised, share = raised_scores(by_head(queries), keys, usable_keys(steps_ref, pair))
    both = jnp.dot(raised.astype(BF16), values, preferred_element_type=F32) * share
    lane = lax.broadcasted_iota(jnp.int32, queries.shape, 1)
    half = PAIR * TILE
    return jnp.where(lane < HEAD, both[:half], both[half:]).astype(BF16)


def interior_kernel(steps_ref, q_ref, kv_ref, out_ref):
    step = PAIR * TILE
    pairs = q_ref.shape[0] // step
    for pair in range(1, pairs - 1):
        window = slice((pair - 1) * step, (pair + 2) * step)
        rows = slice(pair * step, (pair + 1) * step)
        out_ref[rows, :] = attend(
            steps_ref, pair, q_ref[rows, :], kv_ref[window, :COLS], kv_ref[window, COLS:]
        )


def edge_kernel(steps_ref, q_ref, kv_ref, low_ref, high_ref, done_ref, out_ref):
    step = PAIR * TILE
    count = q_ref.shape[0]
    pairs = count // step
    out_ref[step : count - step, :] = done_ref[step : count - step, :]
    first = jnp.concatenate([low_ref[...], kv_ref[: 2 * step, :]], axis=0)
    last = jnp.concatenate([kv_ref[count - 2 * step :, :], high_ref[...]], axis=0)
    for pair, window in ((0, first), (pairs - 1, last)):
        rows = slice(pair * step, (pair + 1) * step)
        out_ref[rows, :] = attend(
            steps_ref, pair, q_ref[rows, :], window[:, :COLS], window[:, COLS:]
        )


def attend_back(steps_ref, pair, queries, grads, keys, values):
    queries, grads = by_head(queries), by_head(grads)
    raised, share = raised_scores(queries, keys, usable_keys(steps_ref, pair))
    probs = raised * share
    grad_probs = lax.dot_general(grads, values, OVER_COLUMNS, preferred_element_type=F32)
    row_delta = jnp.sum(probs * grad_probs, axis=-1, keepdims=True)
    grad_scores = (probs * (grad_probs - row_delta)).astype(BF16)
    key_grad = lax.dot_general(grad_scores, queries, OVER_ROWS, preferred_element_type=F32)
    value_grad = lax.dot_general(probs.astype(BF16), grads, OVER_ROWS, preferred_element_type=F32)
    return key_grad, value_grad


def edge_back_kernel(
    steps_ref, q_ref, kv_ref, low_ref, high_ref, g_ref, part_ref, *rims
):
    outer = []
    step = PAIR * TILE
    count = q_ref.shape[0]
    first = jnp.concatenate([low_ref[...], kv_ref[: 2 * step, :]], axis=0)
    last = jnp.concatenate([kv_ref[count - 2 * step :, :], high_ref[...]], axis=0)
    pairs = count // step
    for edge, pair, window in ((0, 0, first), (1, pairs - 1, last)):
        rows = slice(pair * step, (pair + 1) * step)
        grads = attend_back(
            steps_ref, pair, q_ref[rows, :], g_ref[rows, :], window[:, :COLS], window[:, COLS:]
        )
        rim = slice(0, RIM) if edge == 0 else slice(WINDOW - RIM, WINDOW)
        own = slice(RIM, WINDOW) if edge == 0 else slice(0, WINDOW - RIM)
        for at, grad in enumerate(grads):
            columns = slice(at * COLS, (at + 1) * COLS)
            part_ref[edge, :, columns] = grad[own]
        outer.append(jnp.concatenate([grad[rim].astype(BF16) for grad in grads], axis=1))
    put_rims(rims, *outer)


def interior_back_kernel(steps_ref, q_ref, kv_ref, g_ref, part_ref, out_ref):
    step = PAIR * TILE
    count = q_ref.shape[0]
    pairs = count // step
    reach = 2 * step
    out_ref[:reach, :] = part_ref[0]
    out_ref[reach : count - reach, :] = jnp.zeros((count - 2 * reach, 2 * COLS), F32)
    out_ref[count - reach :, :] = part_ref[1]
    for pair in range(1, pairs - 1):
        window = slice((pair - 1) * step, (pair + 2) * step)
        rows = slice(pair * step, (pair + 1) * step)
        key_grad, value_grad = attend_back(
            steps_ref,
            pair,
            q_ref[rows, :],
            g_ref[rows, :],
            kv_ref[window, :COLS],
            kv_ref[window, COLS:],
        )
        out_ref[window, :COLS] += key_grad
        out_ref[window, COLS:] += value_grad


def slope(spread):
    return spread * lax.rsqrt(spread * spread + SOFT_WIDTH)


def mix_kernel(att_ref, factor_ref, truth_any, w, *refs):
    sources, refs = refs[:-7], refs[-7:]
    pred_ref, grad_ref, a, truth_ref, truth, source, sems = refs
    members_num, part, _ = source.shape
    ens = lax.axis_index("ens")
    pairs = [(truth_any, truth_ref)]
    if len(sources) == 1:
        pairs.append((sources[0], source))
    else:
        pairs += [(rows.at[0], source.at[ens ^ step]) for step, rows in enumerate(sources)]
    others = fetch(pairs, sems)
    for g in range(GROUP):
        for m in range(members_num):
            a[m * part : (m + 1) * part, g * COLS : (g + 1) * COLS] = att_ref[g * members_num + m]
    wait(others)
    lane_part = lax.broadcasted_iota(jnp.int32, (1, a.shape[0]), 1) // part
    own_truth, own_factor = truth_ref[...], factor_ref[...]
    for turn in range(1, members_num):
        at = lane_part - turn
        here = jnp.where(at < 0, at + members_num, at) == ens
        own_truth = jnp.where(here, pltpu.roll(truth_ref[...], turn * part, 1), own_truth)
        own_factor = jnp.where(here, pltpu.roll(factor_ref[...], turn * part, 1), own_factor)
    truth[...] = jnp.zeros_like(truth)
    truth[:FIELD_NUM, :] = own_truth
    hidden = source[...].reshape(a.shape).astype(F32)
    both = w[...].reshape(LATENT_DIM, LATENT_DIM + FIELD_PAD)
    mix, readout = both[:, :LATENT_DIM], both[:, LATENT_DIM:]
    hidden += jnp.dot(a[...], mix, preferred_element_type=F32)
    inverse = lax.rsqrt(jnp.mean(hidden * hidden, axis=-1, keepdims=True) + NORM_EPS)
    decoded = (hidden * inverse).astype(BF16)
    prediction = lax.dot_general(
        readout, decoded, (((0,), (1,)), ((), ())), preferred_element_type=F32
    )
    pred_ref[...] = prediction[:FIELD_NUM]
    spread = jnp.zeros_like(prediction)
    for other in range(1, members_num):
        spread = spread + slope(prediction - pltpu.roll(prediction, other * part, 1))
    derivative = own_factor / FIELD_NUM * (
        slope(prediction - truth[...]) - spread / (members_num - 1)
    )
    grad_decoded = lax.dot_general(
        derivative.astype(BF16), readout, (((0,), (1,)), ((), ())), preferred_element_type=F32
    )
    grad_hidden = inverse * grad_decoded - hidden * inverse**3 * jnp.mean(
        grad_decoded * hidden, axis=-1, keepdims=True
    )
    grads = lax.dot_general(
        grad_hidden.astype(BF16), mix, OVER_COLUMNS, preferred_element_type=F32
    ).astype(BF16)
    for g in range(GROUP):
        for m in range(members_num):
            grad_ref[g * members_num + m] = grads[
                m * part : (m + 1) * part, g * COLS : (g + 1) * COLS
            ]


def product_kernel(normed_ref, grads_ref, out_ref):
    grads = grads_ref[...]
    high = grads.astype(BF16)
    low = (grads - high.astype(F32)).astype(BF16)
    both = lax.dot_general(
        normed_ref[...], jnp.concatenate([high, low], axis=1), OVER_ROWS, preferred_element_type=F32
    )
    out_ref[...] = both[:, : 2 * COLS] + both[:, 2 * COLS :]


def rim_product_kernel(normed_ref, total_ref, *refs):
    arrived, out_ref = refs[:-1], refs[-1]
    last_row = normed_ref.shape[0] - RIM
    half, last = lax.axis_index("half"), lax.axis_size("half") - 1
    if len(arrived) == 1:
        places = [pl.multiple_of(jnp.where(half == 0, last_row, 0), RIM)]
    else:
        places = [0, last_row]
    total = total_ref[...]
    for at, arrived_ref in enumerate(arrived):
        grads = arrived_ref[...]
        if len(arrived) == 2:
            grads = jnp.where((half > 0) if at == 0 else (half < last), grads.astype(F32), 0.0)
            grads = grads.astype(BF16)
        rows = normed_ref[pl.ds(places[at], RIM), :]
        total += lax.dot_general(rows, grads, OVER_ROWS, preferred_element_type=F32)
    out_ref[...] = total.astype(BF16)


def gather_kernel(parts_ref, out_ref):
    halves, _, members_num = parts_ref.shape[:3]
    for g in range(GROUP):
        total = None
        for half in range(halves):
            for m in range(members_num):
                part = parts_ref[half, g, m].astype(F32)
                total = part if total is None else total + part
        out_ref[:, g * COLS : (g + 1) * COLS] = total[:, :COLS]
        out_ref[:, LATENT_DIM + g * COLS : LATENT_DIM + (g + 1) * COLS] = total[:, COLS:]


def exchange(chunks, axes):
    return lax.all_to_all(chunks, axes, 0, 0)


def swap(value, axis, step):
    return lax.ppermute(value, axis, [(i, i ^ step) for i in range(lax.axis_size(axis))])


def in_order(mine, axis, at):
    if lax.axis_size(axis) != 2:
        return lax.all_gather(mine, axis, axis=at)
    other = swap(mine, axis, 1)
    first = lax.axis_index(axis) == 0
    return jnp.stack([jnp.where(first, mine, other), jnp.where(first, other, mine)], axis=at)


def body(members, w_attn, w_mix, readout_matrix, observed_truth, cell_surface_factor, neighbours):
    halves, members_num = lax.axis_size("half"), lax.axis_size("ens")
    nodes = ("half", "quad", "core")
    everyone = nodes + ("ens",)
    shard = w_attn.shape[0]
    node_rows = members.shape[1]
    rows = GROUP * node_rows
    part = node_rows // members_num
    up = [(i, i + 1) for i in range(halves - 1)]
    down = [(target, source) for source, target in up]
    ens = lax.axis_index("ens")
    width = LATENT_DIM + FIELD_PAD
    paired = members_num == 2
    copies = 1 if paired else members_num
    source_parts = 2 if paired else 1

    columns, packed = call(
        weights_kernel,
        "prepare_weights",
        [((halves, GROUP, copies, shard, 3 * COLS), BF16), ((shard, width), BF16)],
        "hhh",
        [
            pltpu.VMEM(w_attn.shape, BF16),
            pltpu.VMEM((GROUP, shard, 3 * COLS), BF16),
            pltpu.VMEM(readout_matrix.shape, BF16),
            pltpu.VMEM((shard, width), BF16),
            pltpu.SemaphoreType.DMA((4 + halves * copies,)),
        ],
        moved=2**20,
        results="hh",
    )(w_attn, w_mix, readout_matrix)
    normed, *sources = call(
        norm_kernel,
        "norm",
        [((node_rows + NOTE_ROWS, LATENT_DIM), BF16)]
        + [((1 if paired else members_num, part, LATENT_DIM), BF16)] * source_parts,
        "hh",
        [
            pltpu.SMEM(neighbours.shape, jnp.int32),
            pltpu.VMEM((node_rows, LATENT_DIM), BF16),
            pltpu.VMEM((node_rows + NOTE_ROWS, LATENT_DIM), BF16),
            pltpu.SemaphoreType.DMA((3 + max(2, members_num),)),
        ],
        flops=2**20,
        moved=2**20,
        results="h" + "h" * source_parts,
    )(neighbours, members.reshape(node_rows, LATENT_DIM))

    packed, normed = lax.optimization_barrier((in_order(packed, "half", 0), normed))
    square = paired and halves == 2 and shard % 16 == 0
    near = [normed, swap(normed, "quad", 1), None, swap(normed, "quad", 3)]
    if paired:
        columns = exchange(columns.reshape(-1, shard, 3 * COLS), nodes)
        if square:
            (wide,) = call(
                attach_kernel,
                "attach_sources",
                [((2, shard, width + LATENT_DIM), BF16)],
                "vh",
                [pltpu.SemaphoreType.DMA((2,))],
                moved=2**19,
            )(packed, sources[1])
            columns, late, wide = lax.optimization_barrier((columns, normed, wide))
        else:
            columns, late = lax.optimization_barrier((columns, normed))
        columns = [columns, swap(columns, "ens", 1)]
    else:
        columns = [exchange(columns.reshape(-1, shard, 3 * COLS), everyone)]
        columns = [columns[0].reshape(LATENT_DIM, 3 * COLS)]
        late = normed
    near[2] = swap(late, "quad", 2)
    near = list(lax.optimization_barrier(tuple(near)))
    far = [swap(piece, "core", 1) for piece in near]
    normed, steps = call(
        collect_kernel,
        "collect",
        [((rows, LATENT_DIM), BF16), ((GROUP, NOTE_ROWS, 128), F32)],
        "a" * (2 * QUAD),
        [pltpu.VMEM((GROUP, NOTE_ROWS, 128), BF16), pltpu.SemaphoreType.DMA((2 * GROUP,))],
        moved=4 * 2**20,
        results="hv",
    )(*near, *far)

    if square:
        packed, arrived = call(
            merge_members_kernel,
            "merge_members",
            [((2, 2, shard, width), BF16), ((1, part, LATENT_DIM), BF16)],
            "vv",
            moved=2**19,
        )(wide, swap(wide, "ens", 1))
        packed = packed.reshape(2, 2 * shard, width)
        sources = [sources[0], arrived]
    else:
        packed = in_order(packed, "ens", 1).reshape(halves, members_num * shard, width)
    packed, near[2] = lax.optimization_barrier((packed, near[2]))
    pieces = [packed] + [swap(packed, "quad", step) for step in range(1, QUAD)]

    rim = ((RIM, 2 * COLS), BF16)
    rims = [rim] if halves == 2 else [rim, rim]
    w_shape = (GROUP * halves, 2, shard, 3 * COLS) if paired else (LATENT_DIM, 3 * COLS)
    weights, *inner = call(
        rims_kernel,
        "project_rims",
        [(w_shape, BF16)] + rims,
        "h" + "a" * len(columns),
        [pltpu.VMEM((len(rims), RIM, LATENT_DIM), BF16), pltpu.SemaphoreType.DMA((4,))],
        flops=RIM * LATENT_DIM * 4 * COLS,
        moved=2**20,
    )(normed, *columns)
    def across(inner):
        if halves == 2:
            got = swap(inner[0], "half", 1)
            return got, got
        return lax.ppermute(inner[1], "half", up), lax.ppermute(inner[0], "half", down)

    if not paired:
        sources = [exchange(sources[0], "ens")]
    elif not square:
        sources = [sources[0], swap(sources[1], "ens", 1)]
    low, high = across(inner)
    queries, own = call(
        project_kernel,
        "project",
        [((rows, COLS), BF16), ((rows, 2 * COLS), BF16)],
        "hv",
        [pltpu.VMEM((rows, LATENT_DIM), BF16), pltpu.SemaphoreType.DMA((CHUNKS,))],
        flops=rows * LATENT_DIM * 6 * COLS,
        moved=4 * 2**20,
    )(normed, weights)

    (outcome,) = call(
        interior_kernel,
        "attention_interior",
        [((rows, COLS), BF16)],
        "vvv",
        flops=rows * COLS * 2048,
        moved=2**21,
        exps=rows * 512,
    )(steps, queries, own)
    (outcome,) = call(
        edge_kernel,
        "attention_edges",
        [((rows, COLS), BF16)],
        "vvvvvv",
        flops=rows * COLS * 512,
        moved=2**20,
        exps=rows * 128,
    )(steps, queries, own, low, high, outcome)
    *pieces, own = lax.optimization_barrier((*pieces, own))
    pieces = pieces + [swap(piece, "core", 1) for piece in pieces]
    attended = exchange(outcome.reshape(GROUP * members_num, part, COLS), ("quad", "core", "ens"))
    block = (halves, QUAD, CORES, members_num * shard, width)
    (weights,) = call(
        assemble_kernel,
        "assemble",
        [(block, BF16)],
        "a" * len(pieces),
        [pltpu.SemaphoreType.DMA((GROUP,))],
        moved=4 * 2**20,
    )(*pieces)

    prediction, grads = call(
        mix_kernel,
        "mix_loss_backward",
        [((FIELD_NUM, node_rows), F32), ((GROUP * members_num, part, COLS), BF16)],
        "vvhv" + "a" * len(sources),
        [
            pltpu.VMEM((node_rows, LATENT_DIM), BF16),
            pltpu.VMEM(observed_truth.shape, F32),
            pltpu.VMEM((FIELD_PAD, node_rows), F32),
            pltpu.VMEM((members_num, part, LATENT_DIM), BF16),
            pltpu.SemaphoreType.DMA((1 + len(sources),)),
        ],
        flops=node_rows * LATENT_DIM * 4 * width,
        moved=2**22,
        room=14,
    )(attended, cell_surface_factor[None], observed_truth, weights, *sources)
    grads = exchange(grads, ("quad", "core", "ens")).reshape(rows, COLS)

    edges, *inner = call(
        edge_back_kernel,
        "attention_edges_back",
        [((2, WINDOW - RIM, 2 * COLS), F32)] + rims,
        "vvvvvv",
        flops=rows * COLS * 1280,
        moved=2**20,
        exps=rows * 128,
    )(steps, queries, own, low, high, grads)
    from_low, from_high = across(inner)
    (kv_grads,) = call(
        interior_back_kernel,
        "attention_interior_back",
        [((rows, 2 * COLS), F32)],
        "vvvvv",
        flops=rows * COLS * 4096,
        moved=2**22,
        exps=rows * 512,
        room=10,
    )(steps, queries, own, grads, edges)
    (total,) = call(
        product_kernel,
        "product",
        [((LATENT_DIM, 2 * COLS), F32)],
        "vv",
        room=16,
    )(normed, kv_grads)
    arrived = [from_low] if halves == 2 else [from_low, from_high]
    (term,) = call(
        rim_product_kernel,
        "product_rims",
        [((LATENT_DIM, 2 * COLS), BF16)],
        "vv" + "v" * len(arrived),
        flops=RIM * LATENT_DIM * 4 * COLS,
        moved=2**21,
        room=16,
    )(normed, total, *arrived)
    term, prediction = lax.optimization_barrier((term, prediction))
    term = exchange(term.reshape(-1, shard, 2 * COLS), everyone)
    (grad_kv,) = call(
        gather_kernel, "gather_sums", [((shard, 2 * LATENT_DIM), F32)], "v", flops=2**17, moved=2**20
    )(term.reshape(halves, GROUP, members_num, shard, 2 * COLS))

    if members_num == 2:
        got = jnp.roll(swap(prediction, "ens", 1), part, axis=1)
        lane = lax.broadcasted_iota(jnp.int32, prediction.shape, 1)
        prediction = jnp.where(lane // part == ens, prediction, got)
    else:
        prediction = prediction.reshape(FIELD_NUM, members_num, part).transpose(1, 0, 2)
        prediction = exchange(prediction, "ens").transpose(1, 0, 2)
    return (prediction.reshape(1, FIELD_NUM, node_rows), grad_kv)


def solution(mesh):
    space, ens = mesh.shape["space"], mesh.shape["ens"]
    split = Mesh(
        mesh.devices.reshape(space // GROUP, QUAD, CORES, ens), ("half", "quad", "core", "ens")
    )
    nodes = ("half", "quad", "core")
    shards = nodes + ("ens",)
    in_specs = (
        P("ens", nodes, None),
        P(shards, None),
        P(shards, None),
        P(shards, None),
        P(None, nodes),
        P(nodes),
        P(nodes, None),
    )
    out_specs = (P("ens", None, nodes), P(shards, None))
    return jax.shard_map(body, mesh=split, in_specs=in_specs, out_specs=out_specs, check_vma=False)
```

```python
import functools

import jax
import jax.numpy as jnp
from jax import lax
from jax.experimental import pallas as pl
from jax.experimental.pallas import tpu as pltpu
from jax.sharding import Mesh
from jax.sharding import PartitionSpec as P

LATENT_DIM = 1024
HEADS = 16
HEAD = 64
FIELD_NUM = 100
TILE = 64
RADIUS = 2
K_NB = 4
QUAD = 4
CORES = 2
GROUP = QUAD * CORES
COLS = LATENT_DIM // GROUP
RIM = RADIUS * TILE
FIELD_PAD = 128
PAIR = 2
WINDOW = (PAIR + 2 * RADIUS) * TILE
NOWHERE = 100
NOTE_ROWS = 16
CHUNKS = 4

NORM_EPS = 1e-06
SOFT_WIDTH = 0.0625
MASKED = -1e30

F32 = jnp.float32
BF16 = jnp.bfloat16

VMEM = pl.BlockSpec(memory_space=pltpu.VMEM)
SMEM = pl.BlockSpec(memory_space=pltpu.SMEM)
HBM = pl.BlockSpec(memory_space=pltpu.HBM)
ANYWHERE = pl.BlockSpec(memory_space=pl.ANY)
OVER_ROWS = (((0,), (0,)), ((), ()))
OVER_COLUMNS = (((1,), (1,)), ((), ()))


def call(kernel, name, outs, ins, scratch=(), flops=0, moved=0, exps=0, room=8, results=None):
    results = results or "v" * len(outs)
    spaces = {"s": SMEM, "v": VMEM, "h": HBM, "a": ANYWHERE}
    made = pl.pallas_call(
        kernel,
        out_shape=[
            pltpu.HBM(shape, kind) if space == "h" else jax.ShapeDtypeStruct(shape, kind)
            for (shape, kind), space in zip(outs, results)
        ],
        in_specs=[spaces[space] for space in ins],
        out_specs=[spaces[space] for space in results],
        scratch_shapes=list(scratch),
        compiler_params=pltpu.CompilerParams(vmem_limit_bytes=room * 2**20),
        cost_estimate=pl.CostEstimate(flops=flops, bytes_accessed=moved, transcendentals=exps),
        name=name,
    )

    def run(*args):
        return made(
            *[
                pltpu.with_memory_space_constraint(arg, pltpu.HBM) if space == "h" else arg
                for arg, space in zip(args, ins)
            ]
        )

    return run


def fetch(pairs, sems, first=0):
    copies = [
        pltpu.make_async_copy(source, target, sems.at[first + at])
        for at, (source, target) in enumerate(pairs)
    ]
    for copy in copies:
        copy.start()
    return copies


def wait(copies):
    for copy in copies:
        copy.wait()


def weights_kernel(w_any, mix_any, readout_any, columns_any, packed_any, *refs):
    w, columns, readout, packed, sems = refs
    copies = fetch(
        [(w_any, w), (readout_any, readout), (mix_any, packed.at[:, :LATENT_DIM])], sems
    )
    copies[0].wait()
    for g in range(GROUP):
        for part in range(3):
            at = (part * GROUP + g) * COLS
            columns[g, :, part * COLS : (part + 1) * COLS] = w[:, at : at + COLS]
    halves, _, members_num = columns_any.shape[:3]
    out = fetch(
        [
            (columns, columns_any.at[half, :, m])
            for half in range(halves)
            for m in range(members_num)
        ],
        sems,
        3,
    )
    wait(copies[1:])
    packed[:, LATENT_DIM:] = jnp.zeros((packed.shape[0], FIELD_PAD), BF16)
    packed[:, LATENT_DIM : LATENT_DIM + FIELD_NUM] = readout[...]
    wait(out + fetch([(packed, packed_any)], sems, 3 + len(out)))


def norm_kernel(near_any, source_any, normed_any, *refs):
    parts, (near, source, normed, sems) = refs[:-4], refs[-4:]
    ens = lax.axis_index("ens")
    copies = fetch([(source_any, source), (near_any, near)], sems)
    rows = source.shape[0]
    copies[0].wait()
    moves = []
    for step, part_any in enumerate(parts):
        count, part, _ = part_any.shape
        for m in range(count):
            place = (ens ^ step) if len(parts) == 2 else m
            place = pl.multiple_of(place * part, part)
            moves.append((source.at[pl.ds(place, part)], part_any.at[m]))
    out = fetch(moves, sems, 2)
    states = source[...].astype(F32)
    inverse = lax.rsqrt(jnp.mean(states * states, axis=-1, keepdims=True) + NORM_EPS)
    normed[:rows, :] = (states * inverse).astype(BF16)
    copies[1].wait()
    row = lax.broadcasted_iota(jnp.int32, (NOTE_ROWS, 128), 0)
    lane = lax.broadcasted_iota(jnp.int32, (NOTE_ROWS, 128), 1)
    note = jnp.zeros((NOTE_ROWS, 128), F32)
    tiles = near.shape[0]
    first_tile = lax.axis_index(("half", "quad", "core")) * tiles
    for tile in range(tiles):
        for slot in range(K_NB):
            at = near[tile, slot]
            step = jnp.where(at >= 0, at - first_tile - tile, NOWHERE).astype(F32)
            note = jnp.where((row == tile) & (lane == slot), step, note)
    normed[rows:, :] = jnp.zeros((NOTE_ROWS, LATENT_DIM), BF16)
    normed[rows:, :128] = note.astype(BF16)
    wait(out + fetch([(normed, normed_any)], sems, 2 + len(out)))


def attach_kernel(packed_ref, sent_any, out_ref, sems):
    width, shard = packed_ref.shape[2], packed_ref.shape[1]
    pairs = [
        (sent_any.at[0, pl.ds(at * shard, shard)], out_ref.at[at, :, width:]) for at in range(2)
    ]
    copies = fetch(pairs, sems)
    out_ref[:, :, :width] = packed_ref[...]
    wait(copies)


def merge_members_kernel(mine_ref, other_ref, packed_ref, source_ref):
    ens = lax.axis_index("ens")
    width = packed_ref.shape[3]
    for half in range(2):
        packed_ref[half, ens] = mine_ref[half, :, :width]
        packed_ref[half, ens ^ 1] = other_ref[half, :, :width]
    source_ref[...] = other_ref[:, :, width:].reshape(source_ref.shape)


def owners():
    core, quad = lax.axis_index("core"), lax.axis_index("quad")
    return [(quad ^ step) * CORES + (core ^ flip) for flip in range(CORES) for step in range(QUAD)]


def collect_kernel(*refs):
    blocks, (normed_any, steps_ref, notes, sems) = refs[:GROUP], refs[GROUP:]
    block = blocks[0].shape[0] - NOTE_ROWS
    pairs = []
    for rows_ref, owner in zip(blocks, owners()):
        place = pl.ds(pl.multiple_of(owner * block, block), block)
        pairs.append((rows_ref.at[:block], normed_any.at[place]))
        pairs.append((rows_ref.at[block:, :128], notes.at[owner]))
    wait(fetch(pairs, sems))
    steps_ref[...] = notes[...].astype(F32)


def put_rims(rims, first, last):
    if len(rims) == 1:
        rims[0][...] = jnp.where(lax.axis_index("half") == 0, last, first)
    else:
        rims[0][...], rims[1][...] = first, last


def rims_kernel(normed_any, *refs):
    rows, sems = refs[-2:]
    if len(refs[0].shape) == 2:
        columns, w, rims = refs[:1], refs[1], refs[2:-2]
        pairs = [(columns[0], w)]
    else:
        columns, w, rims = refs[:2], refs[2], refs[3:-2]
        ens = lax.axis_index("ens")
        pairs = [(part, w.at[:, ens ^ step]) for step, part in enumerate(columns)]
    last = normed_any.shape[0] - RIM
    if len(rims) == 1:
        place = pl.multiple_of(jnp.where(lax.axis_index("half") == 0, last, 0), RIM)
        pairs.append((normed_any.at[pl.ds(place, RIM)], rows.at[0]))
    else:
        pairs += [(normed_any.at[:RIM], rows.at[0]), (normed_any.at[last:], rows.at[1])]
    wait(fetch(pairs, sems))
    weights = w[...].reshape(LATENT_DIM, 3 * COLS)[:, COLS:]
    for at, rim_ref in enumerate(rims):
        rim_ref[...] = jnp.dot(rows[at], weights, preferred_element_type=F32).astype(BF16)


def project_kernel(normed_any, w_ref, q_ref, kv_ref, normed, sems):
    chunk = normed.shape[0] // CHUNKS
    rows = [slice(at * chunk, (at + 1) * chunk) for at in range(CHUNKS)]
    copies = fetch([(normed_any.at[part], normed.at[part]) for part in rows], sems)
    weights = w_ref[...].reshape(LATENT_DIM, 3 * COLS)
    for part, copy in zip(rows, copies):
        copy.wait()
        projected = jnp.dot(normed[part, :], weights, preferred_element_type=F32).astype(BF16)
        q_ref[part, :] = projected[:, :COLS] * jnp.asarray(HEAD**-0.5, BF16)
        kv_ref[part, :] = projected[:, COLS:]


def assemble_kernel(*refs):
    pieces, (w_any, sems) = refs[:GROUP], refs[GROUP:]
    core, quad = lax.axis_index("core"), lax.axis_index("quad")
    pairs = [
        (piece, w_any.at[:, quad ^ (at % QUAD), core ^ (at // QUAD)])
        for at, piece in enumerate(pieces)
    ]
    wait(fetch(pairs, sems))


def by_head(rows):
    lane = lax.broadcasted_iota(jnp.int32, rows.shape, 1)
    zero = jnp.zeros_like(rows)
    return jnp.concatenate(
        [jnp.where(lane < HEAD, rows, zero), jnp.where(lane < HEAD, zero, rows)], axis=0
    )


def usable_keys(steps_ref, pair):
    lane = (lax.broadcasted_iota(jnp.int32, (1, WINDOW), 1) // TILE - RADIUS).astype(F32)
    masks = []
    for query_tile in range(PAIR):
        found = jnp.zeros((1, WINDOW), F32)
        for slot in range(K_NB):
            step = steps_ref[pair, query_tile : query_tile + 1, slot : slot + 1]
            found = jnp.where(lane - query_tile == step, 1.0, found)
        masks.append(found)
    row = lax.broadcasted_iota(jnp.int32, (2 * PAIR * TILE, 1), 0) // TILE % PAIR
    return jnp.where(row == 0, masks[0], masks[1]) > 0


def raised_scores(queries, keys, usable):
    scores = lax.dot_general(queries, keys, OVER_COLUMNS, preferred_element_type=F32)
    scores = jnp.where(usable, scores, MASKED)
    raised = jnp.exp(scores - jnp.max(scores, axis=-1, keepdims=True))
    return raised, 1.0 / jnp.sum(raised, axis=-1, keepdims=True)


def attend(steps_ref, pair, queries, keys, values):
    raised, share = raised_scores(by_head(queries), keys, usable_keys(steps_ref, pair))
    both = jnp.dot(raised.astype(BF16), values, preferred_element_type=F32) * share
    lane = lax.broadcasted_iota(jnp.int32, queries.shape, 1)
    half = PAIR * TILE
    return jnp.where(lane < HEAD, both[:half], both[half:]).astype(BF16)


def interior_kernel(steps_ref, q_ref, kv_ref, out_ref):
    step = PAIR * TILE
    pairs = q_ref.shape[0] // step
    for pair in range(1, pairs - 1):
        window = slice((pair - 1) * step, (pair + 2) * step)
        rows = slice(pair * step, (pair + 1) * step)
        out_ref[rows, :] = attend(
            steps_ref, pair, q_ref[rows, :], kv_ref[window, :COLS], kv_ref[window, COLS:]
        )


def edge_kernel(steps_ref, q_ref, kv_ref, low_ref, high_ref, done_ref, out_ref):
    step = PAIR * TILE
    count = q_ref.shape[0]
    pairs = count // step
    out_ref[step : count - step, :] = done_ref[step : count - step, :]
    first = jnp.concatenate([low_ref[...], kv_ref[: 2 * step, :]], axis=0)
    last = jnp.concatenate([kv_ref[count - 2 * step :, :], high_ref[...]], axis=0)
    for pair, window in ((0, first), (pairs - 1, last)):
        rows = slice(pair * step, (pair + 1) * step)
        out_ref[rows, :] = attend(
            steps_ref, pair, q_ref[rows, :], window[:, :COLS], window[:, COLS:]
        )


def attend_back(steps_ref, pair, queries, grads, keys, values):
    queries, grads = by_head(queries), by_head(grads)
    raised, share = raised_scores(queries, keys, usable_keys(steps_ref, pair))
    probs = raised * share
    grad_probs = lax.dot_general(grads, values, OVER_COLUMNS, preferred_element_type=F32)
    row_delta = jnp.sum(probs * grad_probs, axis=-1, keepdims=True)
    grad_scores = (probs * (grad_probs - row_delta)).astype(BF16)
    key_grad = lax.dot_general(grad_scores, queries, OVER_ROWS, preferred_element_type=F32)
    value_grad = lax.dot_general(probs.astype(BF16), grads, OVER_ROWS, preferred_element_type=F32)
    return key_grad, value_grad


def edge_back_kernel(
    steps_ref, q_ref, kv_ref, low_ref, high_ref, g_ref, part_ref, *rims
):
    outer = []
    step = PAIR * TILE
    count = q_ref.shape[0]
    first = jnp.concatenate([low_ref[...], kv_ref[: 2 * step, :]], axis=0)
    last = jnp.concatenate([kv_ref[count - 2 * step :, :], high_ref[...]], axis=0)
    pairs = count // step
    for edge, pair, window in ((0, 0, first), (1, pairs - 1, last)):
        rows = slice(pair * step, (pair + 1) * step)
        grads = attend_back(
            steps_ref, pair, q_ref[rows, :], g_ref[rows, :], window[:, :COLS], window[:, COLS:]
        )
        rim = slice(0, RIM) if edge == 0 else slice(WINDOW - RIM, WINDOW)
        own = slice(RIM, WINDOW) if edge == 0 else slice(0, WINDOW - RIM)
        for at, grad in enumerate(grads):
            columns = slice(at * COLS, (at + 1) * COLS)
            part_ref[edge, :, columns] = grad[own]
        outer.append(jnp.concatenate([grad[rim].astype(BF16) for grad in grads], axis=1))
    put_rims(rims, *outer)


def interior_back_kernel(steps_ref, q_ref, kv_ref, g_ref, part_ref, out_ref):
    step = PAIR * TILE
    count = q_ref.shape[0]
    pairs = count // step
    reach = 2 * step
    out_ref[:reach, :] = part_ref[0]
    out_ref[reach : count - reach, :] = jnp.zeros((count - 2 * reach, 2 * COLS), F32)
    out_ref[count - reach :, :] = part_ref[1]
    for pair in range(1, pairs - 1):
        window = slice((pair - 1) * step, (pair + 2) * step)
        rows = slice(pair * step, (pair + 1) * step)
        key_grad, value_grad = attend_back(
            steps_ref,
            pair,
            q_ref[rows, :],
            g_ref[rows, :],
            kv_ref[window, :COLS],
            kv_ref[window, COLS:],
        )
        out_ref[window, :COLS] += key_grad
        out_ref[window, COLS:] += value_grad


def slope(spread):
    return spread * lax.rsqrt(spread * spread + SOFT_WIDTH)


def mix_kernel(att_ref, factor_ref, truth_any, w_any, *refs):
    sources, refs = refs[:-8], refs[-8:]
    pred_ref, grad_ref, a, truth_ref, truth, source, w, sems = refs
    members_num, part, _ = source.shape
    halves = w.shape[0]
    ens = lax.axis_index("ens")
    copies = fetch([(w_any.at[0], w.at[0])], sems)
    pairs = [(truth_any, truth_ref)]
    if len(sources) == 1:
        pairs.append((sources[0], source))
    else:
        pairs += [(rows.at[0], source.at[ens ^ step]) for step, rows in enumerate(sources)]
    others = fetch(pairs, sems, halves)
    for g in range(GROUP):
        for m in range(members_num):
            a[m * part : (m + 1) * part, g * COLS : (g + 1) * COLS] = att_ref[g * members_num + m]
    wait(others)
    lane_part = lax.broadcasted_iota(jnp.int32, (1, a.shape[0]), 1) // part
    own_truth, own_factor = truth_ref[...], factor_ref[...]
    for turn in range(1, members_num):
        at = lane_part - turn
        here = jnp.where(at < 0, at + members_num, at) == ens
        own_truth = jnp.where(here, pltpu.roll(truth_ref[...], turn * part, 1), own_truth)
        own_factor = jnp.where(here, pltpu.roll(factor_ref[...], turn * part, 1), own_factor)
    truth[...] = jnp.zeros_like(truth)
    truth[:FIELD_NUM, :] = own_truth
    hidden = source[...].reshape(a.shape).astype(F32)
    count = LATENT_DIM // halves
    for half in range(halves):
        copies[half].wait()
        if half + 1 < halves:
            copies += fetch([(w_any.at[half + 1], w.at[half + 1])], sems, half + 1)
        mix = w[half].reshape(count, LATENT_DIM + FIELD_PAD)[:, :LATENT_DIM]
        hidden += jnp.dot(
            a[:, half * count : (half + 1) * count], mix, preferred_element_type=F32
        )
    both = w[...].reshape(LATENT_DIM, LATENT_DIM + FIELD_PAD)
    mix, readout = both[:, :LATENT_DIM], both[:, LATENT_DIM:]
    inverse = lax.rsqrt(jnp.mean(hidden * hidden, axis=-1, keepdims=True) + NORM_EPS)
    decoded = (hidden * inverse).astype(BF16)
    prediction = lax.dot_general(
        readout, decoded, (((0,), (1,)), ((), ())), preferred_element_type=F32
    )
    pred_ref[...] = prediction[:FIELD_NUM]
    spread = jnp.zeros_like(prediction)
    for other in range(1, members_num):
        spread = spread + slope(prediction - pltpu.roll(prediction, other * part, 1))
    derivative = own_factor / FIELD_NUM * (
        slope(prediction - truth[...]) - spread / (members_num - 1)
    )
    grad_decoded = lax.dot_general(
        derivative.astype(BF16), readout, (((0,), (1,)), ((), ())), preferred_element_type=F32
    )
    grad_hidden = inverse * grad_decoded - hidden * inverse**3 * jnp.mean(
        grad_decoded * hidden, axis=-1, keepdims=True
    )
    grads = lax.dot_general(
        grad_hidden.astype(BF16), mix, OVER_COLUMNS, preferred_element_type=F32
    ).astype(BF16)
    for g in range(GROUP):
        for m in range(members_num):
            grad_ref[g * members_num + m] = grads[
                m * part : (m + 1) * part, g * COLS : (g + 1) * COLS
            ]


def product_kernel(normed_ref, grads_ref, out_ref):
    grads = grads_ref[...]
    high = grads.astype(BF16)
    low = (grads - high.astype(F32)).astype(BF16)
    both = lax.dot_general(
        normed_ref[...], jnp.concatenate([high, low], axis=1), OVER_ROWS, preferred_element_type=F32
    )
    out_ref[...] = both[:, : 2 * COLS] + both[:, 2 * COLS :]


def rim_product_kernel(normed_ref, total_ref, *refs):
    arrived, out_ref = refs[:-1], refs[-1]
    last_row = normed_ref.shape[0] - RIM
    half, last = lax.axis_index("half"), lax.axis_size("half") - 1
    if len(arrived) == 1:
        places = [pl.multiple_of(jnp.where(half == 0, last_row, 0), RIM)]
    else:
        places = [0, last_row]
    total = total_ref[...]
    for at, arrived_ref in enumerate(arrived):
        grads = arrived_ref[...]
        if len(arrived) == 2:
            grads = jnp.where((half > 0) if at == 0 else (half < last), grads.astype(F32), 0.0)
            grads = grads.astype(BF16)
        rows = normed_ref[pl.ds(places[at], RIM), :]
        total += lax.dot_general(rows, grads, OVER_ROWS, preferred_element_type=F32)
    out_ref[...] = total.astype(BF16)


def gather_kernel(parts_ref, out_ref):
    halves, _, members_num = parts_ref.shape[:3]
    for g in range(GROUP):
        total = None
        for half in range(halves):
            for m in range(members_num):
                part = parts_ref[half, g, m].astype(F32)
                total = part if total is None else total + part
        out_ref[:, g * COLS : (g + 1) * COLS] = total[:, :COLS]
        out_ref[:, LATENT_DIM + g * COLS : LATENT_DIM + (g + 1) * COLS] = total[:, COLS:]


def exchange(chunks, axes):
    return lax.all_to_all(chunks, axes, 0, 0)


def swap(value, axis, step):
    return lax.ppermute(value, axis, [(i, i ^ step) for i in range(lax.axis_size(axis))])


def in_order(mine, axis, at):
    if lax.axis_size(axis) != 2:
        return lax.all_gather(mine, axis, axis=at)
    other = swap(mine, axis, 1)
    first = lax.axis_index(axis) == 0
    return jnp.stack([jnp.where(first, mine, other), jnp.where(first, other, mine)], axis=at)


def body(members, w_attn, w_mix, readout_matrix, observed_truth, cell_surface_factor, neighbours):
    halves, members_num = lax.axis_size("half"), lax.axis_size("ens")
    nodes = ("half", "quad", "core")
    everyone = nodes + ("ens",)
    shard = w_attn.shape[0]
    node_rows = members.shape[1]
    rows = GROUP * node_rows
    part = node_rows // members_num
    up = [(i, i + 1) for i in range(halves - 1)]
    down = [(target, source) for source, target in up]
    ens = lax.axis_index("ens")
    width = LATENT_DIM + FIELD_PAD
    paired = members_num == 2
    copies = 1 if paired else members_num
    source_parts = 2 if paired else 1

    columns, packed = call(
        weights_kernel,
        "prepare_weights",
        [((halves, GROUP, copies, shard, 3 * COLS), BF16), ((shard, width), BF16)],
        "hhh",
        [
            pltpu.VMEM(w_attn.shape, BF16),
            pltpu.VMEM((GROUP, shard, 3 * COLS), BF16),
            pltpu.VMEM(readout_matrix.shape, BF16),
            pltpu.VMEM((shard, width), BF16),
            pltpu.SemaphoreType.DMA((4 + halves * copies,)),
        ],
        moved=2**20,
        results="hh",
    )(w_attn, w_mix, readout_matrix)
    normed, *sources = call(
        norm_kernel,
        "norm",
        [((node_rows + NOTE_ROWS, LATENT_DIM), BF16)]
        + [((1 if paired else members_num, part, LATENT_DIM), BF16)] * source_parts,
        "hh",
        [
            pltpu.SMEM(neighbours.shape, jnp.int32),
            pltpu.VMEM((node_rows, LATENT_DIM), BF16),
            pltpu.VMEM((node_rows + NOTE_ROWS, LATENT_DIM), BF16),
            pltpu.SemaphoreType.DMA((3 + max(2, members_num),)),
        ],
        flops=2**20,
        moved=2**20,
        results="h" + "h" * source_parts,
    )(neighbours, members.reshape(node_rows, LATENT_DIM))

    packed, normed = lax.optimization_barrier((in_order(packed, "half", 0), normed))
    square = paired and halves == 2 and shard % 16 == 0
    near = [normed, swap(normed, "quad", 1), None, swap(normed, "quad", 3)]
    if paired:
        columns = exchange(columns.reshape(-1, shard, 3 * COLS), nodes)
        if square:
            (wide,) = call(
                attach_kernel,
                "attach_sources",
                [((2, shard, width + LATENT_DIM), BF16)],
                "vh",
                [pltpu.SemaphoreType.DMA((2,))],
                moved=2**19,
            )(packed, sources[1])
            columns, late, wide = lax.optimization_barrier((columns, normed, wide))
        else:
            columns, late = lax.optimization_barrier((columns, normed))
        columns = [columns, swap(columns, "ens", 1)]
    else:
        columns = [exchange(columns.reshape(-1, shard, 3 * COLS), everyone)]
        columns = [columns[0].reshape(LATENT_DIM, 3 * COLS)]
        late = normed
    near[2] = swap(late, "quad", 2)
    near = list(lax.optimization_barrier(tuple(near)))
    far = [swap(piece, "core", 1) for piece in near]
    normed, steps = call(
        collect_kernel,
        "collect",
        [((rows, LATENT_DIM), BF16), ((GROUP, NOTE_ROWS, 128), F32)],
        "a" * (2 * QUAD),
        [pltpu.VMEM((GROUP, NOTE_ROWS, 128), BF16), pltpu.SemaphoreType.DMA((2 * GROUP,))],
        moved=4 * 2**20,
        results="hv",
    )(*near, *far)

    if square:
        packed, arrived = call(
            merge_members_kernel,
            "merge_members",
            [((2, 2, shard, width), BF16), ((1, part, LATENT_DIM), BF16)],
            "vv",
            moved=2**19,
        )(wide, swap(wide, "ens", 1))
        packed = packed.reshape(2, 2 * shard, width)
        sources = [sources[0], arrived]
    else:
        packed = in_order(packed, "ens", 1).reshape(halves, members_num * shard, width)
    packed, near[2] = lax.optimization_barrier((packed, near[2]))
    pieces = [packed] + [swap(packed, "quad", step) for step in range(1, QUAD)]

    rim = ((RIM, 2 * COLS), BF16)
    rims = [rim] if halves == 2 else [rim, rim]
    w_shape = (GROUP * halves, 2, shard, 3 * COLS) if paired else (LATENT_DIM, 3 * COLS)
    weights, *inner = call(
        rims_kernel,
        "project_rims",
        [(w_shape, BF16)] + rims,
        "h" + "a" * len(columns),
        [pltpu.VMEM((len(rims), RIM, LATENT_DIM), BF16), pltpu.SemaphoreType.DMA((4,))],
        flops=RIM * LATENT_DIM * 4 * COLS,
        moved=2**20,
    )(normed, *columns)
    def across(inner):
        if halves == 2:
            got = swap(inner[0], "half", 1)
            return got, got
        return lax.ppermute(inner[1], "half", up), lax.ppermute(inner[0], "half", down)

    if not paired:
        sources = [exchange(sources[0], "ens")]
    elif not square:
        sources = [sources[0], swap(sources[1], "ens", 1)]
    low, high = across(inner)
    queries, own = call(
        project_kernel,
        "project",
        [((rows, COLS), BF16), ((rows, 2 * COLS), BF16)],
        "hv",
        [pltpu.VMEM((rows, LATENT_DIM), BF16), pltpu.SemaphoreType.DMA((CHUNKS,))],
        flops=rows * LATENT_DIM * 6 * COLS,
        moved=4 * 2**20,
    )(normed, weights)

    (outcome,) = call(
        interior_kernel,
        "attention_interior",
        [((rows, COLS), BF16)],
        "vvv",
        flops=rows * COLS * 2048,
        moved=2**21,
        exps=rows * 512,
    )(steps, queries, own)
    (outcome,) = call(
        edge_kernel,
        "attention_edges",
        [((rows, COLS), BF16)],
        "vvvvvv",
        flops=rows * COLS * 512,
        moved=2**20,
        exps=rows * 128,
    )(steps, queries, own, low, high, outcome)
    *pieces, own = lax.optimization_barrier((*pieces, own))
    pieces = pieces + [swap(piece, "core", 1) for piece in pieces]
    attended = exchange(outcome.reshape(GROUP * members_num, part, COLS), ("quad", "core", "ens"))
    block = (halves, QUAD, CORES, members_num * shard, width)
    (weights,) = call(
        assemble_kernel,
        "assemble",
        [(block, BF16)],
        "a" * len(pieces),
        [pltpu.SemaphoreType.DMA((GROUP,))],
        moved=4 * 2**20,
        results="h",
    )(*pieces)

    prediction, grads = call(
        mix_kernel,
        "mix_loss_backward",
        [((FIELD_NUM, node_rows), F32), ((GROUP * members_num, part, COLS), BF16)],
        "vvhh" + "a" * len(sources),
        [
            pltpu.VMEM((node_rows, LATENT_DIM), BF16),
            pltpu.VMEM(observed_truth.shape, F32),
            pltpu.VMEM((FIELD_PAD, node_rows), F32),
            pltpu.VMEM((members_num, part, LATENT_DIM), BF16),
            pltpu.VMEM(block, BF16),
            pltpu.SemaphoreType.DMA((halves + 1 + len(sources),)),
        ],
        flops=node_rows * LATENT_DIM * 4 * width,
        moved=2**22,
        room=14,
    )(attended, cell_surface_factor[None], observed_truth, weights, *sources)
    grads = exchange(grads, ("quad", "core", "ens")).reshape(rows, COLS)

    edges, *inner = call(
        edge_back_kernel,
        "attention_edges_back",
        [((2, WINDOW - RIM, 2 * COLS), F32)] + rims,
        "vvvvvv",
        flops=rows * COLS * 1280,
        moved=2**20,
        exps=rows * 128,
    )(steps, queries, own, low, high, grads)
    from_low, from_high = across(inner)
    (kv_grads,) = call(
        interior_back_kernel,
        "attention_interior_back",
        [((rows, 2 * COLS), F32)],
        "vvvvv",
        flops=rows * COLS * 4096,
        moved=2**22,
        exps=rows * 512,
        room=10,
    )(steps, queries, own, grads, edges)
    (total,) = call(
        product_kernel,
        "product",
        [((LATENT_DIM, 2 * COLS), F32)],
        "vv",
        room=16,
    )(normed, kv_grads)
    arrived = [from_low] if halves == 2 else [from_low, from_high]
    (term,) = call(
        rim_product_kernel,
        "product_rims",
        [((LATENT_DIM, 2 * COLS), BF16)],
        "vv" + "v" * len(arrived),
        flops=RIM * LATENT_DIM * 4 * COLS,
        moved=2**21,
        room=16,
    )(normed, total, *arrived)
    term, prediction = lax.optimization_barrier((term, prediction))
    term = exchange(term.reshape(-1, shard, 2 * COLS), everyone)
    (grad_kv,) = call(
        gather_kernel, "gather_sums", [((shard, 2 * LATENT_DIM), F32)], "v", flops=2**17, moved=2**20
    )(term.reshape(halves, GROUP, members_num, shard, 2 * COLS))

    if members_num == 2:
        got = jnp.roll(swap(prediction, "ens", 1), part, axis=1)
        lane = lax.broadcasted_iota(jnp.int32, prediction.shape, 1)
        prediction = jnp.where(lane // part == ens, prediction, got)
    else:
        prediction = prediction.reshape(FIELD_NUM, members_num, part).transpose(1, 0, 2)
        prediction = exchange(prediction, "ens").transpose(1, 0, 2)
    return (prediction.reshape(1, FIELD_NUM, node_rows), grad_kv)


def solution(mesh):
    space, ens = mesh.shape["space"], mesh.shape["ens"]
    split = Mesh(
        mesh.devices.reshape(space // GROUP, QUAD, CORES, ens), ("half", "quad", "core", "ens")
    )
    nodes = ("half", "quad", "core")
    shards = nodes + ("ens",)
    in_specs = (
        P("ens", nodes, None),
        P(shards, None),
        P(shards, None),
        P(shards, None),
        P(None, nodes),
        P(nodes),
        P(nodes, None),
    )
    out_specs = (P("ens", None, nodes), P(shards, None))
    return jax.shard_map(body, mesh=split, in_specs=in_specs, out_specs=out_specs, check_vma=False)
```

```python
import functools

import jax
import jax.numpy as jnp
from jax import lax
from jax.experimental import pallas as pl
from jax.experimental.pallas import tpu as pltpu
from jax.sharding import Mesh
from jax.sharding import PartitionSpec as P

LATENT_DIM = 1024
HEADS = 16
HEAD = 64
FIELD_NUM = 100
TILE = 64
RADIUS = 2
K_NB = 4
QUAD = 4
CORES = 2
GROUP = QUAD * CORES
COLS = LATENT_DIM // GROUP
RIM = RADIUS * TILE
FIELD_PAD = 128
PAIR = 2
WINDOW = (PAIR + 2 * RADIUS) * TILE
NOWHERE = 100
NOTE_ROWS = 16
CHUNKS = 4

NORM_EPS = 1e-06
SOFT_WIDTH = 0.0625
MASKED = -1e30

F32 = jnp.float32
BF16 = jnp.bfloat16

VMEM = pl.BlockSpec(memory_space=pltpu.VMEM)
SMEM = pl.BlockSpec(memory_space=pltpu.SMEM)
HBM = pl.BlockSpec(memory_space=pltpu.HBM)
ANYWHERE = pl.BlockSpec(memory_space=pl.ANY)
OVER_ROWS = (((0,), (0,)), ((), ()))
OVER_COLUMNS = (((1,), (1,)), ((), ()))


def call(kernel, name, outs, ins, scratch=(), flops=0, moved=0, exps=0, room=8, results=None):
    results = results or "v" * len(outs)
    spaces = {"s": SMEM, "v": VMEM, "h": HBM, "a": ANYWHERE}
    made = pl.pallas_call(
        kernel,
        out_shape=[
            pltpu.HBM(shape, kind) if space == "h" else jax.ShapeDtypeStruct(shape, kind)
            for (shape, kind), space in zip(outs, results)
        ],
        in_specs=[spaces[space] for space in ins],
        out_specs=[spaces[space] for space in results],
        scratch_shapes=list(scratch),
        compiler_params=pltpu.CompilerParams(vmem_limit_bytes=room * 2**20),
        cost_estimate=pl.CostEstimate(flops=flops, bytes_accessed=moved, transcendentals=exps),
        name=name,
    )

    def run(*args):
        return made(
            *[
                pltpu.with_memory_space_constraint(arg, pltpu.HBM) if space == "h" else arg
                for arg, space in zip(args, ins)
            ]
        )

    return run


def fetch(pairs, sems, first=0):
    copies = [
        pltpu.make_async_copy(source, target, sems.at[first + at])
        for at, (source, target) in enumerate(pairs)
    ]
    for copy in copies:
        copy.start()
    return copies


def wait(copies):
    for copy in copies:
        copy.wait()


def weights_kernel(w_any, mix_any, readout_any, columns_any, packed_any, *refs):
    w, columns, readout, packed, sems = refs
    copies = fetch(
        [(w_any, w), (readout_any, readout), (mix_any, packed.at[:, :LATENT_DIM])], sems
    )
    copies[0].wait()
    for g in range(GROUP):
        for part in range(3):
            at = (part * GROUP + g) * COLS
            columns[g, :, part * COLS : (part + 1) * COLS] = w[:, at : at + COLS]
    halves, _, members_num = columns_any.shape[:3]
    out = fetch(
        [
            (columns, columns_any.at[half, :, m])
            for half in range(halves)
            for m in range(members_num)
        ],
        sems,
        3,
    )
    wait(copies[1:])
    packed[:, LATENT_DIM:] = jnp.zeros((packed.shape[0], FIELD_PAD), BF16)
    packed[:, LATENT_DIM : LATENT_DIM + FIELD_NUM] = readout[...]
    wait(out + fetch([(packed, packed_any)], sems, 3 + len(out)))


def norm_kernel(near_any, source_any, normed_any, *refs):
    parts, (near, source, normed, sems) = refs[:-4], refs[-4:]
    ens = lax.axis_index("ens")
    copies = fetch([(source_any, source), (near_any, near)], sems)
    rows = source.shape[0]
    copies[0].wait()
    moves = []
    for step, part_any in enumerate(parts):
        count, part, _ = part_any.shape
        for m in range(count):
            place = (ens ^ step) if len(parts) == 2 else m
            place = pl.multiple_of(place * part, part)
            moves.append((source.at[pl.ds(place, part)], part_any.at[m]))
    out = fetch(moves, sems, 2)
    states = source[...].astype(F32)
    inverse = lax.rsqrt(jnp.mean(states * states, axis=-1, keepdims=True) + NORM_EPS)
    normed[:rows, :] = (states * inverse).astype(BF16)
    copies[1].wait()
    row = lax.broadcasted_iota(jnp.int32, (NOTE_ROWS, 128), 0)
    lane = lax.broadcasted_iota(jnp.int32, (NOTE_ROWS, 128), 1)
    note = jnp.zeros((NOTE_ROWS, 128), F32)
    tiles = near.shape[0]
    first_tile = lax.axis_index(("half", "quad", "core")) * tiles
    for tile in range(tiles):
        for slot in range(K_NB):
            at = near[tile, slot]
            step = jnp.where(at >= 0, at - first_tile - tile, NOWHERE).astype(F32)
            note = jnp.where((row == tile) & (lane == slot), step, note)
    normed[rows:, :] = jnp.zeros((NOTE_ROWS, LATENT_DIM), BF16)
    normed[rows:, :128] = note.astype(BF16)
    wait(out + fetch([(normed, normed_any)], sems, 2 + len(out)))


def attach_kernel(packed_ref, sent_any, out_ref, sems):
    width, shard = packed_ref.shape[2], packed_ref.shape[1]
    pairs = [
        (sent_any.at[0, pl.ds(at * shard, shard)], out_ref.at[at, :, width:]) for at in range(2)
    ]
    copies = fetch(pairs, sems)
    out_ref[:, :, :width] = packed_ref[...]
    wait(copies)


def merge_members_kernel(mine_ref, other_ref, packed_ref, source_ref):
    ens = lax.axis_index("ens")
    width = packed_ref.shape[3]
    for half in range(2):
        packed_ref[half, ens] = mine_ref[half, :, :width]
        packed_ref[half, ens ^ 1] = other_ref[half, :, :width]
    source_ref[...] = other_ref[:, :, width:].reshape(source_ref.shape)


def owners():
    core, quad = lax.axis_index("core"), lax.axis_index("quad")
    return [(quad ^ step) * CORES + (core ^ flip) for flip in range(CORES) for step in range(QUAD)]


def collect_kernel(*refs):
    blocks, (normed_any, steps_ref, notes, sems) = refs[:GROUP], refs[GROUP:]
    block = blocks[0].shape[0] - NOTE_ROWS
    pairs = []
    for rows_ref, owner in zip(blocks, owners()):
        place = pl.ds(pl.multiple_of(owner * block, block), block)
        pairs.append((rows_ref.at[:block], normed_any.at[place]))
        pairs.append((rows_ref.at[block:, :128], notes.at[owner]))
    wait(fetch(pairs, sems))
    steps_ref[...] = notes[...].astype(F32)


def put_rims(rims, first, last):
    if len(rims) == 1:
        rims[0][...] = jnp.where(lax.axis_index("half") == 0, last, first)
    else:
        rims[0][...], rims[1][...] = first, last


def rims_kernel(normed_any, *refs):
    rows, sems = refs[-2:]
    if len(refs[0].shape) == 2:
        columns, w, rims = refs[:1], refs[1], refs[2:-2]
        pairs = [(columns[0], w)]
    else:
        columns, w, rims = refs[:2], refs[2], refs[3:-2]
        ens = lax.axis_index("ens")
        pairs = [(part, w.at[:, ens ^ step]) for step, part in enumerate(columns)]
    last = normed_any.shape[0] - RIM
    if len(rims) == 1:
        place = pl.multiple_of(jnp.where(lax.axis_index("half") == 0, last, 0), RIM)
        pairs.append((normed_any.at[pl.ds(place, RIM)], rows.at[0]))
    else:
        pairs += [(normed_any.at[:RIM], rows.at[0]), (normed_any.at[last:], rows.at[1])]
    wait(fetch(pairs, sems))
    weights = w[...].reshape(LATENT_DIM, 3 * COLS)[:, COLS:]
    for at, rim_ref in enumerate(rims):
        rim_ref[...] = jnp.dot(rows[at], weights, preferred_element_type=F32).astype(BF16)


def project_kernel(normed_any, w_ref, q_ref, kv_ref, normed, sems):
    chunk = normed.shape[0] // CHUNKS
    rows = [slice(at * chunk, (at + 1) * chunk) for at in range(CHUNKS)]
    copies = fetch([(normed_any.at[part], normed.at[part]) for part in rows], sems)
    weights = w_ref[...].reshape(LATENT_DIM, 3 * COLS)
    for part, copy in zip(rows, copies):
        copy.wait()
        projected = jnp.dot(normed[part, :], weights, preferred_element_type=F32).astype(BF16)
        q_ref[part, :] = projected[:, :COLS] * jnp.asarray(HEAD**-0.5, BF16)
        kv_ref[part, :] = projected[:, COLS:]


def assemble_kernel(*refs):
    pieces, (w_any, sems) = refs[:GROUP], refs[GROUP:]
    core, quad = lax.axis_index("core"), lax.axis_index("quad")
    pairs = [
        (piece, w_any.at[:, quad ^ (at % QUAD), core ^ (at // QUAD)])
        for at, piece in enumerate(pieces)
    ]
    wait(fetch(pairs, sems))


def by_head(rows):
    lane = lax.broadcasted_iota(jnp.int32, rows.shape, 1)
    zero = jnp.zeros_like(rows)
    return jnp.concatenate(
        [jnp.where(lane < HEAD, rows, zero), jnp.where(lane < HEAD, zero, rows)], axis=0
    )


def usable_keys(steps_ref, pair):
    lane = (lax.broadcasted_iota(jnp.int32, (1, WINDOW), 1) // TILE - RADIUS).astype(F32)
    masks = []
    for query_tile in range(PAIR):
        found = jnp.zeros((1, WINDOW), F32)
        for slot in range(K_NB):
            step = steps_ref[pair, query_tile : query_tile + 1, slot : slot + 1]
            found = jnp.where(lane - query_tile == step, 1.0, found)
        masks.append(found)
    row = lax.broadcasted_iota(jnp.int32, (2 * PAIR * TILE, 1), 0) // TILE % PAIR
    return jnp.where(row == 0, masks[0], masks[1]) > 0


def raised_scores(queries, keys, usable):
    scores = lax.dot_general(queries, keys, OVER_COLUMNS, preferred_element_type=F32)
    scores = jnp.where(usable, scores, MASKED)
    raised = jnp.exp(scores - jnp.max(scores, axis=-1, keepdims=True))
    return raised, 1.0 / jnp.sum(raised, axis=-1, keepdims=True)


def attend(steps_ref, pair, queries, keys, values):
    raised, share = raised_scores(by_head(queries), keys, usable_keys(steps_ref, pair))
    both = jnp.dot(raised.astype(BF16), values, preferred_element_type=F32) * share
    lane = lax.broadcasted_iota(jnp.int32, queries.shape, 1)
    half = PAIR * TILE
    return jnp.where(lane < HEAD, both[:half], both[half:]).astype(BF16)


def interior_kernel(steps_ref, q_ref, kv_ref, out_ref):
    step = PAIR * TILE
    pairs = q_ref.shape[0] // step
    for pair in range(1, pairs - 1):
        window = slice((pair - 1) * step, (pair + 2) * step)
        rows = slice(pair * step, (pair + 1) * step)
        out_ref[rows, :] = attend(
            steps_ref, pair, q_ref[rows, :], kv_ref[window, :COLS], kv_ref[window, COLS:]
        )


def edge_kernel(steps_ref, q_ref, kv_ref, low_ref, high_ref, done_ref, out_ref):
    step = PAIR * TILE
    count = q_ref.shape[0]
    pairs = count // step
    out_ref[step : count - step, :] = done_ref[step : count - step, :]
    first = jnp.concatenate([low_ref[...], kv_ref[: 2 * step, :]], axis=0)
    last = jnp.concatenate([kv_ref[count - 2 * step :, :], high_ref[...]], axis=0)
    for pair, window in ((0, first), (pairs - 1, last)):
        rows = slice(pair * step, (pair + 1) * step)
        out_ref[rows, :] = attend(
            steps_ref, pair, q_ref[rows, :], window[:, :COLS], window[:, COLS:]
        )


def attend_back(steps_ref, pair, queries, grads, keys, values):
    queries, grads = by_head(queries), by_head(grads)
    raised, share = raised_scores(queries, keys, usable_keys(steps_ref, pair))
    probs = raised * share
    grad_probs = lax.dot_general(grads, values, OVER_COLUMNS, preferred_element_type=F32)
    row_delta = jnp.sum(probs * grad_probs, axis=-1, keepdims=True)
    grad_scores = (probs * (grad_probs - row_delta)).astype(BF16)
    key_grad = lax.dot_general(grad_scores, queries, OVER_ROWS, preferred_element_type=F32)
    value_grad = lax.dot_general(probs.astype(BF16), grads, OVER_ROWS, preferred_element_type=F32)
    return key_grad, value_grad


def edge_back_kernel(
    steps_ref, q_ref, kv_ref, low_ref, high_ref, g_ref, part_ref, *rims
):
    outer = []
    step = PAIR * TILE
    count = q_ref.shape[0]
    first = jnp.concatenate([low_ref[...], kv_ref[: 2 * step, :]], axis=0)
    last = jnp.concatenate([kv_ref[count - 2 * step :, :], high_ref[...]], axis=0)
    pairs = count // step
    for edge, pair, window in ((0, 0, first), (1, pairs - 1, last)):
        rows = slice(pair * step, (pair + 1) * step)
        grads = attend_back(
            steps_ref, pair, q_ref[rows, :], g_ref[rows, :], window[:, :COLS], window[:, COLS:]
        )
        rim = slice(0, RIM) if edge == 0 else slice(WINDOW - RIM, WINDOW)
        own = slice(RIM, WINDOW) if edge == 0 else slice(0, WINDOW - RIM)
        for at, grad in enumerate(grads):
            columns = slice(at * COLS, (at + 1) * COLS)
            part_ref[edge, :, columns] = grad[own]
        outer.append(jnp.concatenate([grad[rim].astype(BF16) for grad in grads], axis=1))
    put_rims(rims, *outer)


def interior_back_kernel(steps_ref, q_ref, kv_ref, g_ref, part_ref, out_ref):
    step = PAIR * TILE
    count = q_ref.shape[0]
    pairs = count // step
    reach = 2 * step
    out_ref[:reach, :] = part_ref[0]
    out_ref[reach : count - reach, :] = jnp.zeros((count - 2 * reach, 2 * COLS), F32)
    out_ref[count - reach :, :] = part_ref[1]
    for pair in range(1, pairs - 1):
        window = slice((pair - 1) * step, (pair + 2) * step)
        rows = slice(pair * step, (pair + 1) * step)
        key_grad, value_grad = attend_back(
            steps_ref,
            pair,
            q_ref[rows, :],
            g_ref[rows, :],
            kv_ref[window, :COLS],
            kv_ref[window, COLS:],
        )
        out_ref[window, :COLS] += key_grad
        out_ref[window, COLS:] += value_grad


def slope(spread):
    return spread * lax.rsqrt(spread * spread + SOFT_WIDTH)


def mix_kernel(att_ref, factor_ref, truth_any, w_any, *refs):
    sources, refs = refs[:-8], refs[-8:]
    pred_ref, grad_ref, a, truth_ref, truth, source, w, sems = refs
    members_num, part, _ = source.shape
    halves = w.shape[0]
    ens = lax.axis_index("ens")
    copies = fetch([(w_any.at[half], w.at[half]) for half in range(halves)], sems)
    pairs = [(truth_any, truth_ref)]
    if len(sources) == 1:
        pairs.append((sources[0], source))
    else:
        pairs += [(rows.at[0], source.at[ens ^ step]) for step, rows in enumerate(sources)]
    others = fetch(pairs, sems, halves)
    for g in range(GROUP):
        for m in range(members_num):
            a[m * part : (m + 1) * part, g * COLS : (g + 1) * COLS] = att_ref[g * members_num + m]
    wait(others)
    lane_part = lax.broadcasted_iota(jnp.int32, (1, a.shape[0]), 1) // part
    own_truth, own_factor = truth_ref[...], factor_ref[...]
    for turn in range(1, members_num):
        at = lane_part - turn
        here = jnp.where(at < 0, at + members_num, at) == ens
        own_truth = jnp.where(here, pltpu.roll(truth_ref[...], turn * part, 1), own_truth)
        own_factor = jnp.where(here, pltpu.roll(factor_ref[...], turn * part, 1), own_factor)
    truth[...] = jnp.zeros_like(truth)
    truth[:FIELD_NUM, :] = own_truth
    hidden = source[...].reshape(a.shape).astype(F32)
    count = LATENT_DIM // halves
    for half in range(halves):
        copies[half].wait()
        mix = w[half].reshape(count, LATENT_DIM + FIELD_PAD)[:, :LATENT_DIM]
        hidden += jnp.dot(
            a[:, half * count : (half + 1) * count], mix, preferred_element_type=F32
        )
    both = w[...].reshape(LATENT_DIM, LATENT_DIM + FIELD_PAD)
    mix, readout = both[:, :LATENT_DIM], both[:, LATENT_DIM:]
    inverse = lax.rsqrt(jnp.mean(hidden * hidden, axis=-1, keepdims=True) + NORM_EPS)
    decoded = (hidden * inverse).astype(BF16)
    prediction = lax.dot_general(
        readout, decoded, (((0,), (1,)), ((), ())), preferred_element_type=F32
    )
    pred_ref[...] = prediction[:FIELD_NUM]
    spread = jnp.zeros_like(prediction)
    for other in range(1, members_num):
        spread = spread + slope(prediction - pltpu.roll(prediction, other * part, 1))
    derivative = own_factor / FIELD_NUM * (
        slope(prediction - truth[...]) - spread / (members_num - 1)
    )
    grad_decoded = lax.dot_general(
        derivative.astype(BF16), readout, (((0,), (1,)), ((), ())), preferred_element_type=F32
    )
    grad_hidden = inverse * grad_decoded - hidden * inverse**3 * jnp.mean(
        grad_decoded * hidden, axis=-1, keepdims=True
    )
    grads = lax.dot_general(
        grad_hidden.astype(BF16), mix, OVER_COLUMNS, preferred_element_type=F32
    ).astype(BF16)
    for g in range(GROUP):
        for m in range(members_num):
            grad_ref[g * members_num + m] = grads[
                m * part : (m + 1) * part, g * COLS : (g + 1) * COLS
            ]


def product_kernel(normed_ref, grads_ref, out_ref):
    grads = grads_ref[...]
    high = grads.astype(BF16)
    low = (grads - high.astype(F32)).astype(BF16)
    both = lax.dot_general(
        normed_ref[...], jnp.concatenate([high, low], axis=1), OVER_ROWS, preferred_element_type=F32
    )
    out_ref[...] = both[:, : 2 * COLS] + both[:, 2 * COLS :]


def rim_product_kernel(normed_ref, total_ref, *refs):
    arrived, out_ref = refs[:-1], refs[-1]
    last_row = normed_ref.shape[0] - RIM
    half, last = lax.axis_index("half"), lax.axis_size("half") - 1
    if len(arrived) == 1:
        places = [pl.multiple_of(jnp.where(half == 0, last_row, 0), RIM)]
    else:
        places = [0, last_row]
    total = total_ref[...]
    for at, arrived_ref in enumerate(arrived):
        grads = arrived_ref[...]
        if len(arrived) == 2:
            grads = jnp.where((half > 0) if at == 0 else (half < last), grads.astype(F32), 0.0)
            grads = grads.astype(BF16)
        rows = normed_ref[pl.ds(places[at], RIM), :]
        total += lax.dot_general(rows, grads, OVER_ROWS, preferred_element_type=F32)
    out_ref[...] = total.astype(BF16)


def gather_kernel(parts_ref, out_ref):
    halves, _, members_num = parts_ref.shape[:3]
    for g in range(GROUP):
        total = None
        for half in range(halves):
            for m in range(members_num):
                part = parts_ref[half, g, m].astype(F32)
                total = part if total is None else total + part
        out_ref[:, g * COLS : (g + 1) * COLS] = total[:, :COLS]
        out_ref[:, LATENT_DIM + g * COLS : LATENT_DIM + (g + 1) * COLS] = total[:, COLS:]


def exchange(chunks, axes):
    return lax.all_to_all(chunks, axes, 0, 0)


def swap(value, axis, step):
    return lax.ppermute(value, axis, [(i, i ^ step) for i in range(lax.axis_size(axis))])


def in_order(mine, axis, at):
    if lax.axis_size(axis) != 2:
        return lax.all_gather(mine, axis, axis=at)
    other = swap(mine, axis, 1)
    first = lax.axis_index(axis) == 0
    return jnp.stack([jnp.where(first, mine, other), jnp.where(first, other, mine)], axis=at)


def body(members, w_attn, w_mix, readout_matrix, observed_truth, cell_surface_factor, neighbours):
    halves, members_num = lax.axis_size("half"), lax.axis_size("ens")
    nodes = ("half", "quad", "core")
    everyone = nodes + ("ens",)
    shard = w_attn.shape[0]
    node_rows = members.shape[1]
    rows = GROUP * node_rows
    part = node_rows // members_num
    up = [(i, i + 1) for i in range(halves - 1)]
    down = [(target, source) for source, target in up]
    ens = lax.axis_index("ens")
    width = LATENT_DIM + FIELD_PAD
    paired = members_num == 2
    copies = 1 if paired else members_num
    source_parts = 2 if paired else 1

    columns, packed = call(
        weights_kernel,
        "prepare_weights",
        [((halves, GROUP, copies, shard, 3 * COLS), BF16), ((shard, width), BF16)],
        "hhh",
        [
            pltpu.VMEM(w_attn.shape, BF16),
            pltpu.VMEM((GROUP, shard, 3 * COLS), BF16),
            pltpu.VMEM(readout_matrix.shape, BF16),
            pltpu.VMEM((shard, width), BF16),
            pltpu.SemaphoreType.DMA((4 + halves * copies,)),
        ],
        moved=2**20,
        results="hh",
    )(w_attn, w_mix, readout_matrix)
    normed, *sources = call(
        norm_kernel,
        "norm",
        [((node_rows + NOTE_ROWS, LATENT_DIM), BF16)]
        + [((1 if paired else members_num, part, LATENT_DIM), BF16)] * source_parts,
        "hh",
        [
            pltpu.SMEM(neighbours.shape, jnp.int32),
            pltpu.VMEM((node_rows, LATENT_DIM), BF16),
            pltpu.VMEM((node_rows + NOTE_ROWS, LATENT_DIM), BF16),
            pltpu.SemaphoreType.DMA((3 + max(2, members_num),)),
        ],
        flops=2**20,
        moved=2**20,
        results="h" + "h" * source_parts,
    )(neighbours, members.reshape(node_rows, LATENT_DIM))

    packed, normed = lax.optimization_barrier((in_order(packed, "half", 0), normed))
    square = paired and halves == 2 and shard % 16 == 0
    near = [normed, swap(normed, "quad", 1), None, swap(normed, "quad", 3)]
    if paired:
        columns = exchange(columns.reshape(-1, shard, 3 * COLS), nodes)
        if square:
            (wide,) = call(
                attach_kernel,
                "attach_sources",
                [((2, shard, width + LATENT_DIM), BF16)],
                "vh",
                [pltpu.SemaphoreType.DMA((2,))],
                moved=2**19,
            )(packed, sources[1])
            columns, late, wide = lax.optimization_barrier((columns, normed, wide))
        else:
            columns, late = lax.optimization_barrier((columns, normed))
        columns = [columns, swap(columns, "ens", 1)]
    else:
        columns = [exchange(columns.reshape(-1, shard, 3 * COLS), everyone)]
        columns = [columns[0].reshape(LATENT_DIM, 3 * COLS)]
        late = normed
    near[2] = swap(late, "quad", 2)
    near = list(lax.optimization_barrier(tuple(near)))
    far = [swap(piece, "core", 1) for piece in near]
    normed, steps = call(
        collect_kernel,
        "collect",
        [((rows, LATENT_DIM), BF16), ((GROUP, NOTE_ROWS, 128), F32)],
        "a" * (2 * QUAD),
        [pltpu.VMEM((GROUP, NOTE_ROWS, 128), BF16), pltpu.SemaphoreType.DMA((2 * GROUP,))],
        moved=4 * 2**20,
        results="hv",
    )(*near, *far)

    if square:
        packed, arrived = call(
            merge_members_kernel,
            "merge_members",
            [((2, 2, shard, width), BF16), ((1, part, LATENT_DIM), BF16)],
            "vv",
            moved=2**19,
        )(wide, swap(wide, "ens", 1))
        packed = packed.reshape(2, 2 * shard, width)
        sources = [sources[0], arrived]
    else:
        packed = in_order(packed, "ens", 1).reshape(halves, members_num * shard, width)
    packed, near[2] = lax.optimization_barrier((packed, near[2]))
    pieces = [packed] + [swap(packed, "quad", step) for step in range(1, QUAD - 1)]

    rim = ((RIM, 2 * COLS), BF16)
    rims = [rim] if halves == 2 else [rim, rim]
    w_shape = (GROUP * halves, 2, shard, 3 * COLS) if paired else (LATENT_DIM, 3 * COLS)
    weights, *inner = call(
        rims_kernel,
        "project_rims",
        [(w_shape, BF16)] + rims,
        "h" + "a" * len(columns),
        [pltpu.VMEM((len(rims), RIM, LATENT_DIM), BF16), pltpu.SemaphoreType.DMA((4,))],
        flops=RIM * LATENT_DIM * 4 * COLS,
        moved=2**20,
    )(normed, *columns)
    def across(inner):
        if halves == 2:
            got = swap(inner[0], "half", 1)
            return got, got
        return lax.ppermute(inner[1], "half", up), lax.ppermute(inner[0], "half", down)

    if not paired:
        sources = [exchange(sources[0], "ens")]
    elif not square:
        sources = [sources[0], swap(sources[1], "ens", 1)]
    low, high = across(inner)
    queries, own = call(
        project_kernel,
        "project",
        [((rows, COLS), BF16), ((rows, 2 * COLS), BF16)],
        "hv",
        [pltpu.VMEM((rows, LATENT_DIM), BF16), pltpu.SemaphoreType.DMA((CHUNKS,))],
        flops=rows * LATENT_DIM * 6 * COLS,
        moved=4 * 2**20,
    )(normed, weights)

    (outcome,) = call(
        interior_kernel,
        "attention_interior",
        [((rows, COLS), BF16)],
        "vvv",
        flops=rows * COLS * 2048,
        moved=2**21,
        exps=rows * 512,
    )(steps, queries, own)
    (outcome,) = call(
        edge_kernel,
        "attention_edges",
        [((rows, COLS), BF16)],
        "vvvvvv",
        flops=rows * COLS * 512,
        moved=2**20,
        exps=rows * 128,
    )(steps, queries, own, low, high, outcome)
    *pieces, own = lax.optimization_barrier((*pieces, own))
    packed, low = lax.optimization_barrier((packed, low))
    pieces.append(swap(packed, "quad", QUAD - 1))
    pieces = pieces + [swap(piece, "core", 1) for piece in pieces]
    attended = exchange(outcome.reshape(GROUP * members_num, part, COLS), ("quad", "core", "ens"))
    block = (halves, QUAD, CORES, members_num * shard, width)
    (weights,) = call(
        assemble_kernel,
        "assemble",
        [(block, BF16)],
        "a" * len(pieces),
        [pltpu.SemaphoreType.DMA((GROUP,))],
        moved=4 * 2**20,
        results="h",
    )(*pieces)

    prediction, grads = call(
        mix_kernel,
        "mix_loss_backward",
        [((FIELD_NUM, node_rows), F32), ((GROUP * members_num, part, COLS), BF16)],
        "vvhh" + "a" * len(sources),
        [
            pltpu.VMEM((node_rows, LATENT_DIM), BF16),
            pltpu.VMEM(observed_truth.shape, F32),
            pltpu.VMEM((FIELD_PAD, node_rows), F32),
            pltpu.VMEM((members_num, part, LATENT_DIM), BF16),
            pltpu.VMEM(block, BF16),
            pltpu.SemaphoreType.DMA((halves + 1 + len(sources),)),
        ],
        flops=node_rows * LATENT_DIM * 4 * width,
        moved=2**22,
        room=14,
    )(attended, cell_surface_factor[None], observed_truth, weights, *sources)
    grads = exchange(grads, ("quad", "core", "ens")).reshape(rows, COLS)

    edges, *inner = call(
        edge_back_kernel,
        "attention_edges_back",
        [((2, WINDOW - RIM, 2 * COLS), F32)] + rims,
        "vvvvvv",
        flops=rows * COLS * 1280,
        moved=2**20,
        exps=rows * 128,
    )(steps, queries, own, low, high, grads)
    from_low, from_high = across(inner)
    (kv_grads,) = call(
        interior_back_kernel,
        "attention_interior_back",
        [((rows, 2 * COLS), F32)],
        "vvvvv",
        flops=rows * COLS * 4096,
        moved=2**22,
        exps=rows * 512,
        room=10,
    )(steps, queries, own, grads, edges)
    (total,) = call(
        product_kernel,
        "product",
        [((LATENT_DIM, 2 * COLS), F32)],
        "vv",
        room=16,
    )(normed, kv_grads)
    arrived = [from_low] if halves == 2 else [from_low, from_high]
    (term,) = call(
        rim_product_kernel,
        "product_rims",
        [((LATENT_DIM, 2 * COLS), BF16)],
        "vv" + "v" * len(arrived),
        flops=RIM * LATENT_DIM * 4 * COLS,
        moved=2**21,
        room=16,
    )(normed, total, *arrived)
    term, prediction = lax.optimization_barrier((term, prediction))
    term = exchange(term.reshape(-1, shard, 2 * COLS), everyone)
    (grad_kv,) = call(
        gather_kernel, "gather_sums", [((shard, 2 * LATENT_DIM), F32)], "v", flops=2**17, moved=2**20
    )(term.reshape(halves, GROUP, members_num, shard, 2 * COLS))

    if members_num == 2:
        got = jnp.roll(swap(prediction, "ens", 1), part, axis=1)
        lane = lax.broadcasted_iota(jnp.int32, prediction.shape, 1)
        prediction = jnp.where(lane // part == ens, prediction, got)
    else:
        prediction = prediction.reshape(FIELD_NUM, members_num, part).transpose(1, 0, 2)
        prediction = exchange(prediction, "ens").transpose(1, 0, 2)
    return (prediction.reshape(1, FIELD_NUM, node_rows), grad_kv)


def solution(mesh):
    space, ens = mesh.shape["space"], mesh.shape["ens"]
    split = Mesh(
        mesh.devices.reshape(space // GROUP, QUAD, CORES, ens), ("half", "quad", "core", "ens")
    )
    nodes = ("half", "quad", "core")
    shards = nodes + ("ens",)
    in_specs = (
        P("ens", nodes, None),
        P(shards, None),
        P(shards, None),
        P(shards, None),
        P(None, nodes),
        P(nodes),
        P(nodes, None),
    )
    out_specs = (P("ens", None, nodes), P(shards, None))
    return jax.shard_map(body, mesh=split, in_specs=in_specs, out_specs=out_specs, check_vma=False)
```

```python
import functools

import jax
import jax.numpy as jnp
from jax import lax
from jax.experimental import pallas as pl
from jax.experimental.pallas import tpu as pltpu
from jax.sharding import Mesh
from jax.sharding import PartitionSpec as P

LATENT_DIM = 1024
HEADS = 16
HEAD = 64
FIELD_NUM = 100
TILE = 64
RADIUS = 2
K_NB = 4
QUAD = 4
CORES = 2
GROUP = QUAD * CORES
COLS = LATENT_DIM // GROUP
RIM = RADIUS * TILE
FIELD_PAD = 128
PAIR = 2
WINDOW = (PAIR + 2 * RADIUS) * TILE
NOWHERE = 100
NOTE_ROWS = 16
CHUNKS = 4

NORM_EPS = 1e-06
SOFT_WIDTH = 0.0625
MASKED = -1e30

F32 = jnp.float32
BF16 = jnp.bfloat16

VMEM = pl.BlockSpec(memory_space=pltpu.VMEM)
SMEM = pl.BlockSpec(memory_space=pltpu.SMEM)
HBM = pl.BlockSpec(memory_space=pltpu.HBM)
ANYWHERE = pl.BlockSpec(memory_space=pl.ANY)
OVER_ROWS = (((0,), (0,)), ((), ()))
OVER_COLUMNS = (((1,), (1,)), ((), ()))


def call(kernel, name, outs, ins, scratch=(), flops=0, moved=0, exps=0, room=8, results=None):
    results = results or "v" * len(outs)
    spaces = {"s": SMEM, "v": VMEM, "h": HBM, "a": ANYWHERE}
    made = pl.pallas_call(
        kernel,
        out_shape=[
            pltpu.HBM(shape, kind) if space == "h" else jax.ShapeDtypeStruct(shape, kind)
            for (shape, kind), space in zip(outs, results)
        ],
        in_specs=[spaces[space] for space in ins],
        out_specs=[spaces[space] for space in results],
        scratch_shapes=list(scratch),
        compiler_params=pltpu.CompilerParams(vmem_limit_bytes=room * 2**20),
        cost_estimate=pl.CostEstimate(flops=flops, bytes_accessed=moved, transcendentals=exps),
        name=name,
    )

    def run(*args):
        return made(
            *[
                pltpu.with_memory_space_constraint(arg, pltpu.HBM) if space == "h" else arg
                for arg, space in zip(args, ins)
            ]
        )

    return run


def fetch(pairs, sems, first=0):
    copies = [
        pltpu.make_async_copy(source, target, sems.at[first + at])
        for at, (source, target) in enumerate(pairs)
    ]
    for copy in copies:
        copy.start()
    return copies


def wait(copies):
    for copy in copies:
        copy.wait()


def weights_kernel(w_any, mix_any, readout_any, columns_any, packed_any, *refs):
    w, columns, readout, packed, sems = refs
    copies = fetch(
        [(w_any, w), (readout_any, readout), (mix_any, packed.at[:, :LATENT_DIM])], sems
    )
    copies[0].wait()
    for g in range(GROUP):
        for part in range(3):
            at = (part * GROUP + g) * COLS
            columns[g, :, part * COLS : (part + 1) * COLS] = w[:, at : at + COLS]
    halves, _, members_num = columns_any.shape[:3]
    out = fetch(
        [
            (columns, columns_any.at[half, :, m])
            for half in range(halves)
            for m in range(members_num)
        ],
        sems,
        3,
    )
    wait(copies[1:])
    packed[:, LATENT_DIM:] = jnp.zeros((packed.shape[0], FIELD_PAD), BF16)
    packed[:, LATENT_DIM : LATENT_DIM + FIELD_NUM] = readout[...]
    wait(out + fetch([(packed, packed_any)], sems, 3 + len(out)))


def norm_kernel(near_any, source_any, normed_any, *refs):
    parts, (near, source, normed, sems) = refs[:-4], refs[-4:]
    ens = lax.axis_index("ens")
    copies = fetch([(source_any, source), (near_any, near)], sems)
    rows = source.shape[0]
    copies[0].wait()
    moves = []
    for step, part_any in enumerate(parts):
        count, part, _ = part_any.shape
        for m in range(count):
            place = (ens ^ step) if len(parts) == 2 else m
            place = pl.multiple_of(place * part, part)
            moves.append((source.at[pl.ds(place, part)], part_any.at[m]))
    out = fetch(moves, sems, 2)
    states = source[...].astype(F32)
    inverse = lax.rsqrt(jnp.mean(states * states, axis=-1, keepdims=True) + NORM_EPS)
    normed[:rows, :] = (states * inverse).astype(BF16)
    copies[1].wait()
    row = lax.broadcasted_iota(jnp.int32, (NOTE_ROWS, 128), 0)
    lane = lax.broadcasted_iota(jnp.int32, (NOTE_ROWS, 128), 1)
    note = jnp.zeros((NOTE_ROWS, 128), F32)
    tiles = near.shape[0]
    first_tile = lax.axis_index(("half", "quad", "core")) * tiles
    for tile in range(tiles):
        for slot in range(K_NB):
            at = near[tile, slot]
            step = jnp.where(at >= 0, at - first_tile - tile, NOWHERE).astype(F32)
            note = jnp.where((row == tile) & (lane == slot), step, note)
    normed[rows:, :] = jnp.zeros((NOTE_ROWS, LATENT_DIM), BF16)
    normed[rows:, :128] = note.astype(BF16)
    wait(out + fetch([(normed, normed_any)], sems, 2 + len(out)))


def attach_kernel(packed_ref, sent_any, out_ref, sems):
    width, shard = packed_ref.shape[2], packed_ref.shape[1]
    pairs = [
        (sent_any.at[0, pl.ds(at * shard, shard)], out_ref.at[at, :, width:]) for at in range(2)
    ]
    copies = fetch(pairs, sems)
    out_ref[:, :, :width] = packed_ref[...]
    wait(copies)


def merge_members_kernel(mine_ref, other_ref, packed_ref, source_ref):
    ens = lax.axis_index("ens")
    width = packed_ref.shape[3]
    for half in range(2):
        packed_ref[half, ens] = mine_ref[half, :, :width]
        packed_ref[half, ens ^ 1] = other_ref[half, :, :width]
    source_ref[...] = other_ref[:, :, width:].reshape(source_ref.shape)


def owners():
    core, quad = lax.axis_index("core"), lax.axis_index("quad")
    return [(quad ^ step) * CORES + (core ^ flip) for flip in range(CORES) for step in range(QUAD)]


def collect_kernel(*refs):
    blocks, (normed_any, steps_ref, notes, sems) = refs[:GROUP], refs[GROUP:]
    block = blocks[0].shape[0] - NOTE_ROWS
    pairs = []
    for rows_ref, owner in zip(blocks, owners()):
        place = pl.ds(pl.multiple_of(owner * block, block), block)
        pairs.append((rows_ref.at[:block], normed_any.at[place]))
        pairs.append((rows_ref.at[block:, :128], notes.at[owner]))
    wait(fetch(pairs, sems))
    steps_ref[...] = notes[...].astype(F32)


def put_rims(rims, first, last):
    if len(rims) == 1:
        rims[0][...] = jnp.where(lax.axis_index("half") == 0, last, first)
    else:
        rims[0][...], rims[1][...] = first, last


def rims_kernel(normed_any, *refs):
    rows, sems = refs[-2:]
    if len(refs[0].shape) == 2:
        columns, w, rims = refs[:1], refs[1], refs[2:-2]
        pairs = [(columns[0], w)]
    else:
        columns, w, rims = refs[:2], refs[2], refs[3:-2]
        ens = lax.axis_index("ens")
        pairs = [(part, w.at[:, ens ^ step]) for step, part in enumerate(columns)]
    last = normed_any.shape[0] - RIM
    if len(rims) == 1:
        place = pl.multiple_of(jnp.where(lax.axis_index("half") == 0, last, 0), RIM)
        pairs.append((normed_any.at[pl.ds(place, RIM)], rows.at[0]))
    else:
        pairs += [(normed_any.at[:RIM], rows.at[0]), (normed_any.at[last:], rows.at[1])]
    wait(fetch(pairs, sems))
    weights = w[...].reshape(LATENT_DIM, 3 * COLS)[:, COLS:]
    for at, rim_ref in enumerate(rims):
        rim_ref[...] = jnp.dot(rows[at], weights, preferred_element_type=F32).astype(BF16)


def project_kernel(normed_any, w_ref, q_ref, kv_ref, normed, sems):
    chunk = normed.shape[0] // CHUNKS
    rows = [slice(at * chunk, (at + 1) * chunk) for at in range(CHUNKS)]
    copies = fetch([(normed_any.at[part], normed.at[part]) for part in rows], sems)
    weights = w_ref[...].reshape(LATENT_DIM, 3 * COLS)
    for part, copy in zip(rows, copies):
        copy.wait()
        projected = jnp.dot(normed[part, :], weights, preferred_element_type=F32).astype(BF16)
        q_ref[part, :] = projected[:, :COLS] * jnp.asarray(HEAD**-0.5, BF16)
        kv_ref[part, :] = projected[:, COLS:]


def assemble_kernel(*refs):
    pieces, (w_any, sems) = refs[:GROUP], refs[GROUP:]
    core, quad = lax.axis_index("core"), lax.axis_index("quad")
    pairs = [
        (piece, w_any.at[:, quad ^ (at % QUAD), core ^ (at // QUAD)])
        for at, piece in enumerate(pieces)
    ]
    wait(fetch(pairs, sems))


def by_head(rows):
    lane = lax.broadcasted_iota(jnp.int32, rows.shape, 1)
    zero = jnp.zeros_like(rows)
    return jnp.concatenate(
        [jnp.where(lane < HEAD, rows, zero), jnp.where(lane < HEAD, zero, rows)], axis=0
    )


def usable_keys(steps_ref, pair):
    lane = (lax.broadcasted_iota(jnp.int32, (1, WINDOW), 1) // TILE - RADIUS).astype(F32)
    masks = []
    for query_tile in range(PAIR):
        found = jnp.zeros((1, WINDOW), F32)
        for slot in range(K_NB):
            step = steps_ref[pair, query_tile : query_tile + 1, slot : slot + 1]
            found = jnp.where(lane - query_tile == step, 1.0, found)
        masks.append(found)
    row = lax.broadcasted_iota(jnp.int32, (2 * PAIR * TILE, 1), 0) // TILE % PAIR
    return jnp.where(row == 0, masks[0], masks[1]) > 0


def raised_scores(queries, keys, usable):
    scores = lax.dot_general(queries, keys, OVER_COLUMNS, preferred_element_type=F32)
    scores = jnp.where(usable, scores, MASKED)
    raised = jnp.exp(scores - jnp.max(scores, axis=-1, keepdims=True))
    return raised, 1.0 / jnp.sum(raised, axis=-1, keepdims=True)


def attend(steps_ref, pair, queries, keys, values):
    raised, share = raised_scores(by_head(queries), keys, usable_keys(steps_ref, pair))
    both = jnp.dot(raised.astype(BF16), values, preferred_element_type=F32) * share
    lane = lax.broadcasted_iota(jnp.int32, queries.shape, 1)
    half = PAIR * TILE
    return jnp.where(lane < HEAD, both[:half], both[half:]).astype(BF16)


def interior_kernel(steps_ref, q_ref, kv_ref, out_ref):
    step = PAIR * TILE
    pairs = q_ref.shape[0] // step
    for pair in range(1, pairs - 1):
        window = slice((pair - 1) * step, (pair + 2) * step)
        rows = slice(pair * step, (pair + 1) * step)
        out_ref[rows, :] = attend(
            steps_ref, pair, q_ref[rows, :], kv_ref[window, :COLS], kv_ref[window, COLS:]
        )


def edge_kernel(steps_ref, q_ref, kv_ref, low_ref, high_ref, done_ref, out_ref):
    step = PAIR * TILE
    count = q_ref.shape[0]
    pairs = count // step
    out_ref[step : count - step, :] = done_ref[step : count - step, :]
    first = jnp.concatenate([low_ref[...], kv_ref[: 2 * step, :]], axis=0)
    last = jnp.concatenate([kv_ref[count - 2 * step :, :], high_ref[...]], axis=0)
    for pair, window in ((0, first), (pairs - 1, last)):
        rows = slice(pair * step, (pair + 1) * step)
        out_ref[rows, :] = attend(
            steps_ref, pair, q_ref[rows, :], window[:, :COLS], window[:, COLS:]
        )


def attend_back(steps_ref, pair, queries, grads, keys, values):
    queries, grads = by_head(queries), by_head(grads)
    raised, share = raised_scores(queries, keys, usable_keys(steps_ref, pair))
    probs = raised * share
    grad_probs = lax.dot_general(grads, values, OVER_COLUMNS, preferred_element_type=F32)
    row_delta = jnp.sum(probs * grad_probs, axis=-1, keepdims=True)
    grad_scores = (probs * (grad_probs - row_delta)).astype(BF16)
    key_grad = lax.dot_general(grad_scores, queries, OVER_ROWS, preferred_element_type=F32)
    value_grad = lax.dot_general(probs.astype(BF16), grads, OVER_ROWS, preferred_element_type=F32)
    return key_grad, value_grad


def edge_back_kernel(
    steps_ref, q_ref, kv_ref, low_ref, high_ref, g_ref, part_ref, *rims
):
    outer = []
    step = PAIR * TILE
    count = q_ref.shape[0]
    first = jnp.concatenate([low_ref[...], kv_ref[: 2 * step, :]], axis=0)
    last = jnp.concatenate([kv_ref[count - 2 * step :, :], high_ref[...]], axis=0)
    pairs = count // step
    for edge, pair, window in ((0, 0, first), (1, pairs - 1, last)):
        rows = slice(pair * step, (pair + 1) * step)
        grads = attend_back(
            steps_ref, pair, q_ref[rows, :], g_ref[rows, :], window[:, :COLS], window[:, COLS:]
        )
        rim = slice(0, RIM) if edge == 0 else slice(WINDOW - RIM, WINDOW)
        own = slice(RIM, WINDOW) if edge == 0 else slice(0, WINDOW - RIM)
        for at, grad in enumerate(grads):
            columns = slice(at * COLS, (at + 1) * COLS)
            part_ref[edge, :, columns] = grad[own]
        outer.append(jnp.concatenate([grad[rim].astype(BF16) for grad in grads], axis=1))
    put_rims(rims, *outer)


def interior_back_kernel(steps_ref, q_ref, kv_ref, g_ref, part_ref, out_ref):
    step = PAIR * TILE
    count = q_ref.shape[0]
    pairs = count // step
    reach = 2 * step
    out_ref[:reach, :] = part_ref[0]
    out_ref[reach : count - reach, :] = jnp.zeros((count - 2 * reach, 2 * COLS), F32)
    out_ref[count - reach :, :] = part_ref[1]
    for pair in range(1, pairs - 1):
        window = slice((pair - 1) * step, (pair + 2) * step)
        rows = slice(pair * step, (pair + 1) * step)
        key_grad, value_grad = attend_back(
            steps_ref,
            pair,
            q_ref[rows, :],
            g_ref[rows, :],
            kv_ref[window, :COLS],
            kv_ref[window, COLS:],
        )
        out_ref[window, :COLS] += key_grad
        out_ref[window, COLS:] += value_grad


def slope(spread):
    return spread * lax.rsqrt(spread * spread + SOFT_WIDTH)


def mix_kernel(att_ref, factor_ref, truth_any, w_any, *refs):
    sources, refs = refs[:-8], refs[-8:]
    pred_ref, grad_ref, a, truth_ref, truth, source, w, sems = refs
    members_num, part, _ = source.shape
    halves = w.shape[0]
    ens = lax.axis_index("ens")
    copies = fetch([(w_any.at[half], w.at[half]) for half in range(halves)], sems)
    pairs = [(truth_any, truth_ref)]
    if len(sources) == 1:
        pairs.append((sources[0], source))
    else:
        pairs += [(rows.at[0], source.at[ens ^ step]) for step, rows in enumerate(sources)]
    others = fetch(pairs, sems, halves)
    for g in range(GROUP):
        for m in range(members_num):
            a[m * part : (m + 1) * part, g * COLS : (g + 1) * COLS] = att_ref[g * members_num + m]
    wait(others)
    lane_part = lax.broadcasted_iota(jnp.int32, (1, a.shape[0]), 1) // part
    own_truth, own_factor = truth_ref[...], factor_ref[...]
    for turn in range(1, members_num):
        at = lane_part - turn
        here = jnp.where(at < 0, at + members_num, at) == ens
        own_truth = jnp.where(here, pltpu.roll(truth_ref[...], turn * part, 1), own_truth)
        own_factor = jnp.where(here, pltpu.roll(factor_ref[...], turn * part, 1), own_factor)
    truth[...] = jnp.zeros_like(truth)
    truth[:FIELD_NUM, :] = own_truth
    hidden = source[...].reshape(a.shape).astype(F32)
    count = LATENT_DIM // halves
    for half in range(halves):
        copies[half].wait()
        mix = w[half].reshape(count, LATENT_DIM + FIELD_PAD)[:, :LATENT_DIM]
        hidden += jnp.dot(
            a[:, half * count : (half + 1) * count], mix, preferred_element_type=F32
        )
    both = w[...].reshape(LATENT_DIM, LATENT_DIM + FIELD_PAD)
    mix, readout = both[:, :LATENT_DIM], both[:, LATENT_DIM:]
    inverse = lax.rsqrt(jnp.mean(hidden * hidden, axis=-1, keepdims=True) + NORM_EPS)
    decoded = (hidden * inverse).astype(BF16)
    prediction = lax.dot_general(
        readout, decoded, (((0,), (1,)), ((), ())), preferred_element_type=F32
    )
    pred_ref[...] = prediction[:FIELD_NUM]
    spread = jnp.zeros_like(prediction)
    for other in range(1, members_num):
        spread = spread + slope(prediction - pltpu.roll(prediction, other * part, 1))
    derivative = own_factor / FIELD_NUM * (
        slope(prediction - truth[...]) - spread / (members_num - 1)
    )
    grad_decoded = lax.dot_general(
        derivative.astype(BF16), readout, (((0,), (1,)), ((), ())), preferred_element_type=F32
    )
    grad_hidden = inverse * grad_decoded - hidden * inverse**3 * jnp.mean(
        grad_decoded * hidden, axis=-1, keepdims=True
    )
    grads = lax.dot_general(
        grad_hidden.astype(BF16), mix, OVER_COLUMNS, preferred_element_type=F32
    ).astype(BF16)
    for g in range(GROUP):
        for m in range(members_num):
            grad_ref[g * members_num + m] = grads[
                m * part : (m + 1) * part, g * COLS : (g + 1) * COLS
            ]


def product_kernel(normed_ref, grads_ref, out_ref):
    grads = grads_ref[...]
    high = grads.astype(BF16)
    low = (grads - high.astype(F32)).astype(BF16)
    both = lax.dot_general(
        normed_ref[...], jnp.concatenate([high, low], axis=1), OVER_ROWS, preferred_element_type=F32
    )
    out_ref[...] = both[:, : 2 * COLS] + both[:, 2 * COLS :]


def rim_product_kernel(normed_ref, total_ref, *refs):
    arrived, out_ref = refs[:-1], refs[-1]
    last_row = normed_ref.shape[0] - RIM
    half, last = lax.axis_index("half"), lax.axis_size("half") - 1
    if len(arrived) == 1:
        places = [pl.multiple_of(jnp.where(half == 0, last_row, 0), RIM)]
    else:
        places = [0, last_row]
    total = total_ref[...]
    for at, arrived_ref in enumerate(arrived):
        grads = arrived_ref[...]
        if len(arrived) == 2:
            grads = jnp.where((half > 0) if at == 0 else (half < last), grads.astype(F32), 0.0)
            grads = grads.astype(BF16)
        rows = normed_ref[pl.ds(places[at], RIM), :]
        total += lax.dot_general(rows, grads, OVER_ROWS, preferred_element_type=F32)
    out_ref[...] = total.astype(BF16)


def gather_kernel(parts_ref, out_ref):
    halves, _, members_num = parts_ref.shape[:3]
    for g in range(GROUP):
        total = None
        for half in range(halves):
            for m in range(members_num):
                part = parts_ref[half, g, m].astype(F32)
                total = part if total is None else total + part
        out_ref[:, g * COLS : (g + 1) * COLS] = total[:, :COLS]
        out_ref[:, LATENT_DIM + g * COLS : LATENT_DIM + (g + 1) * COLS] = total[:, COLS:]


def exchange(chunks, axes):
    return lax.all_to_all(chunks, axes, 0, 0)


def swap(value, axis, step):
    return lax.ppermute(value, axis, [(i, i ^ step) for i in range(lax.axis_size(axis))])


def in_order(mine, axis, at):
    if lax.axis_size(axis) != 2:
        return lax.all_gather(mine, axis, axis=at)
    other = swap(mine, axis, 1)
    first = lax.axis_index(axis) == 0
    return jnp.stack([jnp.where(first, mine, other), jnp.where(first, other, mine)], axis=at)


def body(members, w_attn, w_mix, readout_matrix, observed_truth, cell_surface_factor, neighbours):
    halves, members_num = lax.axis_size("half"), lax.axis_size("ens")
    nodes = ("half", "quad", "core")
    everyone = nodes + ("ens",)
    shard = w_attn.shape[0]
    node_rows = members.shape[1]
    rows = GROUP * node_rows
    part = node_rows // members_num
    up = [(i, i + 1) for i in range(halves - 1)]
    down = [(target, source) for source, target in up]
    ens = lax.axis_index("ens")
    width = LATENT_DIM + FIELD_PAD
    paired = members_num == 2
    copies = 1 if paired else members_num
    source_parts = 2 if paired else 1

    columns, packed = call(
        weights_kernel,
        "prepare_weights",
        [((halves, GROUP, copies, shard, 3 * COLS), BF16), ((shard, width), BF16)],
        "hhh",
        [
            pltpu.VMEM(w_attn.shape, BF16),
            pltpu.VMEM((GROUP, shard, 3 * COLS), BF16),
            pltpu.VMEM(readout_matrix.shape, BF16),
            pltpu.VMEM((shard, width), BF16),
            pltpu.SemaphoreType.DMA((4 + halves * copies,)),
        ],
        moved=2**20,
        results="hh",
    )(w_attn, w_mix, readout_matrix)
    normed, *sources = call(
        norm_kernel,
        "norm",
        [((node_rows + NOTE_ROWS, LATENT_DIM), BF16)]
        + [((1 if paired else members_num, part, LATENT_DIM), BF16)] * source_parts,
        "hh",
        [
            pltpu.SMEM(neighbours.shape, jnp.int32),
            pltpu.VMEM((node_rows, LATENT_DIM), BF16),
            pltpu.VMEM((node_rows + NOTE_ROWS, LATENT_DIM), BF16),
            pltpu.SemaphoreType.DMA((3 + max(2, members_num),)),
        ],
        flops=2**20,
        moved=2**20,
        results="h" + "h" * source_parts,
    )(neighbours, members.reshape(node_rows, LATENT_DIM))

    packed, normed = lax.optimization_barrier((in_order(packed, "half", 0), normed))
    square = paired and halves == 2 and shard % 16 == 0
    near = [normed, swap(normed, "quad", 1), None, swap(normed, "quad", 3)]
    if paired:
        columns = exchange(columns.reshape(-1, shard, 3 * COLS), nodes)
        if square:
            (wide,) = call(
                attach_kernel,
                "attach_sources",
                [((2, shard, width + LATENT_DIM), BF16)],
                "vh",
                [pltpu.SemaphoreType.DMA((2,))],
                moved=2**19,
            )(packed, sources[1])
            columns, late, wide = lax.optimization_barrier((columns, normed, wide))
        else:
            columns, late = lax.optimization_barrier((columns, normed))
        columns = [columns, swap(columns, "ens", 1)]
    else:
        columns = [exchange(columns.reshape(-1, shard, 3 * COLS), everyone)]
        columns = [columns[0].reshape(LATENT_DIM, 3 * COLS)]
        late = normed
    near[2] = swap(late, "quad", 2)
    near = list(lax.optimization_barrier(tuple(near)))
    far = [swap(piece, "core", 1) for piece in near]
    normed, steps = call(
        collect_kernel,
        "collect",
        [((rows, LATENT_DIM), BF16), ((GROUP, NOTE_ROWS, 128), F32)],
        "a" * (2 * QUAD),
        [pltpu.VMEM((GROUP, NOTE_ROWS, 128), BF16), pltpu.SemaphoreType.DMA((2 * GROUP,))],
        moved=4 * 2**20,
        results="hv",
    )(*near, *far)

    if square:
        packed, arrived = call(
            merge_members_kernel,
            "merge_members",
            [((2, 2, shard, width), BF16), ((1, part, LATENT_DIM), BF16)],
            "vv",
            moved=2**19,
        )(wide, swap(wide, "ens", 1))
        packed = packed.reshape(2, 2 * shard, width)
        sources = [sources[0], arrived]
    else:
        packed = in_order(packed, "ens", 1).reshape(halves, members_num * shard, width)
    packed, near[2] = lax.optimization_barrier((packed, near[2]))
    pieces = [packed] + [swap(packed, "quad", step) for step in range(1, QUAD)]

    rim = ((RIM, 2 * COLS), BF16)
    rims = [rim] if halves == 2 else [rim, rim]
    w_shape = (GROUP * halves, 2, shard, 3 * COLS) if paired else (LATENT_DIM, 3 * COLS)
    weights, *inner = call(
        rims_kernel,
        "project_rims",
        [(w_shape, BF16)] + rims,
        "h" + "a" * len(columns),
        [pltpu.VMEM((len(rims), RIM, LATENT_DIM), BF16), pltpu.SemaphoreType.DMA((4,))],
        flops=RIM * LATENT_DIM * 4 * COLS,
        moved=2**20,
    )(normed, *columns)
    def across(inner):
        if halves == 2:
            got = swap(inner[0], "half", 1)
            return got, got
        return lax.ppermute(inner[1], "half", up), lax.ppermute(inner[0], "half", down)

    if not paired:
        sources = [exchange(sources[0], "ens")]
    elif not square:
        sources = [sources[0], swap(sources[1], "ens", 1)]
    low, high = across(inner)
    queries, own = call(
        project_kernel,
        "project",
        [((rows, COLS), BF16), ((rows, 2 * COLS), BF16)],
        "hv",
        [pltpu.VMEM((rows, LATENT_DIM), BF16), pltpu.SemaphoreType.DMA((CHUNKS,))],
        flops=rows * LATENT_DIM * 6 * COLS,
        moved=4 * 2**20,
    )(normed, weights)

    (outcome,) = call(
        interior_kernel,
        "attention_interior",
        [((rows, COLS), BF16)],
        "vvv",
        flops=rows * COLS * 2048,
        moved=2**21,
        exps=rows * 512,
    )(steps, queries, own)
    (outcome,) = call(
        edge_kernel,
        "attention_edges",
        [((rows, COLS), BF16)],
        "vvvvvv",
        flops=rows * COLS * 512,
        moved=2**20,
        exps=rows * 128,
    )(steps, queries, own, low, high, outcome)
    *pieces, own = lax.optimization_barrier((*pieces, own))
    pieces = pieces + [swap(piece, "core", 1) for piece in pieces]
    attended = exchange(outcome.reshape(GROUP * members_num, part, COLS), ("quad", "core", "ens"))
    block = (halves, QUAD, CORES, members_num * shard, width)
    (weights,) = call(
        assemble_kernel,
        "assemble",
        [(block, BF16)],
        "a" * len(pieces),
        [pltpu.SemaphoreType.DMA((GROUP,))],
        moved=4 * 2**20,
        results="h",
    )(*pieces)

    prediction, grads = call(
        mix_kernel,
        "mix_loss_backward",
        [((FIELD_NUM, node_rows), F32), ((GROUP * members_num, part, COLS), BF16)],
        "vvhh" + "a" * len(sources),
        [
            pltpu.VMEM((node_rows, LATENT_DIM), BF16),
            pltpu.VMEM(observed_truth.shape, F32),
            pltpu.VMEM((FIELD_PAD, node_rows), F32),
            pltpu.VMEM((members_num, part, LATENT_DIM), BF16),
            pltpu.VMEM(block, BF16),
            pltpu.SemaphoreType.DMA((halves + 1 + len(sources),)),
        ],
        flops=node_rows * LATENT_DIM * 4 * width,
        moved=2**22,
        room=14,
    )(attended, cell_surface_factor[None], observed_truth, weights, *sources)
    grads = exchange(grads, ("quad", "core", "ens")).reshape(rows, COLS)

    edges, *inner = call(
        edge_back_kernel,
        "attention_edges_back",
        [((2, WINDOW - RIM, 2 * COLS), F32)] + rims,
        "vvvvvv",
        flops=rows * COLS * 1280,
        moved=2**20,
        exps=rows * 128,
    )(steps, queries, own, low, high, grads)
    from_low, from_high = across(inner)
    (kv_grads,) = call(
        interior_back_kernel,
        "attention_interior_back",
        [((rows, 2 * COLS), F32)],
        "vvvvv",
        flops=rows * COLS * 4096,
        moved=2**22,
        exps=rows * 512,
        room=10,
    )(steps, queries, own, grads, edges)
    (total,) = call(
        product_kernel,
        "product",
        [((LATENT_DIM, 2 * COLS), F32)],
        "vv",
        room=16,
    )(normed, kv_grads)
    arrived = [from_low] if halves == 2 else [from_low, from_high]
    (term,) = call(
        rim_product_kernel,
        "product_rims",
        [((LATENT_DIM, 2 * COLS), BF16)],
        "vv" + "v" * len(arrived),
        flops=RIM * LATENT_DIM * 4 * COLS,
        moved=2**21,
        room=16,
    )(normed, total, *arrived)
    term, prediction = lax.optimization_barrier((term, prediction))
    term = exchange(term.reshape(-1, shard, 2 * COLS), everyone)
    (grad_kv,) = call(
        gather_kernel, "gather_sums", [((shard, 2 * LATENT_DIM), F32)], "v", flops=2**17, moved=2**20
    )(term.reshape(halves, GROUP, members_num, shard, 2 * COLS))

    if members_num == 2:
        got = jnp.roll(swap(prediction, "ens", 1), part, axis=1)
        lane = lax.broadcasted_iota(jnp.int32, prediction.shape, 1)
        prediction = jnp.where(lane // part == ens, prediction, got)
    else:
        prediction = prediction.reshape(FIELD_NUM, members_num, part).transpose(1, 0, 2)
        prediction = exchange(prediction, "ens").transpose(1, 0, 2)
    return (prediction.reshape(1, FIELD_NUM, node_rows), grad_kv)


def solution(mesh):
    space, ens = mesh.shape["space"], mesh.shape["ens"]
    split = Mesh(
        mesh.devices.reshape(space // GROUP, QUAD, CORES, ens), ("half", "quad", "core", "ens")
    )
    nodes = ("half", "quad", "core")
    shards = nodes + ("ens",)
    in_specs = (
        P("ens", nodes, None),
        P(shards, None),
        P(shards, None),
        P(shards, None),
        P(None, nodes),
        P(nodes),
        P(nodes, None),
    )
    out_specs = (P("ens", None, nodes), P(shards, None))
    return jax.shard_map(body, mesh=split, in_specs=in_specs, out_specs=out_specs, check_vma=False)
```

```python
import functools

import jax
import jax.numpy as jnp
from jax import lax
from jax.experimental import pallas as pl
from jax.experimental.pallas import tpu as pltpu
from jax.sharding import Mesh
from jax.sharding import PartitionSpec as P

LATENT_DIM = 1024
HEADS = 16
HEAD = 64
FIELD_NUM = 100
TILE = 64
RADIUS = 2
K_NB = 4
QUAD = 4
CORES = 2
GROUP = QUAD * CORES
COLS = LATENT_DIM // GROUP
RIM = RADIUS * TILE
FIELD_PAD = 128
PAIR = 2
WINDOW = (PAIR + 2 * RADIUS) * TILE
NOWHERE = 100
NOTE_ROWS = 16
CHUNKS = 4

NORM_EPS = 1e-06
SOFT_WIDTH = 0.0625
MASKED = -1e30

F32 = jnp.float32
BF16 = jnp.bfloat16

VMEM = pl.BlockSpec(memory_space=pltpu.VMEM)
SMEM = pl.BlockSpec(memory_space=pltpu.SMEM)
HBM = pl.BlockSpec(memory_space=pltpu.HBM)
ANYWHERE = pl.BlockSpec(memory_space=pl.ANY)
OVER_ROWS = (((0,), (0,)), ((), ()))
OVER_COLUMNS = (((1,), (1,)), ((), ()))


def call(kernel, name, outs, ins, scratch=(), flops=0, moved=0, exps=0, room=8, results=None):
    results = results or "v" * len(outs)
    spaces = {"s": SMEM, "v": VMEM, "h": HBM, "a": ANYWHERE}
    made = pl.pallas_call(
        kernel,
        out_shape=[
            pltpu.HBM(shape, kind) if space == "h" else jax.ShapeDtypeStruct(shape, kind)
            for (shape, kind), space in zip(outs, results)
        ],
        in_specs=[spaces[space] for space in ins],
        out_specs=[spaces[space] for space in results],
        scratch_shapes=list(scratch),
        compiler_params=pltpu.CompilerParams(vmem_limit_bytes=room * 2**20),
        cost_estimate=pl.CostEstimate(flops=flops, bytes_accessed=moved, transcendentals=exps),
        name=name,
    )

    def run(*args):
        return made(
            *[
                pltpu.with_memory_space_constraint(arg, pltpu.HBM) if space == "h" else arg
                for arg, space in zip(args, ins)
            ]
        )

    return run


def fetch(pairs, sems, first=0):
    copies = [
        pltpu.make_async_copy(source, target, sems.at[first + at])
        for at, (source, target) in enumerate(pairs)
    ]
    for copy in copies:
        copy.start()
    return copies


def wait(copies):
    for copy in copies:
        copy.wait()


def weights_kernel(w_any, mix_any, readout_any, columns_any, packed_any, *refs):
    w, columns, readout, packed, sems = refs
    copies = fetch(
        [(w_any, w), (readout_any, readout), (mix_any, packed.at[:, :LATENT_DIM])], sems
    )
    copies[0].wait()
    for g in range(GROUP):
        for part in range(3):
            at = (part * GROUP + g) * COLS
            columns[g, :, part * COLS : (part + 1) * COLS] = w[:, at : at + COLS]
    halves, _, members_num = columns_any.shape[:3]
    out = fetch(
        [
            (columns, columns_any.at[half, :, m])
            for half in range(halves)
            for m in range(members_num)
        ],
        sems,
        3,
    )
    wait(copies[1:])
    packed[:, LATENT_DIM:] = jnp.zeros((packed.shape[0], FIELD_PAD), BF16)
    packed[:, LATENT_DIM : LATENT_DIM + FIELD_NUM] = readout[...]
    wait(out + fetch([(packed, packed_any)], sems, 3 + len(out)))


def norm_kernel(near_any, source_any, normed_any, *refs):
    parts, (near, source, normed, sems) = refs[:-4], refs[-4:]
    ens = lax.axis_index("ens")
    copies = fetch([(source_any, source), (near_any, near)], sems)
    rows = source.shape[0]
    copies[0].wait()
    moves = []
    for step, part_any in enumerate(parts):
        count, part, _ = part_any.shape
        for m in range(count):
            place = (ens ^ step) if len(parts) == 2 else m
            place = pl.multiple_of(place * part, part)
            moves.append((source.at[pl.ds(place, part)], part_any.at[m]))
    out = fetch(moves, sems, 2)
    states = source[...].astype(F32)
    inverse = lax.rsqrt(jnp.mean(states * states, axis=-1, keepdims=True) + NORM_EPS)
    normed[:rows, :] = (states * inverse).astype(BF16)
    copies[1].wait()
    row = lax.broadcasted_iota(jnp.int32, (NOTE_ROWS, 128), 0)
    lane = lax.broadcasted_iota(jnp.int32, (NOTE_ROWS, 128), 1)
    note = jnp.zeros((NOTE_ROWS, 128), F32)
    tiles = near.shape[0]
    first_tile = lax.axis_index(("half", "quad", "core")) * tiles
    for tile in range(tiles):
        for slot in range(K_NB):
            at = near[tile, slot]
            step = jnp.where(at >= 0, at - first_tile - tile, NOWHERE).astype(F32)
            note = jnp.where((row == tile) & (lane == slot), step, note)
    normed[rows:, :] = jnp.zeros((NOTE_ROWS, LATENT_DIM), BF16)
    normed[rows:, :128] = note.astype(BF16)
    wait(out + fetch([(normed, normed_any)], sems, 2 + len(out)))


def attach_kernel(packed_ref, sent_any, out_ref, sems):
    width, shard = packed_ref.shape[2], packed_ref.shape[1]
    pairs = [
        (sent_any.at[0, pl.ds(at * shard, shard)], out_ref.at[at, :, width:]) for at in range(2)
    ]
    copies = fetch(pairs, sems)
    out_ref[:, :, :width] = packed_ref[...]
    wait(copies)


def merge_members_kernel(mine_ref, other_ref, packed_ref, source_ref):
    ens = lax.axis_index("ens")
    width = packed_ref.shape[3]
    for half in range(2):
        packed_ref[half, ens] = mine_ref[half, :, :width]
        packed_ref[half, ens ^ 1] = other_ref[half, :, :width]
    source_ref[...] = other_ref[:, :, width:].reshape(source_ref.shape)


def owners():
    core, quad = lax.axis_index("core"), lax.axis_index("quad")
    return [(quad ^ step) * CORES + (core ^ flip) for flip in range(CORES) for step in range(QUAD)]


def collect_kernel(*refs):
    blocks, (normed_any, steps_ref, notes, sems) = refs[:GROUP], refs[GROUP:]
    block = blocks[0].shape[0] - NOTE_ROWS
    pairs = []
    for rows_ref, owner in zip(blocks, owners()):
        place = pl.ds(pl.multiple_of(owner * block, block), block)
        pairs.append((rows_ref.at[:block], normed_any.at[place]))
        pairs.append((rows_ref.at[block:, :128], notes.at[owner]))
    wait(fetch(pairs, sems))
    steps_ref[...] = notes[...].astype(F32)


def put_rims(rims, first, last):
    if len(rims) == 1:
        rims[0][...] = jnp.where(lax.axis_index("half") == 0, last, first)
    else:
        rims[0][...], rims[1][...] = first, last


def rims_kernel(normed_any, *refs):
    rows, sems = refs[-2:]
    if len(refs[0].shape) == 2:
        columns, w, rims = refs[:1], refs[1], refs[2:-2]
        pairs = [(columns[0], w)]
    else:
        columns, w, rims = refs[:2], refs[2], refs[3:-2]
        ens = lax.axis_index("ens")
        pairs = [(part, w.at[:, ens ^ step]) for step, part in enumerate(columns)]
    last = normed_any.shape[0] - RIM
    if len(rims) == 1:
        place = pl.multiple_of(jnp.where(lax.axis_index("half") == 0, last, 0), RIM)
        pairs.append((normed_any.at[pl.ds(place, RIM)], rows.at[0]))
    else:
        pairs += [(normed_any.at[:RIM], rows.at[0]), (normed_any.at[last:], rows.at[1])]
    wait(fetch(pairs, sems))
    weights = w[...].reshape(LATENT_DIM, 3 * COLS)[:, COLS:]
    for at, rim_ref in enumerate(rims):
        rim_ref[...] = jnp.dot(rows[at], weights, preferred_element_type=F32).astype(BF16)


def project_kernel(normed_any, w_ref, q_ref, kv_ref, normed, sems):
    chunk = normed.shape[0] // CHUNKS
    rows = [slice(at * chunk, (at + 1) * chunk) for at in range(CHUNKS)]
    copies = fetch([(normed_any.at[part], normed.at[part]) for part in rows], sems)
    weights = w_ref[...].reshape(LATENT_DIM, 3 * COLS)
    for part, copy in zip(rows, copies):
        copy.wait()
        projected = jnp.dot(normed[part, :], weights, preferred_element_type=F32).astype(BF16)
        q_ref[part, :] = projected[:, :COLS] * jnp.asarray(HEAD**-0.5, BF16)
        kv_ref[part, :] = projected[:, COLS:]


def assemble_kernel(*refs):
    pieces, (w_any, sems) = refs[:GROUP], refs[GROUP:]
    core, quad = lax.axis_index("core"), lax.axis_index("quad")
    pairs = [
        (piece, w_any.at[:, quad ^ (at % QUAD), core ^ (at // QUAD)])
        for at, piece in enumerate(pieces)
    ]
    wait(fetch(pairs, sems))


def by_head(rows):
    lane = lax.broadcasted_iota(jnp.int32, rows.shape, 1)
    zero = jnp.zeros_like(rows)
    return jnp.concatenate(
        [jnp.where(lane < HEAD, rows, zero), jnp.where(lane < HEAD, zero, rows)], axis=0
    )


def usable_keys(steps_ref, pair):
    lane = (lax.broadcasted_iota(jnp.int32, (1, WINDOW), 1) // TILE - RADIUS).astype(F32)
    masks = []
    for query_tile in range(PAIR):
        found = jnp.zeros((1, WINDOW), F32)
        for slot in range(K_NB):
            step = steps_ref[pair, query_tile : query_tile + 1, slot : slot + 1]
            found = jnp.where(lane - query_tile == step, 1.0, found)
        masks.append(found)
    row = lax.broadcasted_iota(jnp.int32, (2 * PAIR * TILE, 1), 0) // TILE % PAIR
    return jnp.where(row == 0, masks[0], masks[1]) > 0


def raised_scores(queries, keys, usable):
    scores = lax.dot_general(queries, keys, OVER_COLUMNS, preferred_element_type=F32)
    scores = jnp.where(usable, scores, MASKED)
    raised = jnp.exp(scores - jnp.max(scores, axis=-1, keepdims=True))
    return raised, 1.0 / jnp.sum(raised, axis=-1, keepdims=True)


def attend(steps_ref, pair, queries, keys, values):
    raised, share = raised_scores(by_head(queries), keys, usable_keys(steps_ref, pair))
    both = jnp.dot(raised.astype(BF16), values, preferred_element_type=F32) * share
    lane = lax.broadcasted_iota(jnp.int32, queries.shape, 1)
    half = PAIR * TILE
    return jnp.where(lane < HEAD, both[:half], both[half:]).astype(BF16)


def interior_kernel(steps_ref, q_ref, kv_ref, out_ref):
    step = PAIR * TILE
    pairs = q_ref.shape[0] // step
    for pair in range(1, pairs - 1):
        window = slice((pair - 1) * step, (pair + 2) * step)
        rows = slice(pair * step, (pair + 1) * step)
        out_ref[rows, :] = attend(
            steps_ref, pair, q_ref[rows, :], kv_ref[window, :COLS], kv_ref[window, COLS:]
        )


def edge_kernel(steps_ref, q_ref, kv_ref, low_ref, high_ref, done_ref, out_ref):
    step = PAIR * TILE
    count = q_ref.shape[0]
    pairs = count // step
    out_ref[step : count - step, :] = done_ref[step : count - step, :]
    first = jnp.concatenate([low_ref[...], kv_ref[: 2 * step, :]], axis=0)
    last = jnp.concatenate([kv_ref[count - 2 * step :, :], high_ref[...]], axis=0)
    for pair, window in ((0, first), (pairs - 1, last)):
        rows = slice(pair * step, (pair + 1) * step)
        out_ref[rows, :] = attend(
            steps_ref, pair, q_ref[rows, :], window[:, :COLS], window[:, COLS:]
        )


def attend_back(steps_ref, pair, queries, grads, keys, values):
    queries, grads = by_head(queries), by_head(grads)
    raised, share = raised_scores(queries, keys, usable_keys(steps_ref, pair))
    probs = raised * share
    grad_probs = lax.dot_general(grads, values, OVER_COLUMNS, preferred_element_type=F32)
    row_delta = jnp.sum(probs * grad_probs, axis=-1, keepdims=True)
    grad_scores = (probs * (grad_probs - row_delta)).astype(BF16)
    key_grad = lax.dot_general(grad_scores, queries, OVER_ROWS, preferred_element_type=F32)
    value_grad = lax.dot_general(probs.astype(BF16), grads, OVER_ROWS, preferred_element_type=F32)
    return key_grad, value_grad


def edge_back_kernel(
    steps_ref, q_ref, kv_ref, low_ref, high_ref, g_ref, part_ref, *rims
):
    outer = []
    step = PAIR * TILE
    count = q_ref.shape[0]
    first = jnp.concatenate([low_ref[...], kv_ref[: 2 * step, :]], axis=0)
    last = jnp.concatenate([kv_ref[count - 2 * step :, :], high_ref[...]], axis=0)
    pairs = count // step
    for edge, pair, window in ((0, 0, first), (1, pairs - 1, last)):
        rows = slice(pair * step, (pair + 1) * step)
        grads = attend_back(
            steps_ref, pair, q_ref[rows, :], g_ref[rows, :], window[:, :COLS], window[:, COLS:]
        )
        rim = slice(0, RIM) if edge == 0 else slice(WINDOW - RIM, WINDOW)
        own = slice(RIM, WINDOW) if edge == 0 else slice(0, WINDOW - RIM)
        for at, grad in enumerate(grads):
            columns = slice(at * COLS, (at + 1) * COLS)
            part_ref[edge, :, columns] = grad[own]
        outer.append(jnp.concatenate([grad[rim].astype(BF16) for grad in grads], axis=1))
    put_rims(rims, *outer)


def interior_back_kernel(steps_ref, q_ref, kv_ref, g_ref, part_ref, out_ref):
    step = PAIR * TILE
    count = q_ref.shape[0]
    pairs = count // step
    reach = 2 * step
    out_ref[:reach, :] = part_ref[0]
    out_ref[reach : count - reach, :] = jnp.zeros((count - 2 * reach, 2 * COLS), F32)
    out_ref[count - reach :, :] = part_ref[1]
    for pair in range(1, pairs - 1):
        window = slice((pair - 1) * step, (pair + 2) * step)
        rows = slice(pair * step, (pair + 1) * step)
        key_grad, value_grad = attend_back(
            steps_ref,
            pair,
            q_ref[rows, :],
            g_ref[rows, :],
            kv_ref[window, :COLS],
            kv_ref[window, COLS:],
        )
        out_ref[window, :COLS] += key_grad
        out_ref[window, COLS:] += value_grad


def slope(spread):
    return spread * lax.rsqrt(spread * spread + SOFT_WIDTH)


def mix_kernel(att_ref, factor_ref, truth_any, w_any, *refs):
    sources, refs = refs[:-8], refs[-8:]
    pred_ref, grad_ref, a, truth_ref, truth, source, w, sems = refs
    members_num, part, _ = source.shape
    halves = w.shape[0]
    ens = lax.axis_index("ens")
    copies = fetch([(w_any.at[half], w.at[half]) for half in range(halves)], sems)
    pairs = [(truth_any, truth_ref)]
    if len(sources) == 1:
        pairs.append((sources[0], source))
    else:
        pairs += [(rows.at[0], source.at[ens ^ step]) for step, rows in enumerate(sources)]
    others = fetch(pairs, sems, halves)
    for g in range(GROUP):
        for m in range(members_num):
            a[m * part : (m + 1) * part, g * COLS : (g + 1) * COLS] = att_ref[g * members_num + m]
    wait(others)
    lane_part = lax.broadcasted_iota(jnp.int32, (1, a.shape[0]), 1) // part
    own_truth, own_factor = truth_ref[...], factor_ref[...]
    for turn in range(1, members_num):
        at = lane_part - turn
        here = jnp.where(at < 0, at + members_num, at) == ens
        own_truth = jnp.where(here, pltpu.roll(truth_ref[...], turn * part, 1), own_truth)
        own_factor = jnp.where(here, pltpu.roll(factor_ref[...], turn * part, 1), own_factor)
    truth[...] = jnp.zeros_like(truth)
    truth[:FIELD_NUM, :] = own_truth
    hidden = source[...].reshape(a.shape).astype(F32)
    count = LATENT_DIM // halves
    for half in range(halves):
        copies[half].wait()
        mix = w[half].reshape(count, LATENT_DIM + FIELD_PAD)[:, :LATENT_DIM]
        hidden += jnp.dot(
            a[:, half * count : (half + 1) * count], mix, preferred_element_type=F32
        )
    both = w[...].reshape(LATENT_DIM, LATENT_DIM + FIELD_PAD)
    mix, readout = both[:, :LATENT_DIM], both[:, LATENT_DIM:]
    inverse = lax.rsqrt(jnp.mean(hidden * hidden, axis=-1, keepdims=True) + NORM_EPS)
    decoded = (hidden * inverse).astype(BF16)
    prediction = lax.dot_general(
        readout, decoded, (((0,), (1,)), ((), ())), preferred_element_type=F32
    )
    pred_ref[...] = prediction[:FIELD_NUM]
    spread = jnp.zeros_like(prediction)
    for other in range(1, members_num):
        spread = spread + slope(prediction - pltpu.roll(prediction, other * part, 1))
    derivative = own_factor / FIELD_NUM * (
        slope(prediction - truth[...]) - spread / (members_num - 1)
    )
    grad_decoded = lax.dot_general(
        derivative.astype(BF16), readout, (((0,), (1,)), ((), ())), preferred_element_type=F32
    )
    grad_hidden = inverse * grad_decoded - hidden * inverse**3 * jnp.mean(
        grad_decoded * hidden, axis=-1, keepdims=True
    )
    grads = lax.dot_general(
        grad_hidden.astype(BF16), mix, OVER_COLUMNS, preferred_element_type=F32
    ).astype(BF16)
    for g in range(GROUP):
        for m in range(members_num):
            grad_ref[g * members_num + m] = grads[
                m * part : (m + 1) * part, g * COLS : (g + 1) * COLS
            ]


def product_kernel(normed_ref, grads_ref, out_ref):
    grads = grads_ref[...]
    high = grads.astype(BF16)
    low = (grads - high.astype(F32)).astype(BF16)
    both = lax.dot_general(
        normed_ref[...], jnp.concatenate([high, low], axis=1), OVER_ROWS, preferred_element_type=F32
    )
    out_ref[...] = both[:, : 2 * COLS] + both[:, 2 * COLS :]


def rim_product_kernel(normed_ref, total_ref, *refs):
    arrived, out_ref = refs[:-1], refs[-1]
    last_row = normed_ref.shape[0] - RIM
    half, last = lax.axis_index("half"), lax.axis_size("half") - 1
    if len(arrived) == 1:
        places = [pl.multiple_of(jnp.where(half == 0, last_row, 0), RIM)]
    else:
        places = [0, last_row]
    total = total_ref[...]
    for at, arrived_ref in enumerate(arrived):
        grads = arrived_ref[...]
        if len(arrived) == 2:
            grads = jnp.where((half > 0) if at == 0 else (half < last), grads.astype(F32), 0.0)
            grads = grads.astype(BF16)
        rows = normed_ref[pl.ds(places[at], RIM), :]
        total += lax.dot_general(rows, grads, OVER_ROWS, preferred_element_type=F32)
    out_ref[...] = total.astype(BF16)


def gather_kernel(parts_ref, out_ref):
    halves, _, members_num = parts_ref.shape[:3]
    for g in range(GROUP):
        total = None
        for half in range(halves):
            for m in range(members_num):
                part = parts_ref[half, g, m].astype(F32)
                total = part if total is None else total + part
        out_ref[:, g * COLS : (g + 1) * COLS] = total[:, :COLS]
        out_ref[:, LATENT_DIM + g * COLS : LATENT_DIM + (g + 1) * COLS] = total[:, COLS:]


def exchange(chunks, axes):
    return lax.all_to_all(chunks, axes, 0, 0)


def swap(value, axis, step):
    return lax.ppermute(value, axis, [(i, i ^ step) for i in range(lax.axis_size(axis))])


def in_order(mine, axis, at):
    if lax.axis_size(axis) != 2:
        return lax.all_gather(mine, axis, axis=at)
    other = swap(mine, axis, 1)
    first = lax.axis_index(axis) == 0
    return jnp.stack([jnp.where(first, mine, other), jnp.where(first, other, mine)], axis=at)


def body(members, w_attn, w_mix, readout_matrix, observed_truth, cell_surface_factor, neighbours):
    halves, members_num = lax.axis_size("half"), lax.axis_size("ens")
    nodes = ("half", "quad", "core")
    everyone = nodes + ("ens",)
    shard = w_attn.shape[0]
    node_rows = members.shape[1]
    rows = GROUP * node_rows
    part = node_rows // members_num
    up = [(i, i + 1) for i in range(halves - 1)]
    down = [(target, source) for source, target in up]
    ens = lax.axis_index("ens")
    width = LATENT_DIM + FIELD_PAD
    paired = members_num == 2
    copies = 1 if paired else members_num
    source_parts = 2 if paired else 1

    columns, packed = call(
        weights_kernel,
        "prepare_weights",
        [((halves, GROUP, copies, shard, 3 * COLS), BF16), ((shard, width), BF16)],
        "hhh",
        [
            pltpu.VMEM(w_attn.shape, BF16),
            pltpu.VMEM((GROUP, shard, 3 * COLS), BF16),
            pltpu.VMEM(readout_matrix.shape, BF16),
            pltpu.VMEM((shard, width), BF16),
            pltpu.SemaphoreType.DMA((4 + halves * copies,)),
        ],
        moved=2**20,
        results="hh",
    )(w_attn, w_mix, readout_matrix)
    normed, *sources = call(
        norm_kernel,
        "norm",
        [((node_rows + NOTE_ROWS, LATENT_DIM), BF16)]
        + [((1 if paired else members_num, part, LATENT_DIM), BF16)] * source_parts,
        "hh",
        [
            pltpu.SMEM(neighbours.shape, jnp.int32),
            pltpu.VMEM((node_rows, LATENT_DIM), BF16),
            pltpu.VMEM((node_rows + NOTE_ROWS, LATENT_DIM), BF16),
            pltpu.SemaphoreType.DMA((3 + max(2, members_num),)),
        ],
        flops=2**20,
        moved=2**20,
        results="h" + "h" * source_parts,
    )(neighbours, members.reshape(node_rows, LATENT_DIM))

    packed, normed = lax.optimization_barrier((in_order(packed, "half", 0), normed))
    square = paired and halves == 2 and shard % 16 == 0
    near = [normed, swap(normed, "quad", 1), None, swap(normed, "quad", 3)]
    if paired:
        columns = exchange(columns.reshape(-1, shard, 3 * COLS), nodes)
        if square:
            (wide,) = call(
                attach_kernel,
                "attach_sources",
                [((2, shard, width + LATENT_DIM), BF16)],
                "vh",
                [pltpu.SemaphoreType.DMA((2,))],
                moved=2**19,
            )(packed, sources[1])
            columns, late, wide = lax.optimization_barrier((columns, normed, wide))
        else:
            columns, late = lax.optimization_barrier((columns, normed))
        columns = [columns, swap(columns, "ens", 1)]
    else:
        columns = [exchange(columns.reshape(-1, shard, 3 * COLS), everyone)]
        columns = [columns[0].reshape(LATENT_DIM, 3 * COLS)]
        late = normed
    near[2] = swap(late, "quad", 2)
    near = list(lax.optimization_barrier(tuple(near)))
    far = [swap(piece, "core", 1) for piece in near]
    normed, steps = call(
        collect_kernel,
        "collect",
        [((rows, LATENT_DIM), BF16), ((GROUP, NOTE_ROWS, 128), F32)],
        "a" * (2 * QUAD),
        [pltpu.VMEM((GROUP, NOTE_ROWS, 128), BF16), pltpu.SemaphoreType.DMA((2 * GROUP,))],
        moved=4 * 2**20,
        results="hv",
    )(*near, *far)

    if square:
        packed, arrived = call(
            merge_members_kernel,
            "merge_members",
            [((2, 2, shard, width), BF16), ((1, part, LATENT_DIM), BF16)],
            "vv",
            moved=2**19,
        )(wide, swap(wide, "ens", 1))
        packed = packed.reshape(2, 2 * shard, width)
        sources = [sources[0], arrived]
    else:
        packed = in_order(packed, "ens", 1).reshape(halves, members_num * shard, width)
    packed, near[2] = lax.optimization_barrier((packed, near[2]))
    pieces = {step: swap(packed, "quad", step) for step in (2, 3, 1)}
    pieces = [packed] + [pieces[step] for step in range(1, QUAD)]

    rim = ((RIM, 2 * COLS), BF16)
    rims = [rim] if halves == 2 else [rim, rim]
    w_shape = (GROUP * halves, 2, shard, 3 * COLS) if paired else (LATENT_DIM, 3 * COLS)
    weights, *inner = call(
        rims_kernel,
        "project_rims",
        [(w_shape, BF16)] + rims,
        "h" + "a" * len(columns),
        [pltpu.VMEM((len(rims), RIM, LATENT_DIM), BF16), pltpu.SemaphoreType.DMA((4,))],
        flops=RIM * LATENT_DIM * 4 * COLS,
        moved=2**20,
    )(normed, *columns)
    def across(inner):
        if halves == 2:
            got = swap(inner[0], "half", 1)
            return got, got
        return lax.ppermute(inner[1], "half", up), lax.ppermute(inner[0], "half", down)

    if not paired:
        sources = [exchange(sources[0], "ens")]
    elif not square:
        sources = [sources[0], swap(sources[1], "ens", 1)]
    low, high = across(inner)
    queries, own = call(
        project_kernel,
        "project",
        [((rows, COLS), BF16), ((rows, 2 * COLS), BF16)],
        "hv",
        [pltpu.VMEM((rows, LATENT_DIM), BF16), pltpu.SemaphoreType.DMA((CHUNKS,))],
        flops=rows * LATENT_DIM * 6 * COLS,
        moved=4 * 2**20,
    )(normed, weights)

    (outcome,) = call(
        interior_kernel,
        "attention_interior",
        [((rows, COLS), BF16)],
        "vvv",
        flops=rows * COLS * 2048,
        moved=2**21,
        exps=rows * 512,
    )(steps, queries, own)
    (outcome,) = call(
        edge_kernel,
        "attention_edges",
        [((rows, COLS), BF16)],
        "vvvvvv",
        flops=rows * COLS * 512,
        moved=2**20,
        exps=rows * 128,
    )(steps, queries, own, low, high, outcome)
    *pieces, own = lax.optimization_barrier((*pieces, own))
    pieces = pieces + [swap(piece, "core", 1) for piece in pieces]
    attended = exchange(outcome.reshape(GROUP * members_num, part, COLS), ("quad", "core", "ens"))
    block = (halves, QUAD, CORES, members_num * shard, width)
    (weights,) = call(
        assemble_kernel,
        "assemble",
        [(block, BF16)],
        "a" * len(pieces),
        [pltpu.SemaphoreType.DMA((GROUP,))],
        moved=4 * 2**20,
        results="h",
    )(*pieces)

    prediction, grads = call(
        mix_kernel,
        "mix_loss_backward",
        [((FIELD_NUM, node_rows), F32), ((GROUP * members_num, part, COLS), BF16)],
        "vvhh" + "a" * len(sources),
        [
            pltpu.VMEM((node_rows, LATENT_DIM), BF16),
            pltpu.VMEM(observed_truth.shape, F32),
            pltpu.VMEM((FIELD_PAD, node_rows), F32),
            pltpu.VMEM((members_num, part, LATENT_DIM), BF16),
            pltpu.VMEM(block, BF16),
            pltpu.SemaphoreType.DMA((halves + 1 + len(sources),)),
        ],
        flops=node_rows * LATENT_DIM * 4 * width,
        moved=2**22,
        room=14,
    )(attended, cell_surface_factor[None], observed_truth, weights, *sources)
    grads = exchange(grads, ("quad", "core", "ens")).reshape(rows, COLS)

    edges, *inner = call(
        edge_back_kernel,
        "attention_edges_back",
        [((2, WINDOW - RIM, 2 * COLS), F32)] + rims,
        "vvvvvv",
        flops=rows * COLS * 1280,
        moved=2**20,
        exps=rows * 128,
    )(steps, queries, own, low, high, grads)
    from_low, from_high = across(inner)
    (kv_grads,) = call(
        interior_back_kernel,
        "attention_interior_back",
        [((rows, 2 * COLS), F32)],
        "vvvvv",
        flops=rows * COLS * 4096,
        moved=2**22,
        exps=rows * 512,
        room=10,
    )(steps, queries, own, grads, edges)
    (total,) = call(
        product_kernel,
        "product",
        [((LATENT_DIM, 2 * COLS), F32)],
        "vv",
        room=16,
    )(normed, kv_grads)
    arrived = [from_low] if halves == 2 else [from_low, from_high]
    (term,) = call(
        rim_product_kernel,
        "product_rims",
        [((LATENT_DIM, 2 * COLS), BF16)],
        "vv" + "v" * len(arrived),
        flops=RIM * LATENT_DIM * 4 * COLS,
        moved=2**21,
        room=16,
    )(normed, total, *arrived)
    term, prediction = lax.optimization_barrier((term, prediction))
    term = exchange(term.reshape(-1, shard, 2 * COLS), everyone)
    (grad_kv,) = call(
        gather_kernel, "gather_sums", [((shard, 2 * LATENT_DIM), F32)], "v", flops=2**17, moved=2**20
    )(term.reshape(halves, GROUP, members_num, shard, 2 * COLS))

    if members_num == 2:
        got = jnp.roll(swap(prediction, "ens", 1), part, axis=1)
        lane = lax.broadcasted_iota(jnp.int32, prediction.shape, 1)
        prediction = jnp.where(lane // part == ens, prediction, got)
    else:
        prediction = prediction.reshape(FIELD_NUM, members_num, part).transpose(1, 0, 2)
        prediction = exchange(prediction, "ens").transpose(1, 0, 2)
    return (prediction.reshape(1, FIELD_NUM, node_rows), grad_kv)


def solution(mesh):
    space, ens = mesh.shape["space"], mesh.shape["ens"]
    split = Mesh(
        mesh.devices.reshape(space // GROUP, QUAD, CORES, ens), ("half", "quad", "core", "ens")
    )
    nodes = ("half", "quad", "core")
    shards = nodes + ("ens",)
    in_specs = (
        P("ens", nodes, None),
        P(shards, None),
        P(shards, None),
        P(shards, None),
        P(None, nodes),
        P(nodes),
        P(nodes, None),
    )
    out_specs = (P("ens", None, nodes), P(shards, None))
    return jax.shard_map(body, mesh=split, in_specs=in_specs, out_specs=out_specs, check_vma=False)
```

```python
import functools

import jax
import jax.numpy as jnp
from jax import lax
from jax.experimental import pallas as pl
from jax.experimental.pallas import tpu as pltpu
from jax.sharding import Mesh
from jax.sharding import PartitionSpec as P

LATENT_DIM = 1024
HEADS = 16
HEAD = 64
FIELD_NUM = 100
TILE = 64
RADIUS = 2
K_NB = 4
QUAD = 4
CORES = 2
GROUP = QUAD * CORES
COLS = LATENT_DIM // GROUP
RIM = RADIUS * TILE
FIELD_PAD = 128
PAIR = 2
WINDOW = (PAIR + 2 * RADIUS) * TILE
NOWHERE = 100
NOTE_ROWS = 16
CHUNKS = 4

NORM_EPS = 1e-06
SOFT_WIDTH = 0.0625
MASKED = -1e30

F32 = jnp.float32
BF16 = jnp.bfloat16

VMEM = pl.BlockSpec(memory_space=pltpu.VMEM)
SMEM = pl.BlockSpec(memory_space=pltpu.SMEM)
HBM = pl.BlockSpec(memory_space=pltpu.HBM)
ANYWHERE = pl.BlockSpec(memory_space=pl.ANY)
OVER_ROWS = (((0,), (0,)), ((), ()))
OVER_COLUMNS = (((1,), (1,)), ((), ()))


def call(kernel, name, outs, ins, scratch=(), flops=0, moved=0, exps=0, room=8, results=None):
    results = results or "v" * len(outs)
    spaces = {"s": SMEM, "v": VMEM, "h": HBM, "a": ANYWHERE}
    made = pl.pallas_call(
        kernel,
        out_shape=[
            pltpu.HBM(shape, kind) if space == "h" else jax.ShapeDtypeStruct(shape, kind)
            for (shape, kind), space in zip(outs, results)
        ],
        in_specs=[spaces[space] for space in ins],
        out_specs=[spaces[space] for space in results],
        scratch_shapes=list(scratch),
        compiler_params=pltpu.CompilerParams(vmem_limit_bytes=room * 2**20),
        cost_estimate=pl.CostEstimate(flops=flops, bytes_accessed=moved, transcendentals=exps),
        name=name,
    )

    def run(*args):
        return made(
            *[
                pltpu.with_memory_space_constraint(arg, pltpu.HBM) if space == "h" else arg
                for arg, space in zip(args, ins)
            ]
        )

    return run


def fetch(pairs, sems, first=0):
    copies = [
        pltpu.make_async_copy(source, target, sems.at[first + at])
        for at, (source, target) in enumerate(pairs)
    ]
    for copy in copies:
        copy.start()
    return copies


def wait(copies):
    for copy in copies:
        copy.wait()


def weights_kernel(w_any, mix_any, readout_any, columns_any, packed_any, *refs):
    w, columns, readout, packed, sems = refs
    copies = fetch(
        [(w_any, w), (readout_any, readout), (mix_any, packed.at[:, :LATENT_DIM])], sems
    )
    copies[0].wait()
    for g in range(GROUP):
        for part in range(3):
            at = (part * GROUP + g) * COLS
            columns[g, :, part * COLS : (part + 1) * COLS] = w[:, at : at + COLS]
    halves, _, members_num = columns_any.shape[:3]
    out = fetch(
        [
            (columns, columns_any.at[half, :, m])
            for half in range(halves)
            for m in range(members_num)
        ],
        sems,
        3,
    )
    wait(copies[1:])
    packed[:, LATENT_DIM:] = jnp.zeros((packed.shape[0], FIELD_PAD), BF16)
    packed[:, LATENT_DIM : LATENT_DIM + FIELD_NUM] = readout[...]
    wait(out + fetch([(packed, packed_any)], sems, 3 + len(out)))


def norm_kernel(near_any, source_any, normed_any, *refs):
    parts, (normed, near, source, sems) = refs[:-4], refs[-4:]
    ens = lax.axis_index("ens")
    copies = fetch([(source_any, source), (near_any, near)], sems)
    rows = source.shape[0]
    copies[0].wait()
    moves = []
    for step, part_any in enumerate(parts):
        count, part, _ = part_any.shape
        for m in range(count):
            place = (ens ^ step) if len(parts) == 2 else m
            place = pl.multiple_of(place * part, part)
            moves.append((source.at[pl.ds(place, part)], part_any.at[m]))
    out = fetch(moves, sems, 2)
    states = source[...].astype(F32)
    inverse = lax.rsqrt(jnp.mean(states * states, axis=-1, keepdims=True) + NORM_EPS)
    normed[:rows, :] = (states * inverse).astype(BF16)
    copies[1].wait()
    row = lax.broadcasted_iota(jnp.int32, (NOTE_ROWS, 128), 0)
    lane = lax.broadcasted_iota(jnp.int32, (NOTE_ROWS, 128), 1)
    note = jnp.zeros((NOTE_ROWS, 128), F32)
    tiles = near.shape[0]
    first_tile = lax.axis_index(("half", "quad", "core")) * tiles
    for tile in range(tiles):
        for slot in range(K_NB):
            at = near[tile, slot]
            step = jnp.where(at >= 0, at - first_tile - tile, NOWHERE).astype(F32)
            note = jnp.where((row == tile) & (lane == slot), step, note)
    normed[rows:, :] = jnp.zeros((NOTE_ROWS, LATENT_DIM), BF16)
    normed[rows:, :128] = note.astype(BF16)
    wait(out + fetch([(normed, normed_any)], sems, 2 + len(out)))


def attach_kernel(packed_ref, sent_any, out_ref, sems):
    width, shard = packed_ref.shape[2], packed_ref.shape[1]
    pairs = [
        (sent_any.at[0, pl.ds(at * shard, shard)], out_ref.at[at, :, width:]) for at in range(2)
    ]
    copies = fetch(pairs, sems)
    out_ref[:, :, :width] = packed_ref[...]
    wait(copies)


def merge_members_kernel(mine_ref, other_ref, packed_ref, source_ref):
    ens = lax.axis_index("ens")
    width = packed_ref.shape[3]
    for half in range(2):
        packed_ref[half, ens] = mine_ref[half, :, :width]
        packed_ref[half, ens ^ 1] = other_ref[half, :, :width]
    source_ref[...] = other_ref[:, :, width:].reshape(source_ref.shape)


def owners():
    core, quad = lax.axis_index("core"), lax.axis_index("quad")
    return [(quad ^ step) * CORES + (core ^ flip) for flip in range(CORES) for step in range(QUAD)]


def collect_kernel(*refs):
    blocks, (normed_any, steps_ref, notes, sems) = refs[:GROUP], refs[GROUP:]
    block = blocks[0].shape[0] - NOTE_ROWS
    pairs = []
    for rows_ref, owner in zip(blocks, owners()):
        place = pl.ds(pl.multiple_of(owner * block, block), block)
        pairs.append((rows_ref.at[:block], normed_any.at[place]))
        pairs.append((rows_ref.at[block:, :128], notes.at[owner]))
    wait(fetch(pairs, sems))
    steps_ref[...] = notes[...].astype(F32)


def put_rims(rims, first, last):
    if len(rims) == 1:
        rims[0][...] = jnp.where(lax.axis_index("half") == 0, last, first)
    else:
        rims[0][...], rims[1][...] = first, last


def rims_kernel(normed_any, *refs):
    rows, sems = refs[-2:]
    if len(refs[0].shape) == 2:
        columns, w, rims = refs[:1], refs[1], refs[2:-2]
        pairs = [(columns[0], w)]
    else:
        columns, w, rims = refs[:2], refs[2], refs[3:-2]
        ens = lax.axis_index("ens")
        pairs = [(part, w.at[:, ens ^ step]) for step, part in enumerate(columns)]
    last = normed_any.shape[0] - RIM
    if len(rims) == 1:
        place = pl.multiple_of(jnp.where(lax.axis_index("half") == 0, last, 0), RIM)
        pairs.append((normed_any.at[pl.ds(place, RIM)], rows.at[0]))
    else:
        pairs += [(normed_any.at[:RIM], rows.at[0]), (normed_any.at[last:], rows.at[1])]
    wait(fetch(pairs, sems))
    weights = w[...].reshape(LATENT_DIM, 3 * COLS)[:, COLS:]
    for at, rim_ref in enumerate(rims):
        rim_ref[...] = jnp.dot(rows[at], weights, preferred_element_type=F32).astype(BF16)


def project_kernel(normed_any, w_ref, q_ref, kv_ref, normed, sems):
    chunk = normed.shape[0] // CHUNKS
    rows = [slice(at * chunk, (at + 1) * chunk) for at in range(CHUNKS)]
    copies = fetch([(normed_any.at[part], normed.at[part]) for part in rows], sems)
    weights = w_ref[...].reshape(LATENT_DIM, 3 * COLS)
    for part, copy in zip(rows, copies):
        copy.wait()
        projected = jnp.dot(normed[part, :], weights, preferred_element_type=F32).astype(BF16)
        q_ref[part, :] = projected[:, :COLS] * jnp.asarray(HEAD**-0.5, BF16)
        kv_ref[part, :] = projected[:, COLS:]


def assemble_kernel(*refs):
    pieces, (w_any, sems) = refs[:GROUP], refs[GROUP:]
    core, quad = lax.axis_index("core"), lax.axis_index("quad")
    pairs = [
        (piece, w_any.at[:, quad ^ (at % QUAD), core ^ (at // QUAD)])
        for at, piece in enumerate(pieces)
    ]
    wait(fetch(pairs, sems))


def by_head(rows):
    lane = lax.broadcasted_iota(jnp.int32, rows.shape, 1)
    zero = jnp.zeros_like(rows)
    return jnp.concatenate(
        [jnp.where(lane < HEAD, rows, zero), jnp.where(lane < HEAD, zero, rows)], axis=0
    )


def usable_keys(steps_ref, pair):
    lane = (lax.broadcasted_iota(jnp.int32, (1, WINDOW), 1) // TILE - RADIUS).astype(F32)
    masks = []
    for query_tile in range(PAIR):
        found = jnp.zeros((1, WINDOW), F32)
        for slot in range(K_NB):
            step = steps_ref[pair, query_tile : query_tile + 1, slot : slot + 1]
            found = jnp.where(lane - query_tile == step, 1.0, found)
        masks.append(found)
    row = lax.broadcasted_iota(jnp.int32, (2 * PAIR * TILE, 1), 0) // TILE % PAIR
    return jnp.where(row == 0, masks[0], masks[1]) > 0


def raised_scores(queries, keys, usable):
    scores = lax.dot_general(queries, keys, OVER_COLUMNS, preferred_element_type=F32)
    scores = jnp.where(usable, scores, MASKED)
    raised = jnp.exp(scores - jnp.max(scores, axis=-1, keepdims=True))
    return raised, 1.0 / jnp.sum(raised, axis=-1, keepdims=True)


def attend(steps_ref, pair, queries, keys, values):
    raised, share = raised_scores(by_head(queries), keys, usable_keys(steps_ref, pair))
    both = jnp.dot(raised.astype(BF16), values, preferred_element_type=F32) * share
    lane = lax.broadcasted_iota(jnp.int32, queries.shape, 1)
    half = PAIR * TILE
    return jnp.where(lane < HEAD, both[:half], both[half:]).astype(BF16)


def interior_kernel(steps_ref, q_ref, kv_ref, out_ref):
    step = PAIR * TILE
    pairs = q_ref.shape[0] // step
    for pair in range(1, pairs - 1):
        window = slice((pair - 1) * step, (pair + 2) * step)
        rows = slice(pair * step, (pair + 1) * step)
        out_ref[rows, :] = attend(
            steps_ref, pair, q_ref[rows, :], kv_ref[window, :COLS], kv_ref[window, COLS:]
        )


def edge_kernel(steps_ref, q_ref, kv_ref, low_ref, high_ref, done_ref, out_ref):
    step = PAIR * TILE
    count = q_ref.shape[0]
    pairs = count // step
    out_ref[step : count - step, :] = done_ref[step : count - step, :]
    first = jnp.concatenate([low_ref[...], kv_ref[: 2 * step, :]], axis=0)
    last = jnp.concatenate([kv_ref[count - 2 * step :, :], high_ref[...]], axis=0)
    for pair, window in ((0, first), (pairs - 1, last)):
        rows = slice(pair * step, (pair + 1) * step)
        out_ref[rows, :] = attend(
            steps_ref, pair, q_ref[rows, :], window[:, :COLS], window[:, COLS:]
        )


def attend_back(steps_ref, pair, queries, grads, keys, values):
    queries, grads = by_head(queries), by_head(grads)
    raised, share = raised_scores(queries, keys, usable_keys(steps_ref, pair))
    probs = raised * share
    grad_probs = lax.dot_general(grads, values, OVER_COLUMNS, preferred_element_type=F32)
    row_delta = jnp.sum(probs * grad_probs, axis=-1, keepdims=True)
    grad_scores = (probs * (grad_probs - row_delta)).astype(BF16)
    key_grad = lax.dot_general(grad_scores, queries, OVER_ROWS, preferred_element_type=F32)
    value_grad = lax.dot_general(probs.astype(BF16), grads, OVER_ROWS, preferred_element_type=F32)
    return key_grad, value_grad


def edge_back_kernel(
    steps_ref, q_ref, kv_ref, low_ref, high_ref, g_ref, part_ref, *rims
):
    outer = []
    step = PAIR * TILE
    count = q_ref.shape[0]
    first = jnp.concatenate([low_ref[...], kv_ref[: 2 * step, :]], axis=0)
    last = jnp.concatenate([kv_ref[count - 2 * step :, :], high_ref[...]], axis=0)
    pairs = count // step
    for edge, pair, window in ((0, 0, first), (1, pairs - 1, last)):
        rows = slice(pair * step, (pair + 1) * step)
        grads = attend_back(
            steps_ref, pair, q_ref[rows, :], g_ref[rows, :], window[:, :COLS], window[:, COLS:]
        )
        rim = slice(0, RIM) if edge == 0 else slice(WINDOW - RIM, WINDOW)
        own = slice(RIM, WINDOW) if edge == 0 else slice(0, WINDOW - RIM)
        for at, grad in enumerate(grads):
            columns = slice(at * COLS, (at + 1) * COLS)
            part_ref[edge, :, columns] = grad[own]
        outer.append(jnp.concatenate([grad[rim].astype(BF16) for grad in grads], axis=1))
    put_rims(rims, *outer)


def interior_back_kernel(steps_ref, q_ref, kv_ref, g_ref, part_ref, out_ref):
    step = PAIR * TILE
    count = q_ref.shape[0]
    pairs = count // step
    reach = 2 * step
    out_ref[:reach, :] = part_ref[0]
    out_ref[reach : count - reach, :] = jnp.zeros((count - 2 * reach, 2 * COLS), F32)
    out_ref[count - reach :, :] = part_ref[1]
    for pair in range(1, pairs - 1):
        window = slice((pair - 1) * step, (pair + 2) * step)
        rows = slice(pair * step, (pair + 1) * step)
        key_grad, value_grad = attend_back(
            steps_ref,
            pair,
            q_ref[rows, :],
            g_ref[rows, :],
            kv_ref[window, :COLS],
            kv_ref[window, COLS:],
        )
        out_ref[window, :COLS] += key_grad
        out_ref[window, COLS:] += value_grad


def slope(spread):
    return spread * lax.rsqrt(spread * spread + SOFT_WIDTH)


def mix_kernel(att_ref, factor_ref, truth_any, w_any, *refs):
    sources, refs = refs[:-8], refs[-8:]
    pred_ref, grad_ref, a, truth_ref, truth, source, w, sems = refs
    members_num, part, _ = source.shape
    halves = w.shape[0]
    ens = lax.axis_index("ens")
    copies = fetch([(w_any.at[half], w.at[half]) for half in range(halves)], sems)
    pairs = [(truth_any, truth_ref)]
    if len(sources) == 1:
        pairs.append((sources[0], source))
    else:
        pairs += [(rows.at[0], source.at[ens ^ step]) for step, rows in enumerate(sources)]
    others = fetch(pairs, sems, halves)
    for g in range(GROUP):
        for m in range(members_num):
            a[m * part : (m + 1) * part, g * COLS : (g + 1) * COLS] = att_ref[g * members_num + m]
    wait(others)
    lane_part = lax.broadcasted_iota(jnp.int32, (1, a.shape[0]), 1) // part
    own_truth, own_factor = truth_ref[...], factor_ref[...]
    for turn in range(1, members_num):
        at = lane_part - turn
        here = jnp.where(at < 0, at + members_num, at) == ens
        own_truth = jnp.where(here, pltpu.roll(truth_ref[...], turn * part, 1), own_truth)
        own_factor = jnp.where(here, pltpu.roll(factor_ref[...], turn * part, 1), own_factor)
    truth[...] = jnp.zeros_like(truth)
    truth[:FIELD_NUM, :] = own_truth
    hidden = source[...].reshape(a.shape).astype(F32)
    count = LATENT_DIM // halves
    for half in range(halves):
        copies[half].wait()
        mix = w[half].reshape(count, LATENT_DIM + FIELD_PAD)[:, :LATENT_DIM]
        hidden += jnp.dot(
            a[:, half * count : (half + 1) * count], mix, preferred_element_type=F32
        )
    both = w[...].reshape(LATENT_DIM, LATENT_DIM + FIELD_PAD)
    mix, readout = both[:, :LATENT_DIM], both[:, LATENT_DIM:]
    inverse = lax.rsqrt(jnp.mean(hidden * hidden, axis=-1, keepdims=True) + NORM_EPS)
    decoded = (hidden * inverse).astype(BF16)
    prediction = lax.dot_general(
        readout, decoded, (((0,), (1,)), ((), ())), preferred_element_type=F32
    )
    pred_ref[...] = prediction[:FIELD_NUM]
    spread = jnp.zeros_like(prediction)
    for other in range(1, members_num):
        spread = spread + slope(prediction - pltpu.roll(prediction, other * part, 1))
    derivative = own_factor / FIELD_NUM * (
        slope(prediction - truth[...]) - spread / (members_num - 1)
    )
    grad_decoded = lax.dot_general(
        derivative.astype(BF16), readout, (((0,), (1,)), ((), ())), preferred_element_type=F32
    )
    grad_hidden = inverse * grad_decoded - hidden * inverse**3 * jnp.mean(
        grad_decoded * hidden, axis=-1, keepdims=True
    )
    grads = lax.dot_general(
        grad_hidden.astype(BF16), mix, OVER_COLUMNS, preferred_element_type=F32
    ).astype(BF16)
    for g in range(GROUP):
        for m in range(members_num):
            grad_ref[g * members_num + m] = grads[
                m * part : (m + 1) * part, g * COLS : (g + 1) * COLS
            ]


def product_kernel(normed_ref, grads_ref, out_ref):
    grads = grads_ref[...]
    high = grads.astype(BF16)
    low = (grads - high.astype(F32)).astype(BF16)
    both = lax.dot_general(
        normed_ref[...], jnp.concatenate([high, low], axis=1), OVER_ROWS, preferred_element_type=F32
    )
    out_ref[...] = both[:, : 2 * COLS] + both[:, 2 * COLS :]


def rim_product_kernel(normed_ref, total_ref, *refs):
    arrived, out_ref = refs[:-1], refs[-1]
    last_row = normed_ref.shape[0] - RIM
    half, last = lax.axis_index("half"), lax.axis_size("half") - 1
    if len(arrived) == 1:
        places = [pl.multiple_of(jnp.where(half == 0, last_row, 0), RIM)]
    else:
        places = [0, last_row]
    total = total_ref[...]
    for at, arrived_ref in enumerate(arrived):
        grads = arrived_ref[...]
        if len(arrived) == 2:
            grads = jnp.where((half > 0) if at == 0 else (half < last), grads.astype(F32), 0.0)
            grads = grads.astype(BF16)
        rows = normed_ref[pl.ds(places[at], RIM), :]
        total += lax.dot_general(rows, grads, OVER_ROWS, preferred_element_type=F32)
    out_ref[...] = total.astype(BF16)


def gather_kernel(parts_ref, out_ref):
    halves, _, members_num = parts_ref.shape[:3]
    for g in range(GROUP):
        total = None
        for half in range(halves):
            for m in range(members_num):
                part = parts_ref[half, g, m].astype(F32)
                total = part if total is None else total + part
        out_ref[:, g * COLS : (g + 1) * COLS] = total[:, :COLS]
        out_ref[:, LATENT_DIM + g * COLS : LATENT_DIM + (g + 1) * COLS] = total[:, COLS:]


def exchange(chunks, axes):
    return lax.all_to_all(chunks, axes, 0, 0)


def swap(value, axis, step):
    return lax.ppermute(value, axis, [(i, i ^ step) for i in range(lax.axis_size(axis))])


def in_order(mine, axis, at):
    if lax.axis_size(axis) != 2:
        return lax.all_gather(mine, axis, axis=at)
    other = swap(mine, axis, 1)
    first = lax.axis_index(axis) == 0
    return jnp.stack([jnp.where(first, mine, other), jnp.where(first, other, mine)], axis=at)


def body(members, w_attn, w_mix, readout_matrix, observed_truth, cell_surface_factor, neighbours):
    halves, members_num = lax.axis_size("half"), lax.axis_size("ens")
    nodes = ("half", "quad", "core")
    everyone = nodes + ("ens",)
    shard = w_attn.shape[0]
    node_rows = members.shape[1]
    rows = GROUP * node_rows
    part = node_rows // members_num
    up = [(i, i + 1) for i in range(halves - 1)]
    down = [(target, source) for source, target in up]
    ens = lax.axis_index("ens")
    width = LATENT_DIM + FIELD_PAD
    paired = members_num == 2
    copies = 1 if paired else members_num
    source_parts = 2 if paired else 1

    columns, packed = call(
        weights_kernel,
        "prepare_weights",
        [((halves, GROUP, copies, shard, 3 * COLS), BF16), ((shard, width), BF16)],
        "hhh",
        [
            pltpu.VMEM(w_attn.shape, BF16),
            pltpu.VMEM((GROUP, shard, 3 * COLS), BF16),
            pltpu.VMEM(readout_matrix.shape, BF16),
            pltpu.VMEM((shard, width), BF16),
            pltpu.SemaphoreType.DMA((4 + halves * copies,)),
        ],
        moved=2**20,
        results="hh",
    )(w_attn, w_mix, readout_matrix)
    normed, *sources, own_block = call(
        norm_kernel,
        "norm",
        [((node_rows + NOTE_ROWS, LATENT_DIM), BF16)]
        + [((1 if paired else members_num, part, LATENT_DIM), BF16)] * source_parts
        + [((node_rows + NOTE_ROWS, LATENT_DIM), BF16)],
        "hh",
        [
            pltpu.SMEM(neighbours.shape, jnp.int32),
            pltpu.VMEM((node_rows, LATENT_DIM), BF16),
            pltpu.SemaphoreType.DMA((3 + max(2, members_num),)),
        ],
        flops=2**20,
        moved=2**20,
        results="h" + "h" * source_parts + "v",
    )(neighbours, members.reshape(node_rows, LATENT_DIM))

    packed, normed = lax.optimization_barrier((in_order(packed, "half", 0), normed))
    square = paired and halves == 2 and shard % 16 == 0
    near = [normed, swap(normed, "quad", 1), None, swap(normed, "quad", 3)]
    if paired:
        columns = exchange(columns.reshape(-1, shard, 3 * COLS), nodes)
        if square:
            (wide,) = call(
                attach_kernel,
                "attach_sources",
                [((2, shard, width + LATENT_DIM), BF16)],
                "vh",
                [pltpu.SemaphoreType.DMA((2,))],
                moved=2**19,
            )(packed, sources[1])
            columns, late, wide = lax.optimization_barrier((columns, normed, wide))
        else:
            columns, late = lax.optimization_barrier((columns, normed))
        columns = [columns, swap(columns, "ens", 1)]
    else:
        columns = [exchange(columns.reshape(-1, shard, 3 * COLS), everyone)]
        columns = [columns[0].reshape(LATENT_DIM, 3 * COLS)]
        late = normed
    near[2] = swap(late, "quad", 2)
    near = list(lax.optimization_barrier(tuple(near)))
    far = [swap(piece, "core", 1) for piece in near]
    normed, steps = call(
        collect_kernel,
        "collect",
        [((rows, LATENT_DIM), BF16), ((GROUP, NOTE_ROWS, 128), F32)],
        "a" * (2 * QUAD),
        [pltpu.VMEM((GROUP, NOTE_ROWS, 128), BF16), pltpu.SemaphoreType.DMA((2 * GROUP,))],
        moved=4 * 2**20,
        results="hv",
    )(own_block, *near[1:], *far)

    if square:
        packed, arrived = call(
            merge_members_kernel,
            "merge_members",
            [((2, 2, shard, width), BF16), ((1, part, LATENT_DIM), BF16)],
            "vv",
            moved=2**19,
        )(wide, swap(wide, "ens", 1))
        packed = packed.reshape(2, 2 * shard, width)
        sources = [sources[0], arrived]
    else:
        packed = in_order(packed, "ens", 1).reshape(halves, members_num * shard, width)
    packed, near[2] = lax.optimization_barrier((packed, near[2]))
    pieces = {step: swap(packed, "quad", step) for step in (2, 3, 1)}
    pieces = [packed] + [pieces[step] for step in range(1, QUAD)]

    rim = ((RIM, 2 * COLS), BF16)
    rims = [rim] if halves == 2 else [rim, rim]
    w_shape = (GROUP * halves, 2, shard, 3 * COLS) if paired else (LATENT_DIM, 3 * COLS)
    weights, *inner = call(
        rims_kernel,
        "project_rims",
        [(w_shape, BF16)] + rims,
        "h" + "a" * len(columns),
        [pltpu.VMEM((len(rims), RIM, LATENT_DIM), BF16), pltpu.SemaphoreType.DMA((4,))],
        flops=RIM * LATENT_DIM * 4 * COLS,
        moved=2**20,
    )(normed, *columns)
    def across(inner):
        if halves == 2:
            got = swap(inner[0], "half", 1)
            return got, got
        return lax.ppermute(inner[1], "half", up), lax.ppermute(inner[0], "half", down)

    if not paired:
        sources = [exchange(sources[0], "ens")]
    elif not square:
        sources = [sources[0], swap(sources[1], "ens", 1)]
    low, high = across(inner)
    queries, own = call(
        project_kernel,
        "project",
        [((rows, COLS), BF16), ((rows, 2 * COLS), BF16)],
        "hv",
        [pltpu.VMEM((rows, LATENT_DIM), BF16), pltpu.SemaphoreType.DMA((CHUNKS,))],
        flops=rows * LATENT_DIM * 6 * COLS,
        moved=4 * 2**20,
    )(normed, weights)

    (outcome,) = call(
        interior_kernel,
        "attention_interior",
        [((rows, COLS), BF16)],
        "vvv",
        flops=rows * COLS * 2048,
        moved=2**21,
        exps=rows * 512,
    )(steps, queries, own)
    (outcome,) = call(
        edge_kernel,
        "attention_edges",
        [((rows, COLS), BF16)],
        "vvvvvv",
        flops=rows * COLS * 512,
        moved=2**20,
        exps=rows * 128,
    )(steps, queries, own, low, high, outcome)
    *pieces, own = lax.optimization_barrier((*pieces, own))
    pieces = pieces + [swap(piece, "core", 1) for piece in pieces]
    attended = exchange(outcome.reshape(GROUP * members_num, part, COLS), ("quad", "core", "ens"))
    block = (halves, QUAD, CORES, members_num * shard, width)
    (weights,) = call(
        assemble_kernel,
        "assemble",
        [(block, BF16)],
        "a" * len(pieces),
        [pltpu.SemaphoreType.DMA((GROUP,))],
        moved=4 * 2**20,
        results="h",
    )(*pieces)

    prediction, grads = call(
        mix_kernel,
        "mix_loss_backward",
        [((FIELD_NUM, node_rows), F32), ((GROUP * members_num, part, COLS), BF16)],
        "vvhh" + "a" * len(sources),
        [
            pltpu.VMEM((node_rows, LATENT_DIM), BF16),
            pltpu.VMEM(observed_truth.shape, F32),
            pltpu.VMEM((FIELD_PAD, node_rows), F32),
            pltpu.VMEM((members_num, part, LATENT_DIM), BF16),
            pltpu.VMEM(block, BF16),
            pltpu.SemaphoreType.DMA((halves + 1 + len(sources),)),
        ],
        flops=node_rows * LATENT_DIM * 4 * width,
        moved=2**22,
        room=14,
    )(attended, cell_surface_factor[None], observed_truth, weights, *sources)
    grads = exchange(grads, ("quad", "core", "ens")).reshape(rows, COLS)

    edges, *inner = call(
        edge_back_kernel,
        "attention_edges_back",
        [((2, WINDOW - RIM, 2 * COLS), F32)] + rims,
        "vvvvvv",
        flops=rows * COLS * 1280,
        moved=2**20,
        exps=rows * 128,
    )(steps, queries, own, low, high, grads)
    from_low, from_high = across(inner)
    (kv_grads,) = call(
        interior_back_kernel,
        "attention_interior_back",
        [((rows, 2 * COLS), F32)],
        "vvvvv",
        flops=rows * COLS * 4096,
        moved=2**22,
        exps=rows * 512,
        room=10,
    )(steps, queries, own, grads, edges)
    (total,) = call(
        product_kernel,
        "product",
        [((LATENT_DIM, 2 * COLS), F32)],
        "vv",
        room=16,
    )(normed, kv_grads)
    arrived = [from_low] if halves == 2 else [from_low, from_high]
    (term,) = call(
        rim_product_kernel,
        "product_rims",
        [((LATENT_DIM, 2 * COLS), BF16)],
        "vv" + "v" * len(arrived),
        flops=RIM * LATENT_DIM * 4 * COLS,
        moved=2**21,
        room=16,
    )(normed, total, *arrived)
    term, prediction = lax.optimization_barrier((term, prediction))
    term = exchange(term.reshape(-1, shard, 2 * COLS), everyone)
    (grad_kv,) = call(
        gather_kernel, "gather_sums", [((shard, 2 * LATENT_DIM), F32)], "v", flops=2**17, moved=2**20
    )(term.reshape(halves, GROUP, members_num, shard, 2 * COLS))

    if members_num == 2:
        got = jnp.roll(swap(prediction, "ens", 1), part, axis=1)
        lane = lax.broadcasted_iota(jnp.int32, prediction.shape, 1)
        prediction = jnp.where(lane // part == ens, prediction, got)
    else:
        prediction = prediction.reshape(FIELD_NUM, members_num, part).transpose(1, 0, 2)
        prediction = exchange(prediction, "ens").transpose(1, 0, 2)
    return (prediction.reshape(1, FIELD_NUM, node_rows), grad_kv)


def solution(mesh):
    space, ens = mesh.shape["space"], mesh.shape["ens"]
    split = Mesh(
        mesh.devices.reshape(space // GROUP, QUAD, CORES, ens), ("half", "quad", "core", "ens")
    )
    nodes = ("half", "quad", "core")
    shards = nodes + ("ens",)
    in_specs = (
        P("ens", nodes, None),
        P(shards, None),
        P(shards, None),
        P(shards, None),
        P(None, nodes),
        P(nodes),
        P(nodes, None),
    )
    out_specs = (P("ens", None, nodes), P(shards, None))
    return jax.shard_map(body, mesh=split, in_specs=in_specs, out_specs=out_specs, check_vma=False)
```
